32 devices in a mesh: dp: 8 (over z, y), tensor: 4 (over x, core).
Axes of the slice: x: 2, y: 2, z: 4, core: 2. Of those that a mesh axis runs over, the one named last changes fastest.
Arguments:
- tokens: bfloat16 [8, 1536, 1024], P('dp'), may hold values from -6 to 6
- cotangent: bfloat16 [8, 1536, 1024], P('dp'), may hold values from -12 to 12
- parents: int32 [8, 13], replicated, may hold values from 0 to 4, as said below
- token_segment: int32 [8, 1536], P('dp'), may hold values from 0 to 12, never falling along the last dimension, each value on 1 to 384 neighbouring positions
- tree_id: int32 [8], P('dp'), may hold values from 0 to 7
- projection_weight: float32 [1024, 8, 4, 128], P('dp', 'tensor'), may hold values from -0.1875 to 0.1875
- projection_first_moment: float32 [1024, 8, 4, 128], P('dp', 'tensor'), may hold values from -1280 to 1280
- projection_second_moment: float32 [1024, 8, 4, 128], P('dp', 'tensor'), may hold values from 49152 to 196608
- merge_master: float32 [2048, 1024], P('tensor', 'dp'), may hold values from -0.75 to 0.75
- merge_mean: float32 [2048, 1024], P('tensor', 'dp'), may hold values from -160 to 160
- merge_square: float32 [2048, 1024], P('tensor', 'dp'), may hold values from 384 to 3072
- expand_master: float32 [1024, 2, 3072], P('dp', None, 'tensor'), may hold values from -0.1875 to 0.1875
- expand_mean: float32 [1024, 2, 3072], P('dp', None, 'tensor'), may hold values from -384 to 384
- expand_square: float32 [1024, 2, 3072], P('dp', None, 'tensor'), may hold values from 2048 to 12288
- shrink_master: float32 [3072, 1024], P('tensor', 'dp'), may hold values from -0.109375 to 0.109375
- shrink_mean: float32 [3072, 1024], P('tensor', 'dp'), may hold values from -640 to 640
- shrink_square: float32 [3072, 1024], P('tensor', 'dp'), may hold values from 6144 to 49152
- gain_master: float32 [2304], replicated, may hold values from 0.5 to 1.5
- gain_mean: float32 [2304], replicated, may hold values from -640 to 640
- gain_square: float32 [2304], replicated, may hold values from 3072 to 49152
Outputs:
- output: bfloat16 [8, 1536, 1024], P('dp', 'tensor')
- input_grad: bfloat16 [8, 1536, 1024], P('dp', 'tensor')
- project_next: float32 [1024, 8, 4, 128], P('dp', 'tensor')
- project_mean_next: float32 [1024, 8, 4, 128], P('dp', 'tensor')
- project_square_next: float32 [1024, 8, 4, 128], P('dp', 'tensor')
- project_copy: bfloat16 [1024, 8, 4, 128], P('dp', 'tensor')
- merge_next: float32 [2048, 1024], P('tensor', 'dp')
- merge_mean_next: float32 [2048, 1024], P('tensor', 'dp')
- merge_square_next: float32 [2048, 1024], P('tensor', 'dp')
- merge_copy: bfloat16 [2048, 1024], P('tensor', 'dp')
- expand_next: float32 [1024, 2, 3072], P('dp', None, 'tensor')
- expand_mean_next: float32 [1024, 2, 3072], P('dp', None, 'tensor')
- expand_square_next: float32 [1024, 2, 3072], P('dp', None, 'tensor')
- expand_copy: bfloat16 [1024, 2, 3072], P('dp', None, 'tensor')
- shrink_next: float32 [3072, 1024], P('tensor', 'dp')
- shrink_mean_next: float32 [3072, 1024], P('tensor', 'dp')
- shrink_square_next: float32 [3072, 1024], P('tensor', 'dp')
- shrink_copy: bfloat16 [3072, 1024], P('tensor', 'dp')
- gain_mean_next: float32 [2304], replicated
- gain_square_next: float32 [2304], replicated
- gain_next: float32 [2304], replicated
The draws below stay inside these ranges and needn't reach their ends.
Inputs may be any that keep to these rules, and one draw needn't show every extreme that they name: `parents`: in each row segment 0 is the trunk and its own parent, segments 1 to 4 have parent 0, and every later segment has a parent among 1 to 4. `token_segment`: within a tree the segment numbers never fall and all 13 segments are present.
All inputs are finite; a program needn't handle non-finite values.
Results may differ from the reference program's by a relative error of at most 0.015.
Values may be sent and summed in bfloat16 or wider, within the bound.
A program may use at most 192 MiB of HBM per device.

```python
import math
import jax
import jax.numpy as jnp
import numpy as np
from jax import lax

MODEL_DIMENSION = 1024
HQ = 16
KEY_VALUE_HEADS = 8
HEAD_SIZE = 128
FF = 3072
TREE_TOKENS = 1536
SEGS = 13
BRANCHES = 4
SHAPES = 8
STEP = 5
SEQS = 8
QUERY_HEADS_EACH = 2
N_DP = 8


def draw_cotangent(key, part):
    key = jax.random.fold_in(key, 11)
    steps = jnp.arange(SEQS, dtype=jnp.float32) / (SEQS - 1)
    rising = 1.0 + 2.0 * steps
    base = jax.random.truncated_normal(key, -4.0, 4.0, (SEQS, TREE_TOKENS, MODEL_DIMENSION), jnp.float32)
    return (base * rising[:, None, None]).astype(jnp.bfloat16)


def draw_parents(key, part):
    key = jax.random.fold_in(key, 5)
    labels = jnp.arange(SEGS, dtype=jnp.int32)
    picks = jax.random.randint(key, (SHAPES, SEGS), 1, BRANCHES + 1, dtype=jnp.int32)
    return jnp.where(labels[None, :] > BRANCHES, picks, 0).astype(jnp.int32)


def touch_ends(array, stream_key, smallest, largest):
    dims = array.shape
    spot = [jax.random.randint(jax.random.fold_in(stream_key, axis), (), 0, dims[axis]) for axis in range(len(dims))]
    array = array.at[tuple(spot)].set(smallest)
    longest = dims.index(max(dims))
    spot[longest] = (spot[longest] + 1) % dims[longest]
    return array.at[tuple(spot)].set(largest)


def level_of(own_key, shape, pieces, least, largest):
    def one(dim, shards_of):
        heights = jax.random.uniform(jax.random.fold_in(jax.random.fold_in(own_key, 6), dim), (shards_of,), jnp.float32, least / len(pieces), largest / len(pieces))
        return jnp.repeat(jnp.exp(heights), shape[dim] // shards_of).reshape((-1,) + (1,) * (len(shape) - dim - 1))

    gain = one(*pieces[0])
    for cut in pieces[1:]:
        gain = gain * one(*cut)
    return gain


def profile(number_of, total, reach, skew):
    loads = [(1 << 20) // math.isqrt(standing ** skew) + 1 for standing in range(2, number_of + 1)]
    rest, given = total - reach - (number_of - 1), [1] * (number_of - 1)
    while rest > 0:
        movable = [i for i in range(number_of - 1) if given[i] < reach]
        whole, left = sum([loads[i] for i in movable]), rest
        for i in movable:
            addition = min(reach - given[i], max(1, left * loads[i] // whole), rest)
            given[i] = given[i] + addition
            rest = rest - addition
    return np.array([reach] + given)


def uneven(stream_key, amount, total, bound, skew):
    if amount == 2:
        one = jax.random.randint(stream_key, (), max(1, total - bound), min(bound, total - 1) + 1)
        return jnp.stack([one, total - one])
    tallies = jnp.asarray(profile(amount, total, bound, skew), jnp.int32)
    pairs = (amount - 1) // 2
    giver, sink = tallies[1:1 + 2 * pairs:2], tallies[2:2 + 2 * pairs:2]
    slack = jnp.minimum(giver - 1, bound - sink)
    passed = jax.random.randint(jax.random.fold_in(stream_key, 1), (pairs,), 0, 1 << 20) % (slack + 1)
    tallies = tallies.at[1:1 + 2 * pairs:2].set(giver - passed).at[2:2 + 2 * pairs:2].set(sink + passed)
    return tallies[jax.random.permutation(jax.random.fold_in(stream_key, 2), amount)]


def noise(own_key, extent, deviation, reach, pieces=(), kind=jnp.bfloat16):
    entries = jax.random.normal(own_key, extent, jnp.float32) * deviation
    if len(pieces) > 0:
        entries = level_of(own_key, extent, pieces, -0.22, 0.18) * entries
    return jnp.clip(entries, min=-reach, max=reach).astype(kind)


def setup_inputs(seed: int = 0) -> dict:
    seeds = jax.random.split(jax.random.key(seed), 21)
    return {
        "tokens": noise(seeds[0], (SEQS, TREE_TOKENS, MODEL_DIMENSION), 1.0, 6.0, ((0, 8),)),
        "cotangent": draw_cotangent(jax.random.fold_in(seeds[20], 71), 0),
        "parents": draw_parents(jax.random.fold_in(seeds[20], 71), 0),
        "token_segment": jax.vmap(lambda own: jnp.searchsorted(jnp.cumsum(uneven(own, SEGS, TREE_TOKENS, TREE_TOKENS // 4, 1)), jnp.arange(TREE_TOKENS), side="right"))(jax.random.split(seeds[3], SEQS)).reshape((SEQS, TREE_TOKENS)).astype(jnp.int32),
        "tree_id": touch_ends(jax.random.randint(seeds[4], (SEQS,), 0, SHAPES), jax.random.fold_in(seeds[4], 1), 0, SHAPES - 1).astype(jnp.int32),
        "projection_weight": noise(seeds[5], (MODEL_DIMENSION, KEY_VALUE_HEADS, QUERY_HEADS_EACH + 2, HEAD_SIZE), MODEL_DIMENSION ** -0.5, 0.1875, ((0, 8), (1, 4)), jnp.float32),
        "projection_first_moment": noise(seeds[6], (MODEL_DIMENSION, KEY_VALUE_HEADS, QUERY_HEADS_EACH + 2, HEAD_SIZE), ((TREE_TOKENS * N_DP * 4) ** 0.5), 1280.0, ((0, 8), (1, 4)), jnp.float32),
        "projection_second_moment": jnp.clip(jnp.exp(math.log(196608.0) - 1.3862944 * jax.random.uniform(seeds[7], (MODEL_DIMENSION, KEY_VALUE_HEADS, QUERY_HEADS_EACH + 2, HEAD_SIZE), jnp.float32) ** level_of(seeds[7], (MODEL_DIMENSION, KEY_VALUE_HEADS, QUERY_HEADS_EACH + 2, HEAD_SIZE), ((0, 8), (1, 4)), -0.2, 0.2)), 49152.0, 196608.0),
        "merge_master": noise(seeds[8], (HQ * HEAD_SIZE, MODEL_DIMENSION), (HQ * HEAD_SIZE // 32) ** -0.5, 0.75, ((0, 4), (1, 8)), jnp.float32),
        "merge_mean": noise(seeds[9], (HQ * HEAD_SIZE, MODEL_DIMENSION), ((TREE_TOKENS * N_DP // 16) ** 0.5), 160.0, ((0, 4), (1, 8)), jnp.float32),
        "merge_square": jnp.clip(jnp.exp(math.log(3072.0) - 2.0794415 * jax.random.uniform(seeds[10], (HQ * HEAD_SIZE, MODEL_DIMENSION), jnp.float32) ** level_of(seeds[10], (HQ * HEAD_SIZE, MODEL_DIMENSION), ((0, 4), (1, 8)), -0.2, 0.2)), 384.0, 3072.0),
        "expand_master": noise(seeds[11], (MODEL_DIMENSION, 2, FF), MODEL_DIMENSION ** -0.5, 0.1875, ((0, 8), (2, 4)), jnp.float32),
        "expand_mean": noise(seeds[12], (MODEL_DIMENSION, 2, FF), ((TREE_TOKENS * N_DP // 3) ** 0.5), 384.0, ((0, 8), (2, 4)), jnp.float32),
        "expand_square": jnp.clip(jnp.exp(math.log(12288.0) - 1.7917595 * jax.random.uniform(seeds[13], (MODEL_DIMENSION, 2, FF), jnp.float32) ** level_of(seeds[13], (MODEL_DIMENSION, 2, FF), ((0, 8), (2, 4)), -0.2, 0.2)), 2048.0, 12288.0),
        "shrink_master": noise(seeds[14], (FF, MODEL_DIMENSION), FF ** -0.5, 0.109375, ((0, 4), (1, 8)), jnp.float32),
        "shrink_mean": noise(seeds[15], (FF, MODEL_DIMENSION), ((TREE_TOKENS * N_DP) ** 0.5), 640.0, ((0, 4), (1, 8)), jnp.float32),
        "shrink_square": jnp.clip(jnp.exp(math.log(49152.0) - 2.0794415 * jax.random.uniform(seeds[16], (FF, MODEL_DIMENSION), jnp.float32) ** level_of(seeds[16], (FF, MODEL_DIMENSION), ((0, 4), (1, 8)), -0.2, 0.2)), 6144.0, 49152.0),
        "gain_master": jnp.clip(1.0 + 0.1 * jax.random.normal(seeds[17], (2 * MODEL_DIMENSION + 2 * HEAD_SIZE,), jnp.float32), 0.5, 1.5),
        "gain_mean": noise(seeds[18], (2 * MODEL_DIMENSION + 2 * HEAD_SIZE,), ((TREE_TOKENS * N_DP) ** 0.5), 640.0, (), jnp.float32),
        "gain_square": jnp.clip(jnp.exp(jax.random.uniform(seeds[19], (2 * MODEL_DIMENSION + 2 * HEAD_SIZE,), jnp.float32, math.log(3072.0), math.log(49152.0))), 3072.0, 49152.0),
    }


EPS_NORM = 1e-06
THETA = 1000000.0
BETA_ONE = 0.5
BETA_TWO = 0.5
EPS_ADAM = 1e-08
DECAY = 0.1
RATE_PROJECT = 0.05
RATE_MERGE = 0.3
RATE_EXPAND = 0.05
RATE_SHRINK = 0.03
RATE_GAIN = 0.3
HIGHEST = lax.Precision.HIGHEST

@jax.custom_vjp
def low(v):
    return lax.optimization_barrier(v.astype(jnp.bfloat16)).astype(jnp.float32)

@jax.custom_vjp
def low_back(v):
    return v

def low_keep(v):
    return (low(v), None)

def low_pass(kept, grad):
    return (grad,)

def back_keep(v):
    return (v, None)

def back_low(kept, grad):
    return (low(grad),)
low.defvjp(low_keep, low_pass)
low_back.defvjp(back_keep, back_low)

def rms_scale(values, scales):
    return values * lax.rsqrt(lax.optimization_barrier(jnp.mean(values * values, axis=-1, keepdims=True)) + EPS_NORM) * scales

def rotate(values, cosines, sines):
    half_dim = values.shape[-1] // 2
    front = values[..., :half_dim]
    behind = values[..., half_dim:]
    return jnp.concatenate([front * cosines - behind * sines, behind * cosines + front * sines], axis=-1)

def tree_tables(segment_ids, parent_row, head_dim):
    seg_count = parent_row.shape[0]
    length = segment_ids.shape[0]
    labels = jnp.arange(seg_count, dtype=jnp.int32)
    onehot = (segment_ids[:, None] == labels[None, :]).astype(jnp.float32)
    parent_map = (parent_row[:, None] == labels[None, :]).astype(jnp.float32)
    identity = jnp.eye(seg_count, dtype=jnp.float32)
    reached = identity
    walker = identity
    for repeat in range(seg_count):
        walker = jnp.dot(walker, parent_map, precision=HIGHEST)
        reached = jnp.maximum(reached, walker)
    seg_lengths = lax.optimization_barrier(jnp.sum(onehot, axis=0))
    starts = jnp.cumsum(seg_lengths) - seg_lengths
    offsets = jnp.dot(reached - identity, seg_lengths, precision=HIGHEST)
    position = jnp.arange(length).astype(jnp.float32) + jnp.dot(onehot, offsets - starts, precision=HIGHEST)
    frequency = THETA ** (-jnp.arange(head_dim // 2).astype(jnp.float32) * 2.0 / head_dim)
    angles = position[:, None] * frequency[None, :]
    columns = jnp.dot(reached, onehot.T, precision=HIGHEST)
    return (onehot, columns, jnp.cos(angles), jnp.sin(angles))

def adamw_step(weight, moment_one, moment_two, gradient, step_rate, decay):
    mean_next = BETA_ONE * moment_one + (1.0 - BETA_ONE) * gradient
    square_next = BETA_TWO * moment_two + (1.0 - BETA_TWO) * gradient * gradient
    mean_hat = mean_next / (1.0 - BETA_ONE ** STEP)
    square_hat = square_next / (1.0 - BETA_TWO ** STEP)
    weight_next = weight - step_rate * (mean_hat / (jnp.sqrt(square_hat) + EPS_ADAM) + decay * weight)
    return (weight_next, mean_next, square_next)

def forward(tokens, project, merge, expand, shrink, gains, allowed, cosines, sines):
    length, model_width = tokens.shape
    head_dim = project.shape[3]
    group_size = project.shape[2] - 2
    norm_one = gains[:model_width]
    norm_two = gains[model_width:2 * model_width]
    query_gain = gains[2 * model_width:2 * model_width + head_dim]
    key_gain = gains[2 * model_width + head_dim:]
    normed = low(rms_scale(tokens, norm_one))
    projected = low_back(jnp.einsum('sd,dhcn->shcn', normed, project, precision=HIGHEST))
    queries = low(rotate(rms_scale(projected[:, :, :group_size], query_gain), cosines[:, None, None], sines[:, None, None]))
    key_rows = low(rotate(rms_scale(projected[:, :, group_size], key_gain), cosines[:, None], sines[:, None]))
    value_rows = low(projected[:, :, group_size + 1])
    scores = low_back(jnp.einsum('qhgn,khn->hgqk', queries, key_rows, precision=HIGHEST) * head_dim ** (-0.5))
    probabilities = low(jax.nn.softmax(jnp.where(allowed, scores, -jnp.inf), axis=-1))
    context = low(low_back(jnp.einsum('hgqk,khn->qhgn', probabilities, value_rows, precision=HIGHEST)))
    attended = low_back(jnp.dot(context.reshape(length, -1), merge, precision=HIGHEST))
    hidden = tokens + attended
    normed_two = low(rms_scale(hidden, norm_two))
    gate_up = low_back(jnp.einsum('sd,dcf->scf', normed_two, expand, precision=HIGHEST))
    active = low(jax.nn.silu(gate_up[:, 0]) * gate_up[:, 1])
    branch = low_back(jnp.dot(active, shrink, precision=HIGHEST))
    return hidden + branch

def reference(tokens, cotangent, parents, token_segment, tree_id, projection_weight, projection_first_moment, projection_second_moment, merge_master, merge_mean, merge_square, expand_master, expand_mean, expand_square, shrink_master, shrink_mean, shrink_square, gain_master, gain_mean, gain_square):
    weights_low = (low(projection_weight), low(merge_master), low(expand_master), low(shrink_master))
    shapes_count = parents.shape[0]
    row_ids = jnp.arange(TREE_TOKENS)
    causal = row_ids[None, :] <= row_ids[:, None]

    def per_tree(carried, item):
        seq_tokens, seq_cot, seq_segments, seq_tree = item
        chosen = (jnp.arange(shapes_count) == seq_tree).astype(parents.dtype)
        parent_row = lax.optimization_barrier(jnp.sum(parents * chosen[:, None], axis=0)).astype(jnp.int32)
        onehot, columns, cosines, sines = tree_tables(seq_segments.astype(jnp.int32), parent_row, HEAD_SIZE)
        allowed = (jnp.dot(onehot, columns, precision=HIGHEST) > 0.5) & causal

        def layer_forward(tok, project, merge, expand, shrink, gains):
            return forward(tok, project, merge, expand, shrink, gains, allowed, cosines, sines)
        result, pull_back = jax.vjp(layer_forward, seq_tokens.astype(jnp.float32), *weights_low, gain_master)
        gradients = pull_back(seq_cot.astype(jnp.float32))
        summed = jax.tree.map(jnp.add, carried, tuple(gradients[1:]))
        return (summed, (result.astype(jnp.bfloat16), gradients[0].astype(jnp.bfloat16)))
    zero_grads = tuple((jnp.zeros_like(weight) for weight in weights_low)) + (jnp.zeros_like(gain_master),)
    totals, (output, input_grad) = lax.scan(per_tree, zero_grads, (tokens, cotangent, token_segment, tree_id))
    project_next, project_mean_next, project_square_next = adamw_step(projection_weight, projection_first_moment, projection_second_moment, totals[0], RATE_PROJECT, DECAY)
    merge_next, merge_mean_next, merge_square_next = adamw_step(merge_master, merge_mean, merge_square, totals[1], RATE_MERGE, DECAY)
    expand_next, expand_mean_next, expand_square_next = adamw_step(expand_master, expand_mean, expand_square, totals[2], RATE_EXPAND, DECAY)
    shrink_next, shrink_mean_next, shrink_square_next = adamw_step(shrink_master, shrink_mean, shrink_square, totals[3], RATE_SHRINK, DECAY)
    gain_next, gain_mean_next, gain_square_next = adamw_step(gain_master, gain_mean, gain_square, totals[4], RATE_GAIN, 0.0)
    return (output, input_grad, project_next, project_mean_next, project_square_next, project_next.astype(jnp.bfloat16), merge_next, merge_mean_next, merge_square_next, merge_next.astype(jnp.bfloat16), expand_next, expand_mean_next, expand_square_next, expand_next.astype(jnp.bfloat16), shrink_next, shrink_mean_next, shrink_square_next, shrink_next.astype(jnp.bfloat16), gain_mean_next, gain_square_next, gain_next)
```

```python
import math
from functools import partial

import jax
import jax.numpy as jnp
from jax import lax
from jax.experimental import pallas as pl
from jax.experimental.pallas import tpu as pltpu
from jax.sharding import PartitionSpec as P

STEP = 5
EPS_NORM = 1e-06
THETA = 1000000.0
BETA_ONE = 0.5
BETA_TWO = 0.5
EPS_ADAM = 1e-08
DECAY = 0.1
RATE_PROJECT = 0.05
RATE_MERGE = 0.3
RATE_EXPAND = 0.05
RATE_SHRINK = 0.03
RATE_GAIN = 0.3

BF = jnp.bfloat16
FP = jnp.float32
ROWS = 256
LANES = 128
BLOCKED = -1e30
VMEM_LIMIT = 60 * 2**20


def params(**more):
    return pltpu.CompilerParams(vmem_limit_bytes=VMEM_LIMIT, **more)


def dot(a, b, ca=1, cb=0):
    return lax.dot_general(a, b, (((ca,), (cb,)), ((), ())), preferred_element_type=FP)


def inverse_rms(values):
    return lax.rsqrt(jnp.mean(values * values, axis=-1, keepdims=True) + EPS_NORM)


def rms_pull(values, scales, grad):
    r = inverse_rms(values)
    scaled = grad * scales
    mean = jnp.mean(values * scaled, axis=-1, keepdims=True)
    return r * scaled - values * (r * r * r * mean), grad * values * r


def fold_rows(values):
    n, w = values.shape
    return jnp.sum(values.reshape(n // 8, 8, w), axis=0)


def front_kernel(kv, group, x_ref, g1_ref, gq_ref, gk_ref, cos_ref, sin_ref, wp_ref,
                 xn_ref, q_ref, k_ref, v_ref, kt_ref, vt_ref, raw_ref):
    x = x_ref[...].astype(FP)
    xn = (x * inverse_rms(x) * g1_ref[...]).astype(BF)
    xn_ref[...] = xn
    qkv = dot(xn, wp_ref[...])
    cosines, sines = cos_ref[...], sin_ref[...]
    n = LANES
    per = group + 2
    keys, values = [], []
    for h in range(kv):
        for c in range(group + 1):
            raw = qkv[:, (h * per + c) * n:(h * per + c + 1) * n]
            at = (h * (group + 1) + c) * n
            raw_ref[:, at:at + n] = raw
            y = raw * inverse_rms(raw) * (gq_ref[...] if c < group else gk_ref[...])
            turned = y * cosines + pltpu.roll(y, n // 2, 1) * sines
            if c < group:
                to = (h * group + c) * n
                q_ref[:, to:to + n] = turned.astype(BF)
            else:
                keys.append(turned)
        values.append(qkv[:, (h * per + group + 1) * n:(h * per + group + 2) * n])
    for h in range(kv):
        k_ref[:, h * n:(h + 1) * n] = keys[h].astype(BF)
        v_ref[:, h * n:(h + 1) * n] = values[h].astype(BF)
        kt_ref[h * n:(h + 1) * n, :] = keys[h].T.astype(BF)
        vt_ref[h * n:(h + 1) * n, :] = values[h].T.astype(BF)


def front(x, g1, gq, gk, cosines, sines, wp, kv, group):
    length, d = x.shape
    n = LANES
    steps = length // ROWS
    whole = lambda a: pl.BlockSpec(a.shape, lambda i: (0,) * a.ndim)
    rows = lambda w: pl.BlockSpec((ROWS, w), lambda i: (i, 0))
    cols = pl.BlockSpec((kv * n, ROWS), lambda i: (0, i))
    out = lambda w, t: jax.ShapeDtypeStruct((length, w), t)
    raw_w = kv * (group + 1) * n
    return pl.pallas_call(
        partial(front_kernel, kv, group),
        grid=(steps,),
        in_specs=[rows(d), whole(g1), whole(gq), whole(gk), rows(n), rows(n), whole(wp)],
        out_specs=[rows(d), rows(kv * group * n), rows(kv * n), rows(kv * n), cols, cols, rows(raw_w)],
        out_shape=[out(d, BF), out(kv * group * n, BF), out(kv * n, BF), out(kv * n, BF),
                   jax.ShapeDtypeStruct((kv * n, length), BF), jax.ShapeDtypeStruct((kv * n, length), BF),
                   out(raw_w, FP)],
        compiler_params=params(),
        name="front",
    )(x, g1, gq, gk, cosines, sines, wp)


def stacked(ref_block, h, group):
    n = LANES
    return jnp.concatenate(
        [ref_block[:, (h * group + g) * n:(h * group + g + 1) * n] for g in range(group)], axis=0)


def causal_tile(group):
    key_at = lax.broadcasted_iota(jnp.int32, (ROWS, ROWS * group), 0)
    query_at = lax.broadcasted_iota(jnp.int32, (ROWS, ROWS * group), 1) % ROWS
    return key_at <= query_at


def attend_kernel(kv, group, unit, q_ref, k_ref, vt_ref, tags_ref, bars_ref, wm_ref,
                  ctx_ref, lse_ref, part_ref, acc_ref, sum_ref):
    i = pl.program_id(0)
    n = LANES
    bars = bars_ref[...]
    bars = jnp.concatenate([bars] * group, axis=0)
    q = q_ref[...]
    wide = [jnp.concatenate([stacked(q, h, group), bars], axis=1) for h in range(kv)]
    acc_ref[...] = jnp.zeros_like(acc_ref)
    sum_ref[...] = jnp.zeros_like(sum_ref)

    def chunk(j, diagonal):
        at = pl.ds(pl.multiple_of(j * ROWS, ROWS), ROWS)
        tags = tags_ref[at, :]
        for h in range(kv):
            keys = jnp.concatenate([k_ref[at, h * n:(h + 1) * n], tags], axis=1)
            scores = dot(keys, wide[h], 1, 1)
            e = jnp.exp2(scores * unit)
            if diagonal:
                e = jnp.where(causal_tile(group), e, 0.0)
            sum_ref[h] += fold_rows(e)
            acc_ref[h] += dot(vt_ref[h * n:(h + 1) * n, at], e.astype(BF))

    lax.fori_loop(0, i, lambda j, c: (chunk(j, False), c)[1], 0)
    chunk(i, True)
    parts = []
    for h in range(kv):
        total = jnp.sum(sum_ref[h], axis=0, keepdims=True)
        lse_ref[0, h:h + 1, :] = jnp.log2(total)
        ctx = (acc_ref[h] / total).T
        parts += [ctx[g * ROWS:(g + 1) * ROWS] for g in range(group)]
    ctx = jnp.concatenate(parts, axis=1).astype(BF)
    ctx_ref[...] = ctx
    part_ref[...] = dot(ctx, wm_ref[...]).astype(part_ref.dtype)


def attend(q, k, vt, tags, bars, wm, kv, group, unit):
    length = q.shape[0]
    n = LANES
    d = wm.shape[1]
    steps = length // ROWS
    whole = lambda a: pl.BlockSpec(a.shape, lambda i: (0,) * a.ndim)
    rows = lambda w: pl.BlockSpec((ROWS, w), lambda i: (i, 0))
    return pl.pallas_call(
        partial(attend_kernel, kv, group, unit),
        grid=(steps,),
        in_specs=[rows(q.shape[1]), whole(k), whole(vt), whole(tags), rows(n), whole(wm)],
        out_specs=[rows(q.shape[1]), pl.BlockSpec((1, 8, ROWS * group), lambda i: (i, 0, 0)), rows(d)],
        out_shape=[jax.ShapeDtypeStruct(q.shape, BF),
                   jax.ShapeDtypeStruct((steps, 8, ROWS * group), FP),
                   jax.ShapeDtypeStruct((length, d), BF)],
        scratch_shapes=[pltpu.VMEM((kv, n, ROWS * group), FP), pltpu.VMEM((kv, 8, ROWS * group), FP)],
        compiler_params=params(),
        name="attend",
    )(q, k, vt, tags, bars, wm)


def feed_kernel(units, xn_ref, dy_ref, we_ref, ws_ref, branch_ref, dxn_ref, gex_ref, gsh_ref, a_ref, dgu_ref):
    i = pl.program_id(0)
    at = pl.ds(pl.multiple_of(i * ROWS, ROWS), ROWS)
    xn, dy = xn_ref[at, :], dy_ref[at, :]
    gu = dot(xn, we_ref[...])
    gate, up = gu[:, :units], gu[:, units:]
    sig = 1.0 / (1.0 + jnp.exp(-gate))
    silu = gate * sig
    a = (silu * up).astype(BF)
    a_ref[at, :] = a
    branch_ref[...] = dot(a, ws_ref[...]).astype(branch_ref.dtype)
    da = dot(dy, ws_ref[...], 1, 1)
    dgu = jnp.concatenate([da * up * (sig * (1.0 + gate * (1.0 - sig))), da * silu], axis=1).astype(BF)
    dgu_ref[at, :] = dgu
    dxn_ref[...] = dot(dgu, we_ref[...], 1, 1).astype(dxn_ref.dtype)

    @pl.when(i == pl.num_programs(0) - 1)
    def _():
        tile = 256

        def shrink_tile(t, c):
            cut = pl.ds(pl.multiple_of(t * tile, tile), tile)
            gsh_ref[:, cut] = dot(a_ref[...], dy_ref[:, cut], 0, 0).astype(gsh_ref.dtype)
            return c

        def expand_tile(t, c):
            cut = pl.ds(pl.multiple_of(t * tile, tile), tile)
            gex_ref[:, cut] = dot(xn_ref[...], dgu_ref[:, cut], 0, 0).astype(gex_ref.dtype)
            return c

        lax.fori_loop(0, gsh_ref.shape[1] // tile, shrink_tile, 0)
        lax.fori_loop(0, gex_ref.shape[1] // tile, expand_tile, 0)


def feed(xn, dy, we, ws, grad_type=FP):
    length, d = xn.shape
    units = ws.shape[0]
    whole = lambda s: pl.BlockSpec(s, lambda i: (0,) * len(s))
    rows = lambda w: pl.BlockSpec((ROWS, w), lambda i: (i, 0))
    return pl.pallas_call(
        partial(feed_kernel, units),
        grid=(length // ROWS,),
        in_specs=[whole(xn.shape), whole(dy.shape), whole(we.shape), whole(ws.shape)],
        out_specs=[rows(d), rows(d), whole(we.shape), whole(ws.shape)],
        out_shape=[jax.ShapeDtypeStruct((length, d), BF), jax.ShapeDtypeStruct((length, d), BF),
                   jax.ShapeDtypeStruct(we.shape, grad_type), jax.ShapeDtypeStruct(ws.shape, grad_type)],
        scratch_shapes=[pltpu.VMEM((length, units), BF), pltpu.VMEM((length, 2 * units), BF)],
        compiler_params=params(),
        name="feed",
    )(xn, dy, we, ws)


def back_kernel(kv, group, unit, scale, steps, q_ref, k_ref, v_ref, kt_ref, tags_ref, bars_ref, lse_ref, ctx_ref,
                dh_ref, wm_ref, wp_ref, raw_ref, cos_ref, sin_ref, gq_ref, gk_ref, xn_ref,
                dxn_ref, gm_ref, gp_ref, gains_ref, dk_ref, dv_ref, dq_ref, dqkv_ref):
    i = steps - 1 - pl.program_id(0)
    n = LANES
    here = pl.ds(pl.multiple_of(i * ROWS, ROWS), ROWS)

    @pl.when(pl.program_id(0) == 0)
    def _():
        dk_ref[...] = jnp.zeros_like(dk_ref)
        dv_ref[...] = jnp.zeros_like(dv_ref)
        gains_ref[...] = jnp.zeros_like(gains_ref)

    dctx = dot(dh_ref[here, :], wm_ref[...], 1, 1).astype(BF)
    ctx, q = ctx_ref[here, :], q_ref[...]
    bars = jnp.concatenate([bars_ref[...]] * group, axis=0)
    wide, queries, grads, centres, lses = [], [], [], [], []
    for h in range(kv):
        queries.append(stacked(q, h, group))
        wide.append(jnp.concatenate([queries[h], bars], axis=1))
        grads.append(stacked(dctx, h, group))
        both = grads[h].astype(FP) * stacked(ctx, h, group).astype(FP)
        centres.append(jnp.sum(both.T, axis=0, keepdims=True))
        lses.append(lse_ref[0, h:h + 1, :])
    dq_ref[...] = jnp.zeros_like(dq_ref)

    def chunk(j, diagonal):
        at = pl.ds(pl.multiple_of(j * ROWS, ROWS), ROWS)
        tags = tags_ref[at, :]
        for h in range(kv):
            cut = slice(h * n, (h + 1) * n)
            keys = jnp.concatenate([k_ref[at, cut], tags], axis=1)
            p = jnp.exp2(dot(keys, wide[h], 1, 1) * unit - lses[h])
            if diagonal:
                p = jnp.where(causal_tile(group), p, 0.0)
            dp = dot(v_ref[at, cut], grads[h], 1, 1)
            ds = (p * (dp - centres[h])).astype(BF)
            dv_ref[at, cut] += dot(p.astype(BF), grads[h])
            dk_ref[at, cut] += dot(ds, queries[h])
            dq_ref[h] += dot(kt_ref[cut, at], ds)

    lax.fori_loop(0, i, lambda j, c: (chunk(j, False), c)[1], 0)
    chunk(i, True)

    cosines, sines = cos_ref[...], sin_ref[...]
    pieces = []
    for h in range(kv):
        dq = dq_ref[h].T
        for c in range(group + 1):
            if c < group:
                d, gain, row = dq[c * ROWS:(c + 1) * ROWS] * scale, gq_ref[...], 0
            else:
                d, gain, row = dk_ref[here, h * n:(h + 1) * n] * scale, gk_ref[...], 1
            d = d * cosines - pltpu.roll(d, n // 2, 1) * sines
            at = (h * (group + 1) + c) * n
            piece, gain_grad = rms_pull(raw_ref[:, at:at + n], gain, d)
            gains_ref[row] += fold_rows(gain_grad)
            pieces.append(piece)
        pieces.append(dv_ref[here, h * n:(h + 1) * n])
    dqkv = jnp.concatenate(pieces, axis=1).astype(BF)
    dqkv_ref[here, :] = dqkv
    dxn_ref[...] = dot(dqkv, wp_ref[...], 1, 1).astype(dxn_ref.dtype)

    @pl.when(i == 0)
    def _():
        tile = 256

        def project_tile(t, c):
            cut = pl.ds(pl.multiple_of(t * tile, tile), tile)
            gp_ref[:, cut] = dot(xn_ref[...], dqkv_ref[:, cut], 0, 0).astype(gp_ref.dtype)
            return c

        def merge_tile(t, c):
            cut = pl.ds(pl.multiple_of(t * tile, tile), tile)
            gm_ref[:, cut] = dot(ctx_ref[...], dh_ref[:, cut], 0, 0).astype(gm_ref.dtype)
            return c

        lax.fori_loop(0, gm_ref.shape[1] // tile, merge_tile, 0)
        lax.fori_loop(0, gp_ref.shape[1] // tile, project_tile, 0)


def back(q, k, v, kt, tags, bars, lse, ctx, dh, wm, wp, raw, cosines, sines, gq, gk, xn, kv, group, unit, scale,
         grad_type=FP):
    length = q.shape[0]
    n = LANES
    d = wm.shape[1]
    steps = length // ROWS
    whole = lambda a: pl.BlockSpec(a.shape, lambda i: (0,) * a.ndim)
    rows = lambda w: pl.BlockSpec((ROWS, w), lambda i: (steps - 1 - i, 0))
    return pl.pallas_call(
        partial(back_kernel, kv, group, unit, scale, steps),
        grid=(steps,),
        in_specs=[rows(q.shape[1]), whole(k), whole(v), whole(kt), whole(tags), rows(n),
                  pl.BlockSpec((1, 8, ROWS * group), lambda i: (steps - 1 - i, 0, 0)), whole(ctx), whole(dh),
                  whole(wm), whole(wp), rows(raw.shape[1]), rows(n), rows(n), whole(gq), whole(gk), whole(xn)],
        out_specs=[rows(d), whole(wm), whole(wp), pl.BlockSpec((2, 8, n), lambda i: (0, 0, 0))],
        out_shape=[jax.ShapeDtypeStruct((length, d), BF), jax.ShapeDtypeStruct(wm.shape, grad_type),
                   jax.ShapeDtypeStruct(wp.shape, grad_type), jax.ShapeDtypeStruct((2, 8, n), FP)],
        scratch_shapes=[pltpu.VMEM((length, kv * n), FP), pltpu.VMEM((length, kv * n), FP),
                        pltpu.VMEM((kv, n, ROWS * group), FP), pltpu.VMEM((length, wp.shape[1]), BF)],
        compiler_params=params(),
        name="back",
    )(q, k, v, kt, tags, bars, lse, ctx, dh, wm, wp, raw, cosines, sines, gq, gk, xn)


def adamw_step(weight, moment_one, moment_two, gradient, step_rate, decay):
    mean_next = BETA_ONE * moment_one + (1.0 - BETA_ONE) * gradient
    square_next = BETA_TWO * moment_two + (1.0 - BETA_TWO) * gradient * gradient
    mean_hat = mean_next / (1.0 - BETA_ONE**STEP)
    square_hat = square_next / (1.0 - BETA_TWO**STEP)
    weight_next = weight - step_rate * (mean_hat / (jnp.sqrt(square_hat) + EPS_ADAM) + decay * weight)
    return weight_next, mean_next, square_next


def tree_tables(segments, parent_row):
    count = parent_row.shape[0]
    length = segments.shape[0]
    labels = jnp.arange(count, dtype=jnp.int32)
    onehot = segments[:, None] == labels[None, :]
    sizes = jnp.sum(onehot.astype(FP), axis=0)
    starts = jnp.cumsum(sizes) - sizes
    reach = (labels[:, None] == labels[None, :]) | (parent_row[:, None] == labels[None, :]) | (labels[None, :] == 0)
    proper = reach & (labels[:, None] != labels[None, :])
    offsets = jnp.sum(jnp.where(proper, sizes[None, :], 0.0), axis=1)
    position = jnp.arange(length).astype(FP) + jnp.sum(jnp.where(onehot, (offsets - starts)[None, :], 0.0), axis=1)
    parent = jnp.sum(jnp.where(onehot, parent_row[None, :], 0), axis=1)
    lanes = jnp.arange(LANES, dtype=jnp.int32)
    tags = (segments[:, None] == lanes[None, :]).astype(BF)
    seen = (lanes[None, :] == segments[:, None]) | (lanes[None, :] == parent[:, None]) | (lanes[None, :] == 0)
    bars = jnp.where(seen | (lanes[None, :] >= count), 0.0, BLOCKED).astype(BF)
    half = lanes % (LANES // 2)
    frequency = THETA ** (-half.astype(FP) * 2.0 / LANES)
    angles = position[:, None] * frequency[None, :]
    sines = jnp.where(lanes[None, :] < LANES // 2, -jnp.sin(angles), jnp.sin(angles))
    return tags, bars, jnp.cos(angles), sines


def shards(
    tokens, cotangent, parents, token_segment, tree_id,
    projection_weight, projection_first_moment, projection_second_moment,
    merge_master, merge_mean, merge_square,
    expand_master, expand_mean, expand_square,
    shrink_master, shrink_mean, shrink_square,
    gain_master, gain_mean, gain_square,
):
    parts = lax.axis_size("tensor")
    part = lax.axis_index("tensor")
    x = tokens[0]
    dy = cotangent[0]
    length, d = x.shape
    share = length // parts
    first = part * share
    d_own, kv, per, n = projection_weight.shape
    group = per - 2
    units = expand_master.shape[2]
    scale = n ** (-0.5)
    unit = scale * math.log2(math.e)

    wp = lax.all_gather(projection_weight.astype(BF).reshape(d_own, kv * per * n), "dp", axis=0, tiled=True)
    wm = lax.all_gather(merge_master.astype(BF), "dp", axis=1, tiled=True)
    we = lax.all_gather(expand_master.astype(BF).reshape(expand_master.shape[0], 2 * units), "dp", axis=0, tiled=True)
    ws = lax.all_gather(shrink_master.astype(BF), "dp", axis=1, tiled=True)

    chosen = (jnp.arange(parents.shape[0], dtype=jnp.int32) == tree_id[0]).astype(jnp.int32)
    parent_row = jnp.sum(parents * chosen[:, None], axis=0)
    tags, bars, cosines, sines = tree_tables(token_segment[0], parent_row)
    g1, g2 = gain_master[None, :d], gain_master[None, d:2 * d]
    gq, gk = gain_master[None, 2 * d:2 * d + n], gain_master[None, 2 * d + n:]

    xn1, q, k, v, kt, vt, raw = front(x, g1, gq, gk, cosines, sines, wp, kv, group)
    ctx, lse, partial_h = attend(q, k, vt, tags, bars, wm, kv, group, unit)

    own = lambda a: lax.dynamic_slice_in_dim(a, first, share, 0)
    attended = lax.psum_scatter(partial_h, "tensor", scatter_dimension=0, tiled=True).astype(FP)
    hidden = own(x).astype(FP) + attended
    xn2 = lax.all_gather((hidden * inverse_rms(hidden) * g2).astype(BF), "tensor", axis=0, tiled=True)
    branch, dxn2, expand_grad, shrink_grad = feed(xn2, dy, we, ws)
    branch = lax.psum_scatter(branch, "tensor", scatter_dimension=0, tiled=True).astype(FP)
    output = (hidden + branch).astype(BF)[None]
    dxn2 = lax.psum_scatter(dxn2, "tensor", scatter_dimension=0, tiled=True).astype(FP)
    pulled, dg2 = rms_pull(hidden, g2, dxn2)
    dh = own(dy).astype(FP) + pulled
    dhb = lax.all_gather(dh.astype(BF), "tensor", axis=0, tiled=True)
    dxn1, merge_grad, project_grad, head_gains = back(
        q, k, v, kt, tags, bars, lse, ctx, dhb, wm, wp, raw, cosines, sines, gq, gk, xn1, kv, group, unit, scale)
    dxn1 = lax.psum_scatter(dxn1, "tensor", scatter_dimension=0, tiled=True).astype(FP)
    pulled, dg1 = rms_pull(own(x).astype(FP), g1, dxn1)
    input_grad = (dh + pulled).astype(BF)[None]
    gain_grad = lax.psum(
        jnp.concatenate([jnp.sum(dg1, axis=0), jnp.sum(dg2, axis=0),
                         jnp.sum(head_gains, axis=1).reshape(2 * n)]), ("dp", "tensor"))
    project_sum = lax.psum_scatter(project_grad.astype(BF), "dp", scatter_dimension=0, tiled=True)
    merge_sum = lax.psum_scatter(merge_grad.astype(BF), "dp", scatter_dimension=1, tiled=True)
    expand_sum = lax.psum_scatter(expand_grad.astype(BF), "dp", scatter_dimension=0, tiled=True)
    shrink_sum = lax.psum_scatter(shrink_grad.astype(BF), "dp", scatter_dimension=1, tiled=True)

    outs = [output, input_grad]
    for weight, mean, square, grad, rate in (
        (projection_weight, projection_first_moment, projection_second_moment, project_sum, RATE_PROJECT),
        (merge_master, merge_mean, merge_square, merge_sum, RATE_MERGE),
        (expand_master, expand_mean, expand_square, expand_sum, RATE_EXPAND),
        (shrink_master, shrink_mean, shrink_square, shrink_sum, RATE_SHRINK),
    ):
        grad = grad.astype(FP).reshape(weight.shape)
        after, mean_next, square_next = adamw_step(weight, mean, square, grad, rate, DECAY)
        outs += [after, mean_next, square_next, after.astype(BF)]
    gain_next, gain_mean_next, gain_square_next = adamw_step(
        gain_master, gain_mean, gain_square, gain_grad, RATE_GAIN, 0.0)
    return (*outs, gain_mean_next, gain_square_next, gain_next)


def solution(mesh):
    tokens = P("dp", None, None)
    project = P("dp", "tensor", None, None)
    columns = P("tensor", "dp")
    expand = P("dp", None, "tensor")
    shared = P("dp", "tensor", None)
    return jax.shard_map(
        shards,
        mesh=mesh,
        in_specs=(tokens, tokens, P(), P("dp", None), P("dp"), *[project] * 3, *[columns] * 3, *[expand] * 3,
                  *[columns] * 3, P(), P(), P()),
        out_specs=(shared, shared, *[project] * 4, *[columns] * 4, *[expand] * 4, *[columns] * 4, P(), P(), P()),
        check_vma=False,
    )
```

```python
import math
from functools import partial

import jax
import jax.numpy as jnp
from jax import lax
from jax.experimental import pallas as pl
from jax.experimental.pallas import tpu as pltpu
from jax.sharding import PartitionSpec as P

STEP = 5
EPS_NORM = 1e-06
THETA = 1000000.0
BETA_ONE = 0.5
BETA_TWO = 0.5
EPS_ADAM = 1e-08
DECAY = 0.1
RATE_PROJECT = 0.05
RATE_MERGE = 0.3
RATE_EXPAND = 0.05
RATE_SHRINK = 0.03
RATE_GAIN = 0.3

BF = jnp.bfloat16
FP = jnp.float32
ROWS = 256
LANES = 128
SUB = 128
MESH = pl.DeviceIdType.MESH
BLOCKED = -1e30
VMEM_LIMIT = 60 * 2**20


def params(**more):
    return pltpu.CompilerParams(vmem_limit_bytes=VMEM_LIMIT, **more)


def dot(a, b, ca=1, cb=0):
    return lax.dot_general(a, b, (((ca,), (cb,)), ((), ())), preferred_element_type=FP)


def inverse_rms(values):
    return lax.rsqrt(jnp.mean(values * values, axis=-1, keepdims=True) + EPS_NORM)


def rms_pull(values, scales, grad):
    r = inverse_rms(values)
    scaled = grad * scales
    mean = jnp.mean(values * scaled, axis=-1, keepdims=True)
    return r * scaled - values * (r * r * r * mean), grad * values * r


def fold_rows(values):
    n, w = values.shape
    return jnp.sum(values.reshape(n // 8, 8, w), axis=0)


class Place:
    def __init__(self, line):
        self.line = line
        self.dp, self.t = lax.axis_index("dp"), lax.axis_index("tensor")
        self.z, self.y = self.dp // 2, self.dp % 2
        self.x, self.c = self.t // 2, self.t % 2
        self.has_up, self.has_down = self.z < line - 1, self.z > 0
        self.up, self.down = (self.dp + 2, self.t), (self.dp - 2, self.t)
        self.across = (self.dp + 1 - 2 * self.y, self.t)
        self.sibling = (self.dp, self.t + 1 - 2 * self.c)
        self.chip = (self.dp, (1 - self.x) * 2 + self.c)

    def greet(self, tensor, line):
        barrier = pltpu.get_barrier_semaphore()

        def signal(device):
            pl.semaphore_signal(barrier, inc=1, device_id=device, device_id_type=MESH)

        if tensor:
            signal(self.sibling)
            signal(self.chip)
        if line:
            signal(self.across)
            pl.when(self.has_up)(lambda: signal(self.up))
            pl.when(self.has_down)(lambda: signal(self.down))
        peers = (2 if tensor else 0) + (1 if line else 0)
        if line:
            peers = peers + jnp.where(self.has_up, 1, 0) + jnp.where(self.has_down, 1, 0)
        pl.semaphore_wait(barrier, peers)


def send(src, dst, sent, arrived, device):
    return pltpu.make_async_remote_copy(
        src_ref=src, dst_ref=dst, send_sem=sent, recv_sem=arrived, device_id=device, device_id_type=MESH)


def row_cut(size):
    return lambda j: (pl.ds(pl.multiple_of(j * size, size), size), slice(None))


def column_cut(size):
    return lambda j: (slice(None), pl.ds(pl.multiple_of(j * size, size), size))


class Gather:
    def __init__(self, place, own, full, cut, sems, local):
        self.place, self.own, self.full, self.cut, self.sems, self.local = place, own, full, cut, sems, local

    def copy(self, kind, src, j):
        p = self.place
        device = (p.up, p.down, p.across)[kind]
        return send(src, self.full.at[self.cut(j)], self.sems.at[kind, j], self.sems.at[3, j], device)

    def kept(self):
        return pltpu.make_async_copy(self.own, self.full.at[self.cut(self.place.dp)], self.local)

    def start(self):
        p = self.place
        self.copy(2, self.own, p.dp).start()
        pl.when(p.has_up)(lambda: self.copy(0, self.own, p.dp).start())
        pl.when(p.has_down)(lambda: self.copy(1, self.own, p.dp).start())
        self.kept().start()

    def arrivals(self, k):
        p = self.place
        return ((0, p.z >= k, (p.z - k) * 2 + p.y, p.has_up), (1, p.z + k < p.line, (p.z + k) * 2 + p.y, p.has_down))

    def hop(self, k):
        for kind, here, j, further in self.arrivals(k):
            @pl.when(here)
            def _(kind=kind, j=j, further=further):
                piece = self.full.at[self.cut(j)]
                self.copy(kind, piece, j).wait_recv()
                pl.when(further)(lambda: self.copy(kind, piece, j).start())
                self.copy(2, piece, j).start()

    def finish(self):
        p = self.place
        self.kept().wait()
        for zz in range(p.line):
            j = zz * 2 + 1 - p.y
            self.copy(2, self.full.at[self.cut(j)], j).wait_recv()

    def drain(self):
        p = self.place
        self.copy(2, self.own, p.dp).wait_send()
        pl.when(p.has_up)(lambda: self.copy(0, self.own, p.dp).wait_send())
        pl.when(p.has_down)(lambda: self.copy(1, self.own, p.dp).wait_send())
        for k in range(1, p.line):
            for kind, here, j, further in self.arrivals(k):
                @pl.when(here)
                def _(kind=kind, j=j, further=further):
                    piece = self.full.at[self.cut(j)]
                    pl.when(further)(lambda: self.copy(kind, piece, j).wait_send())
                    self.copy(2, piece, j).wait_send()


class Reduce:
    def __init__(self, place, grad, cut, across, lined, sems):
        self.place, self.grad, self.cut, self.sems = place, grad, cut, sems
        self.across, self.lined = across, lined

    def cross(self, zz):
        p = self.place
        return send(self.grad.at[self.cut(zz * 2 + 1 - p.y)], self.across.at[zz],
                    self.sems.at[0, zz], self.sems.at[1, zz], p.across)

    def climb(self, t):
        return send(self.across.at[t], self.lined.at[t + 1], self.sems.at[2, t], self.sems.at[3, t], self.place.up)

    def sink(self, t):
        return send(self.across.at[t], self.lined.at[t], self.sems.at[4, t], self.sems.at[5, t], self.place.down)

    def mine(self, zz):
        return self.grad[self.cut(zz * 2 + self.place.y)].astype(FP)

    def start(self):
        p = self.place
        for h in range(1, p.line):
            pl.when(p.z < h)(lambda h=h: self.cross(p.z + p.line - h).start())
            pl.when(p.z >= p.line - h)(lambda h=h: self.cross(p.z - p.line + h).start())
        self.cross(p.z).start()

    def hop(self, h):
        p = self.place

        def pass_on(t, coming, more, slot):
            self.cross(t).wait_recv()

            @pl.when(jnp.logical_not(more))
            def _():
                self.across[t] = (self.mine(t) + self.across[t].astype(FP)).astype(BF)

            @pl.when(more)
            def _():
                coming(t).wait_recv()
                self.across[t] = (self.mine(t) + self.across[t].astype(FP) + self.lined[slot].astype(FP)).astype(BF)

            coming(t).start()

        pl.when(p.z < h)(lambda: pass_on(p.z + p.line - h, self.climb, p.has_down, p.z + p.line - h + 1))
        pl.when(p.z >= p.line - h)(lambda: pass_on(p.z - p.line + h, self.sink, p.has_up, p.z - p.line + h))

    def finish(self, out):
        p = self.place
        self.cross(p.z).wait_recv()
        out[...] = self.mine(p.z) + self.across[p.z].astype(FP)

        @pl.when(p.has_down)
        def _():
            self.climb(p.z).wait_recv()
            out[...] += self.lined[p.z + 1].astype(FP)

        @pl.when(p.has_up)
        def _():
            self.sink(p.z).wait_recv()
            out[...] += self.lined[p.z].astype(FP)

    def drain(self):
        p = self.place
        for zz in range(p.line):
            self.cross(zz).wait_send()
            pl.when(zz > p.z)(lambda zz=zz: self.climb(zz).wait_send())
            pl.when(zz < p.z)(lambda zz=zz: self.sink(zz).wait_send())


def reduce_scratch(line, shape):
    return [pltpu.VMEM((line, *shape), BF), pltpu.VMEM((line + 1, *shape), BF), pltpu.SemaphoreType.DMA((6, line))]


class Exchange:
    def __init__(self, place, per, held, near, far, total, sems):
        self.place, self.per, self.held, self.near, self.far = place, per, held, near, far
        self.total, self.sems = total, sems

    def owner(self, s):
        t = s // self.per
        return t // 2, t % 2

    def to_sibling(self, s):
        slot = (s // (2 * self.per)) * self.per + s % self.per
        return send(self.held.at[s], self.near.at[slot], self.sems.at[0, s], self.sems.at[1, s], self.place.sibling)

    def to_chip(self, s):
        return send(self.held.at[s], self.far.at[s % self.per], self.sems.at[2, s], self.sems.at[3, s],
                    self.place.chip)

    def out(self, s):
        pl.when(self.place.c != self.owner(s)[1])(lambda: self.to_sibling(s).start())

    def add(self, s):
        p = self.place
        ox, oc = self.owner(s)
        slot = (s // (2 * self.per)) * self.per + s % self.per

        @pl.when(p.c == oc)
        def _():
            self.to_sibling(s).wait_recv()

            @pl.when(p.x != ox)
            def _():
                self.held[s] = (self.held[s].astype(FP) + self.near[slot].astype(FP)).astype(BF)
                self.to_chip(s).start()

            @pl.when(p.x == ox)
            def _():
                self.total[s % self.per] = self.held[s].astype(FP) + self.near[slot].astype(FP)

    def take(self, s, use):
        p = self.place

        @pl.when(s // self.per == p.t)
        def _():
            k = s % self.per
            self.to_chip(s).wait_recv()
            use(s, k, self.total[k] + self.far[k].astype(FP))

    def drain(self):
        p = self.place

        def one(s, carry):
            ox, oc = self.owner(s)
            pl.when(p.c != oc)(lambda: self.to_sibling(s).wait_send())
            pl.when(jnp.logical_and(p.c == oc, p.x != ox))(lambda: self.to_chip(s).wait_send())
            return carry

        lax.fori_loop(0, 4 * self.per, one, 0)


class Pairs:
    def __init__(self, place, per, held, near, sems):
        self.place, self.per, self.held, self.near, self.sems = place, per, held, near, sems

    def copy(self, s):
        slot = (s // (2 * self.per)) * self.per + s % self.per
        return send(self.held.at[s], self.near.at[slot], self.sems.at[0, s], self.sems.at[1, s], self.place.sibling)

    def out(self, s):
        pl.when(self.place.c != (s // self.per) % 2)(lambda: self.copy(s).start())

    def add(self, s, use):
        t = s // self.per
        slot = (s // (2 * self.per)) * self.per + s % self.per

        @pl.when(self.place.c == t % 2)
        def _():
            self.copy(s).wait_recv()
            use(self.place.x == t // 2, s % self.per, self.held[s].astype(FP) + self.near[slot].astype(FP))

    def drain(self):
        def one(s, carry):
            pl.when(self.place.c != (s // self.per) % 2)(lambda: self.copy(s).wait_send())
            return carry

        lax.fori_loop(0, 4 * self.per, one, 0)


def exchange_scratch(per, d):
    return [pltpu.VMEM((4 * per, SUB, d), BF), pltpu.VMEM((2 * per, SUB, d), BF), pltpu.VMEM((per, SUB, d), BF), pltpu.VMEM((per, SUB, d), FP),
                   pltpu.SemaphoreType.DMA((4, 4 * per))]


class Spread:
    def __init__(self, place, per, stage, full, sems):
        self.place, self.per, self.stage, self.full, self.sems = place, per, stage, full, sems

    def copy(self, kind, src, s):
        device = (self.place.chip, self.place.sibling)[kind]
        return send(src, self.full.at[s], self.sems.at[kind, s], self.sems.at[2, s], device)

    def kept(self, s):
        return pltpu.make_async_copy(self.stage.at[s % self.per], self.full.at[s], self.sems.at[3, s])

    def send(self, s):
        for kind in (0, 1):
            self.copy(kind, self.stage.at[s % self.per], s).start()
        self.kept(s).start()

    def passes(self, s):
        t = s // self.per
        return jnp.logical_and(self.place.c == t % 2, self.place.x != t // 2)

    def pass_on(self, s):
        @pl.when(self.passes(s))
        def _():
            self.copy(1, self.full.at[s], s).wait_recv()
            self.copy(1, self.full.at[s], s).start()

    def finish(self):
        def one(s, carry):
            @pl.when(s // self.per == self.place.t)
            def _():
                self.copy(0, self.stage.at[s % self.per], s).wait_send()
                self.copy(1, self.stage.at[s % self.per], s).wait_send()
                self.kept(s).wait()

            pl.when(self.passes(s))(lambda: self.copy(1, self.full.at[s], s).wait_send())
            pl.when((s // self.per) % 2 != self.place.c)(lambda: self.copy(1, self.full.at[s], s).wait_recv())
            return carry

        lax.fori_loop(0, 4 * self.per, one, 0)


def spread_scratch(per, d):
    return [pltpu.VMEM((per, SUB, d), BF), pltpu.SemaphoreType.DMA((4, 4 * per))]


def whole(shape):
    return pl.BlockSpec(tuple(shape), lambda i: (0,) * len(shape), pipeline_mode=pl.Buffered(1))


ANYWHERE = pl.BlockSpec(memory_space=pl.ANY)
GATHER_SEMS = lambda shards: [pltpu.SemaphoreType.DMA((4, shards)), pltpu.SemaphoreType.DMA]


def front_kernel(kv, group, line, *refs):
    refs = list(refs)
    take = lambda count: [refs.pop(0) for _ in range(count)]
    x_ref, g1_ref, gq_ref, gk_ref, cos_ref, sin_ref = take(6)
    own = take(2) if line else take(1)
    xn_ref, q_ref, k_ref, v_ref, kt_ref, vt_ref, raw_ref = take(7)
    if line:
        wp_out, wm_out = take(2)
        wp_ref, p_sems, p_local, m_sems, m_local, out_sem = take(6)
    else:
        wp_ref = own[0]
    xn_full, xn_sem = take(2)
    i = pl.program_id(0)
    last = pl.num_programs(0) - 1
    if line:
        place = Place(line)
        size = own[0].shape[0]
        project = Gather(place, own[0], wp_ref, row_cut(size), p_sems, p_local)
        merge = Gather(place, own[1], wm_out, column_cut(own[1].shape[1]), m_sems, m_local)
        written = pltpu.make_async_copy(wp_ref, wp_out, out_sem)
    normed = pltpu.make_async_copy(xn_full, xn_ref, xn_sem)

    @pl.when(i == 0)
    def _():
        if line:
            place.greet(False, True)
            project.start()

        def norm(b, carry):
            at = pl.ds(pl.multiple_of(b * ROWS, ROWS), ROWS)
            x = x_ref[at, :].astype(FP)
            xn_full[at, :] = (x * inverse_rms(x) * g1_ref[...]).astype(BF)
            return carry

        lax.fori_loop(0, x_ref.shape[0] // ROWS, norm, 0)
        normed.start()
        if line:
            for k in range(1, line):
                project.hop(k)
            merge.start()
            project.finish()
            written.start()

    if line:
        for k in range(1, line):
            pl.when(i == k + 1)(lambda k=k: merge.hop(k))
    at = pl.ds(pl.multiple_of(i * ROWS, ROWS), ROWS)
    qkv = dot(xn_full[at, :], wp_ref[...])
    cosines, sines = cos_ref[...], sin_ref[...]
    n = LANES
    per = group + 2
    keys, values = [], []
    for h in range(kv):
        for c in range(group + 1):
            raw = qkv[:, (h * per + c) * n:(h * per + c + 1) * n]
            to = (h * (group + 1) + c) * n
            raw_ref[:, to:to + n] = raw
            y = raw * inverse_rms(raw) * (gq_ref[...] if c < group else gk_ref[...])
            turned = y * cosines + pltpu.roll(y, n // 2, 1) * sines
            if c < group:
                to = (h * group + c) * n
                q_ref[:, to:to + n] = turned.astype(BF)
            else:
                keys.append(turned)
        values.append(qkv[:, (h * per + group + 1) * n:(h * per + group + 2) * n])
    for h in range(kv):
        k_ref[:, h * n:(h + 1) * n] = keys[h].astype(BF)
        v_ref[:, h * n:(h + 1) * n] = values[h].astype(BF)
        kt_ref[h * n:(h + 1) * n, :] = keys[h].T.astype(BF)
        vt_ref[h * n:(h + 1) * n, :] = values[h].T.astype(BF)

    @pl.when(i == last)
    def _():
        normed.wait()
        if line:
            merge.finish()
            merge.drain()
            project.drain()
            written.wait()


def front(x, g1, gq, gk, cosines, sines, own, kv, group, line):
    length, d = x.shape
    n = LANES
    rows = lambda w: pl.BlockSpec((ROWS, w), lambda i: (i, 0))
    cols = pl.BlockSpec((kv * n, ROWS), lambda i: (0, i))
    out = lambda w, t: jax.ShapeDtypeStruct((length, w), t)
    raw_w = kv * (group + 1) * n
    shards = 2 * line
    more_specs, more_shapes, scratch = [], [], []
    own_specs = [whole(own[0].shape)]
    if line:
        wp_shape = (own[0].shape[0] * shards, own[0].shape[1])
        wm_shape = (own[1].shape[0], own[1].shape[1] * shards)
        own_specs.append(ANYWHERE)
        more_specs = [ANYWHERE, ANYWHERE]
        more_shapes = [jax.ShapeDtypeStruct(wp_shape, BF), jax.ShapeDtypeStruct(wm_shape, BF)]
        scratch = [pltpu.VMEM(wp_shape, BF), *GATHER_SEMS(shards), *GATHER_SEMS(shards), pltpu.SemaphoreType.DMA]
    return pl.pallas_call(
        partial(front_kernel, kv, group, line),
        grid=(length // ROWS,),
        in_specs=[whole(x.shape), whole(g1.shape), whole(gq.shape), whole(gk.shape), rows(n), rows(n), *own_specs],
        out_specs=[ANYWHERE, rows(kv * group * n), rows(kv * n), rows(kv * n), cols, cols, rows(raw_w), *more_specs],
        out_shape=[out(d, BF), out(kv * group * n, BF), out(kv * n, BF), out(kv * n, BF),
                   jax.ShapeDtypeStruct((kv * n, length), BF), jax.ShapeDtypeStruct((kv * n, length), BF),
                   out(raw_w, FP), *more_shapes],
        scratch_shapes=[*scratch, pltpu.VMEM((length, d), BF), pltpu.SemaphoreType.DMA],
        compiler_params=params(**({"collective_id": 0, "has_side_effects": True} if line else {})),
        name="front",
    )(x, g1, gq, gk, cosines, sines, *own)


def stacked(ref_block, h, group):
    n = LANES
    return jnp.concatenate(
        [ref_block[:, (h * group + g) * n:(h * group + g + 1) * n] for g in range(group)], axis=0)


def causal_tile(group):
    key_at = lax.broadcasted_iota(jnp.int32, (ROWS, ROWS * group), 0)
    query_at = lax.broadcasted_iota(jnp.int32, (ROWS, ROWS * group), 1) % ROWS
    return key_at <= query_at


def attend_kernel(kv, group, unit, line, per, blocks, *refs):
    refs = list(refs)
    take = lambda count: [refs.pop(0) for _ in range(count)]
    q_ref, k_ref, vt_ref, tags_ref, bars_ref, wm_ref, x_ref, g2_ref = take(8)
    own = take(2) if line else []
    ctx_ref, lse_ref, h_ref, xn_ref = take(4)
    full = take(2) if line else []
    acc_ref, sum_ref = take(2)
    held, near, far, total, e_sems, stage, s_sems = take(7)
    gathers = []
    place = Place(line)
    if line:
        cuts = (row_cut(own[0].shape[0]), column_cut(own[1].shape[1]))
        for w in range(2):
            gathers.append(Gather(place, own[w], full[w], cuts[w], *take(2)))
    i = pl.program_id(0)
    n = LANES
    exchange = Exchange(place, per, held, near, far, total, e_sems)
    spread = Spread(place, per, stage, xn_ref, s_sems)
    subs = ROWS // SUB

    @pl.when(i == 0)
    def _():
        place.greet(True, bool(line))
        for g in gathers:
            g.start()

    @pl.when(i < blocks)
    def _():
        bars = jnp.concatenate([bars_ref[...]] * group, axis=0)
        q = q_ref[...]
        wide = [jnp.concatenate([stacked(q, h, group), bars], axis=1) for h in range(kv)]
        acc_ref[...] = jnp.zeros_like(acc_ref)
        sum_ref[...] = jnp.zeros_like(sum_ref)

        def chunk(j, diagonal):
            at = pl.ds(pl.multiple_of(j * ROWS, ROWS), ROWS)
            tags = tags_ref[at, :]
            for h in range(kv):
                keys = jnp.concatenate([k_ref[at, h * n:(h + 1) * n], tags], axis=1)
                scores = dot(keys, wide[h], 1, 1)
                e = jnp.exp2(scores * unit)
                if diagonal:
                    e = jnp.where(causal_tile(group), e, 0.0)
                sum_ref[h] += fold_rows(e)
                acc_ref[h] += dot(vt_ref[h * n:(h + 1) * n, at], e.astype(BF))

        lax.fori_loop(0, i, lambda j, c: (chunk(j, False), c)[1], 0)
        chunk(i, True)
        parts = []
        for h in range(kv):
            sums = jnp.sum(sum_ref[h], axis=0, keepdims=True)
            lse_ref[0, h:h + 1, :] = jnp.log2(sums)
            ctx = (acc_ref[h] / sums).T
            parts += [ctx[g * ROWS:(g + 1) * ROWS] for g in range(group)]
        ctx = jnp.concatenate(parts, axis=1).astype(BF)
        ctx_ref[...] = ctx
        part = dot(ctx, wm_ref[...]).astype(BF)
        for u in range(subs):
            held[subs * i + u] = part[u * SUB:(u + 1) * SUB]
            exchange.out(subs * i + u)

    def own_rows(s, k, summed):
        at = pl.ds(pl.multiple_of(k * SUB, SUB), SUB)
        hidden = x_ref[at, :].astype(FP) + summed
        h_ref[at, :] = hidden
        stage[k] = (hidden * inverse_rms(hidden) * g2_ref[...]).astype(BF)
        spread.send(s)

    def stages(step):
        for behind, act in ((1, exchange.add), (2, lambda s: exchange.take(s, own_rows)), (3, spread.pass_on)):
            @pl.when(jnp.logical_and(step - behind >= 0, step - behind < blocks))
            def _(behind=behind, act=act):
                for u in range(subs):
                    act(subs * (step - behind) + u)

    stages(i)
    if line:
        for k in range(1, line):
            @pl.when(i == min(2 + 2 * k, blocks + 2))
            def _(k=k):
                for g in gathers:
                    g.hop(k)

    @pl.when(i == blocks + 2)
    def _():
        exchange.drain()
        spread.finish()
        for g in gathers:
            g.finish()
            g.drain()


def attend(q, k, vt, tags, bars, wm, x_own, g2, own, kv, group, unit, line):
    length = q.shape[0]
    n = LANES
    d = wm.shape[1]
    blocks = length // ROWS
    per = x_own.shape[0] // SUB
    rows = lambda w: pl.BlockSpec((ROWS, w), lambda i: (jnp.minimum(i, blocks - 1), 0))
    shards = 2 * line
    full = []
    if line:
        full = [jax.ShapeDtypeStruct((own[0].shape[0] * shards, own[0].shape[1]), BF),
                jax.ShapeDtypeStruct((own[1].shape[0], own[1].shape[1] * shards), BF)]
    return pl.pallas_call(
        partial(attend_kernel, kv, group, unit, line, per, blocks),
        grid=(blocks + 3,),
        in_specs=[rows(q.shape[1]), whole(k.shape), whole(vt.shape), whole(tags.shape), rows(n), whole(wm.shape),
                  whole(x_own.shape), whole(g2.shape)] + [ANYWHERE] * len(own),
        out_specs=[rows(q.shape[1]),
                   pl.BlockSpec((1, 8, ROWS * group), lambda i: (jnp.minimum(i, blocks - 1), 0, 0)),
                   whole(x_own.shape), ANYWHERE] + [ANYWHERE] * len(full),
        out_shape=[jax.ShapeDtypeStruct(q.shape, BF),
                   jax.ShapeDtypeStruct((blocks, 8, ROWS * group), FP),
                   jax.ShapeDtypeStruct(x_own.shape, FP),
                   jax.ShapeDtypeStruct((length // SUB, SUB, d), BF), *full],
        scratch_shapes=[pltpu.VMEM((kv, n, ROWS * group), FP), pltpu.VMEM((kv, 8, ROWS * group), FP),
                        *exchange_scratch(per, d), *spread_scratch(per, d)]
                       + (GATHER_SEMS(shards) * 2 if line else []),
        compiler_params=params(collective_id=1, has_side_effects=True),
        name="attend",
    )(q, k, vt, tags, bars, wm, x_own, g2, *own)


def feed_kernel(units, per, blocks, xn_ref, dy_ref, we_ref, ws_ref, h_ref, g2_ref,
                base_ref, other_ref, gex_ref, gsh_ref, dh_ref, dhb_ref, dg_ref,
                a_ref, dgu_ref, held, near, far, total, e_sems, stage, s_sems, b_held, b_near, b_sems):
    i = pl.program_id(0)
    place = Place(0)
    exchange = Exchange(place, per, held, near, far, total, e_sems)
    spread = Spread(place, per, stage, dhb_ref, s_sems)
    pairs = Pairs(place, per, b_held, b_near, b_sems)
    subs = ROWS // SUB
    tile = 256

    @pl.when(i == 0)
    def _():
        place.greet(True, False)
        dg_ref[...] = jnp.zeros_like(dg_ref)

    @pl.when(i < blocks)
    def _():
        at = pl.ds(pl.multiple_of(i * ROWS, ROWS), ROWS)
        xn, dy = xn_ref[at, :], dy_ref[at, :]
        gu = dot(xn, we_ref[...])
        gate, up = gu[:, :units], gu[:, units:]
        sig = 1.0 / (1.0 + jnp.exp(-gate))
        silu = gate * sig
        a = (silu * up).astype(BF)
        a_ref[at, :] = a
        da = dot(dy, ws_ref[...], 1, 1)
        dgu = jnp.concatenate([da * up * (sig * (1.0 + gate * (1.0 - sig))), da * silu], axis=1).astype(BF)
        dgu_ref[at, :] = dgu
        part = dot(dgu, we_ref[...], 1, 1).astype(BF)
        for u in range(subs):
            held[subs * i + u] = part[u * SUB:(u + 1) * SUB]
            exchange.out(subs * i + u)
        part = dot(a, ws_ref[...]).astype(BF)
        for u in range(subs):
            b_held[subs * i + u] = part[u * SUB:(u + 1) * SUB]
            pairs.out(subs * i + u)

    def own_rows(s, k, summed):
        at = pl.ds(pl.multiple_of(k * SUB, SUB), SUB)
        pulled, gain_grad = rms_pull(h_ref[at, :], g2_ref[...], summed)
        dh = dy_ref[pl.ds(pl.multiple_of(s * SUB, SUB), SUB), :].astype(FP) + pulled
        dh_ref[at, :] = dh
        dg_ref[...] += fold_rows(gain_grad)
        stage[k] = dh.astype(BF)
        spread.send(s)

    def chip_rows(mine, k, summed):
        at = pl.ds(pl.multiple_of(k * SUB, SUB), SUB)

        @pl.when(mine)
        def _():
            base_ref[at, :] = h_ref[at, :] + summed

        @pl.when(jnp.logical_not(mine))
        def _():
            other_ref[k] = summed.astype(BF)

    for behind, act in ((1, exchange.add), (2, lambda s: exchange.take(s, own_rows)), (3, spread.pass_on),
                        (2, lambda s: pairs.add(s, chip_rows))):
        @pl.when(jnp.logical_and(i - behind >= 0, i - behind < blocks))
        def _(behind=behind, act=act):
            for u in range(subs):
                act(subs * (i - behind) + u)

    def tiles(grad_ref, left_ref, right_ref, first, count):
        def one(t, carry):
            cut = pl.ds(pl.multiple_of(t * tile, tile), tile)
            grad_ref[:, cut] = dot(left_ref[...], right_ref[:, cut], 0, 0).astype(grad_ref.dtype)
            return carry

        lax.fori_loop(first, first + count, one, 0)

    half = gex_ref.shape[1] // tile // 2
    pl.when(i == blocks)(lambda: tiles(gsh_ref, a_ref, dy_ref, 0, gsh_ref.shape[1] // tile))
    pl.when(i == blocks + 1)(lambda: tiles(gex_ref, xn_ref, dgu_ref, 0, half))

    @pl.when(i == blocks + 2)
    def _():
        tiles(gex_ref, xn_ref, dgu_ref, half, half)
        exchange.drain()
        pairs.drain()
        spread.finish()


def feed(xn, dy, we, ws, h, g2):
    length, d = xn.shape
    units = ws.shape[0]
    blocks = length // ROWS
    per = h.shape[0] // SUB
    return pl.pallas_call(
        partial(feed_kernel, units, per, blocks),
        grid=(blocks + 3,),
        in_specs=[whole(xn.shape), whole(dy.shape), whole(we.shape), whole(ws.shape), whole(h.shape), whole(g2.shape)],
        out_specs=[whole(h.shape), whole((per, SUB, d)), whole(we.shape), whole(ws.shape), whole(h.shape), ANYWHERE,
                   whole((8, d))],
        out_shape=[jax.ShapeDtypeStruct(h.shape, FP), jax.ShapeDtypeStruct((per, SUB, d), BF),
                   jax.ShapeDtypeStruct(we.shape, BF),
                   jax.ShapeDtypeStruct(ws.shape, BF), jax.ShapeDtypeStruct(h.shape, FP),
                   jax.ShapeDtypeStruct((length // SUB, SUB, d), BF), jax.ShapeDtypeStruct((8, d), FP)],
        scratch_shapes=[pltpu.VMEM((length, units), BF), pltpu.VMEM((length, 2 * units), BF),
                        *exchange_scratch(per, d), *spread_scratch(per, d), pltpu.VMEM((4 * per, SUB, d), BF),
                        pltpu.VMEM((2 * per, SUB, d), BF), pltpu.SemaphoreType.DMA((2, 4 * per))],
        compiler_params=params(collective_id=2, has_side_effects=True),
        name="feed",
    )(xn, dy, we, ws, h, g2)


def back_kernel(kv, group, unit, scale, blocks, per, line, *refs):
    refs = list(refs)
    take = lambda count: [refs.pop(0) for _ in range(count)]
    q_ref, k_ref, v_ref, kt_ref, tags_ref, bars_ref, lse_ref, ctx_ref, dh_ref, wm_ref, wp_ref = take(11)
    raw_ref, cos_ref, sin_ref, gq_ref, gk_ref, xn_ref = take(6)
    x_ref, base_ref, dh_own, g1_ref, other_ref = take(5)
    grads = take(2) if line else []
    in_ref, out_ref, gp_ref, gains_ref, dg_ref = take(5)
    sums = take(3) if line else take(1)
    dk_ref, dv_ref, dq_ref, dqkv_ref = take(4)
    exchange_refs = take(5)
    b_far, b_sems = take(2)
    place = Place(line)
    i = pl.program_id(0)
    b = blocks - 1 - i
    n = LANES
    exchange = Exchange(place, per, *exchange_refs)
    subs = ROWS // SUB
    tile = 256
    reduces = []
    if line:
        gm_ref = take(1)[0]
        shards = 2 * line
        for grad, cut in ((grads[0], row_cut(grads[0].shape[0] // shards)),
                          (grads[1], column_cut(grads[1].shape[1] // shards)),
                          (gm_ref, column_cut(gm_ref.shape[1] // shards))):
            reduces.append(Reduce(place, grad, cut, *take(3)))
    else:
        gm_ref = sums[0]

    def tiles(grad_ref, left_ref, right_ref):
        def one(t, carry):
            cut = pl.ds(pl.multiple_of(t * tile, tile), tile)
            grad_ref[:, cut] = dot(left_ref[...], right_ref[:, cut], 0, 0).astype(grad_ref.dtype)
            return carry

        lax.fori_loop(0, grad_ref.shape[1] // tile, one, 0)

    def branch(k):
        return send(other_ref.at[k], b_far.at[k], b_sems.at[0, k], b_sems.at[1, k], place.chip)

    @pl.when(i == 0)
    def _():
        place.greet(True, bool(line))
        for r in reduces[:2]:
            r.start()

        for k in range(per):
            branch(k).start()
        dk_ref[...] = jnp.zeros_like(dk_ref)
        dv_ref[...] = jnp.zeros_like(dv_ref)
        gains_ref[...] = jnp.zeros_like(gains_ref)
        dg_ref[...] = jnp.zeros_like(dg_ref)
        tiles(gm_ref, ctx_ref, dh_ref)
        for r in reduces[2:]:
            r.start()

    @pl.when(i < blocks)
    def _():
        here = pl.ds(pl.multiple_of(b * ROWS, ROWS), ROWS)
        dctx = dot(dh_ref[here, :], wm_ref[...], 1, 1).astype(BF)
        ctx, q = ctx_ref[here, :], q_ref[...]
        bars = jnp.concatenate([bars_ref[...]] * group, axis=0)
        wide, queries, outward, centres, lses = [], [], [], [], []
        for h in range(kv):
            queries.append(stacked(q, h, group))
            wide.append(jnp.concatenate([queries[h], bars], axis=1))
            outward.append(stacked(dctx, h, group))
            both = outward[h].astype(FP) * stacked(ctx, h, group).astype(FP)
            centres.append(jnp.sum(both.T, axis=0, keepdims=True))
            lses.append(lse_ref[0, h:h + 1, :])
        dq_ref[...] = jnp.zeros_like(dq_ref)

        def chunk(j, diagonal):
            at = pl.ds(pl.multiple_of(j * ROWS, ROWS), ROWS)
            tags = tags_ref[at, :]
            for h in range(kv):
                cut = slice(h * n, (h + 1) * n)
                keys = jnp.concatenate([k_ref[at, cut], tags], axis=1)
                p = jnp.exp2(dot(keys, wide[h], 1, 1) * unit - lses[h])
                if diagonal:
                    p = jnp.where(causal_tile(group), p, 0.0)
                dp = dot(v_ref[at, cut], outward[h], 1, 1)
                ds = (p * (dp - centres[h])).astype(BF)
                dv_ref[at, cut] += dot(p.astype(BF), outward[h])
                dk_ref[at, cut] += dot(ds, queries[h])
                dq_ref[h] += dot(kt_ref[cut, at], ds)

        lax.fori_loop(0, b, lambda j, c: (chunk(j, False), c)[1], 0)
        chunk(b, True)

        cosines, sines = cos_ref[...], sin_ref[...]
        pieces = []
        for h in range(kv):
            dq = dq_ref[h].T
            for c in range(group + 1):
                if c < group:
                    d, gain, row = dq[c * ROWS:(c + 1) * ROWS] * scale, gq_ref[...], 0
                else:
                    d, gain, row = dk_ref[here, h * n:(h + 1) * n] * scale, gk_ref[...], 1
                d = d * cosines - pltpu.roll(d, n // 2, 1) * sines
                at = (h * (group + 1) + c) * n
                piece, gain_grad = rms_pull(raw_ref[:, at:at + n], gain, d)
                gains_ref[row] += fold_rows(gain_grad)
                pieces.append(piece)
            pieces.append(dv_ref[here, h * n:(h + 1) * n])
        dqkv = jnp.concatenate(pieces, axis=1).astype(BF)
        dqkv_ref[here, :] = dqkv
        part = dot(dqkv, wp_ref[...], 1, 1).astype(BF)
        for u in range(subs):
            exchange.held[subs * b + u] = part[u * SUB:(u + 1) * SUB]
            exchange.out(subs * b + u)

    def input_rows(s, k, summed):
        at = pl.ds(pl.multiple_of(k * SUB, SUB), SUB)
        pulled, gain_grad = rms_pull(x_ref[at, :].astype(FP), g1_ref[...], summed)
        in_ref[at, :] = (dh_own[at, :] + pulled).astype(BF)
        dg_ref[...] += fold_rows(gain_grad)

    for behind, act in ((1, exchange.add), (2, lambda s: exchange.take(s, input_rows))):
        @pl.when(jnp.logical_and(i - behind >= 0, i - behind < blocks))
        def _(behind=behind, act=act):
            for u in range(subs):
                act(subs * (b + behind) + u)

    @pl.when(i == 3)
    def _():
        for k in range(per):
            branch(k).wait()
            at = slice(k * SUB, (k + 1) * SUB)
            out_ref[at, :] = (base_ref[at, :] + b_far[k].astype(FP)).astype(BF)

    if line:
        for k in range(1, line):
            @pl.when(i == min((1, 2, 4)[k - 1] if line == 4 else k, blocks))
            def _(k=k):
                for r in reduces:
                    r.hop(k)
    pl.when(i == blocks)(lambda: tiles(gp_ref, xn_ref, dqkv_ref))

    @pl.when(i == blocks + 1)
    def _():
        exchange.drain()
        for r, out in zip(reduces, sums):
            r.finish(out)
            r.drain()


def back(q, k, v, kt, tags, bars, lse, ctx, dh, wm, wp, raw, cosines, sines, gq, gk, xn,
         x_own, base, dh_own, g1, other, grads, kv, group, unit, scale, line):
    length = q.shape[0]
    n = LANES
    d = wm.shape[1]
    blocks = length // ROWS
    per = x_own.shape[0] // SUB
    block_of = lambda i: jnp.maximum(blocks - 1 - i, 0)
    rows = lambda w: pl.BlockSpec((ROWS, w), lambda i: (block_of(i), 0))
    shards = 2 * line
    scratch = [pltpu.VMEM((length, kv * n), FP), pltpu.VMEM((length, kv * n), FP),
               pltpu.VMEM((kv, n, ROWS * group), FP), pltpu.VMEM((length, wp.shape[1]), BF),
               *exchange_scratch(per, d), pltpu.VMEM((per, SUB, d), BF), pltpu.SemaphoreType.DMA((2, per))]
    if line:
        own = [(grads[0].shape[0] // shards, grads[0].shape[1]), (grads[1].shape[0], grads[1].shape[1] // shards),
               (wm.shape[0], wm.shape[1] // shards)]
        sums = [jax.ShapeDtypeStruct(s, FP) for s in own]
        scratch += [pltpu.VMEM(wm.shape, BF)]
        for s in own:
            scratch += reduce_scratch(line, s)
    else:
        sums = [jax.ShapeDtypeStruct(wm.shape, BF)]
    args = [q, k, v, kt, tags, bars, lse, ctx, dh, wm, wp, raw, cosines, sines, gq, gk, xn,
            x_own, base, dh_own, g1, other, *grads]
    specs = [whole(a.shape) for a in args]
    specs[21] = ANYWHERE
    for at in (0, 5, 11, 12, 13):
        specs[at] = rows(args[at].shape[1])
    specs[6] = pl.BlockSpec((1, 8, ROWS * group), lambda i: (block_of(i), 0, 0))
    return pl.pallas_call(
        partial(back_kernel, kv, group, unit, scale, blocks, per, line),
        grid=(blocks + 2,),
        in_specs=specs,
        out_specs=[whole(x_own.shape), whole(x_own.shape), whole(wp.shape), whole((2, 8, n)),
                   whole((8, d))] + [whole(s.shape) for s in sums],
        out_shape=[jax.ShapeDtypeStruct(x_own.shape, BF), jax.ShapeDtypeStruct(x_own.shape, BF),
                   jax.ShapeDtypeStruct(wp.shape, BF), jax.ShapeDtypeStruct((2, 8, n), FP),
                   jax.ShapeDtypeStruct((8, d), FP), *sums],
        scratch_shapes=scratch,
        compiler_params=params(collective_id=3, has_side_effects=True),
        name="back",
    )(*args)


def last_kernel(line, gp_ref, gains_ref, sum_ref, all_ref, *refs):
    across, passing, sems, near, far, over, lined, g_sems = refs
    place = Place(line)
    barrier = pltpu.get_barrier_semaphore()
    others = []
    for step in range(1, line):
        z = (place.z + step) % line
        others.append((z, (z * 2 + place.y, place.t)))
    partners = [place.sibling, place.chip, place.across] + [device for _, device in others]
    for device in partners:
        pl.semaphore_signal(barrier, inc=1, device_id=device, device_id_type=MESH)
    pl.semaphore_wait(barrier, len(partners))
    reduce = Reduce(place, gp_ref, row_cut(gp_ref.shape[0] // (2 * line)), across, passing, sems)
    reduce.start()
    copies = []
    all_ref[...] = gains_ref[...]
    for turn, (buffer, device) in enumerate(((near, place.sibling), (far, place.chip), (over, place.across))):
        source = lined.at[line + turn]
        source[...] = all_ref[...]
        copy = send(source, buffer, g_sems.at[0, turn], g_sems.at[1, turn], device)
        copy.start()
        copy.wait_recv()
        all_ref[...] = source[...] + buffer[...]
        copies.append(copy)
    lined[place.z] = all_ref[...]
    for step in range(1, line):
        z, device = others[step - 1]
        copy = send(lined.at[place.z], lined.at[place.z], g_sems.at[0, 2 + step], g_sems.at[1, 2 + step], device)
        copy.start()
        copies.append(copy)
    reduce.hop(1)
    for step in range(1, line):
        z = (place.z - step + line) % line
        send(lined.at[z], lined.at[z], g_sems.at[0, 2 + step], g_sems.at[1, 2 + step], place.sibling).wait_recv()
    all_sum = lined[0]
    for z in range(1, line):
        all_sum = all_sum + lined[z]
    all_ref[...] = all_sum
    for k in range(2, line):
        reduce.hop(k)
    reduce.finish(sum_ref)
    reduce.drain()
    for copy in copies:
        copy.wait_send()


def last(gp, gains, line):
    own = (gp.shape[0] // (2 * line), gp.shape[1])
    vmem = pl.BlockSpec(memory_space=pltpu.VMEM)
    return pl.pallas_call(
        partial(last_kernel, line),
        in_specs=[vmem, vmem],
        out_specs=[vmem, vmem],
        out_shape=[jax.ShapeDtypeStruct(own, FP), jax.ShapeDtypeStruct(gains.shape, FP)],
        scratch_shapes=[*reduce_scratch(line, own), *[pltpu.VMEM(gains.shape, FP)] * 3,
                        pltpu.VMEM((line + 3, *gains.shape), FP), pltpu.SemaphoreType.DMA((2, 2 + line))],
        compiler_params=params(collective_id=4, has_side_effects=True),
        name="last",
    )(gp, gains)


def adamw_step(weight, moment_one, moment_two, gradient, step_rate, decay):
    mean_next = BETA_ONE * moment_one + (1.0 - BETA_ONE) * gradient
    square_next = BETA_TWO * moment_two + (1.0 - BETA_TWO) * gradient * gradient
    mean_hat = mean_next / (1.0 - BETA_ONE**STEP)
    square_hat = square_next / (1.0 - BETA_TWO**STEP)
    weight_next = weight - step_rate * (mean_hat / (jnp.sqrt(square_hat) + EPS_ADAM) + decay * weight)
    return weight_next, mean_next, square_next


def tree_tables(segments, parent_row):
    count = parent_row.shape[0]
    length = segments.shape[0]
    labels = jnp.arange(count, dtype=jnp.int32)
    onehot = segments[:, None] == labels[None, :]
    sizes = jnp.sum(onehot.astype(FP), axis=0)
    starts = jnp.cumsum(sizes) - sizes
    reach = (labels[:, None] == labels[None, :]) | (parent_row[:, None] == labels[None, :]) | (labels[None, :] == 0)
    proper = reach & (labels[:, None] != labels[None, :])
    offsets = jnp.sum(jnp.where(proper, sizes[None, :], 0.0), axis=1)
    position = jnp.arange(length).astype(FP) + jnp.sum(jnp.where(onehot, (offsets - starts)[None, :], 0.0), axis=1)
    parent = jnp.sum(jnp.where(onehot, parent_row[None, :], 0), axis=1)
    lanes = jnp.arange(LANES, dtype=jnp.int32)
    tags = (segments[:, None] == lanes[None, :]).astype(BF)
    seen = (lanes[None, :] == segments[:, None]) | (lanes[None, :] == parent[:, None]) | (lanes[None, :] == 0)
    bars = jnp.where(seen | (lanes[None, :] >= count), 0.0, BLOCKED).astype(BF)
    half = lanes % (LANES // 2)
    frequency = THETA ** (-half.astype(FP) * 2.0 / LANES)
    angles = position[:, None] * frequency[None, :]
    sines = jnp.where(lanes[None, :] < LANES // 2, -jnp.sin(angles), jnp.sin(angles))
    return tags, bars, jnp.cos(angles), sines


def shards(
    tokens, cotangent, parents, token_segment, tree_id,
    projection_weight, projection_first_moment, projection_second_moment,
    merge_master, merge_mean, merge_square,
    expand_master, expand_mean, expand_square,
    shrink_master, shrink_mean, shrink_square,
    gain_master, gain_mean, gain_square,
):
    parts = lax.axis_size("tensor")
    part = lax.axis_index("tensor")
    x = tokens[0]
    dy = cotangent[0]
    length, d = x.shape
    share = length // parts
    first = part * share
    d_own, kv, per, n = projection_weight.shape
    group = per - 2
    units = expand_master.shape[2]
    scale = n ** (-0.5)
    unit = scale * math.log2(math.e)

    dp = lax.axis_size("dp")
    line = dp // 2 if dp <= 8 and dp % 2 == 0 and d_own % LANES == 0 and parts == 4 else 0
    low = (
        projection_weight.astype(BF).reshape(d_own, kv * per * n),
        merge_master.astype(BF),
        expand_master.astype(BF).reshape(d_own, 2 * units),
        shrink_master.astype(BF),
    )
    if not line:
        wp, we = (lax.all_gather(low[w], "dp", axis=0, tiled=True) for w in (0, 2))
        wm, ws = (lax.all_gather(low[w], "dp", axis=1, tiled=True) for w in (1, 3))

    chosen = (jnp.arange(parents.shape[0], dtype=jnp.int32) == tree_id[0]).astype(jnp.int32)
    parent_row = jnp.sum(parents * chosen[:, None], axis=0)
    tags, bars, cosines, sines = tree_tables(token_segment[0], parent_row)
    g1, g2 = gain_master[None, :d], gain_master[None, d:2 * d]
    gq, gk = gain_master[None, 2 * d:2 * d + n], gain_master[None, 2 * d + n:]
    x_own = lax.dynamic_slice_in_dim(x, first, share, 0)

    fronts = front(x, g1, gq, gk, cosines, sines, low[:2] if line else (wp,), kv, group, line)
    xn1, q, k, v, kt, vt, raw = fronts[:7]
    if line:
        wp, wm = fronts[7:]
    attends = attend(q, k, vt, tags, bars, wm, x_own, g2, low[2:] if line else (), kv, group, unit, line)
    ctx, lse, hidden, xn2 = attends[:4]
    if line:
        we, ws = attends[4:]
    base, other, expand_grad, shrink_grad, dh, dhb, dg2 = feed(xn2.reshape(length, d), dy, we, ws, hidden, g2)
    backs = back(q, k, v, kt, tags, bars, lse, ctx, dhb.reshape(length, d), wm, wp, raw, cosines, sines, gq, gk, xn1,
                 x_own, base, dh, g1, other, (expand_grad, shrink_grad) if line else (),
                 kv, group, unit, scale, line)
    input_grad, output, project_grad, head_gains, dg1 = backs[:5]
    output, input_grad = output[None], input_grad[None]
    gains = jnp.concatenate([dg1, dg2, head_gains[0], head_gains[1]], axis=1)
    if line:
        expand_sum, shrink_sum, merge_sum = backs[5:]
        project_sum, gains = last(project_grad, gains, line)
    else:
        gains = lax.psum(gains, ("dp", "tensor"))
        project_sum, expand_sum = (
            lax.psum_scatter(g, "dp", scatter_dimension=0, tiled=True) for g in (project_grad, expand_grad))
        merge_sum, shrink_sum = (
            lax.psum_scatter(g, "dp", scatter_dimension=1, tiled=True) for g in (backs[5], shrink_grad))
    gain_grad = jnp.sum(gains, axis=0)

    outs = [output, input_grad]
    for weight, mean, square, grad, rate in (
        (projection_weight, projection_first_moment, projection_second_moment, project_sum, RATE_PROJECT),
        (merge_master, merge_mean, merge_square, merge_sum, RATE_MERGE),
        (expand_master, expand_mean, expand_square, expand_sum, RATE_EXPAND),
        (shrink_master, shrink_mean, shrink_square, shrink_sum, RATE_SHRINK),
    ):
        grad = grad.astype(FP).reshape(weight.shape)
        after, mean_next, square_next = adamw_step(weight, mean, square, grad, rate, DECAY)
        outs += [after, mean_next, square_next, after.astype(BF)]
    gain_next, gain_mean_next, gain_square_next = adamw_step(
        gain_master, gain_mean, gain_square, gain_grad, RATE_GAIN, 0.0)
    return (*outs, gain_mean_next, gain_square_next, gain_next)


def solution(mesh):
    tokens = P("dp", None, None)
    project = P("dp", "tensor", None, None)
    columns = P("tensor", "dp")
    expand = P("dp", None, "tensor")
    shared = P("dp", "tensor", None)
    return jax.shard_map(
        shards,
        mesh=mesh,
        in_specs=(tokens, tokens, P(), P("dp", None), P("dp"), *[project] * 3, *[columns] * 3, *[expand] * 3,
                  *[columns] * 3, P(), P(), P()),
        out_specs=(shared, shared, *[project] * 4, *[columns] * 4, *[expand] * 4, *[columns] * 4, P(), P(), P()),
        check_vma=False,
    )
```

```python
import math
from functools import partial

import jax
import jax.numpy as jnp
from jax import lax
from jax.experimental import pallas as pl
from jax.experimental.pallas import tpu as pltpu
from jax.sharding import PartitionSpec as P

STEP = 5
EPS_NORM = 1e-06
THETA = 1000000.0
BETA_ONE = 0.5
BETA_TWO = 0.5
EPS_ADAM = 1e-08
DECAY = 0.1
RATE_PROJECT = 0.05
RATE_MERGE = 0.3
RATE_EXPAND = 0.05
RATE_SHRINK = 0.03
RATE_GAIN = 0.3

BF = jnp.bfloat16
FP = jnp.float32
ROWS = 256
LANES = 128
SUB = 128
MESH = pl.DeviceIdType.MESH
BLOCKED = -1e30
VMEM_LIMIT = 60 * 2**20


def params(**more):
    return pltpu.CompilerParams(vmem_limit_bytes=VMEM_LIMIT, **more)


def dot(a, b, ca=1, cb=0):
    return lax.dot_general(a, b, (((ca,), (cb,)), ((), ())), preferred_element_type=FP)


def inverse_rms(values):
    return lax.rsqrt(jnp.mean(values * values, axis=-1, keepdims=True) + EPS_NORM)


def rms_pull(values, scales, grad):
    r = inverse_rms(values)
    scaled = grad * scales
    mean = jnp.mean(values * scaled, axis=-1, keepdims=True)
    return r * scaled - values * (r * r * r * mean), grad * values * r


def fold_rows(values):
    n, w = values.shape
    return jnp.sum(values.reshape(n // 8, 8, w), axis=0)


class Place:
    def __init__(self, line):
        self.line = line
        self.dp, self.t = lax.axis_index("dp"), lax.axis_index("tensor")
        self.z, self.y = self.dp // 2, self.dp % 2
        self.x, self.c = self.t // 2, self.t % 2
        self.has_up, self.has_down = self.z < line - 1, self.z > 0
        self.up, self.down = (self.dp + 2, self.t), (self.dp - 2, self.t)
        self.across = (self.dp + 1 - 2 * self.y, self.t)
        self.sibling = (self.dp, self.t + 1 - 2 * self.c)
        self.chip = (self.dp, (1 - self.x) * 2 + self.c)

    def greet(self, tensor, line):
        barrier = pltpu.get_barrier_semaphore()

        def signal(device):
            pl.semaphore_signal(barrier, inc=1, device_id=device, device_id_type=MESH)

        if tensor:
            signal(self.sibling)
            signal(self.chip)
        if line:
            signal(self.across)
            pl.when(self.has_up)(lambda: signal(self.up))
            pl.when(self.has_down)(lambda: signal(self.down))
        peers = (2 if tensor else 0) + (1 if line else 0)
        if line:
            peers = peers + jnp.where(self.has_up, 1, 0) + jnp.where(self.has_down, 1, 0)
        pl.semaphore_wait(barrier, peers)


def send(src, dst, sent, arrived, device):
    return pltpu.make_async_remote_copy(
        src_ref=src, dst_ref=dst, send_sem=sent, recv_sem=arrived, device_id=device, device_id_type=MESH)


def row_cut(size):
    return lambda j: (pl.ds(pl.multiple_of(j * size, size), size), slice(None))


def column_cut(size):
    return lambda j: (slice(None), pl.ds(pl.multiple_of(j * size, size), size))


class Gather:
    def __init__(self, place, own, full, cut, sems, local):
        self.place, self.own, self.full, self.cut, self.sems, self.local = place, own, full, cut, sems, local

    def copy(self, kind, src, j):
        p = self.place
        device = (p.up, p.down, p.across)[kind]
        return send(src, self.full.at[self.cut(j)], self.sems.at[kind, j], self.sems.at[3, j], device)

    def kept(self):
        return pltpu.make_async_copy(self.own, self.full.at[self.cut(self.place.dp)], self.local)

    def start(self):
        p = self.place
        self.copy(2, self.own, p.dp).start()
        pl.when(p.has_up)(lambda: self.copy(0, self.own, p.dp).start())
        pl.when(p.has_down)(lambda: self.copy(1, self.own, p.dp).start())
        self.kept().start()

    def arrivals(self, k):
        p = self.place
        return ((0, p.z >= k, (p.z - k) * 2 + p.y, p.has_up), (1, p.z + k < p.line, (p.z + k) * 2 + p.y, p.has_down))

    def hop(self, k):
        for kind, here, j, further in self.arrivals(k):
            @pl.when(here)
            def _(kind=kind, j=j, further=further):
                piece = self.full.at[self.cut(j)]
                self.copy(kind, piece, j).wait_recv()
                pl.when(further)(lambda: self.copy(kind, piece, j).start())
                self.copy(2, piece, j).start()

    def finish(self):
        p = self.place
        self.kept().wait()
        for zz in range(p.line):
            j = zz * 2 + 1 - p.y
            self.copy(2, self.full.at[self.cut(j)], j).wait_recv()

    def drain(self):
        p = self.place
        self.copy(2, self.own, p.dp).wait_send()
        pl.when(p.has_up)(lambda: self.copy(0, self.own, p.dp).wait_send())
        pl.when(p.has_down)(lambda: self.copy(1, self.own, p.dp).wait_send())
        for k in range(1, p.line):
            for kind, here, j, further in self.arrivals(k):
                @pl.when(here)
                def _(kind=kind, j=j, further=further):
                    piece = self.full.at[self.cut(j)]
                    pl.when(further)(lambda: self.copy(kind, piece, j).wait_send())
                    self.copy(2, piece, j).wait_send()


class Reduce:
    def __init__(self, place, grad, cut, across, lined, sems):
        self.place, self.grad, self.cut, self.sems = place, grad, cut, sems
        self.across, self.lined = across, lined

    def cross(self, zz):
        p = self.place
        return send(self.grad.at[self.cut(zz * 2 + 1 - p.y)], self.across.at[zz],
                    self.sems.at[0, zz], self.sems.at[1, zz], p.across)

    def climb(self, t):
        return send(self.across.at[t], self.lined.at[t + 1], self.sems.at[2, t], self.sems.at[3, t], self.place.up)

    def sink(self, t):
        return send(self.across.at[t], self.lined.at[t], self.sems.at[4, t], self.sems.at[5, t], self.place.down)

    def mine(self, zz):
        return self.grad[self.cut(zz * 2 + self.place.y)].astype(FP)

    def turn(self, q):
        z = self.place.z
        low = z < 2
        if q == 0:
            return jnp.where(low, 3, 0)
        if q == 1:
            return jnp.where(low, 2, 1)
        if q == 2:
            return jnp.where(low, 1 - z, 5 - z)
        return z

    def start(self):
        self.cross(self.turn(0)).start()

    def advance(self, q):
        self.cross(self.turn(q - 1)).wait_send()
        self.cross(self.turn(q)).start()

    def hop(self, h):
        p = self.place

        def pass_on(t, coming, more, slot):
            self.cross(t).wait_recv()

            @pl.when(jnp.logical_not(more))
            def _():
                self.across[t] = (self.mine(t) + self.across[t].astype(FP)).astype(BF)

            @pl.when(more)
            def _():
                coming(t).wait_recv()
                self.across[t] = (self.mine(t) + self.across[t].astype(FP) + self.lined[slot].astype(FP)).astype(BF)

            coming(t).start()

        pl.when(p.z < h)(lambda: pass_on(p.z + p.line - h, self.climb, p.has_down, p.z + p.line - h + 1))
        pl.when(p.z >= p.line - h)(lambda: pass_on(p.z - p.line + h, self.sink, p.has_up, p.z - p.line + h))

    def finish(self, out):
        p = self.place
        self.cross(p.z).wait_recv()
        out[...] = self.mine(p.z) + self.across[p.z].astype(FP)

        @pl.when(p.has_down)
        def _():
            self.climb(p.z).wait_recv()
            out[...] += self.lined[p.z + 1].astype(FP)

        @pl.when(p.has_up)
        def _():
            self.sink(p.z).wait_recv()
            out[...] += self.lined[p.z].astype(FP)

    def drain(self):
        p = self.place
        self.cross(p.z).wait_send()
        for zz in range(p.line):
            pl.when(zz > p.z)(lambda zz=zz: self.climb(zz).wait_send())
            pl.when(zz < p.z)(lambda zz=zz: self.sink(zz).wait_send())


def reduce_scratch(line, shape):
    return [pltpu.VMEM((line, *shape), BF), pltpu.VMEM((line + 1, *shape), BF), pltpu.SemaphoreType.DMA((6, line))]


class Exchange:
    def __init__(self, place, per, held, near, far, total, sems):
        self.place, self.per, self.held, self.near, self.far = place, per, held, near, far
        self.total, self.sems = total, sems

    def owner(self, s):
        t = s // self.per
        return t // 2, t % 2

    def to_sibling(self, s):
        slot = (s // (2 * self.per)) * self.per + s % self.per
        return send(self.held.at[s], self.near.at[slot], self.sems.at[0, s], self.sems.at[1, s], self.place.sibling)

    def to_chip(self, s):
        slot = (s // (2 * self.per)) * self.per + s % self.per
        return send(self.near.at[slot], self.far.at[s % self.per], self.sems.at[2, s], self.sems.at[3, s],
                    self.place.chip)

    def out(self, s):
        pl.when(self.place.c != self.owner(s)[1])(lambda: self.to_sibling(s).start())

    def add(self, s):
        p = self.place
        ox, oc = self.owner(s)
        slot = (s // (2 * self.per)) * self.per + s % self.per

        @pl.when(p.c == oc)
        def _():
            self.to_sibling(s).wait_recv()

            @pl.when(p.x != ox)
            def _():
                self.near[slot] = (self.held[s].astype(FP) + self.near[slot].astype(FP)).astype(BF)
                self.to_chip(s).start()

            @pl.when(p.x == ox)
            def _():
                self.total[s % self.per] = self.held[s].astype(FP) + self.near[slot].astype(FP)

    def take(self, s, use):
        p = self.place

        @pl.when(s // self.per == p.t)
        def _():
            k = s % self.per
            self.to_chip(s).wait_recv()
            use(s, k, self.total[k] + self.far[k].astype(FP))

    def drain(self):
        p = self.place

        def one(s, carry):
            ox, oc = self.owner(s)
            pl.when(p.c != oc)(lambda: self.to_sibling(s).wait_send())
            pl.when(jnp.logical_and(p.c == oc, p.x != ox))(lambda: self.to_chip(s).wait_send())
            return carry

        lax.fori_loop(0, 4 * self.per, one, 0)


class Pairs:
    def __init__(self, place, per, held, near, sems):
        self.place, self.per, self.held, self.near, self.sems = place, per, held, near, sems

    def copy(self, s):
        slot = (s // (2 * self.per)) * self.per + s % self.per
        return send(self.held.at[s], self.near.at[slot], self.sems.at[0, s], self.sems.at[1, s], self.place.sibling)

    def out(self, s):
        pl.when(self.place.c != (s // self.per) % 2)(lambda: self.copy(s).start())

    def add(self, s, use):
        t = s // self.per
        slot = (s // (2 * self.per)) * self.per + s % self.per

        @pl.when(self.place.c == t % 2)
        def _():
            self.copy(s).wait_recv()
            use(self.place.x == t // 2, s % self.per, self.held[s].astype(FP) + self.near[slot].astype(FP))

    def drain(self):
        def one(s, carry):
            pl.when(self.place.c != (s // self.per) % 2)(lambda: self.copy(s).wait_send())
            return carry

        lax.fori_loop(0, 4 * self.per, one, 0)


def pair_of(step, per):
    t = step % 2
    return t * per + step // 2, (3 - t) * per + step // 2


def exchange_scratch(per, d, held=True):
    return [pltpu.VMEM((4 * per, SUB, d), BF)] * held + [pltpu.VMEM((2 * per, SUB, d), BF), pltpu.VMEM((per, SUB, d), BF), pltpu.VMEM((per, SUB, d), FP),
                   pltpu.SemaphoreType.DMA((4, 4 * per))]


class Spread:
    def __init__(self, place, per, stage, full, sems):
        self.place, self.per, self.stage, self.full, self.sems = place, per, stage, full, sems

    def copy(self, kind, src, s):
        device = (self.place.chip, self.place.sibling)[kind]
        return send(src, self.full.at[s], self.sems.at[kind, s], self.sems.at[2, s], device)

    def kept(self, s):
        return pltpu.make_async_copy(self.stage.at[s % self.per], self.full.at[s], self.sems.at[3, s])

    def send(self, s):
        for kind in (0, 1):
            self.copy(kind, self.stage.at[s % self.per], s).start()
        self.kept(s).start()

    def passes(self, s):
        t = s // self.per
        return jnp.logical_and(self.place.c == t % 2, self.place.x != t // 2)

    def pass_on(self, s):
        @pl.when(self.passes(s))
        def _():
            self.copy(1, self.full.at[s], s).wait_recv()
            self.copy(1, self.full.at[s], s).start()

    def finish(self):
        def one(s, carry):
            @pl.when(s // self.per == self.place.t)
            def _():
                self.copy(0, self.stage.at[s % self.per], s).wait_send()
                self.copy(1, self.stage.at[s % self.per], s).wait_send()
                self.kept(s).wait()

            pl.when(self.passes(s))(lambda: self.copy(1, self.full.at[s], s).wait_send())
            pl.when((s // self.per) % 2 != self.place.c)(lambda: self.copy(1, self.full.at[s], s).wait_recv())
            return carry

        lax.fori_loop(0, 4 * self.per, one, 0)


def spread_scratch(per, d):
    return [pltpu.VMEM((per, SUB, d), BF), pltpu.SemaphoreType.DMA((4, 4 * per))]


def whole(shape):
    return pl.BlockSpec(tuple(shape), lambda i: (0,) * len(shape), pipeline_mode=pl.Buffered(1))


ANYWHERE = pl.BlockSpec(memory_space=pl.ANY)
GATHER_SEMS = lambda shards: [pltpu.SemaphoreType.DMA((4, shards)), pltpu.SemaphoreType.DMA]


def front_kernel(kv, group, line, *refs):
    refs = list(refs)
    take = lambda count: [refs.pop(0) for _ in range(count)]
    x_ref, g1_ref, gq_ref, gk_ref, cos_ref, sin_ref = take(6)
    own = take(2) if line else take(1)
    xn_ref, q_ref, k_ref, v_ref, kt_ref, vt_ref, raw_ref = take(7)
    if line:
        wp_out, wm_out = take(2)
        wp_ref, p_sems, p_local, m_sems, m_local, out_sem = take(6)
    else:
        wp_ref = own[0]
    xn_full, xn_sem = take(2)
    i = pl.program_id(0)
    last = pl.num_programs(0) - 1
    if line:
        place = Place(line)
        size = own[0].shape[0]
        project = Gather(place, own[0], wp_ref, row_cut(size), p_sems, p_local)
        merge = Gather(place, own[1], wm_out, column_cut(own[1].shape[1]), m_sems, m_local)
        written = pltpu.make_async_copy(wp_ref, wp_out, out_sem)
    normed = pltpu.make_async_copy(xn_full, xn_ref, xn_sem)

    @pl.when(i == 0)
    def _():
        if line:
            place.greet(False, True)
            project.start()

        def norm(b, carry):
            at = pl.ds(pl.multiple_of(b * ROWS, ROWS), ROWS)
            x = x_ref[at, :].astype(FP)
            xn_full[at, :] = (x * inverse_rms(x) * g1_ref[...]).astype(BF)
            return carry

        lax.fori_loop(0, x_ref.shape[0] // ROWS, norm, 0)
        normed.start()
        if line:
            for k in range(1, line):
                project.hop(k)
            merge.start()
            project.finish()
            written.start()

    if line:
        for k in range(1, line):
            pl.when(i == k + 1)(lambda k=k: merge.hop(k))
    at = pl.ds(pl.multiple_of(i * ROWS, ROWS), ROWS)
    qkv = dot(xn_full[at, :], wp_ref[...])
    cosines, sines = cos_ref[...], sin_ref[...]
    n = LANES
    per = group + 2
    keys, values = [], []
    for h in range(kv):
        for c in range(group + 1):
            raw = qkv[:, (h * per + c) * n:(h * per + c + 1) * n]
            to = (h * (group + 1) + c) * n
            raw_ref[:, to:to + n] = raw
            y = raw * inverse_rms(raw) * (gq_ref[...] if c < group else gk_ref[...])
            turned = y * cosines + pltpu.roll(y, n // 2, 1) * sines
            if c < group:
                to = (h * group + c) * n
                q_ref[:, to:to + n] = turned.astype(BF)
            else:
                keys.append(turned)
        values.append(qkv[:, (h * per + group + 1) * n:(h * per + group + 2) * n])
    for h in range(kv):
        k_ref[:, h * n:(h + 1) * n] = keys[h].astype(BF)
        v_ref[:, h * n:(h + 1) * n] = values[h].astype(BF)
        kt_ref[h * n:(h + 1) * n, :] = keys[h].T.astype(BF)
        vt_ref[h * n:(h + 1) * n, :] = values[h].T.astype(BF)

    @pl.when(i == last)
    def _():
        normed.wait()
        if line:
            merge.finish()
            merge.drain()
            project.drain()
            written.wait()


def front(x, g1, gq, gk, cosines, sines, own, kv, group, line):
    length, d = x.shape
    n = LANES
    rows = lambda w: pl.BlockSpec((ROWS, w), lambda i: (i, 0))
    cols = pl.BlockSpec((kv * n, ROWS), lambda i: (0, i))
    out = lambda w, t: jax.ShapeDtypeStruct((length, w), t)
    raw_w = kv * (group + 1) * n
    shards = 2 * line
    more_specs, more_shapes, scratch = [], [], []
    own_specs = [whole(own[0].shape)]
    if line:
        wp_shape = (own[0].shape[0] * shards, own[0].shape[1])
        wm_shape = (own[1].shape[0], own[1].shape[1] * shards)
        own_specs.append(ANYWHERE)
        more_specs = [ANYWHERE, ANYWHERE]
        more_shapes = [jax.ShapeDtypeStruct(wp_shape, BF), jax.ShapeDtypeStruct(wm_shape, BF)]
        scratch = [pltpu.VMEM(wp_shape, BF), *GATHER_SEMS(shards), *GATHER_SEMS(shards), pltpu.SemaphoreType.DMA]
    return pl.pallas_call(
        partial(front_kernel, kv, group, line),
        grid=(length // ROWS,),
        in_specs=[whole(x.shape), whole(g1.shape), whole(gq.shape), whole(gk.shape), rows(n), rows(n), *own_specs],
        out_specs=[ANYWHERE, rows(kv * group * n), rows(kv * n), rows(kv * n), cols, cols, rows(raw_w), *more_specs],
        out_shape=[out(d, BF), out(kv * group * n, BF), out(kv * n, BF), out(kv * n, BF),
                   jax.ShapeDtypeStruct((kv * n, length), BF), jax.ShapeDtypeStruct((kv * n, length), BF),
                   out(raw_w, FP), *more_shapes],
        scratch_shapes=[*scratch, pltpu.VMEM((length, d), BF), pltpu.SemaphoreType.DMA],
        compiler_params=params(**({"collective_id": 0, "has_side_effects": True} if line else {})),
        name="front",
    )(x, g1, gq, gk, cosines, sines, *own)


def stacked(ref_block, h, group):
    n = LANES
    return jnp.concatenate(
        [ref_block[:, (h * group + g) * n:(h * group + g + 1) * n] for g in range(group)], axis=0)


def causal_tile(group, rows=ROWS, after=0):
    key_at = lax.broadcasted_iota(jnp.int32, (ROWS, rows * group), 0)
    query_at = lax.broadcasted_iota(jnp.int32, (ROWS, rows * group), 1) % rows
    return key_at <= query_at + after


def in_turn(i, steps, per, acts):
    for behind, act in enumerate(acts, 1):
        @pl.when(jnp.logical_and(i - behind >= 0, i - behind < steps))
        def _(behind=behind, act=act):
            for s in pair_of(i - behind, per):
                act(s)


def attend_kernel(kv, group, unit, line, per, steps, *refs):
    refs = list(refs)
    take = lambda count: [refs.pop(0) for _ in range(count)]
    q_ref, k_ref, vt_ref, tags_ref, bars_ref, wm_ref, x_ref, g2_ref = take(8)
    own = take(2) if line else []
    ctx_ref, lse_ref, h_ref, xn_ref = take(4)
    full = take(2) if line else []
    acc_ref, sum_ref = take(2)
    held, near, far, total, e_sems, stage, s_sems = take(7)
    gathers = []
    place = Place(line)
    if line:
        cuts = (row_cut(own[0].shape[0]), column_cut(own[1].shape[1]))
        for w in range(2):
            gathers.append(Gather(place, own[w], full[w], cuts[w], *take(2)))
    i = pl.program_id(0)
    n = LANES
    exchange = Exchange(place, per, held, near, far, total, e_sems)
    spread = Spread(place, per, stage, xn_ref, s_sems)

    @pl.when(i == 0)
    def _():
        place.greet(True, bool(line))
        for g in gathers:
            g.start()

    def block(s):
        here = pl.ds(pl.multiple_of(s * SUB, SUB), SUB)
        bars = jnp.concatenate([bars_ref[here, :]] * group, axis=0)
        q = q_ref[here, :]
        wide = [jnp.concatenate([stacked(q, h, group), bars], axis=1) for h in range(kv)]
        acc_ref[...] = jnp.zeros_like(acc_ref)
        sum_ref[...] = jnp.zeros_like(sum_ref)

        def chunk(j, diagonal):
            at = pl.ds(pl.multiple_of(j * ROWS, ROWS), ROWS)
            tags = tags_ref[at, :]
            for h in range(kv):
                keys = jnp.concatenate([k_ref[at, h * n:(h + 1) * n], tags], axis=1)
                scores = dot(keys, wide[h], 1, 1)
                e = jnp.exp2(scores * unit)
                if diagonal:
                    e = jnp.where(causal_tile(group, SUB, (s % 2) * SUB), e, 0.0)
                sum_ref[h] += fold_rows(e)
                acc_ref[h] += dot(vt_ref[h * n:(h + 1) * n, at], e.astype(BF))

        lax.fori_loop(0, s // 2, lambda j, c: (chunk(j, False), c)[1], 0)
        chunk(s // 2, True)
        parts = []
        for h in range(kv):
            sums = jnp.sum(sum_ref[h], axis=0, keepdims=True)
            lse_ref[s, h:h + 1, :] = jnp.log2(sums)
            ctx = (acc_ref[h] / sums).T
            parts += [ctx[g * SUB:(g + 1) * SUB] for g in range(group)]
        ctx_ref[here, :] = jnp.concatenate(parts, axis=1).astype(BF)

    @pl.when(i < steps)
    def _():
        blocks = pair_of(i, per)
        for s in blocks:
            block(s)
        ctx = [ctx_ref[pl.ds(pl.multiple_of(s * SUB, SUB), SUB), :] for s in blocks]
        part = dot(jnp.concatenate(ctx, axis=0), wm_ref[...]).astype(BF)
        for u, s in enumerate(blocks):
            held[s] = part[u * SUB:(u + 1) * SUB]
            exchange.out(s)

    def own_rows(s, k, summed):
        at = pl.ds(pl.multiple_of(k * SUB, SUB), SUB)
        hidden = x_ref[at, :].astype(FP) + summed
        h_ref[at, :] = hidden
        stage[k] = (hidden * inverse_rms(hidden) * g2_ref[...]).astype(BF)
        spread.send(s)

    in_turn(i, steps, per, (exchange.add, lambda s: exchange.take(s, own_rows), spread.pass_on))
    if line:
        for k in range(1, line):
            @pl.when(i == min(2 + 2 * k, steps + 2))
            def _(k=k):
                for g in gathers:
                    g.hop(k)

    @pl.when(i == steps + 2)
    def _():
        exchange.drain()
        spread.finish()
        for g in gathers:
            g.finish()
            g.drain()


def attend(q, k, vt, tags, bars, wm, x_own, g2, own, kv, group, unit, line):
    length = q.shape[0]
    n = LANES
    d = wm.shape[1]
    per = x_own.shape[0] // SUB
    steps = 2 * per
    shards = 2 * line
    full = []
    if line:
        full = [jax.ShapeDtypeStruct((own[0].shape[0] * shards, own[0].shape[1]), BF),
                jax.ShapeDtypeStruct((own[1].shape[0], own[1].shape[1] * shards), BF)]
    return pl.pallas_call(
        partial(attend_kernel, kv, group, unit, line, per, steps),
        grid=(steps + 3,),
        in_specs=[whole(q.shape), whole(k.shape), whole(vt.shape), whole(tags.shape), whole(bars.shape), whole(wm.shape),
                  whole(x_own.shape), whole(g2.shape)] + [ANYWHERE] * len(own),
        out_specs=[whole(q.shape), whole((length // SUB, 8, SUB * group)),
                   whole(x_own.shape), ANYWHERE] + [ANYWHERE] * len(full),
        out_shape=[jax.ShapeDtypeStruct(q.shape, BF),
                   jax.ShapeDtypeStruct((length // SUB, 8, SUB * group), FP),
                   jax.ShapeDtypeStruct(x_own.shape, FP),
                   jax.ShapeDtypeStruct((length // SUB, SUB, d), BF), *full],
        scratch_shapes=[pltpu.VMEM((kv, n, SUB * group), FP), pltpu.VMEM((kv, 8, SUB * group), FP),
                        *exchange_scratch(per, d), *spread_scratch(per, d)]
                       + (GATHER_SEMS(shards) * 2 if line else []),
        compiler_params=params(collective_id=1, has_side_effects=True),
        name="attend",
    )(q, k, vt, tags, bars, wm, x_own, g2, *own)


def feed_kernel(units, per, steps, xn_ref, dy_ref, we_ref, ws_ref, h_ref, g2_ref,
                base_ref, other_ref, gex_ref, gsh_ref, dh_ref, dhb_ref, dg_ref,
                a_ref, dgu_ref, held, near, far, total, e_sems, stage, s_sems, b_held, b_near, b_sems):
    i = pl.program_id(0)
    place = Place(0)
    exchange = Exchange(place, per, held, near, far, total, e_sems)
    spread = Spread(place, per, stage, dhb_ref, s_sems)
    pairs = Pairs(place, per, b_held, b_near, b_sems)
    tile = 256

    @pl.when(i == 0)
    def _():
        place.greet(True, False)
        dg_ref[...] = jnp.zeros_like(dg_ref)

    @pl.when(i < steps)
    def _():
        blocks = pair_of(i, per)
        places = [pl.ds(pl.multiple_of(s * SUB, SUB), SUB) for s in blocks]
        xn, dy = (jnp.concatenate([ref[at, :] for at in places], axis=0) for ref in (xn_ref, dy_ref))

        def keep(ref, values):
            for u, at in enumerate(places):
                ref[at, :] = values[u * SUB:(u + 1) * SUB]

        gu = dot(xn, we_ref[...])
        gate, up = gu[:, :units], gu[:, units:]
        sig = 1.0 / (1.0 + jnp.exp(-gate))
        silu = gate * sig
        a = (silu * up).astype(BF)
        keep(a_ref, a)
        da = dot(dy, ws_ref[...], 1, 1)
        dgu = jnp.concatenate([da * up * (sig * (1.0 + gate * (1.0 - sig))), da * silu], axis=1).astype(BF)
        keep(dgu_ref, dgu)
        part = dot(dgu, we_ref[...], 1, 1).astype(BF)
        for u, s in enumerate(blocks):
            held[s] = part[u * SUB:(u + 1) * SUB]
            exchange.out(s)
        part = dot(a, ws_ref[...]).astype(BF)
        for u, s in enumerate(blocks):
            b_held[s] = part[u * SUB:(u + 1) * SUB]
            pairs.out(s)

    def own_rows(s, k, summed):
        at = pl.ds(pl.multiple_of(k * SUB, SUB), SUB)
        pulled, gain_grad = rms_pull(h_ref[at, :], g2_ref[...], summed)
        dh = dy_ref[pl.ds(pl.multiple_of(s * SUB, SUB), SUB), :].astype(FP) + pulled
        dh_ref[at, :] = dh
        dg_ref[...] += fold_rows(gain_grad)
        stage[k] = dh.astype(BF)
        spread.send(s)

    def chip_rows(mine, k, summed):
        at = pl.ds(pl.multiple_of(k * SUB, SUB), SUB)

        @pl.when(mine)
        def _():
            base_ref[at, :] = h_ref[at, :] + summed

        @pl.when(jnp.logical_not(mine))
        def _():
            other_ref[k] = summed.astype(BF)

    def added(s):
        pairs.add(s, chip_rows)
        exchange.take(s, own_rows)

    in_turn(i, steps, per, (exchange.add, added, spread.pass_on))

    def tiles(grad_ref, left_ref, right_ref, first, count):
        def one(t, carry):
            cut = pl.ds(pl.multiple_of(t * tile, tile), tile)
            grad_ref[:, cut] = dot(left_ref[...], right_ref[:, cut], 0, 0).astype(grad_ref.dtype)
            return carry

        lax.fori_loop(first, first + count, one, 0)

    half = gex_ref.shape[1] // tile // 2
    pl.when(i == steps)(lambda: tiles(gsh_ref, a_ref, dy_ref, 0, gsh_ref.shape[1] // tile))
    pl.when(i == steps + 1)(lambda: tiles(gex_ref, xn_ref, dgu_ref, 0, half))

    @pl.when(i == steps + 2)
    def _():
        tiles(gex_ref, xn_ref, dgu_ref, half, half)
        exchange.drain()
        pairs.drain()
        spread.finish()


def feed(xn, dy, we, ws, h, g2):
    length, d = xn.shape
    units = ws.shape[0]
    per = h.shape[0] // SUB
    steps = 2 * per
    return pl.pallas_call(
        partial(feed_kernel, units, per, steps),
        grid=(steps + 3,),
        in_specs=[whole(xn.shape), whole(dy.shape), whole(we.shape), whole(ws.shape), whole(h.shape), whole(g2.shape)],
        out_specs=[whole(h.shape), whole((per, SUB, d)), whole(we.shape), whole(ws.shape), whole(h.shape), ANYWHERE,
                   whole((8, d))],
        out_shape=[jax.ShapeDtypeStruct(h.shape, FP), jax.ShapeDtypeStruct((per, SUB, d), BF),
                   jax.ShapeDtypeStruct(we.shape, BF),
                   jax.ShapeDtypeStruct(ws.shape, BF), jax.ShapeDtypeStruct(h.shape, FP),
                   jax.ShapeDtypeStruct((length // SUB, SUB, d), BF), jax.ShapeDtypeStruct((8, d), FP)],
        scratch_shapes=[pltpu.VMEM((length, units), BF), pltpu.VMEM((length, 2 * units), BF),
                        *exchange_scratch(per, d), *spread_scratch(per, d), pltpu.VMEM((4 * per, SUB, d), BF),
                        pltpu.VMEM((2 * per, SUB, d), BF), pltpu.SemaphoreType.DMA((2, 4 * per))],
        compiler_params=params(collective_id=2, has_side_effects=True),
        name="feed",
    )(xn, dy, we, ws, h, g2)


def back_kernel(kv, group, unit, scale, blocks, per, line, *refs):
    refs = list(refs)
    take = lambda count: [refs.pop(0) for _ in range(count)]
    q_ref, k_ref, v_ref, kt_ref, tags_ref, bars_ref, lse_ref, ctx_ref, dh_ref, wm_ref, wp_ref = take(11)
    raw_ref, cos_ref, sin_ref, gq_ref, gk_ref, xn_ref = take(6)
    base_ref, other_ref = take(2)
    grads = take(2) if line else []
    part_ref, out_ref, gp_ref, gm_ref, gains_ref = take(5)
    sums = take(2) if line else []
    dk_ref, dv_ref, dq_ref, dqkv_ref = take(4)
    b_far, b_sems = take(2)
    place = Place(line)
    i = pl.program_id(0)
    b = blocks - 1 - i
    n = LANES
    tile = 256
    reduces = []
    if line:
        shards = 2 * line
        for grad, cut in ((grads[0], row_cut(grads[0].shape[0] // shards)),
                          (grads[1], column_cut(grads[1].shape[1] // shards))):
            reduces.append(Reduce(place, grad, cut, *take(3)))

    def tiles(grad_ref, left_ref, right_ref):
        def one(t, carry):
            cut = pl.ds(pl.multiple_of(t * tile, tile), tile)
            grad_ref[:, cut] = dot(left_ref[...], right_ref[:, cut], 0, 0).astype(grad_ref.dtype)
            return carry

        lax.fori_loop(0, grad_ref.shape[1] // tile, one, 0)

    def branch(k):
        return send(other_ref.at[k], b_far.at[k], b_sems.at[0, k], b_sems.at[1, k], place.chip)

    @pl.when(i == 0)
    def _():
        place.greet(True, bool(line))
        for r in reduces:
            r.start()
        for k in range(per):
            branch(k).start()
        dk_ref[...] = jnp.zeros_like(dk_ref)
        dv_ref[...] = jnp.zeros_like(dv_ref)
        gains_ref[...] = jnp.zeros_like(gains_ref)
        tiles(gm_ref, ctx_ref, dh_ref)

    @pl.when(i < blocks)
    def _():
        here = pl.ds(pl.multiple_of(b * ROWS, ROWS), ROWS)
        dctx = dot(dh_ref[here, :], wm_ref[...], 1, 1).astype(BF)
        ctx, q = ctx_ref[here, :], q_ref[...]
        bars = jnp.concatenate([bars_ref[...]] * group, axis=0)
        wide, queries, outward, centres, lses = [], [], [], [], []
        for h in range(kv):
            queries.append(stacked(q, h, group))
            wide.append(jnp.concatenate([queries[h], bars], axis=1))
            outward.append(stacked(dctx, h, group))
            both = outward[h].astype(FP) * stacked(ctx, h, group).astype(FP)
            centres.append(jnp.sum(both.T, axis=0, keepdims=True))
            lses.append(jnp.concatenate([lse_ref[u, h:h + 1, g * SUB:(g + 1) * SUB]
                                         for g in range(group) for u in range(ROWS // SUB)], axis=1))
        dq_ref[...] = jnp.zeros_like(dq_ref)

        def chunk(j, diagonal):
            at = pl.ds(pl.multiple_of(j * ROWS, ROWS), ROWS)
            tags = tags_ref[at, :]
            for h in range(kv):
                cut = slice(h * n, (h + 1) * n)
                keys = jnp.concatenate([k_ref[at, cut], tags], axis=1)
                p = jnp.exp2(dot(keys, wide[h], 1, 1) * unit - lses[h])
                if diagonal:
                    p = jnp.where(causal_tile(group), p, 0.0)
                dp = dot(v_ref[at, cut], outward[h], 1, 1)
                ds = (p * (dp - centres[h])).astype(BF)
                dv_ref[at, cut] += dot(p.astype(BF), outward[h])
                dk_ref[at, cut] += dot(ds, queries[h])
                dq_ref[h] += dot(kt_ref[cut, at], ds)

        lax.fori_loop(0, b, lambda j, c: (chunk(j, False), c)[1], 0)
        chunk(b, True)

        cosines, sines = cos_ref[...], sin_ref[...]
        pieces = []
        for h in range(kv):
            dq = dq_ref[h].T
            for c in range(group + 1):
                if c < group:
                    d, gain, row = dq[c * ROWS:(c + 1) * ROWS] * scale, gq_ref[...], 0
                else:
                    d, gain, row = dk_ref[here, h * n:(h + 1) * n] * scale, gk_ref[...], 1
                d = d * cosines - pltpu.roll(d, n // 2, 1) * sines
                at = (h * (group + 1) + c) * n
                piece, gain_grad = rms_pull(raw_ref[:, at:at + n], gain, d)
                gains_ref[row] += fold_rows(gain_grad)
                pieces.append(piece)
            pieces.append(dv_ref[here, h * n:(h + 1) * n])
        dqkv = jnp.concatenate(pieces, axis=1).astype(BF)
        dqkv_ref[here, :] = dqkv
        part_ref[...] = dot(dqkv, wp_ref[...], 1, 1).astype(BF)

    @pl.when(i == 3)
    def _():
        for k in range(per):
            branch(k).wait()
            at = slice(k * SUB, (k + 1) * SUB)
            out_ref[at, :] = (base_ref[at, :] + b_far[k].astype(FP)).astype(BF)

    for k, step in enumerate((0, 1, 3), 1):
        @pl.when(i == step)
        def _(k=k):
            for r in reduces:
                r.advance(k)
            for r in reduces:
                r.hop(k)

    @pl.when(i == blocks)
    def _():
        tiles(gp_ref, xn_ref, dqkv_ref)
        for r, out in zip(reduces, sums):
            r.finish(out)
            r.drain()


def back(q, k, v, kt, tags, bars, lse, ctx, dh, wm, wp, raw, cosines, sines, gq, gk, xn,
         base, other, grads, kv, group, unit, scale, line):
    length = q.shape[0]
    n = LANES
    d = wm.shape[1]
    blocks = length // ROWS
    per = other.shape[0]
    block_of = lambda i: jnp.maximum(blocks - 1 - i, 0)
    rows = lambda w: pl.BlockSpec((ROWS, w), lambda i: (block_of(i), 0))
    scratch = [pltpu.VMEM((length, kv * n), FP), pltpu.VMEM((length, kv * n), FP),
               pltpu.VMEM((kv, n, ROWS * group), FP), pltpu.VMEM((length, wp.shape[1]), BF),
               pltpu.VMEM((per, SUB, d), BF), pltpu.SemaphoreType.DMA((2, per))]
    sums = []
    if line:
        shards = 2 * line
        own = [(grads[0].shape[0] // shards, grads[0].shape[1]), (grads[1].shape[0], grads[1].shape[1] // shards)]
        sums = [jax.ShapeDtypeStruct(s, FP) for s in own]
        for s in own:
            scratch += reduce_scratch(line, s)
    args = [q, k, v, kt, tags, bars, lse, ctx, dh, wm, wp, raw, cosines, sines, gq, gk, xn, base, other, *grads]
    specs = [whole(a.shape) for a in args]
    specs[18] = ANYWHERE
    for at in (0, 5, 11, 12, 13):
        specs[at] = rows(args[at].shape[1])
    specs[6] = pl.BlockSpec((ROWS // SUB, 8, SUB * group), lambda i: (block_of(i), 0, 0))
    return pl.pallas_call(
        partial(back_kernel, kv, group, unit, scale, blocks, per, line),
        grid=(blocks + 1,),
        in_specs=specs,
        out_specs=[rows(d), whole(base.shape), whole(wp.shape), whole(wm.shape), whole((2, 8, n))]
                  + [whole(s.shape) for s in sums],
        out_shape=[jax.ShapeDtypeStruct((length, d), BF), jax.ShapeDtypeStruct(base.shape, BF),
                   jax.ShapeDtypeStruct(wp.shape, BF), jax.ShapeDtypeStruct(wm.shape, BF),
                   jax.ShapeDtypeStruct((2, 8, n), FP), *sums],
        scratch_shapes=scratch,
        compiler_params=params(collective_id=3, has_side_effects=True),
        name="back",
    )(*args)


def last_kernel(line, per, part_ref, x_ref, dh_ref, g1_ref, dg2_ref, head_ref, *refs):
    refs = list(refs)
    take = lambda count: [refs.pop(0) for _ in range(count)]
    grads = take(2) if line else []
    in_ref, all_ref = take(2)
    sums = take(2) if line else []
    exchange_refs = take(4)
    place = Place(line)
    exchange = Exchange(place, per, part_ref, *exchange_refs)
    d = x_ref.shape[1]
    n = LANES
    reduces, others = [], []
    if line:
        shards = 2 * line
        for grad, cut in zip(grads, (row_cut(grads[0].shape[0] // shards), column_cut(grads[1].shape[1] // shards))):
            reduces.append(Reduce(place, grad, cut, *take(3)))
        near, far, over, lined, g_sems = take(5)
        for step in range(1, line):
            z = (place.z + step) % line
            others.append((z * 2 + place.y, place.t))
    barrier = pltpu.get_barrier_semaphore()
    partners = [place.sibling, place.chip] + ([place.across] if line else []) + others
    for device in partners:
        pl.semaphore_signal(barrier, inc=1, device_id=device, device_id_type=MESH)
    pl.semaphore_wait(barrier, len(partners))
    for r in reduces:
        r.start()

    def each(act):
        lax.fori_loop(0, 4 * per, lambda s, c: (act(s), c)[1], 0)

    def hop(k):
        for r in reduces:
            r.advance(k)
        for r in reduces:
            r.hop(k)

    each(exchange.out)
    all_ref[:, :d] = jnp.zeros((8, d), FP)
    all_ref[:, d:2 * d] = dg2_ref[...]
    all_ref[:, 2 * d:2 * d + n] = head_ref[0]
    all_ref[:, 2 * d + n:] = head_ref[1]
    each(exchange.add)
    hop(1)
    hop(2)

    def input_rows(s, k, summed):
        at = pl.ds(pl.multiple_of(k * SUB, SUB), SUB)
        pulled, gain_grad = rms_pull(x_ref[at, :].astype(FP), g1_ref[...], summed)
        in_ref[at, :] = (dh_ref[at, :] + pulled).astype(BF)
        all_ref[:, :d] += fold_rows(gain_grad)

    each(lambda s: exchange.take(s, input_rows))
    exchange.drain()
    if not line:
        return
    copies = []

    def swap(turn, buffer, device):
        source = lined.at[line + turn]
        source[...] = all_ref[...]
        copy = send(source, buffer, g_sems.at[0, turn], g_sems.at[1, turn], device)
        copy.start()
        copy.wait_recv()
        all_ref[...] = source[...] + buffer[...]
        copies.append(copy)

    swap(0, near, place.sibling)
    swap(1, far, place.chip)
    hop(3)
    swap(2, over, place.across)
    lined[place.z] = all_ref[...]
    for step in range(1, line):
        copy = send(lined.at[place.z], lined.at[place.z], g_sems.at[0, 2 + step], g_sems.at[1, 2 + step],
                    others[step - 1])
        copy.start()
        copies.append(copy)
    for r, out in zip(reduces, sums):
        r.finish(out)
    for step in range(1, line):
        z = (place.z - step + line) % line
        send(lined.at[z], lined.at[z], g_sems.at[0, 2 + step], g_sems.at[1, 2 + step], place.sibling).wait_recv()
    all_sum = lined[0]
    for z in range(1, line):
        all_sum = all_sum + lined[z]
    all_ref[...] = all_sum
    for r in reduces:
        r.drain()
    for copy in copies:
        copy.wait_send()


def last(part, x_own, dh, g1, dg2, heads, grads, line):
    d = x_own.shape[1]
    per = x_own.shape[0] // SUB
    gains = (8, 2 * d + 2 * LANES)
    vmem = pl.BlockSpec(memory_space=pltpu.VMEM)
    args = [part.reshape(4 * per, SUB, d), x_own, dh, g1, dg2, heads, *grads]
    scratch = [*exchange_scratch(per, d, held=False)]
    own = []
    if line:
        shards = 2 * line
        own = [(grads[0].shape[0] // shards, grads[0].shape[1]), (grads[1].shape[0], grads[1].shape[1] // shards)]
        for s in own:
            scratch += reduce_scratch(line, s)
        scratch += [*[pltpu.VMEM(gains, FP)] * 3, pltpu.VMEM((line + 3, *gains), FP),
                    pltpu.SemaphoreType.DMA((2, 2 + line))]
    return pl.pallas_call(
        partial(last_kernel, line, per),
        in_specs=[vmem] * len(args),
        out_specs=[vmem] * (2 + len(own)),
        out_shape=[jax.ShapeDtypeStruct(x_own.shape, BF), jax.ShapeDtypeStruct(gains, FP),
                   *[jax.ShapeDtypeStruct(s, FP) for s in own]],
        scratch_shapes=scratch,
        compiler_params=params(collective_id=4, has_side_effects=True),
        name="last",
    )(*args)


def adamw_step(weight, moment_one, moment_two, gradient, step_rate, decay):
    mean_next = BETA_ONE * moment_one + (1.0 - BETA_ONE) * gradient
    square_next = BETA_TWO * moment_two + (1.0 - BETA_TWO) * gradient * gradient
    mean_hat = mean_next / (1.0 - BETA_ONE**STEP)
    square_hat = square_next / (1.0 - BETA_TWO**STEP)
    weight_next = weight - step_rate * (mean_hat / (jnp.sqrt(square_hat) + EPS_ADAM) + decay * weight)
    return weight_next, mean_next, square_next


def tree_tables(segments, parent_row):
    count = parent_row.shape[0]
    length = segments.shape[0]
    labels = jnp.arange(count, dtype=jnp.int32)
    onehot = segments[:, None] == labels[None, :]
    sizes = jnp.sum(onehot.astype(FP), axis=0)
    starts = jnp.cumsum(sizes) - sizes
    reach = (labels[:, None] == labels[None, :]) | (parent_row[:, None] == labels[None, :]) | (labels[None, :] == 0)
    proper = reach & (labels[:, None] != labels[None, :])
    offsets = jnp.sum(jnp.where(proper, sizes[None, :], 0.0), axis=1)
    position = jnp.arange(length).astype(FP) + jnp.sum(jnp.where(onehot, (offsets - starts)[None, :], 0.0), axis=1)
    parent = jnp.sum(jnp.where(onehot, parent_row[None, :], 0), axis=1)
    lanes = jnp.arange(LANES, dtype=jnp.int32)
    tags = (segments[:, None] == lanes[None, :]).astype(BF)
    seen = (lanes[None, :] == segments[:, None]) | (lanes[None, :] == parent[:, None]) | (lanes[None, :] == 0)
    bars = jnp.where(seen | (lanes[None, :] >= count), 0.0, BLOCKED).astype(BF)
    half = lanes % (LANES // 2)
    frequency = THETA ** (-half.astype(FP) * 2.0 / LANES)
    angles = position[:, None] * frequency[None, :]
    sines = jnp.where(lanes[None, :] < LANES // 2, -jnp.sin(angles), jnp.sin(angles))
    return tags, bars, jnp.cos(angles), sines


def shards(
    tokens, cotangent, parents, token_segment, tree_id,
    projection_weight, projection_first_moment, projection_second_moment,
    merge_master, merge_mean, merge_square,
    expand_master, expand_mean, expand_square,
    shrink_master, shrink_mean, shrink_square,
    gain_master, gain_mean, gain_square,
):
    parts = lax.axis_size("tensor")
    part = lax.axis_index("tensor")
    x = tokens[0]
    dy = cotangent[0]
    length, d = x.shape
    share = length // parts
    first = part * share
    d_own, kv, per, n = projection_weight.shape
    group = per - 2
    units = expand_master.shape[2]
    scale = n ** (-0.5)
    unit = scale * math.log2(math.e)

    dp = lax.axis_size("dp")
    line = 4 if dp == 8 and d_own % LANES == 0 else 0
    low = (
        projection_weight.astype(BF).reshape(d_own, kv * per * n),
        merge_master.astype(BF),
        expand_master.astype(BF).reshape(d_own, 2 * units),
        shrink_master.astype(BF),
    )
    if not line:
        wp, we = (lax.all_gather(low[w], "dp", axis=0, tiled=True) for w in (0, 2))
        wm, ws = (lax.all_gather(low[w], "dp", axis=1, tiled=True) for w in (1, 3))

    chosen = (jnp.arange(parents.shape[0], dtype=jnp.int32) == tree_id[0]).astype(jnp.int32)
    parent_row = jnp.sum(parents * chosen[:, None], axis=0)
    tags, bars, cosines, sines = tree_tables(token_segment[0], parent_row)
    g1, g2 = gain_master[None, :d], gain_master[None, d:2 * d]
    gq, gk = gain_master[None, 2 * d:2 * d + n], gain_master[None, 2 * d + n:]
    x_own = lax.dynamic_slice_in_dim(x, first, share, 0)

    fronts = front(x, g1, gq, gk, cosines, sines, low[:2] if line else (wp,), kv, group, line)
    xn1, q, k, v, kt, vt, raw = fronts[:7]
    if line:
        wp, wm = fronts[7:]
    attends = attend(q, k, vt, tags, bars, wm, x_own, g2, low[2:] if line else (), kv, group, unit, line)
    ctx, lse, hidden, xn2 = attends[:4]
    if line:
        we, ws = attends[4:]
    base, other, expand_grad, shrink_grad, dh, dhb, dg2 = feed(xn2.reshape(length, d), dy, we, ws, hidden, g2)
    backs = back(q, k, v, kt, tags, bars, lse, ctx, dhb.reshape(length, d), wm, wp, raw, cosines, sines, gq, gk, xn1,
                 base, other, (expand_grad, shrink_grad) if line else (), kv, group, unit, scale, line)
    partial_x, output, project_grad, merge_grad, head_gains = backs[:5]
    lasts = last(partial_x, x_own, dh, g1, dg2, head_gains, (project_grad, merge_grad) if line else (), line)
    input_grad, gains = lasts[:2]
    output, input_grad = output[None], input_grad[None]
    if line:
        expand_sum, shrink_sum = backs[5:]
        project_sum, merge_sum = lasts[2:]
    else:
        gains = lax.psum(gains, ("dp", "tensor"))
        project_sum, expand_sum = (
            lax.psum_scatter(g, "dp", scatter_dimension=0, tiled=True) for g in (project_grad, expand_grad))
        merge_sum, shrink_sum = (
            lax.psum_scatter(g, "dp", scatter_dimension=1, tiled=True) for g in (merge_grad, shrink_grad))
    gain_grad = jnp.sum(gains, axis=0)

    outs = [output, input_grad]
    for weight, mean, square, grad, rate in (
        (projection_weight, projection_first_moment, projection_second_moment, project_sum, RATE_PROJECT),
        (merge_master, merge_mean, merge_square, merge_sum, RATE_MERGE),
        (expand_master, expand_mean, expand_square, expand_sum, RATE_EXPAND),
        (shrink_master, shrink_mean, shrink_square, shrink_sum, RATE_SHRINK),
    ):
        grad = grad.astype(FP).reshape(weight.shape)
        after, mean_next, square_next = adamw_step(weight, mean, square, grad, rate, DECAY)
        outs += [after, mean_next, square_next, after.astype(BF)]
    gain_next, gain_mean_next, gain_square_next = adamw_step(
        gain_master, gain_mean, gain_square, gain_grad, RATE_GAIN, 0.0)
    return (*outs, gain_mean_next, gain_square_next, gain_next)


def solution(mesh):
    tokens = P("dp", None, None)
    project = P("dp", "tensor", None, None)
    columns = P("tensor", "dp")
    expand = P("dp", None, "tensor")
    shared = P("dp", "tensor", None)
    return jax.shard_map(
        shards,
        mesh=mesh,
        in_specs=(tokens, tokens, P(), P("dp", None), P("dp"), *[project] * 3, *[columns] * 3, *[expand] * 3,
                  *[columns] * 3, P(), P(), P()),
        out_specs=(shared, shared, *[project] * 4, *[columns] * 4, *[expand] * 4, *[columns] * 4, P(), P(), P()),
        check_vma=False,
    )
```

```python
import math
from functools import partial

import jax
import jax.numpy as jnp
from jax import lax
from jax.experimental import pallas as pl
from jax.experimental.pallas import tpu as pltpu
from jax.sharding import PartitionSpec as P

STEP = 5
EPS_NORM = 1e-06
THETA = 1000000.0
BETA_ONE = 0.5
BETA_TWO = 0.5
EPS_ADAM = 1e-08
DECAY = 0.1
RATE_PROJECT = 0.05
RATE_MERGE = 0.3
RATE_EXPAND = 0.05
RATE_SHRINK = 0.03
RATE_GAIN = 0.3

BF = jnp.bfloat16
FP = jnp.float32
ROWS = 256
LANES = 128
SUB = 128
MESH = pl.DeviceIdType.MESH
BLOCKED = -1e30
VMEM_LIMIT = 60 * 2**20


def params(**more):
    return pltpu.CompilerParams(vmem_limit_bytes=VMEM_LIMIT, **more)


def dot(a, b, ca=1, cb=0):
    return lax.dot_general(a, b, (((ca,), (cb,)), ((), ())), preferred_element_type=FP)


def inverse_rms(values):
    return lax.rsqrt(jnp.mean(values * values, axis=-1, keepdims=True) + EPS_NORM)


def rms_pull(values, scales, grad):
    r = inverse_rms(values)
    scaled = grad * scales
    mean = jnp.mean(values * scaled, axis=-1, keepdims=True)
    return r * scaled - values * (r * r * r * mean), grad * values * r


def fold_rows(values):
    n, w = values.shape
    return jnp.sum(values.reshape(n // 8, 8, w), axis=0)


class Place:
    def __init__(self, line):
        self.line = line
        self.dp, self.t = lax.axis_index("dp"), lax.axis_index("tensor")
        self.z, self.y = self.dp // 2, self.dp % 2
        self.x, self.c = self.t // 2, self.t % 2
        self.has_up, self.has_down = self.z < line - 1, self.z > 0
        self.up, self.down = (self.dp + 2, self.t), (self.dp - 2, self.t)
        self.across = (self.dp + 1 - 2 * self.y, self.t)
        self.sibling = (self.dp, self.t + 1 - 2 * self.c)
        self.chip = (self.dp, (1 - self.x) * 2 + self.c)

    def greet(self, tensor, line):
        barrier = pltpu.get_barrier_semaphore()

        def signal(device):
            pl.semaphore_signal(barrier, inc=1, device_id=device, device_id_type=MESH)

        if tensor:
            signal(self.sibling)
            signal(self.chip)
        if line:
            signal(self.across)
            pl.when(self.has_up)(lambda: signal(self.up))
            pl.when(self.has_down)(lambda: signal(self.down))
        peers = (2 if tensor else 0) + (1 if line else 0)
        if line:
            peers = peers + jnp.where(self.has_up, 1, 0) + jnp.where(self.has_down, 1, 0)
        pl.semaphore_wait(barrier, peers)


def send(src, dst, sent, arrived, device):
    return pltpu.make_async_remote_copy(
        src_ref=src, dst_ref=dst, send_sem=sent, recv_sem=arrived, device_id=device, device_id_type=MESH)


def row_cut(size):
    return lambda j: (pl.ds(pl.multiple_of(j * size, size), size), slice(None))


def column_cut(size):
    return lambda j: (slice(None), pl.ds(pl.multiple_of(j * size, size), size))


class Gather:
    def __init__(self, place, own, full, cut, sems, local):
        self.place, self.own, self.full, self.cut, self.sems, self.local = place, own, full, cut, sems, local

    def copy(self, kind, src, j):
        p = self.place
        device = (p.up, p.down, p.across)[kind]
        return send(src, self.full.at[self.cut(j)], self.sems.at[kind, j], self.sems.at[3, j], device)

    def kept(self):
        return pltpu.make_async_copy(self.own, self.full.at[self.cut(self.place.dp)], self.local)

    def start(self):
        p = self.place
        self.copy(2, self.own, p.dp).start()
        pl.when(p.has_up)(lambda: self.copy(0, self.own, p.dp).start())
        pl.when(p.has_down)(lambda: self.copy(1, self.own, p.dp).start())
        self.kept().start()

    def arrivals(self, k):
        p = self.place
        return ((0, p.z >= k, (p.z - k) * 2 + p.y, p.has_up), (1, p.z + k < p.line, (p.z + k) * 2 + p.y, p.has_down))

    def hop(self, k):
        for kind, here, j, further in self.arrivals(k):
            @pl.when(here)
            def _(kind=kind, j=j, further=further):
                piece = self.full.at[self.cut(j)]
                self.copy(kind, piece, j).wait_recv()
                pl.when(further)(lambda: self.copy(kind, piece, j).start())
                self.copy(2, piece, j).start()

    def finish(self):
        p = self.place
        self.kept().wait()
        for zz in range(p.line):
            j = zz * 2 + 1 - p.y
            self.copy(2, self.full.at[self.cut(j)], j).wait_recv()

    def drain(self):
        p = self.place
        self.copy(2, self.own, p.dp).wait_send()
        pl.when(p.has_up)(lambda: self.copy(0, self.own, p.dp).wait_send())
        pl.when(p.has_down)(lambda: self.copy(1, self.own, p.dp).wait_send())
        for k in range(1, p.line):
            for kind, here, j, further in self.arrivals(k):
                @pl.when(here)
                def _(kind=kind, j=j, further=further):
                    piece = self.full.at[self.cut(j)]
                    pl.when(further)(lambda: self.copy(kind, piece, j).wait_send())
                    self.copy(2, piece, j).wait_send()


class Reduce:
    def __init__(self, place, grad, cut, kept, across, lined, sems):
        self.place, self.grad, self.cut, self.kept, self.sems = place, grad, cut, kept, sems
        self.across, self.lined = across, lined

    def cross(self, zz):
        p = self.place
        return send(self.grad.at[self.cut(zz * 2 + 1 - p.y)], self.across.at[zz],
                    self.sems.at[0, zz], self.sems.at[1, zz], p.across)

    def climb(self, t):
        return send(self.across.at[t], self.lined.at[t + 1], self.sems.at[2, t], self.sems.at[3, t], self.place.up)

    def sink(self, t):
        return send(self.across.at[t], self.lined.at[t], self.sems.at[4, t], self.sems.at[5, t], self.place.down)

    def load(self, zz):
        return pltpu.make_async_copy(self.grad.at[self.cut(zz * 2 + self.place.y)], self.kept.at[zz], self.sems.at[6, zz])

    def mine(self, zz):
        return self.kept[zz].astype(FP)

    def turn(self, q):
        z = self.place.z
        low = z < 2
        if q == 0:
            return jnp.where(low, 3, 0)
        if q == 1:
            return jnp.where(low, 2, 1)
        if q == 2:
            return jnp.where(low, 1 - z, 5 - z)
        return z

    def start(self):
        self.cross(self.turn(0)).start()
        for zz in range(self.place.line):
            self.load(zz).start()

    def advance(self, q):
        self.cross(self.turn(q - 1)).wait_send()
        self.cross(self.turn(q)).start()

    def hop(self, h):
        p = self.place

        def pass_on(t, coming, more, slot):
            self.load(t).wait()
            self.cross(t).wait_recv()

            @pl.when(jnp.logical_not(more))
            def _():
                self.across[t] = (self.mine(t) + self.across[t].astype(FP)).astype(BF)

            @pl.when(more)
            def _():
                coming(t).wait_recv()
                self.across[t] = (self.mine(t) + self.across[t].astype(FP) + self.lined[slot].astype(FP)).astype(BF)

            coming(t).start()

        pl.when(p.z < h)(lambda: pass_on(p.z + p.line - h, self.climb, p.has_down, p.z + p.line - h + 1))
        pl.when(p.z >= p.line - h)(lambda: pass_on(p.z - p.line + h, self.sink, p.has_up, p.z - p.line + h))

    def finish(self, out):
        p = self.place
        self.load(p.z).wait()
        self.cross(p.z).wait_recv()
        out[...] = self.mine(p.z) + self.across[p.z].astype(FP)

        @pl.when(p.has_down)
        def _():
            self.climb(p.z).wait_recv()
            out[...] += self.lined[p.z + 1].astype(FP)

        @pl.when(p.has_up)
        def _():
            self.sink(p.z).wait_recv()
            out[...] += self.lined[p.z].astype(FP)

    def step(self, k):
        self.advance(k)
        self.hop(k)

    def drain(self):
        p = self.place
        self.cross(p.z).wait_send()
        for zz in range(p.line):
            pl.when(zz > p.z)(lambda zz=zz: self.climb(zz).wait_send())
            pl.when(zz < p.z)(lambda zz=zz: self.sink(zz).wait_send())


def reduce_scratch(line, shape):
    return [pltpu.VMEM((line, *shape), BF), pltpu.VMEM((line, *shape), BF), pltpu.VMEM((line + 1, *shape), BF),
            pltpu.SemaphoreType.DMA((7, line))]


class Exchange:
    def __init__(self, place, per, held, near, far, total, sems):
        self.place, self.per, self.held, self.near, self.far = place, per, held, near, far
        self.total, self.sems = total, sems

    def owner(self, s):
        t = s // self.per
        return t // 2, t % 2

    def to_sibling(self, s):
        slot = (s // (2 * self.per)) * self.per + s % self.per
        return send(self.held.at[s], self.near.at[slot], self.sems.at[0, s], self.sems.at[1, s], self.place.sibling)

    def to_chip(self, s):
        slot = (s // (2 * self.per)) * self.per + s % self.per
        return send(self.near.at[slot], self.far.at[s % self.per], self.sems.at[2, s], self.sems.at[3, s],
                    self.place.chip)

    def out(self, s):
        pl.when(self.place.c != self.owner(s)[1])(lambda: self.to_sibling(s).start())

    def add(self, s):
        p = self.place
        ox, oc = self.owner(s)
        slot = (s // (2 * self.per)) * self.per + s % self.per

        @pl.when(p.c == oc)
        def _():
            self.to_sibling(s).wait_recv()

            @pl.when(p.x != ox)
            def _():
                self.near[slot] = (self.held[s].astype(FP) + self.near[slot].astype(FP)).astype(BF)
                self.to_chip(s).start()

            @pl.when(p.x == ox)
            def _():
                self.total[s % self.per] = self.held[s].astype(FP) + self.near[slot].astype(FP)

    def take(self, s, use):
        p = self.place

        @pl.when(s // self.per == p.t)
        def _():
            k = s % self.per
            self.to_chip(s).wait_recv()
            use(s, k, self.total[k] + self.far[k].astype(FP))

    def drain(self):
        p = self.place

        def one(s, carry):
            ox, oc = self.owner(s)
            pl.when(p.c != oc)(lambda: self.to_sibling(s).wait_send())
            pl.when(jnp.logical_and(p.c == oc, p.x != ox))(lambda: self.to_chip(s).wait_send())
            return carry

        lax.fori_loop(0, 4 * self.per, one, 0)


class Pairs:
    def __init__(self, place, per, held, near, sems):
        self.place, self.per, self.held, self.near, self.sems = place, per, held, near, sems

    def copy(self, s):
        slot = (s // (2 * self.per)) * self.per + s % self.per
        return send(self.held.at[s], self.near.at[slot], self.sems.at[0, s], self.sems.at[1, s], self.place.sibling)

    def out(self, s):
        pl.when(self.place.c != (s // self.per) % 2)(lambda: self.copy(s).start())

    def add(self, s, use):
        t = s // self.per
        slot = (s // (2 * self.per)) * self.per + s % self.per

        @pl.when(self.place.c == t % 2)
        def _():
            self.copy(s).wait_recv()
            use(self.place.x == t // 2, s % self.per, self.held[s].astype(FP) + self.near[slot].astype(FP))

    def drain(self):
        def one(s, carry):
            pl.when(self.place.c != (s // self.per) % 2)(lambda: self.copy(s).wait_send())
            return carry

        lax.fori_loop(0, 4 * self.per, one, 0)


def pair_of(step, per):
    t = step % 2
    return t * per + step // 2, (3 - t) * per + step // 2


def exchange_scratch(per, d, held=True):
    return [pltpu.VMEM((4 * per, SUB, d), BF)] * held + [pltpu.VMEM((2 * per, SUB, d), BF), pltpu.VMEM((per, SUB, d), BF), pltpu.VMEM((per, SUB, d), FP),
                   pltpu.SemaphoreType.DMA((4, 4 * per))]


class Spread:
    def __init__(self, place, per, stage, full, sems):
        self.place, self.per, self.stage, self.full, self.sems = place, per, stage, full, sems

    def copy(self, kind, src, s):
        device = (self.place.chip, self.place.sibling)[kind]
        return send(src, self.full.at[s], self.sems.at[kind, s], self.sems.at[2, s], device)

    def kept(self, s):
        return pltpu.make_async_copy(self.stage.at[s % self.per], self.full.at[s], self.sems.at[3, s])

    def send(self, s):
        for kind in (0, 1):
            self.copy(kind, self.stage.at[s % self.per], s).start()
        self.kept(s).start()

    def passes(self, s):
        t = s // self.per
        return jnp.logical_and(self.place.c == t % 2, self.place.x != t // 2)

    def pass_on(self, s):
        @pl.when(self.passes(s))
        def _():
            self.copy(1, self.full.at[s], s).wait_recv()
            self.copy(1, self.full.at[s], s).start()

    def finish(self):
        def one(s, carry):
            @pl.when(s // self.per == self.place.t)
            def _():
                self.copy(0, self.stage.at[s % self.per], s).wait_send()
                self.copy(1, self.stage.at[s % self.per], s).wait_send()
                self.kept(s).wait()

            pl.when(self.passes(s))(lambda: self.copy(1, self.full.at[s], s).wait_send())
            pl.when((s // self.per) % 2 != self.place.c)(lambda: self.copy(1, self.full.at[s], s).wait_recv())
            return carry

        lax.fori_loop(0, 4 * self.per, one, 0)


def spread_scratch(per, d):
    return [pltpu.VMEM((per, SUB, d), BF), pltpu.SemaphoreType.DMA((4, 4 * per))]


def whole(shape):
    return pl.BlockSpec(tuple(shape), lambda i: (0,) * len(shape), pipeline_mode=pl.Buffered(1))


ANYWHERE = pl.BlockSpec(memory_space=pl.ANY)
GATHER_SEMS = lambda shards: [pltpu.SemaphoreType.DMA((4, shards)), pltpu.SemaphoreType.DMA]


def front_kernel(kv, group, line, *refs):
    refs = list(refs)
    take = lambda count: [refs.pop(0) for _ in range(count)]
    x_ref, g1_ref, gq_ref, gk_ref, cos_ref, sin_ref = take(6)
    own = take(2) if line else take(1)
    xn_ref, q_ref, k_ref, v_ref, kt_ref, vt_ref, raw_ref = take(7)
    if line:
        wp_out, wm_out = take(2)
        wp_ref, p_sems, p_local, m_sems, m_local, out_sem = take(6)
    else:
        wp_ref = own[0]
    xn_full, xn_sem = take(2)
    i = pl.program_id(0)
    last = pl.num_programs(0) - 1
    if line:
        place = Place(line)
        size = own[0].shape[0]
        project = Gather(place, own[0], wp_ref, row_cut(size), p_sems, p_local)
        merge = Gather(place, own[1], wm_out, column_cut(own[1].shape[1]), m_sems, m_local)
        written = pltpu.make_async_copy(wp_ref, wp_out, out_sem)
    normed = pltpu.make_async_copy(xn_full, xn_ref, xn_sem)

    @pl.when(i == 0)
    def _():
        if line:
            place.greet(False, True)
            project.start()

        def norm(b, carry):
            at = pl.ds(pl.multiple_of(b * ROWS, ROWS), ROWS)
            x = x_ref[at, :].astype(FP)
            xn_full[at, :] = (x * inverse_rms(x) * g1_ref[...]).astype(BF)
            return carry

        lax.fori_loop(0, x_ref.shape[0] // ROWS, norm, 0)
        normed.start()
        if line:
            for k in range(1, line):
                project.hop(k)
            merge.start()
            project.finish()
            written.start()

    if line:
        for k in range(1, line):
            pl.when(i == k + 1)(lambda k=k: merge.hop(k))
    at = pl.ds(pl.multiple_of(i * ROWS, ROWS), ROWS)
    qkv = dot(xn_full[at, :], wp_ref[...])
    cosines, sines = cos_ref[...], sin_ref[...]
    n = LANES
    per = group + 2
    keys, values = [], []
    for h in range(kv):
        for c in range(group + 1):
            raw = qkv[:, (h * per + c) * n:(h * per + c + 1) * n]
            to = (h * (group + 1) + c) * n
            raw_ref[:, to:to + n] = raw
            y = raw * inverse_rms(raw) * (gq_ref[...] if c < group else gk_ref[...])
            turned = y * cosines + pltpu.roll(y, n // 2, 1) * sines
            if c < group:
                to = (h * group + c) * n
                q_ref[:, to:to + n] = turned.astype(BF)
            else:
                keys.append(turned)
        values.append(qkv[:, (h * per + group + 1) * n:(h * per + group + 2) * n])
    for h in range(kv):
        k_ref[:, h * n:(h + 1) * n] = keys[h].astype(BF)
        v_ref[:, h * n:(h + 1) * n] = values[h].astype(BF)
        kt_ref[h * n:(h + 1) * n, :] = keys[h].T.astype(BF)
        vt_ref[h * n:(h + 1) * n, :] = values[h].T.astype(BF)

    @pl.when(i == last)
    def _():
        normed.wait()
        if line:
            merge.finish()
            merge.drain()
            project.drain()
            written.wait()


def front(x, g1, gq, gk, cosines, sines, own, kv, group, line):
    length, d = x.shape
    n = LANES
    rows = lambda w: pl.BlockSpec((ROWS, w), lambda i: (i, 0))
    cols = pl.BlockSpec((kv * n, ROWS), lambda i: (0, i))
    out = lambda w, t: jax.ShapeDtypeStruct((length, w), t)
    raw_w = kv * (group + 1) * n
    shards = 2 * line
    more_specs, more_shapes, scratch = [], [], []
    own_specs = [whole(own[0].shape)]
    if line:
        wp_shape = (own[0].shape[0] * shards, own[0].shape[1])
        wm_shape = (own[1].shape[0], own[1].shape[1] * shards)
        own_specs.append(ANYWHERE)
        more_specs = [ANYWHERE, ANYWHERE]
        more_shapes = [jax.ShapeDtypeStruct(wp_shape, BF), jax.ShapeDtypeStruct(wm_shape, BF)]
        scratch = [pltpu.VMEM(wp_shape, BF), *GATHER_SEMS(shards), *GATHER_SEMS(shards), pltpu.SemaphoreType.DMA]
    return pl.pallas_call(
        partial(front_kernel, kv, group, line),
        grid=(length // ROWS,),
        in_specs=[whole(x.shape), whole(g1.shape), whole(gq.shape), whole(gk.shape), rows(n), rows(n), *own_specs],
        out_specs=[ANYWHERE, rows(kv * group * n), rows(kv * n), rows(kv * n), cols, cols, rows(raw_w), *more_specs],
        out_shape=[out(d, BF), out(kv * group * n, BF), out(kv * n, BF), out(kv * n, BF),
                   jax.ShapeDtypeStruct((kv * n, length), BF), jax.ShapeDtypeStruct((kv * n, length), BF),
                   out(raw_w, FP), *more_shapes],
        scratch_shapes=[*scratch, pltpu.VMEM((length, d), BF), pltpu.SemaphoreType.DMA],
        compiler_params=params(**({"collective_id": 0, "has_side_effects": True} if line else {})),
        name="front",
    )(x, g1, gq, gk, cosines, sines, *own)


def stacked(ref_block, h, group):
    n = LANES
    return jnp.concatenate(
        [ref_block[:, (h * group + g) * n:(h * group + g + 1) * n] for g in range(group)], axis=0)


def causal_tile(group, rows=ROWS, after=0):
    key_at = lax.broadcasted_iota(jnp.int32, (ROWS, rows * group), 0)
    query_at = lax.broadcasted_iota(jnp.int32, (ROWS, rows * group), 1) % rows
    return key_at <= query_at + after


def in_turn(i, steps, per, acts):
    for behind, act in enumerate(acts, 1):
        @pl.when(jnp.logical_and(i - behind >= 0, i - behind < steps))
        def _(behind=behind, act=act):
            for s in pair_of(i - behind, per):
                act(s)


def attend_kernel(kv, group, unit, line, per, steps, *refs):
    refs = list(refs)
    take = lambda count: [refs.pop(0) for _ in range(count)]
    q_ref, k_ref, vt_ref, tags_ref, bars_ref, wm_ref, x_ref, g2_ref = take(8)
    own = take(2) if line else []
    ctx_ref, lse_ref, h_ref, xn_ref = take(4)
    full = take(2) if line else []
    acc_ref, sum_ref = take(2)
    held, near, far, total, e_sems, stage, s_sems = take(7)
    gathers = []
    place = Place(line)
    if line:
        cuts = (row_cut(own[0].shape[0]), column_cut(own[1].shape[1]))
        for w in range(2):
            gathers.append(Gather(place, own[w], full[w], cuts[w], *take(2)))
    i = pl.program_id(0)
    n = LANES
    exchange = Exchange(place, per, held, near, far, total, e_sems)
    spread = Spread(place, per, stage, xn_ref, s_sems)

    @pl.when(i == 0)
    def _():
        place.greet(True, bool(line))
        for g in gathers:
            g.start()

    def block(s):
        here = pl.ds(pl.multiple_of(s * SUB, SUB), SUB)
        bars = jnp.concatenate([bars_ref[here, :]] * group, axis=0)
        q = q_ref[here, :]
        wide = [jnp.concatenate([stacked(q, h, group), bars], axis=1) for h in range(kv)]
        acc_ref[...] = jnp.zeros_like(acc_ref)
        sum_ref[...] = jnp.zeros_like(sum_ref)

        def chunk(j, diagonal):
            at = pl.ds(pl.multiple_of(j * ROWS, ROWS), ROWS)
            tags = tags_ref[at, :]
            for h in range(kv):
                keys = jnp.concatenate([k_ref[at, h * n:(h + 1) * n], tags], axis=1)
                scores = dot(keys, wide[h], 1, 1)
                e = jnp.exp2(scores * unit)
                if diagonal:
                    e = jnp.where(causal_tile(group, SUB, (s % 2) * SUB), e, 0.0)
                sum_ref[h] += fold_rows(e)
                acc_ref[h] += dot(vt_ref[h * n:(h + 1) * n, at], e.astype(BF))

        lax.fori_loop(0, s // 2, lambda j, c: (chunk(j, False), c)[1], 0)
        chunk(s // 2, True)
        parts = []
        for h in range(kv):
            sums = jnp.sum(sum_ref[h], axis=0, keepdims=True)
            lse_ref[s, h:h + 1, :] = jnp.log2(sums)
            ctx = (acc_ref[h] / sums).T
            parts += [ctx[g * SUB:(g + 1) * SUB] for g in range(group)]
        ctx_ref[here, :] = jnp.concatenate(parts, axis=1).astype(BF)

    @pl.when(i < steps)
    def _():
        blocks = pair_of(i, per)
        for s in blocks:
            block(s)
        ctx = [ctx_ref[pl.ds(pl.multiple_of(s * SUB, SUB), SUB), :] for s in blocks]
        part = dot(jnp.concatenate(ctx, axis=0), wm_ref[...]).astype(BF)
        for u, s in enumerate(blocks):
            held[s] = part[u * SUB:(u + 1) * SUB]
            exchange.out(s)

    def own_rows(s, k, summed):
        at = pl.ds(pl.multiple_of(k * SUB, SUB), SUB)
        hidden = x_ref[at, :].astype(FP) + summed
        h_ref[at, :] = hidden
        stage[k] = (hidden * inverse_rms(hidden) * g2_ref[...]).astype(BF)
        spread.send(s)

    in_turn(i, steps, per, (exchange.add, lambda s: exchange.take(s, own_rows), spread.pass_on))
    if line:
        for k in range(1, line):
            @pl.when(i == min(2 * k, steps + 2))
            def _(k=k):
                for g in gathers:
                    g.hop(k)

    @pl.when(i == steps + 2)
    def _():
        exchange.drain()
        spread.finish()
        for g in gathers:
            g.finish()
            g.drain()


def attend(q, k, vt, tags, bars, wm, x_own, g2, own, kv, group, unit, line):
    length = q.shape[0]
    n = LANES
    d = wm.shape[1]
    per = x_own.shape[0] // SUB
    steps = 2 * per
    shards = 2 * line
    full = []
    if line:
        full = [jax.ShapeDtypeStruct((own[0].shape[0] * shards, own[0].shape[1]), BF),
                jax.ShapeDtypeStruct((own[1].shape[0], own[1].shape[1] * shards), BF)]
    return pl.pallas_call(
        partial(attend_kernel, kv, group, unit, line, per, steps),
        grid=(steps + 3,),
        in_specs=[whole(q.shape), whole(k.shape), whole(vt.shape), whole(tags.shape), whole(bars.shape), whole(wm.shape),
                  whole(x_own.shape), whole(g2.shape)] + [ANYWHERE] * len(own),
        out_specs=[whole(q.shape), whole((length // SUB, 8, SUB * group)),
                   whole(x_own.shape), ANYWHERE] + [ANYWHERE] * len(full),
        out_shape=[jax.ShapeDtypeStruct(q.shape, BF),
                   jax.ShapeDtypeStruct((length // SUB, 8, SUB * group), FP),
                   jax.ShapeDtypeStruct(x_own.shape, FP),
                   jax.ShapeDtypeStruct((length // SUB, SUB, d), BF), *full],
        scratch_shapes=[pltpu.VMEM((kv, n, SUB * group), FP), pltpu.VMEM((kv, 8, SUB * group), FP),
                        *exchange_scratch(per, d), *spread_scratch(per, d)]
                       + (GATHER_SEMS(shards) * 2 if line else []),
        compiler_params=params(collective_id=1, has_side_effects=True),
        name="attend",
    )(q, k, vt, tags, bars, wm, x_own, g2, *own)


def feed_kernel(units, per, steps, line, xn_ref, dy_ref, we_ref, ws_ref, h_ref, g2_ref,
                base_ref, other_ref, gex_ref, dh_ref, dhb_ref, dg_ref, gsh_out,
                a_ref, dgu_ref, held, near, far, total, e_sems, stage, s_sems, b_held, b_near, b_sems, *more):
    i = pl.program_id(0)
    place = Place(line)
    if line:
        gsh_ref = more[0]
        shrink = Reduce(place, gsh_ref, column_cut(gsh_ref.shape[1] // (2 * line)), *more[1:])
    else:
        gsh_ref = gsh_out
    exchange = Exchange(place, per, held, near, far, total, e_sems)
    spread = Spread(place, per, stage, dhb_ref, s_sems)
    pairs = Pairs(place, per, b_held, b_near, b_sems)
    tile = 256

    @pl.when(i == 0)
    def _():
        place.greet(True, bool(line))
        dg_ref[...] = jnp.zeros_like(dg_ref)

    @pl.when(i < steps)
    def _():
        blocks = pair_of(i, per)
        places = [pl.ds(pl.multiple_of(s * SUB, SUB), SUB) for s in blocks]
        xn, dy = (jnp.concatenate([ref[at, :] for at in places], axis=0) for ref in (xn_ref, dy_ref))

        def keep(ref, values):
            for u, at in enumerate(places):
                ref[at, :] = values[u * SUB:(u + 1) * SUB]

        gu = dot(xn, we_ref[...])
        gate, up = gu[:, :units], gu[:, units:]
        sig = 1.0 / (1.0 + jnp.exp(-gate))
        silu = gate * sig
        a = (silu * up).astype(BF)
        keep(a_ref, a)
        da = dot(dy, ws_ref[...], 1, 1)
        dgu = jnp.concatenate([da * up * (sig * (1.0 + gate * (1.0 - sig))), da * silu], axis=1).astype(BF)
        keep(dgu_ref, dgu)
        part = dot(dgu, we_ref[...], 1, 1).astype(BF)
        for u, s in enumerate(blocks):
            held[s] = part[u * SUB:(u + 1) * SUB]
            exchange.out(s)
        part = dot(a, ws_ref[...]).astype(BF)
        for u, s in enumerate(blocks):
            b_held[s] = part[u * SUB:(u + 1) * SUB]
            pairs.out(s)

    def own_rows(s, k, summed):
        at = pl.ds(pl.multiple_of(k * SUB, SUB), SUB)
        pulled, gain_grad = rms_pull(h_ref[at, :], g2_ref[...], summed)
        dh = dy_ref[pl.ds(pl.multiple_of(s * SUB, SUB), SUB), :].astype(FP) + pulled
        dh_ref[at, :] = dh
        dg_ref[...] += fold_rows(gain_grad)
        stage[k] = dh.astype(BF)
        spread.send(s)

    def chip_rows(mine, k, summed):
        at = pl.ds(pl.multiple_of(k * SUB, SUB), SUB)

        @pl.when(mine)
        def _():
            base_ref[at, :] = h_ref[at, :] + summed

        @pl.when(jnp.logical_not(mine))
        def _():
            other_ref[k] = summed.astype(BF)

    def added(s):
        pairs.add(s, chip_rows)
        exchange.take(s, own_rows)

    in_turn(i, steps, per, (exchange.add, added, spread.pass_on))

    def tiles(grad_ref, left_ref, right_ref, first, count):
        def one(t, carry):
            cut = pl.ds(pl.multiple_of(t * tile, tile), tile)
            grad_ref[:, cut] = dot(left_ref[...], right_ref[:, cut], 0, 0).astype(grad_ref.dtype)
            return carry

        lax.fori_loop(first, first + count, one, 0)

    half = gex_ref.shape[1] // tile // 2

    @pl.when(i == steps)
    def _():
        tiles(gsh_ref, a_ref, dy_ref, 0, gsh_ref.shape[1] // tile)
        if line:
            shrink.start()

    @pl.when(i == steps + 1)
    def _():
        tiles(gex_ref, xn_ref, dgu_ref, 0, half)
        if line:
            shrink.step(1)

    @pl.when(i == steps + 2)
    def _():
        tiles(gex_ref, xn_ref, dgu_ref, half, half)
        if line:
            for k in range(2, line):
                shrink.step(k)
        exchange.drain()
        pairs.drain()
        if line:
            shrink.finish(gsh_out)
            shrink.drain()
        spread.finish()


def feed(xn, dy, we, ws, h, g2, line):
    length, d = xn.shape
    units = ws.shape[0]
    per = h.shape[0] // SUB
    steps = 2 * per
    more = []
    shrink = jax.ShapeDtypeStruct(ws.shape, BF)
    if line:
        shrink = jax.ShapeDtypeStruct((ws.shape[0], ws.shape[1] // (2 * line)), FP)
        more = [pltpu.VMEM(ws.shape, BF), *reduce_scratch(line, shrink.shape)]
    return pl.pallas_call(
        partial(feed_kernel, units, per, steps, line),
        grid=(steps + 3,),
        in_specs=[whole(xn.shape), whole(dy.shape), whole(we.shape), whole(ws.shape), whole(h.shape), whole(g2.shape)],
        out_specs=[whole(h.shape), whole((per, SUB, d)), whole(we.shape), whole(h.shape), ANYWHERE,
                   whole((8, d)), whole(shrink.shape)],
        out_shape=[jax.ShapeDtypeStruct(h.shape, FP), jax.ShapeDtypeStruct((per, SUB, d), BF),
                   jax.ShapeDtypeStruct(we.shape, BF), jax.ShapeDtypeStruct(h.shape, FP),
                   jax.ShapeDtypeStruct((length // SUB, SUB, d), BF), jax.ShapeDtypeStruct((8, d), FP), shrink],
        scratch_shapes=[pltpu.VMEM((length, units), BF), pltpu.VMEM((length, 2 * units), BF),
                        *exchange_scratch(per, d), *spread_scratch(per, d), pltpu.VMEM((4 * per, SUB, d), BF),
                        pltpu.VMEM((2 * per, SUB, d), BF), pltpu.SemaphoreType.DMA((2, 4 * per)), *more],
        compiler_params=params(collective_id=2, has_side_effects=True),
        name="feed",
    )(xn, dy, we, ws, h, g2)


def back_kernel(kv, group, unit, scale, blocks, per, line, *refs):
    refs = list(refs)
    take = lambda count: [refs.pop(0) for _ in range(count)]
    q_ref, k_ref, v_ref, kt_ref, tags_ref, bars_ref, lse_ref, ctx_block, dh_block, wm_ref = take(10)
    raw_ref, cos_ref, sin_ref, gq_ref, gk_ref, base_ref, other_ref = take(7)
    late_from = take(4)
    grads = take(1) if line else []
    part_ref, out_ref, gp_ref = take(3)
    gm_out = [] if line else take(1)
    gains_ref = take(1)[0]
    sums = take(2) if line else []
    late_to = take(4)
    wp_ref, ctx_ref, dh_ref, xn_ref = late_to
    late_sem = take(1)[0]
    late = [pltpu.make_async_copy(a, b, late_sem.at[w]) for w, (a, b) in enumerate(zip(late_from, late_to))]
    dk_ref, dv_ref, dq_ref, dqkv_ref = take(4)
    b_far, b_sems = take(2)
    place = Place(line)
    i = pl.program_id(0)
    b = blocks - 1 - i
    n = LANES
    tile = 256
    reduces = []
    if line:
        shards = 2 * line
        gm_ref = take(1)[0]
        for grad, cut in ((grads[0], row_cut(grads[0].shape[0] // shards)),
                          (gm_ref, column_cut(gm_ref.shape[1] // shards))):
            reduces.append(Reduce(place, grad, cut, *take(4)))
    else:
        gm_ref = gm_out[0]

    def tiles(grad_ref, left_ref, right_ref):
        def one(t, carry):
            cut = pl.ds(pl.multiple_of(t * tile, tile), tile)
            grad_ref[:, cut] = dot(left_ref[...], right_ref[:, cut], 0, 0).astype(grad_ref.dtype)
            return carry

        lax.fori_loop(0, grad_ref.shape[1] // tile, one, 0)

    def branch(k):
        return send(other_ref.at[k], b_far.at[k], b_sems.at[0, k], b_sems.at[1, k], place.chip)

    @pl.when(i == 0)
    def _():
        place.greet(True, bool(line))
        for r in reduces[:1]:
            r.start()
        for copy in late:
            copy.start()
        for k in range(per):
            branch(k).start()
        dk_ref[...] = jnp.zeros_like(dk_ref)
        dv_ref[...] = jnp.zeros_like(dv_ref)
        gains_ref[...] = jnp.zeros_like(gains_ref)

    @pl.when(i < blocks)
    def _():
        here = pl.ds(pl.multiple_of(b * ROWS, ROWS), ROWS)
        dctx = dot(dh_block[...], wm_ref[...], 1, 1).astype(BF)
        ctx, q = ctx_block[...], q_ref[...]
        bars = jnp.concatenate([bars_ref[...]] * group, axis=0)
        wide, queries, outward, centres, lses = [], [], [], [], []
        for h in range(kv):
            queries.append(stacked(q, h, group))
            wide.append(jnp.concatenate([queries[h], bars], axis=1))
            outward.append(stacked(dctx, h, group))
            both = outward[h].astype(FP) * stacked(ctx, h, group).astype(FP)
            centres.append(jnp.sum(both.T, axis=0, keepdims=True))
            lses.append(jnp.concatenate([lse_ref[u, h:h + 1, g * SUB:(g + 1) * SUB]
                                         for g in range(group) for u in range(ROWS // SUB)], axis=1))
        dq_ref[...] = jnp.zeros_like(dq_ref)

        def chunk(j, diagonal):
            at = pl.ds(pl.multiple_of(j * ROWS, ROWS), ROWS)
            tags = tags_ref[at, :]
            for h in range(kv):
                cut = slice(h * n, (h + 1) * n)
                keys = jnp.concatenate([k_ref[at, cut], tags], axis=1)
                p = jnp.exp2(dot(keys, wide[h], 1, 1) * unit - lses[h])
                if diagonal:
                    p = jnp.where(causal_tile(group), p, 0.0)
                dp = dot(v_ref[at, cut], outward[h], 1, 1)
                ds = (p * (dp - centres[h])).astype(BF)
                dv_ref[at, cut] += dot(p.astype(BF), outward[h])
                dk_ref[at, cut] += dot(ds, queries[h])
                dq_ref[h] += dot(kt_ref[cut, at], ds)

        lax.fori_loop(0, b, lambda j, c: (chunk(j, False), c)[1], 0)
        chunk(b, True)

        cosines, sines = cos_ref[...], sin_ref[...]
        pieces = []
        for h in range(kv):
            dq = dq_ref[h].T
            for c in range(group + 1):
                if c < group:
                    d, gain, row = dq[c * ROWS:(c + 1) * ROWS] * scale, gq_ref[...], 0
                else:
                    d, gain, row = dk_ref[here, h * n:(h + 1) * n] * scale, gk_ref[...], 1
                d = d * cosines - pltpu.roll(d, n // 2, 1) * sines
                at = (h * (group + 1) + c) * n
                piece, gain_grad = rms_pull(raw_ref[:, at:at + n], gain, d)
                gains_ref[row] += fold_rows(gain_grad)
                pieces.append(piece)
            pieces.append(dv_ref[here, h * n:(h + 1) * n])
        dqkv = jnp.concatenate(pieces, axis=1).astype(BF)
        dqkv_ref[here, :] = dqkv
        pl.when(i == 0)(late[0].wait)
        part_ref[...] = dot(dqkv, wp_ref[...], 1, 1).astype(BF)

    @pl.when(i == 3)
    def _():
        for k in range(per):
            branch(k).wait()
            at = slice(k * SUB, (k + 1) * SUB)
            out_ref[at, :] = (base_ref[at, :] + b_far[k].astype(FP)).astype(BF)

    @pl.when(i == 1)
    def _():
        late[1].wait()
        late[2].wait()
        tiles(gm_ref, ctx_ref, dh_ref)

    if line:
        expand, merge = reduces
        for step, act in enumerate((lambda: expand.step(1), lambda: expand.step(2), lambda: expand.step(3), merge.start,
                                    lambda: merge.step(1), lambda: merge.step(2))):
            pl.when(i == step)(act)

    @pl.when(i == blocks)
    def _():
        late[3].wait()
        tiles(gp_ref, xn_ref, dqkv_ref)
        if line:
            merge.step(3)
        for r, out in zip(reduces, sums):
            r.finish(out)
            r.drain()


def back(q, k, v, kt, tags, bars, lse, ctx, dh, wm, wp, raw, cosines, sines, gq, gk, xn,
         base, other, grads, kv, group, unit, scale, line):
    length = q.shape[0]
    n = LANES
    d = wm.shape[1]
    blocks = length // ROWS
    per = other.shape[0]
    block_of = lambda i: jnp.maximum(blocks - 1 - i, 0)
    rows = lambda w: pl.BlockSpec((ROWS, w), lambda i: (block_of(i), 0))
    late = [wp, ctx, dh, xn]
    scratch = [*[pltpu.VMEM(a.shape, BF) for a in late], pltpu.SemaphoreType.DMA((4,)),
               pltpu.VMEM((length, kv * n), FP), pltpu.VMEM((length, kv * n), FP),
               pltpu.VMEM((kv, n, ROWS * group), FP), pltpu.VMEM((length, wp.shape[1]), BF),
               pltpu.VMEM((per, SUB, d), BF), pltpu.SemaphoreType.DMA((2, per))]
    sums = []
    merge = [jax.ShapeDtypeStruct(wm.shape, BF)]
    if line:
        shards = 2 * line
        own = [(grads[0].shape[0] // shards, grads[0].shape[1]), (wm.shape[0], wm.shape[1] // shards)]
        sums = [jax.ShapeDtypeStruct(s, FP) for s in own]
        merge = []
        scratch += [pltpu.VMEM(wm.shape, BF)]
        for s in own:
            scratch += reduce_scratch(line, s)
    args = [q, k, v, kt, tags, bars, lse, ctx, dh, wm, raw, cosines, sines, gq, gk, base]
    specs = [whole(a.shape) for a in args] + [ANYWHERE] * (1 + len(late) + len(grads))
    for at in (0, 5, 7, 8, 10, 11, 12):
        specs[at] = rows(args[at].shape[1])
    specs[6] = pl.BlockSpec((ROWS // SUB, 8, SUB * group), lambda i: (block_of(i), 0, 0))
    return pl.pallas_call(
        partial(back_kernel, kv, group, unit, scale, blocks, per, line),
        grid=(blocks + 1,),
        in_specs=specs,
        out_specs=[rows(d), whole(base.shape), whole(wp.shape), *[whole(s.shape) for s in merge], whole((2, 8, n))]
                  + [whole(s.shape) for s in sums],
        out_shape=[jax.ShapeDtypeStruct((length, d), BF), jax.ShapeDtypeStruct(base.shape, BF),
                   jax.ShapeDtypeStruct(wp.shape, BF), *merge, jax.ShapeDtypeStruct((2, 8, n), FP), *sums],
        scratch_shapes=scratch,
        compiler_params=params(collective_id=3, has_side_effects=True),
        name="back",
    )(*args, other, *late, *grads)


def last_kernel(line, per, part_ref, x_ref, dh_ref, g1_ref, dg2_ref, head_ref, *refs):
    refs = list(refs)
    take = lambda count: [refs.pop(0) for _ in range(count)]
    grads = take(1) if line else []
    in_ref, all_ref = take(2)
    sums = take(1) if line else []
    exchange_refs = take(4)
    place = Place(line)
    exchange = Exchange(place, per, part_ref, *exchange_refs)
    d = x_ref.shape[1]
    n = LANES
    reduces, others = [], []
    if line:
        shards = 2 * line
        for grad, cut in zip(grads, (row_cut(grads[0].shape[0] // shards),)):
            reduces.append(Reduce(place, grad, cut, *take(4)))
        near, far, over, lined, g_sems = take(5)
        for step in range(1, line):
            z = (place.z + step) % line
            others.append((z * 2 + place.y, place.t))
    barrier = pltpu.get_barrier_semaphore()
    partners = [place.sibling, place.chip] + ([place.across] if line else []) + others
    for device in partners:
        pl.semaphore_signal(barrier, inc=1, device_id=device, device_id_type=MESH)
    pl.semaphore_wait(barrier, len(partners))
    for r in reduces:
        r.start()

    def each(act):
        lax.fori_loop(0, 4 * per, lambda s, c: (act(s), c)[1], 0)

    def hop(k):
        for r in reduces:
            r.advance(k)
        for r in reduces:
            r.hop(k)

    each(exchange.out)
    all_ref[:, :d] = jnp.zeros((8, d), FP)
    all_ref[:, d:2 * d] = dg2_ref[...]
    all_ref[:, 2 * d:2 * d + n] = head_ref[0]
    all_ref[:, 2 * d + n:] = head_ref[1]
    each(exchange.add)
    hop(1)
    hop(2)

    def input_rows(s, k, summed):
        at = pl.ds(pl.multiple_of(k * SUB, SUB), SUB)
        pulled, gain_grad = rms_pull(x_ref[at, :].astype(FP), g1_ref[...], summed)
        in_ref[at, :] = (dh_ref[at, :] + pulled).astype(BF)
        all_ref[:, :d] += fold_rows(gain_grad)

    each(lambda s: exchange.take(s, input_rows))
    exchange.drain()
    if not line:
        return
    copies = []

    def swap(turn, buffer, device):
        source = lined.at[line + turn]
        source[...] = all_ref[...]
        copy = send(source, buffer, g_sems.at[0, turn], g_sems.at[1, turn], device)
        copy.start()
        copy.wait_recv()
        all_ref[...] = source[...] + buffer[...]
        copies.append(copy)

    swap(0, near, place.sibling)
    swap(1, far, place.chip)
    hop(3)
    swap(2, over, place.across)
    lined[place.z] = all_ref[...]
    for step in range(1, line):
        copy = send(lined.at[place.z], lined.at[place.z], g_sems.at[0, 2 + step], g_sems.at[1, 2 + step],
                    others[step - 1])
        copy.start()
        copies.append(copy)
    for r, out in zip(reduces, sums):
        r.finish(out)
    for step in range(1, line):
        z = (place.z - step + line) % line
        send(lined.at[z], lined.at[z], g_sems.at[0, 2 + step], g_sems.at[1, 2 + step], place.sibling).wait_recv()
    all_sum = lined[0]
    for z in range(1, line):
        all_sum = all_sum + lined[z]
    all_ref[...] = all_sum
    for r in reduces:
        r.drain()
    for copy in copies:
        copy.wait_send()


def last(part, x_own, dh, g1, dg2, heads, grads, line):
    d = x_own.shape[1]
    per = x_own.shape[0] // SUB
    gains = (8, 2 * d + 2 * LANES)
    vmem = pl.BlockSpec(memory_space=pltpu.VMEM)
    args = [part.reshape(4 * per, SUB, d), x_own, dh, g1, dg2, heads, *grads]
    scratch = [*exchange_scratch(per, d, held=False)]
    own = []
    if line:
        shards = 2 * line
        own = [(grads[0].shape[0] // shards, grads[0].shape[1])]
        for s in own:
            scratch += reduce_scratch(line, s)
        scratch += [*[pltpu.VMEM(gains, FP)] * 3, pltpu.VMEM((line + 3, *gains), FP),
                    pltpu.SemaphoreType.DMA((2, 2 + line))]
    return pl.pallas_call(
        partial(last_kernel, line, per),
        in_specs=[vmem] * 6 + [ANYWHERE] * len(grads),
        out_specs=[vmem] * (2 + len(own)),
        out_shape=[jax.ShapeDtypeStruct(x_own.shape, BF), jax.ShapeDtypeStruct(gains, FP),
                   *[jax.ShapeDtypeStruct(s, FP) for s in own]],
        scratch_shapes=scratch,
        compiler_params=params(collective_id=4, has_side_effects=True),
        name="last",
    )(*args)


def adamw_step(weight, moment_one, moment_two, gradient, step_rate, decay):
    mean_next = BETA_ONE * moment_one + (1.0 - BETA_ONE) * gradient
    square_next = BETA_TWO * moment_two + (1.0 - BETA_TWO) * gradient * gradient
    mean_hat = mean_next / (1.0 - BETA_ONE**STEP)
    square_hat = square_next / (1.0 - BETA_TWO**STEP)
    weight_next = weight - step_rate * (mean_hat / (jnp.sqrt(square_hat) + EPS_ADAM) + decay * weight)
    return weight_next, mean_next, square_next


def tree_tables(segments, parent_row):
    count = parent_row.shape[0]
    length = segments.shape[0]
    labels = jnp.arange(count, dtype=jnp.int32)
    onehot = segments[:, None] == labels[None, :]
    sizes = jnp.sum(onehot.astype(FP), axis=0)
    starts = jnp.cumsum(sizes) - sizes
    reach = (labels[:, None] == labels[None, :]) | (parent_row[:, None] == labels[None, :]) | (labels[None, :] == 0)
    proper = reach & (labels[:, None] != labels[None, :])
    offsets = jnp.sum(jnp.where(proper, sizes[None, :], 0.0), axis=1)
    position = jnp.arange(length).astype(FP) + jnp.sum(jnp.where(onehot, (offsets - starts)[None, :], 0.0), axis=1)
    parent = jnp.sum(jnp.where(onehot, parent_row[None, :], 0), axis=1)
    lanes = jnp.arange(LANES, dtype=jnp.int32)
    tags = (segments[:, None] == lanes[None, :]).astype(BF)
    seen = (lanes[None, :] == segments[:, None]) | (lanes[None, :] == parent[:, None]) | (lanes[None, :] == 0)
    bars = jnp.where(seen | (lanes[None, :] >= count), 0.0, BLOCKED).astype(BF)
    half = lanes % (LANES // 2)
    frequency = THETA ** (-half.astype(FP) * 2.0 / LANES)
    angles = position[:, None] * frequency[None, :]
    sines = jnp.where(lanes[None, :] < LANES // 2, -jnp.sin(angles), jnp.sin(angles))
    return tags, bars, jnp.cos(angles), sines


def shards(
    tokens, cotangent, parents, token_segment, tree_id,
    projection_weight, projection_first_moment, projection_second_moment,
    merge_master, merge_mean, merge_square,
    expand_master, expand_mean, expand_square,
    shrink_master, shrink_mean, shrink_square,
    gain_master, gain_mean, gain_square,
):
    parts = lax.axis_size("tensor")
    part = lax.axis_index("tensor")
    x = tokens[0]
    dy = cotangent[0]
    length, d = x.shape
    share = length // parts
    first = part * share
    d_own, kv, per, n = projection_weight.shape
    group = per - 2
    units = expand_master.shape[2]
    scale = n ** (-0.5)
    unit = scale * math.log2(math.e)

    dp = lax.axis_size("dp")
    line = 4 if dp == 8 and d_own % LANES == 0 else 0
    low = (
        projection_weight.astype(BF).reshape(d_own, kv * per * n),
        merge_master.astype(BF),
        expand_master.astype(BF).reshape(d_own, 2 * units),
        shrink_master.astype(BF),
    )
    if not line:
        wp, we = (lax.all_gather(low[w], "dp", axis=0, tiled=True) for w in (0, 2))
        wm, ws = (lax.all_gather(low[w], "dp", axis=1, tiled=True) for w in (1, 3))

    chosen = (jnp.arange(parents.shape[0], dtype=jnp.int32) == tree_id[0]).astype(jnp.int32)
    parent_row = jnp.sum(parents * chosen[:, None], axis=0)
    tags, bars, cosines, sines = tree_tables(token_segment[0], parent_row)
    g1, g2 = gain_master[None, :d], gain_master[None, d:2 * d]
    gq, gk = gain_master[None, 2 * d:2 * d + n], gain_master[None, 2 * d + n:]
    x_own = lax.dynamic_slice_in_dim(x, first, share, 0)

    fronts = front(x, g1, gq, gk, cosines, sines, low[:2] if line else (wp,), kv, group, line)
    xn1, q, k, v, kt, vt, raw = fronts[:7]
    if line:
        wp, wm = fronts[7:]
    attends = attend(q, k, vt, tags, bars, wm, x_own, g2, low[2:] if line else (), kv, group, unit, line)
    ctx, lse, hidden, xn2 = attends[:4]
    if line:
        we, ws = attends[4:]
    base, other, expand_grad, dh, dhb, dg2, shrink_sum = feed(xn2.reshape(length, d), dy, we, ws, hidden, g2, line)
    backs = back(q, k, v, kt, tags, bars, lse, ctx, dhb.reshape(length, d), wm, wp, raw, cosines, sines, gq, gk, xn1,
                 base, other, (expand_grad,) if line else (), kv, group, unit, scale, line)
    partial_x, output, project_grad = backs[:3]
    head_gains = backs[3 if line else 4]
    lasts = last(partial_x, x_own, dh, g1, dg2, head_gains, (project_grad,) if line else (), line)
    input_grad, gains = lasts[:2]
    if line:
        expand_sum, merge_sum = backs[4:]
        project_sum = lasts[2]
    else:
        gains = lax.psum(gains, ("dp", "tensor"))
        project_sum, expand_sum = (
            lax.psum_scatter(g, "dp", scatter_dimension=0, tiled=True) for g in (project_grad, expand_grad))
        merge_sum, shrink_sum = (
            lax.psum_scatter(g, "dp", scatter_dimension=1, tiled=True) for g in (backs[3], shrink_sum))
    output, input_grad = output[None], input_grad[None]
    gain_grad = jnp.sum(gains, axis=0)

    outs = [output, input_grad]
    for weight, mean, square, grad, rate in (
        (projection_weight, projection_first_moment, projection_second_moment, project_sum, RATE_PROJECT),
        (merge_master, merge_mean, merge_square, merge_sum, RATE_MERGE),
        (expand_master, expand_mean, expand_square, expand_sum, RATE_EXPAND),
        (shrink_master, shrink_mean, shrink_square, shrink_sum, RATE_SHRINK),
    ):
        grad = grad.astype(FP).reshape(weight.shape)
        after, mean_next, square_next = adamw_step(weight, mean, square, grad, rate, DECAY)
        outs += [after, mean_next, square_next, after.astype(BF)]
    gain_next, gain_mean_next, gain_square_next = adamw_step(
        gain_master, gain_mean, gain_square, gain_grad, RATE_GAIN, 0.0)
    return (*outs, gain_mean_next, gain_square_next, gain_next)


def solution(mesh):
    tokens = P("dp", None, None)
    project = P("dp", "tensor", None, None)
    columns = P("tensor", "dp")
    expand = P("dp", None, "tensor")
    shared = P("dp", "tensor", None)
    return jax.shard_map(
        shards,
        mesh=mesh,
        in_specs=(tokens, tokens, P(), P("dp", None), P("dp"), *[project] * 3, *[columns] * 3, *[expand] * 3,
                  *[columns] * 3, P(), P(), P()),
        out_specs=(shared, shared, *[project] * 4, *[columns] * 4, *[expand] * 4, *[columns] * 4, P(), P(), P()),
        check_vma=False,
    )
```

```python
import math
from functools import partial

import jax
import jax.numpy as jnp
import numpy as np
from jax import lax
from jax.experimental import pallas as pl
from jax.experimental.pallas import tpu as pltpu
from jax.sharding import PartitionSpec as P

STEP = 5
EPS_NORM = 1e-06
THETA = 1000000.0
BETA_ONE = 0.5
BETA_TWO = 0.5
EPS_ADAM = 1e-08
DECAY = 0.1
RATE_PROJECT = 0.05
RATE_MERGE = 0.3
RATE_EXPAND = 0.05
RATE_SHRINK = 0.03
RATE_GAIN = 0.3

BF = jnp.bfloat16
FP = jnp.float32
ROWS = 256
LANES = 128
SUB = 128
MESH = pl.DeviceIdType.MESH
BLOCKED = -1e30
VMEM_LIMIT = 60 * 2**20


def params(**more):
    return pltpu.CompilerParams(vmem_limit_bytes=VMEM_LIMIT, **more)


def dot(a, b, ca=1, cb=0):
    return lax.dot_general(a, b, (((ca,), (cb,)), ((), ())), preferred_element_type=FP)


def inverse_rms(values):
    return lax.rsqrt(jnp.mean(values * values, axis=-1, keepdims=True) + EPS_NORM)


def rms_pull(values, scales, grad):
    r = inverse_rms(values)
    scaled = grad * scales
    mean = jnp.mean(values * scaled, axis=-1, keepdims=True)
    return r * scaled - values * (r * r * r * mean), grad * values * r


def fold_rows(values):
    n, w = values.shape
    return jnp.sum(values.reshape(n // 8, 8, w), axis=0)


class Place:
    def __init__(self, line):
        self.line = line
        self.dp, self.t = lax.axis_index("dp"), lax.axis_index("tensor")
        self.z, self.y = self.dp // 2, self.dp % 2
        self.x, self.c = self.t // 2, self.t % 2
        self.has_up, self.has_down = self.z < line - 1, self.z > 0
        self.up, self.down = (self.dp + 2, self.t), (self.dp - 2, self.t)
        self.across = (self.dp + 1 - 2 * self.y, self.t)
        self.sibling = (self.dp, self.t + 1 - 2 * self.c)
        self.chip = (self.dp, (1 - self.x) * 2 + self.c)

    def greet(self, tensor, line, meanwhile=None):
        barrier = pltpu.get_barrier_semaphore()

        def signal(device):
            pl.semaphore_signal(barrier, inc=1, device_id=device, device_id_type=MESH)

        if tensor:
            signal(self.sibling)
            signal(self.chip)
        if line:
            signal(self.across)
            pl.when(self.has_up)(lambda: signal(self.up))
            pl.when(self.has_down)(lambda: signal(self.down))
        peers = (2 if tensor else 0) + (1 if line else 0)
        if line:
            peers = peers + jnp.where(self.has_up, 1, 0) + jnp.where(self.has_down, 1, 0)
        if meanwhile is not None:
            meanwhile()
        pl.semaphore_wait(barrier, peers)


def send(src, dst, sent, arrived, device):
    return pltpu.make_async_remote_copy(
        src_ref=src, dst_ref=dst, send_sem=sent, recv_sem=arrived, device_id=device, device_id_type=MESH)


def row_cut(size):
    return lambda j: (pl.ds(pl.multiple_of(j * size, size), size), slice(None))


def column_cut(size):
    return lambda j: (slice(None), pl.ds(pl.multiple_of(j * size, size), size))


class Gather:
    def __init__(self, place, own, full, cut, sems, local):
        self.place, self.own, self.full, self.cut, self.sems, self.local = place, own, full, cut, sems, local

    def copy(self, kind, src, j):
        p = self.place
        device = (p.up, p.down, p.across)[kind]
        return send(src, self.full.at[self.cut(j)], self.sems.at[kind, j], self.sems.at[3, j], device)

    def kept(self):
        return pltpu.make_async_copy(self.own, self.full.at[self.cut(self.place.dp)], self.local)

    def source(self):
        return self.full.at[self.cut(self.place.dp)] if self.own is None else self.own

    def start(self):
        p = self.place
        self.copy(2, self.source(), p.dp).start()
        pl.when(p.has_up)(lambda: self.copy(0, self.source(), p.dp).start())
        pl.when(p.has_down)(lambda: self.copy(1, self.source(), p.dp).start())
        if self.own is not None:
            self.kept().start()

    def arrivals(self, k):
        p = self.place
        return ((0, p.z >= k, (p.z - k) * 2 + p.y, p.has_up), (1, p.z + k < p.line, (p.z + k) * 2 + p.y, p.has_down))

    def hop(self, k):
        for kind, here, j, further in self.arrivals(k):
            @pl.when(here)
            def _(kind=kind, j=j, further=further):
                piece = self.full.at[self.cut(j)]
                self.copy(kind, piece, j).wait_recv()
                pl.when(further)(lambda: self.copy(kind, piece, j).start())
                self.copy(2, piece, j).start()

    def finish(self):
        p = self.place
        if self.own is not None:
            self.kept().wait()
        for zz in range(p.line):
            j = zz * 2 + 1 - p.y
            self.copy(2, self.full.at[self.cut(j)], j).wait_recv()

    def drain(self):
        p = self.place
        self.copy(2, self.source(), p.dp).wait_send()
        pl.when(p.has_up)(lambda: self.copy(0, self.source(), p.dp).wait_send())
        pl.when(p.has_down)(lambda: self.copy(1, self.source(), p.dp).wait_send())
        for k in range(1, p.line):
            for kind, here, j, further in self.arrivals(k):
                @pl.when(here)
                def _(kind=kind, j=j, further=further):
                    piece = self.full.at[self.cut(j)]
                    pl.when(further)(lambda: self.copy(kind, piece, j).wait_send())
                    self.copy(2, piece, j).wait_send()


class Reduce:
    def __init__(self, place, grad, cut, kept, across, lined, sems):
        self.place, self.grad, self.cut, self.kept, self.sems = place, grad, cut, kept, sems
        self.across, self.lined = across, lined

    def cross(self, zz):
        p = self.place
        return send(self.grad.at[self.cut(zz * 2 + 1 - p.y)], self.across.at[zz],
                    self.sems.at[0, zz], self.sems.at[1, zz], p.across)

    def climb(self, t):
        return send(self.across.at[t], self.lined.at[t + 1], self.sems.at[2, t], self.sems.at[3, t], self.place.up)

    def sink(self, t):
        return send(self.across.at[t], self.lined.at[t], self.sems.at[4, t], self.sems.at[5, t], self.place.down)

    def load(self, zz):
        return pltpu.make_async_copy(self.grad.at[self.cut(zz * 2 + self.place.y)], self.kept.at[zz], self.sems.at[6, zz])

    def mine(self, zz):
        return self.kept[zz].astype(FP)

    def turn(self, q):
        z = self.place.z
        low = z < 2
        if q == 0:
            return jnp.where(low, 3, 0)
        if q == 1:
            return jnp.where(low, 2, 1)
        if q == 2:
            return jnp.where(low, 1 - z, 5 - z)
        return z

    def start(self):
        self.cross(self.turn(0)).start()
        for zz in range(self.place.line):
            self.load(zz).start()

    def advance(self, q):
        self.cross(self.turn(q - 1)).wait_send()
        self.cross(self.turn(q)).start()

    def hop(self, h):
        p = self.place

        def pass_on(t, coming, more, slot):
            self.load(t).wait()
            self.cross(t).wait_recv()

            @pl.when(jnp.logical_not(more))
            def _():
                self.across[t] = (self.mine(t) + self.across[t].astype(FP)).astype(BF)

            @pl.when(more)
            def _():
                coming(t).wait_recv()
                self.across[t] = (self.mine(t) + self.across[t].astype(FP) + self.lined[slot].astype(FP)).astype(BF)

            coming(t).start()

        pl.when(p.z < h)(lambda: pass_on(p.z + p.line - h, self.climb, p.has_down, p.z + p.line - h + 1))
        pl.when(p.z >= p.line - h)(lambda: pass_on(p.z - p.line + h, self.sink, p.has_up, p.z - p.line + h))

    def finish(self, out):
        p = self.place
        self.load(p.z).wait()
        self.cross(p.z).wait_recv()
        out[...] = self.mine(p.z) + self.across[p.z].astype(FP)

        @pl.when(p.has_down)
        def _():
            self.climb(p.z).wait_recv()
            out[...] += self.lined[p.z + 1].astype(FP)

        @pl.when(p.has_up)
        def _():
            self.sink(p.z).wait_recv()
            out[...] += self.lined[p.z].astype(FP)

    def step(self, k):
        self.advance(k)
        self.hop(k)

    def drain(self):
        p = self.place
        self.cross(p.z).wait_send()
        for zz in range(p.line):
            pl.when(zz > p.z)(lambda zz=zz: self.climb(zz).wait_send())
            pl.when(zz < p.z)(lambda zz=zz: self.sink(zz).wait_send())


def reduce_scratch(line, shape):
    return [pltpu.VMEM((line, *shape), BF), pltpu.VMEM((line, *shape), BF), pltpu.VMEM((line + 1, *shape), BF),
            pltpu.SemaphoreType.DMA((7, line))]


class Exchange:
    def __init__(self, place, per, held, near, far, total, sems):
        self.place, self.per, self.held, self.near, self.far = place, per, held, near, far
        self.total, self.sems = total, sems

    def owner(self, s):
        t = s // self.per
        return t // 2, t % 2

    def to_sibling(self, s):
        slot = (s // (2 * self.per)) * self.per + s % self.per
        return send(self.held.at[s], self.near.at[slot], self.sems.at[0, s], self.sems.at[1, s], self.place.sibling)

    def to_chip(self, s):
        slot = (s // (2 * self.per)) * self.per + s % self.per
        return send(self.near.at[slot], self.far.at[s % self.per], self.sems.at[2, s], self.sems.at[3, s],
                    self.place.chip)

    def out(self, s):
        pl.when(self.place.c != self.owner(s)[1])(lambda: self.to_sibling(s).start())

    def add(self, s):
        p = self.place
        ox, oc = self.owner(s)
        slot = (s // (2 * self.per)) * self.per + s % self.per

        @pl.when(p.c == oc)
        def _():
            self.to_sibling(s).wait_recv()

            @pl.when(p.x != ox)
            def _():
                self.near[slot] = (self.held[s].astype(FP) + self.near[slot].astype(FP)).astype(BF)
                self.to_chip(s).start()

            @pl.when(p.x == ox)
            def _():
                self.total[s % self.per] = self.held[s].astype(FP) + self.near[slot].astype(FP)

    def take(self, s, use):
        p = self.place

        @pl.when(s // self.per == p.t)
        def _():
            k = s % self.per
            self.to_chip(s).wait_recv()
            use(s, k, self.total[k] + self.far[k].astype(FP))

    def drain(self):
        p = self.place

        def one(s, carry):
            ox, oc = self.owner(s)
            pl.when(p.c != oc)(lambda: self.to_sibling(s).wait_send())
            pl.when(jnp.logical_and(p.c == oc, p.x != ox))(lambda: self.to_chip(s).wait_send())
            return carry

        lax.fori_loop(0, 4 * self.per, one, 0)


class Pairs:
    def __init__(self, place, per, held, near, sems):
        self.place, self.per, self.held, self.near, self.sems = place, per, held, near, sems

    def copy(self, s):
        slot = (s // (2 * self.per)) * self.per + s % self.per
        return send(self.held.at[s % self.held.shape[0]], self.near.at[slot], self.sems.at[0, s], self.sems.at[1, s],
                    self.place.sibling)

    def sends(self, s):
        return self.place.c != (s // self.per) % 2

    def out(self, s):
        pl.when(self.sends(s))(lambda: self.copy(s).start())

    def sent(self, s):
        pl.when(self.sends(s))(lambda: self.copy(s).wait_send())

    def add(self, s, use):
        t = s // self.per
        slot = (s // (2 * self.per)) * self.per + s % self.per

        @pl.when(self.place.c == t % 2)
        def _():
            self.copy(s).wait_recv()
            use(self.place.x == t // 2, s % self.per,
                self.held[s % self.held.shape[0]].astype(FP) + self.near[slot].astype(FP))

    def drain(self):
        def one(s, carry):
            self.sent(s)
            return carry

        lax.fori_loop(0, 4 * self.per, one, 0)


def pair_of(step, per):
    t = step % 2
    return t * per + step // 2, (3 - t) * per + step // 2


def exchange_scratch(per, d, held=True):
    return [pltpu.VMEM((4 * per, SUB, d), BF)] * held + [pltpu.VMEM((2 * per, SUB, d), BF), pltpu.VMEM((per, SUB, d), BF), pltpu.VMEM((per, SUB, d), FP),
                   pltpu.SemaphoreType.DMA((4, 4 * per))]


class Spread:
    def __init__(self, place, per, stage, full, sems):
        self.place, self.per, self.stage, self.full, self.sems = place, per, stage, full, sems

    def copy(self, kind, src, s):
        device = (self.place.chip, self.place.sibling)[kind]
        return send(src, self.full.at[s], self.sems.at[kind, s], self.sems.at[2, s], device)

    def kept(self, s):
        return pltpu.make_async_copy(self.stage.at[s % self.per], self.full.at[s], self.sems.at[3, s])

    def send(self, s):
        for kind in (0, 1):
            self.copy(kind, self.stage.at[s % self.per], s).start()
        self.kept(s).start()

    def passes(self, s):
        t = s // self.per
        return jnp.logical_and(self.place.c == t % 2, self.place.x != t // 2)

    def pass_on(self, s):
        @pl.when(self.passes(s))
        def _():
            self.copy(1, self.full.at[s], s).wait_recv()
            self.copy(1, self.full.at[s], s).start()

    def finish(self):
        def one(s, carry):
            @pl.when(s // self.per == self.place.t)
            def _():
                self.copy(0, self.stage.at[s % self.per], s).wait_send()
                self.copy(1, self.stage.at[s % self.per], s).wait_send()
                self.kept(s).wait()

            pl.when(self.passes(s))(lambda: self.copy(1, self.full.at[s], s).wait_send())
            pl.when((s // self.per) % 2 != self.place.c)(lambda: self.copy(1, self.full.at[s], s).wait_recv())
            return carry

        lax.fori_loop(0, 4 * self.per, one, 0)


def spread_scratch(per, d):
    return [pltpu.VMEM((per, SUB, d), BF), pltpu.SemaphoreType.DMA((4, 4 * per))]


def whole(shape):
    return pl.BlockSpec(tuple(shape), lambda i: (0,) * len(shape), pipeline_mode=pl.Buffered(1))


ANYWHERE = pl.BlockSpec(memory_space=pl.ANY)
GATHER_SEMS = lambda shards: [pltpu.SemaphoreType.DMA((4, shards)), pltpu.SemaphoreType.DMA]


def make_tables(seg_ref, parents_ref, tree_ref, freq_ref, tags_ref, bars_ref, cos_ref, sin_ref):
    count = parents_ref.shape[1]
    n = LANES
    blocks = sin_ref.shape[0] // ROWS
    lane = lax.broadcasted_iota(jnp.int32, (1, n), 1).astype(FP)
    place_of = lambda b: pl.ds(pl.multiple_of(b * ROWS, ROWS), ROWS)

    def columns(b, carry):
        sin_ref[place_of(b), :] = jnp.broadcast_to(seg_ref[:, place_of(b)].astype(FP), (n, ROWS)).T
        return carry

    def tally(b, carry):
        column = sin_ref[place_of(b), :]
        return (carry[0] + fold_rows(jnp.where(column == lane, 1.0, 0.0)),
                carry[1] + fold_rows(jnp.where(column < lane, 1.0, 0.0)))

    lax.fori_loop(0, blocks, columns, 0)
    sizes, starts = lax.fori_loop(0, blocks, tally, (jnp.zeros((8, n), FP), jnp.zeros((8, n), FP)))
    sizes, starts = (jnp.sum(a, axis=0, keepdims=True) for a in (sizes, starts))
    table = parents_ref[...]
    chosen = jnp.where(lax.broadcasted_iota(jnp.int32, table.shape, 0) == tree_ref[0], table, 0)
    chosen = jnp.sum(chosen.astype(FP), axis=0, keepdims=True)
    parents = jnp.zeros((1, n), FP)
    for b in range(count):
        parents = jnp.where(lane == b, chosen[:, b:b + 1], parents)
    shifts = jnp.where(lane != 0, sizes[:, :1], 0.0) - starts

    def rows(b, carry):
        at = place_of(b)
        column = sin_ref[at, :]
        hot = column == lane
        parent = jnp.sum(jnp.where(hot, parents, 0.0), axis=1, keepdims=True)
        above = jnp.where(jnp.logical_and(lane == parent, lane != 0), sizes, 0.0)
        first = (b * ROWS).astype(FP)
        position = (lax.broadcasted_iota(jnp.int32, (ROWS, 1), 0).astype(FP) + first
                    + jnp.sum(jnp.where(hot, shifts, 0.0) + above, axis=1, keepdims=True))
        tags_ref[at, :] = jnp.where(hot, 1.0, 0.0).astype(BF)
        open_to = jnp.logical_or(jnp.logical_or(hot, lane == parent), jnp.logical_or(lane == 0, lane >= count))
        bars_ref[at, :] = jnp.where(open_to, 0.0, BLOCKED).astype(BF)
        angles = position * freq_ref[...]
        cos_ref[at, :] = jnp.cos(angles)
        turned = jnp.sin(angles)
        sin_ref[at, :] = jnp.where(lane < n // 2, -turned, turned)
        return carry

    lax.fori_loop(0, blocks, rows, 0)


def front_kernel(kv, group, line, *refs):
    refs = list(refs)
    take = lambda count: [refs.pop(0) for _ in range(count)]
    x_ref, gains_ref, seg_ref, parents_ref, tree_ref, freq_ref = take(6)
    masters = take(4) if line else take(1)
    xn_ref, q_ref, k_ref, v_ref, kt_ref, vt_ref, raw_ref, tags_ref, bars_ref, cos_ref, sin_ref = take(11)
    if line:
        wp_out, wm_out, we_low, ws_low = take(4)
        wp_ref, wm_low, p_sems, p_local, m_sems, m_local, out_sem = take(7)
    else:
        wp_ref = masters[0]
    xn_full, xn_sem = take(2)
    i = pl.program_id(0)
    final = pl.num_programs(0) - 1
    d = x_ref.shape[1]
    n = LANES
    per = group + 2
    if line:
        place = Place(line)
        size = masters[0].shape[0]
        project = Gather(place, None, wp_ref, row_cut(size), p_sems, p_local)
        merge = Gather(place, wm_low, wm_out, column_cut(wm_low.shape[1]), m_sems, m_local)
        written = pltpu.make_async_copy(wp_ref, wp_out, out_sem)
    normed = pltpu.make_async_copy(xn_full, xn_ref, xn_sem)

    def round_projection():
        at = pl.ds(pl.multiple_of(place.dp * size, size), size)
        for j in range(kv * per):
            wp_ref[at, j * n:(j + 1) * n] = masters[0][:, j, :].astype(BF)

    def norm(b, carry):
        at = pl.ds(pl.multiple_of(b * ROWS, ROWS), ROWS)
        x = x_ref[at, :].astype(FP)
        xn_full[at, :] = (x * inverse_rms(x) * gains_ref[:, :d]).astype(BF)
        return carry

    @pl.when(i == 0)
    def _():
        if line:
            place.greet(False, True, round_projection)
            project.start()
        lax.fori_loop(0, x_ref.shape[0] // ROWS, norm, 0)
        normed.start()
        if line:
            project.hop(1)
        make_tables(seg_ref, parents_ref, tree_ref, freq_ref, tags_ref, bars_ref, cos_ref, sin_ref)
        if line:
            project.hop(2)
            wm_low[...] = masters[1][...].astype(BF)
            units = masters[2].shape[2]
            for half in range(2):
                we_low[:, half * units:(half + 1) * units] = masters[2][:, half, :].astype(BF)
            ws_low[...] = masters[3][...].astype(BF)
            project.hop(3)
            merge.start()
            project.finish()
            written.start()

    if line:
        for k in range(1, line):
            pl.when(i == k + 1)(lambda k=k: merge.hop(k))
    at = pl.ds(pl.multiple_of(i * ROWS, ROWS), ROWS)
    qkv = dot(xn_full[at, :], wp_ref[...])
    cosines, sines = cos_ref[at, :], sin_ref[at, :]
    gq, gk = gains_ref[:, 2 * d:2 * d + n], gains_ref[:, 2 * d + n:]
    keys, values = [], []
    for h in range(kv):
        for c in range(group + 1):
            raw = qkv[:, (h * per + c) * n:(h * per + c + 1) * n]
            to = (h * (group + 1) + c) * n
            raw_ref[:, to:to + n] = raw
            y = raw * inverse_rms(raw) * (gq if c < group else gk)
            turned = y * cosines + pltpu.roll(y, n // 2, 1) * sines
            if c < group:
                to = (h * group + c) * n
                q_ref[:, to:to + n] = turned.astype(BF)
            else:
                keys.append(turned)
        values.append(qkv[:, (h * per + group + 1) * n:(h * per + group + 2) * n])
    for h in range(kv):
        k_ref[:, h * n:(h + 1) * n] = keys[h].astype(BF)
        v_ref[:, h * n:(h + 1) * n] = values[h].astype(BF)
        kt_ref[h * n:(h + 1) * n, :] = keys[h].T.astype(BF)
        vt_ref[h * n:(h + 1) * n, :] = values[h].T.astype(BF)

    @pl.when(i == final)
    def _():
        normed.wait()
        if line:
            merge.finish()
            merge.drain()
            project.drain()
            written.wait()


def front(x, gains, segments, parents, tree, masters, kv, group, line):
    length, d = x.shape
    n = LANES
    rows = lambda w: pl.BlockSpec((ROWS, w), lambda i: (i, 0))
    cols = pl.BlockSpec((kv * n, ROWS), lambda i: (0, i))
    out = lambda w, t: jax.ShapeDtypeStruct((length, w), t)
    raw_w = kv * (group + 1) * n
    freq = np.float32(THETA ** (-(np.arange(n) % (n // 2)) * 2.0 / n))[None]
    more_specs, more_shapes, scratch = [], [], []
    if line:
        shards = 2 * line
        project, merge, expand, shrink = (m.shape for m in masters)
        wp_shape = (project[0] * shards, project[1] * n)
        more_shapes = [jax.ShapeDtypeStruct(wp_shape, BF), jax.ShapeDtypeStruct((merge[0], merge[1] * shards), BF),
                       jax.ShapeDtypeStruct((expand[0], 2 * expand[2]), BF), jax.ShapeDtypeStruct(shrink, BF)]
        more_specs = [ANYWHERE, ANYWHERE, whole(more_shapes[2].shape), whole(more_shapes[3].shape)]
        scratch = [pltpu.VMEM(wp_shape, BF), pltpu.VMEM(merge, BF), *GATHER_SEMS(shards), *GATHER_SEMS(shards),
                   pltpu.SemaphoreType.DMA]
    table = whole((length, n))
    return pl.pallas_call(
        partial(front_kernel, kv, group, line),
        grid=(length // ROWS,),
        in_specs=[whole(x.shape), whole(gains.shape), whole(segments.shape), whole(parents.shape),
                  pl.BlockSpec(memory_space=pltpu.SMEM), whole(freq.shape), *[whole(m.shape) for m in masters]],
        out_specs=[ANYWHERE, rows(kv * group * n), rows(kv * n), rows(kv * n), cols, cols, rows(raw_w),
                   table, table, table, table, *more_specs],
        out_shape=[out(d, BF), out(kv * group * n, BF), out(kv * n, BF), out(kv * n, BF),
                   jax.ShapeDtypeStruct((kv * n, length), BF), jax.ShapeDtypeStruct((kv * n, length), BF),
                   out(raw_w, FP), out(n, BF), out(n, BF), out(n, FP), out(n, FP), *more_shapes],
        scratch_shapes=[*scratch, pltpu.VMEM((length, d), BF), pltpu.SemaphoreType.DMA],
        compiler_params=params(**({"collective_id": 0, "has_side_effects": True} if line else {})),
        name="front",
    )(x, gains, segments, parents, tree, freq, *masters)


def stacked(ref_block, h, group):
    n = LANES
    return jnp.concatenate(
        [ref_block[:, (h * group + g) * n:(h * group + g + 1) * n] for g in range(group)], axis=0)


def causal_tile(group, rows=ROWS, after=0):
    key_at = lax.broadcasted_iota(jnp.int32, (ROWS, rows * group), 0)
    query_at = lax.broadcasted_iota(jnp.int32, (ROWS, rows * group), 1) % rows
    return key_at <= query_at + after


def in_turn(i, steps, per, acts):
    for behind, act in acts:
        @pl.when(jnp.logical_and(i - behind >= 0, i - behind < steps))
        def _(behind=behind, act=act):
            for s in pair_of(i - behind, per):
                act(s)


def attend_kernel(kv, group, unit, line, per, steps, *refs):
    refs = list(refs)
    take = lambda count: [refs.pop(0) for _ in range(count)]
    q_ref, k_ref, vt_ref, tags_ref, bars_ref, wm_ref, x_all, gains_ref = take(8)
    own = take(2) if line else []
    ctx_ref, lse_ref, h_ref, xn_ref = take(4)
    full = take(2) if line else []
    acc_ref, sum_ref, x_ref, x_sem = take(4)
    held, near, far, total, e_sems, stage, s_sems = take(7)
    gathers = []
    place = Place(line)
    if line:
        cuts = (row_cut(own[0].shape[0]), column_cut(own[1].shape[1]))
        for w in range(2):
            gathers.append(Gather(place, own[w], full[w], cuts[w], *take(2)))
    i = pl.program_id(0)
    n = LANES
    exchange = Exchange(place, per, held, near, far, total, e_sems)
    spread = Spread(place, per, stage, xn_ref, s_sems)

    share, d = x_ref.shape
    x_copy = pltpu.make_async_copy(x_all.at[pl.ds(pl.multiple_of(place.t * share, share), share), :], x_ref, x_sem)

    @pl.when(i == 0)
    def _():
        place.greet(True, bool(line))
        for g in gathers:
            g.start()
        x_copy.start()

    pl.when(i == 1)(x_copy.wait)

    def block(s):
        here = pl.ds(pl.multiple_of(s * SUB, SUB), SUB)
        bars = jnp.concatenate([bars_ref[here, :]] * group, axis=0)
        q = q_ref[here, :]
        wide = [jnp.concatenate([stacked(q, h, group), bars], axis=1) for h in range(kv)]
        acc_ref[...] = jnp.zeros_like(acc_ref)
        sum_ref[...] = jnp.zeros_like(sum_ref)

        def chunk(j, diagonal):
            at = pl.ds(pl.multiple_of(j * ROWS, ROWS), ROWS)
            tags = tags_ref[at, :]
            for h in range(kv):
                keys = jnp.concatenate([k_ref[at, h * n:(h + 1) * n], tags], axis=1)
                scores = dot(keys, wide[h], 1, 1)
                e = jnp.exp2(scores * unit)
                if diagonal:
                    e = jnp.where(causal_tile(group, SUB, (s % 2) * SUB), e, 0.0)
                sum_ref[h] += fold_rows(e)
                acc_ref[h] += dot(vt_ref[h * n:(h + 1) * n, at], e.astype(BF))

        lax.fori_loop(0, s // 2, lambda j, c: (chunk(j, False), c)[1], 0)
        chunk(s // 2, True)
        parts = []
        for h in range(kv):
            sums = jnp.sum(sum_ref[h], axis=0, keepdims=True)
            lse_ref[s, h:h + 1, :] = jnp.log2(sums)
            ctx = (acc_ref[h] / sums).T
            parts += [ctx[g * SUB:(g + 1) * SUB] for g in range(group)]
        ctx_ref[here, :] = jnp.concatenate(parts, axis=1).astype(BF)

    @pl.when(i < steps)
    def _():
        blocks = pair_of(i, per)
        for s in blocks:
            block(s)
        ctx = [ctx_ref[pl.ds(pl.multiple_of(s * SUB, SUB), SUB), :] for s in blocks]
        part = dot(jnp.concatenate(ctx, axis=0), wm_ref[...]).astype(BF)
        for u, s in enumerate(blocks):
            held[s] = part[u * SUB:(u + 1) * SUB]
            exchange.out(s)

    def own_rows(s, k, summed):
        at = pl.ds(pl.multiple_of(k * SUB, SUB), SUB)
        hidden = x_ref[at, :].astype(FP) + summed
        h_ref[at, :] = hidden
        stage[k] = (hidden * inverse_rms(hidden) * gains_ref[:, d:2 * d]).astype(BF)
        spread.send(s)

    in_turn(i, steps, per, ((1, exchange.add), (2, lambda s: exchange.take(s, own_rows)), (3, spread.pass_on)))
    if line:
        for k in range(1, line):
            @pl.when(i == min(2 * k, steps + 2))
            def _(k=k):
                for g in gathers:
                    g.hop(k)

    @pl.when(i == steps + 2)
    def _():
        exchange.drain()
        spread.finish()
        for g in gathers:
            g.finish()
            g.drain()


def attend(q, k, vt, tags, bars, wm, x, gains, own, kv, group, unit, line):
    length = q.shape[0]
    n = LANES
    d = wm.shape[1]
    share = (length // 4, d)
    per = share[0] // SUB
    steps = 2 * per
    shards = 2 * line
    full = []
    if line:
        full = [jax.ShapeDtypeStruct((own[0].shape[0] * shards, own[0].shape[1]), BF),
                jax.ShapeDtypeStruct((own[1].shape[0], own[1].shape[1] * shards), BF)]
    return pl.pallas_call(
        partial(attend_kernel, kv, group, unit, line, per, steps),
        grid=(steps + 3,),
        in_specs=[whole(q.shape), whole(k.shape), whole(vt.shape), whole(tags.shape), whole(bars.shape), whole(wm.shape),
                  ANYWHERE, whole(gains.shape)] + [ANYWHERE] * len(own),
        out_specs=[whole(q.shape), whole((length // SUB, 8, SUB * group)),
                   whole(share), ANYWHERE] + [ANYWHERE] * len(full),
        out_shape=[jax.ShapeDtypeStruct(q.shape, BF),
                   jax.ShapeDtypeStruct((length // SUB, 8, SUB * group), FP),
                   jax.ShapeDtypeStruct(share, FP),
                   jax.ShapeDtypeStruct((length // SUB, SUB, d), BF), *full],
        scratch_shapes=[pltpu.VMEM((kv, n, SUB * group), FP), pltpu.VMEM((kv, 8, SUB * group), FP),
                        pltpu.VMEM(share, BF), pltpu.SemaphoreType.DMA,
                        *exchange_scratch(per, d), *spread_scratch(per, d)]
                       + (GATHER_SEMS(shards) * 2 if line else []),
        compiler_params=params(collective_id=1, has_side_effects=True),
        name="attend",
    )(q, k, vt, tags, bars, wm, x, gains, *own)


def feed_kernel(units, per, steps, line, xn_ref, dy_ref, we_ref, ws_ref, h_ref, gains_ref,
                base_ref, other_ref, gex_ref, dh_ref, dhb_ref, dg_ref, gsh_out,
                a_ref, dgu_ref, held, near, far, total, e_sems, stage, s_sems, b_held, b_near, b_sems, *more):
    i = pl.program_id(0)
    place = Place(line)
    if line:
        gsh_ref = more[0]
        shrink = Reduce(place, gsh_ref, column_cut(gsh_ref.shape[1] // (2 * line)), *more[1:])
    else:
        gsh_ref = gsh_out
    exchange = Exchange(place, per, held, near, far, total, e_sems)
    spread = Spread(place, per, stage, dhb_ref, s_sems)
    pairs = Pairs(place, per, b_held, b_near, b_sems)
    tile = 256

    @pl.when(i == 0)
    def _():
        place.greet(True, bool(line))
        dg_ref[...] = jnp.zeros_like(dg_ref)

    @pl.when(i < steps)
    def _():
        blocks = pair_of(i, per)
        places = [pl.ds(pl.multiple_of(s * SUB, SUB), SUB) for s in blocks]
        xn, dy = (jnp.concatenate([ref[at, :] for at in places], axis=0) for ref in (xn_ref, dy_ref))

        def keep(ref, values):
            for u, at in enumerate(places):
                ref[at, :] = values[u * SUB:(u + 1) * SUB]

        gu = dot(xn, we_ref[...])
        gate, up = gu[:, :units], gu[:, units:]
        sig = 1.0 / (1.0 + jnp.exp(-gate))
        silu = gate * sig
        a = (silu * up).astype(BF)
        keep(a_ref, a)
        da = dot(dy, ws_ref[...], 1, 1)
        dgu = jnp.concatenate([da * up * (sig * (1.0 + gate * (1.0 - sig))), da * silu], axis=1).astype(BF)
        keep(dgu_ref, dgu)
        part = dot(dgu, we_ref[...], 1, 1).astype(BF)
        for u, s in enumerate(blocks):
            held[s] = part[u * SUB:(u + 1) * SUB]
            exchange.out(s)
        part = dot(a, ws_ref[...]).astype(BF)
        for u, s in enumerate(blocks):
            b_held[s] = part[u * SUB:(u + 1) * SUB]
            pairs.out(s)

    def own_rows(s, k, summed):
        at = pl.ds(pl.multiple_of(k * SUB, SUB), SUB)
        pulled, gain_grad = rms_pull(h_ref[at, :], gains_ref[:, summed.shape[1]:2 * summed.shape[1]], summed)
        dh = dy_ref[pl.ds(pl.multiple_of(s * SUB, SUB), SUB), :].astype(FP) + pulled
        dh_ref[at, :] = dh
        dg_ref[...] += fold_rows(gain_grad)
        stage[k] = dh.astype(BF)
        spread.send(s)

    def chip_rows(mine, k, summed):
        at = pl.ds(pl.multiple_of(k * SUB, SUB), SUB)

        @pl.when(mine)
        def _():
            base_ref[at, :] = h_ref[at, :] + summed

        @pl.when(jnp.logical_not(mine))
        def _():
            other_ref[k] = summed.astype(BF)

    in_turn(i, steps, per, ((1, exchange.add), (2, lambda s: pairs.add(s, chip_rows)),
                            (3, lambda s: exchange.take(s, own_rows)), (5, spread.pass_on)))

    def tiles(grad_ref, left_ref, right_ref, first, count):
        def one(t, carry):
            cut = pl.ds(pl.multiple_of(t * tile, tile), tile)
            grad_ref[:, cut] = dot(left_ref[...], right_ref[:, cut], 0, 0).astype(grad_ref.dtype)
            return carry

        lax.fori_loop(first, first + count, one, 0)

    half = gex_ref.shape[1] // tile // 2

    @pl.when(i == steps)
    def _():
        tiles(gsh_ref, a_ref, dy_ref, 0, gsh_ref.shape[1] // tile)
        if line:
            shrink.start()

    @pl.when(i == steps + 1)
    def _():
        tiles(gex_ref, xn_ref, dgu_ref, 0, half)
        if line:
            shrink.step(1)

    @pl.when(i == steps + 2)
    def _():
        tiles(gex_ref, xn_ref, dgu_ref, half, half)
        if line:
            shrink.step(2)

    if line:
        pl.when(i == steps + 3)(lambda: shrink.step(3))

    @pl.when(i == steps + 4)
    def _():
        exchange.drain()
        pairs.drain()
        if line:
            shrink.finish(gsh_out)
            shrink.drain()
        spread.finish()


def feed(xn, dy, we, ws, h, gains, line):
    length, d = xn.shape
    units = ws.shape[0]
    per = h.shape[0] // SUB
    steps = 2 * per
    more = []
    shrink = jax.ShapeDtypeStruct(ws.shape, BF)
    if line:
        shrink = jax.ShapeDtypeStruct((ws.shape[0], ws.shape[1] // (2 * line)), FP)
        more = [pltpu.VMEM(ws.shape, BF), *reduce_scratch(line, shrink.shape)]
    return pl.pallas_call(
        partial(feed_kernel, units, per, steps, line),
        grid=(steps + 5,),
        in_specs=[whole(xn.shape), whole(dy.shape), whole(we.shape), whole(ws.shape), whole(h.shape), whole(gains.shape)],
        out_specs=[whole(h.shape), whole((per, SUB, d)), whole(we.shape), whole(h.shape), ANYWHERE,
                   whole((8, d)), whole(shrink.shape)],
        out_shape=[jax.ShapeDtypeStruct(h.shape, FP), jax.ShapeDtypeStruct((per, SUB, d), BF),
                   jax.ShapeDtypeStruct(we.shape, BF), jax.ShapeDtypeStruct(h.shape, FP),
                   jax.ShapeDtypeStruct((length // SUB, SUB, d), BF), jax.ShapeDtypeStruct((8, d), FP), shrink],
        scratch_shapes=[pltpu.VMEM((length, units), BF), pltpu.VMEM((length, 2 * units), BF),
                        *exchange_scratch(per, d), *spread_scratch(per, d), pltpu.VMEM((4 * per, SUB, d), BF),
                        pltpu.VMEM((2 * per, SUB, d), BF), pltpu.SemaphoreType.DMA((2, 4 * per)), *more],
        compiler_params=params(collective_id=2, has_side_effects=True),
        name="feed",
    )(xn, dy, we, ws, h, gains)


def back_kernel(kv, group, unit, scale, blocks, per, line, *refs):
    refs = list(refs)
    take = lambda count: [refs.pop(0) for _ in range(count)]
    q_ref, k_ref, v_ref, kt_ref, tags_ref, bars_ref, lse_ref, ctx_block, dh_block, wm_ref = take(10)
    raw_ref, cos_ref, sin_ref, all_gains, base_ref, other_ref = take(6)
    late_from = take(4)
    grads = take(1) if line else []
    mine_ref, far_ref, out_ref, gp_ref = take(4)
    gm_out = [] if line else take(1)
    gains_ref = take(1)[0]
    sums = take(2) if line else []
    late_to = take(4)
    wp_ref, ctx_ref, dh_ref, xn_ref = late_to
    late_sem = take(1)[0]
    late = [pltpu.make_async_copy(a, b, late_sem.at[w]) for w, (a, b) in enumerate(zip(late_from, late_to))]
    dk_ref, dv_ref, dq_ref, dqkv_ref = take(4)
    b_far, b_sems, x_held, x_near, x_sems = take(5)
    place = Place(line)
    i = pl.program_id(0)
    b = blocks - 1 - i
    n = LANES
    pairs = Pairs(place, per, x_held, x_near, x_sems)
    subs = ROWS // SUB
    d = wm_ref.shape[1]
    gq, gk = all_gains[:, 2 * d:2 * d + n], all_gains[:, 2 * d + n:]
    tile = 256
    reduces = []
    if line:
        shards = 2 * line
        gm_ref = take(1)[0]
        for grad, cut in ((grads[0], row_cut(grads[0].shape[0] // shards)),
                          (gm_ref, column_cut(gm_ref.shape[1] // shards))):
            reduces.append(Reduce(place, grad, cut, *take(4)))
    else:
        gm_ref = gm_out[0]

    def tiles(grad_ref, left_ref, right_ref):
        def one(t, carry):
            cut = pl.ds(pl.multiple_of(t * tile, tile), tile)
            grad_ref[:, cut] = dot(left_ref[...], right_ref[:, cut], 0, 0).astype(grad_ref.dtype)
            return carry

        lax.fori_loop(0, grad_ref.shape[1] // tile, one, 0)

    def branch(k):
        return send(other_ref.at[k], b_far.at[k], b_sems.at[0, k], b_sems.at[1, k], place.chip)

    @pl.when(i == 0)
    def _():
        place.greet(True, bool(line))
        for r in reduces[:1]:
            r.start()
        for copy in late:
            copy.start()
        for k in range(per):
            branch(k).start()
        dk_ref[...] = jnp.zeros_like(dk_ref)
        dv_ref[...] = jnp.zeros_like(dv_ref)
        gains_ref[...] = jnp.zeros_like(gains_ref)

    @pl.when(i < blocks)
    def _():
        here = pl.ds(pl.multiple_of(b * ROWS, ROWS), ROWS)
        dctx = dot(dh_block[...], wm_ref[...], 1, 1).astype(BF)
        ctx, q = ctx_block[...], q_ref[...]
        bars = jnp.concatenate([bars_ref[...]] * group, axis=0)
        wide, queries, outward, centres, lses = [], [], [], [], []
        for h in range(kv):
            queries.append(stacked(q, h, group))
            wide.append(jnp.concatenate([queries[h], bars], axis=1))
            outward.append(stacked(dctx, h, group))
            both = outward[h].astype(FP) * stacked(ctx, h, group).astype(FP)
            centres.append(jnp.sum(both.T, axis=0, keepdims=True))
            lses.append(jnp.concatenate([lse_ref[u, h:h + 1, g * SUB:(g + 1) * SUB]
                                         for g in range(group) for u in range(ROWS // SUB)], axis=1))
        dq_ref[...] = jnp.zeros_like(dq_ref)

        def chunk(j, diagonal):
            at = pl.ds(pl.multiple_of(j * ROWS, ROWS), ROWS)
            tags = tags_ref[at, :]
            for h in range(kv):
                cut = slice(h * n, (h + 1) * n)
                keys = jnp.concatenate([k_ref[at, cut], tags], axis=1)
                p = jnp.exp2(dot(keys, wide[h], 1, 1) * unit - lses[h])
                if diagonal:
                    p = jnp.where(causal_tile(group), p, 0.0)
                dp = dot(v_ref[at, cut], outward[h], 1, 1)
                ds = (p * (dp - centres[h])).astype(BF)
                dv_ref[at, cut] += dot(p.astype(BF), outward[h])
                dk_ref[at, cut] += dot(ds, queries[h])
                dq_ref[h] += dot(kt_ref[cut, at], ds)

        lax.fori_loop(0, b, lambda j, c: (chunk(j, False), c)[1], 0)
        chunk(b, True)

        cosines, sines = cos_ref[...], sin_ref[...]
        pieces = []
        for h in range(kv):
            dq = dq_ref[h].T
            for c in range(group + 1):
                if c < group:
                    grad, gain, row = dq[c * ROWS:(c + 1) * ROWS] * scale, gq, 0
                else:
                    grad, gain, row = dk_ref[here, h * n:(h + 1) * n] * scale, gk, 1
                grad = grad * cosines - pltpu.roll(grad, n // 2, 1) * sines
                at = (h * (group + 1) + c) * n
                piece, gain_grad = rms_pull(raw_ref[:, at:at + n], gain, grad)
                gains_ref[row] += fold_rows(gain_grad)
                pieces.append(piece)
            pieces.append(dv_ref[here, h * n:(h + 1) * n])
        dqkv = jnp.concatenate(pieces, axis=1).astype(BF)
        dqkv_ref[here, :] = dqkv
        pl.when(i == 0)(late[0].wait)
        part = dot(dqkv, wp_ref[...], 1, 1).astype(BF)
        for u in range(subs):
            s = subs * b + u
            pl.when(i >= 2)(lambda s=s: pairs.sent(s + 2 * subs))
            x_held[s % (2 * subs)] = part[u * SUB:(u + 1) * SUB]
            pairs.out(s)

    def chip_rows(mine, k, summed):
        @pl.when(mine)
        def _():
            mine_ref[pl.ds(pl.multiple_of(k * SUB, SUB), SUB), :] = summed

        @pl.when(jnp.logical_not(mine))
        def _():
            far_ref[k] = summed.astype(BF)

    @pl.when(i >= 1)
    def _():
        for u in range(subs):
            pairs.add(subs * (b + 1) + u, chip_rows)

    @pl.when(i == 3)
    def _():
        for k in range(per):
            branch(k).wait()
            at = slice(k * SUB, (k + 1) * SUB)
            out_ref[at, :] = (base_ref[at, :] + b_far[k].astype(FP)).astype(BF)

    @pl.when(i == 1)
    def _():
        late[1].wait()
        late[2].wait()
        tiles(gm_ref, ctx_ref, dh_ref)

    if line:
        expand, merge = reduces
        for step, act in enumerate((lambda: expand.step(1), lambda: expand.step(2), lambda: expand.step(3), merge.start,
                                    lambda: merge.step(1), lambda: merge.step(2))):
            pl.when(i == step)(act)

    @pl.when(i == blocks)
    def _():
        late[3].wait()
        tiles(gp_ref, xn_ref, dqkv_ref)
        if line:
            merge.step(3)
        for s in range(2 * subs):
            pairs.sent(s)
        for r, out in zip(reduces, sums):
            r.finish(out)
            r.drain()


def back(q, k, v, kt, tags, bars, lse, ctx, dh, wm, wp, raw, cosines, sines, gains, xn,
         base, other, grads, kv, group, unit, scale, line):
    length = q.shape[0]
    n = LANES
    d = wm.shape[1]
    blocks = length // ROWS
    per = other.shape[0]
    block_of = lambda i: jnp.maximum(blocks - 1 - i, 0)
    rows = lambda w: pl.BlockSpec((ROWS, w), lambda i: (block_of(i), 0))
    late = [wp, ctx, dh, xn]
    scratch = [*[pltpu.VMEM(a.shape, BF) for a in late], pltpu.SemaphoreType.DMA((4,)),
               pltpu.VMEM((length, kv * n), FP), pltpu.VMEM((length, kv * n), FP),
               pltpu.VMEM((kv, n, ROWS * group), FP), pltpu.VMEM((length, wp.shape[1]), BF),
               pltpu.VMEM((per, SUB, d), BF), pltpu.SemaphoreType.DMA((2, per)),
               pltpu.VMEM((2 * ROWS // SUB, SUB, d), BF), pltpu.VMEM((2 * per, SUB, d), BF),
               pltpu.SemaphoreType.DMA((2, 4 * per))]
    sums = []
    merge = [jax.ShapeDtypeStruct(wm.shape, BF)]
    if line:
        shards = 2 * line
        own = [(grads[0].shape[0] // shards, grads[0].shape[1]), (wm.shape[0], wm.shape[1] // shards)]
        sums = [jax.ShapeDtypeStruct(s, FP) for s in own]
        merge = []
        scratch += [pltpu.VMEM(wm.shape, BF)]
        for s in own:
            scratch += reduce_scratch(line, s)
    args = [q, k, v, kt, tags, bars, lse, ctx, dh, wm, raw, cosines, sines, gains, base]
    specs = [whole(a.shape) for a in args] + [ANYWHERE] * (1 + len(late) + len(grads))
    for at in (0, 5, 7, 8, 10, 11, 12):
        specs[at] = rows(args[at].shape[1])
    specs[6] = pl.BlockSpec((ROWS // SUB, 8, SUB * group), lambda i: (block_of(i), 0, 0))
    return pl.pallas_call(
        partial(back_kernel, kv, group, unit, scale, blocks, per, line),
        grid=(blocks + 1,),
        in_specs=specs,
        out_specs=[whole(base.shape), whole((per, SUB, d)), whole(base.shape), whole(wp.shape), *[whole(s.shape) for s in merge], whole((2, 8, n))]
                  + [whole(s.shape) for s in sums],
        out_shape=[jax.ShapeDtypeStruct(base.shape, FP), jax.ShapeDtypeStruct((per, SUB, d), BF),
                   jax.ShapeDtypeStruct(base.shape, BF), jax.ShapeDtypeStruct(wp.shape, BF), *merge, jax.ShapeDtypeStruct((2, 8, n), FP), *sums],
        scratch_shapes=scratch,
        compiler_params=params(collective_id=3, has_side_effects=True),
        name="back",
    )(*args, other, *late, *grads)


def last_kernel(line, per, mine_ref, x_all, dh_ref, gains_ref, dg2_ref, head_ref, other_ref, *refs):
    refs = list(refs)
    take = lambda count: [refs.pop(0) for _ in range(count)]
    grads = take(1) if line else []
    in_ref, all_ref = take(2)
    sums = take(1) if line else []
    far, f_sems, x_ref, x_sem = take(4)
    place = Place(line)
    share, d = x_ref.shape
    n = LANES
    reduces, peers, copies = [], [], []
    tensors = lax.axis_size("tensor")
    if line:
        shards = 2 * line
        for grad, cut in zip(grads, (row_cut(grads[0].shape[0] // shards),)):
            reduces.append(Reduce(place, grad, cut, *take(4)))
        shown, over, g_sems = take(3)
        peers = [((place.dp + step) % shards, place.t) for step in range(1, shards)]
    mates = [(place.dp, (place.t + step) % tensors) for step in range(1, tensors)]
    barrier = pltpu.get_barrier_semaphore()
    partners = mates + peers
    for device in partners:
        pl.semaphore_signal(barrier, inc=1, device_id=device, device_id_type=MESH)
    x_copy = pltpu.make_async_copy(x_all.at[pl.ds(pl.multiple_of(place.t * share, share), share), :], x_ref, x_sem)
    x_copy.start()
    pl.semaphore_wait(barrier, len(partners))

    def chip(k):
        return send(other_ref.at[k], far.at[k], f_sems.at[0, k], f_sems.at[1, k], place.chip)

    for k in range(per):
        chip(k).start()
    for r in reduces:
        r.start()
    all_ref[:, :d] = jnp.zeros((8, d), FP)
    all_ref[:, d:2 * d] = dg2_ref[...]
    all_ref[:, 2 * d:2 * d + n] = head_ref[0]
    all_ref[:, 2 * d + n:] = head_ref[1]
    x_copy.wait()

    def input_rows(k):
        at = slice(k * SUB, (k + 1) * SUB)
        chip(k).wait()
        summed = mine_ref[at, :] + far[k].astype(FP)
        pulled, gain_grad = rms_pull(x_ref[at, :].astype(FP), gains_ref[:, :d], summed)
        in_ref[at, :] = (dh_ref[at, :] + pulled).astype(BF)
        all_ref[:, :d] += fold_rows(gain_grad)

    def step(k):
        for r in reduces:
            r.step(k)

    step(1)
    step(2)
    step(3)
    for k in range(per):
        input_rows(k)
    if not line:
        return

    def round_of(buffer, me, devices, first):
        buffer[me] = all_ref[...]
        count = len(devices) + 1
        for step, device in enumerate(devices, 1):
            copy = send(buffer.at[me], buffer.at[me], g_sems.at[0, first + step], g_sems.at[1, first + step], device)
            copy.start()
            copies.append(copy)
        for step in range(1, count):
            who = (me - step + count) % count
            send(buffer.at[who], buffer.at[who], g_sems.at[0, first + step], g_sems.at[1, first + step],
                 place.sibling).wait_recv()
        total = buffer[0]
        for who in range(1, count):
            total = total + buffer[who]
        all_ref[...] = total

    round_of(shown, place.t, mates, 0)
    for r, out in zip(reduces, sums):
        r.finish(out)
    round_of(over, place.dp, peers, tensors)
    for r in reduces:
        r.drain()
    for copy in copies:
        copy.wait_send()


def last(mine, x, dh, all_gains, dg2, heads, other, grads, line):
    share, d = mine.shape
    per = share // SUB
    gains = (8, 2 * d + 2 * LANES)
    vmem = pl.BlockSpec(memory_space=pltpu.VMEM)
    scratch = [pltpu.VMEM((per, SUB, d), BF), pltpu.SemaphoreType.DMA((2, per)), pltpu.VMEM((share, d), BF),
               pltpu.SemaphoreType.DMA]
    own = []
    if line:
        shards = 2 * line
        own = [(grads[0].shape[0] // shards, grads[0].shape[1])]
        for s in own:
            scratch += reduce_scratch(line, s)
        scratch += [pltpu.VMEM((4, *gains), FP), pltpu.VMEM((shards, *gains), FP),
                    pltpu.SemaphoreType.DMA((2, 4 + shards))]
    return pl.pallas_call(
        partial(last_kernel, line, per),
        in_specs=[vmem, ANYWHERE, vmem, vmem, vmem, vmem, ANYWHERE] + [ANYWHERE] * len(grads),
        out_specs=[vmem] * (2 + len(own)),
        out_shape=[jax.ShapeDtypeStruct(mine.shape, BF), jax.ShapeDtypeStruct(gains, FP),
                   *[jax.ShapeDtypeStruct(s, FP) for s in own]],
        scratch_shapes=scratch,
        compiler_params=params(collective_id=4, has_side_effects=True),
        name="last",
    )(mine, x, dh, all_gains, dg2, heads, other, *grads)


def adamw_step(weight, moment_one, moment_two, gradient, step_rate, decay):
    mean_next = BETA_ONE * moment_one + (1.0 - BETA_ONE) * gradient
    square_next = BETA_TWO * moment_two + (1.0 - BETA_TWO) * gradient * gradient
    mean_hat = mean_next / (1.0 - BETA_ONE**STEP)
    square_hat = square_next / (1.0 - BETA_TWO**STEP)
    weight_next = weight - step_rate * (mean_hat / (jnp.sqrt(square_hat) + EPS_ADAM) + decay * weight)
    return weight_next, mean_next, square_next


def shards(
    tokens, cotangent, parents, token_segment, tree_id,
    projection_weight, projection_first_moment, projection_second_moment,
    merge_master, merge_mean, merge_square,
    expand_master, expand_mean, expand_square,
    shrink_master, shrink_mean, shrink_square,
    gain_master, gain_mean, gain_square,
):
    x = tokens[0]
    dy = cotangent[0]
    length, d = x.shape
    d_own, kv, per, n = projection_weight.shape
    group = per - 2
    units = expand_master.shape[2]
    scale = n ** (-0.5)
    unit = scale * math.log2(math.e)
    line = 4 if lax.axis_size("dp") == 8 and d_own % LANES == 0 else 0
    if line:
        masters = (projection_weight.reshape(d_own, kv * per, n), merge_master, expand_master, shrink_master)
    else:
        wp, we = (lax.all_gather(w.astype(BF).reshape(d_own, -1), "dp", axis=0, tiled=True)
                  for w in (projection_weight, expand_master))
        wm, ws = (lax.all_gather(w.astype(BF), "dp", axis=1, tiled=True) for w in (merge_master, shrink_master))
        masters = (wp,)

    gains = gain_master[None]
    fronts = front(x, gains, token_segment, parents, tree_id, masters, kv, group, line)
    xn1, q, k, v, kt, vt, raw, tags, bars, cosines, sines = fronts[:11]
    low = ()
    if line:
        wp, wm, *low = fronts[11:]
    attends = attend(q, k, vt, tags, bars, wm, x, gains, low, kv, group, unit, line)
    ctx, lse, hidden, xn2 = attends[:4]
    if line:
        we, ws = attends[4:]
    base, other, expand_grad, dh, dhb, dg2, shrink_sum = feed(xn2.reshape(length, d), dy, we, ws, hidden, gains, line)
    backs = back(q, k, v, kt, tags, bars, lse, ctx, dhb.reshape(length, d), wm, wp, raw, cosines, sines, gains, xn1,
                 base, other, (expand_grad,) if line else (), kv, group, unit, scale, line)
    mine, other, output, project_grad = backs[:4]
    head_gains = backs[4 if line else 5]
    lasts = last(mine, x, dh, gains, dg2, head_gains, other, (project_grad,) if line else (), line)
    input_grad, gains = lasts[:2]
    if line:
        expand_sum, merge_sum = backs[5:]
        project_sum = lasts[2]
    else:
        gains = lax.psum(gains, ("dp", "tensor"))
        project_sum, expand_sum = (
            lax.psum_scatter(g, "dp", scatter_dimension=0, tiled=True) for g in (project_grad, expand_grad))
        merge_sum, shrink_sum = (
            lax.psum_scatter(g, "dp", scatter_dimension=1, tiled=True) for g in (backs[4], shrink_sum))
    output, input_grad = output[None], input_grad[None]
    gain_grad = jnp.sum(gains, axis=0)

    outs = [output, input_grad]
    for weight, mean, square, grad, rate in (
        (projection_weight, projection_first_moment, projection_second_moment, project_sum, RATE_PROJECT),
        (merge_master, merge_mean, merge_square, merge_sum, RATE_MERGE),
        (expand_master, expand_mean, expand_square, expand_sum, RATE_EXPAND),
        (shrink_master, shrink_mean, shrink_square, shrink_sum, RATE_SHRINK),
    ):
        grad = grad.astype(FP).reshape(weight.shape)
        after, mean_next, square_next = adamw_step(weight, mean, square, grad, rate, DECAY)
        outs += [after, mean_next, square_next, after.astype(BF)]
    gain_next, gain_mean_next, gain_square_next = adamw_step(
        gain_master, gain_mean, gain_square, gain_grad, RATE_GAIN, 0.0)
    return (*outs, gain_mean_next, gain_square_next, gain_next)


def solution(mesh):
    tokens = P("dp", None, None)
    project = P("dp", "tensor", None, None)
    columns = P("tensor", "dp")
    expand = P("dp", None, "tensor")
    shared = P("dp", "tensor", None)
    return jax.shard_map(
        shards,
        mesh=mesh,
        in_specs=(tokens, tokens, P(), P("dp", None), P("dp"), *[project] * 3, *[columns] * 3, *[expand] * 3,
                  *[columns] * 3, P(), P(), P()),
        out_specs=(shared, shared, *[project] * 4, *[columns] * 4, *[expand] * 4, *[columns] * 4, P(), P(), P()),
        check_vma=False,
    )
```

```python
import math
from functools import partial

import jax
import jax.numpy as jnp
import numpy as np
from jax import lax
from jax.experimental import pallas as pl
from jax.experimental.pallas import tpu as pltpu
from jax.sharding import PartitionSpec as P

STEP = 5
EPS_NORM = 1e-06
THETA = 1000000.0
BETA_ONE = 0.5
BETA_TWO = 0.5
EPS_ADAM = 1e-08
DECAY = 0.1
RATE_PROJECT = 0.05
RATE_MERGE = 0.3
RATE_EXPAND = 0.05
RATE_SHRINK = 0.03
RATE_GAIN = 0.3

BF = jnp.bfloat16
FP = jnp.float32
ROWS = 256
LANES = 128
SUB = 128
MESH = pl.DeviceIdType.MESH
BLOCKED = -1e30
VMEM_LIMIT = 60 * 2**20


def params(**more):
    return pltpu.CompilerParams(vmem_limit_bytes=VMEM_LIMIT, **more)


def dot(a, b, ca=1, cb=0):
    return lax.dot_general(a, b, (((ca,), (cb,)), ((), ())), preferred_element_type=FP)


def inverse_rms(values):
    return lax.rsqrt(jnp.mean(values * values, axis=-1, keepdims=True) + EPS_NORM)


def rms_pull(values, scales, grad):
    r = inverse_rms(values)
    scaled = grad * scales
    mean = jnp.mean(values * scaled, axis=-1, keepdims=True)
    return r * scaled - values * (r * r * r * mean), grad * values * r


def fold_rows(values):
    n, w = values.shape
    return jnp.sum(values.reshape(n // 8, 8, w), axis=0)


class Place:
    def __init__(self, line):
        self.line = line
        self.dp, self.t = lax.axis_index("dp"), lax.axis_index("tensor")
        self.z, self.y = self.dp // 2, self.dp % 2
        self.x, self.c = self.t // 2, self.t % 2
        self.has_up, self.has_down = self.z < line - 1, self.z > 0
        self.up, self.down = (self.dp + 2, self.t), (self.dp - 2, self.t)
        self.across = (self.dp + 1 - 2 * self.y, self.t)
        self.sibling = (self.dp, self.t + 1 - 2 * self.c)
        self.chip = (self.dp, (1 - self.x) * 2 + self.c)

    def greet(self, tensor, line, meanwhile=None):
        barrier = pltpu.get_barrier_semaphore()

        def signal(device):
            pl.semaphore_signal(barrier, inc=1, device_id=device, device_id_type=MESH)

        if tensor:
            signal(self.sibling)
            signal(self.chip)
        if line:
            signal(self.across)
            pl.when(self.has_up)(lambda: signal(self.up))
            pl.when(self.has_down)(lambda: signal(self.down))
        peers = (2 if tensor else 0) + (1 if line else 0)
        if line:
            peers = peers + jnp.where(self.has_up, 1, 0) + jnp.where(self.has_down, 1, 0)
        if meanwhile is not None:
            meanwhile()
        pl.semaphore_wait(barrier, peers)


def send(src, dst, sent, arrived, device):
    return pltpu.make_async_remote_copy(
        src_ref=src, dst_ref=dst, send_sem=sent, recv_sem=arrived, device_id=device, device_id_type=MESH)


def row_cut(size):
    return lambda j: (pl.ds(pl.multiple_of(j * size, size), size), slice(None))


def column_cut(size):
    return lambda j: (slice(None), pl.ds(pl.multiple_of(j * size, size), size))


class Gather:
    def __init__(self, place, own, full, cut, sems, local):
        self.place, self.own, self.full, self.cut, self.sems, self.local = place, own, full, cut, sems, local

    def copy(self, kind, src, j):
        p = self.place
        device = (p.up, p.down, p.across)[kind]
        return send(src, self.full.at[self.cut(j)], self.sems.at[kind, j], self.sems.at[3, j], device)

    def kept(self):
        return pltpu.make_async_copy(self.own, self.full.at[self.cut(self.place.dp)], self.local)

    def source(self):
        return self.full.at[self.cut(self.place.dp)] if self.own is None else self.own

    def start(self):
        p = self.place
        self.copy(2, self.source(), p.dp).start()
        pl.when(p.has_up)(lambda: self.copy(0, self.source(), p.dp).start())
        pl.when(p.has_down)(lambda: self.copy(1, self.source(), p.dp).start())
        if self.own is not None:
            self.kept().start()

    def arrivals(self, k):
        p = self.place
        return ((0, p.z >= k, (p.z - k) * 2 + p.y, p.has_up), (1, p.z + k < p.line, (p.z + k) * 2 + p.y, p.has_down))

    def hop(self, k):
        for kind, here, j, further in self.arrivals(k):
            @pl.when(here)
            def _(kind=kind, j=j, further=further):
                piece = self.full.at[self.cut(j)]
                self.copy(kind, piece, j).wait_recv()
                pl.when(further)(lambda: self.copy(kind, piece, j).start())
                self.copy(2, piece, j).start()

    def finish(self):
        p = self.place
        if self.own is not None:
            self.kept().wait()
        for zz in range(p.line):
            j = zz * 2 + 1 - p.y
            self.copy(2, self.full.at[self.cut(j)], j).wait_recv()

    def drain(self):
        p = self.place
        self.copy(2, self.source(), p.dp).wait_send()
        pl.when(p.has_up)(lambda: self.copy(0, self.source(), p.dp).wait_send())
        pl.when(p.has_down)(lambda: self.copy(1, self.source(), p.dp).wait_send())
        for k in range(1, p.line):
            for kind, here, j, further in self.arrivals(k):
                @pl.when(here)
                def _(kind=kind, j=j, further=further):
                    piece = self.full.at[self.cut(j)]
                    pl.when(further)(lambda: self.copy(kind, piece, j).wait_send())
                    self.copy(2, piece, j).wait_send()


class Reduce:
    def __init__(self, place, grad, cut, kept, across, lined, sems):
        self.place, self.grad, self.cut, self.kept, self.sems = place, grad, cut, kept, sems
        self.across, self.lined = across, lined

    def cross(self, zz):
        p = self.place
        return send(self.grad.at[self.cut(zz * 2 + 1 - p.y)], self.across.at[zz],
                    self.sems.at[0, zz], self.sems.at[1, zz], p.across)

    def climb(self, t):
        return send(self.across.at[t], self.lined.at[t + 1], self.sems.at[2, t], self.sems.at[3, t], self.place.up)

    def sink(self, t):
        return send(self.across.at[t], self.lined.at[t], self.sems.at[4, t], self.sems.at[5, t], self.place.down)

    def load(self, zz):
        return pltpu.make_async_copy(self.grad.at[self.cut(zz * 2 + self.place.y)], self.kept.at[zz], self.sems.at[6, zz])

    def mine(self, zz):
        if self.kept is None:
            return self.grad[self.cut(zz * 2 + self.place.y)].astype(FP)
        return self.kept[zz].astype(FP)

    def loaded(self, zz):
        if self.kept is not None:
            self.load(zz).wait()

    def turn(self, q):
        z = self.place.z
        low = z < 2
        if q == 0:
            return jnp.where(low, 3, 0)
        if q == 1:
            return jnp.where(low, 2, 1)
        if q == 2:
            return jnp.where(low, 1 - z, 5 - z)
        return z

    def start(self):
        self.cross(self.turn(0)).start()
        if self.kept is not None:
            for zz in range(self.place.line):
                self.load(zz).start()

    def advance(self, q):
        self.cross(self.turn(q - 1)).wait_send()
        self.cross(self.turn(q)).start()

    def hop(self, h):
        p = self.place

        def pass_on(t, coming, more, slot):
            self.loaded(t)
            self.cross(t).wait_recv()

            @pl.when(jnp.logical_not(more))
            def _():
                self.across[t] = (self.mine(t) + self.across[t].astype(FP)).astype(BF)

            @pl.when(more)
            def _():
                coming(t).wait_recv()
                self.across[t] = (self.mine(t) + self.across[t].astype(FP) + self.lined[slot].astype(FP)).astype(BF)

            coming(t).start()

        pl.when(p.z < h)(lambda: pass_on(p.z + p.line - h, self.climb, p.has_down, p.z + p.line - h + 1))
        pl.when(p.z >= p.line - h)(lambda: pass_on(p.z - p.line + h, self.sink, p.has_up, p.z - p.line + h))

    def finish(self, out):
        p = self.place
        self.loaded(p.z)
        self.cross(p.z).wait_recv()
        out[...] = self.mine(p.z) + self.across[p.z].astype(FP)

        @pl.when(p.has_down)
        def _():
            self.climb(p.z).wait_recv()
            out[...] += self.lined[p.z + 1].astype(FP)

        @pl.when(p.has_up)
        def _():
            self.sink(p.z).wait_recv()
            out[...] += self.lined[p.z].astype(FP)

    def step(self, k):
        self.advance(k)
        self.hop(k)

    def drain(self):
        p = self.place
        self.cross(p.z).wait_send()
        for zz in range(p.line):
            pl.when(zz > p.z)(lambda zz=zz: self.climb(zz).wait_send())
            pl.when(zz < p.z)(lambda zz=zz: self.sink(zz).wait_send())


def reduce_scratch(line, shape, kept=False):
    return [pltpu.VMEM((line, *shape), BF)] * kept + [pltpu.VMEM((line, *shape), BF), pltpu.VMEM((line + 1, *shape), BF),
                                                      pltpu.SemaphoreType.DMA((7, line))]


class Exchange:
    def __init__(self, place, per, held, near, far, total, sems):
        self.place, self.per, self.held, self.near, self.far = place, per, held, near, far
        self.total, self.sems = total, sems

    def owner(self, s):
        t = s // self.per
        return t // 2, t % 2

    def to_sibling(self, s):
        slot = (s // (2 * self.per)) * self.per + s % self.per
        return send(self.held.at[s], self.near.at[slot], self.sems.at[0, s], self.sems.at[1, s], self.place.sibling)

    def to_chip(self, s):
        slot = (s // (2 * self.per)) * self.per + s % self.per
        return send(self.near.at[slot], self.far.at[s % self.per], self.sems.at[2, s], self.sems.at[3, s],
                    self.place.chip)

    def out(self, s):
        pl.when(self.place.c != self.owner(s)[1])(lambda: self.to_sibling(s).start())

    def add(self, s):
        p = self.place
        ox, oc = self.owner(s)
        slot = (s // (2 * self.per)) * self.per + s % self.per

        @pl.when(p.c == oc)
        def _():
            self.to_sibling(s).wait_recv()

            @pl.when(p.x != ox)
            def _():
                self.near[slot] = (self.held[s].astype(FP) + self.near[slot].astype(FP)).astype(BF)
                self.to_chip(s).start()

            @pl.when(p.x == ox)
            def _():
                self.total[s % self.per] = self.held[s].astype(FP) + self.near[slot].astype(FP)

    def take(self, s, use):
        p = self.place

        @pl.when(s // self.per == p.t)
        def _():
            k = s % self.per
            self.to_chip(s).wait_recv()
            use(s, k, self.total[k] + self.far[k].astype(FP))

    def drain(self):
        p = self.place

        def one(s, carry):
            ox, oc = self.owner(s)
            pl.when(p.c != oc)(lambda: self.to_sibling(s).wait_send())
            pl.when(jnp.logical_and(p.c == oc, p.x != ox))(lambda: self.to_chip(s).wait_send())
            return carry

        lax.fori_loop(0, 4 * self.per, one, 0)


class Pairs:
    def __init__(self, place, per, held, near, sems):
        self.place, self.per, self.held, self.near, self.sems = place, per, held, near, sems

    def copy(self, s):
        slot = (s // (2 * self.per)) * self.per + s % self.per
        return send(self.held.at[s % self.held.shape[0]], self.near.at[slot], self.sems.at[0, s], self.sems.at[1, s],
                    self.place.sibling)

    def sends(self, s):
        return self.place.c != (s // self.per) % 2

    def out(self, s):
        pl.when(self.sends(s))(lambda: self.copy(s).start())

    def sent(self, s):
        pl.when(self.sends(s))(lambda: self.copy(s).wait_send())

    def add(self, s, use):
        t = s // self.per
        slot = (s // (2 * self.per)) * self.per + s % self.per

        @pl.when(self.place.c == t % 2)
        def _():
            self.copy(s).wait_recv()
            use(self.place.x == t // 2, s % self.per,
                self.held[s % self.held.shape[0]].astype(FP) + self.near[slot].astype(FP))

    def drain(self):
        def one(s, carry):
            self.sent(s)
            return carry

        lax.fori_loop(0, 4 * self.per, one, 0)


def pair_of(step, per):
    t = step % 2
    return t * per + step // 2, (3 - t) * per + step // 2


def exchange_scratch(per, d, held=True):
    return [pltpu.VMEM((4 * per, SUB, d), BF)] * held + [pltpu.VMEM((2 * per, SUB, d), BF), pltpu.VMEM((per, SUB, d), BF), pltpu.VMEM((per, SUB, d), FP),
                   pltpu.SemaphoreType.DMA((4, 4 * per))]


class Spread:
    def __init__(self, place, per, stage, full, sems):
        self.place, self.per, self.stage, self.full, self.sems = place, per, stage, full, sems

    def copy(self, kind, src, s):
        device = (self.place.chip, self.place.sibling)[kind]
        return send(src, self.full.at[s], self.sems.at[kind, s], self.sems.at[2, s], device)

    def kept(self, s):
        return pltpu.make_async_copy(self.stage.at[s % self.per], self.full.at[s], self.sems.at[3, s])

    def send(self, s):
        for kind in (0, 1):
            self.copy(kind, self.stage.at[s % self.per], s).start()
        self.kept(s).start()

    def passes(self, s):
        t = s // self.per
        return jnp.logical_and(self.place.c == t % 2, self.place.x != t // 2)

    def pass_on(self, s):
        @pl.when(self.passes(s))
        def _():
            self.copy(1, self.full.at[s], s).wait_recv()
            self.copy(1, self.full.at[s], s).start()

    def finish(self):
        def one(s, carry):
            @pl.when(s // self.per == self.place.t)
            def _():
                self.copy(0, self.stage.at[s % self.per], s).wait_send()
                self.copy(1, self.stage.at[s % self.per], s).wait_send()
                self.kept(s).wait()

            pl.when(self.passes(s))(lambda: self.copy(1, self.full.at[s], s).wait_send())
            pl.when((s // self.per) % 2 != self.place.c)(lambda: self.copy(1, self.full.at[s], s).wait_recv())
            return carry

        lax.fori_loop(0, 4 * self.per, one, 0)


def spread_scratch(per, d):
    return [pltpu.VMEM((per, SUB, d), BF), pltpu.SemaphoreType.DMA((4, 4 * per))]


def whole(shape):
    return pl.BlockSpec(tuple(shape), lambda i: (0,) * len(shape), pipeline_mode=pl.Buffered(1))


ANYWHERE = pl.BlockSpec(memory_space=pl.ANY)
GATHER_SEMS = lambda shards: [pltpu.SemaphoreType.DMA((4, shards)), pltpu.SemaphoreType.DMA]


def make_tables(seg_ref, parents_ref, tree_ref, freq_ref, tags_ref, bars_ref, cos_ref, sin_ref):
    count = parents_ref.shape[1]
    n = LANES
    blocks = sin_ref.shape[0] // ROWS
    lane = lax.broadcasted_iota(jnp.int32, (1, n), 1).astype(FP)
    place_of = lambda b: pl.ds(pl.multiple_of(b * ROWS, ROWS), ROWS)

    def columns(b, carry):
        sin_ref[place_of(b), :] = jnp.broadcast_to(seg_ref[:, place_of(b)].astype(FP), (n, ROWS)).T
        return carry

    def tally(b, carry):
        column = sin_ref[place_of(b), :]
        return (carry[0] + fold_rows(jnp.where(column == lane, 1.0, 0.0)),
                carry[1] + fold_rows(jnp.where(column < lane, 1.0, 0.0)))

    lax.fori_loop(0, blocks, columns, 0)
    sizes, starts = lax.fori_loop(0, blocks, tally, (jnp.zeros((8, n), FP), jnp.zeros((8, n), FP)))
    sizes, starts = (jnp.sum(a, axis=0, keepdims=True) for a in (sizes, starts))
    table = parents_ref[...]
    chosen = jnp.where(lax.broadcasted_iota(jnp.int32, table.shape, 0) == tree_ref[0], table, 0)
    chosen = jnp.sum(chosen.astype(FP), axis=0, keepdims=True)
    parents = jnp.zeros((1, n), FP)
    for b in range(count):
        parents = jnp.where(lane == b, chosen[:, b:b + 1], parents)
    shifts = jnp.where(lane != 0, sizes[:, :1], 0.0) - starts

    def rows(b, carry):
        at = place_of(b)
        column = sin_ref[at, :]
        hot = column == lane
        parent = jnp.sum(jnp.where(hot, parents, 0.0), axis=1, keepdims=True)
        above = jnp.where(jnp.logical_and(lane == parent, lane != 0), sizes, 0.0)
        first = (b * ROWS).astype(FP)
        position = (lax.broadcasted_iota(jnp.int32, (ROWS, 1), 0).astype(FP) + first
                    + jnp.sum(jnp.where(hot, shifts, 0.0) + above, axis=1, keepdims=True))
        tags_ref[at, :] = jnp.where(hot, 1.0, 0.0).astype(BF)
        open_to = jnp.logical_or(jnp.logical_or(hot, lane == parent), jnp.logical_or(lane == 0, lane >= count))
        bars_ref[at, :] = jnp.where(open_to, 0.0, BLOCKED).astype(BF)
        angles = position * freq_ref[...]
        cos_ref[at, :] = jnp.cos(angles)
        turned = jnp.sin(angles)
        sin_ref[at, :] = jnp.where(lane < n // 2, -turned, turned)
        return carry

    lax.fori_loop(0, blocks, rows, 0)


def front_kernel(kv, group, line, *refs):
    refs = list(refs)
    take = lambda count: [refs.pop(0) for _ in range(count)]
    x_ref, gains_ref, seg_ref, parents_ref, tree_ref, freq_ref = take(6)
    masters = take(4) if line else take(1)
    xn_ref, q_ref, k_ref, v_ref, kt_ref, vt_ref, raw_ref, tags_ref, bars_ref, cos_ref, sin_ref = take(11)
    if line:
        wp_out, wm_out, we_low, ws_low = take(4)
        wp_ref, wm_low, p_sems, p_local, m_sems, m_local, out_sem = take(7)
    else:
        wp_ref = masters[0]
    xn_full, xn_sem = take(2)
    i = pl.program_id(0)
    final = pl.num_programs(0) - 1
    d = x_ref.shape[1]
    n = LANES
    per = group + 2
    if line:
        place = Place(line)
        size = masters[0].shape[0]
        project = Gather(place, None, wp_ref, row_cut(size), p_sems, p_local)
        merge = Gather(place, wm_low, wm_out, column_cut(wm_low.shape[1]), m_sems, m_local)
        written = pltpu.make_async_copy(wp_ref, wp_out, out_sem)
    normed = pltpu.make_async_copy(xn_full, xn_ref, xn_sem)

    def round_projection():
        at = pl.ds(pl.multiple_of(place.dp * size, size), size)
        for j in range(kv * per):
            wp_ref[at, j * n:(j + 1) * n] = masters[0][:, j, :].astype(BF)

    def norm(b, carry):
        at = pl.ds(pl.multiple_of(b * ROWS, ROWS), ROWS)
        x = x_ref[at, :].astype(FP)
        xn_full[at, :] = (x * inverse_rms(x) * gains_ref[:, :d]).astype(BF)
        return carry

    @pl.when(i == 0)
    def _():
        if line:
            place.greet(False, True, round_projection)
            project.start()
        lax.fori_loop(0, x_ref.shape[0] // ROWS, norm, 0)
        normed.start()
        if line:
            project.hop(1)
        make_tables(seg_ref, parents_ref, tree_ref, freq_ref, tags_ref, bars_ref, cos_ref, sin_ref)
        if line:
            project.hop(2)
            wm_low[...] = masters[1][...].astype(BF)
            units = masters[2].shape[2]
            for half in range(2):
                we_low[:, half * units:(half + 1) * units] = masters[2][:, half, :].astype(BF)
            ws_low[...] = masters[3][...].astype(BF)
            project.hop(3)
            merge.start()
            project.finish()
            written.start()

    if line:
        for k in range(1, line):
            pl.when(i == k + 1)(lambda k=k: merge.hop(k))
    at = pl.ds(pl.multiple_of(i * ROWS, ROWS), ROWS)
    qkv = dot(xn_full[at, :], wp_ref[...])
    cosines, sines = cos_ref[at, :], sin_ref[at, :]
    gq, gk = gains_ref[:, 2 * d:2 * d + n], gains_ref[:, 2 * d + n:]
    keys, values = [], []
    for h in range(kv):
        for c in range(group + 1):
            raw = qkv[:, (h * per + c) * n:(h * per + c + 1) * n]
            to = (h * (group + 1) + c) * n
            raw_ref[:, to:to + n] = raw
            y = raw * inverse_rms(raw) * (gq if c < group else gk)
            turned = y * cosines + pltpu.roll(y, n // 2, 1) * sines
            if c < group:
                to = (h * group + c) * n
                q_ref[:, to:to + n] = turned.astype(BF)
            else:
                keys.append(turned)
        values.append(qkv[:, (h * per + group + 1) * n:(h * per + group + 2) * n])
    for h in range(kv):
        k_ref[:, h * n:(h + 1) * n] = keys[h].astype(BF)
        v_ref[:, h * n:(h + 1) * n] = values[h].astype(BF)
        kt_ref[h * n:(h + 1) * n, :] = keys[h].T.astype(BF)
        vt_ref[h * n:(h + 1) * n, :] = values[h].T.astype(BF)

    @pl.when(i == final)
    def _():
        normed.wait()
        if line:
            merge.finish()
            merge.drain()
            project.drain()
            written.wait()


def front(x, gains, segments, parents, tree, masters, kv, group, line):
    length, d = x.shape
    n = LANES
    rows = lambda w: pl.BlockSpec((ROWS, w), lambda i: (i, 0))
    cols = pl.BlockSpec((kv * n, ROWS), lambda i: (0, i))
    out = lambda w, t: jax.ShapeDtypeStruct((length, w), t)
    raw_w = kv * (group + 1) * n
    freq = np.float32(THETA ** (-(np.arange(n) % (n // 2)) * 2.0 / n))[None]
    more_specs, more_shapes, scratch = [], [], []
    if line:
        shards = 2 * line
        project, merge, expand, shrink = (m.shape for m in masters)
        wp_shape = (project[0] * shards, project[1] * n)
        more_shapes = [jax.ShapeDtypeStruct(wp_shape, BF), jax.ShapeDtypeStruct((merge[0], merge[1] * shards), BF),
                       jax.ShapeDtypeStruct((expand[0], 2 * expand[2]), BF), jax.ShapeDtypeStruct(shrink, BF)]
        more_specs = [ANYWHERE, ANYWHERE, whole(more_shapes[2].shape), whole(more_shapes[3].shape)]
        scratch = [pltpu.VMEM(wp_shape, BF), pltpu.VMEM(merge, BF), *GATHER_SEMS(shards), *GATHER_SEMS(shards),
                   pltpu.SemaphoreType.DMA]
    table = whole((length, n))
    return pl.pallas_call(
        partial(front_kernel, kv, group, line),
        grid=(length // ROWS,),
        in_specs=[whole(x.shape), whole(gains.shape), whole(segments.shape), whole(parents.shape),
                  pl.BlockSpec(memory_space=pltpu.SMEM), whole(freq.shape), *[whole(m.shape) for m in masters]],
        out_specs=[ANYWHERE, rows(kv * group * n), rows(kv * n), rows(kv * n), cols, cols, rows(raw_w),
                   table, table, table, table, *more_specs],
        out_shape=[out(d, BF), out(kv * group * n, BF), out(kv * n, BF), out(kv * n, BF),
                   jax.ShapeDtypeStruct((kv * n, length), BF), jax.ShapeDtypeStruct((kv * n, length), BF),
                   out(raw_w, FP), out(n, BF), out(n, BF), out(n, FP), out(n, FP), *more_shapes],
        scratch_shapes=[*scratch, pltpu.VMEM((length, d), BF), pltpu.SemaphoreType.DMA],
        compiler_params=params(**({"collective_id": 0, "has_side_effects": True} if line else {})),
        name="front",
    )(x, gains, segments, parents, tree, freq, *masters)


def stacked(ref_block, h, group):
    n = LANES
    return jnp.concatenate(
        [ref_block[:, (h * group + g) * n:(h * group + g + 1) * n] for g in range(group)], axis=0)


def causal_tile(group, rows=ROWS, after=0):
    key_at = lax.broadcasted_iota(jnp.int32, (ROWS, rows * group), 0)
    query_at = lax.broadcasted_iota(jnp.int32, (ROWS, rows * group), 1) % rows
    return key_at <= query_at + after


def in_turn(i, steps, per, acts):
    for behind, act in acts:
        @pl.when(jnp.logical_and(i - behind >= 0, i - behind < steps))
        def _(behind=behind, act=act):
            for s in pair_of(i - behind, per):
                act(s)


def attend_kernel(kv, group, unit, line, per, steps, *refs):
    refs = list(refs)
    take = lambda count: [refs.pop(0) for _ in range(count)]
    q_ref, k_ref, vt_ref, tags_ref, bars_ref, wm_ref, x_all, gains_ref = take(8)
    own = take(2) if line else []
    ctx_ref, lse_ref, h_ref, xn_ref = take(4)
    full = take(2) if line else []
    acc_ref, sum_ref, x_ref, x_sem = take(4)
    held, near, far, total, e_sems, stage, s_sems = take(7)
    gathers = []
    place = Place(line)
    if line:
        cuts = (row_cut(own[0].shape[0]), column_cut(own[1].shape[1]))
        for w in range(2):
            gathers.append(Gather(place, own[w], full[w], cuts[w], *take(2)))
    i = pl.program_id(0)
    n = LANES
    exchange = Exchange(place, per, held, near, far, total, e_sems)
    spread = Spread(place, per, stage, xn_ref, s_sems)

    share, d = x_ref.shape
    x_copy = pltpu.make_async_copy(x_all.at[pl.ds(pl.multiple_of(place.t * share, share), share), :], x_ref, x_sem)

    @pl.when(i == 0)
    def _():
        place.greet(True, bool(line))
        for g in gathers:
            g.start()
        x_copy.start()

    pl.when(i == 1)(x_copy.wait)

    def block(s):
        here = pl.ds(pl.multiple_of(s * SUB, SUB), SUB)
        bars = jnp.concatenate([bars_ref[here, :]] * group, axis=0)
        q = q_ref[here, :]
        wide = [jnp.concatenate([stacked(q, h, group), bars], axis=1) for h in range(kv)]
        acc_ref[...] = jnp.zeros_like(acc_ref)
        sum_ref[...] = jnp.zeros_like(sum_ref)

        def chunk(j, diagonal):
            at = pl.ds(pl.multiple_of(j * ROWS, ROWS), ROWS)
            tags = tags_ref[at, :]
            for h in range(kv):
                keys = jnp.concatenate([k_ref[at, h * n:(h + 1) * n], tags], axis=1)
                scores = dot(keys, wide[h], 1, 1)
                e = jnp.exp2(scores * unit)
                if diagonal:
                    e = jnp.where(causal_tile(group, SUB, (s % 2) * SUB), e, 0.0)
                sum_ref[h] += fold_rows(e)
                acc_ref[h] += dot(vt_ref[h * n:(h + 1) * n, at], e.astype(BF))

        lax.fori_loop(0, s // 2, lambda j, c: (chunk(j, False), c)[1], 0)
        chunk(s // 2, True)
        parts = []
        for h in range(kv):
            sums = jnp.sum(sum_ref[h], axis=0, keepdims=True)
            lse_ref[s, h:h + 1, :] = jnp.log2(sums)
            ctx = (acc_ref[h] / sums).T
            parts += [ctx[g * SUB:(g + 1) * SUB] for g in range(group)]
        ctx_ref[here, :] = jnp.concatenate(parts, axis=1).astype(BF)

    @pl.when(i < steps)
    def _():
        blocks = pair_of(i, per)
        for s in blocks:
            block(s)
        ctx = [ctx_ref[pl.ds(pl.multiple_of(s * SUB, SUB), SUB), :] for s in blocks]
        part = dot(jnp.concatenate(ctx, axis=0), wm_ref[...]).astype(BF)
        for u, s in enumerate(blocks):
            held[s] = part[u * SUB:(u + 1) * SUB]
            exchange.out(s)

    def own_rows(s, k, summed):
        at = pl.ds(pl.multiple_of(k * SUB, SUB), SUB)
        hidden = x_ref[at, :].astype(FP) + summed
        h_ref[at, :] = hidden
        stage[k] = (hidden * inverse_rms(hidden) * gains_ref[:, d:2 * d]).astype(BF)
        spread.send(s)

    in_turn(i, steps, per, ((1, exchange.add), (2, lambda s: exchange.take(s, own_rows)), (3, spread.pass_on)))
    if line:
        for k in range(1, line):
            @pl.when(i == min(2 * k, steps + 2))
            def _(k=k):
                for g in gathers:
                    g.hop(k)

    @pl.when(i == steps + 2)
    def _():
        exchange.drain()
        spread.finish()
        for g in gathers:
            g.finish()
            g.drain()


def attend(q, k, vt, tags, bars, wm, x, gains, own, kv, group, unit, line):
    length = q.shape[0]
    n = LANES
    d = wm.shape[1]
    share = (length // 4, d)
    per = share[0] // SUB
    steps = 2 * per
    shards = 2 * line
    full = []
    if line:
        full = [jax.ShapeDtypeStruct((own[0].shape[0] * shards, own[0].shape[1]), BF),
                jax.ShapeDtypeStruct((own[1].shape[0], own[1].shape[1] * shards), BF)]
    return pl.pallas_call(
        partial(attend_kernel, kv, group, unit, line, per, steps),
        grid=(steps + 3,),
        in_specs=[whole(q.shape), whole(k.shape), whole(vt.shape), whole(tags.shape), whole(bars.shape), whole(wm.shape),
                  ANYWHERE, whole(gains.shape)] + [ANYWHERE] * len(own),
        out_specs=[whole(q.shape), whole((length // SUB, 8, SUB * group)),
                   whole(share), ANYWHERE] + [ANYWHERE] * len(full),
        out_shape=[jax.ShapeDtypeStruct(q.shape, BF),
                   jax.ShapeDtypeStruct((length // SUB, 8, SUB * group), FP),
                   jax.ShapeDtypeStruct(share, FP),
                   jax.ShapeDtypeStruct((length // SUB, SUB, d), BF), *full],
        scratch_shapes=[pltpu.VMEM((kv, n, SUB * group), FP), pltpu.VMEM((kv, 8, SUB * group), FP),
                        pltpu.VMEM(share, BF), pltpu.SemaphoreType.DMA,
                        *exchange_scratch(per, d), *spread_scratch(per, d)]
                       + (GATHER_SEMS(shards) * 2 if line else []),
        compiler_params=params(collective_id=1, has_side_effects=True),
        name="attend",
    )(q, k, vt, tags, bars, wm, x, gains, *own)


def feed_kernel(units, per, steps, line, xn_ref, dy_ref, we_ref, ws_ref, h_ref, gains_ref,
                base_ref, other_ref, gex_ref, dh_ref, dhb_ref, dg_ref, gsh_out,
                a_ref, dgu_ref, held, near, far, total, e_sems, stage, s_sems, b_held, b_near, b_sems, *more):
    i = pl.program_id(0)
    place = Place(line)
    if line:
        gsh_ref = more[0]
        shrink = Reduce(place, gsh_ref, column_cut(gsh_ref.shape[1] // (2 * line)), None, *more[1:])
    else:
        gsh_ref = gsh_out
    exchange = Exchange(place, per, held, near, far, total, e_sems)
    spread = Spread(place, per, stage, dhb_ref, s_sems)
    pairs = Pairs(place, per, b_held, b_near, b_sems)
    tile = 256

    @pl.when(i == 0)
    def _():
        place.greet(True, bool(line))
        dg_ref[...] = jnp.zeros_like(dg_ref)

    @pl.when(i < steps)
    def _():
        blocks = pair_of(i, per)
        places = [pl.ds(pl.multiple_of(s * SUB, SUB), SUB) for s in blocks]
        xn, dy = (jnp.concatenate([ref[at, :] for at in places], axis=0) for ref in (xn_ref, dy_ref))

        def keep(ref, values):
            for u, at in enumerate(places):
                ref[at, :] = values[u * SUB:(u + 1) * SUB]

        gu = dot(xn, we_ref[...])
        gate, up = gu[:, :units], gu[:, units:]
        sig = 1.0 / (1.0 + jnp.exp(-gate))
        silu = gate * sig
        a = (silu * up).astype(BF)
        keep(a_ref, a)
        da = dot(dy, ws_ref[...], 1, 1)
        dgu = jnp.concatenate([da * up * (sig * (1.0 + gate * (1.0 - sig))), da * silu], axis=1).astype(BF)
        keep(dgu_ref, dgu)
        part = dot(dgu, we_ref[...], 1, 1).astype(BF)
        for u, s in enumerate(blocks):
            held[s] = part[u * SUB:(u + 1) * SUB]
            exchange.out(s)
        part = dot(a, ws_ref[...]).astype(BF)
        for u, s in enumerate(blocks):
            b_held[s] = part[u * SUB:(u + 1) * SUB]
            pairs.out(s)

    def own_rows(s, k, summed):
        at = pl.ds(pl.multiple_of(k * SUB, SUB), SUB)
        pulled, gain_grad = rms_pull(h_ref[at, :], gains_ref[:, summed.shape[1]:2 * summed.shape[1]], summed)
        dh = dy_ref[pl.ds(pl.multiple_of(s * SUB, SUB), SUB), :].astype(FP) + pulled
        dh_ref[at, :] = dh
        dg_ref[...] += fold_rows(gain_grad)
        stage[k] = dh.astype(BF)
        spread.send(s)

    def chip_rows(mine, k, summed):
        at = pl.ds(pl.multiple_of(k * SUB, SUB), SUB)

        @pl.when(mine)
        def _():
            base_ref[at, :] = h_ref[at, :] + summed

        @pl.when(jnp.logical_not(mine))
        def _():
            other_ref[k] = summed.astype(BF)

    in_turn(i, steps, per, ((1, exchange.add), (2, lambda s: pairs.add(s, chip_rows)),
                            (3, lambda s: exchange.take(s, own_rows)), (5, spread.pass_on)))

    def tiles(grad_ref, left_ref, right_ref, first, count):
        def one(t, carry):
            cut = pl.ds(pl.multiple_of(t * tile, tile), tile)
            grad_ref[:, cut] = dot(left_ref[...], right_ref[:, cut], 0, 0).astype(grad_ref.dtype)
            return carry

        lax.fori_loop(first, first + count, one, 0)

    half = gex_ref.shape[1] // tile // 2

    @pl.when(i == steps)
    def _():
        tiles(gsh_ref, a_ref, dy_ref, 0, gsh_ref.shape[1] // tile)
        if line:
            shrink.start()

    @pl.when(i == steps + 1)
    def _():
        tiles(gex_ref, xn_ref, dgu_ref, 0, half)
        if line:
            shrink.step(1)

    @pl.when(i == steps + 2)
    def _():
        tiles(gex_ref, xn_ref, dgu_ref, half, half)
        if line:
            shrink.step(2)

    if line:
        pl.when(i == steps + 3)(lambda: shrink.step(3))

    @pl.when(i == steps + 4)
    def _():
        exchange.drain()
        pairs.drain()
        if line:
            shrink.finish(gsh_out)
            shrink.drain()
        spread.finish()


def feed(xn, dy, we, ws, h, gains, line):
    length, d = xn.shape
    units = ws.shape[0]
    per = h.shape[0] // SUB
    steps = 2 * per
    more = []
    shrink = jax.ShapeDtypeStruct(ws.shape, BF)
    if line:
        shrink = jax.ShapeDtypeStruct((ws.shape[0], ws.shape[1] // (2 * line)), FP)
        more = [pltpu.VMEM(ws.shape, BF), *reduce_scratch(line, shrink.shape)]
    return pl.pallas_call(
        partial(feed_kernel, units, per, steps, line),
        grid=(steps + 5,),
        in_specs=[whole(xn.shape), whole(dy.shape), whole(we.shape), whole(ws.shape), whole(h.shape), whole(gains.shape)],
        out_specs=[whole(h.shape), whole((per, SUB, d)), whole(we.shape), whole(h.shape), ANYWHERE,
                   whole((8, d)), whole(shrink.shape)],
        out_shape=[jax.ShapeDtypeStruct(h.shape, FP), jax.ShapeDtypeStruct((per, SUB, d), BF),
                   jax.ShapeDtypeStruct(we.shape, BF), jax.ShapeDtypeStruct(h.shape, FP),
                   jax.ShapeDtypeStruct((length // SUB, SUB, d), BF), jax.ShapeDtypeStruct((8, d), FP), shrink],
        scratch_shapes=[pltpu.VMEM((length, units), BF), pltpu.VMEM((length, 2 * units), BF),
                        *exchange_scratch(per, d), *spread_scratch(per, d), pltpu.VMEM((4 * per, SUB, d), BF),
                        pltpu.VMEM((2 * per, SUB, d), BF), pltpu.SemaphoreType.DMA((2, 4 * per)), *more],
        compiler_params=params(collective_id=2, has_side_effects=True),
        name="feed",
    )(xn, dy, we, ws, h, gains)


def back_kernel(kv, group, unit, scale, blocks, per, line, *refs):
    refs = list(refs)
    take = lambda count: [refs.pop(0) for _ in range(count)]
    q_ref, k_ref, v_ref, kt_ref, tags_ref, bars_ref, lse_ref, ctx_block, dh_block, wm_ref = take(10)
    raw_ref, cos_ref, sin_ref, all_gains, base_ref, dg2_ref, other_ref = take(7)
    x_all, dh_all = take(2)
    late_from = take(4)
    grads = take(1) if line else []
    in_ref, out_ref, gains_out = take(3)
    sums = take(3) if line else []
    weight_grads = [] if line else take(2)
    late_to = take(4)
    wp_ref, ctx_ref, dh_ref, xn_ref = late_to
    late_sem = take(1)[0]
    late = [pltpu.make_async_copy(a, b, late_sem.at[w]) for w, (a, b) in enumerate(zip(late_from, late_to))]
    dk_ref, dv_ref, dq_ref, dqkv_ref = take(4)
    b_far, b_sems, x_held, x_near, x_sems = take(5)
    mine_ref, far_ref, x_far, f_sems, x_ref, dh_own, own_sems, heads_ref, fold_ref = take(9)
    place = Place(line)
    i = pl.program_id(0)
    b = blocks - 1 - i
    n = LANES
    pairs = Pairs(place, per, x_held, x_near, x_sems)
    subs = ROWS // SUB
    share, d = x_ref.shape
    gq, gk = all_gains[:, 2 * d:2 * d + n], all_gains[:, 2 * d + n:]
    tile = 256
    tensors = lax.axis_size("tensor")
    mates = [(place.dp, (place.t + step) % tensors) for step in range(1, tensors)]
    peers = []
    own_rows = pl.ds(pl.multiple_of(place.t * share, share), share)
    own_copies = [pltpu.make_async_copy(x_all.at[own_rows, :], x_ref, own_sems.at[0]),
                  pltpu.make_async_copy(dh_all, dh_own, own_sems.at[1])]
    if line:
        shards = 2 * line
        gm_ref, gp_ref = take(2)
        expand = Reduce(place, grads[0], row_cut(grads[0].shape[0] // shards), *take(4))
        merge = Reduce(place, gm_ref, column_cut(gm_ref.shape[1] // shards), None, *take(3))
        project = Reduce(place, gp_ref, row_cut(gp_ref.shape[0] // shards), None, *take(3))
        shown, over, g_sems = take(3)
        peers = [((place.dp + step) % shards, place.t) for step in range(1, shards)]
    else:
        gp_ref, gm_ref = weight_grads

    def tiles(grad_ref, left_ref, right_ref):
        def one(t, carry):
            cut = pl.ds(pl.multiple_of(t * tile, tile), tile)
            grad_ref[:, cut] = dot(left_ref[...], right_ref[:, cut], 0, 0).astype(grad_ref.dtype)
            return carry

        lax.fori_loop(0, grad_ref.shape[1] // tile, one, 0)

    def project_rows(t):
        cut = pl.ds(pl.multiple_of(t * tile, tile), tile)
        gp_ref[cut, :] = dot(xn_ref[:, cut], dqkv_ref[...], 0, 0).astype(BF)

    def chip(k):
        return send(far_ref.at[k], x_far.at[k], f_sems.at[0, k], f_sems.at[1, k], place.chip)

    def branch(k):
        return send(other_ref.at[k], b_far.at[k], b_sems.at[0, k], b_sems.at[1, k], place.chip)

    @pl.when(i == 0)
    def _():
        barrier = pltpu.get_barrier_semaphore()
        for device in mates + peers:
            pl.semaphore_signal(barrier, inc=1, device_id=device, device_id_type=MESH)
        for copy in late:
            copy.start()
        pl.semaphore_wait(barrier, len(mates + peers))
        if line:
            expand.start()
        for k in range(per):
            branch(k).start()
        dk_ref[...] = jnp.zeros_like(dk_ref)
        dv_ref[...] = jnp.zeros_like(dv_ref)
        heads_ref[...] = jnp.zeros_like(heads_ref)

    @pl.when(i < blocks)
    def _():
        here = pl.ds(pl.multiple_of(b * ROWS, ROWS), ROWS)
        dctx = dot(dh_block[...], wm_ref[...], 1, 1).astype(BF)
        ctx, q = ctx_block[...], q_ref[...]
        bars = jnp.concatenate([bars_ref[...]] * group, axis=0)
        wide, queries, outward, centres, lses = [], [], [], [], []
        for h in range(kv):
            queries.append(stacked(q, h, group))
            wide.append(jnp.concatenate([queries[h], bars], axis=1))
            outward.append(stacked(dctx, h, group))
            both = outward[h].astype(FP) * stacked(ctx, h, group).astype(FP)
            centres.append(jnp.sum(both.T, axis=0, keepdims=True))
            lses.append(jnp.concatenate([lse_ref[u, h:h + 1, g * SUB:(g + 1) * SUB]
                                         for g in range(group) for u in range(ROWS // SUB)], axis=1))
        dq_ref[...] = jnp.zeros_like(dq_ref)

        def chunk(j, diagonal):
            at = pl.ds(pl.multiple_of(j * ROWS, ROWS), ROWS)
            tags = tags_ref[at, :]
            for h in range(kv):
                cut = slice(h * n, (h + 1) * n)
                keys = jnp.concatenate([k_ref[at, cut], tags], axis=1)
                p = jnp.exp2(dot(keys, wide[h], 1, 1) * unit - lses[h])
                if diagonal:
                    p = jnp.where(causal_tile(group), p, 0.0)
                dp = dot(v_ref[at, cut], outward[h], 1, 1)
                ds = (p * (dp - centres[h])).astype(BF)
                dv_ref[at, cut] += dot(p.astype(BF), outward[h])
                dk_ref[at, cut] += dot(ds, queries[h])
                dq_ref[h] += dot(kt_ref[cut, at], ds)

        lax.fori_loop(0, b, lambda j, c: (chunk(j, False), c)[1], 0)
        chunk(b, True)

        cosines, sines = cos_ref[...], sin_ref[...]
        pieces = []
        for h in range(kv):
            dq = dq_ref[h].T
            for c in range(group + 1):
                if c < group:
                    grad, gain, row = dq[c * ROWS:(c + 1) * ROWS] * scale, gq, 0
                else:
                    grad, gain, row = dk_ref[here, h * n:(h + 1) * n] * scale, gk, 1
                grad = grad * cosines - pltpu.roll(grad, n // 2, 1) * sines
                at = (h * (group + 1) + c) * n
                piece, gain_grad = rms_pull(raw_ref[:, at:at + n], gain, grad)
                heads_ref[row] += fold_rows(gain_grad)
                pieces.append(piece)
            pieces.append(dv_ref[here, h * n:(h + 1) * n])
        dqkv = jnp.concatenate(pieces, axis=1).astype(BF)
        dqkv_ref[here, :] = dqkv
        pl.when(i == 0)(late[0].wait)
        part = dot(dqkv, wp_ref[...], 1, 1).astype(BF)
        for u in range(subs):
            s = subs * b + u
            pl.when(i >= 2)(lambda s=s: pairs.sent(s + 2 * subs))
            x_held[s % (2 * subs)] = part[u * SUB:(u + 1) * SUB]
            pairs.out(s)

    def chip_rows(mine, k, summed):
        @pl.when(mine)
        def _():
            mine_ref[pl.ds(pl.multiple_of(k * SUB, SUB), SUB), :] = summed

        @pl.when(jnp.logical_not(mine))
        def _():
            far_ref[k] = summed.astype(BF)
            chip(k).start()

    @pl.when(i >= 1)
    def _():
        for u in range(subs):
            pairs.add(subs * (b + 1) + u, chip_rows)

    @pl.when(i == 3)
    def _():
        for k in range(per):
            branch(k).wait()
            at = slice(k * SUB, (k + 1) * SUB)
            out_ref[at, :] = (base_ref[at, :] + b_far[k].astype(FP)).astype(BF)
        for copy in own_copies:
            copy.start()

    @pl.when(i == 1)
    def _():
        late[1].wait()
        late[2].wait()
        tiles(gm_ref, ctx_ref, dh_ref)

    if line:
        for step, act in enumerate((lambda: expand.step(1), lambda: expand.step(2), lambda: expand.step(3), merge.start,
                                    lambda: merge.step(1), lambda: merge.step(2))):
            pl.when(i == step)(act)

    def input_rows(k):
        at = slice(k * SUB, (k + 1) * SUB)
        chip(k).wait()
        summed = mine_ref[at, :] + x_far[k].astype(FP)
        pulled, gain_grad = rms_pull(x_ref[at, :].astype(FP), all_gains[:, :d], summed)
        in_ref[at, :] = (dh_own[at, :] + pulled).astype(BF)
        fold_ref[...] += fold_rows(gain_grad)

    def folded(ref):
        pieces = [fold_ref[...], dg2_ref[...], heads_ref[0], heads_ref[1]]
        row = jnp.sum(jnp.concatenate(pieces, axis=1), axis=0, keepdims=True)
        count = row.shape[1] // n
        for j in range(count):
            ref[j:j + 1, :] = row[:, j * n:(j + 1) * n]
        ref[count:, :] = jnp.zeros((ref.shape[0] - count, n), FP)

    def show(buffer, me, devices, first):
        copies = [send(buffer.at[me], buffer.at[me], g_sems.at[0, first + step], g_sems.at[1, first + step], device)
                  for step, device in enumerate(devices, 1)]
        for copy in copies:
            copy.start()
        return copies

    def added(buffer, me, devices, first):
        count = len(devices) + 1
        for step in range(1, count):
            who = (me - step + count) % count
            send(buffer.at[who], buffer.at[who], g_sems.at[0, first + step], g_sems.at[1, first + step],
                 place.sibling).wait_recv()
        total = buffer[0]
        for who in range(1, count):
            total = total + buffer[who]
        return total

    @pl.when(i == blocks)
    def _():
        fold_ref[...] = jnp.zeros_like(fold_ref)
        late[3].wait()
        for copy in own_copies:
            copy.wait()
        if not line:
            tiles(gp_ref, xn_ref, dqkv_ref)
            for k in range(per):
                input_rows(k)
            folded(gains_out)
        else:
            project_rows(project.turn(0))
            project.start()
            for q in range(1, line):
                project_rows(project.turn(q))
            merge.step(3)
            expand.finish(sums[0])
            project.step(1)
            merge.finish(sums[1])
            project.step(2)
            for k in range(per):
                input_rows(k)
            folded(shown.at[place.t])
            copies = show(shown, place.t, mates, 0)
            project.step(3)
            over[place.dp] = added(shown, place.t, mates, 0)
            copies += show(over, place.dp, peers, tensors)
            project.finish(sums[2])
            gains_out[...] = added(over, place.dp, peers, tensors)
            for copy in copies:
                copy.wait_send()
            for r in (expand, merge, project):
                r.drain()
        for s in range(2 * subs):
            pairs.sent(s)


def back(q, k, v, kt, tags, bars, lse, ctx, dh, wm, wp, raw, cosines, sines, gains, xn, base, dg2, other, x, dh_own,
         grads, kv, group, unit, scale, line):
    length = q.shape[0]
    n = LANES
    d = wm.shape[1]
    blocks = length // ROWS
    per = other.shape[0]
    share = base.shape
    block_of = lambda i: jnp.maximum(blocks - 1 - i, 0)
    rows = lambda w: pl.BlockSpec((ROWS, w), lambda i: (block_of(i), 0))
    late = [wp, ctx, dh, xn]
    gain_rows = (-(-(gains.shape[1] // n) // 8) * 8, n)
    scratch = [*[pltpu.VMEM(a.shape, BF) for a in late], pltpu.SemaphoreType.DMA((4,)),
               pltpu.VMEM((length, kv * n), FP), pltpu.VMEM((length, kv * n), FP),
               pltpu.VMEM((kv, n, ROWS * group), FP), pltpu.VMEM((length, wp.shape[1]), BF),
               pltpu.VMEM((per, SUB, d), BF), pltpu.SemaphoreType.DMA((2, per)),
               pltpu.VMEM((2 * ROWS // SUB, SUB, d), BF), pltpu.VMEM((2 * per, SUB, d), BF),
               pltpu.SemaphoreType.DMA((2, 4 * per)),
               pltpu.VMEM(share, FP), pltpu.VMEM((per, SUB, d), BF), pltpu.VMEM((per, SUB, d), BF),
               pltpu.SemaphoreType.DMA((2, per)), pltpu.VMEM(share, BF), pltpu.VMEM(share, FP),
               pltpu.SemaphoreType.DMA((2,)), pltpu.VMEM((2, 8, n), FP), pltpu.VMEM((8, d), FP)]
    results = [jax.ShapeDtypeStruct(share, BF), jax.ShapeDtypeStruct(share, BF), jax.ShapeDtypeStruct(gain_rows, FP)]
    if line:
        shards = 2 * line
        own = [(grads[0].shape[0] // shards, grads[0].shape[1]), (wm.shape[0], wm.shape[1] // shards),
               (wp.shape[0] // shards, wp.shape[1])]
        results += [jax.ShapeDtypeStruct(s, FP) for s in own]
        scratch += [pltpu.VMEM(wm.shape, BF), pltpu.VMEM(wp.shape, BF)]
        for w, s in enumerate(own):
            scratch += reduce_scratch(line, s, w == 0)
        scratch += [pltpu.VMEM((4, *gain_rows), FP), pltpu.VMEM((shards, *gain_rows), FP),
                    pltpu.SemaphoreType.DMA((2, 4 + shards))]
    else:
        results += [jax.ShapeDtypeStruct(wp.shape, BF), jax.ShapeDtypeStruct(wm.shape, BF)]
    args = [q, k, v, kt, tags, bars, lse, ctx, dh, wm, raw, cosines, sines, gains, base, dg2]
    more = [other, x, dh_own, *late, *grads]
    specs = [whole(a.shape) for a in args] + [ANYWHERE] * len(more)
    for at in (0, 5, 7, 8, 10, 11, 12):
        specs[at] = rows(args[at].shape[1])
    specs[6] = pl.BlockSpec((ROWS // SUB, 8, SUB * group), lambda i: (block_of(i), 0, 0))
    return pl.pallas_call(
        partial(back_kernel, kv, group, unit, scale, blocks, per, line),
        grid=(blocks + 1,),
        in_specs=specs,
        out_specs=[whole(r.shape) for r in results],
        out_shape=results,
        scratch_shapes=scratch,
        compiler_params=params(collective_id=3, has_side_effects=True),
        name="back",
    )(*args, *more)


def adamw_step(weight, moment_one, moment_two, gradient, step_rate, decay):
    mean_next = BETA_ONE * moment_one + (1.0 - BETA_ONE) * gradient
    square_next = BETA_TWO * moment_two + (1.0 - BETA_TWO) * gradient * gradient
    mean_hat = mean_next / (1.0 - BETA_ONE**STEP)
    square_hat = square_next / (1.0 - BETA_TWO**STEP)
    weight_next = weight - step_rate * (mean_hat / (jnp.sqrt(square_hat) + EPS_ADAM) + decay * weight)
    return weight_next, mean_next, square_next


def shards(
    tokens, cotangent, parents, token_segment, tree_id,
    projection_weight, projection_first_moment, projection_second_moment,
    merge_master, merge_mean, merge_square,
    expand_master, expand_mean, expand_square,
    shrink_master, shrink_mean, shrink_square,
    gain_master, gain_mean, gain_square,
):
    x = tokens[0]
    dy = cotangent[0]
    length, d = x.shape
    d_own, kv, per, n = projection_weight.shape
    group = per - 2
    units = expand_master.shape[2]
    scale = n ** (-0.5)
    unit = scale * math.log2(math.e)
    line = 4 if lax.axis_size("dp") == 8 and d_own % LANES == 0 else 0
    if line:
        masters = (projection_weight.reshape(d_own, kv * per, n), merge_master, expand_master, shrink_master)
    else:
        wp, we = (lax.all_gather(w.astype(BF).reshape(d_own, -1), "dp", axis=0, tiled=True)
                  for w in (projection_weight, expand_master))
        wm, ws = (lax.all_gather(w.astype(BF), "dp", axis=1, tiled=True) for w in (merge_master, shrink_master))
        masters = (wp,)

    gains = gain_master[None]
    fronts = front(x, gains, token_segment, parents, tree_id, masters, kv, group, line)
    xn1, q, k, v, kt, vt, raw, tags, bars, cosines, sines = fronts[:11]
    low = ()
    if line:
        wp, wm, *low = fronts[11:]
    attends = attend(q, k, vt, tags, bars, wm, x, gains, low, kv, group, unit, line)
    ctx, lse, hidden, xn2 = attends[:4]
    if line:
        we, ws = attends[4:]
    base, other, expand_grad, dh, dhb, dg2, shrink_sum = feed(xn2.reshape(length, d), dy, we, ws, hidden, gains, line)
    backs = back(q, k, v, kt, tags, bars, lse, ctx, dhb.reshape(length, d), wm, wp, raw, cosines, sines, gains, xn1,
                 base, dg2, other, x, dh, (expand_grad,) if line else (), kv, group, unit, scale, line)
    input_grad, output, gain_rows = backs[:3]
    if line:
        expand_sum, merge_sum, project_sum = backs[3:]
    else:
        gain_rows = lax.psum(gain_rows, ("dp", "tensor"))
        project_sum, expand_sum = (
            lax.psum_scatter(g, "dp", scatter_dimension=0, tiled=True) for g in (backs[3], expand_grad))
        merge_sum, shrink_sum = (
            lax.psum_scatter(g, "dp", scatter_dimension=1, tiled=True) for g in (backs[4], shrink_sum))
    output, input_grad = output[None], input_grad[None]
    gain_grad = gain_rows.reshape(-1)[:gain_master.shape[0]]

    outs = [output, input_grad]
    for weight, mean, square, grad, rate in (
        (projection_weight, projection_first_moment, projection_second_moment, project_sum, RATE_PROJECT),
        (merge_master, merge_mean, merge_square, merge_sum, RATE_MERGE),
        (expand_master, expand_mean, expand_square, expand_sum, RATE_EXPAND),
        (shrink_master, shrink_mean, shrink_square, shrink_sum, RATE_SHRINK),
    ):
        grad = grad.astype(FP).reshape(weight.shape)
        after, mean_next, square_next = adamw_step(weight, mean, square, grad, rate, DECAY)
        outs += [after, mean_next, square_next, after.astype(BF)]
    gain_next, gain_mean_next, gain_square_next = adamw_step(
        gain_master, gain_mean, gain_square, gain_grad, RATE_GAIN, 0.0)
    return (*outs, gain_mean_next, gain_square_next, gain_next)


def solution(mesh):
    tokens = P("dp", None, None)
    project = P("dp", "tensor", None, None)
    columns = P("tensor", "dp")
    expand = P("dp", None, "tensor")
    shared = P("dp", "tensor", None)
    return jax.shard_map(
        shards,
        mesh=mesh,
        in_specs=(tokens, tokens, P(), P("dp", None), P("dp"), *[project] * 3, *[columns] * 3, *[expand] * 3,
                  *[columns] * 3, P(), P(), P()),
        out_specs=(shared, shared, *[project] * 4, *[columns] * 4, *[expand] * 4, *[columns] * 4, P(), P(), P()),
        check_vma=False,
    )
```

```python
import math
from functools import partial

import jax
import jax.numpy as jnp
import numpy as np
from jax import lax
from jax.experimental import pallas as pl
from jax.experimental.pallas import tpu as pltpu
from jax.sharding import PartitionSpec as P

STEP = 5
EPS_NORM = 1e-06
THETA = 1000000.0
BETA_ONE = 0.5
BETA_TWO = 0.5
EPS_ADAM = 1e-08
DECAY = 0.1
RATE_PROJECT = 0.05
RATE_MERGE = 0.3
RATE_EXPAND = 0.05
RATE_SHRINK = 0.03
RATE_GAIN = 0.3

BF = jnp.bfloat16
FP = jnp.float32
ROWS = 256
LANES = 128
SUB = 128
MESH = pl.DeviceIdType.MESH
BLOCKED = -1e30
VMEM_LIMIT = 60 * 2**20


def params(**more):
    return pltpu.CompilerParams(vmem_limit_bytes=VMEM_LIMIT, **more)


def dot(a, b, ca=1, cb=0):
    return lax.dot_general(a, b, (((ca,), (cb,)), ((), ())), preferred_element_type=FP)


def inverse_rms(values):
    return lax.rsqrt(jnp.mean(values * values, axis=-1, keepdims=True) + EPS_NORM)


def rms_pull(values, scales, grad):
    r = inverse_rms(values)
    scaled = grad * scales
    mean = jnp.mean(values * scaled, axis=-1, keepdims=True)
    return r * scaled - values * (r * r * r * mean), grad * values * r


def fold_rows(values):
    n, w = values.shape
    return jnp.sum(values.reshape(n // 8, 8, w), axis=0)


class Place:
    def __init__(self, line):
        self.line = line
        self.dp, self.t = lax.axis_index("dp"), lax.axis_index("tensor")
        self.z, self.y = self.dp // 2, self.dp % 2
        self.x, self.c = self.t // 2, self.t % 2
        self.has_up, self.has_down = self.z < line - 1, self.z > 0
        self.up, self.down = (self.dp + 2, self.t), (self.dp - 2, self.t)
        self.across = (self.dp + 1 - 2 * self.y, self.t)
        self.sibling = (self.dp, self.t + 1 - 2 * self.c)
        self.chip = (self.dp, (1 - self.x) * 2 + self.c)

    def greet(self, tensor, line, meanwhile=None):
        barrier = pltpu.get_barrier_semaphore()

        def signal(device):
            pl.semaphore_signal(barrier, inc=1, device_id=device, device_id_type=MESH)

        if tensor:
            signal(self.sibling)
            signal(self.chip)
        if line:
            signal(self.across)
            pl.when(self.has_up)(lambda: signal(self.up))
            pl.when(self.has_down)(lambda: signal(self.down))
        peers = (2 if tensor else 0) + (1 if line else 0)
        if line:
            peers = peers + jnp.where(self.has_up, 1, 0) + jnp.where(self.has_down, 1, 0)
        if meanwhile is not None:
            meanwhile()
        pl.semaphore_wait(barrier, peers)


def send(src, dst, sent, arrived, device):
    return pltpu.make_async_remote_copy(
        src_ref=src, dst_ref=dst, send_sem=sent, recv_sem=arrived, device_id=device, device_id_type=MESH)


def row_cut(size):
    return lambda j: (pl.ds(pl.multiple_of(j * size, size), size), slice(None))


def column_cut(size):
    return lambda j: (slice(None), pl.ds(pl.multiple_of(j * size, size), size))


class Gather:
    def __init__(self, place, own, full, cut, sems, local):
        self.place, self.own, self.full, self.cut, self.sems, self.local = place, own, full, cut, sems, local

    def copy(self, kind, src, j):
        p = self.place
        device = (p.up, p.down, p.across)[kind]
        return send(src, self.full.at[self.cut(j)], self.sems.at[kind, j], self.sems.at[3, j], device)

    def kept(self):
        return pltpu.make_async_copy(self.own, self.full.at[self.cut(self.place.dp)], self.local)

    def source(self):
        return self.full.at[self.cut(self.place.dp)] if self.own is None else self.own

    def start(self):
        p = self.place
        self.copy(2, self.source(), p.dp).start()
        pl.when(p.has_up)(lambda: self.copy(0, self.source(), p.dp).start())
        pl.when(p.has_down)(lambda: self.copy(1, self.source(), p.dp).start())
        if self.own is not None:
            self.kept().start()

    def arrivals(self, k):
        p = self.place
        return ((0, p.z >= k, (p.z - k) * 2 + p.y, p.has_up), (1, p.z + k < p.line, (p.z + k) * 2 + p.y, p.has_down))

    def hop(self, k):
        for kind, here, j, further in self.arrivals(k):
            @pl.when(here)
            def _(kind=kind, j=j, further=further):
                piece = self.full.at[self.cut(j)]
                self.copy(kind, piece, j).wait_recv()
                pl.when(further)(lambda: self.copy(kind, piece, j).start())
                self.copy(2, piece, j).start()

    def finish(self):
        p = self.place
        if self.own is not None:
            self.kept().wait()
        for zz in range(p.line):
            j = zz * 2 + 1 - p.y
            self.copy(2, self.full.at[self.cut(j)], j).wait_recv()

    def drain(self):
        p = self.place
        self.copy(2, self.source(), p.dp).wait_send()
        pl.when(p.has_up)(lambda: self.copy(0, self.source(), p.dp).wait_send())
        pl.when(p.has_down)(lambda: self.copy(1, self.source(), p.dp).wait_send())
        for k in range(1, p.line):
            for kind, here, j, further in self.arrivals(k):
                @pl.when(here)
                def _(kind=kind, j=j, further=further):
                    piece = self.full.at[self.cut(j)]
                    pl.when(further)(lambda: self.copy(kind, piece, j).wait_send())
                    self.copy(2, piece, j).wait_send()


class Reduce:
    def __init__(self, place, grad, cut, kept, across, lined, sems):
        self.place, self.grad, self.cut, self.kept, self.sems = place, grad, cut, kept, sems
        self.across, self.lined = across, lined

    def cross(self, zz):
        p = self.place
        return send(self.grad.at[self.cut(zz * 2 + 1 - p.y)], self.across.at[zz],
                    self.sems.at[0, zz], self.sems.at[1, zz], p.across)

    def climb(self, t):
        return send(self.across.at[t], self.lined.at[t + 1], self.sems.at[2, t], self.sems.at[3, t], self.place.up)

    def sink(self, t):
        return send(self.across.at[t], self.lined.at[t], self.sems.at[4, t], self.sems.at[5, t], self.place.down)

    def load(self, zz):
        return pltpu.make_async_copy(self.grad.at[self.cut(zz * 2 + self.place.y)], self.kept.at[zz], self.sems.at[6, zz])

    def mine(self, zz):
        if self.kept is None:
            return self.grad[self.cut(zz * 2 + self.place.y)].astype(FP)
        return self.kept[zz].astype(FP)

    def loaded(self, zz):
        if self.kept is not None:
            self.load(zz).wait()

    def turn(self, q):
        z = self.place.z
        low = z < 2
        if q == 0:
            return jnp.where(low, 3, 0)
        if q == 1:
            return jnp.where(low, 2, 1)
        if q == 2:
            return jnp.where(low, 1 - z, 5 - z)
        return z

    def start(self):
        self.cross(self.turn(0)).start()
        if self.kept is not None:
            for zz in range(self.place.line):
                self.load(zz).start()

    def advance(self, q):
        self.cross(self.turn(q - 1)).wait_send()
        self.cross(self.turn(q)).start()

    def hop(self, h):
        p = self.place

        def pass_on(t, coming, more, slot):
            self.loaded(t)
            self.cross(t).wait_recv()

            @pl.when(jnp.logical_not(more))
            def _():
                self.across[t] = (self.mine(t) + self.across[t].astype(FP)).astype(BF)

            @pl.when(more)
            def _():
                coming(t).wait_recv()
                self.across[t] = (self.mine(t) + self.across[t].astype(FP) + self.lined[slot].astype(FP)).astype(BF)

            coming(t).start()

        pl.when(p.z < h)(lambda: pass_on(p.z + p.line - h, self.climb, p.has_down, p.z + p.line - h + 1))
        pl.when(p.z >= p.line - h)(lambda: pass_on(p.z - p.line + h, self.sink, p.has_up, p.z - p.line + h))

    def finish(self, out):
        p = self.place
        self.loaded(p.z)
        self.cross(p.z).wait_recv()
        out[...] = self.mine(p.z) + self.across[p.z].astype(FP)

        @pl.when(p.has_down)
        def _():
            self.climb(p.z).wait_recv()
            out[...] += self.lined[p.z + 1].astype(FP)

        @pl.when(p.has_up)
        def _():
            self.sink(p.z).wait_recv()
            out[...] += self.lined[p.z].astype(FP)

    def step(self, k):
        self.advance(k)
        self.hop(k)

    def drain(self):
        p = self.place
        self.cross(p.z).wait_send()
        for zz in range(p.line):
            pl.when(zz > p.z)(lambda zz=zz: self.climb(zz).wait_send())
            pl.when(zz < p.z)(lambda zz=zz: self.sink(zz).wait_send())


def reduce_scratch(line, shape, kept=False):
    return [pltpu.VMEM((line, *shape), BF)] * kept + [pltpu.VMEM((line, *shape), BF), pltpu.VMEM((line + 1, *shape), BF),
                                                      pltpu.SemaphoreType.DMA((7, line))]


class Pairs:
    def __init__(self, place, per, held, near, sems, slot_of):
        self.place, self.per, self.held, self.near, self.sems, self.slot_of = place, per, held, near, sems, slot_of

    def near_slot(self, s):
        return (s // (2 * self.per)) * self.per + s % self.per

    def to_sibling(self, s):
        return send(self.held.at[self.slot_of(s)], self.near.at[self.near_slot(s)], self.sems.at[0, s],
                    self.sems.at[1, s], self.place.sibling)

    def sends(self, s):
        return self.place.c != (s // self.per) % 2

    def sent(self, s):
        pl.when(self.sends(s))(lambda: self.to_sibling(s).wait_send())

    def put(self, s, rows, before=None):
        if before is not None:
            pl.when(before[0])(lambda: self.sent(before[1]))
        self.held[self.slot_of(s)] = rows
        pl.when(self.sends(s))(lambda: self.to_sibling(s).start())

    def put_next(self, s, rows):
        self.put(s, rows, (s % self.per >= 1, s - 1))

    def add(self, s, use):
        t = s // self.per

        @pl.when(self.place.c == t % 2)
        def _():
            self.to_sibling(s).wait_recv()
            use(self.place.x == t // 2, s % self.per,
                self.held[self.slot_of(s)].astype(FP) + self.near[self.near_slot(s)].astype(FP))


class Exchange(Pairs):
    def __init__(self, place, per, held, near, far, total, sems):
        super().__init__(place, per, held, near, sems, lambda s: s // per)
        self.far, self.total = far, total

    def rows(self, k):
        return pl.ds(pl.multiple_of(k * SUB, SUB), SUB)

    def to_chip(self, s):
        return send(self.near.at[self.near_slot(s)], self.far.at[s % self.per], self.sems.at[2, s], self.sems.at[3, s],
                    self.place.chip)

    def add_chip(self, s):
        def use(mine, k, summed):
            @pl.when(jnp.logical_not(mine))
            def _():
                self.near[self.near_slot(s)] = summed.astype(BF)
                self.to_chip(s).start()

            @pl.when(mine)
            def _():
                self.total[self.rows(k), :] = summed

        self.add(s, use)

    def take(self, s, use):
        @pl.when(s // self.per == self.place.t)
        def _():
            k = s % self.per
            self.to_chip(s).wait_recv()
            use(s, self.rows(k), self.total[self.rows(k), :] + self.far[k].astype(FP))

    def drain(self):
        p = self.place

        def one(s, carry):
            t = s // self.per
            pl.when(s % self.per == self.per - 1)(lambda: self.sent(s))
            pl.when(jnp.logical_and(p.c == t % 2, p.x != t // 2))(lambda: self.to_chip(s).wait_send())
            return carry

        lax.fori_loop(0, 4 * self.per, one, 0)


def pair_of(step, per):
    t = step % 2
    return t * per + step // 2, (3 - t) * per + step // 2


def pairs_scratch(per, d, exchange):
    rows = [pltpu.VMEM((4, SUB, d), BF), pltpu.VMEM((2 * per, SUB, d), BF)]
    return rows + [pltpu.VMEM((per, SUB, d), BF)] * exchange + [pltpu.SemaphoreType.DMA((4 if exchange else 2, 4 * per))]


class Spread:
    def __init__(self, place, per, stage, full, sems):
        self.place, self.per, self.stage, self.full, self.sems = place, per, stage, full, sems

    def rows(self, s):
        return self.full.at[pl.ds(pl.multiple_of(s * SUB, SUB), SUB), :]

    def source(self, s):
        return self.rows(s) if self.stage is None else self.stage.at[s % self.per]

    def copy(self, kind, src, s):
        device = (self.place.chip, self.place.sibling)[kind]
        return send(src, self.rows(s), self.sems.at[kind, s], self.sems.at[2, s], device)

    def kept(self, s):
        return pltpu.make_async_copy(self.source(s), self.rows(s), self.sems.at[3, s])

    def send(self, s):
        for kind in (0, 1):
            self.copy(kind, self.source(s), s).start()
        if self.stage is not None:
            self.kept(s).start()

    def owns(self, s):
        return s // self.per == self.place.t

    def passes(self, s):
        t = s // self.per
        return jnp.logical_and(self.place.c == t % 2, self.place.x != t // 2)

    def pass_on(self, s):
        @pl.when(self.passes(s))
        def _():
            self.copy(1, self.rows(s), s).wait_recv()
            self.copy(1, self.rows(s), s).start()

    def ready(self, s):
        if self.stage is not None:
            pl.when(self.owns(s))(lambda: self.kept(s).wait())
        pl.when((s // self.per) % 2 != self.place.c)(lambda: self.copy(1, self.rows(s), s).wait_recv())

    def drain(self):
        def one(s, carry):
            @pl.when(self.owns(s))
            def _():
                self.copy(0, self.source(s), s).wait_send()
                self.copy(1, self.source(s), s).wait_send()

            pl.when(self.passes(s))(lambda: self.copy(1, self.rows(s), s).wait_send())
            return carry

        lax.fori_loop(0, 4 * self.per, one, 0)


def whole(shape):
    return pl.BlockSpec(tuple(shape), lambda i: (0,) * len(shape), pipeline_mode=pl.Buffered(1))


ANYWHERE = pl.BlockSpec(memory_space=pl.ANY)
GATHER_SEMS = lambda shards: [pltpu.SemaphoreType.DMA((4, shards)), pltpu.SemaphoreType.DMA]


def make_tables(seg_ref, parents_ref, tree_ref, freq_ref, tags_ref, bars_ref, cos_ref, sin_ref):
    count = parents_ref.shape[1]
    n = LANES
    blocks = sin_ref.shape[0] // ROWS
    lane = lax.broadcasted_iota(jnp.int32, (1, n), 1).astype(FP)
    place_of = lambda b: pl.ds(pl.multiple_of(b * ROWS, ROWS), ROWS)

    def columns(b, carry):
        sin_ref[place_of(b), :] = jnp.broadcast_to(seg_ref[:, place_of(b)].astype(FP), (n, ROWS)).T
        return carry

    def tally(b, carry):
        column = sin_ref[place_of(b), :]
        return (carry[0] + fold_rows(jnp.where(column == lane, 1.0, 0.0)),
                carry[1] + fold_rows(jnp.where(column < lane, 1.0, 0.0)))

    lax.fori_loop(0, blocks, columns, 0)
    sizes, starts = lax.fori_loop(0, blocks, tally, (jnp.zeros((8, n), FP), jnp.zeros((8, n), FP)))
    sizes, starts = (jnp.sum(a, axis=0, keepdims=True) for a in (sizes, starts))
    table = parents_ref[...]
    chosen = jnp.where(lax.broadcasted_iota(jnp.int32, table.shape, 0) == tree_ref[0], table, 0)
    chosen = jnp.sum(chosen.astype(FP), axis=0, keepdims=True)
    parents = jnp.zeros((1, n), FP)
    for b in range(count):
        parents = jnp.where(lane == b, chosen[:, b:b + 1], parents)
    shifts = jnp.where(lane != 0, sizes[:, :1], 0.0) - starts

    def rows(b, carry):
        at = place_of(b)
        column = sin_ref[at, :]
        hot = column == lane
        parent = jnp.sum(jnp.where(hot, parents, 0.0), axis=1, keepdims=True)
        above = jnp.where(jnp.logical_and(lane == parent, lane != 0), sizes, 0.0)
        first = (b * ROWS).astype(FP)
        position = (lax.broadcasted_iota(jnp.int32, (ROWS, 1), 0).astype(FP) + first
                    + jnp.sum(jnp.where(hot, shifts, 0.0) + above, axis=1, keepdims=True))
        tags_ref[at, :] = jnp.where(hot, 1.0, 0.0).astype(BF)
        open_to = jnp.logical_or(jnp.logical_or(hot, lane == parent), jnp.logical_or(lane == 0, lane >= count))
        bars_ref[at, :] = jnp.where(open_to, 0.0, BLOCKED).astype(BF)
        angles = position * freq_ref[...]
        cos_ref[at, :] = jnp.cos(angles)
        turned = jnp.sin(angles)
        sin_ref[at, :] = jnp.where(lane < n // 2, -turned, turned)
        return carry

    lax.fori_loop(0, blocks, rows, 0)


def front_kernel(kv, group, line, *refs):
    refs = list(refs)
    take = lambda count: [refs.pop(0) for _ in range(count)]
    x_ref, gains_ref, seg_ref, parents_ref, tree_ref, freq_ref = take(6)
    masters = take(4) if line else take(1)
    xn_ref, q_ref, k_ref, v_ref, kt_ref, vt_ref, raw_ref, tags_ref, bars_ref, cos_ref, sin_ref = take(11)
    if line:
        wp_out, wm_out, we_low, ws_low = take(4)
        wp_ref, wm_low, p_sems, p_local, m_sems, m_local, out_sem = take(7)
    else:
        wp_ref = masters[0]
    xn_full, xn_sem = take(2)
    i = pl.program_id(0)
    final = pl.num_programs(0) - 1
    d = x_ref.shape[1]
    n = LANES
    per = group + 2
    if line:
        place = Place(line)
        size = masters[0].shape[0]
        project = Gather(place, None, wp_ref, row_cut(size), p_sems, p_local)
        merge = Gather(place, wm_low, wm_out, column_cut(wm_low.shape[1]), m_sems, m_local)
        written = pltpu.make_async_copy(wp_ref, wp_out, out_sem)
    normed = pltpu.make_async_copy(xn_full, xn_ref, xn_sem)

    def round_projection():
        at = pl.ds(pl.multiple_of(place.dp * size, size), size)
        for j in range(kv * per):
            wp_ref[at, j * n:(j + 1) * n] = masters[0][:, j, :].astype(BF)

    def norm(b, carry):
        at = pl.ds(pl.multiple_of(b * ROWS, ROWS), ROWS)
        x = x_ref[at, :].astype(FP)
        xn_full[at, :] = (x * inverse_rms(x) * gains_ref[:, :d]).astype(BF)
        return carry

    @pl.when(i == 0)
    def _():
        if line:
            place.greet(False, True, round_projection)
            project.start()
        lax.fori_loop(0, x_ref.shape[0] // ROWS, norm, 0)
        normed.start()
        if line:
            project.hop(1)
        make_tables(seg_ref, parents_ref, tree_ref, freq_ref, tags_ref, bars_ref, cos_ref, sin_ref)
        if line:
            project.hop(2)
            wm_low[...] = masters[1][...].astype(BF)
            units = masters[2].shape[2]
            for half in range(2):
                we_low[:, half * units:(half + 1) * units] = masters[2][:, half, :].astype(BF)
            ws_low[...] = masters[3][...].astype(BF)
            project.hop(3)
            merge.start()
            project.finish()
            written.start()

    if line:
        for k in range(1, line):
            pl.when(i == k + 1)(lambda k=k: merge.hop(k))
    at = pl.ds(pl.multiple_of(i * ROWS, ROWS), ROWS)
    qkv = dot(xn_full[at, :], wp_ref[...])
    cosines, sines = cos_ref[at, :], sin_ref[at, :]
    gq, gk = gains_ref[:, 2 * d:2 * d + n], gains_ref[:, 2 * d + n:]
    keys, values = [], []
    for h in range(kv):
        for c in range(group + 1):
            raw = qkv[:, (h * per + c) * n:(h * per + c + 1) * n]
            to = (h * (group + 1) + c) * n
            raw_ref[:, to:to + n] = raw
            y = raw * inverse_rms(raw) * (gq if c < group else gk)
            turned = y * cosines + pltpu.roll(y, n // 2, 1) * sines
            if c < group:
                to = (h * group + c) * n
                q_ref[:, to:to + n] = turned.astype(BF)
            else:
                keys.append(turned)
        values.append(qkv[:, (h * per + group + 1) * n:(h * per + group + 2) * n])
    for h in range(kv):
        k_ref[:, h * n:(h + 1) * n] = keys[h].astype(BF)
        v_ref[:, h * n:(h + 1) * n] = values[h].astype(BF)
        kt_ref[h * n:(h + 1) * n, :] = keys[h].T.astype(BF)
        vt_ref[h * n:(h + 1) * n, :] = values[h].T.astype(BF)

    @pl.when(i == final)
    def _():
        normed.wait()
        if line:
            merge.finish()
            merge.drain()
            project.drain()
            written.wait()


def front(x, gains, segments, parents, tree, masters, kv, group, line):
    length, d = x.shape
    n = LANES
    rows = lambda w: pl.BlockSpec((ROWS, w), lambda i: (i, 0))
    cols = pl.BlockSpec((kv * n, ROWS), lambda i: (0, i))
    out = lambda w, t: jax.ShapeDtypeStruct((length, w), t)
    raw_w = kv * (group + 1) * n
    freq = np.float32(THETA ** (-(np.arange(n) % (n // 2)) * 2.0 / n))[None]
    more_specs, more_shapes, scratch = [], [], []
    if line:
        shards = 2 * line
        project, merge, expand, shrink = (m.shape for m in masters)
        wp_shape = (project[0] * shards, project[1] * n)
        more_shapes = [jax.ShapeDtypeStruct(wp_shape, BF), jax.ShapeDtypeStruct((merge[0], merge[1] * shards), BF),
                       jax.ShapeDtypeStruct((expand[0], 2 * expand[2]), BF), jax.ShapeDtypeStruct(shrink, BF)]
        more_specs = [ANYWHERE, ANYWHERE, whole(more_shapes[2].shape), whole(more_shapes[3].shape)]
        scratch = [pltpu.VMEM(wp_shape, BF), pltpu.VMEM(merge, BF), *GATHER_SEMS(shards), *GATHER_SEMS(shards),
                   pltpu.SemaphoreType.DMA]
    table = whole((length, n))
    return pl.pallas_call(
        partial(front_kernel, kv, group, line),
        grid=(length // ROWS,),
        in_specs=[whole(x.shape), whole(gains.shape), whole(segments.shape), whole(parents.shape),
                  pl.BlockSpec(memory_space=pltpu.SMEM), whole(freq.shape), *[whole(m.shape) for m in masters]],
        out_specs=[ANYWHERE, rows(kv * group * n), rows(kv * n), rows(kv * n), cols, cols, rows(raw_w),
                   table, table, table, table, *more_specs],
        out_shape=[out(d, BF), out(kv * group * n, BF), out(kv * n, BF), out(kv * n, BF),
                   jax.ShapeDtypeStruct((kv * n, length), BF), jax.ShapeDtypeStruct((kv * n, length), BF),
                   out(raw_w, FP), out(n, BF), out(n, BF), out(n, FP), out(n, FP), *more_shapes],
        scratch_shapes=[*scratch, pltpu.VMEM((length, d), BF), pltpu.SemaphoreType.DMA],
        compiler_params=params(**({"collective_id": 0, "has_side_effects": True} if line else {})),
        name="front",
    )(x, gains, segments, parents, tree, freq, *masters)


def stacked(ref_block, h, group):
    n = LANES
    return jnp.concatenate(
        [ref_block[:, (h * group + g) * n:(h * group + g + 1) * n] for g in range(group)], axis=0)


def causal_tile(group, rows=ROWS, after=0):
    key_at = lax.broadcasted_iota(jnp.int32, (ROWS, rows * group), 0)
    query_at = lax.broadcasted_iota(jnp.int32, (ROWS, rows * group), 1) % rows
    return key_at <= query_at + after


def in_turn(i, first, steps, per, acts):
    for behind, act in acts:
        @pl.when(jnp.logical_and(i - first - behind >= 0, i - first - behind < steps))
        def _(behind=behind, act=act):
            for s in pair_of(i - first - behind, per):
                act(s)


def middle_kernel(kv, group, unit, line, per, steps, *refs):
    refs = list(refs)
    take = lambda count: [refs.pop(0) for _ in range(count)]
    q_ref, k_ref, vt_ref, tags_ref, bars_ref, wm_ref, gains_ref, x_all, dy_all = take(9)
    weights = take(2)
    ctx_ref, lse_ref, base_ref, other_ref, gex_ref, dh_ref, dhb_ref, dg_ref, gsh_out = take(9)
    acc_ref, sum_ref, x_ref, dy_ref, we_ref, ws_ref, copy_sems = take(7)
    h_ref, xn_ref, a_ref, dgu_ref = take(4)
    h_held, h_near, h_far, h_sems, xn_sems = take(5)
    d_held, d_near, d_far, d_sems, stage, dh_sems = take(6)
    b_held, b_near, b_sems = take(3)
    place = Place(line)
    i = pl.program_id(0)
    n = LANES
    share, d = x_ref.shape
    units = ws_ref.shape[0]
    tile = 256
    attended = Exchange(place, per, h_held, h_near, h_far, h_ref, h_sems)
    norms = Spread(place, per, None, xn_ref, xn_sems)
    pulled_back = Exchange(place, per, d_held, d_near, d_far, dh_ref, d_sems)
    grads = Spread(place, per, stage, dhb_ref, dh_sems)
    branch = Pairs(place, per, b_held, b_near, b_sems, lambda s: s // per)
    own_share = x_all.at[pl.ds(pl.multiple_of(place.t * share, share), share), :]
    copies = [pltpu.make_async_copy(own_share, x_ref, copy_sems.at[0]),
              pltpu.make_async_copy(dy_all, dy_ref, copy_sems.at[1])]
    if line:
        gsh_ref = take(1)[0]
        shrink = Reduce(place, gsh_ref, column_cut(gsh_ref.shape[1] // (2 * line)), None, *take(3))
        cuts = (row_cut(weights[0].shape[0]), column_cut(weights[1].shape[1]))
        first, second = [Gather(place, weights[w], (we_ref, ws_ref)[w], cuts[w], *take(2)) for w in range(2)]
    else:
        gsh_ref = gsh_out
        copies += [pltpu.make_async_copy(weights[0], we_ref, copy_sems.at[2]),
                   pltpu.make_async_copy(weights[1], ws_ref, copy_sems.at[3])]
    rows_of = lambda s: pl.ds(pl.multiple_of(s * SUB, SUB), SUB)

    def at_step(step, *acts):
        @pl.when(i == step)
        def _():
            for act in acts:
                act()

    @pl.when(i == 0)
    def _():
        place.greet(True, bool(line))
        if line:
            first.start()
        for copy in copies:
            copy.start()
        dg_ref[...] = jnp.zeros_like(dg_ref)


    def block(s):
        here = rows_of(s)
        bars = jnp.concatenate([bars_ref[here, :]] * group, axis=0)
        q = q_ref[here, :]
        wide = [jnp.concatenate([stacked(q, h, group), bars], axis=1) for h in range(kv)]
        acc_ref[...] = jnp.zeros_like(acc_ref)
        sum_ref[...] = jnp.zeros_like(sum_ref)

        def chunk(j, diagonal):
            at = pl.ds(pl.multiple_of(j * ROWS, ROWS), ROWS)
            tags = tags_ref[at, :]
            for h in range(kv):
                keys = jnp.concatenate([k_ref[at, h * n:(h + 1) * n], tags], axis=1)
                scores = dot(keys, wide[h], 1, 1)
                e = jnp.exp2(scores * unit)
                if diagonal:
                    e = jnp.where(causal_tile(group, SUB, (s % 2) * SUB), e, 0.0)
                sum_ref[h] += fold_rows(e)
                acc_ref[h] += dot(vt_ref[h * n:(h + 1) * n, at], e.astype(BF))

        lax.fori_loop(0, s // 2, lambda j, c: (chunk(j, False), c)[1], 0)
        chunk(s // 2, True)
        parts = []
        for h in range(kv):
            sums = jnp.sum(sum_ref[h], axis=0, keepdims=True)
            lse_ref[s, h:h + 1, :] = jnp.log2(sums)
            ctx = (acc_ref[h] / sums).T
            parts += [ctx[g * SUB:(g + 1) * SUB] for g in range(group)]
        ctx_ref[here, :] = jnp.concatenate(parts, axis=1).astype(BF)

    def put_pair(pairs, blocks, part):
        for u, s in enumerate(blocks):
            pairs.put_next(s, part[u * SUB:(u + 1) * SUB])

    @pl.when(i < steps)
    def _():
        blocks = pair_of(i, per)
        for s in blocks:
            block(s)
        ctx = jnp.concatenate([ctx_ref[rows_of(s), :] for s in blocks], axis=0)
        put_pair(attended, blocks, dot(ctx, wm_ref[...]).astype(BF))

    def hidden_rows(s, at, summed):
        hidden = x_ref[at, :].astype(FP) + summed
        h_ref[at, :] = hidden
        xn_ref[rows_of(s), :] = (hidden * inverse_rms(hidden) * gains_ref[:, d:2 * d]).astype(BF)
        norms.send(s)

    at_step(1, copies[0].wait)
    in_turn(i, 0, steps, per, ((1, attended.add_chip), (3, lambda s: attended.take(s, hidden_rows)), (5, norms.pass_on)))
    swiglu, feed = steps + 3, 2 * steps + 3
    if line:
        at_step(2, lambda: first.hop(1))
        at_step(4, lambda: first.hop(2))
        at_step(6, lambda: first.hop(3), second.start)
        at_step(8, lambda: second.hop(1))
        at_step(9, lambda: second.hop(2), first.finish)
        at_step(10, lambda: second.hop(3))
        at_step(feed, second.finish)
    else:
        at_step(swiglu, copies[2].wait, copies[3].wait)


    def opened(blocks):
        xn = jnp.concatenate([xn_ref[rows_of(s), :] for s in blocks], axis=0)
        gu = dot(xn, we_ref[...])
        gate, up = gu[:, :units], gu[:, units:]
        sig = 1.0 / (1.0 + jnp.exp(-gate))
        return gate, up, sig

    def keep(ref, blocks, values):
        for u, s in enumerate(blocks):
            ref[rows_of(s), :] = values[u * SUB:(u + 1) * SUB]

    def tiles(grad_ref, left_ref, right_ref, start, count):
        def one(t, carry):
            cut = pl.ds(pl.multiple_of(t * tile, tile), tile)
            grad_ref[:, cut] = dot(left_ref[...], right_ref[:, cut], 0, 0).astype(grad_ref.dtype)
            return carry

        lax.fori_loop(start, start + count, one, 0)

    @pl.when(jnp.logical_and(i >= swiglu, i < feed))
    def _():
        blocks = pair_of(i - swiglu, per)
        for s in blocks:
            norms.ready(s)
        gate, up, sig = opened(blocks)
        keep(a_ref, blocks, (gate * sig * up).astype(BF))

    at_step(feed - 1, copies[1].wait, lambda: tiles(gsh_ref, a_ref, dy_ref, 0, gsh_ref.shape[1] // tile))
    if line:
        at_step(feed, shrink.start)

    @pl.when(jnp.logical_and(i >= feed, i < feed + steps))
    def _():
        blocks = pair_of(i - feed, per)
        gate, up, sig = opened(blocks)
        dy, a = (jnp.concatenate([ref[rows_of(s), :] for s in blocks], axis=0) for ref in (dy_ref, a_ref))
        da = dot(dy, ws_ref[...], 1, 1)
        dgu = jnp.concatenate([da * up * (sig * (1.0 + gate * (1.0 - sig))), da * (gate * sig)], axis=1).astype(BF)
        keep(dgu_ref, blocks, dgu)
        put_pair(pulled_back, blocks, dot(dgu, we_ref[...], 1, 1).astype(BF))
        put_pair(branch, blocks, dot(a, ws_ref[...]).astype(BF))

    def grad_rows(s, at, summed):
        pulled, gain_grad = rms_pull(h_ref[at, :], gains_ref[:, d:2 * d], summed)
        dh = dy_ref[rows_of(s), :].astype(FP) + pulled
        dh_ref[at, :] = dh
        dg_ref[...] += fold_rows(gain_grad)
        stage[s % per] = dh.astype(BF)
        grads.send(s)

    def chip_rows(mine, k, summed):
        at = rows_of(k)

        @pl.when(mine)
        def _():
            base_ref[at, :] = h_ref[at, :] + summed

        @pl.when(jnp.logical_not(mine))
        def _():
            other_ref[k] = summed.astype(BF)

    in_turn(i, feed, steps, per, ((1, pulled_back.add_chip), (1, lambda s: branch.add(s, chip_rows)),
                                  (3, lambda s: pulled_back.take(s, grad_rows)), (5, grads.pass_on)))
    if line:
        for k in range(1, line):
            at_step(feed + k, lambda k=k: shrink.step(k))
    half = gex_ref.shape[1] // tile // 2
    at_step(feed + steps, lambda: tiles(gex_ref, xn_ref, dgu_ref, 0, half))
    at_step(feed + steps + 1, lambda: tiles(gex_ref, xn_ref, dgu_ref, half, half))

    @pl.when(i == feed + steps + 4)
    def _():
        attended.drain()
        pulled_back.drain()
        norms.drain()
        grads.drain()
        for t in range(4):
            branch.sent(t * per + per - 1)
        lax.fori_loop(0, 4 * per, lambda s, c: (grads.ready(s), c)[1], 0)
        if line:
            shrink.finish(gsh_out)
            shrink.drain()
            first.drain()
            second.drain()


def middle(q, k, vt, tags, bars, wm, x, dy, gains, weights, kv, group, unit, line):
    length = q.shape[0]
    n = LANES
    d = wm.shape[1]
    share = (length // 4, d)
    per = share[0] // SUB
    steps = 2 * per
    we, ws = (w.shape for w in weights)
    shards = 2 * line
    shrink = jax.ShapeDtypeStruct(ws, BF)
    more = []
    if line:
        shrink = jax.ShapeDtypeStruct(ws, FP)
        we, ws = (we[0] * shards, we[1]), (ws[0], ws[1] * shards)
        more = [pltpu.VMEM(ws, BF), *reduce_scratch(line, shrink.shape), *GATHER_SEMS(shards), *GATHER_SEMS(shards)]
    units = ws[0]
    results = [jax.ShapeDtypeStruct(q.shape, BF), jax.ShapeDtypeStruct((length // SUB, 8, SUB * group), FP),
               jax.ShapeDtypeStruct(share, FP), jax.ShapeDtypeStruct((per, SUB, d), BF), jax.ShapeDtypeStruct(we, BF),
               jax.ShapeDtypeStruct(share, FP), jax.ShapeDtypeStruct((length, d), BF), jax.ShapeDtypeStruct((8, d), FP),
               shrink]
    out_specs = [whole(r.shape) for r in results]
    out_specs[6] = ANYWHERE
    held = [q, k, vt, tags, bars, wm, gains]
    return pl.pallas_call(
        partial(middle_kernel, kv, group, unit, line, per, steps),
        grid=(3 * steps + 8,),
        in_specs=[whole(a.shape) for a in held] + [ANYWHERE] * 4,
        out_specs=out_specs,
        out_shape=results,
        scratch_shapes=[pltpu.VMEM((kv, n, SUB * group), FP), pltpu.VMEM((kv, 8, SUB * group), FP),
                        pltpu.VMEM(share, BF), pltpu.VMEM((length, d), BF), pltpu.VMEM(we, BF), pltpu.VMEM(ws, BF),
                        pltpu.SemaphoreType.DMA((4,)),
                        pltpu.VMEM(share, FP), pltpu.VMEM((length, d), BF), pltpu.VMEM((length, units), BF),
                        pltpu.VMEM((length, 2 * units), BF),
                        *pairs_scratch(per, d, True), pltpu.SemaphoreType.DMA((4, 4 * per)),
                        *pairs_scratch(per, d, True), pltpu.VMEM((per, SUB, d), BF),
                        pltpu.SemaphoreType.DMA((4, 4 * per)),
                        *pairs_scratch(per, d, False), *more],
        compiler_params=params(collective_id=1, has_side_effects=True),
        name="middle",
    )(*held, x, dy, *weights)


def back_kernel(kv, group, unit, scale, blocks, per, line, *refs):
    refs = list(refs)
    take = lambda count: [refs.pop(0) for _ in range(count)]
    q_ref, k_ref, v_ref, kt_ref, tags_ref, bars_ref, lse_ref, ctx_block, dh_block, wm_ref = take(10)
    raw_ref, cos_ref, sin_ref, all_gains, base_ref, dg2_ref, other_ref = take(7)
    x_all, dh_all = take(2)
    late_from = take(4)
    grads = take(1) if line else []
    in_ref, out_ref, gains_out = take(3)
    sums = take(3) if line else []
    weight_grads = [] if line else take(2)
    late_to = take(4)
    wp_ref, ctx_ref, dh_ref, xn_ref = late_to
    late_sem = take(1)[0]
    late = [pltpu.make_async_copy(a, b, late_sem.at[w]) for w, (a, b) in enumerate(zip(late_from, late_to))]
    dk_ref, dv_ref, dq_ref, dqkv_ref = take(4)
    b_far, b_sems, x_held, x_near, x_sems = take(5)
    mine_ref, far_ref, x_far, f_sems, x_ref, dh_own, own_sems, heads_ref, fold_ref = take(9)
    place = Place(line)
    i = pl.program_id(0)
    b = blocks - 1 - i
    n = LANES
    pairs = Pairs(place, per, x_held, x_near, x_sems, lambda s: s % x_held.shape[0])
    subs = ROWS // SUB
    share, d = x_ref.shape
    gq, gk = all_gains[:, 2 * d:2 * d + n], all_gains[:, 2 * d + n:]
    tile = 256
    tensors = lax.axis_size("tensor")
    mates = [(place.dp, (place.t + step) % tensors) for step in range(1, tensors)]
    peers = []
    own_rows = pl.ds(pl.multiple_of(place.t * share, share), share)
    own_copies = [pltpu.make_async_copy(x_all.at[own_rows, :], x_ref, own_sems.at[0]),
                  pltpu.make_async_copy(dh_all, dh_own, own_sems.at[1])]
    if line:
        shards = 2 * line
        gm_ref, gp_ref = take(2)
        expand = Reduce(place, grads[0], row_cut(grads[0].shape[0] // shards), *take(4))
        merge = Reduce(place, gm_ref, column_cut(gm_ref.shape[1] // shards), None, *take(3))
        project = Reduce(place, gp_ref, row_cut(gp_ref.shape[0] // shards), None, *take(3))
        shown, over, g_sems = take(3)
        peers = [((place.dp + step) % shards, place.t) for step in range(1, shards)]
    else:
        gp_ref, gm_ref = weight_grads

    def tiles(grad_ref, left_ref, right_ref):
        def one(t, carry):
            cut = pl.ds(pl.multiple_of(t * tile, tile), tile)
            grad_ref[:, cut] = dot(left_ref[...], right_ref[:, cut], 0, 0).astype(grad_ref.dtype)
            return carry

        lax.fori_loop(0, grad_ref.shape[1] // tile, one, 0)

    def project_rows(t):
        cut = pl.ds(pl.multiple_of(t * tile, tile), tile)
        gp_ref[cut, :] = dot(xn_ref[:, cut], dqkv_ref[...], 0, 0).astype(BF)

    def chip(k):
        return send(far_ref.at[k], x_far.at[k], f_sems.at[0, k], f_sems.at[1, k], place.chip)

    def branch(k):
        return send(other_ref.at[k], b_far.at[k], b_sems.at[0, k], b_sems.at[1, k], place.chip)

    @pl.when(i == 0)
    def _():
        barrier = pltpu.get_barrier_semaphore()
        for device in mates + peers:
            pl.semaphore_signal(barrier, inc=1, device_id=device, device_id_type=MESH)
        for copy in late:
            copy.start()
        pl.semaphore_wait(barrier, len(mates + peers))
        if line:
            expand.start()
        for k in range(per):
            branch(k).start()
        dk_ref[...] = jnp.zeros_like(dk_ref)
        dv_ref[...] = jnp.zeros_like(dv_ref)
        heads_ref[...] = jnp.zeros_like(heads_ref)

    @pl.when(i < blocks)
    def _():
        here = pl.ds(pl.multiple_of(b * ROWS, ROWS), ROWS)
        dctx = dot(dh_block[...], wm_ref[...], 1, 1).astype(BF)
        ctx, q = ctx_block[...], q_ref[...]
        bars = jnp.concatenate([bars_ref[...]] * group, axis=0)
        wide, queries, outward, centres, lses = [], [], [], [], []
        for h in range(kv):
            queries.append(stacked(q, h, group))
            wide.append(jnp.concatenate([queries[h], bars], axis=1))
            outward.append(stacked(dctx, h, group))
            both = outward[h].astype(FP) * stacked(ctx, h, group).astype(FP)
            centres.append(jnp.sum(both.T, axis=0, keepdims=True))
            lses.append(jnp.concatenate([lse_ref[u, h:h + 1, g * SUB:(g + 1) * SUB]
                                         for g in range(group) for u in range(ROWS // SUB)], axis=1))
        dq_ref[...] = jnp.zeros_like(dq_ref)

        def chunk(j, diagonal):
            at = pl.ds(pl.multiple_of(j * ROWS, ROWS), ROWS)
            tags = tags_ref[at, :]
            for h in range(kv):
                cut = slice(h * n, (h + 1) * n)
                keys = jnp.concatenate([k_ref[at, cut], tags], axis=1)
                p = jnp.exp2(dot(keys, wide[h], 1, 1) * unit - lses[h])
                if diagonal:
                    p = jnp.where(causal_tile(group), p, 0.0)
                dp = dot(v_ref[at, cut], outward[h], 1, 1)
                ds = (p * (dp - centres[h])).astype(BF)
                dv_ref[at, cut] += dot(p.astype(BF), outward[h])
                dk_ref[at, cut] += dot(ds, queries[h])
                dq_ref[h] += dot(kt_ref[cut, at], ds)

        lax.fori_loop(0, b, lambda j, c: (chunk(j, False), c)[1], 0)
        chunk(b, True)

        cosines, sines = cos_ref[...], sin_ref[...]
        pieces = []
        for h in range(kv):
            dq = dq_ref[h].T
            for c in range(group + 1):
                if c < group:
                    grad, gain, row = dq[c * ROWS:(c + 1) * ROWS] * scale, gq, 0
                else:
                    grad, gain, row = dk_ref[here, h * n:(h + 1) * n] * scale, gk, 1
                grad = grad * cosines - pltpu.roll(grad, n // 2, 1) * sines
                at = (h * (group + 1) + c) * n
                piece, gain_grad = rms_pull(raw_ref[:, at:at + n], gain, grad)
                heads_ref[row] += fold_rows(gain_grad)
                pieces.append(piece)
            pieces.append(dv_ref[here, h * n:(h + 1) * n])
        dqkv = jnp.concatenate(pieces, axis=1).astype(BF)
        dqkv_ref[here, :] = dqkv
        pl.when(i == 0)(late[0].wait)
        part = dot(dqkv, wp_ref[...], 1, 1).astype(BF)
        for u in range(subs):
            s = subs * b + u
            pairs.put(s, part[u * SUB:(u + 1) * SUB], (i >= 2, s + 2 * subs))

    def chip_rows(mine, k, summed):
        @pl.when(mine)
        def _():
            mine_ref[pl.ds(pl.multiple_of(k * SUB, SUB), SUB), :] = summed

        @pl.when(jnp.logical_not(mine))
        def _():
            far_ref[k] = summed.astype(BF)
            chip(k).start()

    @pl.when(i >= 1)
    def _():
        for u in range(subs):
            pairs.add(subs * (b + 1) + u, chip_rows)

    @pl.when(i == 3)
    def _():
        for k in range(per):
            branch(k).wait()
            at = slice(k * SUB, (k + 1) * SUB)
            out_ref[at, :] = (base_ref[at, :] + b_far[k].astype(FP)).astype(BF)
        for copy in own_copies:
            copy.start()

    @pl.when(i == 1)
    def _():
        late[1].wait()
        late[2].wait()
        tiles(gm_ref, ctx_ref, dh_ref)

    if line:
        for step, act in enumerate((lambda: expand.step(1), lambda: expand.step(2), lambda: expand.step(3), merge.start,
                                    lambda: merge.step(1), lambda: merge.step(2))):
            pl.when(i == step)(act)

    def input_rows(k):
        at = slice(k * SUB, (k + 1) * SUB)
        chip(k).wait()
        summed = mine_ref[at, :] + x_far[k].astype(FP)
        pulled, gain_grad = rms_pull(x_ref[at, :].astype(FP), all_gains[:, :d], summed)
        in_ref[at, :] = (dh_own[at, :] + pulled).astype(BF)
        fold_ref[...] += fold_rows(gain_grad)

    def folded(ref):
        pieces = [fold_ref[...], dg2_ref[...], heads_ref[0], heads_ref[1]]
        row = jnp.sum(jnp.concatenate(pieces, axis=1), axis=0, keepdims=True)
        count = row.shape[1] // n
        for j in range(count):
            ref[j:j + 1, :] = row[:, j * n:(j + 1) * n]
        ref[count:, :] = jnp.zeros((ref.shape[0] - count, n), FP)

    def show(buffer, me, devices, first):
        copies = [send(buffer.at[me], buffer.at[me], g_sems.at[0, first + step], g_sems.at[1, first + step], device)
                  for step, device in enumerate(devices, 1)]
        for copy in copies:
            copy.start()
        return copies

    def added(buffer, me, devices, first):
        count = len(devices) + 1
        for step in range(1, count):
            who = (me - step + count) % count
            send(buffer.at[who], buffer.at[who], g_sems.at[0, first + step], g_sems.at[1, first + step],
                 place.sibling).wait_recv()
        total = buffer[0]
        for who in range(1, count):
            total = total + buffer[who]
        return total

    @pl.when(i == blocks)
    def _():
        fold_ref[...] = jnp.zeros_like(fold_ref)
        late[3].wait()
        for copy in own_copies:
            copy.wait()
        if not line:
            tiles(gp_ref, xn_ref, dqkv_ref)
            for k in range(per):
                input_rows(k)
            folded(gains_out)
        else:
            project_rows(project.turn(0))
            project.start()
            for q in range(1, line):
                project_rows(project.turn(q))
            merge.step(3)
            expand.finish(sums[0])
            project.step(1)
            merge.finish(sums[1])
            project.step(2)
            for k in range(per):
                input_rows(k)
            folded(shown.at[place.t])
            copies = show(shown, place.t, mates, 0)
            project.step(3)
            over[place.dp] = added(shown, place.t, mates, 0)
            copies += show(over, place.dp, peers, tensors)
            project.finish(sums[2])
            gains_out[...] = added(over, place.dp, peers, tensors)
            for copy in copies:
                copy.wait_send()
            for r in (expand, merge, project):
                r.drain()
        for s in range(2 * subs):
            pairs.sent(s)


def back(q, k, v, kt, tags, bars, lse, ctx, dh, wm, wp, raw, cosines, sines, gains, xn, base, dg2, other, x, dh_own,
         grads, kv, group, unit, scale, line):
    length = q.shape[0]
    n = LANES
    d = wm.shape[1]
    blocks = length // ROWS
    per = other.shape[0]
    share = base.shape
    block_of = lambda i: jnp.maximum(blocks - 1 - i, 0)
    rows = lambda w: pl.BlockSpec((ROWS, w), lambda i: (block_of(i), 0))
    late = [wp, ctx, dh, xn]
    gain_rows = (-(-(gains.shape[1] // n) // 8) * 8, n)
    scratch = [*[pltpu.VMEM(a.shape, BF) for a in late], pltpu.SemaphoreType.DMA((4,)),
               pltpu.VMEM((length, kv * n), FP), pltpu.VMEM((length, kv * n), FP),
               pltpu.VMEM((kv, n, ROWS * group), FP), pltpu.VMEM((length, wp.shape[1]), BF),
               pltpu.VMEM((per, SUB, d), BF), pltpu.SemaphoreType.DMA((2, per)),
               pltpu.VMEM((2 * ROWS // SUB, SUB, d), BF), pltpu.VMEM((2 * per, SUB, d), BF),
               pltpu.SemaphoreType.DMA((2, 4 * per)),
               pltpu.VMEM(share, FP), pltpu.VMEM((per, SUB, d), BF), pltpu.VMEM((per, SUB, d), BF),
               pltpu.SemaphoreType.DMA((2, per)), pltpu.VMEM(share, BF), pltpu.VMEM(share, FP),
               pltpu.SemaphoreType.DMA((2,)), pltpu.VMEM((2, 8, n), FP), pltpu.VMEM((8, d), FP)]
    results = [jax.ShapeDtypeStruct(share, BF), jax.ShapeDtypeStruct(share, BF), jax.ShapeDtypeStruct(gain_rows, FP)]
    if line:
        shards = 2 * line
        own = [(grads[0].shape[0] // shards, grads[0].shape[1]), (wm.shape[0], wm.shape[1] // shards),
               (wp.shape[0] // shards, wp.shape[1])]
        results += [jax.ShapeDtypeStruct(s, FP) for s in own]
        scratch += [pltpu.VMEM(wm.shape, BF), pltpu.VMEM(wp.shape, BF)]
        for w, s in enumerate(own):
            scratch += reduce_scratch(line, s, w == 0)
        scratch += [pltpu.VMEM((4, *gain_rows), FP), pltpu.VMEM((shards, *gain_rows), FP),
                    pltpu.SemaphoreType.DMA((2, 4 + shards))]
    else:
        results += [jax.ShapeDtypeStruct(wp.shape, BF), jax.ShapeDtypeStruct(wm.shape, BF)]
    args = [q, k, v, kt, tags, bars, lse, ctx, dh, wm, raw, cosines, sines, gains, base, dg2]
    more = [other, x, dh_own, *late, *grads]
    specs = [whole(a.shape) for a in args] + [ANYWHERE] * len(more)
    for at in (0, 5, 7, 8, 10, 11, 12):
        specs[at] = rows(args[at].shape[1])
    specs[6] = pl.BlockSpec((ROWS // SUB, 8, SUB * group), lambda i: (block_of(i), 0, 0))
    return pl.pallas_call(
        partial(back_kernel, kv, group, unit, scale, blocks, per, line),
        grid=(blocks + 1,),
        in_specs=specs,
        out_specs=[whole(r.shape) for r in results],
        out_shape=results,
        scratch_shapes=scratch,
        compiler_params=params(collective_id=3, has_side_effects=True),
        name="back",
    )(*args, *more)


def adamw_step(weight, moment_one, moment_two, gradient, step_rate, decay):
    mean_next = BETA_ONE * moment_one + (1.0 - BETA_ONE) * gradient
    square_next = BETA_TWO * moment_two + (1.0 - BETA_TWO) * gradient * gradient
    mean_hat = mean_next / (1.0 - BETA_ONE**STEP)
    square_hat = square_next / (1.0 - BETA_TWO**STEP)
    weight_next = weight - step_rate * (mean_hat / (jnp.sqrt(square_hat) + EPS_ADAM) + decay * weight)
    return weight_next, mean_next, square_next


def shards(
    tokens, cotangent, parents, token_segment, tree_id,
    projection_weight, projection_first_moment, projection_second_moment,
    merge_master, merge_mean, merge_square,
    expand_master, expand_mean, expand_square,
    shrink_master, shrink_mean, shrink_square,
    gain_master, gain_mean, gain_square,
):
    x = tokens[0]
    dy = cotangent[0]
    length, d = x.shape
    d_own, kv, per, n = projection_weight.shape
    group = per - 2
    units = expand_master.shape[2]
    scale = n ** (-0.5)
    unit = scale * math.log2(math.e)
    line = 4 if lax.axis_size("dp") == 8 and d_own % LANES == 0 else 0
    if line:
        masters = (projection_weight.reshape(d_own, kv * per, n), merge_master, expand_master, shrink_master)
    else:
        wp, we = (lax.all_gather(w.astype(BF).reshape(d_own, -1), "dp", axis=0, tiled=True)
                  for w in (projection_weight, expand_master))
        wm, ws = (lax.all_gather(w.astype(BF), "dp", axis=1, tiled=True) for w in (merge_master, shrink_master))
        masters = (wp,)

    gains = gain_master[None]
    fronts = front(x, gains, token_segment, parents, tree_id, masters, kv, group, line)
    xn1, q, k, v, kt, vt, raw, tags, bars, cosines, sines = fronts[:11]
    if line:
        wp, wm, *low = fronts[11:]
    else:
        low = (we, ws)
    ctx, lse, base, other, expand_grad, dh, dhb, dg2, shrink_sum = middle(
        q, k, vt, tags, bars, wm, x, dy, gains, low, kv, group, unit, line)
    backs = back(q, k, v, kt, tags, bars, lse, ctx, dhb, wm, wp, raw, cosines, sines, gains, xn1,
                 base, dg2, other, x, dh, (expand_grad,) if line else (), kv, group, unit, scale, line)
    input_grad, output, gain_rows = backs[:3]
    if line:
        expand_sum, merge_sum, project_sum = backs[3:]
    else:
        gain_rows = lax.psum(gain_rows, ("dp", "tensor"))
        project_sum, expand_sum = (
            lax.psum_scatter(g, "dp", scatter_dimension=0, tiled=True) for g in (backs[3], expand_grad))
        merge_sum, shrink_sum = (
            lax.psum_scatter(g, "dp", scatter_dimension=1, tiled=True) for g in (backs[4], shrink_sum))
    output, input_grad = output[None], input_grad[None]
    gain_grad = gain_rows.reshape(-1)[:gain_master.shape[0]]

    outs = [output, input_grad]
    for weight, mean, square, grad, rate in (
        (projection_weight, projection_first_moment, projection_second_moment, project_sum, RATE_PROJECT),
        (merge_master, merge_mean, merge_square, merge_sum, RATE_MERGE),
        (expand_master, expand_mean, expand_square, expand_sum, RATE_EXPAND),
        (shrink_master, shrink_mean, shrink_square, shrink_sum, RATE_SHRINK),
    ):
        grad = grad.astype(FP).reshape(weight.shape)
        after, mean_next, square_next = adamw_step(weight, mean, square, grad, rate, DECAY)
        outs += [after, mean_next, square_next, after.astype(BF)]
    gain_next, gain_mean_next, gain_square_next = adamw_step(
        gain_master, gain_mean, gain_square, gain_grad, RATE_GAIN, 0.0)
    return (*outs, gain_mean_next, gain_square_next, gain_next)


def solution(mesh):
    tokens = P("dp", None, None)
    project = P("dp", "tensor", None, None)
    columns = P("tensor", "dp")
    expand = P("dp", None, "tensor")
    shared = P("dp", "tensor", None)
    return jax.shard_map(
        shards,
        mesh=mesh,
        in_specs=(tokens, tokens, P(), P("dp", None), P("dp"), *[project] * 3, *[columns] * 3, *[expand] * 3,
                  *[columns] * 3, P(), P(), P()),
        out_specs=(shared, shared, *[project] * 4, *[columns] * 4, *[expand] * 4, *[columns] * 4, P(), P(), P()),
        check_vma=False,
    )
```

```python
import math
from functools import partial

import jax
import jax.numpy as jnp
import numpy as np
from jax import lax
from jax.experimental import pallas as pl
from jax.experimental.pallas import tpu as pltpu
from jax.sharding import PartitionSpec as P

STEP = 5
EPS_NORM = 1e-06
THETA = 1000000.0
BETA_ONE = 0.5
BETA_TWO = 0.5
EPS_ADAM = 1e-08
DECAY = 0.1
RATE_PROJECT = 0.05
RATE_MERGE = 0.3
RATE_EXPAND = 0.05
RATE_SHRINK = 0.03
RATE_GAIN = 0.3

BF = jnp.bfloat16
FP = jnp.float32
ROWS = 256
LANES = 128
SUB = 128
MESH = pl.DeviceIdType.MESH
BLOCKED = -1e30
VMEM_LIMIT = 56 * 2**20


def params(**more):
    return pltpu.CompilerParams(vmem_limit_bytes=VMEM_LIMIT, **more)


def dot(a, b, ca=1, cb=0):
    return lax.dot_general(a, b, (((ca,), (cb,)), ((), ())), preferred_element_type=FP)


def inverse_rms(values):
    return lax.rsqrt(jnp.mean(values * values, axis=-1, keepdims=True) + EPS_NORM)


def rms_pull(values, scales, grad):
    r = inverse_rms(values)
    scaled = grad * scales
    mean = jnp.mean(values * scaled, axis=-1, keepdims=True)
    return r * scaled - values * (r * r * r * mean), grad * values * r


def fold_rows(values):
    n, w = values.shape
    return jnp.sum(values.reshape(n // 8, 8, w), axis=0)


class Place:
    def __init__(self, line):
        self.line = line
        self.dp, self.t = lax.axis_index("dp"), lax.axis_index("tensor")
        self.z, self.y = self.dp // 2, self.dp % 2
        self.x, self.c = self.t // 2, self.t % 2
        self.has_up, self.has_down = self.z < line - 1, self.z > 0
        self.up, self.down = (self.dp + 2, self.t), (self.dp - 2, self.t)
        self.across = (self.dp + 1 - 2 * self.y, self.t)
        self.sibling = (self.dp, self.t + 1 - 2 * self.c)
        self.chip = (self.dp, (1 - self.x) * 2 + self.c)

    def greet(self, tensor, line, meanwhile=None):
        barrier = pltpu.get_barrier_semaphore()

        def signal(device):
            pl.semaphore_signal(barrier, inc=1, device_id=device, device_id_type=MESH)

        if tensor:
            signal(self.sibling)
            signal(self.chip)
        if line:
            signal(self.across)
            pl.when(self.has_up)(lambda: signal(self.up))
            pl.when(self.has_down)(lambda: signal(self.down))
        peers = (2 if tensor else 0) + (1 if line else 0)
        if line:
            peers = peers + jnp.where(self.has_up, 1, 0) + jnp.where(self.has_down, 1, 0)
        if meanwhile is not None:
            meanwhile()
        pl.semaphore_wait(barrier, peers)


def send(src, dst, sent, arrived, device):
    return pltpu.make_async_remote_copy(
        src_ref=src, dst_ref=dst, send_sem=sent, recv_sem=arrived, device_id=device, device_id_type=MESH)


def row_cut(size):
    return lambda j: (pl.ds(pl.multiple_of(j * size, size), size), slice(None))


def column_cut(size):
    return lambda j: (slice(None), pl.ds(pl.multiple_of(j * size, size), size))


class Gather:
    def __init__(self, place, own, full, cut, sems, local):
        self.place, self.own, self.full, self.cut, self.sems, self.local = place, own, full, cut, sems, local

    def copy(self, kind, src, j):
        p = self.place
        device = (p.up, p.down, p.across)[kind]
        return send(src, self.full.at[self.cut(j)], self.sems.at[kind, j], self.sems.at[3, j], device)

    def kept(self):
        return pltpu.make_async_copy(self.own, self.full.at[self.cut(self.place.dp)], self.local)

    def source(self):
        return self.full.at[self.cut(self.place.dp)] if self.own is None else self.own

    def start(self):
        p = self.place
        self.copy(2, self.source(), p.dp).start()
        pl.when(p.has_up)(lambda: self.copy(0, self.source(), p.dp).start())
        pl.when(p.has_down)(lambda: self.copy(1, self.source(), p.dp).start())
        if self.own is not None:
            self.kept().start()

    def arrivals(self, k):
        p = self.place
        return ((0, p.z >= k, (p.z - k) * 2 + p.y, p.has_up), (1, p.z + k < p.line, (p.z + k) * 2 + p.y, p.has_down))

    def hop(self, k):
        for kind, here, j, further in self.arrivals(k):
            @pl.when(here)
            def _(kind=kind, j=j, further=further):
                piece = self.full.at[self.cut(j)]
                self.copy(kind, piece, j).wait_recv()
                pl.when(further)(lambda: self.copy(kind, piece, j).start())
                self.copy(2, piece, j).start()

    def finish(self):
        p = self.place
        if self.own is not None:
            self.kept().wait()
        for zz in range(p.line):
            j = zz * 2 + 1 - p.y
            self.copy(2, self.full.at[self.cut(j)], j).wait_recv()

    def drain(self):
        p = self.place
        self.copy(2, self.source(), p.dp).wait_send()
        pl.when(p.has_up)(lambda: self.copy(0, self.source(), p.dp).wait_send())
        pl.when(p.has_down)(lambda: self.copy(1, self.source(), p.dp).wait_send())
        for k in range(1, p.line):
            for kind, here, j, further in self.arrivals(k):
                @pl.when(here)
                def _(kind=kind, j=j, further=further):
                    piece = self.full.at[self.cut(j)]
                    pl.when(further)(lambda: self.copy(kind, piece, j).wait_send())
                    self.copy(2, piece, j).wait_send()


class Reduce:
    def __init__(self, place, grad, cut, kept, across, lined, sems):
        self.place, self.grad, self.cut, self.kept, self.sems = place, grad, cut, kept, sems
        self.across, self.lined = across, lined

    def cross(self, zz):
        p = self.place
        return send(self.grad.at[self.cut(zz * 2 + 1 - p.y)], self.across.at[zz],
                    self.sems.at[0, zz], self.sems.at[1, zz], p.across)

    def climb(self, t):
        return send(self.across.at[t], self.lined.at[t + 1], self.sems.at[2, t], self.sems.at[3, t], self.place.up)

    def sink(self, t):
        return send(self.across.at[t], self.lined.at[t], self.sems.at[4, t], self.sems.at[5, t], self.place.down)

    def load(self, zz):
        return pltpu.make_async_copy(self.grad.at[self.cut(zz * 2 + self.place.y)], self.kept.at[zz], self.sems.at[6, zz])

    def mine(self, zz):
        if self.kept is None:
            return self.grad[self.cut(zz * 2 + self.place.y)].astype(FP)
        return self.kept[zz].astype(FP)

    def loaded(self, zz):
        if self.kept is not None:
            self.load(zz).wait()

    def turn(self, q):
        z = self.place.z
        low = z < 2
        if q == 0:
            return jnp.where(low, 3, 0)
        if q == 1:
            return jnp.where(low, 2, 1)
        if q == 2:
            return jnp.where(low, 1 - z, 5 - z)
        return z

    def start(self):
        self.cross(self.turn(0)).start()
        if self.kept is not None:
            for zz in range(self.place.line):
                self.load(zz).start()

    def advance(self, q):
        self.cross(self.turn(q - 1)).wait_send()
        self.cross(self.turn(q)).start()

    def hop(self, h):
        p = self.place

        def pass_on(t, coming, more, slot):
            self.loaded(t)
            self.cross(t).wait_recv()

            @pl.when(jnp.logical_not(more))
            def _():
                self.across[t] = (self.mine(t) + self.across[t].astype(FP)).astype(BF)

            @pl.when(more)
            def _():
                coming(t).wait_recv()
                self.across[t] = (self.mine(t) + self.across[t].astype(FP) + self.lined[slot].astype(FP)).astype(BF)

            coming(t).start()

        pl.when(p.z < h)(lambda: pass_on(p.z + p.line - h, self.climb, p.has_down, p.z + p.line - h + 1))
        pl.when(p.z >= p.line - h)(lambda: pass_on(p.z - p.line + h, self.sink, p.has_up, p.z - p.line + h))

    def finish(self, write):
        p = self.place
        self.loaded(p.z)
        self.cross(p.z).wait_recv()
        pl.when(p.has_down)(lambda: self.climb(p.z).wait_recv())
        pl.when(p.has_up)(lambda: self.sink(p.z).wait_recv())
        from_below = jnp.where(p.has_down, self.lined[p.z + 1].astype(FP), 0.0)
        from_above = jnp.where(p.has_up, self.lined[p.z].astype(FP), 0.0)
        write(self.mine(p.z) + self.across[p.z].astype(FP) + from_below + from_above)

    def step(self, k):
        self.advance(k)
        self.hop(k)

    def drain(self):
        p = self.place
        self.cross(p.z).wait_send()
        for zz in range(p.line):
            pl.when(zz > p.z)(lambda zz=zz: self.climb(zz).wait_send())
            pl.when(zz < p.z)(lambda zz=zz: self.sink(zz).wait_send())


def write_to(ref):
    def write(values):
        if len(ref.shape) == 2:
            ref[...] = values
            return
        width = ref.shape[2]
        for j in range(ref.shape[1]):
            ref[:, j, :] = values[:, j * width:(j + 1) * width]

    return write


def reduce_scratch(line, shape, kept=False):
    return [pltpu.VMEM((line, *shape), BF)] * kept + [pltpu.VMEM((line, *shape), BF), pltpu.VMEM((line + 1, *shape), BF),
                                                      pltpu.SemaphoreType.DMA((7, line))]


class Pairs:
    def __init__(self, place, per, held, near, sems, slot_of):
        self.place, self.per, self.held, self.near, self.sems, self.slot_of = place, per, held, near, sems, slot_of

    def near_slot(self, s):
        return (s // (2 * self.per)) * self.per + s % self.per

    def to_sibling(self, s):
        return send(self.held.at[self.slot_of(s)], self.near.at[self.near_slot(s)], self.sems.at[0, s],
                    self.sems.at[1, s], self.place.sibling)

    def sends(self, s):
        return self.place.c != (s // self.per) % 2

    def sent(self, s):
        pl.when(self.sends(s))(lambda: self.to_sibling(s).wait_send())

    def put(self, s, rows, before=None):
        if before is not None:
            pl.when(before[0])(lambda: self.sent(before[1]))
        self.held[self.slot_of(s)] = rows
        pl.when(self.sends(s))(lambda: self.to_sibling(s).start())

    def put_next(self, s, rows):
        self.put(s, rows, (s % self.per >= 1, s - 1))

    def add(self, s, use):
        t = s // self.per

        @pl.when(self.place.c == t % 2)
        def _():
            self.to_sibling(s).wait_recv()
            use(self.place.x == t // 2, s % self.per,
                self.held[self.slot_of(s)].astype(FP) + self.near[self.near_slot(s)].astype(FP))


class Exchange(Pairs):
    def __init__(self, place, per, held, near, far, total, sems):
        super().__init__(place, per, held, near, sems, lambda s: s // per)
        self.far, self.total = far, total

    def rows(self, k):
        return pl.ds(pl.multiple_of(k * SUB, SUB), SUB)

    def to_chip(self, s):
        return send(self.near.at[self.near_slot(s)], self.far.at[s % self.per], self.sems.at[2, s], self.sems.at[3, s],
                    self.place.chip)

    def add_chip(self, s):
        def use(mine, k, summed):
            @pl.when(jnp.logical_not(mine))
            def _():
                self.near[self.near_slot(s)] = summed.astype(BF)
                self.to_chip(s).start()

            @pl.when(mine)
            def _():
                self.total[self.rows(k), :] = summed

        self.add(s, use)

    def take(self, s, use):
        @pl.when(s // self.per == self.place.t)
        def _():
            k = s % self.per
            self.to_chip(s).wait_recv()
            use(s, self.rows(k), self.total[self.rows(k), :] + self.far[k].astype(FP))

    def drain(self):
        p = self.place

        def one(s, carry):
            t = s // self.per
            pl.when(s % self.per == self.per - 1)(lambda: self.sent(s))
            pl.when(jnp.logical_and(p.c == t % 2, p.x != t // 2))(lambda: self.to_chip(s).wait_send())
            return carry

        lax.fori_loop(0, 4 * self.per, one, 0)


def pair_of(step, per):
    t = step % 2
    return t * per + step // 2, (3 - t) * per + step // 2


def pairs_scratch(per, d, exchange):
    rows = [pltpu.VMEM((4, SUB, d), BF), pltpu.VMEM((2 * per, SUB, d), BF)]
    return rows + [pltpu.VMEM((per, SUB, d), BF)] * exchange + [pltpu.SemaphoreType.DMA((4 if exchange else 2, 4 * per))]


class Spread:
    def __init__(self, place, per, stage, full, sems):
        self.place, self.per, self.stage, self.full, self.sems = place, per, stage, full, sems

    def rows(self, s):
        return self.full.at[pl.ds(pl.multiple_of(s * SUB, SUB), SUB), :]

    def source(self, s):
        return self.rows(s) if self.stage is None else self.stage.at[s % self.per]

    def copy(self, kind, src, s):
        device = (self.place.chip, self.place.sibling)[kind]
        return send(src, self.rows(s), self.sems.at[kind, s], self.sems.at[2, s], device)

    def kept(self, s):
        return pltpu.make_async_copy(self.source(s), self.rows(s), self.sems.at[3, s])

    def send(self, s):
        for kind in (0, 1):
            self.copy(kind, self.source(s), s).start()
        if self.stage is not None:
            self.kept(s).start()

    def owns(self, s):
        return s // self.per == self.place.t

    def passes(self, s):
        t = s // self.per
        return jnp.logical_and(self.place.c == t % 2, self.place.x != t // 2)

    def pass_on(self, s):
        @pl.when(self.passes(s))
        def _():
            self.copy(1, self.rows(s), s).wait_recv()
            self.copy(1, self.rows(s), s).start()

    def ready(self, s):
        if self.stage is not None:
            pl.when(self.owns(s))(lambda: self.kept(s).wait())
        pl.when((s // self.per) % 2 != self.place.c)(lambda: self.copy(1, self.rows(s), s).wait_recv())

    def drain(self):
        def one(s, carry):
            @pl.when(self.owns(s))
            def _():
                self.copy(0, self.source(s), s).wait_send()
                self.copy(1, self.source(s), s).wait_send()

            pl.when(self.passes(s))(lambda: self.copy(1, self.rows(s), s).wait_send())
            return carry

        lax.fori_loop(0, 4 * self.per, one, 0)


def whole(shape):
    return pl.BlockSpec(tuple(shape), lambda i: (0,) * len(shape), pipeline_mode=pl.Buffered(1))


ANYWHERE = pl.BlockSpec(memory_space=pl.ANY)
GATHER_SEMS = lambda shards: [pltpu.SemaphoreType.DMA((4, shards)), pltpu.SemaphoreType.DMA]


def make_tables(seg_ref, parents_ref, tree_ref, freq_ref, tags_ref, bars_ref, cos_ref, sin_ref):
    count = parents_ref.shape[1]
    n = LANES
    blocks = sin_ref.shape[0] // ROWS
    lane = lax.broadcasted_iota(jnp.int32, (1, n), 1).astype(FP)
    place_of = lambda b: pl.ds(pl.multiple_of(b * ROWS, ROWS), ROWS)

    def columns(b, carry):
        sin_ref[place_of(b), :] = jnp.broadcast_to(seg_ref[:, place_of(b)].astype(FP), (n, ROWS)).T
        return carry

    def tally(b, carry):
        column = sin_ref[place_of(b), :]
        return (carry[0] + fold_rows(jnp.where(column == lane, 1.0, 0.0)),
                carry[1] + fold_rows(jnp.where(column < lane, 1.0, 0.0)))

    lax.fori_loop(0, blocks, columns, 0)
    sizes, starts = lax.fori_loop(0, blocks, tally, (jnp.zeros((8, n), FP), jnp.zeros((8, n), FP)))
    sizes, starts = (jnp.sum(a, axis=0, keepdims=True) for a in (sizes, starts))
    table = parents_ref[...]
    chosen = jnp.where(lax.broadcasted_iota(jnp.int32, table.shape, 0) == tree_ref[0], table, 0)
    chosen = jnp.sum(chosen.astype(FP), axis=0, keepdims=True)
    parents = jnp.zeros((1, n), FP)
    for b in range(count):
        parents = jnp.where(lane == b, chosen[:, b:b + 1], parents)
    shifts = jnp.where(lane != 0, sizes[:, :1], 0.0) - starts

    def rows(b, carry):
        at = place_of(b)
        column = sin_ref[at, :]
        hot = column == lane
        parent = jnp.sum(jnp.where(hot, parents, 0.0), axis=1, keepdims=True)
        above = jnp.where(jnp.logical_and(lane == parent, lane != 0), sizes, 0.0)
        first = (b * ROWS).astype(FP)
        position = (lax.broadcasted_iota(jnp.int32, (ROWS, 1), 0).astype(FP) + first
                    + jnp.sum(jnp.where(hot, shifts, 0.0) + above, axis=1, keepdims=True))
        tags_ref[at, :] = jnp.where(hot, 1.0, 0.0).astype(BF)
        open_to = jnp.logical_or(jnp.logical_or(hot, lane == parent), jnp.logical_or(lane == 0, lane >= count))
        bars_ref[at, :] = jnp.where(open_to, 0.0, BLOCKED).astype(BF)
        angles = position * freq_ref[...]
        cos_ref[at, :] = jnp.cos(angles)
        turned = jnp.sin(angles)
        sin_ref[at, :] = jnp.where(lane < n // 2, -turned, turned)
        return carry

    lax.fori_loop(0, blocks, rows, 0)


def front_kernel(kv, group, line, *refs):
    refs = list(refs)
    take = lambda count: [refs.pop(0) for _ in range(count)]
    x_ref, gains_ref, seg_ref, parents_ref, tree_ref, freq_ref = take(6)
    masters = take(4) if line else take(1)
    xn_ref, q_ref, k_ref, v_ref, kt_ref, vt_ref, raw_ref, tags_ref, bars_ref, cos_ref, sin_ref = take(11)
    if line:
        wp_out, wm_out, we_low, ws_low = take(4)
        wp_ref, wm_low, p_sems, p_local, m_sems, m_local, out_sem = take(7)
    else:
        wp_ref = masters[0]
    xn_full, xn_sem = take(2)
    i = pl.program_id(0)
    final = pl.num_programs(0) - 1
    d = x_ref.shape[1]
    n = LANES
    per = group + 2
    if line:
        place = Place(line)
        size = masters[0].shape[0]
        project = Gather(place, None, wp_ref, row_cut(size), p_sems, p_local)
        merge = Gather(place, wm_low, wm_out, column_cut(wm_low.shape[1]), m_sems, m_local)
        written = pltpu.make_async_copy(wp_ref, wp_out, out_sem)
    normed = pltpu.make_async_copy(xn_full, xn_ref, xn_sem)

    def round_projection():
        at = pl.ds(pl.multiple_of(place.dp * size, size), size)
        for j in range(kv * per):
            wp_ref[at, j * n:(j + 1) * n] = masters[0][:, j, :].astype(BF)

    def norm(b, carry):
        at = pl.ds(pl.multiple_of(b * ROWS, ROWS), ROWS)
        x = x_ref[at, :].astype(FP)
        xn_full[at, :] = (x * inverse_rms(x) * gains_ref[:, :d]).astype(BF)
        return carry

    @pl.when(i == 0)
    def _():
        if line:
            place.greet(False, True, round_projection)
            project.start()
        lax.fori_loop(0, x_ref.shape[0] // ROWS, norm, 0)
        normed.start()
        if line:
            project.hop(1)
        make_tables(seg_ref, parents_ref, tree_ref, freq_ref, tags_ref, bars_ref, cos_ref, sin_ref)
        if line:
            project.hop(2)
            wm_low[...] = masters[1][...].astype(BF)
            units = masters[2].shape[2]
            for half in range(2):
                we_low[:, half * units:(half + 1) * units] = masters[2][:, half, :].astype(BF)
            ws_low[...] = masters[3][...].astype(BF)
            project.hop(3)
            merge.start()
            project.finish()
            written.start()

    if line:
        for k in range(1, line):
            pl.when(i == k + 1)(lambda k=k: merge.hop(k))
    at = pl.ds(pl.multiple_of(i * ROWS, ROWS), ROWS)
    qkv = dot(xn_full[at, :], wp_ref[...])
    cosines, sines = cos_ref[at, :], sin_ref[at, :]
    gq, gk = gains_ref[:, 2 * d:2 * d + n], gains_ref[:, 2 * d + n:]
    keys, values = [], []
    for h in range(kv):
        for c in range(group + 1):
            raw = qkv[:, (h * per + c) * n:(h * per + c + 1) * n]
            to = (h * (group + 1) + c) * n
            raw_ref[:, to:to + n] = raw
            y = raw * inverse_rms(raw) * (gq if c < group else gk)
            turned = y * cosines + pltpu.roll(y, n // 2, 1) * sines
            if c < group:
                to = (h * group + c) * n
                q_ref[:, to:to + n] = turned.astype(BF)
            else:
                keys.append(turned)
        values.append(qkv[:, (h * per + group + 1) * n:(h * per + group + 2) * n])
    for h in range(kv):
        k_ref[:, h * n:(h + 1) * n] = keys[h].astype(BF)
        v_ref[:, h * n:(h + 1) * n] = values[h].astype(BF)
        kt_ref[h * n:(h + 1) * n, :] = keys[h].T.astype(BF)
        vt_ref[h * n:(h + 1) * n, :] = values[h].T.astype(BF)

    @pl.when(i == final)
    def _():
        normed.wait()
        if line:
            merge.finish()
            merge.drain()
            project.drain()
            written.wait()


def front(x, gains, segments, parents, tree, masters, kv, group, line):
    length, d = x.shape
    n = LANES
    rows = lambda w: pl.BlockSpec((ROWS, w), lambda i: (i, 0))
    cols = pl.BlockSpec((kv * n, ROWS), lambda i: (0, i))
    out = lambda w, t: jax.ShapeDtypeStruct((length, w), t)
    raw_w = kv * (group + 1) * n
    freq = np.float32(THETA ** (-(np.arange(n) % (n // 2)) * 2.0 / n))[None]
    more_specs, more_shapes, scratch = [], [], []
    if line:
        shards = 2 * line
        project, merge, expand, shrink = (m.shape for m in masters)
        wp_shape = (project[0] * shards, project[1] * n)
        more_shapes = [jax.ShapeDtypeStruct(wp_shape, BF), jax.ShapeDtypeStruct((merge[0], merge[1] * shards), BF),
                       jax.ShapeDtypeStruct((expand[0], 2 * expand[2]), BF), jax.ShapeDtypeStruct(shrink, BF)]
        more_specs = [ANYWHERE, ANYWHERE, whole(more_shapes[2].shape), whole(more_shapes[3].shape)]
        scratch = [pltpu.VMEM(wp_shape, BF), pltpu.VMEM(merge, BF), *GATHER_SEMS(shards), *GATHER_SEMS(shards),
                   pltpu.SemaphoreType.DMA]
    table = whole((length, n))
    return pl.pallas_call(
        partial(front_kernel, kv, group, line),
        grid=(length // ROWS,),
        in_specs=[whole(x.shape), whole(gains.shape), whole(segments.shape), whole(parents.shape),
                  pl.BlockSpec(memory_space=pltpu.SMEM), whole(freq.shape), *[whole(m.shape) for m in masters]],
        out_specs=[ANYWHERE, rows(kv * group * n), rows(kv * n), rows(kv * n), cols, cols, rows(raw_w),
                   table, table, table, table, *more_specs],
        out_shape=[out(d, BF), out(kv * group * n, BF), out(kv * n, BF), out(kv * n, BF),
                   jax.ShapeDtypeStruct((kv * n, length), BF), jax.ShapeDtypeStruct((kv * n, length), BF),
                   out(raw_w, FP), out(n, BF), out(n, BF), out(n, FP), out(n, FP), *more_shapes],
        scratch_shapes=[*scratch, pltpu.VMEM((length, d), BF), pltpu.SemaphoreType.DMA],
        compiler_params=params(**({"collective_id": 0, "has_side_effects": True} if line else {})),
        name="front",
    )(x, gains, segments, parents, tree, freq, *masters)


def stacked(ref_block, h, group):
    n = LANES
    return jnp.concatenate(
        [ref_block[:, (h * group + g) * n:(h * group + g + 1) * n] for g in range(group)], axis=0)


def causal_tile(group, rows=ROWS, after=0):
    key_at = lax.broadcasted_iota(jnp.int32, (ROWS, rows * group), 0)
    query_at = lax.broadcasted_iota(jnp.int32, (ROWS, rows * group), 1) % rows
    return key_at <= query_at + after


def in_turn(i, first, steps, per, acts):
    for behind, act in acts:
        @pl.when(jnp.logical_and(i - first - behind >= 0, i - first - behind < steps))
        def _(behind=behind, act=act):
            for s in pair_of(i - first - behind, per):
                act(s)


def middle_kernel(kv, group, unit, line, per, steps, *refs):
    refs = list(refs)
    take = lambda count: [refs.pop(0) for _ in range(count)]
    q_ref, k_ref, vt_ref, tags_ref, bars_ref, wm_ref, gains_ref, x_all, dy_all = take(9)
    weights = take(2)
    ctx_ref, lse_ref, base_ref, other_ref, gex_ref, dh_ref, dhb_ref, dg_ref, gsh_out = take(9)
    acc_ref, sum_ref, x_ref, dy_ref, we_ref, ws_ref, copy_sems = take(7)
    h_ref, xn_ref, a_ref, dgu_ref = take(4)
    h_held, h_near, h_far, h_sems, xn_sems = take(5)
    d_held, d_near, d_far, d_sems, stage, dh_sems = take(6)
    b_held, b_near, b_sems = take(3)
    place = Place(line)
    i = pl.program_id(0)
    n = LANES
    share, d = x_ref.shape
    units = ws_ref.shape[0]
    tile = 256
    attended = Exchange(place, per, h_held, h_near, h_far, h_ref, h_sems)
    norms = Spread(place, per, None, xn_ref, xn_sems)
    pulled_back = Exchange(place, per, d_held, d_near, d_far, dh_ref, d_sems)
    grads = Spread(place, per, stage, dhb_ref, dh_sems)
    branch = Pairs(place, per, b_held, b_near, b_sems, lambda s: s // per)
    own_share = x_all.at[pl.ds(pl.multiple_of(place.t * share, share), share), :]
    copies = [pltpu.make_async_copy(own_share, x_ref, copy_sems.at[0]),
              pltpu.make_async_copy(dy_all, dy_ref, copy_sems.at[1])]
    if line:
        gsh_ref = take(1)[0]
        shrink = Reduce(place, gsh_ref, column_cut(gsh_ref.shape[1] // (2 * line)), None, *take(3))
        cuts = (row_cut(weights[0].shape[0]), column_cut(weights[1].shape[1]))
        first, second = [Gather(place, weights[w], (we_ref, ws_ref)[w], cuts[w], *take(2)) for w in range(2)]
    else:
        gsh_ref = gsh_out
        copies += [pltpu.make_async_copy(weights[0], we_ref, copy_sems.at[2]),
                   pltpu.make_async_copy(weights[1], ws_ref, copy_sems.at[3])]
    rows_of = lambda s: pl.ds(pl.multiple_of(s * SUB, SUB), SUB)

    def at_step(step, *acts):
        @pl.when(i == step)
        def _():
            for act in acts:
                act()

    @pl.when(i == 0)
    def _():
        place.greet(True, bool(line))
        if line:
            first.start()
        for copy in copies:
            copy.start()
        dg_ref[...] = jnp.zeros_like(dg_ref)


    def block(s):
        here = rows_of(s)
        bars = jnp.concatenate([bars_ref[here, :]] * group, axis=0)
        q = q_ref[here, :]
        wide = [jnp.concatenate([stacked(q, h, group), bars], axis=1) for h in range(kv)]
        acc_ref[...] = jnp.zeros_like(acc_ref)
        sum_ref[...] = jnp.zeros_like(sum_ref)

        def chunk(j, diagonal):
            at = pl.ds(pl.multiple_of(j * ROWS, ROWS), ROWS)
            tags = tags_ref[at, :]
            for h in range(kv):
                keys = jnp.concatenate([k_ref[at, h * n:(h + 1) * n], tags], axis=1)
                scores = dot(keys, wide[h], 1, 1)
                e = jnp.exp2(scores * unit)
                if diagonal:
                    e = jnp.where(causal_tile(group, SUB, (s % 2) * SUB), e, 0.0)
                sum_ref[h] += fold_rows(e)
                acc_ref[h] += dot(vt_ref[h * n:(h + 1) * n, at], e.astype(BF))

        lax.fori_loop(0, s // 2, lambda j, c: (chunk(j, False), c)[1], 0)
        chunk(s // 2, True)
        parts = []
        for h in range(kv):
            sums = jnp.sum(sum_ref[h], axis=0, keepdims=True)
            lse_ref[s, h:h + 1, :] = jnp.log2(sums)
            ctx = (acc_ref[h] / sums).T
            parts += [ctx[g * SUB:(g + 1) * SUB] for g in range(group)]
        ctx_ref[here, :] = jnp.concatenate(parts, axis=1).astype(BF)

    def put_pair(pairs, blocks, part):
        for u, s in enumerate(blocks):
            pairs.put_next(s, part[u * SUB:(u + 1) * SUB])

    @pl.when(i < steps)
    def _():
        blocks = pair_of(i, per)
        for s in blocks:
            block(s)
        ctx = jnp.concatenate([ctx_ref[rows_of(s), :] for s in blocks], axis=0)
        put_pair(attended, blocks, dot(ctx, wm_ref[...]).astype(BF))

    def hidden_rows(s, at, summed):
        hidden = x_ref[at, :].astype(FP) + summed
        h_ref[at, :] = hidden
        xn_ref[rows_of(s), :] = (hidden * inverse_rms(hidden) * gains_ref[:, d:2 * d]).astype(BF)
        norms.send(s)

    at_step(1, copies[0].wait)
    in_turn(i, 0, steps, per, ((1, attended.add_chip), (3, lambda s: attended.take(s, hidden_rows)), (5, norms.pass_on)))
    swiglu, feed = steps + 3, 2 * steps + 3
    if line:
        at_step(1, lambda: first.hop(1))
        at_step(3, lambda: first.hop(2))
        at_step(5, lambda: first.hop(3), second.start)
        at_step(7, lambda: second.hop(1))
        at_step(8, lambda: second.hop(2))
        at_step(9, lambda: second.hop(3), first.finish)
        at_step(feed, second.finish)
    else:
        at_step(swiglu, copies[2].wait, copies[3].wait)


    def opened(blocks):
        xn = jnp.concatenate([xn_ref[rows_of(s), :] for s in blocks], axis=0)
        gu = dot(xn, we_ref[...])
        gate, up = gu[:, :units], gu[:, units:]
        sig = 1.0 / (1.0 + jnp.exp(-gate))
        return gate, up, sig

    def keep(ref, blocks, values):
        for u, s in enumerate(blocks):
            ref[rows_of(s), :] = values[u * SUB:(u + 1) * SUB]

    def tiles(grad_ref, left_ref, right_ref, start, count):
        def one(t, carry):
            cut = pl.ds(pl.multiple_of(t * tile, tile), tile)
            grad_ref[:, cut] = dot(left_ref[...], right_ref[:, cut], 0, 0).astype(grad_ref.dtype)
            return carry

        lax.fori_loop(start, start + count, one, 0)

    @pl.when(jnp.logical_and(i >= swiglu, i < feed))
    def _():
        blocks = pair_of(i - swiglu, per)
        for s in blocks:
            norms.ready(s)
        gate, up, sig = opened(blocks)
        keep(a_ref, blocks, (gate * sig * up).astype(BF))

    at_step(feed - 1, copies[1].wait, lambda: tiles(gsh_ref, a_ref, dy_ref, 0, gsh_ref.shape[1] // tile))
    if line:
        at_step(feed, shrink.start)

    @pl.when(jnp.logical_and(i >= feed, i < feed + steps))
    def _():
        blocks = pair_of(i - feed, per)
        gate, up, sig = opened(blocks)
        dy, a = (jnp.concatenate([ref[rows_of(s), :] for s in blocks], axis=0) for ref in (dy_ref, a_ref))
        da = dot(dy, ws_ref[...], 1, 1)
        dgu = jnp.concatenate([da * up * (sig * (1.0 + gate * (1.0 - sig))), da * (gate * sig)], axis=1).astype(BF)
        keep(dgu_ref, blocks, dgu)
        put_pair(pulled_back, blocks, dot(dgu, we_ref[...], 1, 1).astype(BF))
        put_pair(branch, blocks, dot(a, ws_ref[...]).astype(BF))

    def grad_rows(s, at, summed):
        pulled, gain_grad = rms_pull(h_ref[at, :], gains_ref[:, d:2 * d], summed)
        dh = dy_ref[rows_of(s), :].astype(FP) + pulled
        dh_ref[at, :] = dh
        dg_ref[...] += fold_rows(gain_grad)
        stage[s % per] = dh.astype(BF)
        grads.send(s)

    def chip_rows(mine, k, summed):
        at = rows_of(k)

        @pl.when(mine)
        def _():
            base_ref[at, :] = h_ref[at, :] + summed

        @pl.when(jnp.logical_not(mine))
        def _():
            other_ref[k] = summed.astype(BF)

    in_turn(i, feed, steps, per, ((1, pulled_back.add_chip), (1, lambda s: branch.add(s, chip_rows)),
                                  (3, lambda s: pulled_back.take(s, grad_rows)), (5, grads.pass_on)))
    if line:
        for k in range(1, line):
            at_step(feed + k, lambda k=k: shrink.step(k))
    half = gex_ref.shape[1] // tile // 2
    at_step(feed + steps, lambda: tiles(gex_ref, xn_ref, dgu_ref, 0, half))
    at_step(feed + steps + 1, lambda: tiles(gex_ref, xn_ref, dgu_ref, half, half))

    @pl.when(i == feed + steps + 4)
    def _():
        attended.drain()
        pulled_back.drain()
        norms.drain()
        grads.drain()
        for t in range(4):
            branch.sent(t * per + per - 1)
        lax.fori_loop(0, 4 * per, lambda s, c: (grads.ready(s), c)[1], 0)
        if line:
            shrink.finish(write_to(gsh_out))
            shrink.drain()
            first.drain()
            second.drain()


def middle(q, k, vt, tags, bars, wm, x, dy, gains, weights, kv, group, unit, line):
    length = q.shape[0]
    n = LANES
    d = wm.shape[1]
    share = (length // 4, d)
    per = share[0] // SUB
    steps = 2 * per
    we, ws = (w.shape for w in weights)
    shards = 2 * line
    shrink = jax.ShapeDtypeStruct(ws, BF)
    more = []
    if line:
        shrink = jax.ShapeDtypeStruct(ws, FP)
        we, ws = (we[0] * shards, we[1]), (ws[0], ws[1] * shards)
        more = [pltpu.VMEM(ws, BF), *reduce_scratch(line, shrink.shape), *GATHER_SEMS(shards), *GATHER_SEMS(shards)]
    units = ws[0]
    results = [jax.ShapeDtypeStruct(q.shape, BF), jax.ShapeDtypeStruct((length // SUB, 8, SUB * group), FP),
               jax.ShapeDtypeStruct(share, FP), jax.ShapeDtypeStruct((per, SUB, d), BF), jax.ShapeDtypeStruct(we, BF),
               jax.ShapeDtypeStruct(share, FP), jax.ShapeDtypeStruct((length, d), BF), jax.ShapeDtypeStruct((8, d), FP),
               shrink]
    out_specs = [whole(r.shape) for r in results]
    out_specs[6] = ANYWHERE
    held = [q, k, vt, tags, bars, wm, gains]
    return pl.pallas_call(
        partial(middle_kernel, kv, group, unit, line, per, steps),
        grid=(3 * steps + 8,),
        in_specs=[whole(a.shape) for a in held] + [ANYWHERE] * 4,
        out_specs=out_specs,
        out_shape=results,
        scratch_shapes=[pltpu.VMEM((kv, n, SUB * group), FP), pltpu.VMEM((kv, 8, SUB * group), FP),
                        pltpu.VMEM(share, BF), pltpu.VMEM((length, d), BF), pltpu.VMEM(we, BF), pltpu.VMEM(ws, BF),
                        pltpu.SemaphoreType.DMA((4,)),
                        pltpu.VMEM(share, FP), pltpu.VMEM((length, d), BF), pltpu.VMEM((length, units), BF),
                        pltpu.VMEM((length, 2 * units), BF),
                        *pairs_scratch(per, d, True), pltpu.SemaphoreType.DMA((4, 4 * per)),
                        *pairs_scratch(per, d, True), pltpu.VMEM((per, SUB, d), BF),
                        pltpu.SemaphoreType.DMA((4, 4 * per)),
                        *pairs_scratch(per, d, False), *more],
        compiler_params=params(collective_id=1, has_side_effects=True),
        name="middle",
    )(*held, x, dy, *weights)


def back_kernel(kv, group, unit, scale, blocks, per, line, *refs):
    refs = list(refs)
    take = lambda count: [refs.pop(0) for _ in range(count)]
    q_ref, k_ref, v_ref, kt_ref, tags_ref, bars_ref, lse_ref, ctx_block, dh_block, wm_ref = take(10)
    raw_ref, cos_ref, sin_ref, all_gains, base_ref, dg2_ref, other_ref = take(7)
    x_all, dh_all = take(2)
    late_from = take(4)
    grads = take(1) if line else []
    in_ref, out_ref, gains_out = take(3)
    sums = take(3) if line else []
    weight_grads = [] if line else take(2)
    late_to = take(4)
    wp_ref, ctx_ref, dh_ref, xn_ref = late_to
    late_sem = take(1)[0]
    late = [pltpu.make_async_copy(a, b, late_sem.at[w]) for w, (a, b) in enumerate(zip(late_from, late_to))]
    dk_ref, dv_ref, dq_ref, dqkv_ref = take(4)
    b_far, b_sems, x_held, x_near, x_sems = take(5)
    mine_ref, far_ref, x_far, f_sems, x_ref, dh_own, own_sems, heads_ref, fold_ref = take(9)
    place = Place(line)
    i = pl.program_id(0)
    b = blocks - 1 - i
    n = LANES
    pairs = Pairs(place, per, x_held, x_near, x_sems, lambda s: s % x_held.shape[0])
    subs = ROWS // SUB
    share, d = x_ref.shape
    gq, gk = all_gains[:, 2 * d:2 * d + n], all_gains[:, 2 * d + n:]
    tile = 256
    tensors = lax.axis_size("tensor")
    mates = [(place.dp, (place.t + step) % tensors) for step in range(1, tensors)]
    peers = []
    own_rows = pl.ds(pl.multiple_of(place.t * share, share), share)
    own_copies = [pltpu.make_async_copy(x_all.at[own_rows, :], x_ref, own_sems.at[0]),
                  pltpu.make_async_copy(dh_all, dh_own, own_sems.at[1])]
    if line:
        shards = 2 * line
        gm_ref, gp_ref = take(2)
        expand = Reduce(place, grads[0], row_cut(grads[0].shape[0] // shards), *take(4))
        merge = Reduce(place, gm_ref, column_cut(gm_ref.shape[1] // shards), None, *take(3))
        project = Reduce(place, gp_ref, row_cut(gp_ref.shape[0] // shards), None, *take(3))
        shown, over, g_sems = take(3)
        peers = [((place.dp + step) % shards, place.t) for step in range(1, shards)]
    else:
        gp_ref, gm_ref = weight_grads

    def tiles(grad_ref, left_ref, right_ref):
        def one(t, carry):
            cut = pl.ds(pl.multiple_of(t * tile, tile), tile)
            grad_ref[:, cut] = dot(left_ref[...], right_ref[:, cut], 0, 0).astype(grad_ref.dtype)
            return carry

        lax.fori_loop(0, grad_ref.shape[1] // tile, one, 0)

    def project_rows(t):
        cut = pl.ds(pl.multiple_of(t * tile, tile), tile)
        gp_ref[cut, :] = dot(xn_ref[:, cut], dqkv_ref[...], 0, 0).astype(BF)

    def chip(k):
        return send(far_ref.at[k], x_far.at[k], f_sems.at[0, k], f_sems.at[1, k], place.chip)

    def branch(k):
        return send(other_ref.at[k], b_far.at[k], b_sems.at[0, k], b_sems.at[1, k], place.chip)

    @pl.when(i == 0)
    def _():
        barrier = pltpu.get_barrier_semaphore()
        for device in mates + peers:
            pl.semaphore_signal(barrier, inc=1, device_id=device, device_id_type=MESH)
        for copy in late:
            copy.start()
        pl.semaphore_wait(barrier, len(mates + peers))
        if line:
            expand.start()
        for k in range(per):
            branch(k).start()
        dk_ref[...] = jnp.zeros_like(dk_ref)
        dv_ref[...] = jnp.zeros_like(dv_ref)
        heads_ref[...] = jnp.zeros_like(heads_ref)

    @pl.when(i < blocks)
    def _():
        here = pl.ds(pl.multiple_of(b * ROWS, ROWS), ROWS)
        dctx = dot(dh_block[...], wm_ref[...], 1, 1).astype(BF)
        ctx, q = ctx_block[...], q_ref[...]
        bars = jnp.concatenate([bars_ref[...]] * group, axis=0)
        wide, queries, outward, centres, lses = [], [], [], [], []
        for h in range(kv):
            queries.append(stacked(q, h, group))
            wide.append(jnp.concatenate([queries[h], bars], axis=1))
            outward.append(stacked(dctx, h, group))
            both = outward[h].astype(FP) * stacked(ctx, h, group).astype(FP)
            centres.append(jnp.sum(both.T, axis=0, keepdims=True))
            lses.append(jnp.concatenate([lse_ref[u, h:h + 1, g * SUB:(g + 1) * SUB]
                                         for g in range(group) for u in range(ROWS // SUB)], axis=1))
        dq_ref[...] = jnp.zeros_like(dq_ref)

        def chunk(j, diagonal):
            at = pl.ds(pl.multiple_of(j * ROWS, ROWS), ROWS)
            tags = tags_ref[at, :]
            for h in range(kv):
                cut = slice(h * n, (h + 1) * n)
                keys = jnp.concatenate([k_ref[at, cut], tags], axis=1)
                p = jnp.exp2(dot(keys, wide[h], 1, 1) * unit - lses[h])
                if diagonal:
                    p = jnp.where(causal_tile(group), p, 0.0)
                dp = dot(v_ref[at, cut], outward[h], 1, 1)
                ds = (p * (dp - centres[h])).astype(BF)
                dv_ref[at, cut] += dot(p.astype(BF), outward[h])
                dk_ref[at, cut] += dot(ds, queries[h])
                dq_ref[h] += dot(kt_ref[cut, at], ds)

        lax.fori_loop(0, b, lambda j, c: (chunk(j, False), c)[1], 0)
        chunk(b, True)

        cosines, sines = cos_ref[...], sin_ref[...]
        pieces = []
        for h in range(kv):
            dq = dq_ref[h].T
            for c in range(group + 1):
                if c < group:
                    grad, gain, row = dq[c * ROWS:(c + 1) * ROWS] * scale, gq, 0
                else:
                    grad, gain, row = dk_ref[here, h * n:(h + 1) * n] * scale, gk, 1
                grad = grad * cosines - pltpu.roll(grad, n // 2, 1) * sines
                at = (h * (group + 1) + c) * n
                piece, gain_grad = rms_pull(raw_ref[:, at:at + n], gain, grad)
                heads_ref[row] += fold_rows(gain_grad)
                pieces.append(piece)
            pieces.append(dv_ref[here, h * n:(h + 1) * n])
        dqkv = jnp.concatenate(pieces, axis=1).astype(BF)
        dqkv_ref[here, :] = dqkv
        pl.when(i == 0)(late[0].wait)
        part = dot(dqkv, wp_ref[...], 1, 1).astype(BF)
        for u in range(subs):
            s = subs * b + u
            pairs.put(s, part[u * SUB:(u + 1) * SUB], (i >= 2, s + 2 * subs))

    def chip_rows(mine, k, summed):
        @pl.when(mine)
        def _():
            mine_ref[pl.ds(pl.multiple_of(k * SUB, SUB), SUB), :] = summed

        @pl.when(jnp.logical_not(mine))
        def _():
            far_ref[k] = summed.astype(BF)
            chip(k).start()

    @pl.when(i >= 1)
    def _():
        for u in range(subs):
            pairs.add(subs * (b + 1) + u, chip_rows)

    @pl.when(i == 3)
    def _():
        for k in range(per):
            branch(k).wait()
            at = slice(k * SUB, (k + 1) * SUB)
            out_ref[at, :] = (base_ref[at, :] + b_far[k].astype(FP)).astype(BF)
        for copy in own_copies:
            copy.start()

    @pl.when(i == 1)
    def _():
        late[1].wait()
        late[2].wait()
        tiles(gm_ref, ctx_ref, dh_ref)

    if line:
        for step, act in enumerate((lambda: expand.step(1), lambda: expand.step(2), lambda: expand.step(3), merge.start,
                                    lambda: merge.step(1), lambda: merge.step(2))):
            pl.when(i == step)(act)

    def input_rows(k):
        at = slice(k * SUB, (k + 1) * SUB)
        chip(k).wait()
        summed = mine_ref[at, :] + x_far[k].astype(FP)
        pulled, gain_grad = rms_pull(x_ref[at, :].astype(FP), all_gains[:, :d], summed)
        in_ref[at, :] = (dh_own[at, :] + pulled).astype(BF)
        fold_ref[...] += fold_rows(gain_grad)

    def folded(ref):
        pieces = [fold_ref[...], dg2_ref[...], heads_ref[0], heads_ref[1]]
        row = jnp.sum(jnp.concatenate(pieces, axis=1), axis=0, keepdims=True)
        count = row.shape[1] // n
        for j in range(count):
            ref[j:j + 1, :] = row[:, j * n:(j + 1) * n]
        ref[count:, :] = jnp.zeros((ref.shape[0] - count, n), FP)

    def show(buffer, me, devices, first):
        copies = [send(buffer.at[me], buffer.at[me], g_sems.at[0, first + step], g_sems.at[1, first + step], device)
                  for step, device in enumerate(devices, 1)]
        for copy in copies:
            copy.start()
        return copies

    def added(buffer, me, devices, first):
        count = len(devices) + 1
        for step in range(1, count):
            who = (me - step + count) % count
            send(buffer.at[who], buffer.at[who], g_sems.at[0, first + step], g_sems.at[1, first + step],
                 place.sibling).wait_recv()
        total = buffer[0]
        for who in range(1, count):
            total = total + buffer[who]
        return total

    @pl.when(i == blocks)
    def _():
        fold_ref[...] = jnp.zeros_like(fold_ref)
        late[3].wait()
        for copy in own_copies:
            copy.wait()
        if not line:
            tiles(gp_ref, xn_ref, dqkv_ref)
            for k in range(per):
                input_rows(k)
            folded(gains_out)
        else:
            project_rows(project.turn(0))
            project.start()
            for q in range(1, line):
                project_rows(project.turn(q))
            merge.step(3)
            expand.finish(write_to(sums[0]))
            project.step(1)
            merge.finish(write_to(sums[1]))
            project.step(2)
            for k in range(per):
                input_rows(k)
            folded(shown.at[place.t])
            copies = show(shown, place.t, mates, 0)
            project.step(3)
            over[place.dp] = added(shown, place.t, mates, 0)
            copies += show(over, place.dp, peers, tensors)
            project.finish(write_to(sums[2]))
            gains_out[...] = added(over, place.dp, peers, tensors)
            for copy in copies:
                copy.wait_send()
            for r in (expand, merge, project):
                r.drain()
        for s in range(2 * subs):
            pairs.sent(s)


def back(q, k, v, kt, tags, bars, lse, ctx, dh, wm, wp, raw, cosines, sines, gains, xn, base, dg2, other, x, dh_own,
         grads, kv, group, unit, scale, line):
    length = q.shape[0]
    n = LANES
    d = wm.shape[1]
    blocks = length // ROWS
    per = other.shape[0]
    share = base.shape
    block_of = lambda i: jnp.maximum(blocks - 1 - i, 0)
    rows = lambda w: pl.BlockSpec((ROWS, w), lambda i: (block_of(i), 0))
    late = [wp, ctx, dh, xn]
    gain_rows = (-(-(gains.shape[1] // n) // 8) * 8, n)
    scratch = [*[pltpu.VMEM(a.shape, BF) for a in late], pltpu.SemaphoreType.DMA((4,)),
               pltpu.VMEM((length, kv * n), FP), pltpu.VMEM((length, kv * n), FP),
               pltpu.VMEM((kv, n, ROWS * group), FP), pltpu.VMEM((length, wp.shape[1]), BF),
               pltpu.VMEM((per, SUB, d), BF), pltpu.SemaphoreType.DMA((2, per)),
               pltpu.VMEM((2 * ROWS // SUB, SUB, d), BF), pltpu.VMEM((2 * per, SUB, d), BF),
               pltpu.SemaphoreType.DMA((2, 4 * per)),
               pltpu.VMEM(share, FP), pltpu.VMEM((per, SUB, d), BF), pltpu.VMEM((per, SUB, d), BF),
               pltpu.SemaphoreType.DMA((2, per)), pltpu.VMEM(share, BF), pltpu.VMEM(share, FP),
               pltpu.SemaphoreType.DMA((2,)), pltpu.VMEM((2, 8, n), FP), pltpu.VMEM((8, d), FP)]
    results = [jax.ShapeDtypeStruct(share, BF), jax.ShapeDtypeStruct(share, BF), jax.ShapeDtypeStruct(gain_rows, FP)]
    if line:
        shards = 2 * line
        own = [(grads[0].shape[0] // shards, grads[0].shape[1]), (wm.shape[0], wm.shape[1] // shards),
               (wp.shape[0] // shards, wp.shape[1])]
        views = ((own[0][0], 2, own[0][1] // 2), own[1], (own[2][0], own[2][1] // n, n))
        results += [jax.ShapeDtypeStruct(s, FP) for s in views]
        scratch += [pltpu.VMEM(wm.shape, BF), pltpu.VMEM(wp.shape, BF)]
        for w, s in enumerate(own):
            scratch += reduce_scratch(line, s, w == 0)
        scratch += [pltpu.VMEM((4, *gain_rows), FP), pltpu.VMEM((shards, *gain_rows), FP),
                    pltpu.SemaphoreType.DMA((2, 4 + shards))]
    else:
        results += [jax.ShapeDtypeStruct(wp.shape, BF), jax.ShapeDtypeStruct(wm.shape, BF)]
    args = [q, k, v, kt, tags, bars, lse, ctx, dh, wm, raw, cosines, sines, gains, base, dg2]
    more = [other, x, dh_own, *late, *grads]
    specs = [whole(a.shape) for a in args] + [ANYWHERE] * len(more)
    for at in (0, 5, 7, 8, 10, 11, 12):
        specs[at] = rows(args[at].shape[1])
    specs[6] = pl.BlockSpec((ROWS // SUB, 8, SUB * group), lambda i: (block_of(i), 0, 0))
    return pl.pallas_call(
        partial(back_kernel, kv, group, unit, scale, blocks, per, line),
        grid=(blocks + 1,),
        in_specs=specs,
        out_specs=[whole(r.shape) for r in results],
        out_shape=results,
        scratch_shapes=scratch,
        compiler_params=params(collective_id=3, has_side_effects=True),
        name="back",
    )(*args, *more)


def adamw_step(weight, moment_one, moment_two, gradient, step_rate, decay):
    mean_next = BETA_ONE * moment_one + (1.0 - BETA_ONE) * gradient
    square_next = BETA_TWO * moment_two + (1.0 - BETA_TWO) * gradient * gradient
    mean_hat = mean_next / (1.0 - BETA_ONE**STEP)
    square_hat = square_next / (1.0 - BETA_TWO**STEP)
    weight_next = weight - step_rate * (mean_hat / (jnp.sqrt(square_hat) + EPS_ADAM) + decay * weight)
    return weight_next, mean_next, square_next


def shards(
    tokens, cotangent, parents, token_segment, tree_id,
    projection_weight, projection_first_moment, projection_second_moment,
    merge_master, merge_mean, merge_square,
    expand_master, expand_mean, expand_square,
    shrink_master, shrink_mean, shrink_square,
    gain_master, gain_mean, gain_square,
):
    x = tokens[0]
    dy = cotangent[0]
    length, d = x.shape
    d_own, kv, per, n = projection_weight.shape
    group = per - 2
    units = expand_master.shape[2]
    scale = n ** (-0.5)
    unit = scale * math.log2(math.e)
    line = 4 if lax.axis_size("dp") == 8 and d_own % LANES == 0 else 0
    if line:
        masters = (projection_weight.reshape(d_own, kv * per, n), merge_master, expand_master, shrink_master)
    else:
        wp, we = (lax.all_gather(w.astype(BF).reshape(d_own, -1), "dp", axis=0, tiled=True)
                  for w in (projection_weight, expand_master))
        wm, ws = (lax.all_gather(w.astype(BF), "dp", axis=1, tiled=True) for w in (merge_master, shrink_master))
        masters = (wp,)

    gains = gain_master[None]
    fronts = front(x, gains, token_segment, parents, tree_id, masters, kv, group, line)
    xn1, q, k, v, kt, vt, raw, tags, bars, cosines, sines = fronts[:11]
    if line:
        wp, wm, *low = fronts[11:]
    else:
        low = (we, ws)
    ctx, lse, base, other, expand_grad, dh, dhb, dg2, shrink_sum = middle(
        q, k, vt, tags, bars, wm, x, dy, gains, low, kv, group, unit, line)
    backs = back(q, k, v, kt, tags, bars, lse, ctx, dhb, wm, wp, raw, cosines, sines, gains, xn1,
                 base, dg2, other, x, dh, (expand_grad,) if line else (), kv, group, unit, scale, line)
    input_grad, output, gain_rows = backs[:3]
    if line:
        expand_sum, merge_sum, project_sum = backs[3:]
    else:
        gain_rows = lax.psum(gain_rows, ("dp", "tensor"))
        project_sum, expand_sum = (
            lax.psum_scatter(g, "dp", scatter_dimension=0, tiled=True) for g in (backs[3], expand_grad))
        merge_sum, shrink_sum = (
            lax.psum_scatter(g, "dp", scatter_dimension=1, tiled=True) for g in (backs[4], shrink_sum))
    output, input_grad = output[None], input_grad[None]
    gain_grad = gain_rows.reshape(-1)[:gain_master.shape[0]]

    outs = [output, input_grad]
    for weight, mean, square, grad, rate in (
        (projection_weight, projection_first_moment, projection_second_moment, project_sum, RATE_PROJECT),
        (merge_master, merge_mean, merge_square, merge_sum, RATE_MERGE),
        (expand_master, expand_mean, expand_square, expand_sum, RATE_EXPAND),
        (shrink_master, shrink_mean, shrink_square, shrink_sum, RATE_SHRINK),
    ):
        grad = grad.astype(FP).reshape(weight.shape)
        after, mean_next, square_next = adamw_step(weight, mean, square, grad, rate, DECAY)
        outs += [after, mean_next, square_next, after.astype(BF)]
    gain_next, gain_mean_next, gain_square_next = adamw_step(
        gain_master, gain_mean, gain_square, gain_grad, RATE_GAIN, 0.0)
    return (*outs, gain_mean_next, gain_square_next, gain_next)


def solution(mesh):
    tokens = P("dp", None, None)
    project = P("dp", "tensor", None, None)
    columns = P("tensor", "dp")
    expand = P("dp", None, "tensor")
    shared = P("dp", "tensor", None)
    return jax.shard_map(
        shards,
        mesh=mesh,
        in_specs=(tokens, tokens, P(), P("dp", None), P("dp"), *[project] * 3, *[columns] * 3, *[expand] * 3,
                  *[columns] * 3, P(), P(), P()),
        out_specs=(shared, shared, *[project] * 4, *[columns] * 4, *[expand] * 4, *[columns] * 4, P(), P(), P()),
        check_vma=False,
    )
```

```python
import math
from functools import partial

import jax
import jax.numpy as jnp
import numpy as np
from jax import lax
from jax.experimental import pallas as pl
from jax.experimental.pallas import tpu as pltpu
from jax.sharding import PartitionSpec as P

STEP = 5
EPS_NORM = 1e-06
THETA = 1000000.0
BETA_ONE = 0.5
BETA_TWO = 0.5
EPS_ADAM = 1e-08
DECAY = 0.1
RATE_PROJECT = 0.05
RATE_MERGE = 0.3
RATE_EXPAND = 0.05
RATE_SHRINK = 0.03
RATE_GAIN = 0.3

BF = jnp.bfloat16
FP = jnp.float32
ROWS = 256
LANES = 128
SUB = 128
MESH = pl.DeviceIdType.MESH
BLOCKED = -1e30
VMEM_LIMIT = 56 * 2**20


def params(**more):
    return pltpu.CompilerParams(vmem_limit_bytes=VMEM_LIMIT, **more)


def dot(a, b, ca=1, cb=0):
    return lax.dot_general(a, b, (((ca,), (cb,)), ((), ())), preferred_element_type=FP)


def inverse_rms(values):
    return lax.rsqrt(jnp.mean(values * values, axis=-1, keepdims=True) + EPS_NORM)


def rms_pull(values, scales, grad):
    r = inverse_rms(values)
    scaled = grad * scales
    mean = jnp.mean(values * scaled, axis=-1, keepdims=True)
    return r * scaled - values * (r * r * r * mean), grad * values * r


def fold_rows(values):
    n, w = values.shape
    return jnp.sum(values.reshape(n // 8, 8, w), axis=0)


class Place:
    def __init__(self, line):
        self.line = line
        self.dp, self.t = lax.axis_index("dp"), lax.axis_index("tensor")
        self.z, self.y = self.dp // 2, self.dp % 2
        self.x, self.c = self.t // 2, self.t % 2
        self.has_up, self.has_down = self.z < line - 1, self.z > 0
        self.up, self.down = (self.dp + 2, self.t), (self.dp - 2, self.t)
        self.across = (self.dp + 1 - 2 * self.y, self.t)
        self.sibling = (self.dp, self.t + 1 - 2 * self.c)
        self.chip = (self.dp, (1 - self.x) * 2 + self.c)

    def greet(self, tensor, line, meanwhile=None):
        barrier = pltpu.get_barrier_semaphore()

        def signal(device):
            pl.semaphore_signal(barrier, inc=1, device_id=device, device_id_type=MESH)

        if tensor:
            signal(self.sibling)
            signal(self.chip)
        if line:
            signal(self.across)
            pl.when(self.has_up)(lambda: signal(self.up))
            pl.when(self.has_down)(lambda: signal(self.down))
        peers = (2 if tensor else 0) + (1 if line else 0)
        if line:
            peers = peers + jnp.where(self.has_up, 1, 0) + jnp.where(self.has_down, 1, 0)
        if meanwhile is not None:
            meanwhile()
        pl.semaphore_wait(barrier, peers)


def send(src, dst, sent, arrived, device):
    return pltpu.make_async_remote_copy(
        src_ref=src, dst_ref=dst, send_sem=sent, recv_sem=arrived, device_id=device, device_id_type=MESH)


def row_cut(size):
    return lambda j: (pl.ds(pl.multiple_of(j * size, size), size), slice(None))


def column_cut(size):
    return lambda j: (slice(None), pl.ds(pl.multiple_of(j * size, size), size))


class Gather:
    def __init__(self, place, own, full, cut, sems, local):
        self.place, self.own, self.full, self.cut, self.sems, self.local = place, own, full, cut, sems, local

    def copy(self, kind, src, j):
        p = self.place
        device = (p.up, p.down, p.across)[kind]
        return send(src, self.full.at[self.cut(j)], self.sems.at[kind, j], self.sems.at[3, j], device)

    def kept(self):
        return pltpu.make_async_copy(self.own, self.full.at[self.cut(self.place.dp)], self.local)

    def source(self):
        return self.full.at[self.cut(self.place.dp)] if self.own is None else self.own

    def start(self):
        p = self.place
        self.copy(2, self.source(), p.dp).start()
        pl.when(p.has_up)(lambda: self.copy(0, self.source(), p.dp).start())
        pl.when(p.has_down)(lambda: self.copy(1, self.source(), p.dp).start())
        if self.own is not None:
            self.kept().start()

    def arrivals(self, k):
        p = self.place
        return ((0, p.z >= k, (p.z - k) * 2 + p.y, p.has_up), (1, p.z + k < p.line, (p.z + k) * 2 + p.y, p.has_down))

    def hop(self, k):
        for kind, here, j, further in self.arrivals(k):
            @pl.when(here)
            def _(kind=kind, j=j, further=further):
                piece = self.full.at[self.cut(j)]
                self.copy(kind, piece, j).wait_recv()
                pl.when(further)(lambda: self.copy(kind, piece, j).start())
                self.copy(2, piece, j).start()

    def finish(self):
        p = self.place
        if self.own is not None:
            self.kept().wait()
        for zz in range(p.line):
            j = zz * 2 + 1 - p.y
            self.copy(2, self.full.at[self.cut(j)], j).wait_recv()

    def drain(self):
        p = self.place
        self.copy(2, self.source(), p.dp).wait_send()
        pl.when(p.has_up)(lambda: self.copy(0, self.source(), p.dp).wait_send())
        pl.when(p.has_down)(lambda: self.copy(1, self.source(), p.dp).wait_send())
        for k in range(1, p.line):
            for kind, here, j, further in self.arrivals(k):
                @pl.when(here)
                def _(kind=kind, j=j, further=further):
                    piece = self.full.at[self.cut(j)]
                    pl.when(further)(lambda: self.copy(kind, piece, j).wait_send())
                    self.copy(2, piece, j).wait_send()


class Reduce:
    def __init__(self, place, grad, cut, kept, across, lined, sems):
        self.place, self.grad, self.cut, self.kept, self.sems = place, grad, cut, kept, sems
        self.across, self.lined = across, lined

    def cross(self, zz):
        p = self.place
        return send(self.grad.at[self.cut(zz * 2 + 1 - p.y)], self.across.at[zz],
                    self.sems.at[0, zz], self.sems.at[1, zz], p.across)

    def climb(self, t):
        return send(self.across.at[t], self.lined.at[t + 1], self.sems.at[2, t], self.sems.at[3, t], self.place.up)

    def sink(self, t):
        return send(self.across.at[t], self.lined.at[t], self.sems.at[4, t], self.sems.at[5, t], self.place.down)

    def load(self, zz):
        return pltpu.make_async_copy(self.grad.at[self.cut(zz * 2 + self.place.y)], self.kept.at[zz], self.sems.at[6, zz])

    def mine(self, zz):
        if self.kept is None:
            return self.grad[self.cut(zz * 2 + self.place.y)].astype(FP)
        return self.kept[zz].astype(FP)

    def loaded(self, zz):
        if self.kept is not None:
            self.load(zz).wait()

    def turn(self, q):
        z = self.place.z
        low = z < 2
        if q == 0:
            return jnp.where(low, 3, 0)
        if q == 1:
            return jnp.where(low, 2, 1)
        if q == 2:
            return jnp.where(low, 1 - z, 5 - z)
        return z

    def start(self):
        self.cross(self.turn(0)).start()
        if self.kept is not None:
            for zz in range(self.place.line):
                self.load(zz).start()

    def advance(self, q):
        self.cross(self.turn(q - 1)).wait_send()
        self.cross(self.turn(q)).start()

    def hop(self, h):
        p = self.place

        def pass_on(t, coming, more, slot):
            self.loaded(t)
            self.cross(t).wait_recv()

            @pl.when(jnp.logical_not(more))
            def _():
                self.across[t] = (self.mine(t) + self.across[t].astype(FP)).astype(BF)

            @pl.when(more)
            def _():
                coming(t).wait_recv()
                self.across[t] = (self.mine(t) + self.across[t].astype(FP) + self.lined[slot].astype(FP)).astype(BF)

            coming(t).start()

        pl.when(p.z < h)(lambda: pass_on(p.z + p.line - h, self.climb, p.has_down, p.z + p.line - h + 1))
        pl.when(p.z >= p.line - h)(lambda: pass_on(p.z - p.line + h, self.sink, p.has_up, p.z - p.line + h))

    def finish(self, write):
        p = self.place
        self.loaded(p.z)
        self.cross(p.z).wait_recv()
        pl.when(p.has_down)(lambda: self.climb(p.z).wait_recv())
        pl.when(p.has_up)(lambda: self.sink(p.z).wait_recv())
        from_below = jnp.where(p.has_down, self.lined[p.z + 1].astype(FP), 0.0)
        from_above = jnp.where(p.has_up, self.lined[p.z].astype(FP), 0.0)
        write(self.mine(p.z) + self.across[p.z].astype(FP) + from_below + from_above)

    def step(self, k):
        self.advance(k)
        self.hop(k)

    def drain(self):
        p = self.place
        self.cross(p.z).wait_send()
        for zz in range(p.line):
            pl.when(zz > p.z)(lambda zz=zz: self.climb(zz).wait_send())
            pl.when(zz < p.z)(lambda zz=zz: self.sink(zz).wait_send())


def write_to(ref):
    def write(values):
        if len(ref.shape) == 2:
            ref[...] = values
            return
        width = ref.shape[2]
        for j in range(ref.shape[1]):
            ref[:, j, :] = values[:, j * width:(j + 1) * width]

    return write


def reduce_scratch(line, shape, kept=False):
    return [pltpu.VMEM((line, *shape), BF)] * kept + [pltpu.VMEM((line, *shape), BF), pltpu.VMEM((line + 1, *shape), BF),
                                                      pltpu.SemaphoreType.DMA((7, line))]


class Pairs:
    def __init__(self, place, per, held, near, sems, slot_of):
        self.place, self.per, self.held, self.near, self.sems, self.slot_of = place, per, held, near, sems, slot_of

    def near_slot(self, s):
        return (s // (2 * self.per)) * self.per + s % self.per

    def to_sibling(self, s):
        return send(self.held.at[self.slot_of(s)], self.near.at[self.near_slot(s)], self.sems.at[0, s],
                    self.sems.at[1, s], self.place.sibling)

    def sends(self, s):
        return self.place.c != (s // self.per) % 2

    def sent(self, s):
        pl.when(self.sends(s))(lambda: self.to_sibling(s).wait_send())

    def put(self, s, rows, before=None):
        if before is not None:
            pl.when(before[0])(lambda: self.sent(before[1]))
        self.held[self.slot_of(s)] = rows
        pl.when(self.sends(s))(lambda: self.to_sibling(s).start())

    def put_next(self, s, rows):
        self.put(s, rows, (s % self.per >= 1, s - 1))

    def add(self, s, use):
        t = s // self.per

        @pl.when(self.place.c == t % 2)
        def _():
            self.to_sibling(s).wait_recv()
            use(self.place.x == t // 2, s % self.per,
                self.held[self.slot_of(s)].astype(FP) + self.near[self.near_slot(s)].astype(FP))


class Exchange(Pairs):
    def __init__(self, place, per, held, near, far, total, sems):
        super().__init__(place, per, held, near, sems, lambda s: s // per)
        self.far, self.total = far, total

    def rows(self, k):
        return pl.ds(pl.multiple_of(k * SUB, SUB), SUB)

    def to_chip(self, s):
        return send(self.near.at[self.near_slot(s)], self.far.at[s % self.per], self.sems.at[2, s], self.sems.at[3, s],
                    self.place.chip)

    def add_chip(self, s):
        def use(mine, k, summed):
            @pl.when(jnp.logical_not(mine))
            def _():
                self.near[self.near_slot(s)] = summed.astype(BF)
                self.to_chip(s).start()

            @pl.when(mine)
            def _():
                self.total[self.rows(k), :] = summed

        self.add(s, use)

    def take(self, s, use):
        @pl.when(s // self.per == self.place.t)
        def _():
            k = s % self.per
            self.to_chip(s).wait_recv()
            use(s, self.rows(k), self.total[self.rows(k), :] + self.far[k].astype(FP))

    def drain(self):
        p = self.place

        def one(s, carry):
            t = s // self.per
            pl.when(s % self.per == self.per - 1)(lambda: self.sent(s))
            pl.when(jnp.logical_and(p.c == t % 2, p.x != t // 2))(lambda: self.to_chip(s).wait_send())
            return carry

        lax.fori_loop(0, 4 * self.per, one, 0)


def pair_of(step, per):
    t = step % 2
    return t * per + step // 2, (3 - t) * per + step // 2


def pairs_scratch(per, d, exchange):
    rows = [pltpu.VMEM((4, SUB, d), BF), pltpu.VMEM((2 * per, SUB, d), BF)]
    return rows + [pltpu.VMEM((per, SUB, d), BF)] * exchange + [pltpu.SemaphoreType.DMA((4 if exchange else 2, 4 * per))]


class Spread:
    def __init__(self, place, per, stage, full, sems):
        self.place, self.per, self.stage, self.full, self.sems = place, per, stage, full, sems

    def rows(self, s):
        return self.full.at[pl.ds(pl.multiple_of(s * SUB, SUB), SUB), :]

    def source(self, s):
        return self.rows(s) if self.stage is None else self.stage.at[s % self.per]

    def copy(self, kind, src, s):
        device = (self.place.chip, self.place.sibling)[kind]
        return send(src, self.rows(s), self.sems.at[kind, s], self.sems.at[2, s], device)

    def kept(self, s):
        return pltpu.make_async_copy(self.source(s), self.rows(s), self.sems.at[3, s])

    def send(self, s):
        for kind in (0, 1):
            self.copy(kind, self.source(s), s).start()
        if self.stage is not None:
            self.kept(s).start()

    def owns(self, s):
        return s // self.per == self.place.t

    def passes(self, s):
        t = s // self.per
        return jnp.logical_and(self.place.c == t % 2, self.place.x != t // 2)

    def pass_on(self, s):
        @pl.when(self.passes(s))
        def _():
            self.copy(1, self.rows(s), s).wait_recv()
            self.copy(1, self.rows(s), s).start()

    def ready(self, s):
        if self.stage is not None:
            pl.when(self.owns(s))(lambda: self.kept(s).wait())
        pl.when((s // self.per) % 2 != self.place.c)(lambda: self.copy(1, self.rows(s), s).wait_recv())

    def drain(self):
        def one(s, carry):
            @pl.when(self.owns(s))
            def _():
                self.copy(0, self.source(s), s).wait_send()
                self.copy(1, self.source(s), s).wait_send()

            pl.when(self.passes(s))(lambda: self.copy(1, self.rows(s), s).wait_send())
            return carry

        lax.fori_loop(0, 4 * self.per, one, 0)


def whole(shape):
    return pl.BlockSpec(tuple(shape), lambda i: (0,) * len(shape), pipeline_mode=pl.Buffered(1))


ANYWHERE = pl.BlockSpec(memory_space=pl.ANY)
GATHER_SEMS = lambda shards: [pltpu.SemaphoreType.DMA((4, shards)), pltpu.SemaphoreType.DMA]


def make_tables(seg_ref, parents_ref, tree_ref, freq_ref, tags_ref, bars_ref, cos_ref, sin_ref):
    count = parents_ref.shape[1]
    n = LANES
    blocks = sin_ref.shape[0] // ROWS
    lane = lax.broadcasted_iota(jnp.int32, (1, n), 1).astype(FP)
    place_of = lambda b: pl.ds(pl.multiple_of(b * ROWS, ROWS), ROWS)

    def columns(b, carry):
        sin_ref[place_of(b), :] = jnp.broadcast_to(seg_ref[:, place_of(b)].astype(FP), (n, ROWS)).T
        return carry

    def tally(b, carry):
        column = sin_ref[place_of(b), :]
        return (carry[0] + fold_rows(jnp.where(column == lane, 1.0, 0.0)),
                carry[1] + fold_rows(jnp.where(column < lane, 1.0, 0.0)))

    lax.fori_loop(0, blocks, columns, 0)
    sizes, starts = lax.fori_loop(0, blocks, tally, (jnp.zeros((8, n), FP), jnp.zeros((8, n), FP)))
    sizes, starts = (jnp.sum(a, axis=0, keepdims=True) for a in (sizes, starts))
    table = parents_ref[...]
    chosen = jnp.where(lax.broadcasted_iota(jnp.int32, table.shape, 0) == tree_ref[0], table, 0)
    chosen = jnp.sum(chosen.astype(FP), axis=0, keepdims=True)
    parents = jnp.zeros((1, n), FP)
    for b in range(count):
        parents = jnp.where(lane == b, chosen[:, b:b + 1], parents)
    shifts = jnp.where(lane != 0, sizes[:, :1], 0.0) - starts

    def rows(b, carry):
        at = place_of(b)
        column = sin_ref[at, :]
        hot = column == lane
        parent = jnp.sum(jnp.where(hot, parents, 0.0), axis=1, keepdims=True)
        above = jnp.where(jnp.logical_and(lane == parent, lane != 0), sizes, 0.0)
        first = (b * ROWS).astype(FP)
        position = (lax.broadcasted_iota(jnp.int32, (ROWS, 1), 0).astype(FP) + first
                    + jnp.sum(jnp.where(hot, shifts, 0.0) + above, axis=1, keepdims=True))
        tags_ref[at, :] = jnp.where(hot, 1.0, 0.0).astype(BF)
        open_to = jnp.logical_or(jnp.logical_or(hot, lane == parent), jnp.logical_or(lane == 0, lane >= count))
        bars_ref[at, :] = jnp.where(open_to, 0.0, BLOCKED).astype(BF)
        angles = position * freq_ref[...]
        cos_ref[at, :] = jnp.cos(angles)
        turned = jnp.sin(angles)
        sin_ref[at, :] = jnp.where(lane < n // 2, -turned, turned)
        return carry

    lax.fori_loop(0, blocks, rows, 0)


def front_kernel(kv, group, line, *refs):
    refs = list(refs)
    take = lambda count: [refs.pop(0) for _ in range(count)]
    x_ref, gains_ref, seg_ref, parents_ref, tree_ref, freq_ref = take(6)
    masters = take(4) if line else take(1)
    xn_ref, q_ref, k_ref, v_ref, kt_ref, vt_ref, raw_ref, tags_ref, bars_ref, cos_ref, sin_ref = take(11)
    if line:
        wp_out, wm_out, we_low, ws_low = take(4)
        wp_ref, wm_low, p_sems, p_local, m_sems, m_local, out_sem = take(7)
    else:
        wp_ref = masters[0]
    xn_full, xn_sem = take(2)
    i = pl.program_id(0)
    final = pl.num_programs(0) - 1
    d = x_ref.shape[1]
    n = LANES
    per = group + 2
    if line:
        place = Place(line)
        size = masters[0].shape[0]
        project = Gather(place, None, wp_ref, row_cut(size), p_sems, p_local)
        merge = Gather(place, wm_low, wm_out, column_cut(wm_low.shape[1]), m_sems, m_local)
        written = pltpu.make_async_copy(wp_ref, wp_out, out_sem)
    normed = pltpu.make_async_copy(xn_full, xn_ref, xn_sem)

    def round_projection():
        at = pl.ds(pl.multiple_of(place.dp * size, size), size)
        for j in range(kv * per):
            wp_ref[at, j * n:(j + 1) * n] = masters[0][:, j, :].astype(BF)

    def norm(b, carry):
        at = pl.ds(pl.multiple_of(b * ROWS, ROWS), ROWS)
        x = x_ref[at, :].astype(FP)
        xn_full[at, :] = (x * inverse_rms(x) * gains_ref[:, :d]).astype(BF)
        return carry

    @pl.when(i == 0)
    def _():
        if line:
            place.greet(False, True, round_projection)
            project.start()
        lax.fori_loop(0, x_ref.shape[0] // ROWS, norm, 0)
        normed.start()
        if line:
            project.hop(1)
        make_tables(seg_ref, parents_ref, tree_ref, freq_ref, tags_ref, bars_ref, cos_ref, sin_ref)
        if line:
            project.hop(2)
            wm_low[...] = masters[1][...].astype(BF)
            units = masters[2].shape[2]
            for half in range(2):
                we_low[:, half * units:(half + 1) * units] = masters[2][:, half, :].astype(BF)
            ws_low[...] = masters[3][...].astype(BF)
            project.hop(3)
            merge.start()
            project.finish()
            written.start()

    if line:
        for k in range(1, line):
            pl.when(i == k + 1)(lambda k=k: merge.hop(k))
    at = pl.ds(pl.multiple_of(i * ROWS, ROWS), ROWS)
    qkv = dot(xn_full[at, :], wp_ref[...])
    cosines, sines = cos_ref[at, :], sin_ref[at, :]
    gq, gk = gains_ref[:, 2 * d:2 * d + n], gains_ref[:, 2 * d + n:]
    keys, values = [], []
    for h in range(kv):
        for c in range(group + 1):
            raw = qkv[:, (h * per + c) * n:(h * per + c + 1) * n]
            to = (h * (group + 1) + c) * n
            raw_ref[:, to:to + n] = raw
            y = raw * inverse_rms(raw) * (gq if c < group else gk)
            turned = y * cosines + pltpu.roll(y, n // 2, 1) * sines
            if c < group:
                to = (h * group + c) * n
                q_ref[:, to:to + n] = turned.astype(BF)
            else:
                keys.append(turned)
        values.append(qkv[:, (h * per + group + 1) * n:(h * per + group + 2) * n])
    for h in range(kv):
        k_ref[:, h * n:(h + 1) * n] = keys[h].astype(BF)
        v_ref[:, h * n:(h + 1) * n] = values[h].astype(BF)
        kt_ref[h * n:(h + 1) * n, :] = keys[h].T.astype(BF)
        vt_ref[h * n:(h + 1) * n, :] = values[h].T.astype(BF)

    @pl.when(i == final)
    def _():
        normed.wait()
        if line:
            merge.finish()
            merge.drain()
            project.drain()
            written.wait()


def front(x, gains, segments, parents, tree, masters, kv, group, line):
    length, d = x.shape
    n = LANES
    rows = lambda w: pl.BlockSpec((ROWS, w), lambda i: (i, 0))
    cols = pl.BlockSpec((kv * n, ROWS), lambda i: (0, i))
    out = lambda w, t: jax.ShapeDtypeStruct((length, w), t)
    raw_w = kv * (group + 1) * n
    freq = np.float32(THETA ** (-(np.arange(n) % (n // 2)) * 2.0 / n))[None]
    more_specs, more_shapes, scratch = [], [], []
    if line:
        shards = 2 * line
        project, merge, expand, shrink = (m.shape for m in masters)
        wp_shape = (project[0] * shards, project[1] * n)
        more_shapes = [jax.ShapeDtypeStruct(wp_shape, BF), jax.ShapeDtypeStruct((merge[0], merge[1] * shards), BF),
                       jax.ShapeDtypeStruct((expand[0], 2 * expand[2]), BF), jax.ShapeDtypeStruct(shrink, BF)]
        more_specs = [ANYWHERE, ANYWHERE, whole(more_shapes[2].shape), whole(more_shapes[3].shape)]
        scratch = [pltpu.VMEM(wp_shape, BF), pltpu.VMEM(merge, BF), *GATHER_SEMS(shards), *GATHER_SEMS(shards),
                   pltpu.SemaphoreType.DMA]
    table = whole((length, n))
    return pl.pallas_call(
        partial(front_kernel, kv, group, line),
        grid=(length // ROWS,),
        in_specs=[whole(x.shape), whole(gains.shape), whole(segments.shape), whole(parents.shape),
                  pl.BlockSpec(memory_space=pltpu.SMEM), whole(freq.shape), *[whole(m.shape) for m in masters]],
        out_specs=[ANYWHERE, rows(kv * group * n), rows(kv * n), rows(kv * n), cols, cols, rows(raw_w),
                   table, table, table, table, *more_specs],
        out_shape=[out(d, BF), out(kv * group * n, BF), out(kv * n, BF), out(kv * n, BF),
                   jax.ShapeDtypeStruct((kv * n, length), BF), jax.ShapeDtypeStruct((kv * n, length), BF),
                   out(raw_w, FP), out(n, BF), out(n, BF), out(n, FP), out(n, FP), *more_shapes],
        scratch_shapes=[*scratch, pltpu.VMEM((length, d), BF), pltpu.SemaphoreType.DMA],
        compiler_params=params(**({"collective_id": 0, "has_side_effects": True} if line else {})),
        name="front",
    )(x, gains, segments, parents, tree, freq, *masters)


def stacked(ref_block, h, group):
    n = LANES
    return jnp.concatenate(
        [ref_block[:, (h * group + g) * n:(h * group + g + 1) * n] for g in range(group)], axis=0)


def causal_tile(group, rows=ROWS, after=0):
    key_at = lax.broadcasted_iota(jnp.int32, (ROWS, rows * group), 0)
    query_at = lax.broadcasted_iota(jnp.int32, (ROWS, rows * group), 1) % rows
    return key_at <= query_at + after


def in_turn(i, first, steps, per, acts):
    for behind, act in acts:
        @pl.when(jnp.logical_and(i - first - behind >= 0, i - first - behind < steps))
        def _(behind=behind, act=act):
            for s in pair_of(i - first - behind, per):
                act(s)


def middle_kernel(kv, group, unit, line, per, steps, *refs):
    refs = list(refs)
    take = lambda count: [refs.pop(0) for _ in range(count)]
    q_ref, k_ref, vt_ref, tags_ref, bars_ref, wm_ref, gains_ref, x_all, dy_all = take(9)
    weights = take(2)
    ctx_out, lse_ref, base_ref, other_ref, gate_out, up_out, dh_ref, dhb_ref, dg_ref, gsh_out = take(10)
    acc_ref, sum_ref, x_ref, dy_ref, we_ref, ws_ref, copy_sems = take(7)
    h_ref, xn_ref, a_ref, dgu_ref, ctx_ref, gup_ref = take(6)
    h_held, h_near, h_far, h_sems, xn_sems = take(5)
    d_held, d_near, d_far, d_sems, stage, dh_sems = take(6)
    b_held, b_near, b_sems = take(3)
    place = Place(line)
    i = pl.program_id(0)
    n = LANES
    share, d = x_ref.shape
    units = ws_ref.shape[0]
    tile = 256
    attended = Exchange(place, per, h_held, h_near, h_far, h_ref, h_sems)
    norms = Spread(place, per, None, xn_ref, xn_sems)
    pulled_back = Exchange(place, per, d_held, d_near, d_far, dh_ref, d_sems)
    grads = Spread(place, per, stage, dhb_ref, dh_sems)
    branch = Pairs(place, per, b_held, b_near, b_sems, lambda s: s // per)
    own_share = x_all.at[pl.ds(pl.multiple_of(place.t * share, share), share), :]
    copies = [pltpu.make_async_copy(own_share, x_ref, copy_sems.at[0]),
              pltpu.make_async_copy(dy_all, dy_ref, copy_sems.at[1])]
    if line:
        gsh_ref = take(1)[0]
        shrink = Reduce(place, gsh_ref, column_cut(gsh_ref.shape[1] // (2 * line)), None, *take(3))
        gate_ref = take(1)[0]
        expand = Reduce(place, gate_ref, row_cut(gate_ref.shape[0] // (2 * line)), None, *take(3))
        cuts = (row_cut(weights[0].shape[0]), column_cut(weights[1].shape[1]))
        first, second = [Gather(place, weights[w], (we_ref, ws_ref)[w], cuts[w], *take(2)) for w in range(2)]
    else:
        gsh_ref, gate_ref = gsh_out, gate_out
        copies += [pltpu.make_async_copy(weights[0], we_ref, copy_sems.at[2]),
                   pltpu.make_async_copy(weights[1], ws_ref, copy_sems.at[3])]
    written = [pltpu.make_async_copy(ctx_ref, ctx_out, copy_sems.at[4]),
               pltpu.make_async_copy(gup_ref, up_out, copy_sems.at[5])]
    rows_of = lambda s: pl.ds(pl.multiple_of(s * SUB, SUB), SUB)

    def at_step(step, *acts):
        @pl.when(i == step)
        def _():
            for act in acts:
                act()

    @pl.when(i == 0)
    def _():
        place.greet(True, bool(line))
        if line:
            first.start()
        for copy in copies:
            copy.start()
        dg_ref[...] = jnp.zeros_like(dg_ref)


    def block(s):
        here = rows_of(s)
        bars = jnp.concatenate([bars_ref[here, :]] * group, axis=0)
        q = q_ref[here, :]
        wide = [jnp.concatenate([stacked(q, h, group), bars], axis=1) for h in range(kv)]
        acc_ref[...] = jnp.zeros_like(acc_ref)
        sum_ref[...] = jnp.zeros_like(sum_ref)

        def chunk(j, diagonal):
            at = pl.ds(pl.multiple_of(j * ROWS, ROWS), ROWS)
            tags = tags_ref[at, :]
            for h in range(kv):
                keys = jnp.concatenate([k_ref[at, h * n:(h + 1) * n], tags], axis=1)
                scores = dot(keys, wide[h], 1, 1)
                e = jnp.exp2(scores * unit)
                if diagonal:
                    e = jnp.where(causal_tile(group, SUB, (s % 2) * SUB), e, 0.0)
                sum_ref[h] += fold_rows(e)
                acc_ref[h] += dot(vt_ref[h * n:(h + 1) * n, at], e.astype(BF))

        lax.fori_loop(0, s // 2, lambda j, c: (chunk(j, False), c)[1], 0)
        chunk(s // 2, True)
        parts = []
        for h in range(kv):
            sums = jnp.sum(sum_ref[h], axis=0, keepdims=True)
            lse_ref[s, h:h + 1, :] = jnp.log2(sums)
            ctx = (acc_ref[h] / sums).T
            parts += [ctx[g * SUB:(g + 1) * SUB] for g in range(group)]
        ctx_ref[here, :] = jnp.concatenate(parts, axis=1).astype(BF)

    def put_pair(pairs, blocks, part):
        for u, s in enumerate(blocks):
            pairs.put_next(s, part[u * SUB:(u + 1) * SUB])

    @pl.when(i < steps)
    def _():
        blocks = pair_of(i, per)
        for s in blocks:
            block(s)
        ctx = jnp.concatenate([ctx_ref[rows_of(s), :] for s in blocks], axis=0)
        put_pair(attended, blocks, dot(ctx, wm_ref[...]).astype(BF))

    def hidden_rows(s, at, summed):
        hidden = x_ref[at, :].astype(FP) + summed
        h_ref[at, :] = hidden
        xn_ref[rows_of(s), :] = (hidden * inverse_rms(hidden) * gains_ref[:, d:2 * d]).astype(BF)
        norms.send(s)

    at_step(1, copies[0].wait)
    at_step(steps, written[0].start)
    in_turn(i, 0, steps, per, ((1, attended.add_chip), (3, lambda s: attended.take(s, hidden_rows)), (5, norms.pass_on)))
    swiglu, feed = steps + 3, 2 * steps + 3
    if line:
        at_step(1, lambda: first.hop(1))
        at_step(3, lambda: first.hop(2))
        at_step(5, lambda: first.hop(3), second.start)
        at_step(7, lambda: second.hop(1))
        at_step(8, lambda: second.hop(2))
        at_step(9, lambda: second.hop(3), first.finish)
        at_step(feed, second.finish)
    else:
        at_step(swiglu, copies[2].wait, copies[3].wait)


    def gathered(ref, blocks):
        return jnp.concatenate([ref[rows_of(s), :] for s in blocks], axis=0)

    def keep(ref, blocks, values):
        for u, s in enumerate(blocks):
            ref[rows_of(s), :] = values[u * SUB:(u + 1) * SUB]

    def tiles(grad_ref, left_ref, right_ref, start, count, after):
        def one(t, carry):
            cut = pl.ds(pl.multiple_of(t * tile, tile), tile)
            there = pl.ds(pl.multiple_of((t + after) * tile, tile), tile)
            grad_ref[:, cut] = dot(left_ref[...], right_ref[:, there], 0, 0).astype(grad_ref.dtype)
            return carry

        lax.fori_loop(start, start + count, one, 0)

    @pl.when(jnp.logical_and(i >= swiglu, i < feed))
    def _():
        blocks = pair_of(i - swiglu, per)
        for s in blocks:
            norms.ready(s)
        gu = dot(gathered(xn_ref, blocks), we_ref[...])
        gate, up = gu[:, :units], gu[:, units:]
        keep(a_ref, blocks, (gate / (1.0 + jnp.exp(-gate)) * up).astype(BF))
        keep(dgu_ref, blocks, gu.astype(BF))

    at_step(feed - 1, copies[1].wait, lambda: tiles(gsh_ref, a_ref, dy_ref, 0, gsh_ref.shape[1] // tile, 0))
    if line:
        at_step(feed, shrink.start)

    @pl.when(jnp.logical_and(i >= feed, i < feed + steps))
    def _():
        blocks = pair_of(i - feed, per)
        gu = gathered(dgu_ref, blocks).astype(FP)
        gate, up = gu[:, :units], gu[:, units:]
        sig = 1.0 / (1.0 + jnp.exp(-gate))
        da = dot(gathered(dy_ref, blocks), ws_ref[...], 1, 1)
        dgu = jnp.concatenate([da * up * (sig * (1.0 + gate * (1.0 - sig))), da * (gate * sig)], axis=1).astype(BF)
        keep(dgu_ref, blocks, dgu)
        put_pair(pulled_back, blocks, dot(dgu, we_ref[...], 1, 1).astype(BF))

    def grad_rows(s, at, summed):
        pulled, gain_grad = rms_pull(h_ref[at, :], gains_ref[:, d:2 * d], summed)
        dh = dy_ref[rows_of(s), :].astype(FP) + pulled
        dh_ref[at, :] = dh
        dg_ref[...] += fold_rows(gain_grad)
        stage[s % per] = dh.astype(BF)
        grads.send(s)

    def chip_rows(mine, k, summed):
        at = rows_of(k)

        @pl.when(mine)
        def _():
            base_ref[at, :] = h_ref[at, :] + summed

        @pl.when(jnp.logical_not(mine))
        def _():
            other_ref[k] = summed.astype(BF)

    in_turn(i, feed, steps, per, ((1, pulled_back.add_chip), (3, lambda s: pulled_back.take(s, grad_rows)),
                                  (5, grads.pass_on)))

    @pl.when(jnp.logical_and(i >= feed + 3, i < feed + 3 + steps))
    def _():
        blocks = pair_of(i - feed - 3, per)
        put_pair(branch, blocks, dot(gathered(a_ref, blocks), ws_ref[...]).astype(BF))

    in_turn(i, feed, steps, per, ((4, lambda s: branch.add(s, chip_rows)),))
    if line:
        for k in range(1, line):
            at_step(feed + k, lambda k=k: shrink.step(k))
    half = units // tile
    at_step(feed + steps, lambda: tiles(gate_ref, xn_ref, dgu_ref, 0, half, 0))
    if line:
        at_step(feed + steps, expand.start)
        for k in range(1, line):
            at_step(feed + steps + k, lambda k=k: expand.step(k))
    at_step(feed + steps + 1, lambda: tiles(gup_ref, xn_ref, dgu_ref, 0, half, half), written[1].start)

    @pl.when(i == feed + steps + 4)
    def _():
        attended.drain()
        pulled_back.drain()
        norms.drain()
        grads.drain()
        for t in range(4):
            branch.sent(t * per + per - 1)
        lax.fori_loop(0, 4 * per, lambda s, c: (grads.ready(s), c)[1], 0)
        for copy in written:
            copy.wait()
        if line:
            shrink.finish(write_to(gsh_out))
            shrink.drain()
            expand.finish(write_to(gate_out))
            expand.drain()
            first.drain()
            second.drain()


def middle(q, k, vt, tags, bars, wm, x, dy, gains, weights, kv, group, unit, line):
    length = q.shape[0]
    n = LANES
    d = wm.shape[1]
    share = (length // 4, d)
    per = share[0] // SUB
    steps = 2 * per
    we, ws = (w.shape for w in weights)
    shards = 2 * line
    shrink = jax.ShapeDtypeStruct(ws, BF)
    gate = jax.ShapeDtypeStruct((we[0], we[1] // 2), BF)
    more = []
    if line:
        shrink = jax.ShapeDtypeStruct(ws, FP)
        gate = jax.ShapeDtypeStruct(gate.shape, FP)
        we, ws = (we[0] * shards, we[1]), (ws[0], ws[1] * shards)
        more = [pltpu.VMEM(ws, BF), *reduce_scratch(line, shrink.shape), pltpu.VMEM((we[0], we[1] // 2), BF),
                *reduce_scratch(line, gate.shape), *GATHER_SEMS(shards), *GATHER_SEMS(shards)]
    units = ws[0]
    results = [jax.ShapeDtypeStruct(q.shape, BF), jax.ShapeDtypeStruct((length // SUB, 8, SUB * group), FP),
               jax.ShapeDtypeStruct(share, FP), jax.ShapeDtypeStruct((per, SUB, d), BF), gate,
               jax.ShapeDtypeStruct((we[0], units), BF), jax.ShapeDtypeStruct(share, FP),
               jax.ShapeDtypeStruct((length, d), BF), jax.ShapeDtypeStruct((8, d), FP),
               shrink]
    out_specs = [whole(r.shape) for r in results]
    for at in (0, 5, 7):
        out_specs[at] = ANYWHERE
    held = [q, k, vt, tags, bars, wm, gains]
    return pl.pallas_call(
        partial(middle_kernel, kv, group, unit, line, per, steps),
        grid=(3 * steps + 8,),
        in_specs=[whole(a.shape) for a in held] + [ANYWHERE] * 4,
        out_specs=out_specs,
        out_shape=results,
        scratch_shapes=[pltpu.VMEM((kv, n, SUB * group), FP), pltpu.VMEM((kv, 8, SUB * group), FP),
                        pltpu.VMEM(share, BF), pltpu.VMEM((length, d), BF), pltpu.VMEM(we, BF), pltpu.VMEM(ws, BF),
                        pltpu.SemaphoreType.DMA((6,)),
                        pltpu.VMEM(share, FP), pltpu.VMEM((length, d), BF), pltpu.VMEM((length, units), BF),
                        pltpu.VMEM((length, 2 * units), BF), pltpu.VMEM(q.shape, BF), pltpu.VMEM((we[0], units), BF),
                        *pairs_scratch(per, d, True), pltpu.SemaphoreType.DMA((4, 4 * per)),
                        *pairs_scratch(per, d, True), pltpu.VMEM((per, SUB, d), BF),
                        pltpu.SemaphoreType.DMA((4, 4 * per)),
                        *pairs_scratch(per, d, False), *more],
        compiler_params=params(collective_id=1, has_side_effects=True),
        name="middle",
    )(*held, x, dy, *weights)


def back_kernel(kv, group, unit, scale, blocks, per, line, *refs):
    refs = list(refs)
    take = lambda count: [refs.pop(0) for _ in range(count)]
    q_ref, k_ref, v_ref, kt_ref, tags_ref, bars_ref, lse_ref, ctx_block, dh_block, wm_ref = take(10)
    raw_ref, cos_ref, sin_ref, all_gains, base_ref, dg2_ref, other_ref = take(7)
    x_all, dh_all = take(2)
    late_from = take(4)
    grads = take(2) if line else []
    in_ref, out_ref, gains_out = take(3)
    sums = take(3) if line else []
    weight_grads = [] if line else take(2)
    late_to = take(4)
    wp_ref, ctx_ref, dh_ref, xn_ref = late_to
    late_sem = take(1)[0]
    late = [pltpu.make_async_copy(a, b, late_sem.at[w]) for w, (a, b) in enumerate(zip(late_from, late_to))]
    dk_ref, dv_ref, dq_ref, dqkv_ref = take(4)
    b_far, b_sems, x_held, x_near, x_sems = take(5)
    mine_ref, far_ref, x_far, f_sems, x_ref, dh_own, own_sems, heads_ref, fold_ref = take(9)
    place = Place(line)
    i = pl.program_id(0)
    b = blocks - 1 - i
    n = LANES
    pairs = Pairs(place, per, x_held, x_near, x_sems, lambda s: s % x_held.shape[0])
    subs = ROWS // SUB
    share, d = x_ref.shape
    gq, gk = all_gains[:, 2 * d:2 * d + n], all_gains[:, 2 * d + n:]
    tile = 256
    tensors = lax.axis_size("tensor")
    mates = [(place.dp, (place.t + step) % tensors) for step in range(1, tensors)]
    peers = []
    own_rows = pl.ds(pl.multiple_of(place.t * share, share), share)
    own_copies = [pltpu.make_async_copy(x_all.at[own_rows, :], x_ref, own_sems.at[0]),
                  pltpu.make_async_copy(dh_all, dh_own, own_sems.at[1])]
    if line:
        shards = 2 * line
        gm_ref, gp_ref = take(2)
        expand = Reduce(place, grads[1], row_cut(grads[1].shape[0] // shards), *take(4))
        merge = Reduce(place, gm_ref, column_cut(gm_ref.shape[1] // shards), None, *take(3))
        project = Reduce(place, gp_ref, row_cut(gp_ref.shape[0] // shards), None, *take(3))
        shown, over, g_sems = take(3)
        peers = [((place.dp + step) % shards, place.t) for step in range(1, shards)]
    else:
        gp_ref, gm_ref = weight_grads

    def tiles(grad_ref, left_ref, right_ref):
        def one(t, carry):
            cut = pl.ds(pl.multiple_of(t * tile, tile), tile)
            grad_ref[:, cut] = dot(left_ref[...], right_ref[:, cut], 0, 0).astype(grad_ref.dtype)
            return carry

        lax.fori_loop(0, grad_ref.shape[1] // tile, one, 0)

    def write_up(values):
        sums[0][:, 0, :] = grads[0][...]
        sums[0][:, 1, :] = values

    def project_rows(t):
        cut = pl.ds(pl.multiple_of(t * tile, tile), tile)
        gp_ref[cut, :] = dot(xn_ref[:, cut], dqkv_ref[...], 0, 0).astype(BF)

    def chip(k):
        return send(far_ref.at[k], x_far.at[k], f_sems.at[0, k], f_sems.at[1, k], place.chip)

    def branch(k):
        return send(other_ref.at[k], b_far.at[k], b_sems.at[0, k], b_sems.at[1, k], place.chip)

    @pl.when(i == 0)
    def _():
        barrier = pltpu.get_barrier_semaphore()
        for device in mates + peers:
            pl.semaphore_signal(barrier, inc=1, device_id=device, device_id_type=MESH)
        for copy in late:
            copy.start()
        pl.semaphore_wait(barrier, len(mates + peers))
        if line:
            expand.start()
        for k in range(per):
            branch(k).start()
        dk_ref[...] = jnp.zeros_like(dk_ref)
        dv_ref[...] = jnp.zeros_like(dv_ref)
        heads_ref[...] = jnp.zeros_like(heads_ref)

    @pl.when(i < blocks)
    def _():
        here = pl.ds(pl.multiple_of(b * ROWS, ROWS), ROWS)
        dctx = dot(dh_block[...], wm_ref[...], 1, 1).astype(BF)
        ctx, q = ctx_block[...], q_ref[...]
        bars = jnp.concatenate([bars_ref[...]] * group, axis=0)
        wide, queries, outward, centres, lses = [], [], [], [], []
        for h in range(kv):
            queries.append(stacked(q, h, group))
            wide.append(jnp.concatenate([queries[h], bars], axis=1))
            outward.append(stacked(dctx, h, group))
            both = outward[h].astype(FP) * stacked(ctx, h, group).astype(FP)
            centres.append(jnp.sum(both.T, axis=0, keepdims=True))
            lses.append(jnp.concatenate([lse_ref[u, h:h + 1, g * SUB:(g + 1) * SUB]
                                         for g in range(group) for u in range(ROWS // SUB)], axis=1))
        dq_ref[...] = jnp.zeros_like(dq_ref)

        def chunk(j, diagonal):
            at = pl.ds(pl.multiple_of(j * ROWS, ROWS), ROWS)
            tags = tags_ref[at, :]
            for h in range(kv):
                cut = slice(h * n, (h + 1) * n)
                keys = jnp.concatenate([k_ref[at, cut], tags], axis=1)
                p = jnp.exp2(dot(keys, wide[h], 1, 1) * unit - lses[h])
                if diagonal:
                    p = jnp.where(causal_tile(group), p, 0.0)
                dp = dot(v_ref[at, cut], outward[h], 1, 1)
                ds = (p * (dp - centres[h])).astype(BF)
                dv_ref[at, cut] += dot(p.astype(BF), outward[h])
                dk_ref[at, cut] += dot(ds, queries[h])
                dq_ref[h] += dot(kt_ref[cut, at], ds)

        lax.fori_loop(0, b, lambda j, c: (chunk(j, False), c)[1], 0)
        chunk(b, True)

        cosines, sines = cos_ref[...], sin_ref[...]
        pieces = []
        for h in range(kv):
            dq = dq_ref[h].T
            for c in range(group + 1):
                if c < group:
                    grad, gain, row = dq[c * ROWS:(c + 1) * ROWS] * scale, gq, 0
                else:
                    grad, gain, row = dk_ref[here, h * n:(h + 1) * n] * scale, gk, 1
                grad = grad * cosines - pltpu.roll(grad, n // 2, 1) * sines
                at = (h * (group + 1) + c) * n
                piece, gain_grad = rms_pull(raw_ref[:, at:at + n], gain, grad)
                heads_ref[row] += fold_rows(gain_grad)
                pieces.append(piece)
            pieces.append(dv_ref[here, h * n:(h + 1) * n])
        dqkv = jnp.concatenate(pieces, axis=1).astype(BF)
        dqkv_ref[here, :] = dqkv
        pl.when(i == 0)(late[0].wait)
        part = dot(dqkv, wp_ref[...], 1, 1).astype(BF)
        for u in range(subs):
            s = subs * b + u
            pairs.put(s, part[u * SUB:(u + 1) * SUB], (i >= 2, s + 2 * subs))

    def chip_rows(mine, k, summed):
        @pl.when(mine)
        def _():
            mine_ref[pl.ds(pl.multiple_of(k * SUB, SUB), SUB), :] = summed

        @pl.when(jnp.logical_not(mine))
        def _():
            far_ref[k] = summed.astype(BF)
            chip(k).start()

    @pl.when(i >= 1)
    def _():
        for u in range(subs):
            pairs.add(subs * (b + 1) + u, chip_rows)

    @pl.when(i == 3)
    def _():
        for k in range(per):
            branch(k).wait()
            at = slice(k * SUB, (k + 1) * SUB)
            out_ref[at, :] = (base_ref[at, :] + b_far[k].astype(FP)).astype(BF)
        for copy in own_copies:
            copy.start()

    @pl.when(i == 1)
    def _():
        late[1].wait()
        late[2].wait()
        tiles(gm_ref, ctx_ref, dh_ref)

    if line:
        for step, act in enumerate((lambda: expand.step(1), lambda: expand.step(2), lambda: expand.step(3), merge.start,
                                    lambda: merge.step(1), lambda: merge.step(2))):
            pl.when(i == step)(act)

    def input_rows(k):
        at = slice(k * SUB, (k + 1) * SUB)
        chip(k).wait()
        summed = mine_ref[at, :] + x_far[k].astype(FP)
        pulled, gain_grad = rms_pull(x_ref[at, :].astype(FP), all_gains[:, :d], summed)
        in_ref[at, :] = (dh_own[at, :] + pulled).astype(BF)
        fold_ref[...] += fold_rows(gain_grad)

    def folded(ref):
        pieces = [fold_ref[...], dg2_ref[...], heads_ref[0], heads_ref[1]]
        row = jnp.sum(jnp.concatenate(pieces, axis=1), axis=0, keepdims=True)
        count = row.shape[1] // n
        for j in range(count):
            ref[j:j + 1, :] = row[:, j * n:(j + 1) * n]
        ref[count:, :] = jnp.zeros((ref.shape[0] - count, n), FP)

    def show(buffer, me, devices, first):
        copies = [send(buffer.at[me], buffer.at[me], g_sems.at[0, first + step], g_sems.at[1, first + step], device)
                  for step, device in enumerate(devices, 1)]
        for copy in copies:
            copy.start()
        return copies

    def added(buffer, me, devices, first):
        count = len(devices) + 1
        for step in range(1, count):
            who = (me - step + count) % count
            send(buffer.at[who], buffer.at[who], g_sems.at[0, first + step], g_sems.at[1, first + step],
                 place.sibling).wait_recv()
        total = buffer[0]
        for who in range(1, count):
            total = total + buffer[who]
        return total

    @pl.when(i == blocks)
    def _():
        fold_ref[...] = jnp.zeros_like(fold_ref)
        late[3].wait()
        for copy in own_copies:
            copy.wait()
        if not line:
            tiles(gp_ref, xn_ref, dqkv_ref)
            for k in range(per):
                input_rows(k)
            folded(gains_out)
        else:
            project_rows(project.turn(0))
            project.start()
            for q in range(1, line):
                project_rows(project.turn(q))
            merge.step(3)
            expand.finish(write_up)
            project.step(1)
            merge.finish(write_to(sums[1]))
            project.step(2)
            for k in range(per):
                input_rows(k)
            folded(shown.at[place.t])
            copies = show(shown, place.t, mates, 0)
            project.step(3)
            over[place.dp] = added(shown, place.t, mates, 0)
            copies += show(over, place.dp, peers, tensors)
            project.finish(write_to(sums[2]))
            gains_out[...] = added(over, place.dp, peers, tensors)
            for copy in copies:
                copy.wait_send()
            for r in (expand, merge, project):
                r.drain()
        for s in range(2 * subs):
            pairs.sent(s)


def back(q, k, v, kt, tags, bars, lse, ctx, dh, wm, wp, raw, cosines, sines, gains, xn, base, dg2, other, x, dh_own,
         grads, kv, group, unit, scale, line):
    length = q.shape[0]
    n = LANES
    d = wm.shape[1]
    blocks = length // ROWS
    per = other.shape[0]
    share = base.shape
    block_of = lambda i: jnp.maximum(blocks - 1 - i, 0)
    rows = lambda w: pl.BlockSpec((ROWS, w), lambda i: (block_of(i), 0))
    late = [wp, ctx, dh, xn]
    gain_rows = (-(-(gains.shape[1] // n) // 8) * 8, n)
    scratch = [*[pltpu.VMEM(a.shape, BF) for a in late], pltpu.SemaphoreType.DMA((4,)),
               pltpu.VMEM((length, kv * n), FP), pltpu.VMEM((length, kv * n), FP),
               pltpu.VMEM((kv, n, ROWS * group), FP), pltpu.VMEM((length, wp.shape[1]), BF),
               pltpu.VMEM((per, SUB, d), BF), pltpu.SemaphoreType.DMA((2, per)),
               pltpu.VMEM((2 * ROWS // SUB, SUB, d), BF), pltpu.VMEM((2 * per, SUB, d), BF),
               pltpu.SemaphoreType.DMA((2, 4 * per)),
               pltpu.VMEM(share, FP), pltpu.VMEM((per, SUB, d), BF), pltpu.VMEM((per, SUB, d), BF),
               pltpu.SemaphoreType.DMA((2, per)), pltpu.VMEM(share, BF), pltpu.VMEM(share, FP),
               pltpu.SemaphoreType.DMA((2,)), pltpu.VMEM((2, 8, n), FP), pltpu.VMEM((8, d), FP)]
    results = [jax.ShapeDtypeStruct(share, BF), jax.ShapeDtypeStruct(share, BF), jax.ShapeDtypeStruct(gain_rows, FP)]
    if line:
        shards = 2 * line
        own = [grads[0].shape, (wm.shape[0], wm.shape[1] // shards),
               (wp.shape[0] // shards, wp.shape[1])]
        views = ((own[0][0], 2, own[0][1]), own[1], (own[2][0], own[2][1] // n, n))
        results += [jax.ShapeDtypeStruct(s, FP) for s in views]
        scratch += [pltpu.VMEM(wm.shape, BF), pltpu.VMEM(wp.shape, BF)]
        for w, s in enumerate(own):
            scratch += reduce_scratch(line, s, w == 0)
        scratch += [pltpu.VMEM((4, *gain_rows), FP), pltpu.VMEM((shards, *gain_rows), FP),
                    pltpu.SemaphoreType.DMA((2, 4 + shards))]
    else:
        results += [jax.ShapeDtypeStruct(wp.shape, BF), jax.ShapeDtypeStruct(wm.shape, BF)]
    args = [q, k, v, kt, tags, bars, lse, ctx, dh, wm, raw, cosines, sines, gains, base, dg2]
    more = [other, x, dh_own, *late, *grads]
    specs = [whole(a.shape) for a in args] + [ANYWHERE] * len(more)
    if line:
        specs[-2] = whole(grads[0].shape)
    for at in (0, 5, 7, 8, 10, 11, 12):
        specs[at] = rows(args[at].shape[1])
    specs[6] = pl.BlockSpec((ROWS // SUB, 8, SUB * group), lambda i: (block_of(i), 0, 0))
    return pl.pallas_call(
        partial(back_kernel, kv, group, unit, scale, blocks, per, line),
        grid=(blocks + 1,),
        in_specs=specs,
        out_specs=[whole(r.shape) for r in results],
        out_shape=results,
        scratch_shapes=scratch,
        compiler_params=params(collective_id=3, has_side_effects=True),
        name="back",
    )(*args, *more)


def adamw_step(weight, moment_one, moment_two, gradient, step_rate, decay):
    mean_next = BETA_ONE * moment_one + (1.0 - BETA_ONE) * gradient
    square_next = BETA_TWO * moment_two + (1.0 - BETA_TWO) * gradient * gradient
    mean_hat = mean_next / (1.0 - BETA_ONE**STEP)
    square_hat = square_next / (1.0 - BETA_TWO**STEP)
    weight_next = weight - step_rate * (mean_hat / (jnp.sqrt(square_hat) + EPS_ADAM) + decay * weight)
    return weight_next, mean_next, square_next


def shards(
    tokens, cotangent, parents, token_segment, tree_id,
    projection_weight, projection_first_moment, projection_second_moment,
    merge_master, merge_mean, merge_square,
    expand_master, expand_mean, expand_square,
    shrink_master, shrink_mean, shrink_square,
    gain_master, gain_mean, gain_square,
):
    x = tokens[0]
    dy = cotangent[0]
    length, d = x.shape
    d_own, kv, per, n = projection_weight.shape
    group = per - 2
    units = expand_master.shape[2]
    scale = n ** (-0.5)
    unit = scale * math.log2(math.e)
    line = 4 if lax.axis_size("dp") == 8 and d_own % LANES == 0 else 0
    if line:
        masters = (projection_weight.reshape(d_own, kv * per, n), merge_master, expand_master, shrink_master)
    else:
        wp, we = (lax.all_gather(w.astype(BF).reshape(d_own, -1), "dp", axis=0, tiled=True)
                  for w in (projection_weight, expand_master))
        wm, ws = (lax.all_gather(w.astype(BF), "dp", axis=1, tiled=True) for w in (merge_master, shrink_master))
        masters = (wp,)

    gains = gain_master[None]
    fronts = front(x, gains, token_segment, parents, tree_id, masters, kv, group, line)
    xn1, q, k, v, kt, vt, raw, tags, bars, cosines, sines = fronts[:11]
    if line:
        wp, wm, *low = fronts[11:]
    else:
        low = (we, ws)
    ctx, lse, base, other, gate_sum, up_grad, dh, dhb, dg2, shrink_sum = middle(
        q, k, vt, tags, bars, wm, x, dy, gains, low, kv, group, unit, line)
    backs = back(q, k, v, kt, tags, bars, lse, ctx, dhb, wm, wp, raw, cosines, sines, gains, xn1,
                 base, dg2, other, x, dh, (gate_sum, up_grad) if line else (), kv, group, unit, scale, line)
    input_grad, output, gain_rows = backs[:3]
    if line:
        expand_sum, merge_sum, project_sum = backs[3:]
    else:
        gain_rows = lax.psum(gain_rows, ("dp", "tensor"))
        project_sum, expand_sum = (
            lax.psum_scatter(g, "dp", scatter_dimension=0, tiled=True) for g in (backs[3], jnp.concatenate([gate_sum, up_grad], axis=1)))
        merge_sum, shrink_sum = (
            lax.psum_scatter(g, "dp", scatter_dimension=1, tiled=True) for g in (backs[4], shrink_sum))
    output, input_grad = output[None], input_grad[None]
    gain_grad = gain_rows.reshape(-1)[:gain_master.shape[0]]

    outs = [output, input_grad]
    for weight, mean, square, grad, rate in (
        (projection_weight, projection_first_moment, projection_second_moment, project_sum, RATE_PROJECT),
        (merge_master, merge_mean, merge_square, merge_sum, RATE_MERGE),
        (expand_master, expand_mean, expand_square, expand_sum, RATE_EXPAND),
        (shrink_master, shrink_mean, shrink_square, shrink_sum, RATE_SHRINK),
    ):
        grad = grad.astype(FP).reshape(weight.shape)
        after, mean_next, square_next = adamw_step(weight, mean, square, grad, rate, DECAY)
        outs += [after, mean_next, square_next, after.astype(BF)]
    gain_next, gain_mean_next, gain_square_next = adamw_step(
        gain_master, gain_mean, gain_square, gain_grad, RATE_GAIN, 0.0)
    return (*outs, gain_mean_next, gain_square_next, gain_next)


def solution(mesh):
    tokens = P("dp", None, None)
    project = P("dp", "tensor", None, None)
    columns = P("tensor", "dp")
    expand = P("dp", None, "tensor")
    shared = P("dp", "tensor", None)
    return jax.shard_map(
        shards,
        mesh=mesh,
        in_specs=(tokens, tokens, P(), P("dp", None), P("dp"), *[project] * 3, *[columns] * 3, *[expand] * 3,
                  *[columns] * 3, P(), P(), P()),
        out_specs=(shared, shared, *[project] * 4, *[columns] * 4, *[expand] * 4, *[columns] * 4, P(), P(), P()),
        check_vma=False,
    )
```

```python
import math
from functools import partial

import jax
import jax.numpy as jnp
import numpy as np
from jax import lax
from jax.experimental import pallas as pl
from jax.experimental.pallas import tpu as pltpu
from jax.sharding import PartitionSpec as P

STEP = 5
EPS_NORM = 1e-06
THETA = 1000000.0
BETA_ONE = 0.5
BETA_TWO = 0.5
EPS_ADAM = 1e-08
DECAY = 0.1
RATE_PROJECT = 0.05
RATE_MERGE = 0.3
RATE_EXPAND = 0.05
RATE_SHRINK = 0.03
RATE_GAIN = 0.3

BF = jnp.bfloat16
FP = jnp.float32
ROWS = 256
LANES = 128
SUB = 128
PARTS = 2
MESH = pl.DeviceIdType.MESH
BLOCKED = -1e30
VMEM_LIMIT = 56 * 2**20


def params(**more):
    return pltpu.CompilerParams(vmem_limit_bytes=VMEM_LIMIT, **more)


def dot(a, b, ca=1, cb=0):
    return lax.dot_general(a, b, (((ca,), (cb,)), ((), ())), preferred_element_type=FP)


def inverse_rms(values):
    return lax.rsqrt(jnp.mean(values * values, axis=-1, keepdims=True) + EPS_NORM)


def rms_pull(values, scales, grad):
    r = inverse_rms(values)
    scaled = grad * scales
    mean = jnp.mean(values * scaled, axis=-1, keepdims=True)
    return r * scaled - values * (r * r * r * mean), grad * values * r


def fold_rows(values):
    n, w = values.shape
    return jnp.sum(values.reshape(n // 8, 8, w), axis=0)


class Place:
    def __init__(self, line):
        self.line = line
        self.dp, self.t = lax.axis_index("dp"), lax.axis_index("tensor")
        self.z, self.y = self.dp // 2, self.dp % 2
        self.x, self.c = self.t // 2, self.t % 2
        self.has_up, self.has_down = self.z < line - 1, self.z > 0
        self.up, self.down = (self.dp + 2, self.t), (self.dp - 2, self.t)
        self.across = (self.dp + 1 - 2 * self.y, self.t)
        self.sibling = (self.dp, self.t + 1 - 2 * self.c)
        self.chip = (self.dp, (1 - self.x) * 2 + self.c)

    def greet(self, tensor, line, meanwhile=None):
        barrier = pltpu.get_barrier_semaphore()

        def signal(device):
            pl.semaphore_signal(barrier, inc=1, device_id=device, device_id_type=MESH)

        if tensor:
            signal(self.sibling)
            signal(self.chip)
        if line:
            signal(self.across)
            pl.when(self.has_up)(lambda: signal(self.up))
            pl.when(self.has_down)(lambda: signal(self.down))
        peers = (2 if tensor else 0) + (1 if line else 0)
        if line:
            peers = peers + jnp.where(self.has_up, 1, 0) + jnp.where(self.has_down, 1, 0)
        if meanwhile is not None:
            meanwhile()
        pl.semaphore_wait(barrier, peers)


def send(src, dst, sent, arrived, device):
    return pltpu.make_async_remote_copy(
        src_ref=src, dst_ref=dst, send_sem=sent, recv_sem=arrived, device_id=device, device_id_type=MESH)


class Several:
    def __init__(self, copies):
        self.copies = copies

    def start(self):
        for copy in self.copies:
            copy.start()

    def wait_send(self):
        for copy in self.copies:
            copy.wait_send()

    def wait_recv(self):
        for copy in self.copies:
            copy.wait_recv()

    def wait(self):
        self.wait_send()
        self.wait_recv()


def send_split(src, dst, sems, device):
    size = SUB // PARTS
    rows = [pl.ds(part * size, size) for part in range(PARTS)]
    return Several([send(src.at[rows[part], :], dst.at[rows[part], :], *sems(part), device) for part in range(PARTS)])


def row_cut(size):
    return lambda j: (pl.ds(pl.multiple_of(j * size, size), size), slice(None))


def column_cut(size):
    return lambda j: (slice(None), pl.ds(pl.multiple_of(j * size, size), size))


class Gather:
    def __init__(self, place, own, full, cut, sems, local):
        self.place, self.own, self.full, self.cut, self.sems, self.local = place, own, full, cut, sems, local

    def copy(self, kind, src, j):
        p = self.place
        device = (p.up, p.down, p.across)[kind]
        return send(src, self.full.at[self.cut(j)], self.sems.at[kind, j], self.sems.at[3, j], device)

    def kept(self):
        return pltpu.make_async_copy(self.own, self.full.at[self.cut(self.place.dp)], self.local)

    def source(self):
        return self.full.at[self.cut(self.place.dp)] if self.own is None else self.own

    def start(self):
        p = self.place
        self.copy(2, self.source(), p.dp).start()
        pl.when(p.has_up)(lambda: self.copy(0, self.source(), p.dp).start())
        pl.when(p.has_down)(lambda: self.copy(1, self.source(), p.dp).start())
        if self.own is not None:
            self.kept().start()

    def arrivals(self, k):
        p = self.place
        return ((0, p.z >= k, (p.z - k) * 2 + p.y, p.has_up), (1, p.z + k < p.line, (p.z + k) * 2 + p.y, p.has_down))

    def hop(self, k):
        for kind, here, j, further in self.arrivals(k):
            @pl.when(here)
            def _(kind=kind, j=j, further=further):
                piece = self.full.at[self.cut(j)]
                self.copy(kind, piece, j).wait_recv()
                pl.when(further)(lambda: self.copy(kind, piece, j).start())
                self.copy(2, piece, j).start()

    def finish(self):
        p = self.place
        if self.own is not None:
            self.kept().wait()
        for zz in range(p.line):
            j = zz * 2 + 1 - p.y
            self.copy(2, self.full.at[self.cut(j)], j).wait_recv()

    def drain(self):
        p = self.place
        self.copy(2, self.source(), p.dp).wait_send()
        pl.when(p.has_up)(lambda: self.copy(0, self.source(), p.dp).wait_send())
        pl.when(p.has_down)(lambda: self.copy(1, self.source(), p.dp).wait_send())
        for k in range(1, p.line):
            for kind, here, j, further in self.arrivals(k):
                @pl.when(here)
                def _(kind=kind, j=j, further=further):
                    piece = self.full.at[self.cut(j)]
                    pl.when(further)(lambda: self.copy(kind, piece, j).wait_send())
                    self.copy(2, piece, j).wait_send()


class Reduce:
    def __init__(self, place, grad, cut, kept, across, lined, sems):
        self.place, self.grad, self.cut, self.kept, self.sems = place, grad, cut, kept, sems
        self.across, self.lined = across, lined

    def cross(self, zz):
        p = self.place
        return send(self.grad.at[self.cut(zz * 2 + 1 - p.y)], self.across.at[zz],
                    self.sems.at[0, zz], self.sems.at[1, zz], p.across)

    def climb(self, t):
        return send(self.across.at[t], self.lined.at[t + 1], self.sems.at[2, t], self.sems.at[3, t], self.place.up)

    def sink(self, t):
        return send(self.across.at[t], self.lined.at[t], self.sems.at[4, t], self.sems.at[5, t], self.place.down)

    def load(self, zz):
        return pltpu.make_async_copy(self.grad.at[self.cut(zz * 2 + self.place.y)], self.kept.at[zz], self.sems.at[6, zz])

    def mine(self, zz):
        if self.kept is None:
            return self.grad[self.cut(zz * 2 + self.place.y)].astype(FP)
        return self.kept[zz].astype(FP)

    def loaded(self, zz):
        if self.kept is not None:
            self.load(zz).wait()

    def turn(self, q):
        z = self.place.z
        low = z < 2
        if q == 0:
            return jnp.where(low, 3, 0)
        if q == 1:
            return jnp.where(low, 2, 1)
        if q == 2:
            return jnp.where(low, 1 - z, 5 - z)
        return z

    def start(self):
        self.cross(self.turn(0)).start()
        if self.kept is not None:
            for zz in range(self.place.line):
                self.load(zz).start()

    def advance(self, q):
        self.cross(self.turn(q - 1)).wait_send()
        self.cross(self.turn(q)).start()

    def hop(self, h):
        p = self.place

        def pass_on(t, coming, more, slot):
            self.loaded(t)
            self.cross(t).wait_recv()

            @pl.when(jnp.logical_not(more))
            def _():
                self.across[t] = (self.mine(t) + self.across[t].astype(FP)).astype(BF)

            @pl.when(more)
            def _():
                coming(t).wait_recv()
                self.across[t] = (self.mine(t) + self.across[t].astype(FP) + self.lined[slot].astype(FP)).astype(BF)

            coming(t).start()

        pl.when(p.z < h)(lambda: pass_on(p.z + p.line - h, self.climb, p.has_down, p.z + p.line - h + 1))
        pl.when(p.z >= p.line - h)(lambda: pass_on(p.z - p.line + h, self.sink, p.has_up, p.z - p.line + h))

    def finish(self, write):
        p = self.place
        self.loaded(p.z)
        self.cross(p.z).wait_recv()
        pl.when(p.has_down)(lambda: self.climb(p.z).wait_recv())
        pl.when(p.has_up)(lambda: self.sink(p.z).wait_recv())
        from_below = jnp.where(p.has_down, self.lined[p.z + 1].astype(FP), 0.0)
        from_above = jnp.where(p.has_up, self.lined[p.z].astype(FP), 0.0)
        write(self.mine(p.z) + self.across[p.z].astype(FP) + from_below + from_above)

    def step(self, k):
        self.advance(k)
        self.hop(k)

    def drain(self):
        p = self.place
        self.cross(p.z).wait_send()
        for zz in range(p.line):
            pl.when(zz > p.z)(lambda zz=zz: self.climb(zz).wait_send())
            pl.when(zz < p.z)(lambda zz=zz: self.sink(zz).wait_send())


def write_to(ref):
    def write(values):
        if len(ref.shape) == 2:
            ref[...] = values
            return
        width = ref.shape[2]
        for j in range(ref.shape[1]):
            ref[:, j, :] = values[:, j * width:(j + 1) * width]

    return write


def reduce_scratch(line, shape, kept=False):
    return [pltpu.VMEM((line, *shape), BF)] * kept + [pltpu.VMEM((line, *shape), BF), pltpu.VMEM((line + 1, *shape), BF),
                                                      pltpu.SemaphoreType.DMA((7, line))]


class Pairs:
    def __init__(self, place, per, held, near, sems, slot_of):
        self.place, self.per, self.held, self.near, self.sems, self.slot_of = place, per, held, near, sems, slot_of

    def near_slot(self, s):
        return (s // (2 * self.per)) * self.per + s % self.per

    def to_sibling(self, s):
        return send(self.held.at[self.slot_of(s)], self.near.at[self.near_slot(s)], self.sems.at[0, s],
                    self.sems.at[1, s], self.place.sibling)

    def sends(self, s):
        return self.place.c != (s // self.per) % 2

    def sent(self, s):
        pl.when(self.sends(s))(lambda: self.to_sibling(s).wait_send())

    def put(self, s, rows, before=None):
        if before is not None:
            pl.when(before[0])(lambda: self.sent(before[1]))
        self.held[self.slot_of(s)] = rows
        pl.when(self.sends(s))(lambda: self.to_sibling(s).start())

    def put_next(self, s, rows):
        self.put(s, rows, (s % self.per >= 1, s - 1))

    def add(self, s, use):
        t = s // self.per

        @pl.when(self.place.c == t % 2)
        def _():
            self.to_sibling(s).wait_recv()
            use(self.place.x == t // 2, s % self.per,
                self.held[self.slot_of(s)].astype(FP) + self.near[self.near_slot(s)].astype(FP))


class Exchange(Pairs):
    def __init__(self, place, per, held, near, far, total, sems):
        super().__init__(place, per, held, near, sems, lambda s: s // per)
        self.far, self.total = far, total

    def rows(self, k):
        return pl.ds(pl.multiple_of(k * SUB, SUB), SUB)

    def to_chip(self, s):
        return send_split(self.near.at[self.near_slot(s)], self.far.at[s % self.per],
                          lambda part: (self.sems.at[2 + 2 * part, s], self.sems.at[3 + 2 * part, s]), self.place.chip)

    def add_chip(self, s):
        def use(mine, k, summed):
            @pl.when(jnp.logical_not(mine))
            def _():
                self.near[self.near_slot(s)] = summed.astype(BF)
                self.to_chip(s).start()

            @pl.when(mine)
            def _():
                self.total[self.rows(k), :] = summed

        self.add(s, use)

    def take(self, s, use):
        @pl.when(s // self.per == self.place.t)
        def _():
            k = s % self.per
            self.to_chip(s).wait_recv()
            use(s, self.rows(k), self.total[self.rows(k), :] + self.far[k].astype(FP))

    def drain(self):
        p = self.place

        def one(s, carry):
            t = s // self.per
            pl.when(s % self.per == self.per - 1)(lambda: self.sent(s))
            pl.when(jnp.logical_and(p.c == t % 2, p.x != t // 2))(lambda: self.to_chip(s).wait_send())
            return carry

        lax.fori_loop(0, 4 * self.per, one, 0)


def pair_of(step, per):
    t = step % 2
    return t * per + step // 2, (3 - t) * per + step // 2


def pairs_scratch(per, d, exchange):
    rows = [pltpu.VMEM((4, SUB, d), BF), pltpu.VMEM((2 * per, SUB, d), BF)]
    return rows + [pltpu.VMEM((per, SUB, d), BF)] * exchange + [pltpu.SemaphoreType.DMA((2 + 2 * PARTS * exchange, 4 * per))]


class Spread:
    def __init__(self, place, per, stage, full, sems):
        self.place, self.per, self.stage, self.full, self.sems = place, per, stage, full, sems

    def rows(self, s):
        return self.full.at[pl.ds(pl.multiple_of(s * SUB, SUB), SUB), :]

    def source(self, s):
        return self.rows(s) if self.stage is None else self.stage.at[s % self.per]

    def copy(self, kind, src, s):
        if kind == 0:
            return send_split(src, self.rows(s), lambda part: (self.sems.at[3 + 2 * part, s], self.sems.at[4 + 2 * part, s]),
                              self.place.chip)
        return send(src, self.rows(s), self.sems.at[0, s], self.sems.at[1, s], self.place.sibling)

    def kept(self, s):
        return pltpu.make_async_copy(self.source(s), self.rows(s), self.sems.at[2, s])

    def send(self, s):
        for kind in (0, 1):
            self.copy(kind, self.source(s), s).start()
        if self.stage is not None:
            self.kept(s).start()

    def owns(self, s):
        return s // self.per == self.place.t

    def passes(self, s):
        t = s // self.per
        return jnp.logical_and(self.place.c == t % 2, self.place.x != t // 2)

    def pass_on(self, s):
        @pl.when(self.passes(s))
        def _():
            self.copy(0, self.rows(s), s).wait_recv()
            self.copy(1, self.rows(s), s).start()

    def ready(self, s):
        if self.stage is not None:
            pl.when(self.owns(s))(lambda: self.kept(s).wait())
        pl.when((s // self.per) % 2 != self.place.c)(lambda: self.copy(1, self.rows(s), s).wait_recv())

    def drain(self):
        def one(s, carry):
            @pl.when(self.owns(s))
            def _():
                self.copy(0, self.source(s), s).wait_send()
                self.copy(1, self.source(s), s).wait_send()

            pl.when(self.passes(s))(lambda: self.copy(1, self.rows(s), s).wait_send())
            return carry

        lax.fori_loop(0, 4 * self.per, one, 0)


def whole(shape):
    return pl.BlockSpec(tuple(shape), lambda i: (0,) * len(shape), pipeline_mode=pl.Buffered(1))


ANYWHERE = pl.BlockSpec(memory_space=pl.ANY)
GATHER_SEMS = lambda shards: [pltpu.SemaphoreType.DMA((4, shards)), pltpu.SemaphoreType.DMA]


def make_tables(seg_ref, parents_ref, tree_ref, freq_ref, tags_ref, bars_ref, cos_ref, sin_ref):
    count = parents_ref.shape[1]
    n = LANES
    blocks = sin_ref.shape[0] // ROWS
    lane = lax.broadcasted_iota(jnp.int32, (1, n), 1).astype(FP)
    place_of = lambda b: pl.ds(pl.multiple_of(b * ROWS, ROWS), ROWS)

    def columns(b, carry):
        sin_ref[place_of(b), :] = jnp.broadcast_to(seg_ref[:, place_of(b)].astype(FP), (n, ROWS)).T
        return carry

    def tally(b, carry):
        column = sin_ref[place_of(b), :]
        return (carry[0] + fold_rows(jnp.where(column == lane, 1.0, 0.0)),
                carry[1] + fold_rows(jnp.where(column < lane, 1.0, 0.0)))

    lax.fori_loop(0, blocks, columns, 0)
    sizes, starts = lax.fori_loop(0, blocks, tally, (jnp.zeros((8, n), FP), jnp.zeros((8, n), FP)))
    sizes, starts = (jnp.sum(a, axis=0, keepdims=True) for a in (sizes, starts))
    table = parents_ref[...]
    chosen = jnp.where(lax.broadcasted_iota(jnp.int32, table.shape, 0) == tree_ref[0], table, 0)
    chosen = jnp.sum(chosen.astype(FP), axis=0, keepdims=True)
    parents = jnp.zeros((1, n), FP)
    for b in range(count):
        parents = jnp.where(lane == b, chosen[:, b:b + 1], parents)
    shifts = jnp.where(lane != 0, sizes[:, :1], 0.0) - starts

    def rows(b, carry):
        at = place_of(b)
        column = sin_ref[at, :]
        hot = column == lane
        parent = jnp.sum(jnp.where(hot, parents, 0.0), axis=1, keepdims=True)
        above = jnp.where(jnp.logical_and(lane == parent, lane != 0), sizes, 0.0)
        first = (b * ROWS).astype(FP)
        position = (lax.broadcasted_iota(jnp.int32, (ROWS, 1), 0).astype(FP) + first
                    + jnp.sum(jnp.where(hot, shifts, 0.0) + above, axis=1, keepdims=True))
        tags_ref[at, :] = jnp.where(hot, 1.0, 0.0).astype(BF)
        open_to = jnp.logical_or(jnp.logical_or(hot, lane == parent), jnp.logical_or(lane == 0, lane >= count))
        bars_ref[at, :] = jnp.where(open_to, 0.0, BLOCKED).astype(BF)
        angles = position * freq_ref[...]
        cos_ref[at, :] = jnp.cos(angles)
        turned = jnp.sin(angles)
        sin_ref[at, :] = jnp.where(lane < n // 2, -turned, turned)
        return carry

    lax.fori_loop(0, blocks, rows, 0)


def front_kernel(kv, group, line, *refs):
    refs = list(refs)
    take = lambda count: [refs.pop(0) for _ in range(count)]
    x_ref, gains_ref, seg_ref, parents_ref, tree_ref, freq_ref = take(6)
    masters = take(4) if line else take(1)
    xn_ref, q_ref, k_ref, v_ref, kt_ref, vt_ref, raw_ref, tags_ref, bars_ref, cos_ref, sin_ref = take(11)
    if line:
        wp_out, wm_out, we_low, ws_low = take(4)
        wp_ref, wm_low, p_sems, p_local, m_sems, m_local, out_sem = take(7)
    else:
        wp_ref = masters[0]
    xn_full, xn_sem = take(2)
    i = pl.program_id(0)
    final = pl.num_programs(0) - 1
    d = x_ref.shape[1]
    n = LANES
    per = group + 2
    if line:
        place = Place(line)
        size = masters[0].shape[0]
        project = Gather(place, None, wp_ref, row_cut(size), p_sems, p_local)
        merge = Gather(place, wm_low, wm_out, column_cut(wm_low.shape[1]), m_sems, m_local)
        written = pltpu.make_async_copy(wp_ref, wp_out, out_sem)
    normed = pltpu.make_async_copy(xn_full, xn_ref, xn_sem)

    def round_projection():
        at = pl.ds(pl.multiple_of(place.dp * size, size), size)
        for j in range(kv * per):
            wp_ref[at, j * n:(j + 1) * n] = masters[0][:, j, :].astype(BF)

    def norm(b, carry):
        at = pl.ds(pl.multiple_of(b * ROWS, ROWS), ROWS)
        x = x_ref[at, :].astype(FP)
        xn_full[at, :] = (x * inverse_rms(x) * gains_ref[:, :d]).astype(BF)
        return carry

    @pl.when(i == 0)
    def _():
        if line:
            place.greet(False, True, round_projection)
            project.start()
        lax.fori_loop(0, x_ref.shape[0] // ROWS, norm, 0)
        normed.start()
        if line:
            project.hop(1)
        make_tables(seg_ref, parents_ref, tree_ref, freq_ref, tags_ref, bars_ref, cos_ref, sin_ref)
        if line:
            project.hop(2)
            wm_low[...] = masters[1][...].astype(BF)
            units = masters[2].shape[2]
            for half in range(2):
                we_low[:, half * units:(half + 1) * units] = masters[2][:, half, :].astype(BF)
            ws_low[...] = masters[3][...].astype(BF)
            project.hop(3)
            merge.start()
            project.finish()
            written.start()

    if line:
        for k in range(1, line):
            pl.when(i == k + 1)(lambda k=k: merge.hop(k))
    at = pl.ds(pl.multiple_of(i * ROWS, ROWS), ROWS)
    qkv = dot(xn_full[at, :], wp_ref[...])
    cosines, sines = cos_ref[at, :], sin_ref[at, :]
    gq, gk = gains_ref[:, 2 * d:2 * d + n], gains_ref[:, 2 * d + n:]
    keys, values = [], []
    for h in range(kv):
        for c in range(group + 1):
            raw = qkv[:, (h * per + c) * n:(h * per + c + 1) * n]
            to = (h * (group + 1) + c) * n
            raw_ref[:, to:to + n] = raw
            y = raw * inverse_rms(raw) * (gq if c < group else gk)
            turned = y * cosines + pltpu.roll(y, n // 2, 1) * sines
            if c < group:
                to = (h * group + c) * n
                q_ref[:, to:to + n] = turned.astype(BF)
            else:
                keys.append(turned)
        values.append(qkv[:, (h * per + group + 1) * n:(h * per + group + 2) * n])
    for h in range(kv):
        k_ref[:, h * n:(h + 1) * n] = keys[h].astype(BF)
        v_ref[:, h * n:(h + 1) * n] = values[h].astype(BF)
        kt_ref[h * n:(h + 1) * n, :] = keys[h].T.astype(BF)
        vt_ref[h * n:(h + 1) * n, :] = values[h].T.astype(BF)

    @pl.when(i == final)
    def _():
        normed.wait()
        if line:
            merge.finish()
            merge.drain()
            project.drain()
            written.wait()


def front(x, gains, segments, parents, tree, masters, kv, group, line):
    length, d = x.shape
    n = LANES
    rows = lambda w: pl.BlockSpec((ROWS, w), lambda i: (i, 0))
    cols = pl.BlockSpec((kv * n, ROWS), lambda i: (0, i))
    out = lambda w, t: jax.ShapeDtypeStruct((length, w), t)
    raw_w = kv * (group + 1) * n
    freq = np.float32(THETA ** (-(np.arange(n) % (n // 2)) * 2.0 / n))[None]
    more_specs, more_shapes, scratch = [], [], []
    if line:
        shards = 2 * line
        project, merge, expand, shrink = (m.shape for m in masters)
        wp_shape = (project[0] * shards, project[1] * n)
        more_shapes = [jax.ShapeDtypeStruct(wp_shape, BF), jax.ShapeDtypeStruct((merge[0], merge[1] * shards), BF),
                       jax.ShapeDtypeStruct((expand[0], 2 * expand[2]), BF), jax.ShapeDtypeStruct(shrink, BF)]
        more_specs = [ANYWHERE, ANYWHERE, whole(more_shapes[2].shape), whole(more_shapes[3].shape)]
        scratch = [pltpu.VMEM(wp_shape, BF), pltpu.VMEM(merge, BF), *GATHER_SEMS(shards), *GATHER_SEMS(shards),
                   pltpu.SemaphoreType.DMA]
    table = whole((length, n))
    return pl.pallas_call(
        partial(front_kernel, kv, group, line),
        grid=(length // ROWS,),
        in_specs=[whole(x.shape), whole(gains.shape), whole(segments.shape), whole(parents.shape),
                  pl.BlockSpec(memory_space=pltpu.SMEM), whole(freq.shape), *[whole(m.shape) for m in masters]],
        out_specs=[ANYWHERE, rows(kv * group * n), rows(kv * n), rows(kv * n), cols, cols, rows(raw_w),
                   table, table, table, table, *more_specs],
        out_shape=[out(d, BF), out(kv * group * n, BF), out(kv * n, BF), out(kv * n, BF),
                   jax.ShapeDtypeStruct((kv * n, length), BF), jax.ShapeDtypeStruct((kv * n, length), BF),
                   out(raw_w, FP), out(n, BF), out(n, BF), out(n, FP), out(n, FP), *more_shapes],
        scratch_shapes=[*scratch, pltpu.VMEM((length, d), BF), pltpu.SemaphoreType.DMA],
        compiler_params=params(**({"collective_id": 0, "has_side_effects": True} if line else {})),
        name="front",
    )(x, gains, segments, parents, tree, freq, *masters)


def stacked(ref_block, h, group):
    n = LANES
    return jnp.concatenate(
        [ref_block[:, (h * group + g) * n:(h * group + g + 1) * n] for g in range(group)], axis=0)


def causal_tile(group, rows=ROWS, after=0):
    key_at = lax.broadcasted_iota(jnp.int32, (ROWS, rows * group), 0)
    query_at = lax.broadcasted_iota(jnp.int32, (ROWS, rows * group), 1) % rows
    return key_at <= query_at + after


def in_turn(i, first, steps, per, acts):
    for behind, act in acts:
        @pl.when(jnp.logical_and(i - first - behind >= 0, i - first - behind < steps))
        def _(behind=behind, act=act):
            for s in pair_of(i - first - behind, per):
                act(s)


def middle_kernel(kv, group, unit, line, per, steps, *refs):
    refs = list(refs)
    take = lambda count: [refs.pop(0) for _ in range(count)]
    q_ref, k_ref, vt_ref, tags_ref, bars_ref, wm_ref, gains_ref, x_all, dy_all = take(9)
    weights = take(2)
    ctx_out, lse_ref, base_ref, other_ref, gate_out, up_out, dh_ref, dhb_ref, dg_ref, gsh_out = take(10)
    acc_ref, sum_ref, x_ref, dy_ref, we_ref, ws_ref, copy_sems = take(7)
    h_ref, xn_ref, a_ref, dgu_ref, ctx_ref, gup_ref = take(6)
    h_held, h_near, h_far, h_sems, xn_sems = take(5)
    d_held, d_near, d_far, d_sems, stage, dh_sems = take(6)
    b_held, b_near, b_sems = take(3)
    place = Place(line)
    i = pl.program_id(0)
    n = LANES
    share, d = x_ref.shape
    units = ws_ref.shape[0]
    tile = 256
    attended = Exchange(place, per, h_held, h_near, h_far, h_ref, h_sems)
    norms = Spread(place, per, None, xn_ref, xn_sems)
    pulled_back = Exchange(place, per, d_held, d_near, d_far, dh_ref, d_sems)
    grads = Spread(place, per, stage, dhb_ref, dh_sems)
    branch = Pairs(place, per, b_held, b_near, b_sems, lambda s: s // per)
    own_share = x_all.at[pl.ds(pl.multiple_of(place.t * share, share), share), :]
    copies = [pltpu.make_async_copy(own_share, x_ref, copy_sems.at[0]),
              pltpu.make_async_copy(dy_all, dy_ref, copy_sems.at[1])]
    if line:
        gsh_ref = take(1)[0]
        shrink = Reduce(place, gsh_ref, column_cut(gsh_ref.shape[1] // (2 * line)), None, *take(3))
        gate_ref = take(1)[0]
        expand = Reduce(place, gate_ref, row_cut(gate_ref.shape[0] // (2 * line)), None, *take(3))
        cuts = (row_cut(weights[0].shape[0]), column_cut(weights[1].shape[1]))
        first, second = [Gather(place, weights[w], (we_ref, ws_ref)[w], cuts[w], *take(2)) for w in range(2)]
    else:
        gsh_ref, gate_ref = gsh_out, gate_out
        copies += [pltpu.make_async_copy(weights[0], we_ref, copy_sems.at[2]),
                   pltpu.make_async_copy(weights[1], ws_ref, copy_sems.at[3])]
    written = [pltpu.make_async_copy(ctx_ref, ctx_out, copy_sems.at[4]),
               pltpu.make_async_copy(gup_ref, up_out, copy_sems.at[5])]
    rows_of = lambda s: pl.ds(pl.multiple_of(s * SUB, SUB), SUB)

    def at_step(step, *acts):
        @pl.when(i == step)
        def _():
            for act in acts:
                act()

    @pl.when(i == 0)
    def _():
        place.greet(True, bool(line))
        if line:
            first.start()
        for copy in copies:
            copy.start()
        dg_ref[...] = jnp.zeros_like(dg_ref)


    def block(s):
        here = rows_of(s)
        bars = jnp.concatenate([bars_ref[here, :]] * group, axis=0)
        q = q_ref[here, :]
        wide = [jnp.concatenate([stacked(q, h, group), bars], axis=1) for h in range(kv)]
        acc_ref[...] = jnp.zeros_like(acc_ref)
        sum_ref[...] = jnp.zeros_like(sum_ref)

        def chunk(j, diagonal):
            at = pl.ds(pl.multiple_of(j * ROWS, ROWS), ROWS)
            tags = tags_ref[at, :]
            for h in range(kv):
                keys = jnp.concatenate([k_ref[at, h * n:(h + 1) * n], tags], axis=1)
                scores = dot(keys, wide[h], 1, 1)
                e = jnp.exp2(scores * unit)
                if diagonal:
                    e = jnp.where(causal_tile(group, SUB, (s % 2) * SUB), e, 0.0)
                sum_ref[h] += fold_rows(e)
                acc_ref[h] += dot(vt_ref[h * n:(h + 1) * n, at], e.astype(BF))

        lax.fori_loop(0, s // 2, lambda j, c: (chunk(j, False), c)[1], 0)
        chunk(s // 2, True)
        parts = []
        for h in range(kv):
            sums = jnp.sum(sum_ref[h], axis=0, keepdims=True)
            lse_ref[s, h:h + 1, :] = jnp.log2(sums)
            ctx = (acc_ref[h] / sums).T
            parts += [ctx[g * SUB:(g + 1) * SUB] for g in range(group)]
        ctx_ref[here, :] = jnp.concatenate(parts, axis=1).astype(BF)

    def put_pair(pairs, blocks, part):
        for u, s in enumerate(blocks):
            pairs.put_next(s, part[u * SUB:(u + 1) * SUB])

    @pl.when(i < steps)
    def _():
        blocks = pair_of(i, per)
        for s in blocks:
            block(s)
        ctx = jnp.concatenate([ctx_ref[rows_of(s), :] for s in blocks], axis=0)
        put_pair(attended, blocks, dot(ctx, wm_ref[...]).astype(BF))

    def hidden_rows(s, at, summed):
        hidden = x_ref[at, :].astype(FP) + summed
        h_ref[at, :] = hidden
        xn_ref[rows_of(s), :] = (hidden * inverse_rms(hidden) * gains_ref[:, d:2 * d]).astype(BF)
        norms.send(s)

    at_step(1, copies[0].wait)
    at_step(steps, written[0].start)
    in_turn(i, 0, steps, per, ((1, attended.add_chip), (3, lambda s: attended.take(s, hidden_rows)), (5, norms.pass_on)))
    swiglu, feed = steps + 3, 2 * steps + 3
    if line:
        at_step(1, lambda: first.hop(1))
        at_step(3, lambda: first.hop(2))
        at_step(5, lambda: first.hop(3), second.start)
        at_step(7, lambda: second.hop(1))
        at_step(8, lambda: second.hop(2))
        at_step(9, lambda: second.hop(3), first.finish)
        at_step(feed, second.finish)
    else:
        at_step(swiglu, copies[2].wait, copies[3].wait)


    def gathered(ref, blocks):
        return jnp.concatenate([ref[rows_of(s), :] for s in blocks], axis=0)

    def keep(ref, blocks, values):
        for u, s in enumerate(blocks):
            ref[rows_of(s), :] = values[u * SUB:(u + 1) * SUB]

    def tiles(grad_ref, left_ref, right_ref, start, count, after):
        def one(t, carry):
            cut = pl.ds(pl.multiple_of(t * tile, tile), tile)
            there = pl.ds(pl.multiple_of((t + after) * tile, tile), tile)
            grad_ref[:, cut] = dot(left_ref[...], right_ref[:, there], 0, 0).astype(grad_ref.dtype)
            return carry

        lax.fori_loop(start, start + count, one, 0)

    @pl.when(jnp.logical_and(i >= swiglu, i < feed))
    def _():
        blocks = pair_of(i - swiglu, per)
        for s in blocks:
            norms.ready(s)
        gu = dot(gathered(xn_ref, blocks), we_ref[...])
        gate, up = gu[:, :units], gu[:, units:]
        keep(a_ref, blocks, (gate / (1.0 + jnp.exp(-gate)) * up).astype(BF))
        keep(dgu_ref, blocks, gu.astype(BF))

    at_step(feed - 1, copies[1].wait, lambda: tiles(gsh_ref, a_ref, dy_ref, 0, gsh_ref.shape[1] // tile, 0))
    if line:
        at_step(feed, shrink.start)

    @pl.when(jnp.logical_and(i >= feed, i < feed + steps))
    def _():
        blocks = pair_of(i - feed, per)
        gu = gathered(dgu_ref, blocks).astype(FP)
        gate, up = gu[:, :units], gu[:, units:]
        sig = 1.0 / (1.0 + jnp.exp(-gate))
        da = dot(gathered(dy_ref, blocks), ws_ref[...], 1, 1)
        dgu = jnp.concatenate([da * up * (sig * (1.0 + gate * (1.0 - sig))), da * (gate * sig)], axis=1).astype(BF)
        keep(dgu_ref, blocks, dgu)
        put_pair(pulled_back, blocks, dot(dgu, we_ref[...], 1, 1).astype(BF))

    def grad_rows(s, at, summed):
        pulled, gain_grad = rms_pull(h_ref[at, :], gains_ref[:, d:2 * d], summed)
        dh = dy_ref[rows_of(s), :].astype(FP) + pulled
        dh_ref[at, :] = dh
        dg_ref[...] += fold_rows(gain_grad)
        stage[s % per] = dh.astype(BF)
        grads.send(s)

    def chip_rows(mine, k, summed):
        at = rows_of(k)

        @pl.when(mine)
        def _():
            base_ref[at, :] = h_ref[at, :] + summed

        @pl.when(jnp.logical_not(mine))
        def _():
            other_ref[k] = summed.astype(BF)

    in_turn(i, feed, steps, per, ((1, pulled_back.add_chip), (3, lambda s: pulled_back.take(s, grad_rows)),
                                  (5, grads.pass_on)))

    @pl.when(jnp.logical_and(i >= feed + 3, i < feed + 3 + steps))
    def _():
        blocks = pair_of(i - feed - 3, per)
        put_pair(branch, blocks, dot(gathered(a_ref, blocks), ws_ref[...]).astype(BF))

    in_turn(i, feed, steps, per, ((4, lambda s: branch.add(s, chip_rows)),))
    if line:
        for k in range(1, line):
            at_step(feed + k, lambda k=k: shrink.step(k))
    half = units // tile
    at_step(feed + steps, lambda: tiles(gate_ref, xn_ref, dgu_ref, 0, half, 0))
    if line:
        at_step(feed + steps, expand.start)
        for k in range(1, line):
            at_step(feed + steps + k, lambda k=k: expand.step(k))
    at_step(feed + steps + 1, lambda: tiles(gup_ref, xn_ref, dgu_ref, 0, half, half), written[1].start)

    @pl.when(i == feed + steps + 4)
    def _():
        attended.drain()
        pulled_back.drain()
        norms.drain()
        grads.drain()
        for t in range(4):
            branch.sent(t * per + per - 1)
        lax.fori_loop(0, 4 * per, lambda s, c: (grads.ready(s), c)[1], 0)
        for copy in written:
            copy.wait()
        if line:
            shrink.finish(write_to(gsh_out))
            shrink.drain()
            expand.finish(write_to(gate_out))
            expand.drain()
            first.drain()
            second.drain()


def middle(q, k, vt, tags, bars, wm, x, dy, gains, weights, kv, group, unit, line):
    length = q.shape[0]
    n = LANES
    d = wm.shape[1]
    share = (length // 4, d)
    per = share[0] // SUB
    steps = 2 * per
    we, ws = (w.shape for w in weights)
    shards = 2 * line
    shrink = jax.ShapeDtypeStruct(ws, BF)
    gate = jax.ShapeDtypeStruct((we[0], we[1] // 2), BF)
    more = []
    if line:
        shrink = jax.ShapeDtypeStruct(ws, FP)
        gate = jax.ShapeDtypeStruct(gate.shape, FP)
        we, ws = (we[0] * shards, we[1]), (ws[0], ws[1] * shards)
        more = [pltpu.VMEM(ws, BF), *reduce_scratch(line, shrink.shape), pltpu.VMEM((we[0], we[1] // 2), BF),
                *reduce_scratch(line, gate.shape), *GATHER_SEMS(shards), *GATHER_SEMS(shards)]
    units = ws[0]
    results = [jax.ShapeDtypeStruct(q.shape, BF), jax.ShapeDtypeStruct((length // SUB, 8, SUB * group), FP),
               jax.ShapeDtypeStruct(share, FP), jax.ShapeDtypeStruct((per, SUB, d), BF), gate,
               jax.ShapeDtypeStruct((we[0], units), BF), jax.ShapeDtypeStruct(share, FP),
               jax.ShapeDtypeStruct((length, d), BF), jax.ShapeDtypeStruct((8, d), FP),
               shrink]
    out_specs = [whole(r.shape) for r in results]
    for at in (0, 5, 7):
        out_specs[at] = ANYWHERE
    held = [q, k, vt, tags, bars, wm, gains]
    return pl.pallas_call(
        partial(middle_kernel, kv, group, unit, line, per, steps),
        grid=(3 * steps + 8,),
        in_specs=[whole(a.shape) for a in held] + [ANYWHERE] * 4,
        out_specs=out_specs,
        out_shape=results,
        scratch_shapes=[pltpu.VMEM((kv, n, SUB * group), FP), pltpu.VMEM((kv, 8, SUB * group), FP),
                        pltpu.VMEM(share, BF), pltpu.VMEM((length, d), BF), pltpu.VMEM(we, BF), pltpu.VMEM(ws, BF),
                        pltpu.SemaphoreType.DMA((6,)),
                        pltpu.VMEM(share, FP), pltpu.VMEM((length, d), BF), pltpu.VMEM((length, units), BF),
                        pltpu.VMEM((length, 2 * units), BF), pltpu.VMEM(q.shape, BF), pltpu.VMEM((we[0], units), BF),
                        *pairs_scratch(per, d, True), pltpu.SemaphoreType.DMA((3 + 2 * PARTS, 4 * per)),
                        *pairs_scratch(per, d, True), pltpu.VMEM((per, SUB, d), BF),
                        pltpu.SemaphoreType.DMA((3 + 2 * PARTS, 4 * per)),
                        *pairs_scratch(per, d, False), *more],
        compiler_params=params(collective_id=1, has_side_effects=True),
        name="middle",
    )(*held, x, dy, *weights)


def back_kernel(kv, group, unit, scale, blocks, per, line, *refs):
    refs = list(refs)
    take = lambda count: [refs.pop(0) for _ in range(count)]
    q_ref, k_ref, v_ref, kt_ref, tags_ref, bars_ref, lse_ref, ctx_block, dh_block, wm_ref = take(10)
    raw_ref, cos_ref, sin_ref, all_gains, base_ref, dg2_ref, other_ref = take(7)
    x_all, dh_all = take(2)
    late_from = take(4)
    grads = take(2) if line else []
    in_ref, out_ref, gains_out = take(3)
    sums = take(3) if line else []
    weight_grads = [] if line else take(2)
    late_to = take(4)
    wp_ref, ctx_ref, dh_ref, xn_ref = late_to
    late_sem = take(1)[0]
    late = [pltpu.make_async_copy(a, b, late_sem.at[w]) for w, (a, b) in enumerate(zip(late_from, late_to))]
    dk_ref, dv_ref, dq_ref, dqkv_ref = take(4)
    b_far, b_sems, x_held, x_near, x_sems = take(5)
    mine_ref, far_ref, x_far, f_sems, x_ref, dh_own, own_sems, heads_ref, fold_ref = take(9)
    place = Place(line)
    i = pl.program_id(0)
    b = blocks - 1 - i
    n = LANES
    pairs = Pairs(place, per, x_held, x_near, x_sems, lambda s: s % x_held.shape[0])
    subs = ROWS // SUB
    share, d = x_ref.shape
    gq, gk = all_gains[:, 2 * d:2 * d + n], all_gains[:, 2 * d + n:]
    tile = 256
    tensors = lax.axis_size("tensor")
    mates = [(place.dp, (place.t + step) % tensors) for step in range(1, tensors)]
    peers = []
    own_rows = pl.ds(pl.multiple_of(place.t * share, share), share)
    own_copies = [pltpu.make_async_copy(x_all.at[own_rows, :], x_ref, own_sems.at[0]),
                  pltpu.make_async_copy(dh_all, dh_own, own_sems.at[1])]
    if line:
        shards = 2 * line
        gm_ref, gp_ref = take(2)
        expand = Reduce(place, grads[1], row_cut(grads[1].shape[0] // shards), *take(4))
        merge = Reduce(place, gm_ref, column_cut(gm_ref.shape[1] // shards), None, *take(3))
        project = Reduce(place, gp_ref, row_cut(gp_ref.shape[0] // shards), None, *take(3))
        shown, over, g_sems = take(3)
        peers = [((place.dp + step) % shards, place.t) for step in range(1, shards)]
    else:
        gp_ref, gm_ref = weight_grads

    def tiles(grad_ref, left_ref, right_ref):
        def one(t, carry):
            cut = pl.ds(pl.multiple_of(t * tile, tile), tile)
            grad_ref[:, cut] = dot(left_ref[...], right_ref[:, cut], 0, 0).astype(grad_ref.dtype)
            return carry

        lax.fori_loop(0, grad_ref.shape[1] // tile, one, 0)

    def write_up(values):
        sums[0][:, 0, :] = grads[0][...]
        sums[0][:, 1, :] = values

    def project_rows(t):
        cut = pl.ds(pl.multiple_of(t * tile, tile), tile)
        gp_ref[cut, :] = dot(xn_ref[:, cut], dqkv_ref[...], 0, 0).astype(BF)

    def chip(k):
        return send_split(far_ref.at[k], x_far.at[k], lambda part: (f_sems.at[2 * part, k], f_sems.at[2 * part + 1, k]),
                          place.chip)

    def branch(k):
        return send_split(other_ref.at[k], b_far.at[k], lambda part: (b_sems.at[2 * part, k], b_sems.at[2 * part + 1, k]),
                          place.chip)

    @pl.when(i == 0)
    def _():
        barrier = pltpu.get_barrier_semaphore()
        for device in mates + peers:
            pl.semaphore_signal(barrier, inc=1, device_id=device, device_id_type=MESH)
        for copy in late:
            copy.start()
        pl.semaphore_wait(barrier, len(mates + peers))
        if line:
            expand.start()
        for k in range(per):
            branch(k).start()
        dk_ref[...] = jnp.zeros_like(dk_ref)
        dv_ref[...] = jnp.zeros_like(dv_ref)
        heads_ref[...] = jnp.zeros_like(heads_ref)

    @pl.when(i < blocks)
    def _():
        here = pl.ds(pl.multiple_of(b * ROWS, ROWS), ROWS)
        dctx = dot(dh_block[...], wm_ref[...], 1, 1).astype(BF)
        ctx, q = ctx_block[...], q_ref[...]
        bars = jnp.concatenate([bars_ref[...]] * group, axis=0)
        wide, queries, outward, centres, lses = [], [], [], [], []
        for h in range(kv):
            queries.append(stacked(q, h, group))
            wide.append(jnp.concatenate([queries[h], bars], axis=1))
            outward.append(stacked(dctx, h, group))
            both = outward[h].astype(FP) * stacked(ctx, h, group).astype(FP)
            centres.append(jnp.sum(both.T, axis=0, keepdims=True))
            lses.append(jnp.concatenate([lse_ref[u, h:h + 1, g * SUB:(g + 1) * SUB]
                                         for g in range(group) for u in range(ROWS // SUB)], axis=1))
        dq_ref[...] = jnp.zeros_like(dq_ref)

        def chunk(j, diagonal):
            at = pl.ds(pl.multiple_of(j * ROWS, ROWS), ROWS)
            tags = tags_ref[at, :]
            for h in range(kv):
                cut = slice(h * n, (h + 1) * n)
                keys = jnp.concatenate([k_ref[at, cut], tags], axis=1)
                p = jnp.exp2(dot(keys, wide[h], 1, 1) * unit - lses[h])
                if diagonal:
                    p = jnp.where(causal_tile(group), p, 0.0)
                dp = dot(v_ref[at, cut], outward[h], 1, 1)
                ds = (p * (dp - centres[h])).astype(BF)
                dv_ref[at, cut] += dot(p.astype(BF), outward[h])
                dk_ref[at, cut] += dot(ds, queries[h])
                dq_ref[h] += dot(kt_ref[cut, at], ds)

        lax.fori_loop(0, b, lambda j, c: (chunk(j, False), c)[1], 0)
        chunk(b, True)

        cosines, sines = cos_ref[...], sin_ref[...]
        pieces = []
        for h in range(kv):
            dq = dq_ref[h].T
            for c in range(group + 1):
                if c < group:
                    grad, gain, row = dq[c * ROWS:(c + 1) * ROWS] * scale, gq, 0
                else:
                    grad, gain, row = dk_ref[here, h * n:(h + 1) * n] * scale, gk, 1
                grad = grad * cosines - pltpu.roll(grad, n // 2, 1) * sines
                at = (h * (group + 1) + c) * n
                piece, gain_grad = rms_pull(raw_ref[:, at:at + n], gain, grad)
                heads_ref[row] += fold_rows(gain_grad)
                pieces.append(piece)
            pieces.append(dv_ref[here, h * n:(h + 1) * n])
        dqkv = jnp.concatenate(pieces, axis=1).astype(BF)
        dqkv_ref[here, :] = dqkv
        pl.when(i == 0)(late[0].wait)
        part = dot(dqkv, wp_ref[...], 1, 1).astype(BF)
        for u in range(subs):
            s = subs * b + u
            pairs.put(s, part[u * SUB:(u + 1) * SUB], (i >= 2, s + 2 * subs))

    def chip_rows(mine, k, summed):
        @pl.when(mine)
        def _():
            mine_ref[pl.ds(pl.multiple_of(k * SUB, SUB), SUB), :] = summed

        @pl.when(jnp.logical_not(mine))
        def _():
            far_ref[k] = summed.astype(BF)
            chip(k).start()

    @pl.when(i >= 1)
    def _():
        for u in range(subs):
            pairs.add(subs * (b + 1) + u, chip_rows)

    @pl.when(i == 3)
    def _():
        for k in range(per):
            branch(k).wait()
            at = slice(k * SUB, (k + 1) * SUB)
            out_ref[at, :] = (base_ref[at, :] + b_far[k].astype(FP)).astype(BF)
        for copy in own_copies:
            copy.start()

    @pl.when(i == 1)
    def _():
        late[1].wait()
        late[2].wait()
        tiles(gm_ref, ctx_ref, dh_ref)

    if line:
        for step, act in enumerate((lambda: expand.step(1), lambda: expand.step(2), lambda: expand.step(3), merge.start,
                                    lambda: merge.step(1), lambda: merge.step(2))):
            pl.when(i == step)(act)

    def input_rows(k):
        at = slice(k * SUB, (k + 1) * SUB)
        chip(k).wait()
        summed = mine_ref[at, :] + x_far[k].astype(FP)
        pulled, gain_grad = rms_pull(x_ref[at, :].astype(FP), all_gains[:, :d], summed)
        in_ref[at, :] = (dh_own[at, :] + pulled).astype(BF)
        fold_ref[...] += fold_rows(gain_grad)

    def folded(ref):
        pieces = [fold_ref[...], dg2_ref[...], heads_ref[0], heads_ref[1]]
        row = jnp.sum(jnp.concatenate(pieces, axis=1), axis=0, keepdims=True)
        count = row.shape[1] // n
        for j in range(count):
            ref[j:j + 1, :] = row[:, j * n:(j + 1) * n]
        ref[count:, :] = jnp.zeros((ref.shape[0] - count, n), FP)

    def show(buffer, me, devices, first):
        copies = [send(buffer.at[me], buffer.at[me], g_sems.at[0, first + step], g_sems.at[1, first + step], device)
                  for step, device in enumerate(devices, 1)]
        for copy in copies:
            copy.start()
        return copies

    def added(buffer, me, devices, first):
        count = len(devices) + 1
        for step in range(1, count):
            who = (me - step + count) % count
            send(buffer.at[who], buffer.at[who], g_sems.at[0, first + step], g_sems.at[1, first + step],
                 place.sibling).wait_recv()
        total = buffer[0]
        for who in range(1, count):
            total = total + buffer[who]
        return total

    @pl.when(i == blocks)
    def _():
        fold_ref[...] = jnp.zeros_like(fold_ref)
        late[3].wait()
        for copy in own_copies:
            copy.wait()
        if not line:
            tiles(gp_ref, xn_ref, dqkv_ref)
            for k in range(per):
                input_rows(k)
            folded(gains_out)
        else:
            project_rows(project.turn(0))
            project.start()
            for q in range(1, line):
                project_rows(project.turn(q))
            merge.step(3)
            expand.finish(write_up)
            project.step(1)
            merge.finish(write_to(sums[1]))
            project.step(2)
            for k in range(per):
                input_rows(k)
            folded(shown.at[place.t])
            copies = show(shown, place.t, mates, 0)
            project.step(3)
            over[place.dp] = added(shown, place.t, mates, 0)
            copies += show(over, place.dp, peers, tensors)
            project.finish(write_to(sums[2]))
            gains_out[...] = added(over, place.dp, peers, tensors)
            for copy in copies:
                copy.wait_send()
            for r in (expand, merge, project):
                r.drain()
        for s in range(2 * subs):
            pairs.sent(s)


def back(q, k, v, kt, tags, bars, lse, ctx, dh, wm, wp, raw, cosines, sines, gains, xn, base, dg2, other, x, dh_own,
         grads, kv, group, unit, scale, line):
    length = q.shape[0]
    n = LANES
    d = wm.shape[1]
    blocks = length // ROWS
    per = other.shape[0]
    share = base.shape
    block_of = lambda i: jnp.maximum(blocks - 1 - i, 0)
    rows = lambda w: pl.BlockSpec((ROWS, w), lambda i: (block_of(i), 0))
    late = [wp, ctx, dh, xn]
    gain_rows = (-(-(gains.shape[1] // n) // 8) * 8, n)
    scratch = [*[pltpu.VMEM(a.shape, BF) for a in late], pltpu.SemaphoreType.DMA((4,)),
               pltpu.VMEM((length, kv * n), FP), pltpu.VMEM((length, kv * n), FP),
               pltpu.VMEM((kv, n, ROWS * group), FP), pltpu.VMEM((length, wp.shape[1]), BF),
               pltpu.VMEM((per, SUB, d), BF), pltpu.SemaphoreType.DMA((2 * PARTS, per)),
               pltpu.VMEM((2 * ROWS // SUB, SUB, d), BF), pltpu.VMEM((2 * per, SUB, d), BF),
               pltpu.SemaphoreType.DMA((2, 4 * per)),
               pltpu.VMEM(share, FP), pltpu.VMEM((per, SUB, d), BF), pltpu.VMEM((per, SUB, d), BF),
               pltpu.SemaphoreType.DMA((2 * PARTS, per)), pltpu.VMEM(share, BF), pltpu.VMEM(share, FP),
               pltpu.SemaphoreType.DMA((2,)), pltpu.VMEM((2, 8, n), FP), pltpu.VMEM((8, d), FP)]
    results = [jax.ShapeDtypeStruct(share, BF), jax.ShapeDtypeStruct(share, BF), jax.ShapeDtypeStruct(gain_rows, FP)]
    if line:
        shards = 2 * line
        own = [grads[0].shape, (wm.shape[0], wm.shape[1] // shards),
               (wp.shape[0] // shards, wp.shape[1])]
        views = ((own[0][0], 2, own[0][1]), own[1], (own[2][0], own[2][1] // n, n))
        results += [jax.ShapeDtypeStruct(s, FP) for s in views]
        scratch += [pltpu.VMEM(wm.shape, BF), pltpu.VMEM(wp.shape, BF)]
        for w, s in enumerate(own):
            scratch += reduce_scratch(line, s, w == 0)
        scratch += [pltpu.VMEM((4, *gain_rows), FP), pltpu.VMEM((shards, *gain_rows), FP),
                    pltpu.SemaphoreType.DMA((2, 4 + shards))]
    else:
        results += [jax.ShapeDtypeStruct(wp.shape, BF), jax.ShapeDtypeStruct(wm.shape, BF)]
    args = [q, k, v, kt, tags, bars, lse, ctx, dh, wm, raw, cosines, sines, gains, base, dg2]
    more = [other, x, dh_own, *late, *grads]
    specs = [whole(a.shape) for a in args] + [ANYWHERE] * len(more)
    if line:
        specs[-2] = whole(grads[0].shape)
    for at in (0, 5, 7, 8, 10, 11, 12):
        specs[at] = rows(args[at].shape[1])
    specs[6] = pl.BlockSpec((ROWS // SUB, 8, SUB * group), lambda i: (block_of(i), 0, 0))
    return pl.pallas_call(
        partial(back_kernel, kv, group, unit, scale, blocks, per, line),
        grid=(blocks + 1,),
        in_specs=specs,
        out_specs=[whole(r.shape) for r in results],
        out_shape=results,
        scratch_shapes=scratch,
        compiler_params=params(collective_id=3, has_side_effects=True),
        name="back",
    )(*args, *more)


def adamw_step(weight, moment_one, moment_two, gradient, step_rate, decay):
    mean_next = BETA_ONE * moment_one + (1.0 - BETA_ONE) * gradient
    square_next = BETA_TWO * moment_two + (1.0 - BETA_TWO) * gradient * gradient
    mean_hat = mean_next / (1.0 - BETA_ONE**STEP)
    square_hat = square_next / (1.0 - BETA_TWO**STEP)
    weight_next = weight - step_rate * (mean_hat / (jnp.sqrt(square_hat) + EPS_ADAM) + decay * weight)
    return weight_next, mean_next, square_next


def shards(
    tokens, cotangent, parents, token_segment, tree_id,
    projection_weight, projection_first_moment, projection_second_moment,
    merge_master, merge_mean, merge_square,
    expand_master, expand_mean, expand_square,
    shrink_master, shrink_mean, shrink_square,
    gain_master, gain_mean, gain_square,
):
    x = tokens[0]
    dy = cotangent[0]
    length, d = x.shape
    d_own, kv, per, n = projection_weight.shape
    group = per - 2
    units = expand_master.shape[2]
    scale = n ** (-0.5)
    unit = scale * math.log2(math.e)
    line = 4 if lax.axis_size("dp") == 8 and d_own % LANES == 0 else 0
    if line:
        masters = (projection_weight.reshape(d_own, kv * per, n), merge_master, expand_master, shrink_master)
    else:
        wp, we = (lax.all_gather(w.astype(BF).reshape(d_own, -1), "dp", axis=0, tiled=True)
                  for w in (projection_weight, expand_master))
        wm, ws = (lax.all_gather(w.astype(BF), "dp", axis=1, tiled=True) for w in (merge_master, shrink_master))
        masters = (wp,)

    gains = gain_master[None]
    fronts = front(x, gains, token_segment, parents, tree_id, masters, kv, group, line)
    xn1, q, k, v, kt, vt, raw, tags, bars, cosines, sines = fronts[:11]
    if line:
        wp, wm, *low = fronts[11:]
    else:
        low = (we, ws)
    ctx, lse, base, other, gate_sum, up_grad, dh, dhb, dg2, shrink_sum = middle(
        q, k, vt, tags, bars, wm, x, dy, gains, low, kv, group, unit, line)
    backs = back(q, k, v, kt, tags, bars, lse, ctx, dhb, wm, wp, raw, cosines, sines, gains, xn1,
                 base, dg2, other, x, dh, (gate_sum, up_grad) if line else (), kv, group, unit, scale, line)
    input_grad, output, gain_rows = backs[:3]
    if line:
        expand_sum, merge_sum, project_sum = backs[3:]
    else:
        gain_rows = lax.psum(gain_rows, ("dp", "tensor"))
        project_sum, expand_sum = (
            lax.psum_scatter(g, "dp", scatter_dimension=0, tiled=True) for g in (backs[3], jnp.concatenate([gate_sum, up_grad], axis=1)))
        merge_sum, shrink_sum = (
            lax.psum_scatter(g, "dp", scatter_dimension=1, tiled=True) for g in (backs[4], shrink_sum))
    output, input_grad = output[None], input_grad[None]
    gain_grad = gain_rows.reshape(-1)[:gain_master.shape[0]]

    outs = [output, input_grad]
    for weight, mean, square, grad, rate in (
        (projection_weight, projection_first_moment, projection_second_moment, project_sum, RATE_PROJECT),
        (merge_master, merge_mean, merge_square, merge_sum, RATE_MERGE),
        (expand_master, expand_mean, expand_square, expand_sum, RATE_EXPAND),
        (shrink_master, shrink_mean, shrink_square, shrink_sum, RATE_SHRINK),
    ):
        grad = grad.astype(FP).reshape(weight.shape)
        after, mean_next, square_next = adamw_step(weight, mean, square, grad, rate, DECAY)
        outs += [after, mean_next, square_next, after.astype(BF)]
    gain_next, gain_mean_next, gain_square_next = adamw_step(
        gain_master, gain_mean, gain_square, gain_grad, RATE_GAIN, 0.0)
    return (*outs, gain_mean_next, gain_square_next, gain_next)


def solution(mesh):
    tokens = P("dp", None, None)
    project = P("dp", "tensor", None, None)
    columns = P("tensor", "dp")
    expand = P("dp", None, "tensor")
    shared = P("dp", "tensor", None)
    return jax.shard_map(
        shards,
        mesh=mesh,
        in_specs=(tokens, tokens, P(), P("dp", None), P("dp"), *[project] * 3, *[columns] * 3, *[expand] * 3,
                  *[columns] * 3, P(), P(), P()),
        out_specs=(shared, shared, *[project] * 4, *[columns] * 4, *[expand] * 4, *[columns] * 4, P(), P(), P()),
        check_vma=False,
    )
```

```python
import math
from functools import partial

import jax
import jax.numpy as jnp
import numpy as np
from jax import lax
from jax.experimental import pallas as pl
from jax.experimental.pallas import tpu as pltpu
from jax.sharding import PartitionSpec as P

STEP = 5
EPS_NORM = 1e-06
THETA = 1000000.0
BETA_ONE = 0.5
BETA_TWO = 0.5
EPS_ADAM = 1e-08
DECAY = 0.1
RATE_PROJECT = 0.05
RATE_MERGE = 0.3
RATE_EXPAND = 0.05
RATE_SHRINK = 0.03
RATE_GAIN = 0.3

BF = jnp.bfloat16
FP = jnp.float32
ROWS = 256
LANES = 128
SUB = 128
PARTS = 1
MESH = pl.DeviceIdType.MESH
BLOCKED = -1e30
VMEM_LIMIT = 56 * 2**20


def params(**more):
    return pltpu.CompilerParams(vmem_limit_bytes=VMEM_LIMIT, **more)


def dot(a, b, ca=1, cb=0):
    return lax.dot_general(a, b, (((ca,), (cb,)), ((), ())), preferred_element_type=FP)


def inverse_rms(values):
    return lax.rsqrt(jnp.mean(values * values, axis=-1, keepdims=True) + EPS_NORM)


def rms_pull(values, scales, grad):
    r = inverse_rms(values)
    scaled = grad * scales
    mean = jnp.mean(values * scaled, axis=-1, keepdims=True)
    return r * scaled - values * (r * r * r * mean), grad * values * r


def fold_rows(values):
    n, w = values.shape
    return jnp.sum(values.reshape(n // 8, 8, w), axis=0)


class Place:
    def __init__(self, line):
        self.line = line
        self.dp, self.t = lax.axis_index("dp"), lax.axis_index("tensor")
        self.z, self.y = self.dp // 2, self.dp % 2
        self.x, self.c = self.t // 2, self.t % 2
        self.has_up, self.has_down = self.z < line - 1, self.z > 0
        self.up, self.down = (self.dp + 2, self.t), (self.dp - 2, self.t)
        self.across = (self.dp + 1 - 2 * self.y, self.t)
        self.sibling = (self.dp, self.t + 1 - 2 * self.c)
        self.chip = (self.dp, (1 - self.x) * 2 + self.c)

    def greet(self, tensor, line, meanwhile=None):
        barrier = pltpu.get_barrier_semaphore()

        def signal(device):
            pl.semaphore_signal(barrier, inc=1, device_id=device, device_id_type=MESH)

        if tensor:
            signal(self.sibling)
            signal(self.chip)
        if line:
            signal(self.across)
            pl.when(self.has_up)(lambda: signal(self.up))
            pl.when(self.has_down)(lambda: signal(self.down))
        peers = (2 if tensor else 0) + (1 if line else 0)
        if line:
            peers = peers + jnp.where(self.has_up, 1, 0) + jnp.where(self.has_down, 1, 0)
        if meanwhile is not None:
            meanwhile()
        pl.semaphore_wait(barrier, peers)


def send(src, dst, sent, arrived, device):
    return pltpu.make_async_remote_copy(
        src_ref=src, dst_ref=dst, send_sem=sent, recv_sem=arrived, device_id=device, device_id_type=MESH)


class Several:
    def __init__(self, copies):
        self.copies = copies

    def start(self):
        for copy in self.copies:
            copy.start()

    def wait_send(self):
        for copy in self.copies:
            copy.wait_send()

    def wait_recv(self):
        for copy in self.copies:
            copy.wait_recv()

    def wait(self):
        self.wait_send()
        self.wait_recv()


def send_split(src, dst, sems, device):
    size = SUB // PARTS
    rows = [pl.ds(part * size, size) for part in range(PARTS)]
    return Several([send(src.at[rows[part], :], dst.at[rows[part], :], *sems(part), device) for part in range(PARTS)])


class Cut:
    def __init__(self, shape, axis):
        self.shape, self.axis = shape, axis
        rows = shape[0]
        self.rows = rows
        self.early_rows = rows // 8 if axis == 0 else max(e for e in range(16, rows // 6 + 1, 16))

    def part(self, j, first, count):
        if self.axis == 0:
            return pl.ds(pl.multiple_of(j * self.rows + first, math.gcd(self.rows, first or self.rows)), count), slice(None)
        width = self.shape[1]
        return pl.ds(first, count), pl.ds(pl.multiple_of(j * width, width), width)

    def whole(self, j):
        return self.part(j, 0, self.rows)

    def early(self, j):
        return self.part(j, 0, self.early_rows)

    def rest(self, j):
        return self.part(j, self.early_rows, self.rows - self.early_rows)


class Gather:
    def __init__(self, place, own, full, cut, sems, local):
        self.place, self.own, self.full, self.cut, self.sems, self.local = place, own, full, cut, sems, local

    def device(self, kind):
        return (self.place.up, self.place.down, self.place.across)[kind]

    def main(self, kind, j, src=None):
        piece = self.full.at[self.cut.whole(j)]
        return send(piece if src is None else src, piece, self.sems.at[kind, j], self.sems.at[3, j], self.device(kind))

    def across(self, j):
        piece = self.full.at[self.cut.rest(j)]
        return send(piece, piece, self.sems.at[2, j], self.sems.at[3, j], self.place.across)

    def side(self, kind, j):
        piece = self.full.at[self.cut.early(j)]
        return send(piece, piece, self.sems.at[4 + kind, j], self.sems.at[6, j], self.device(kind))

    def kept(self):
        return pltpu.make_async_copy(self.own, self.full.at[self.cut.whole(self.place.dp)], self.local)

    def first_sends(self):
        p = self.place
        for kind, there in ((2, None), (0, p.has_up), (1, p.has_down)):
            yield there, self.main(kind, p.dp, self.own)

    def start(self):
        for there, copy in self.first_sends():
            copy.start() if there is None else pl.when(there)(copy.start)
        if self.own is not None:
            self.kept().start()

    def arrivals(self, k):
        p = self.place
        return ((0, p.z >= k, p.z - k, p.has_up), (1, p.z + k < p.line, p.z + k, p.has_down))

    def hop(self, k):
        for kind, here, zz, further in self.arrivals(k):
            @pl.when(here)
            def _(kind=kind, j=zz * 2 + self.place.y, further=further):
                self.main(kind, j).wait_recv()
                pl.when(further)(lambda: self.main(kind, j).start())
                self.across(j).start()
        if k == 1:
            self.turn()
        else:
            self.sides(k - 1)

    def turn(self):
        p = self.place
        j = p.z * 2 + 1 - p.y
        self.main(2, j).wait_recv()
        pl.when(p.has_up)(lambda: self.side(0, j).start())
        pl.when(p.has_down)(lambda: self.side(1, j).start())

    def sides(self, k):
        for kind, here, zz, further in self.arrivals(k):
            @pl.when(here)
            def _(kind=kind, j=zz * 2 + 1 - self.place.y, further=further):
                self.side(kind, j).wait_recv()
                pl.when(further)(lambda: self.side(kind, j).start())

    def finish(self):
        p = self.place
        if self.own is not None:
            self.kept().wait()
        self.sides(p.line - 1)
        for zz in range(p.line):
            pl.when(zz != p.z)(lambda zz=zz: self.across(zz * 2 + 1 - p.y).wait_recv())

    def drain(self):
        p = self.place
        for there, copy in self.first_sends():
            copy.wait_send() if there is None else pl.when(there)(copy.wait_send)
        j = p.z * 2 + 1 - p.y
        pl.when(p.has_up)(lambda: self.side(0, j).wait_send())
        pl.when(p.has_down)(lambda: self.side(1, j).wait_send())
        for k in range(1, p.line):
            for kind, here, zz, further in self.arrivals(k):
                @pl.when(here)
                def _(kind=kind, j=zz * 2 + p.y, i=zz * 2 + 1 - p.y, further=further):
                    self.across(j).wait_send()

                    @pl.when(further)
                    def _():
                        self.main(kind, j).wait_send()
                        self.side(kind, i).wait_send()


class Reduce:
    def __init__(self, place, grad, cut, across, lined, side, side_lined, sems, kept=None, kept_side=None):
        self.place, self.grad, self.cut, self.sems = place, grad, cut, sems
        self.across, self.lined = across, lined
        self.side, self.side_lined, self.kept, self.kept_side = side, side_lined, kept, kept_side
        self.split = cut.early_rows

    def pair(self, first, t):
        return self.sems.at[first, t], self.sems.at[first + 1, t]

    def cross(self, t):
        p = self.place
        return send(self.grad.at[self.cut.rest(t * 2 + 1 - p.y)],
                    self.across.at[t, pl.ds(self.split, self.cut.rows - self.split), :], *self.pair(0, t), p.across)

    def cross_side(self):
        p = self.place
        return send(self.side.at[p.z], self.across.at[p.z, pl.ds(0, self.split), :], *self.pair(10, p.z), p.across)

    def climb(self, t):
        return Several([send(self.across.at[t], self.lined.at[t + 1], *self.pair(2, t), self.place.up),
                        send(self.side.at[t], self.side_lined.at[t + 1], *self.pair(6, t), self.place.up)])

    def sink(self, t):
        return Several([send(self.across.at[t], self.lined.at[t], *self.pair(4, t), self.place.down),
                        send(self.side.at[t], self.side_lined.at[t], *self.pair(8, t), self.place.down)])

    def loads(self, t):
        y = self.place.y
        return [pltpu.make_async_copy(self.grad.at[self.cut.whole(t * 2 + y)], self.kept.at[t], self.sems.at[12, t]),
                pltpu.make_async_copy(self.grad.at[self.cut.early(t * 2 + 1 - y)], self.kept_side.at[t],
                                      self.sems.at[13, t])]

    def loaded(self, t):
        if self.kept is not None:
            for load in self.loads(t):
                load.wait()

    def mine(self, t):
        ref = self.grad[self.cut.whole(t * 2 + self.place.y)] if self.kept is None else self.kept[t]
        return ref.astype(FP)

    def mine_side(self, t):
        ref = self.grad[self.cut.early(t * 2 + 1 - self.place.y)] if self.kept is None else self.kept_side[t]
        return ref.astype(FP)

    def turn(self, q):
        z = self.place.z
        low = z < 2
        if q == 0:
            return jnp.where(low, 3, 0)
        if q == 1:
            return jnp.where(low, 2, 1)
        if q == 2:
            return jnp.where(low, 1 - z, 5 - z)
        return z

    def start(self):
        self.cross(self.turn(0)).start()
        if self.kept is not None:
            for t in range(self.place.line):
                for load in self.loads(t):
                    load.start()

    def advance(self, q):
        self.cross(self.turn(q - 1)).wait_send()
        self.cross(self.turn(q)).start()

    def hop(self, h):
        p = self.place

        def pass_on(t, coming, more, slot):
            self.loaded(t)
            self.cross(t).wait_recv()
            own = self.mine(t)

            def keep(early, rest, side):
                self.across[t, :self.split, :] = early.astype(BF)
                self.across[t, self.split:, :] = (rest + self.across[t, self.split:, :].astype(FP)).astype(BF)
                self.side[t] = side.astype(BF)

            @pl.when(jnp.logical_not(more))
            def _():
                keep(own[:self.split], own[self.split:], self.mine_side(t))

            @pl.when(more)
            def _():
                coming(t).wait_recv()
                summed = own + self.lined[slot].astype(FP)
                keep(summed[:self.split], summed[self.split:], self.mine_side(t) + self.side_lined[slot].astype(FP))

            coming(t).start()

        pl.when(p.z < h)(lambda: pass_on(p.z + p.line - h, self.climb, p.has_down, p.z + p.line - h + 1))
        pl.when(p.z >= p.line - h)(lambda: pass_on(p.z - p.line + h, self.sink, p.has_up, p.z - p.line + h))

    def both_ways(self, ref):
        p = self.place
        return (jnp.where(p.has_down, ref[p.z + 1].astype(FP), 0.0) + jnp.where(p.has_up, ref[p.z].astype(FP), 0.0))

    def finish(self, write):
        p = self.place
        self.loaded(p.z)
        pl.when(p.has_down)(lambda: self.climb(p.z).wait_recv())
        pl.when(p.has_up)(lambda: self.sink(p.z).wait_recv())
        self.side[p.z] = (self.mine_side(p.z) + self.both_ways(self.side_lined)).astype(BF)
        self.cross_side().start()
        partial_sum = self.mine(p.z) + self.both_ways(self.lined)
        self.cross(p.z).wait_recv()
        self.cross_side().wait_recv()
        write(partial_sum + self.across[p.z].astype(FP))

    def step(self, k):
        self.advance(k)
        self.hop(k)

    def drain(self):
        p = self.place
        self.cross(p.z).wait_send()
        self.cross_side().wait_send()
        for zz in range(p.line):
            pl.when(zz > p.z)(lambda zz=zz: self.climb(zz).wait_send())
            pl.when(zz < p.z)(lambda zz=zz: self.sink(zz).wait_send())


def write_to(ref):
    def write(values):
        if len(ref.shape) == 2:
            ref[...] = values
            return
        width = ref.shape[2]
        for j in range(ref.shape[1]):
            ref[:, j, :] = values[:, j * width:(j + 1) * width]

    return write


def reduce_scratch(line, cut, kept=False):
    shape, side = cut.shape, (cut.early_rows, cut.shape[1])
    return [pltpu.VMEM((line, *shape), BF), pltpu.VMEM((line + 1, *shape), BF), pltpu.VMEM((line, *side), BF),
            pltpu.VMEM((line + 1, *side), BF), pltpu.SemaphoreType.DMA((14, line))] + [
                pltpu.VMEM((line, *shape), BF), pltpu.VMEM((line, *side), BF)] * kept


class Pairs:
    def __init__(self, place, per, held, near, sems, slot_of):
        self.place, self.per, self.held, self.near, self.sems, self.slot_of = place, per, held, near, sems, slot_of

    def near_slot(self, s):
        return (s // (2 * self.per)) * self.per + s % self.per

    def to_sibling(self, s):
        return send(self.held.at[self.slot_of(s)], self.near.at[self.near_slot(s)], self.sems.at[0, s],
                    self.sems.at[1, s], self.place.sibling)

    def sends(self, s):
        return self.place.c != (s // self.per) % 2

    def sent(self, s):
        pl.when(self.sends(s))(lambda: self.to_sibling(s).wait_send())

    def put(self, s, rows, before=None):
        if before is not None:
            pl.when(before[0])(lambda: self.sent(before[1]))
        self.held[self.slot_of(s)] = rows
        pl.when(self.sends(s))(lambda: self.to_sibling(s).start())

    def put_next(self, s, rows):
        self.put(s, rows, (s % self.per >= 1, s - 1))

    def add(self, s, use):
        t = s // self.per

        @pl.when(self.place.c == t % 2)
        def _():
            self.to_sibling(s).wait_recv()
            use(self.place.x == t // 2, s % self.per,
                self.held[self.slot_of(s)].astype(FP) + self.near[self.near_slot(s)].astype(FP))


class Exchange(Pairs):
    def __init__(self, place, per, held, near, far, total, sems):
        super().__init__(place, per, held, near, sems, lambda s: s // per)
        self.far, self.total = far, total

    def rows(self, k):
        return pl.ds(pl.multiple_of(k * SUB, SUB), SUB)

    def to_chip(self, s):
        return send_split(self.near.at[self.near_slot(s)], self.far.at[s % self.per],
                          lambda part: (self.sems.at[2 + 2 * part, s], self.sems.at[3 + 2 * part, s]), self.place.chip)

    def add_chip(self, s):
        def use(mine, k, summed):
            @pl.when(jnp.logical_not(mine))
            def _():
                self.near[self.near_slot(s)] = summed.astype(BF)
                self.to_chip(s).start()

            @pl.when(mine)
            def _():
                self.total[self.rows(k), :] = summed

        self.add(s, use)

    def take(self, s, use):
        @pl.when(s // self.per == self.place.t)
        def _():
            k = s % self.per
            self.to_chip(s).wait_recv()
            use(s, self.rows(k), self.total[self.rows(k), :] + self.far[k].astype(FP))

    def drain(self):
        p = self.place

        def one(s, carry):
            t = s // self.per
            pl.when(s % self.per == self.per - 1)(lambda: self.sent(s))
            pl.when(jnp.logical_and(p.c == t % 2, p.x != t // 2))(lambda: self.to_chip(s).wait_send())
            return carry

        lax.fori_loop(0, 4 * self.per, one, 0)


def pair_of(step, per):
    t = step % 2
    return t * per + step // 2, (3 - t) * per + step // 2


def pairs_scratch(per, d, exchange):
    rows = [pltpu.VMEM((4, SUB, d), BF), pltpu.VMEM((2 * per, SUB, d), BF)]
    return rows + [pltpu.VMEM((per, SUB, d), BF)] * exchange + [pltpu.SemaphoreType.DMA((2 + 2 * PARTS * exchange, 4 * per))]


class Spread:
    def __init__(self, place, per, stage, full, sems):
        self.place, self.per, self.stage, self.full, self.sems = place, per, stage, full, sems

    def rows(self, s):
        return self.full.at[pl.ds(pl.multiple_of(s * SUB, SUB), SUB), :]

    def source(self, s):
        return self.rows(s) if self.stage is None else self.stage.at[s % self.per]

    def copy(self, kind, src, s):
        if kind == 0:
            return send_split(src, self.rows(s), lambda part: (self.sems.at[3 + 2 * part, s], self.sems.at[4 + 2 * part, s]),
                              self.place.chip)
        return send(src, self.rows(s), self.sems.at[0, s], self.sems.at[1, s], self.place.sibling)

    def kept(self, s):
        return pltpu.make_async_copy(self.source(s), self.rows(s), self.sems.at[2, s])

    def send(self, s):
        for kind in (0, 1):
            self.copy(kind, self.source(s), s).start()
        if self.stage is not None:
            self.kept(s).start()

    def owns(self, s):
        return s // self.per == self.place.t

    def passes(self, s):
        t = s // self.per
        return jnp.logical_and(self.place.c == t % 2, self.place.x != t // 2)

    def pass_on(self, s):
        @pl.when(self.passes(s))
        def _():
            self.copy(0, self.rows(s), s).wait_recv()
            self.copy(1, self.rows(s), s).start()

    def ready(self, s):
        if self.stage is not None:
            pl.when(self.owns(s))(lambda: self.kept(s).wait())
        pl.when((s // self.per) % 2 != self.place.c)(lambda: self.copy(1, self.rows(s), s).wait_recv())

    def drain(self):
        def one(s, carry):
            @pl.when(self.owns(s))
            def _():
                self.copy(0, self.source(s), s).wait_send()
                self.copy(1, self.source(s), s).wait_send()

            pl.when(self.passes(s))(lambda: self.copy(1, self.rows(s), s).wait_send())
            return carry

        lax.fori_loop(0, 4 * self.per, one, 0)


def whole(shape):
    return pl.BlockSpec(tuple(shape), lambda i: (0,) * len(shape), pipeline_mode=pl.Buffered(1))


ANYWHERE = pl.BlockSpec(memory_space=pl.ANY)
GATHER_SEMS = lambda shards: [pltpu.SemaphoreType.DMA((7, shards)), pltpu.SemaphoreType.DMA]


def make_tables(seg_ref, parents_ref, tree_ref, freq_ref, tags_ref, bars_ref, cos_ref, sin_ref):
    count = parents_ref.shape[1]
    n = LANES
    blocks = sin_ref.shape[0] // ROWS
    lane = lax.broadcasted_iota(jnp.int32, (1, n), 1).astype(FP)
    place_of = lambda b: pl.ds(pl.multiple_of(b * ROWS, ROWS), ROWS)

    def columns(b, carry):
        sin_ref[place_of(b), :] = jnp.broadcast_to(seg_ref[:, place_of(b)].astype(FP), (n, ROWS)).T
        return carry

    def tally(b, carry):
        column = sin_ref[place_of(b), :]
        return (carry[0] + fold_rows(jnp.where(column == lane, 1.0, 0.0)),
                carry[1] + fold_rows(jnp.where(column < lane, 1.0, 0.0)))

    lax.fori_loop(0, blocks, columns, 0)
    sizes, starts = lax.fori_loop(0, blocks, tally, (jnp.zeros((8, n), FP), jnp.zeros((8, n), FP)))
    sizes, starts = (jnp.sum(a, axis=0, keepdims=True) for a in (sizes, starts))
    table = parents_ref[...]
    chosen = jnp.where(lax.broadcasted_iota(jnp.int32, table.shape, 0) == tree_ref[0], table, 0)
    chosen = jnp.sum(chosen.astype(FP), axis=0, keepdims=True)
    parents = jnp.zeros((1, n), FP)
    for b in range(count):
        parents = jnp.where(lane == b, chosen[:, b:b + 1], parents)
    shifts = jnp.where(lane != 0, sizes[:, :1], 0.0) - starts

    def rows(b, carry):
        at = place_of(b)
        column = sin_ref[at, :]
        hot = column == lane
        parent = jnp.sum(jnp.where(hot, parents, 0.0), axis=1, keepdims=True)
        above = jnp.where(jnp.logical_and(lane == parent, lane != 0), sizes, 0.0)
        first = (b * ROWS).astype(FP)
        position = (lax.broadcasted_iota(jnp.int32, (ROWS, 1), 0).astype(FP) + first
                    + jnp.sum(jnp.where(hot, shifts, 0.0) + above, axis=1, keepdims=True))
        tags_ref[at, :] = jnp.where(hot, 1.0, 0.0).astype(BF)
        open_to = jnp.logical_or(jnp.logical_or(hot, lane == parent), jnp.logical_or(lane == 0, lane >= count))
        bars_ref[at, :] = jnp.where(open_to, 0.0, BLOCKED).astype(BF)
        angles = position * freq_ref[...]
        cos_ref[at, :] = jnp.cos(angles)
        turned = jnp.sin(angles)
        sin_ref[at, :] = jnp.where(lane < n // 2, -turned, turned)
        return carry

    lax.fori_loop(0, blocks, rows, 0)


def front_kernel(kv, group, line, *refs):
    refs = list(refs)
    take = lambda count: [refs.pop(0) for _ in range(count)]
    x_ref, gains_ref, seg_ref, parents_ref, tree_ref, freq_ref = take(6)
    masters = take(4) if line else take(1)
    xn_ref, q_ref, k_ref, v_ref, kt_ref, vt_ref, raw_ref, tags_ref, bars_ref, cos_ref, sin_ref = take(11)
    if line:
        wp_out, wm_out, we_low, ws_low = take(4)
        wp_ref, wm_low, p_sems, p_local, m_sems, m_local, out_sem = take(7)
    else:
        wp_ref = masters[0]
    xn_full, xn_sem = take(2)
    i = pl.program_id(0)
    final = pl.num_programs(0) - 1
    d = x_ref.shape[1]
    n = LANES
    per = group + 2
    if line:
        place = Place(line)
        size = masters[0].shape[0]
        project = Gather(place, None, wp_ref, Cut((size, wp_ref.shape[1]), 0), p_sems, p_local)
        merge = Gather(place, wm_low, wm_out, Cut(wm_low.shape, 1), m_sems, m_local)
        written = pltpu.make_async_copy(wp_ref, wp_out, out_sem)
    normed = pltpu.make_async_copy(xn_full, xn_ref, xn_sem)

    def round_projection():
        at = pl.ds(pl.multiple_of(place.dp * size, size), size)
        for j in range(kv * per):
            wp_ref[at, j * n:(j + 1) * n] = masters[0][:, j, :].astype(BF)

    def norm(b, carry):
        at = pl.ds(pl.multiple_of(b * ROWS, ROWS), ROWS)
        x = x_ref[at, :].astype(FP)
        xn_full[at, :] = (x * inverse_rms(x) * gains_ref[:, :d]).astype(BF)
        return carry

    @pl.when(i == 0)
    def _():
        if line:
            place.greet(False, True, round_projection)
            project.start()
        lax.fori_loop(0, x_ref.shape[0] // ROWS, norm, 0)
        normed.start()
        if line:
            project.hop(1)
        make_tables(seg_ref, parents_ref, tree_ref, freq_ref, tags_ref, bars_ref, cos_ref, sin_ref)
        if line:
            project.hop(2)
            wm_low[...] = masters[1][...].astype(BF)
            units = masters[2].shape[2]
            for half in range(2):
                we_low[:, half * units:(half + 1) * units] = masters[2][:, half, :].astype(BF)
            ws_low[...] = masters[3][...].astype(BF)
            project.hop(3)
            merge.start()
            project.finish()
            written.start()

    if line:
        for k in range(1, line):
            pl.when(i == k + 1)(lambda k=k: merge.hop(k))
    at = pl.ds(pl.multiple_of(i * ROWS, ROWS), ROWS)
    qkv = dot(xn_full[at, :], wp_ref[...])
    cosines, sines = cos_ref[at, :], sin_ref[at, :]
    gq, gk = gains_ref[:, 2 * d:2 * d + n], gains_ref[:, 2 * d + n:]
    keys, values = [], []
    for h in range(kv):
        for c in range(group + 1):
            raw = qkv[:, (h * per + c) * n:(h * per + c + 1) * n]
            to = (h * (group + 1) + c) * n
            raw_ref[:, to:to + n] = raw
            y = raw * inverse_rms(raw) * (gq if c < group else gk)
            turned = y * cosines + pltpu.roll(y, n // 2, 1) * sines
            if c < group:
                to = (h * group + c) * n
                q_ref[:, to:to + n] = turned.astype(BF)
            else:
                keys.append(turned)
        values.append(qkv[:, (h * per + group + 1) * n:(h * per + group + 2) * n])
    for h in range(kv):
        k_ref[:, h * n:(h + 1) * n] = keys[h].astype(BF)
        v_ref[:, h * n:(h + 1) * n] = values[h].astype(BF)
        kt_ref[h * n:(h + 1) * n, :] = keys[h].T.astype(BF)
        vt_ref[h * n:(h + 1) * n, :] = values[h].T.astype(BF)

    @pl.when(i == final)
    def _():
        normed.wait()
        if line:
            merge.finish()
            merge.drain()
            project.drain()
            written.wait()


def front(x, gains, segments, parents, tree, masters, kv, group, line):
    length, d = x.shape
    n = LANES
    rows = lambda w: pl.BlockSpec((ROWS, w), lambda i: (i, 0))
    cols = pl.BlockSpec((kv * n, ROWS), lambda i: (0, i))
    out = lambda w, t: jax.ShapeDtypeStruct((length, w), t)
    raw_w = kv * (group + 1) * n
    freq = np.float32(THETA ** (-(np.arange(n) % (n // 2)) * 2.0 / n))[None]
    more_specs, more_shapes, scratch = [], [], []
    if line:
        shards = 2 * line
        project, merge, expand, shrink = (m.shape for m in masters)
        wp_shape = (project[0] * shards, project[1] * n)
        more_shapes = [jax.ShapeDtypeStruct(wp_shape, BF), jax.ShapeDtypeStruct((merge[0], merge[1] * shards), BF),
                       jax.ShapeDtypeStruct((expand[0], 2 * expand[2]), BF), jax.ShapeDtypeStruct(shrink, BF)]
        more_specs = [ANYWHERE, ANYWHERE, whole(more_shapes[2].shape), whole(more_shapes[3].shape)]
        scratch = [pltpu.VMEM(wp_shape, BF), pltpu.VMEM(merge, BF), *GATHER_SEMS(shards), *GATHER_SEMS(shards),
                   pltpu.SemaphoreType.DMA]
    table = whole((length, n))
    return pl.pallas_call(
        partial(front_kernel, kv, group, line),
        grid=(length // ROWS,),
        in_specs=[whole(x.shape), whole(gains.shape), whole(segments.shape), whole(parents.shape),
                  pl.BlockSpec(memory_space=pltpu.SMEM), whole(freq.shape), *[whole(m.shape) for m in masters]],
        out_specs=[ANYWHERE, rows(kv * group * n), rows(kv * n), rows(kv * n), cols, cols, rows(raw_w),
                   table, table, table, table, *more_specs],
        out_shape=[out(d, BF), out(kv * group * n, BF), out(kv * n, BF), out(kv * n, BF),
                   jax.ShapeDtypeStruct((kv * n, length), BF), jax.ShapeDtypeStruct((kv * n, length), BF),
                   out(raw_w, FP), out(n, BF), out(n, BF), out(n, FP), out(n, FP), *more_shapes],
        scratch_shapes=[*scratch, pltpu.VMEM((length, d), BF), pltpu.SemaphoreType.DMA],
        compiler_params=params(**({"collective_id": 0, "has_side_effects": True} if line else {})),
        name="front",
    )(x, gains, segments, parents, tree, freq, *masters)


def stacked(ref_block, h, group):
    n = LANES
    return jnp.concatenate(
        [ref_block[:, (h * group + g) * n:(h * group + g + 1) * n] for g in range(group)], axis=0)


def causal_tile(group, rows=ROWS, after=0):
    key_at = lax.broadcasted_iota(jnp.int32, (ROWS, rows * group), 0)
    query_at = lax.broadcasted_iota(jnp.int32, (ROWS, rows * group), 1) % rows
    return key_at <= query_at + after


def in_turn(i, first, steps, per, acts):
    for behind, act in acts:
        @pl.when(jnp.logical_and(i - first - behind >= 0, i - first - behind < steps))
        def _(behind=behind, act=act):
            for s in pair_of(i - first - behind, per):
                act(s)


def middle_kernel(kv, group, unit, line, per, steps, *refs):
    refs = list(refs)
    take = lambda count: [refs.pop(0) for _ in range(count)]
    q_ref, k_ref, vt_ref, tags_ref, bars_ref, wm_ref, gains_ref, x_all, dy_all = take(9)
    weights = take(2)
    ctx_out, lse_ref, base_ref, other_ref, gate_out, up_out, dh_ref, dhb_ref, dg_ref, gsh_out = take(10)
    acc_ref, sum_ref, x_ref, dy_ref, we_ref, ws_ref, copy_sems = take(7)
    h_ref, xn_ref, a_ref, dgu_ref, ctx_ref, gup_ref = take(6)
    h_held, h_near, h_far, h_sems, xn_sems = take(5)
    d_held, d_near, d_far, d_sems, stage, dh_sems = take(6)
    b_held, b_near, b_sems = take(3)
    place = Place(line)
    i = pl.program_id(0)
    n = LANES
    share, d = x_ref.shape
    units = ws_ref.shape[0]
    tile = 256
    attended = Exchange(place, per, h_held, h_near, h_far, h_ref, h_sems)
    norms = Spread(place, per, None, xn_ref, xn_sems)
    pulled_back = Exchange(place, per, d_held, d_near, d_far, dh_ref, d_sems)
    grads = Spread(place, per, stage, dhb_ref, dh_sems)
    branch = Pairs(place, per, b_held, b_near, b_sems, lambda s: s // per)
    own_share = x_all.at[pl.ds(pl.multiple_of(place.t * share, share), share), :]
    copies = [pltpu.make_async_copy(own_share, x_ref, copy_sems.at[0]),
              pltpu.make_async_copy(dy_all, dy_ref, copy_sems.at[1])]
    if line:
        gsh_ref = take(1)[0]
        shrink = Reduce(place, gsh_ref, Cut(gsh_out.shape, 1), *take(5))
        gate_ref = take(1)[0]
        expand = Reduce(place, gate_ref, Cut(gate_out.shape, 0), *take(5))
        cuts = (Cut(weights[0].shape, 0), Cut(weights[1].shape, 1))
        first, second = [Gather(place, weights[w], (we_ref, ws_ref)[w], cuts[w], *take(2)) for w in range(2)]
    else:
        gsh_ref, gate_ref = gsh_out, gate_out
        copies += [pltpu.make_async_copy(weights[0], we_ref, copy_sems.at[2]),
                   pltpu.make_async_copy(weights[1], ws_ref, copy_sems.at[3])]
    written = [pltpu.make_async_copy(ctx_ref, ctx_out, copy_sems.at[4]),
               pltpu.make_async_copy(gup_ref, up_out, copy_sems.at[5])]
    rows_of = lambda s: pl.ds(pl.multiple_of(s * SUB, SUB), SUB)

    def at_step(step, *acts):
        @pl.when(i == step)
        def _():
            for act in acts:
                act()

    @pl.when(i == 0)
    def _():
        place.greet(True, bool(line))
        if line:
            first.start()
        for copy in copies:
            copy.start()
        dg_ref[...] = jnp.zeros_like(dg_ref)


    def block(s):
        here = rows_of(s)
        bars = jnp.concatenate([bars_ref[here, :]] * group, axis=0)
        q = q_ref[here, :]
        wide = [jnp.concatenate([stacked(q, h, group), bars], axis=1) for h in range(kv)]
        acc_ref[...] = jnp.zeros_like(acc_ref)
        sum_ref[...] = jnp.zeros_like(sum_ref)

        def chunk(j, diagonal):
            at = pl.ds(pl.multiple_of(j * ROWS, ROWS), ROWS)
            tags = tags_ref[at, :]
            for h in range(kv):
                keys = jnp.concatenate([k_ref[at, h * n:(h + 1) * n], tags], axis=1)
                scores = dot(keys, wide[h], 1, 1)
                e = jnp.exp2(scores * unit)
                if diagonal:
                    e = jnp.where(causal_tile(group, SUB, (s % 2) * SUB), e, 0.0)
                sum_ref[h] += fold_rows(e)
                acc_ref[h] += dot(vt_ref[h * n:(h + 1) * n, at], e.astype(BF))

        lax.fori_loop(0, s // 2, lambda j, c: (chunk(j, False), c)[1], 0)
        chunk(s // 2, True)
        parts = []
        for h in range(kv):
            sums = jnp.sum(sum_ref[h], axis=0, keepdims=True)
            lse_ref[s, h:h + 1, :] = jnp.log2(sums)
            ctx = (acc_ref[h] / sums).T
            parts += [ctx[g * SUB:(g + 1) * SUB] for g in range(group)]
        ctx_ref[here, :] = jnp.concatenate(parts, axis=1).astype(BF)

    def put_pair(pairs, blocks, part):
        for u, s in enumerate(blocks):
            pairs.put_next(s, part[u * SUB:(u + 1) * SUB])

    @pl.when(i < steps)
    def _():
        blocks = pair_of(i, per)
        for s in blocks:
            block(s)
        ctx = jnp.concatenate([ctx_ref[rows_of(s), :] for s in blocks], axis=0)
        put_pair(attended, blocks, dot(ctx, wm_ref[...]).astype(BF))

    def hidden_rows(s, at, summed):
        hidden = x_ref[at, :].astype(FP) + summed
        h_ref[at, :] = hidden
        xn_ref[rows_of(s), :] = (hidden * inverse_rms(hidden) * gains_ref[:, d:2 * d]).astype(BF)
        norms.send(s)

    at_step(1, copies[0].wait)
    at_step(steps, written[0].start)
    in_turn(i, 0, steps, per, ((1, attended.add_chip), (3, lambda s: attended.take(s, hidden_rows)), (5, norms.pass_on)))
    swiglu, feed = steps + 3, 2 * steps + 3
    if line:
        at_step(1, lambda: first.hop(1))
        at_step(3, lambda: first.hop(2))
        at_step(5, lambda: first.hop(3), second.start)
        at_step(7, lambda: second.hop(1))
        at_step(8, lambda: second.hop(2))
        at_step(9, lambda: second.hop(3), first.finish)
        at_step(feed, second.finish)
    else:
        at_step(swiglu, copies[2].wait, copies[3].wait)


    def gathered(ref, blocks):
        return jnp.concatenate([ref[rows_of(s), :] for s in blocks], axis=0)

    def keep(ref, blocks, values):
        for u, s in enumerate(blocks):
            ref[rows_of(s), :] = values[u * SUB:(u + 1) * SUB]

    def tiles(grad_ref, left_ref, right_ref, start, count, after):
        def one(t, carry):
            cut = pl.ds(pl.multiple_of(t * tile, tile), tile)
            there = pl.ds(pl.multiple_of((t + after) * tile, tile), tile)
            grad_ref[:, cut] = dot(left_ref[...], right_ref[:, there], 0, 0).astype(grad_ref.dtype)
            return carry

        lax.fori_loop(start, start + count, one, 0)

    @pl.when(jnp.logical_and(i >= swiglu, i < feed))
    def _():
        blocks = pair_of(i - swiglu, per)
        for s in blocks:
            norms.ready(s)
        gu = dot(gathered(xn_ref, blocks), we_ref[...])
        gate, up = gu[:, :units], gu[:, units:]
        keep(a_ref, blocks, (gate / (1.0 + jnp.exp(-gate)) * up).astype(BF))
        keep(dgu_ref, blocks, gu.astype(BF))

    at_step(feed - 1, copies[1].wait, lambda: tiles(gsh_ref, a_ref, dy_ref, 0, gsh_ref.shape[1] // tile, 0))
    if line:
        at_step(feed, shrink.start)

    @pl.when(jnp.logical_and(i >= feed, i < feed + steps))
    def _():
        blocks = pair_of(i - feed, per)
        gu = gathered(dgu_ref, blocks).astype(FP)
        gate, up = gu[:, :units], gu[:, units:]
        sig = 1.0 / (1.0 + jnp.exp(-gate))
        da = dot(gathered(dy_ref, blocks), ws_ref[...], 1, 1)
        dgu = jnp.concatenate([da * up * (sig * (1.0 + gate * (1.0 - sig))), da * (gate * sig)], axis=1).astype(BF)
        keep(dgu_ref, blocks, dgu)
        put_pair(pulled_back, blocks, dot(dgu, we_ref[...], 1, 1).astype(BF))

    def grad_rows(s, at, summed):
        pulled, gain_grad = rms_pull(h_ref[at, :], gains_ref[:, d:2 * d], summed)
        dh = dy_ref[rows_of(s), :].astype(FP) + pulled
        dh_ref[at, :] = dh
        dg_ref[...] += fold_rows(gain_grad)
        stage[s % per] = dh.astype(BF)
        grads.send(s)

    def chip_rows(mine, k, summed):
        at = rows_of(k)

        @pl.when(mine)
        def _():
            base_ref[at, :] = h_ref[at, :] + summed

        @pl.when(jnp.logical_not(mine))
        def _():
            other_ref[k] = summed.astype(BF)

    in_turn(i, feed, steps, per, ((1, pulled_back.add_chip), (3, lambda s: pulled_back.take(s, grad_rows)),
                                  (5, grads.pass_on)))

    @pl.when(jnp.logical_and(i >= feed + 3, i < feed + 3 + steps))
    def _():
        blocks = pair_of(i - feed - 3, per)
        put_pair(branch, blocks, dot(gathered(a_ref, blocks), ws_ref[...]).astype(BF))

    in_turn(i, feed, steps, per, ((4, lambda s: branch.add(s, chip_rows)),))
    if line:
        for k in range(1, line):
            at_step(feed + k, lambda k=k: shrink.step(k))
    half = units // tile
    at_step(feed + steps, lambda: tiles(gate_ref, xn_ref, dgu_ref, 0, half, 0))
    if line:
        at_step(feed + steps, expand.start)
        for k in range(1, line):
            at_step(feed + steps + k, lambda k=k: expand.step(k))
    at_step(feed + steps + 1, lambda: tiles(gup_ref, xn_ref, dgu_ref, 0, half, half), written[1].start)

    @pl.when(i == feed + steps + 4)
    def _():
        attended.drain()
        pulled_back.drain()
        norms.drain()
        grads.drain()
        for t in range(4):
            branch.sent(t * per + per - 1)
        lax.fori_loop(0, 4 * per, lambda s, c: (grads.ready(s), c)[1], 0)
        for copy in written:
            copy.wait()
        if line:
            shrink.finish(write_to(gsh_out))
            shrink.drain()
            expand.finish(write_to(gate_out))
            expand.drain()
            first.drain()
            second.drain()


def middle(q, k, vt, tags, bars, wm, x, dy, gains, weights, kv, group, unit, line):
    length = q.shape[0]
    n = LANES
    d = wm.shape[1]
    share = (length // 4, d)
    per = share[0] // SUB
    steps = 2 * per
    we, ws = (w.shape for w in weights)
    shards = 2 * line
    shrink = jax.ShapeDtypeStruct(ws, BF)
    gate = jax.ShapeDtypeStruct((we[0], we[1] // 2), BF)
    more = []
    if line:
        shrink = jax.ShapeDtypeStruct(ws, FP)
        gate = jax.ShapeDtypeStruct(gate.shape, FP)
        we, ws = (we[0] * shards, we[1]), (ws[0], ws[1] * shards)
        more = [pltpu.VMEM(ws, BF), *reduce_scratch(line, Cut(shrink.shape, 1)), pltpu.VMEM((we[0], we[1] // 2), BF),
                *reduce_scratch(line, Cut(gate.shape, 0)), *GATHER_SEMS(shards), *GATHER_SEMS(shards)]
    units = ws[0]
    results = [jax.ShapeDtypeStruct(q.shape, BF), jax.ShapeDtypeStruct((length // SUB, 8, SUB * group), FP),
               jax.ShapeDtypeStruct(share, FP), jax.ShapeDtypeStruct((per, SUB, d), BF), gate,
               jax.ShapeDtypeStruct((we[0], units), BF), jax.ShapeDtypeStruct(share, FP),
               jax.ShapeDtypeStruct((length, d), BF), jax.ShapeDtypeStruct((8, d), FP),
               shrink]
    out_specs = [whole(r.shape) for r in results]
    for at in (0, 5, 7):
        out_specs[at] = ANYWHERE
    held = [q, k, vt, tags, bars, wm, gains]
    return pl.pallas_call(
        partial(middle_kernel, kv, group, unit, line, per, steps),
        grid=(3 * steps + 8,),
        in_specs=[whole(a.shape) for a in held] + [ANYWHERE] * 4,
        out_specs=out_specs,
        out_shape=results,
        scratch_shapes=[pltpu.VMEM((kv, n, SUB * group), FP), pltpu.VMEM((kv, 8, SUB * group), FP),
                        pltpu.VMEM(share, BF), pltpu.VMEM((length, d), BF), pltpu.VMEM(we, BF), pltpu.VMEM(ws, BF),
                        pltpu.SemaphoreType.DMA((6,)),
                        pltpu.VMEM(share, FP), pltpu.VMEM((length, d), BF), pltpu.VMEM((length, units), BF),
                        pltpu.VMEM((length, 2 * units), BF), pltpu.VMEM(q.shape, BF), pltpu.VMEM((we[0], units), BF),
                        *pairs_scratch(per, d, True), pltpu.SemaphoreType.DMA((3 + 2 * PARTS, 4 * per)),
                        *pairs_scratch(per, d, True), pltpu.VMEM((per, SUB, d), BF),
                        pltpu.SemaphoreType.DMA((3 + 2 * PARTS, 4 * per)),
                        *pairs_scratch(per, d, False), *more],
        compiler_params=params(collective_id=1, has_side_effects=True),
        name="middle",
    )(*held, x, dy, *weights)


def back_kernel(kv, group, unit, scale, blocks, per, line, *refs):
    refs = list(refs)
    take = lambda count: [refs.pop(0) for _ in range(count)]
    q_ref, k_ref, v_ref, kt_ref, tags_ref, bars_ref, lse_ref, ctx_block, dh_block, wm_ref = take(10)
    raw_ref, cos_ref, sin_ref, all_gains, base_ref, dg2_ref, other_ref = take(7)
    x_all, dh_all = take(2)
    late_from = take(4)
    grads = take(2) if line else []
    in_ref, out_ref, gains_out = take(3)
    sums = take(3) if line else []
    weight_grads = [] if line else take(2)
    late_to = take(4)
    wp_ref, ctx_ref, dh_ref, xn_ref = late_to
    late_sem = take(1)[0]
    late = [pltpu.make_async_copy(a, b, late_sem.at[w]) for w, (a, b) in enumerate(zip(late_from, late_to))]
    dk_ref, dv_ref, dq_ref, dqkv_ref = take(4)
    b_far, b_sems, x_held, x_near, x_sems = take(5)
    mine_ref, far_ref, x_far, f_sems, x_ref, dh_own, own_sems, heads_ref, fold_ref = take(9)
    place = Place(line)
    i = pl.program_id(0)
    b = blocks - 1 - i
    n = LANES
    pairs = Pairs(place, per, x_held, x_near, x_sems, lambda s: s % x_held.shape[0])
    subs = ROWS // SUB
    share, d = x_ref.shape
    gq, gk = all_gains[:, 2 * d:2 * d + n], all_gains[:, 2 * d + n:]
    tile = 256
    tensors = lax.axis_size("tensor")
    mates = [(place.dp, (place.t + step) % tensors) for step in range(1, tensors)]
    peers = []
    own_rows = pl.ds(pl.multiple_of(place.t * share, share), share)
    own_copies = [pltpu.make_async_copy(x_all.at[own_rows, :], x_ref, own_sems.at[0]),
                  pltpu.make_async_copy(dh_all, dh_own, own_sems.at[1])]
    if line:
        shards = 2 * line
        gm_ref, gp_ref = take(2)
        expand = Reduce(place, grads[1], Cut(grads[0].shape, 0), *take(7))
        merge = Reduce(place, gm_ref, Cut((gm_ref.shape[0], gm_ref.shape[1] // shards), 1), *take(5))
        project = Reduce(place, gp_ref, Cut((gp_ref.shape[0] // shards, gp_ref.shape[1]), 0), *take(5))
        shown, over, g_sems = take(3)
        peers = [((place.dp + step) % shards, place.t) for step in range(1, shards)]
    else:
        gp_ref, gm_ref = weight_grads

    def tiles(grad_ref, left_ref, right_ref):
        def one(t, carry):
            cut = pl.ds(pl.multiple_of(t * tile, tile), tile)
            grad_ref[:, cut] = dot(left_ref[...], right_ref[:, cut], 0, 0).astype(grad_ref.dtype)
            return carry

        lax.fori_loop(0, grad_ref.shape[1] // tile, one, 0)

    def write_up(values):
        sums[0][:, 0, :] = grads[0][...]
        sums[0][:, 1, :] = values

    def project_rows(t):
        cut = pl.ds(pl.multiple_of(t * tile, tile), tile)
        gp_ref[cut, :] = dot(xn_ref[:, cut], dqkv_ref[...], 0, 0).astype(BF)

    def chip(k):
        return send_split(far_ref.at[k], x_far.at[k], lambda part: (f_sems.at[2 * part, k], f_sems.at[2 * part + 1, k]),
                          place.chip)

    def branch(k):
        return send_split(other_ref.at[k], b_far.at[k], lambda part: (b_sems.at[2 * part, k], b_sems.at[2 * part + 1, k]),
                          place.chip)

    @pl.when(i == 0)
    def _():
        barrier = pltpu.get_barrier_semaphore()
        for device in mates + peers:
            pl.semaphore_signal(barrier, inc=1, device_id=device, device_id_type=MESH)
        for copy in late:
            copy.start()
        pl.semaphore_wait(barrier, len(mates + peers))
        if line:
            expand.start()
        for k in range(per):
            branch(k).start()
        dk_ref[...] = jnp.zeros_like(dk_ref)
        dv_ref[...] = jnp.zeros_like(dv_ref)
        heads_ref[...] = jnp.zeros_like(heads_ref)

    @pl.when(i < blocks)
    def _():
        here = pl.ds(pl.multiple_of(b * ROWS, ROWS), ROWS)
        dctx = dot(dh_block[...], wm_ref[...], 1, 1).astype(BF)
        ctx, q = ctx_block[...], q_ref[...]
        bars = jnp.concatenate([bars_ref[...]] * group, axis=0)
        wide, queries, outward, centres, lses = [], [], [], [], []
        for h in range(kv):
            queries.append(stacked(q, h, group))
            wide.append(jnp.concatenate([queries[h], bars], axis=1))
            outward.append(stacked(dctx, h, group))
            both = outward[h].astype(FP) * stacked(ctx, h, group).astype(FP)
            centres.append(jnp.sum(both.T, axis=0, keepdims=True))
            lses.append(jnp.concatenate([lse_ref[u, h:h + 1, g * SUB:(g + 1) * SUB]
                                         for g in range(group) for u in range(ROWS // SUB)], axis=1))
        dq_ref[...] = jnp.zeros_like(dq_ref)

        def chunk(j, diagonal):
            at = pl.ds(pl.multiple_of(j * ROWS, ROWS), ROWS)
            tags = tags_ref[at, :]
            for h in range(kv):
                cut = slice(h * n, (h + 1) * n)
                keys = jnp.concatenate([k_ref[at, cut], tags], axis=1)
                p = jnp.exp2(dot(keys, wide[h], 1, 1) * unit - lses[h])
                if diagonal:
                    p = jnp.where(causal_tile(group), p, 0.0)
                dp = dot(v_ref[at, cut], outward[h], 1, 1)
                ds = (p * (dp - centres[h])).astype(BF)
                dv_ref[at, cut] += dot(p.astype(BF), outward[h])
                dk_ref[at, cut] += dot(ds, queries[h])
                dq_ref[h] += dot(kt_ref[cut, at], ds)

        lax.fori_loop(0, b, lambda j, c: (chunk(j, False), c)[1], 0)
        chunk(b, True)

        cosines, sines = cos_ref[...], sin_ref[...]
        pieces = []
        for h in range(kv):
            dq = dq_ref[h].T
            for c in range(group + 1):
                if c < group:
                    grad, gain, row = dq[c * ROWS:(c + 1) * ROWS] * scale, gq, 0
                else:
                    grad, gain, row = dk_ref[here, h * n:(h + 1) * n] * scale, gk, 1
                grad = grad * cosines - pltpu.roll(grad, n // 2, 1) * sines
                at = (h * (group + 1) + c) * n
                piece, gain_grad = rms_pull(raw_ref[:, at:at + n], gain, grad)
                heads_ref[row] += fold_rows(gain_grad)
                pieces.append(piece)
            pieces.append(dv_ref[here, h * n:(h + 1) * n])
        dqkv = jnp.concatenate(pieces, axis=1).astype(BF)
        dqkv_ref[here, :] = dqkv
        pl.when(i == 0)(late[0].wait)
        part = dot(dqkv, wp_ref[...], 1, 1).astype(BF)
        for u in range(subs):
            s = subs * b + u
            pairs.put(s, part[u * SUB:(u + 1) * SUB], (i >= 2, s + 2 * subs))

    def chip_rows(mine, k, summed):
        @pl.when(mine)
        def _():
            mine_ref[pl.ds(pl.multiple_of(k * SUB, SUB), SUB), :] = summed

        @pl.when(jnp.logical_not(mine))
        def _():
            far_ref[k] = summed.astype(BF)
            chip(k).start()

    @pl.when(i >= 1)
    def _():
        for u in range(subs):
            pairs.add(subs * (b + 1) + u, chip_rows)

    @pl.when(i == 3)
    def _():
        for k in range(per):
            branch(k).wait()
            at = slice(k * SUB, (k + 1) * SUB)
            out_ref[at, :] = (base_ref[at, :] + b_far[k].astype(FP)).astype(BF)
        for copy in own_copies:
            copy.start()

    @pl.when(i == 1)
    def _():
        late[1].wait()
        late[2].wait()
        tiles(gm_ref, ctx_ref, dh_ref)

    if line:
        for step, act in enumerate((lambda: expand.step(1), lambda: expand.step(2), lambda: expand.step(3), merge.start,
                                    lambda: merge.step(1), lambda: merge.step(2))):
            pl.when(i == step)(act)

    def input_rows(k):
        at = slice(k * SUB, (k + 1) * SUB)
        chip(k).wait()
        summed = mine_ref[at, :] + x_far[k].astype(FP)
        pulled, gain_grad = rms_pull(x_ref[at, :].astype(FP), all_gains[:, :d], summed)
        in_ref[at, :] = (dh_own[at, :] + pulled).astype(BF)
        fold_ref[...] += fold_rows(gain_grad)

    def folded(ref):
        pieces = [fold_ref[...], dg2_ref[...], heads_ref[0], heads_ref[1]]
        row = jnp.sum(jnp.concatenate(pieces, axis=1), axis=0, keepdims=True)
        count = row.shape[1] // n
        for j in range(count):
            ref[j:j + 1, :] = row[:, j * n:(j + 1) * n]
        ref[count:, :] = jnp.zeros((ref.shape[0] - count, n), FP)

    def show(buffer, me, devices, first):
        copies = [send(buffer.at[me], buffer.at[me], g_sems.at[0, first + step], g_sems.at[1, first + step], device)
                  for step, device in enumerate(devices, 1)]
        for copy in copies:
            copy.start()
        return copies

    def added(buffer, me, devices, first):
        count = len(devices) + 1
        for step in range(1, count):
            who = (me - step + count) % count
            send(buffer.at[who], buffer.at[who], g_sems.at[0, first + step], g_sems.at[1, first + step],
                 place.sibling).wait_recv()
        total = buffer[0]
        for who in range(1, count):
            total = total + buffer[who]
        return total

    @pl.when(i == blocks)
    def _():
        fold_ref[...] = jnp.zeros_like(fold_ref)
        late[3].wait()
        for copy in own_copies:
            copy.wait()
        if not line:
            tiles(gp_ref, xn_ref, dqkv_ref)
            for k in range(per):
                input_rows(k)
            folded(gains_out)
        else:
            project_rows(project.turn(0))
            project.start()
            for q in range(1, line):
                project_rows(project.turn(q))
            merge.step(3)
            expand.finish(write_up)
            project.step(1)
            merge.finish(write_to(sums[1]))
            project.step(2)
            for k in range(per):
                input_rows(k)
            folded(shown.at[place.t])
            copies = show(shown, place.t, mates, 0)
            project.step(3)
            over[place.dp] = added(shown, place.t, mates, 0)
            copies += show(over, place.dp, peers, tensors)
            project.finish(write_to(sums[2]))
            gains_out[...] = added(over, place.dp, peers, tensors)
            for copy in copies:
                copy.wait_send()
            for r in (expand, merge, project):
                r.drain()
        for s in range(2 * subs):
            pairs.sent(s)


def back(q, k, v, kt, tags, bars, lse, ctx, dh, wm, wp, raw, cosines, sines, gains, xn, base, dg2, other, x, dh_own,
         grads, kv, group, unit, scale, line):
    length = q.shape[0]
    n = LANES
    d = wm.shape[1]
    blocks = length // ROWS
    per = other.shape[0]
    share = base.shape
    block_of = lambda i: jnp.maximum(blocks - 1 - i, 0)
    rows = lambda w: pl.BlockSpec((ROWS, w), lambda i: (block_of(i), 0))
    late = [wp, ctx, dh, xn]
    gain_rows = (-(-(gains.shape[1] // n) // 8) * 8, n)
    scratch = [*[pltpu.VMEM(a.shape, BF) for a in late], pltpu.SemaphoreType.DMA((4,)),
               pltpu.VMEM((length, kv * n), FP), pltpu.VMEM((length, kv * n), FP),
               pltpu.VMEM((kv, n, ROWS * group), FP), pltpu.VMEM((length, wp.shape[1]), BF),
               pltpu.VMEM((per, SUB, d), BF), pltpu.SemaphoreType.DMA((2 * PARTS, per)),
               pltpu.VMEM((2 * ROWS // SUB, SUB, d), BF), pltpu.VMEM((2 * per, SUB, d), BF),
               pltpu.SemaphoreType.DMA((2, 4 * per)),
               pltpu.VMEM(share, FP), pltpu.VMEM((per, SUB, d), BF), pltpu.VMEM((per, SUB, d), BF),
               pltpu.SemaphoreType.DMA((2 * PARTS, per)), pltpu.VMEM(share, BF), pltpu.VMEM(share, FP),
               pltpu.SemaphoreType.DMA((2,)), pltpu.VMEM((2, 8, n), FP), pltpu.VMEM((8, d), FP)]
    results = [jax.ShapeDtypeStruct(share, BF), jax.ShapeDtypeStruct(share, BF), jax.ShapeDtypeStruct(gain_rows, FP)]
    if line:
        shards = 2 * line
        own = [grads[0].shape, (wm.shape[0], wm.shape[1] // shards),
               (wp.shape[0] // shards, wp.shape[1])]
        views = ((own[0][0], 2, own[0][1]), own[1], (own[2][0], own[2][1] // n, n))
        results += [jax.ShapeDtypeStruct(s, FP) for s in views]
        scratch += [pltpu.VMEM(wm.shape, BF), pltpu.VMEM(wp.shape, BF)]
        for w, s in enumerate(own):
            scratch += reduce_scratch(line, Cut(s, int(w == 1)), w == 0)
        scratch += [pltpu.VMEM((4, *gain_rows), FP), pltpu.VMEM((shards, *gain_rows), FP),
                    pltpu.SemaphoreType.DMA((2, 4 + shards))]
    else:
        results += [jax.ShapeDtypeStruct(wp.shape, BF), jax.ShapeDtypeStruct(wm.shape, BF)]
    args = [q, k, v, kt, tags, bars, lse, ctx, dh, wm, raw, cosines, sines, gains, base, dg2]
    more = [other, x, dh_own, *late, *grads]
    specs = [whole(a.shape) for a in args] + [ANYWHERE] * len(more)
    if line:
        specs[-2] = whole(grads[0].shape)
    for at in (0, 5, 7, 8, 10, 11, 12):
        specs[at] = rows(args[at].shape[1])
    specs[6] = pl.BlockSpec((ROWS // SUB, 8, SUB * group), lambda i: (block_of(i), 0, 0))
    return pl.pallas_call(
        partial(back_kernel, kv, group, unit, scale, blocks, per, line),
        grid=(blocks + 1,),
        in_specs=specs,
        out_specs=[whole(r.shape) for r in results],
        out_shape=results,
        scratch_shapes=scratch,
        compiler_params=params(collective_id=3, has_side_effects=True),
        name="back",
    )(*args, *more)


def adamw_step(weight, moment_one, moment_two, gradient, step_rate, decay):
    mean_next = BETA_ONE * moment_one + (1.0 - BETA_ONE) * gradient
    square_next = BETA_TWO * moment_two + (1.0 - BETA_TWO) * gradient * gradient
    mean_hat = mean_next / (1.0 - BETA_ONE**STEP)
    square_hat = square_next / (1.0 - BETA_TWO**STEP)
    weight_next = weight - step_rate * (mean_hat / (jnp.sqrt(square_hat) + EPS_ADAM) + decay * weight)
    return weight_next, mean_next, square_next


def shards(
    tokens, cotangent, parents, token_segment, tree_id,
    projection_weight, projection_first_moment, projection_second_moment,
    merge_master, merge_mean, merge_square,
    expand_master, expand_mean, expand_square,
    shrink_master, shrink_mean, shrink_square,
    gain_master, gain_mean, gain_square,
):
    x = tokens[0]
    dy = cotangent[0]
    length, d = x.shape
    d_own, kv, per, n = projection_weight.shape
    group = per - 2
    units = expand_master.shape[2]
    scale = n ** (-0.5)
    unit = scale * math.log2(math.e)
    line = 4 if lax.axis_size("dp") == 8 and d_own % LANES == 0 else 0
    if line:
        masters = (projection_weight.reshape(d_own, kv * per, n), merge_master, expand_master, shrink_master)
    else:
        wp, we = (lax.all_gather(w.astype(BF).reshape(d_own, -1), "dp", axis=0, tiled=True)
                  for w in (projection_weight, expand_master))
        wm, ws = (lax.all_gather(w.astype(BF), "dp", axis=1, tiled=True) for w in (merge_master, shrink_master))
        masters = (wp,)

    gains = gain_master[None]
    fronts = front(x, gains, token_segment, parents, tree_id, masters, kv, group, line)
    xn1, q, k, v, kt, vt, raw, tags, bars, cosines, sines = fronts[:11]
    if line:
        wp, wm, *low = fronts[11:]
    else:
        low = (we, ws)
    ctx, lse, base, other, gate_sum, up_grad, dh, dhb, dg2, shrink_sum = middle(
        q, k, vt, tags, bars, wm, x, dy, gains, low, kv, group, unit, line)
    backs = back(q, k, v, kt, tags, bars, lse, ctx, dhb, wm, wp, raw, cosines, sines, gains, xn1,
                 base, dg2, other, x, dh, (gate_sum, up_grad) if line else (), kv, group, unit, scale, line)
    input_grad, output, gain_rows = backs[:3]
    if line:
        expand_sum, merge_sum, project_sum = backs[3:]
    else:
        gain_rows = lax.psum(gain_rows, ("dp", "tensor"))
        project_sum, expand_sum = (
            lax.psum_scatter(g, "dp", scatter_dimension=0, tiled=True) for g in (backs[3], jnp.concatenate([gate_sum, up_grad], axis=1)))
        merge_sum, shrink_sum = (
            lax.psum_scatter(g, "dp", scatter_dimension=1, tiled=True) for g in (backs[4], shrink_sum))
    output, input_grad = output[None], input_grad[None]
    gain_grad = gain_rows.reshape(-1)[:gain_master.shape[0]]

    outs = [output, input_grad]
    for weight, mean, square, grad, rate in (
        (projection_weight, projection_first_moment, projection_second_moment, project_sum, RATE_PROJECT),
        (merge_master, merge_mean, merge_square, merge_sum, RATE_MERGE),
        (expand_master, expand_mean, expand_square, expand_sum, RATE_EXPAND),
        (shrink_master, shrink_mean, shrink_square, shrink_sum, RATE_SHRINK),
    ):
        grad = grad.astype(FP).reshape(weight.shape)
        after, mean_next, square_next = adamw_step(weight, mean, square, grad, rate, DECAY)
        outs += [after, mean_next, square_next, after.astype(BF)]
    gain_next, gain_mean_next, gain_square_next = adamw_step(
        gain_master, gain_mean, gain_square, gain_grad, RATE_GAIN, 0.0)
    return (*outs, gain_mean_next, gain_square_next, gain_next)


def solution(mesh):
    tokens = P("dp", None, None)
    project = P("dp", "tensor", None, None)
    columns = P("tensor", "dp")
    expand = P("dp", None, "tensor")
    shared = P("dp", "tensor", None)
    return jax.shard_map(
        shards,
        mesh=mesh,
        in_specs=(tokens, tokens, P(), P("dp", None), P("dp"), *[project] * 3, *[columns] * 3, *[expand] * 3,
                  *[columns] * 3, P(), P(), P()),
        out_specs=(shared, shared, *[project] * 4, *[columns] * 4, *[expand] * 4, *[columns] * 4, P(), P(), P()),
        check_vma=False,
    )
```

```python
import math
from functools import partial

import jax
import jax.numpy as jnp
import numpy as np
from jax import lax
from jax.experimental import pallas as pl
from jax.experimental.pallas import tpu as pltpu
from jax.sharding import PartitionSpec as P

STEP = 5
EPS_NORM = 1e-06
THETA = 1000000.0
BETA_ONE = 0.5
BETA_TWO = 0.5
EPS_ADAM = 1e-08
DECAY = 0.1
RATE_PROJECT = 0.05
RATE_MERGE = 0.3
RATE_EXPAND = 0.05
RATE_SHRINK = 0.03
RATE_GAIN = 0.3

BF = jnp.bfloat16
FP = jnp.float32
ROWS = 256
LANES = 128
SUB = 128
MESH = pl.DeviceIdType.MESH
BLOCKED = -1e30
VMEM_LIMIT = 56 * 2**20


def params(**more):
    return pltpu.CompilerParams(vmem_limit_bytes=VMEM_LIMIT, **more)


def dot(a, b, ca=1, cb=0):
    return lax.dot_general(a, b, (((ca,), (cb,)), ((), ())), preferred_element_type=FP)


def inverse_rms(values):
    return lax.rsqrt(jnp.mean(values * values, axis=-1, keepdims=True) + EPS_NORM)


def rms_pull(values, scales, grad):
    r = inverse_rms(values)
    scaled = grad * scales
    mean = jnp.mean(values * scaled, axis=-1, keepdims=True)
    return r * scaled - values * (r * r * r * mean), grad * values * r


def fold_rows(values):
    n, w = values.shape
    return jnp.sum(values.reshape(n // 8, 8, w), axis=0)


class Place:
    def __init__(self, line):
        self.line = line
        self.dp, self.t = lax.axis_index("dp"), lax.axis_index("tensor")
        self.z, self.y = self.dp // 2, self.dp % 2
        self.x, self.c = self.t // 2, self.t % 2
        self.has_up, self.has_down = self.z < line - 1, self.z > 0
        self.up, self.down = (self.dp + 2, self.t), (self.dp - 2, self.t)
        self.across = (self.dp + 1 - 2 * self.y, self.t)
        self.sibling = (self.dp, self.t + 1 - 2 * self.c)
        self.chip = (self.dp, (1 - self.x) * 2 + self.c)

    def greet(self, tensor, line, meanwhile=None):
        barrier = pltpu.get_barrier_semaphore()

        def signal(device):
            pl.semaphore_signal(barrier, inc=1, device_id=device, device_id_type=MESH)

        if tensor:
            signal(self.sibling)
            signal(self.chip)
        if line:
            signal(self.across)
            pl.when(self.has_up)(lambda: signal(self.up))
            pl.when(self.has_down)(lambda: signal(self.down))
        peers = (2 if tensor else 0) + (1 if line else 0)
        if line:
            peers = peers + jnp.where(self.has_up, 1, 0) + jnp.where(self.has_down, 1, 0)
        if meanwhile is not None:
            meanwhile()
        pl.semaphore_wait(barrier, peers)


def send(src, dst, sent, arrived, device):
    return pltpu.make_async_remote_copy(
        src_ref=src, dst_ref=dst, send_sem=sent, recv_sem=arrived, device_id=device, device_id_type=MESH)


def row_cut(size, columns=slice(None)):
    return lambda j: (pl.ds(pl.multiple_of(j * size, size), size), columns)


def column_cut(size):
    return lambda j: (slice(None), pl.ds(pl.multiple_of(j * size, size), size))


class Gather:
    def __init__(self, place, own, full, cut, sems, local):
        self.place, self.own, self.full, self.cut, self.sems, self.local = place, own, full, cut, sems, local

    def copy(self, kind, src, j):
        p = self.place
        device = (p.up, p.down, p.across)[kind]
        return send(src, self.full.at[self.cut(j)], self.sems.at[kind, j], self.sems.at[3, j], device)

    def kept(self):
        return pltpu.make_async_copy(self.own, self.full.at[self.cut(self.place.dp)], self.local)

    def source(self):
        return self.full.at[self.cut(self.place.dp)] if self.own is None else self.own

    def start(self):
        p = self.place
        self.copy(2, self.source(), p.dp).start()
        pl.when(p.has_up)(lambda: self.copy(0, self.source(), p.dp).start())
        pl.when(p.has_down)(lambda: self.copy(1, self.source(), p.dp).start())
        if self.own is not None:
            self.kept().start()

    def arrivals(self, k):
        p = self.place
        return ((0, p.z >= k, (p.z - k) * 2 + p.y, p.has_up), (1, p.z + k < p.line, (p.z + k) * 2 + p.y, p.has_down))

    def hop(self, k):
        for kind, here, j, further in self.arrivals(k):
            @pl.when(here)
            def _(kind=kind, j=j, further=further):
                piece = self.full.at[self.cut(j)]
                self.copy(kind, piece, j).wait_recv()
                pl.when(further)(lambda: self.copy(kind, piece, j).start())
                self.copy(2, piece, j).start()

    def finish(self):
        p = self.place
        if self.own is not None:
            self.kept().wait()
        for zz in range(p.line):
            j = zz * 2 + 1 - p.y
            self.copy(2, self.full.at[self.cut(j)], j).wait_recv()

    def drain(self):
        p = self.place
        self.copy(2, self.source(), p.dp).wait_send()
        pl.when(p.has_up)(lambda: self.copy(0, self.source(), p.dp).wait_send())
        pl.when(p.has_down)(lambda: self.copy(1, self.source(), p.dp).wait_send())
        for k in range(1, p.line):
            for kind, here, j, further in self.arrivals(k):
                @pl.when(here)
                def _(kind=kind, j=j, further=further):
                    piece = self.full.at[self.cut(j)]
                    pl.when(further)(lambda: self.copy(kind, piece, j).wait_send())
                    self.copy(2, piece, j).wait_send()


class Reduce:
    def __init__(self, place, grad, cut, kept, across, lined, sems):
        self.place, self.grad, self.cut, self.kept, self.sems = place, grad, cut, kept, sems
        self.across, self.lined = across, lined

    def cross(self, zz):
        p = self.place
        return send(self.grad.at[self.cut(zz * 2 + 1 - p.y)], self.across.at[zz],
                    self.sems.at[0, zz], self.sems.at[1, zz], p.across)

    def climb(self, t):
        return send(self.across.at[t], self.lined.at[t + 1], self.sems.at[2, t], self.sems.at[3, t], self.place.up)

    def sink(self, t):
        return send(self.across.at[t], self.lined.at[t], self.sems.at[4, t], self.sems.at[5, t], self.place.down)

    def load(self, zz):
        return pltpu.make_async_copy(self.grad.at[self.cut(zz * 2 + self.place.y)], self.kept.at[zz], self.sems.at[6, zz])

    def mine(self, zz):
        if self.kept is None:
            return self.grad[self.cut(zz * 2 + self.place.y)].astype(FP)
        return self.kept[zz].astype(FP)

    def loaded(self, zz):
        if self.kept is not None:
            self.load(zz).wait()

    def turn(self, q):
        z = self.place.z
        low = z < 2
        if q == 0:
            return jnp.where(low, 3, 0)
        if q == 1:
            return jnp.where(low, 2, 1)
        if q == 2:
            return jnp.where(low, 1 - z, 5 - z)
        return z

    def start(self):
        self.cross(self.turn(0)).start()
        if self.kept is not None:
            for zz in range(self.place.line):
                self.load(zz).start()

    def advance(self, q):
        self.cross(self.turn(q - 1)).wait_send()
        self.cross(self.turn(q)).start()

    def hop(self, h):
        p = self.place

        def pass_on(t, coming, more, slot):
            self.loaded(t)
            self.cross(t).wait_recv()

            @pl.when(jnp.logical_not(more))
            def _():
                self.across[t] = (self.mine(t) + self.across[t].astype(FP)).astype(BF)

            @pl.when(more)
            def _():
                coming(t).wait_recv()
                self.across[t] = (self.mine(t) + self.across[t].astype(FP) + self.lined[slot].astype(FP)).astype(BF)

            coming(t).start()

        pl.when(p.z < h)(lambda: pass_on(p.z + p.line - h, self.climb, p.has_down, p.z + p.line - h + 1))
        pl.when(p.z >= p.line - h)(lambda: pass_on(p.z - p.line + h, self.sink, p.has_up, p.z - p.line + h))

    def finish(self, write):
        p = self.place
        self.loaded(p.z)
        self.cross(p.z).wait_recv()
        pl.when(p.has_down)(lambda: self.climb(p.z).wait_recv())
        pl.when(p.has_up)(lambda: self.sink(p.z).wait_recv())
        from_below = jnp.where(p.has_down, self.lined[p.z + 1].astype(FP), 0.0)
        from_above = jnp.where(p.has_up, self.lined[p.z].astype(FP), 0.0)
        write(self.mine(p.z) + self.across[p.z].astype(FP) + from_below + from_above)

    def step(self, k):
        self.advance(k)
        self.hop(k)

    def drain(self):
        p = self.place
        self.cross(p.z).wait_send()
        for zz in range(p.line):
            pl.when(zz > p.z)(lambda zz=zz: self.climb(zz).wait_send())
            pl.when(zz < p.z)(lambda zz=zz: self.sink(zz).wait_send())


def write_to(ref, first=0):
    def write(values):
        if len(ref.shape) == 2:
            ref[...] = values
            return
        width = ref.shape[2]
        for j in range(values.shape[1] // width):
            ref[:, first + j, :] = values[:, j * width:(j + 1) * width]

    return write


def reduce_scratch(line, shape, kept=False):
    return [pltpu.VMEM((line, *shape), BF)] * kept + [pltpu.VMEM((line, *shape), BF), pltpu.VMEM((line + 1, *shape), BF),
                                                      pltpu.SemaphoreType.DMA((7, line))]


class Pairs:
    def __init__(self, place, per, held, near, sems, slot_of):
        self.place, self.per, self.held, self.near, self.sems, self.slot_of = place, per, held, near, sems, slot_of

    def near_slot(self, s):
        return (s // (2 * self.per)) * self.per + s % self.per

    def to_sibling(self, s):
        return send(self.held.at[self.slot_of(s)], self.near.at[self.near_slot(s)], self.sems.at[0, s],
                    self.sems.at[1, s], self.place.sibling)

    def sends(self, s):
        return self.place.c != (s // self.per) % 2

    def sent(self, s):
        pl.when(self.sends(s))(lambda: self.to_sibling(s).wait_send())

    def put(self, s, rows, before=None):
        if before is not None:
            pl.when(before[0])(lambda: self.sent(before[1]))
        self.held[self.slot_of(s)] = rows
        pl.when(self.sends(s))(lambda: self.to_sibling(s).start())

    def put_next(self, s, rows):
        self.put(s, rows, (s % self.per >= 1, s - 1))

    def add(self, s, use):
        t = s // self.per

        @pl.when(self.place.c == t % 2)
        def _():
            self.to_sibling(s).wait_recv()
            use(self.place.x == t // 2, s % self.per,
                self.held[self.slot_of(s)].astype(FP) + self.near[self.near_slot(s)].astype(FP))


class Exchange(Pairs):
    def __init__(self, place, per, held, near, far, total, sems):
        super().__init__(place, per, held, near, sems, lambda s: s // per)
        self.far, self.total = far, total

    def rows(self, k):
        return pl.ds(pl.multiple_of(k * SUB, SUB), SUB)

    def to_chip(self, s):
        return send(self.near.at[self.near_slot(s)], self.far.at[s % self.per], self.sems.at[2, s], self.sems.at[3, s],
                    self.place.chip)

    def add_chip(self, s):
        def use(mine, k, summed):
            @pl.when(jnp.logical_not(mine))
            def _():
                self.near[self.near_slot(s)] = summed.astype(BF)
                self.to_chip(s).start()

            @pl.when(mine)
            def _():
                self.total[self.rows(k), :] = summed

        self.add(s, use)

    def take(self, s, use):
        @pl.when(s // self.per == self.place.t)
        def _():
            k = s % self.per
            self.to_chip(s).wait_recv()
            use(s, self.rows(k), self.total[self.rows(k), :] + self.far[k].astype(FP))

    def drain(self):
        p = self.place

        def one(s, carry):
            t = s // self.per
            pl.when(s % self.per == self.per - 1)(lambda: self.sent(s))
            pl.when(jnp.logical_and(p.c == t % 2, p.x != t // 2))(lambda: self.to_chip(s).wait_send())
            return carry

        lax.fori_loop(0, 4 * self.per, one, 0)


def pair_of(step, per):
    t = step % 2
    return t * per + step // 2, (3 - t) * per + step // 2


def pairs_scratch(per, d, exchange):
    rows = [pltpu.VMEM((4, SUB, d), BF), pltpu.VMEM((2 * per, SUB, d), BF)]
    return rows + [pltpu.VMEM((per, SUB, d), BF)] * exchange + [pltpu.SemaphoreType.DMA((4 if exchange else 2, 4 * per))]


class Spread:
    def __init__(self, place, per, stage, full, sems):
        self.place, self.per, self.stage, self.full, self.sems = place, per, stage, full, sems

    def rows(self, s):
        return self.full.at[pl.ds(pl.multiple_of(s * SUB, SUB), SUB), :]

    def source(self, s):
        return self.rows(s) if self.stage is None else self.stage.at[s % self.per]

    def copy(self, kind, src, s):
        device = (self.place.chip, self.place.sibling)[kind]
        return send(src, self.rows(s), self.sems.at[kind, s], self.sems.at[2, s], device)

    def kept(self, s):
        return pltpu.make_async_copy(self.source(s), self.rows(s), self.sems.at[3, s])

    def send(self, s):
        for kind in (0, 1):
            self.copy(kind, self.source(s), s).start()
        if self.stage is not None:
            self.kept(s).start()

    def owns(self, s):
        return s // self.per == self.place.t

    def passes(self, s):
        t = s // self.per
        return jnp.logical_and(self.place.c == t % 2, self.place.x != t // 2)

    def pass_on(self, s):
        @pl.when(self.passes(s))
        def _():
            self.copy(1, self.rows(s), s).wait_recv()
            self.copy(1, self.rows(s), s).start()

    def ready(self, s):
        if self.stage is not None:
            pl.when(self.owns(s))(lambda: self.kept(s).wait())
        pl.when((s // self.per) % 2 != self.place.c)(lambda: self.copy(1, self.rows(s), s).wait_recv())

    def drain(self):
        def one(s, carry):
            @pl.when(self.owns(s))
            def _():
                self.copy(0, self.source(s), s).wait_send()
                self.copy(1, self.source(s), s).wait_send()

            pl.when(self.passes(s))(lambda: self.copy(1, self.rows(s), s).wait_send())
            return carry

        lax.fori_loop(0, 4 * self.per, one, 0)


def whole(shape):
    return pl.BlockSpec(tuple(shape), lambda i: (0,) * len(shape), pipeline_mode=pl.Buffered(1))


ANYWHERE = pl.BlockSpec(memory_space=pl.ANY)
GATHER_SEMS = lambda shards: [pltpu.SemaphoreType.DMA((4, shards)), pltpu.SemaphoreType.DMA]


def make_tables(seg_ref, parents_ref, tree_ref, freq_ref, tags_ref, bars_ref, cos_ref, sin_ref):
    count = parents_ref.shape[1]
    n = LANES
    blocks = sin_ref.shape[0] // ROWS
    lane = lax.broadcasted_iota(jnp.int32, (1, n), 1).astype(FP)
    place_of = lambda b: pl.ds(pl.multiple_of(b * ROWS, ROWS), ROWS)

    def columns(b, carry):
        sin_ref[place_of(b), :] = jnp.broadcast_to(seg_ref[:, place_of(b)].astype(FP), (n, ROWS)).T
        return carry

    def tally(b, carry):
        column = sin_ref[place_of(b), :]
        return (carry[0] + fold_rows(jnp.where(column == lane, 1.0, 0.0)),
                carry[1] + fold_rows(jnp.where(column < lane, 1.0, 0.0)))

    lax.fori_loop(0, blocks, columns, 0)
    sizes, starts = lax.fori_loop(0, blocks, tally, (jnp.zeros((8, n), FP), jnp.zeros((8, n), FP)))
    sizes, starts = (jnp.sum(a, axis=0, keepdims=True) for a in (sizes, starts))
    table = parents_ref[...]
    chosen = jnp.where(lax.broadcasted_iota(jnp.int32, table.shape, 0) == tree_ref[0], table, 0)
    chosen = jnp.sum(chosen.astype(FP), axis=0, keepdims=True)
    parents = jnp.zeros((1, n), FP)
    for b in range(count):
        parents = jnp.where(lane == b, chosen[:, b:b + 1], parents)
    shifts = jnp.where(lane != 0, sizes[:, :1], 0.0) - starts

    def rows(b, carry):
        at = place_of(b)
        column = sin_ref[at, :]
        hot = column == lane
        parent = jnp.sum(jnp.where(hot, parents, 0.0), axis=1, keepdims=True)
        above = jnp.where(jnp.logical_and(lane == parent, lane != 0), sizes, 0.0)
        first = (b * ROWS).astype(FP)
        position = (lax.broadcasted_iota(jnp.int32, (ROWS, 1), 0).astype(FP) + first
                    + jnp.sum(jnp.where(hot, shifts, 0.0) + above, axis=1, keepdims=True))
        tags_ref[at, :] = jnp.where(hot, 1.0, 0.0).astype(BF)
        open_to = jnp.logical_or(jnp.logical_or(hot, lane == parent), jnp.logical_or(lane == 0, lane >= count))
        bars_ref[at, :] = jnp.where(open_to, 0.0, BLOCKED).astype(BF)
        angles = position * freq_ref[...]
        cos_ref[at, :] = jnp.cos(angles)
        turned = jnp.sin(angles)
        sin_ref[at, :] = jnp.where(lane < n // 2, -turned, turned)
        return carry

    lax.fori_loop(0, blocks, rows, 0)


def front_kernel(kv, group, line, *refs):
    refs = list(refs)
    take = lambda count: [refs.pop(0) for _ in range(count)]
    x_ref, gains_ref, seg_ref, parents_ref, tree_ref, freq_ref = take(6)
    masters = take(4) if line else take(1)
    xn_ref, q_ref, k_ref, v_ref, kt_ref, vt_ref, raw_ref, tags_ref, bars_ref, cos_ref, sin_ref = take(11)
    if line:
        wp_out, wm_out, we_low, ws_low = take(4)
        wp_ref, wm_low, p_sems, p_local, m_sems, m_local, out_sem = take(7)
    else:
        wp_ref = masters[0]
    xn_full, xn_sem = take(2)
    i = pl.program_id(0)
    final = pl.num_programs(0) - 1
    d = x_ref.shape[1]
    n = LANES
    per = group + 2
    if line:
        place = Place(line)
        size = masters[0].shape[0]
        project = Gather(place, None, wp_ref, row_cut(size), p_sems, p_local)
        merge = Gather(place, wm_low, wm_out, column_cut(wm_low.shape[1]), m_sems, m_local)
        written = pltpu.make_async_copy(wp_ref, wp_out, out_sem)
    normed = pltpu.make_async_copy(xn_full, xn_ref, xn_sem)

    def round_projection():
        at = pl.ds(pl.multiple_of(place.dp * size, size), size)
        for j in range(kv * per):
            wp_ref[at, j * n:(j + 1) * n] = masters[0][:, j, :].astype(BF)

    def norm(b, carry):
        at = pl.ds(pl.multiple_of(b * ROWS, ROWS), ROWS)
        x = x_ref[at, :].astype(FP)
        xn_full[at, :] = (x * inverse_rms(x) * gains_ref[:, :d]).astype(BF)
        return carry

    @pl.when(i == 0)
    def _():
        if line:
            place.greet(False, True, round_projection)
            project.start()
        lax.fori_loop(0, x_ref.shape[0] // ROWS, norm, 0)
        normed.start()
        if line:
            project.hop(1)
        make_tables(seg_ref, parents_ref, tree_ref, freq_ref, tags_ref, bars_ref, cos_ref, sin_ref)
        if line:
            project.hop(2)
            wm_low[...] = masters[1][...].astype(BF)
            units = masters[2].shape[2]
            for half in range(2):
                we_low[:, half * units:(half + 1) * units] = masters[2][:, half, :].astype(BF)
            ws_low[...] = masters[3][...].astype(BF)
            project.hop(3)
            merge.start()
            project.finish()
            written.start()

    if line:
        for k in range(1, line):
            pl.when(i == k + 1)(lambda k=k: merge.hop(k))
    at = pl.ds(pl.multiple_of(i * ROWS, ROWS), ROWS)
    qkv = dot(xn_full[at, :], wp_ref[...])
    cosines, sines = cos_ref[at, :], sin_ref[at, :]
    gq, gk = gains_ref[:, 2 * d:2 * d + n], gains_ref[:, 2 * d + n:]
    keys, values = [], []
    for h in range(kv):
        for c in range(group + 1):
            raw = qkv[:, (h * per + c) * n:(h * per + c + 1) * n]
            to = (h * (group + 1) + c) * n
            raw_ref[:, to:to + n] = raw
            y = raw * inverse_rms(raw) * (gq if c < group else gk)
            turned = y * cosines + pltpu.roll(y, n // 2, 1) * sines
            if c < group:
                to = (h * group + c) * n
                q_ref[:, to:to + n] = turned.astype(BF)
            else:
                keys.append(turned)
        values.append(qkv[:, (h * per + group + 1) * n:(h * per + group + 2) * n])
    for h in range(kv):
        k_ref[:, h * n:(h + 1) * n] = keys[h].astype(BF)
        v_ref[:, h * n:(h + 1) * n] = values[h].astype(BF)
        kt_ref[h * n:(h + 1) * n, :] = keys[h].T.astype(BF)
        vt_ref[h * n:(h + 1) * n, :] = values[h].T.astype(BF)

    @pl.when(i == final)
    def _():
        normed.wait()
        if line:
            merge.finish()
            merge.drain()
            project.drain()
            written.wait()


def front(x, gains, segments, parents, tree, masters, kv, group, line):
    length, d = x.shape
    n = LANES
    rows = lambda w: pl.BlockSpec((ROWS, w), lambda i: (i, 0))
    cols = pl.BlockSpec((kv * n, ROWS), lambda i: (0, i))
    out = lambda w, t: jax.ShapeDtypeStruct((length, w), t)
    raw_w = kv * (group + 1) * n
    freq = np.float32(THETA ** (-(np.arange(n) % (n // 2)) * 2.0 / n))[None]
    more_specs, more_shapes, scratch = [], [], []
    if line:
        shards = 2 * line
        project, merge, expand, shrink = (m.shape for m in masters)
        wp_shape = (project[0] * shards, project[1] * n)
        more_shapes = [jax.ShapeDtypeStruct(wp_shape, BF), jax.ShapeDtypeStruct((merge[0], merge[1] * shards), BF),
                       jax.ShapeDtypeStruct((expand[0], 2 * expand[2]), BF), jax.ShapeDtypeStruct(shrink, BF)]
        more_specs = [ANYWHERE, ANYWHERE, whole(more_shapes[2].shape), whole(more_shapes[3].shape)]
        scratch = [pltpu.VMEM(wp_shape, BF), pltpu.VMEM(merge, BF), *GATHER_SEMS(shards), *GATHER_SEMS(shards),
                   pltpu.SemaphoreType.DMA]
    table = whole((length, n))
    return pl.pallas_call(
        partial(front_kernel, kv, group, line),
        grid=(length // ROWS,),
        in_specs=[whole(x.shape), whole(gains.shape), whole(segments.shape), whole(parents.shape),
                  pl.BlockSpec(memory_space=pltpu.SMEM), whole(freq.shape), *[whole(m.shape) for m in masters]],
        out_specs=[ANYWHERE, rows(kv * group * n), rows(kv * n), rows(kv * n), cols, cols, rows(raw_w),
                   table, table, table, table, *more_specs],
        out_shape=[out(d, BF), out(kv * group * n, BF), out(kv * n, BF), out(kv * n, BF),
                   jax.ShapeDtypeStruct((kv * n, length), BF), jax.ShapeDtypeStruct((kv * n, length), BF),
                   out(raw_w, FP), out(n, BF), out(n, BF), out(n, FP), out(n, FP), *more_shapes],
        scratch_shapes=[*scratch, pltpu.VMEM((length, d), BF), pltpu.SemaphoreType.DMA],
        compiler_params=params(**({"collective_id": 0, "has_side_effects": True} if line else {})),
        name="front",
    )(x, gains, segments, parents, tree, freq, *masters)


def stacked(ref_block, h, group):
    n = LANES
    return jnp.concatenate(
        [ref_block[:, (h * group + g) * n:(h * group + g + 1) * n] for g in range(group)], axis=0)


def causal_tile(group, rows=ROWS, after=0):
    key_at = lax.broadcasted_iota(jnp.int32, (ROWS, rows * group), 0)
    query_at = lax.broadcasted_iota(jnp.int32, (ROWS, rows * group), 1) % rows
    return key_at <= query_at + after


def in_turn(i, first, steps, per, acts):
    for behind, act in acts:
        @pl.when(jnp.logical_and(i - first - behind >= 0, i - first - behind < steps))
        def _(behind=behind, act=act):
            for s in pair_of(i - first - behind, per):
                act(s)


def middle_kernel(kv, group, unit, line, per, steps, *refs):
    refs = list(refs)
    take = lambda count: [refs.pop(0) for _ in range(count)]
    q_ref, k_ref, vt_ref, tags_ref, bars_ref, wm_ref, gains_ref, x_all, dy_all = take(9)
    weights = take(2)
    ctx_out, lse_ref, base_ref, other_ref, gate_out, up_out, dh_ref, dhb_ref, dg_ref, gsh_out = take(10)
    acc_ref, sum_ref, x_ref, dy_ref, we_ref, ws_ref, copy_sems = take(7)
    h_ref, xn_ref, a_ref, dgu_ref, ctx_ref, gup_ref = take(6)
    h_held, h_near, h_far, h_sems, xn_sems = take(5)
    d_held, d_near, d_far, d_sems, stage, dh_sems = take(6)
    b_held, b_near, b_sems = take(3)
    place = Place(line)
    i = pl.program_id(0)
    n = LANES
    share, d = x_ref.shape
    units = ws_ref.shape[0]
    tile = 256
    attended = Exchange(place, per, h_held, h_near, h_far, h_ref, h_sems)
    norms = Spread(place, per, None, xn_ref, xn_sems)
    pulled_back = Exchange(place, per, d_held, d_near, d_far, dh_ref, d_sems)
    grads = Spread(place, per, stage, dhb_ref, dh_sems)
    branch = Pairs(place, per, b_held, b_near, b_sems, lambda s: s // per)
    own_share = x_all.at[pl.ds(pl.multiple_of(place.t * share, share), share), :]
    copies = [pltpu.make_async_copy(own_share, x_ref, copy_sems.at[0]),
              pltpu.make_async_copy(dy_all, dy_ref, copy_sems.at[1])]
    if line:
        gsh_ref = take(1)[0]
        shrink = Reduce(place, gsh_ref, column_cut(gsh_ref.shape[1] // (2 * line)), None, *take(3))
        gate_ref = take(1)[0]
        expand = Reduce(place, gate_ref, row_cut(gate_ref.shape[0] // (2 * line)), None, *take(3))
        cuts = (row_cut(weights[0].shape[0]), column_cut(weights[1].shape[1]))
        first, second = [Gather(place, weights[w], (we_ref, ws_ref)[w], cuts[w], *take(2)) for w in range(2)]
    else:
        gsh_ref, gate_ref = gsh_out, gate_out
        copies += [pltpu.make_async_copy(weights[0], we_ref, copy_sems.at[2]),
                   pltpu.make_async_copy(weights[1], ws_ref, copy_sems.at[3])]
    written = [pltpu.make_async_copy(ctx_ref, ctx_out, copy_sems.at[4]),
               pltpu.make_async_copy(gup_ref, up_out, copy_sems.at[5])]
    rows_of = lambda s: pl.ds(pl.multiple_of(s * SUB, SUB), SUB)

    def at_step(step, *acts):
        @pl.when(i == step)
        def _():
            for act in acts:
                act()

    @pl.when(i == 0)
    def _():
        place.greet(True, bool(line))
        if line:
            first.start()
        for copy in copies:
            copy.start()
        dg_ref[...] = jnp.zeros_like(dg_ref)


    def block(s):
        here = rows_of(s)
        bars = jnp.concatenate([bars_ref[here, :]] * group, axis=0)
        q = q_ref[here, :]
        wide = [jnp.concatenate([stacked(q, h, group), bars], axis=1) for h in range(kv)]
        acc_ref[...] = jnp.zeros_like(acc_ref)
        sum_ref[...] = jnp.zeros_like(sum_ref)

        def chunk(j, diagonal):
            at = pl.ds(pl.multiple_of(j * ROWS, ROWS), ROWS)
            tags = tags_ref[at, :]
            for h in range(kv):
                keys = jnp.concatenate([k_ref[at, h * n:(h + 1) * n], tags], axis=1)
                scores = dot(keys, wide[h], 1, 1)
                e = jnp.exp2(scores * unit)
                if diagonal:
                    e = jnp.where(causal_tile(group, SUB, (s % 2) * SUB), e, 0.0)
                sum_ref[h] += fold_rows(e)
                acc_ref[h] += dot(vt_ref[h * n:(h + 1) * n, at], e.astype(BF))

        lax.fori_loop(0, s // 2, lambda j, c: (chunk(j, False), c)[1], 0)
        chunk(s // 2, True)
        parts = []
        for h in range(kv):
            sums = jnp.sum(sum_ref[h], axis=0, keepdims=True)
            lse_ref[s, h:h + 1, :] = jnp.log2(sums)
            ctx = (acc_ref[h] / sums).T
            parts += [ctx[g * SUB:(g + 1) * SUB] for g in range(group)]
        ctx_ref[here, :] = jnp.concatenate(parts, axis=1).astype(BF)

    def put_pair(pairs, blocks, part):
        for u, s in enumerate(blocks):
            pairs.put_next(s, part[u * SUB:(u + 1) * SUB])

    @pl.when(i < steps)
    def _():
        blocks = pair_of(i, per)
        for s in blocks:
            block(s)
        ctx = jnp.concatenate([ctx_ref[rows_of(s), :] for s in blocks], axis=0)
        put_pair(attended, blocks, dot(ctx, wm_ref[...]).astype(BF))

    def hidden_rows(s, at, summed):
        hidden = x_ref[at, :].astype(FP) + summed
        h_ref[at, :] = hidden
        xn_ref[rows_of(s), :] = (hidden * inverse_rms(hidden) * gains_ref[:, d:2 * d]).astype(BF)
        norms.send(s)

    at_step(1, copies[0].wait)
    at_step(steps, written[0].start)
    in_turn(i, 0, steps, per, ((1, attended.add_chip), (3, lambda s: attended.take(s, hidden_rows)), (5, norms.pass_on)))
    swiglu, feed = steps + 3, 2 * steps + 3
    if line:
        at_step(1, lambda: first.hop(1))
        at_step(3, lambda: first.hop(2))
        at_step(5, lambda: first.hop(3), second.start)
        at_step(7, lambda: second.hop(1))
        at_step(8, lambda: second.hop(2))
        at_step(9, lambda: second.hop(3), first.finish)
        at_step(feed, second.finish)
    else:
        at_step(swiglu, copies[2].wait, copies[3].wait)


    def gathered(ref, blocks):
        return jnp.concatenate([ref[rows_of(s), :] for s in blocks], axis=0)

    def keep(ref, blocks, values):
        for u, s in enumerate(blocks):
            ref[rows_of(s), :] = values[u * SUB:(u + 1) * SUB]

    def tiles(grad_ref, left_ref, right_ref, start, count, after):
        def one(t, carry):
            cut = pl.ds(pl.multiple_of(t * tile, tile), tile)
            there = pl.ds(pl.multiple_of((t + after) * tile, tile), tile)
            grad_ref[:, cut] = dot(left_ref[...], right_ref[:, there], 0, 0).astype(grad_ref.dtype)
            return carry

        lax.fori_loop(start, start + count, one, 0)

    @pl.when(jnp.logical_and(i >= swiglu, i < feed))
    def _():
        blocks = pair_of(i - swiglu, per)
        for s in blocks:
            norms.ready(s)
        gu = dot(gathered(xn_ref, blocks), we_ref[...])
        gate, up = gu[:, :units], gu[:, units:]
        keep(a_ref, blocks, (gate / (1.0 + jnp.exp(-gate)) * up).astype(BF))
        keep(dgu_ref, blocks, gu.astype(BF))

    at_step(feed - 1, copies[1].wait, lambda: tiles(gsh_ref, a_ref, dy_ref, 0, gsh_ref.shape[1] // tile, 0))
    if line:
        at_step(feed, shrink.start)

    @pl.when(jnp.logical_and(i >= feed, i < feed + steps))
    def _():
        blocks = pair_of(i - feed, per)
        gu = gathered(dgu_ref, blocks).astype(FP)
        gate, up = gu[:, :units], gu[:, units:]
        sig = 1.0 / (1.0 + jnp.exp(-gate))
        da = dot(gathered(dy_ref, blocks), ws_ref[...], 1, 1)
        dgu = jnp.concatenate([da * up * (sig * (1.0 + gate * (1.0 - sig))), da * (gate * sig)], axis=1).astype(BF)
        keep(dgu_ref, blocks, dgu)
        put_pair(pulled_back, blocks, dot(dgu, we_ref[...], 1, 1).astype(BF))

    def grad_rows(s, at, summed):
        pulled, gain_grad = rms_pull(h_ref[at, :], gains_ref[:, d:2 * d], summed)
        dh = dy_ref[rows_of(s), :].astype(FP) + pulled
        dh_ref[at, :] = dh
        dg_ref[...] += fold_rows(gain_grad)
        stage[s % per] = dh.astype(BF)
        grads.send(s)

    def chip_rows(mine, k, summed):
        at = rows_of(k)

        @pl.when(mine)
        def _():
            base_ref[at, :] = h_ref[at, :] + summed

        @pl.when(jnp.logical_not(mine))
        def _():
            other_ref[k] = summed.astype(BF)

    in_turn(i, feed, steps, per, ((1, pulled_back.add_chip), (3, lambda s: pulled_back.take(s, grad_rows)),
                                  (5, grads.pass_on)))

    @pl.when(jnp.logical_and(i >= feed + 3, i < feed + 3 + steps))
    def _():
        blocks = pair_of(i - feed - 3, per)
        put_pair(branch, blocks, dot(gathered(a_ref, blocks), ws_ref[...]).astype(BF))

    in_turn(i, feed, steps, per, ((4, lambda s: branch.add(s, chip_rows)),))
    if line:
        for k, step in enumerate((2, 4, 5), 1):
            at_step(feed + step, lambda k=k: shrink.step(k))
    half = units // tile
    at_step(feed + steps, lambda: tiles(gate_ref, xn_ref, dgu_ref, 0, half, 0))
    if line:
        at_step(feed + steps, expand.start)
        for k in range(1, line):
            at_step(feed + steps + k, lambda k=k: expand.step(k))
    at_step(feed + steps + 1, lambda: tiles(gup_ref, xn_ref, dgu_ref, 0, half, half), written[1].start)

    @pl.when(i == feed + steps + 4)
    def _():
        attended.drain()
        pulled_back.drain()
        norms.drain()
        grads.drain()
        for t in range(4):
            branch.sent(t * per + per - 1)
        lax.fori_loop(0, 4 * per, lambda s, c: (grads.ready(s), c)[1], 0)
        for copy in written:
            copy.wait()
        if line:
            shrink.finish(write_to(gsh_out))
            shrink.drain()
            expand.finish(write_to(gate_out))
            expand.drain()
            first.drain()
            second.drain()


def middle(q, k, vt, tags, bars, wm, x, dy, gains, weights, kv, group, unit, line):
    length = q.shape[0]
    n = LANES
    d = wm.shape[1]
    share = (length // 4, d)
    per = share[0] // SUB
    steps = 2 * per
    we, ws = (w.shape for w in weights)
    shards = 2 * line
    shrink = jax.ShapeDtypeStruct(ws, BF)
    gate = jax.ShapeDtypeStruct((we[0], we[1] // 2), BF)
    more = []
    if line:
        shrink = jax.ShapeDtypeStruct(ws, FP)
        gate = jax.ShapeDtypeStruct(gate.shape, FP)
        we, ws = (we[0] * shards, we[1]), (ws[0], ws[1] * shards)
        more = [pltpu.VMEM(ws, BF), *reduce_scratch(line, shrink.shape), pltpu.VMEM((we[0], we[1] // 2), BF),
                *reduce_scratch(line, gate.shape), *GATHER_SEMS(shards), *GATHER_SEMS(shards)]
    units = ws[0]
    results = [jax.ShapeDtypeStruct(q.shape, BF), jax.ShapeDtypeStruct((length // SUB, 8, SUB * group), FP),
               jax.ShapeDtypeStruct(share, FP), jax.ShapeDtypeStruct((per, SUB, d), BF), gate,
               jax.ShapeDtypeStruct((we[0], units), BF), jax.ShapeDtypeStruct(share, FP),
               jax.ShapeDtypeStruct((length, d), BF), jax.ShapeDtypeStruct((8, d), FP),
               shrink]
    out_specs = [whole(r.shape) for r in results]
    for at in (0, 5, 7):
        out_specs[at] = ANYWHERE
    held = [q, k, vt, tags, bars, wm, gains]
    return pl.pallas_call(
        partial(middle_kernel, kv, group, unit, line, per, steps),
        grid=(3 * steps + 8,),
        in_specs=[whole(a.shape) for a in held] + [ANYWHERE] * 4,
        out_specs=out_specs,
        out_shape=results,
        scratch_shapes=[pltpu.VMEM((kv, n, SUB * group), FP), pltpu.VMEM((kv, 8, SUB * group), FP),
                        pltpu.VMEM(share, BF), pltpu.VMEM((length, d), BF), pltpu.VMEM(we, BF), pltpu.VMEM(ws, BF),
                        pltpu.SemaphoreType.DMA((6,)),
                        pltpu.VMEM(share, FP), pltpu.VMEM((length, d), BF), pltpu.VMEM((length, units), BF),
                        pltpu.VMEM((length, 2 * units), BF), pltpu.VMEM(q.shape, BF), pltpu.VMEM((we[0], units), BF),
                        *pairs_scratch(per, d, True), pltpu.SemaphoreType.DMA((4, 4 * per)),
                        *pairs_scratch(per, d, True), pltpu.VMEM((per, SUB, d), BF),
                        pltpu.SemaphoreType.DMA((4, 4 * per)),
                        *pairs_scratch(per, d, False), *more],
        compiler_params=params(collective_id=1, has_side_effects=True),
        name="middle",
    )(*held, x, dy, *weights)


def back_kernel(kv, group, unit, scale, blocks, per, line, *refs):
    refs = list(refs)
    take = lambda count: [refs.pop(0) for _ in range(count)]
    q_ref, k_ref, v_ref, kt_ref, tags_ref, bars_ref, lse_ref, ctx_block, dh_block, wm_ref = take(10)
    raw_ref, cos_ref, sin_ref, all_gains, base_ref, dg2_ref, other_ref = take(7)
    x_all, dh_all = take(2)
    late_from = take(4)
    grads = take(2) if line else []
    in_ref, out_ref, gains_out = take(3)
    sums = take(3) if line else []
    weight_grads = [] if line else take(2)
    late_to = take(4)
    wp_ref, ctx_ref, dh_ref, xn_ref = late_to
    late_sem = take(1)[0]
    late = [pltpu.make_async_copy(a, b, late_sem.at[w]) for w, (a, b) in enumerate(zip(late_from, late_to))]
    dk_ref, dv_ref, dq_ref, dqkv_ref = take(4)
    b_far, b_sems, x_held, x_near, x_sems = take(5)
    mine_ref, far_ref, x_far, f_sems, x_ref, dh_own, own_sems, heads_ref, fold_ref = take(9)
    place = Place(line)
    i = pl.program_id(0)
    steps = kv * blocks
    head = jnp.minimum(i // blocks, kv - 1)
    b = blocks - 1 - i % blocks
    n = LANES
    wide = (group + 2) * n
    pairs = Pairs(place, per, x_held, x_near, x_sems, lambda s: s % x_held.shape[0])
    subs = ROWS // SUB
    share, d = x_ref.shape
    gq, gk = all_gains[:, 2 * d:2 * d + n], all_gains[:, 2 * d + n:]
    tile = 256
    tensors = lax.axis_size("tensor")
    mates = [(place.dp, (place.t + step) % tensors) for step in range(1, tensors)]
    peers = []
    own_rows = pl.ds(pl.multiple_of(place.t * share, share), share)
    own_copies = [pltpu.make_async_copy(x_all.at[own_rows, :], x_ref, own_sems.at[0]),
                  pltpu.make_async_copy(dh_all, dh_own, own_sems.at[1])]
    if line:
        shards = 2 * line
        gm_ref, gp_ref = take(2)
        expand = Reduce(place, grads[1], row_cut(grads[1].shape[0] // shards), *take(4))
        merge = Reduce(place, gm_ref, column_cut(gm_ref.shape[1] // shards), None, *take(3))
        projects = [Reduce(place, gp_ref, row_cut(gp_ref.shape[0] // shards, slice(h * wide, (h + 1) * wide)), None, *take(3))
                    for h in range(kv)]
        shown, over, g_sems = take(3)
        peers = [((place.dp + step) % shards, place.t) for step in range(1, shards)]
    else:
        gp_ref, gm_ref = weight_grads

    def tiles(grad_ref, left_ref, right_ref):
        def one(t, carry):
            cut = pl.ds(pl.multiple_of(t * tile, tile), tile)
            grad_ref[:, cut] = dot(left_ref[...], right_ref[:, cut], 0, 0).astype(grad_ref.dtype)
            return carry

        lax.fori_loop(0, grad_ref.shape[1] // tile, one, 0)

    def write_up(values):
        sums[0][:, 0, :] = grads[0][...]
        sums[0][:, 1, :] = values

    def project_rows(t, h):
        cut, columns = pl.ds(pl.multiple_of(t * tile, tile), tile), slice(h * wide, (h + 1) * wide)
        gp_ref[cut, columns] = dot(xn_ref[:, cut], dqkv_ref[:, columns], 0, 0).astype(BF)

    def project_start(h):
        project_rows(projects[h].turn(0), h)
        projects[h].start()
        for q in range(1, line):
            project_rows(projects[h].turn(q), h)

    def chip(k):
        return send(far_ref.at[k], x_far.at[k], f_sems.at[0, k], f_sems.at[1, k], place.chip)

    def branch(k):
        return send(other_ref.at[k], b_far.at[k], b_sems.at[0, k], b_sems.at[1, k], place.chip)

    @pl.when(i == 0)
    def _():
        barrier = pltpu.get_barrier_semaphore()
        for device in mates + peers:
            pl.semaphore_signal(barrier, inc=1, device_id=device, device_id_type=MESH)
        for copy in late:
            copy.start()
        pl.semaphore_wait(barrier, len(mates + peers))
        if line:
            expand.start()
        for k in range(per):
            branch(k).start()
        heads_ref[...] = jnp.zeros_like(heads_ref)

    @pl.when(i % blocks == 0)
    def _():
        dk_ref[...] = jnp.zeros_like(dk_ref)
        dv_ref[...] = jnp.zeros_like(dv_ref)

    @pl.when(i < steps)
    def _():
        here = pl.ds(pl.multiple_of(b * ROWS, ROWS), ROWS)
        mine = pl.ds(pl.multiple_of(head * n, n), n)
        merge_rows = pl.ds(pl.multiple_of(head * group * n, group * n), group * n)
        dctx = dot(dh_block[...], wm_ref[merge_rows, :], 1, 1).astype(BF)
        bars = jnp.concatenate([bars_ref[...]] * group, axis=0)
        queries = stacked(q_ref[...], 0, group)
        barred = jnp.concatenate([queries, bars], axis=1)
        outward = stacked(dctx, 0, group)
        both = outward.astype(FP) * stacked(ctx_block[...], 0, group).astype(FP)
        centre = jnp.sum(both.T, axis=0, keepdims=True)
        lses = [jnp.concatenate([lse_ref[u, h:h + 1, g * SUB:(g + 1) * SUB]
                                 for g in range(group) for u in range(subs)], axis=1) for h in range(kv)]
        lse = lses[0]
        for h in range(1, kv):
            lse = jnp.where(head == h, lses[h], lse)
        dq_ref[...] = jnp.zeros_like(dq_ref)

        def chunk(start, size, diagonal):
            at = pl.ds(pl.multiple_of(start, ROWS), size)
            keys = jnp.concatenate([k_ref[at, mine], tags_ref[at, :]], axis=1)
            p = jnp.exp2(dot(keys, barred, 1, 1) * unit - lse)
            if diagonal:
                p = jnp.where(causal_tile(group), p, 0.0)
            dp = dot(v_ref[at, mine], outward, 1, 1)
            ds = (p * (dp - centre)).astype(BF)
            dv_ref[at, :] += dot(p.astype(BF), outward)
            dk_ref[at, :] += dot(ds, queries)
            dq_ref[...] += dot(kt_ref[mine, at], ds)

        lax.fori_loop(0, b // 2, lambda j, c: (chunk(j * 2 * ROWS, 2 * ROWS, False), c)[1], 0)
        pl.when(b % 2 == 1)(lambda: chunk((b - 1) * ROWS, ROWS, False))
        chunk(b * ROWS, ROWS, True)

        cosines, sines = cos_ref[...], sin_ref[...]
        dq = dq_ref[...].T
        pieces = []
        for c in range(group + 1):
            if c < group:
                grad, gain, row = dq[c * ROWS:(c + 1) * ROWS] * scale, gq, 0
            else:
                grad, gain, row = dk_ref[here, :] * scale, gk, 1
            grad = grad * cosines - pltpu.roll(grad, n // 2, 1) * sines
            piece, gain_grad = rms_pull(raw_ref[:, c * n:(c + 1) * n], gain, grad)
            heads_ref[row] += fold_rows(gain_grad)
            pieces.append(piece)
        pieces.append(dv_ref[here, :])
        dqkv_ref[here, pl.ds(pl.multiple_of(head * wide, wide), wide)] = jnp.concatenate(pieces, axis=1).astype(BF)
        pl.when(i == steps - blocks)(late[0].wait)

        @pl.when(i >= steps - blocks)
        def _():
            part = dot(dqkv_ref[here, :], wp_ref[...], 1, 1).astype(BF)
            for u in range(subs):
                s = subs * b + u
                pairs.put(s, part[u * SUB:(u + 1) * SUB], (i >= steps - blocks + 2, s + 2 * subs))

    def chip_rows(mine, k, summed):
        @pl.when(mine)
        def _():
            mine_ref[pl.ds(pl.multiple_of(k * SUB, SUB), SUB), :] = summed

        @pl.when(jnp.logical_not(mine))
        def _():
            far_ref[k] = summed.astype(BF)
            chip(k).start()

    @pl.when(i >= steps - blocks + 1)
    def _():
        for u in range(subs):
            pairs.add(subs * (steps - i) + u, chip_rows)

    @pl.when(i == 3)
    def _():
        for k in range(per):
            branch(k).wait()
            at = slice(k * SUB, (k + 1) * SUB)
            out_ref[at, :] = (base_ref[at, :] + b_far[k].astype(FP)).astype(BF)
        for copy in own_copies:
            copy.start()

    @pl.when(i == 1)
    def _():
        late[1].wait()
        late[2].wait()
        tiles(gm_ref, ctx_ref, dh_ref)

    if line:
        acts = [lambda: expand.step(1), lambda: expand.step(2), lambda: expand.step(3), merge.start,
                lambda: merge.step(1), lambda: merge.step(2)]
        for step, act in enumerate(acts):
            pl.when(i == step)(act)

        @pl.when(i == blocks)
        def _():
            merge.step(3)
            late[3].wait()

        for h in range(kv - 1):
            pl.when(i == (h + 1) * blocks)(lambda h=h: project_start(h))
            for k in range(1, line):
                pl.when(i == (h + 1) * blocks + k)(lambda h=h, k=k: projects[h].step(k))

    def input_rows(k):
        at = slice(k * SUB, (k + 1) * SUB)
        chip(k).wait()
        summed = mine_ref[at, :] + x_far[k].astype(FP)
        pulled, gain_grad = rms_pull(x_ref[at, :].astype(FP), all_gains[:, :d], summed)
        in_ref[at, :] = (dh_own[at, :] + pulled).astype(BF)
        fold_ref[...] += fold_rows(gain_grad)

    def folded(ref):
        pieces = [fold_ref[...], dg2_ref[...], heads_ref[0], heads_ref[1]]
        row = jnp.sum(jnp.concatenate(pieces, axis=1), axis=0, keepdims=True)
        count = row.shape[1] // n
        for j in range(count):
            ref[j:j + 1, :] = row[:, j * n:(j + 1) * n]
        ref[count:, :] = jnp.zeros((ref.shape[0] - count, n), FP)

    def show(buffer, me, devices, first):
        copies = [send(buffer.at[me], buffer.at[me], g_sems.at[0, first + step], g_sems.at[1, first + step], device)
                  for step, device in enumerate(devices, 1)]
        for copy in copies:
            copy.start()
        return copies

    def added(buffer, me, devices, first):
        count = len(devices) + 1
        for step in range(1, count):
            who = (me - step + count) % count
            send(buffer.at[who], buffer.at[who], g_sems.at[0, first + step], g_sems.at[1, first + step],
                 place.sibling).wait_recv()
        total = buffer[0]
        for who in range(1, count):
            total = total + buffer[who]
        return total

    @pl.when(i == steps)
    def _():
        fold_ref[...] = jnp.zeros_like(fold_ref)
        for copy in own_copies:
            copy.wait()
        if not line:
            late[3].wait()
            tiles(gp_ref, xn_ref, dqkv_ref)
            for k in range(per):
                input_rows(k)
            folded(gains_out)
        else:
            project = projects[-1]
            project_start(kv - 1)
            expand.finish(write_up)
            project.step(1)
            merge.finish(write_to(sums[1]))
            project.step(2)
            for h in range(kv - 1):
                projects[h].finish(write_to(sums[2], h * (group + 2)))
            for k in range(per):
                input_rows(k)
            folded(shown.at[place.t])
            copies = show(shown, place.t, mates, 0)
            project.step(3)
            over[place.dp] = added(shown, place.t, mates, 0)
            copies += show(over, place.dp, peers, tensors)
            project.finish(write_to(sums[2], (kv - 1) * (group + 2)))
            gains_out[...] = added(over, place.dp, peers, tensors)
            for copy in copies:
                copy.wait_send()
            for r in (expand, merge, *projects):
                r.drain()
        for s in range(2 * subs):
            pairs.sent(s)


def back(q, k, v, kt, tags, bars, lse, ctx, dh, wm, wp, raw, cosines, sines, gains, xn, base, dg2, other, x, dh_own,
         grads, kv, group, unit, scale, line):
    length = q.shape[0]
    n = LANES
    d = wm.shape[1]
    blocks = length // ROWS
    per = other.shape[0]
    share = base.shape
    steps = kv * blocks
    block_of = lambda i: jnp.where(i < steps, blocks - 1 - i % blocks, 0)
    rows = lambda w: pl.BlockSpec((ROWS, w), lambda i: (block_of(i), 0))
    own_rows = lambda w: pl.BlockSpec((ROWS, w // kv), lambda i: (block_of(i), jnp.minimum(i // blocks, kv - 1)))
    late = [wp, ctx, dh, xn]
    gain_rows = (-(-(gains.shape[1] // n) // 8) * 8, n)
    scratch = [*[pltpu.VMEM(a.shape, BF) for a in late], pltpu.SemaphoreType.DMA((4,)),
               pltpu.VMEM((length, n), FP), pltpu.VMEM((length, n), FP),
               pltpu.VMEM((n, ROWS * group), FP), pltpu.VMEM((length, wp.shape[1]), BF),
               pltpu.VMEM((per, SUB, d), BF), pltpu.SemaphoreType.DMA((2, per)),
               pltpu.VMEM((2 * ROWS // SUB, SUB, d), BF), pltpu.VMEM((2 * per, SUB, d), BF),
               pltpu.SemaphoreType.DMA((2, 4 * per)),
               pltpu.VMEM(share, FP), pltpu.VMEM((per, SUB, d), BF), pltpu.VMEM((per, SUB, d), BF),
               pltpu.SemaphoreType.DMA((2, per)), pltpu.VMEM(share, BF), pltpu.VMEM(share, FP),
               pltpu.SemaphoreType.DMA((2,)), pltpu.VMEM((2, 8, n), FP), pltpu.VMEM((8, d), FP)]
    results = [jax.ShapeDtypeStruct(share, BF), jax.ShapeDtypeStruct(share, BF), jax.ShapeDtypeStruct(gain_rows, FP)]
    if line:
        shards = 2 * line
        own = [grads[0].shape, (wm.shape[0], wm.shape[1] // shards),
               (wp.shape[0] // shards, wp.shape[1])]
        views = ((own[0][0], 2, own[0][1]), own[1], (own[2][0], own[2][1] // n, n))
        results += [jax.ShapeDtypeStruct(s, FP) for s in views]
        scratch += [pltpu.VMEM(wm.shape, BF), pltpu.VMEM(wp.shape, BF)]
        for w, s in enumerate(own[:2] + [(own[2][0], own[2][1] // kv)] * kv):
            scratch += reduce_scratch(line, s, w == 0)
        scratch += [pltpu.VMEM((4, *gain_rows), FP), pltpu.VMEM((shards, *gain_rows), FP),
                    pltpu.SemaphoreType.DMA((2, 4 + shards))]
    else:
        results += [jax.ShapeDtypeStruct(wp.shape, BF), jax.ShapeDtypeStruct(wm.shape, BF)]
    args = [q, k, v, kt, tags, bars, lse, ctx, dh, wm, raw, cosines, sines, gains, base, dg2]
    more = [other, x, dh_own, *late, *grads]
    specs = [whole(a.shape) for a in args] + [ANYWHERE] * len(more)
    if line:
        specs[-2] = whole(grads[0].shape)
    for at in (5, 8, 11, 12):
        specs[at] = rows(args[at].shape[1])
    for at in (0, 7, 10):
        specs[at] = own_rows(args[at].shape[1])
    specs[6] = pl.BlockSpec((ROWS // SUB, 8, SUB * group), lambda i: (block_of(i), 0, 0))
    return pl.pallas_call(
        partial(back_kernel, kv, group, unit, scale, blocks, per, line),
        grid=(steps + 1,),
        in_specs=specs,
        out_specs=[whole(r.shape) for r in results],
        out_shape=results,
        scratch_shapes=scratch,
        compiler_params=params(collective_id=3, has_side_effects=True),
        name="back",
    )(*args, *more)


def adamw_step(weight, moment_one, moment_two, gradient, step_rate, decay):
    mean_next = BETA_ONE * moment_one + (1.0 - BETA_ONE) * gradient
    square_next = BETA_TWO * moment_two + (1.0 - BETA_TWO) * gradient * gradient
    mean_hat = mean_next / (1.0 - BETA_ONE**STEP)
    square_hat = square_next / (1.0 - BETA_TWO**STEP)
    weight_next = weight - step_rate * (mean_hat / (jnp.sqrt(square_hat) + EPS_ADAM) + decay * weight)
    return weight_next, mean_next, square_next


def shards(
    tokens, cotangent, parents, token_segment, tree_id,
    projection_weight, projection_first_moment, projection_second_moment,
    merge_master, merge_mean, merge_square,
    expand_master, expand_mean, expand_square,
    shrink_master, shrink_mean, shrink_square,
    gain_master, gain_mean, gain_square,
):
    x = tokens[0]
    dy = cotangent[0]
    length, d = x.shape
    d_own, kv, per, n = projection_weight.shape
    group = per - 2
    units = expand_master.shape[2]
    scale = n ** (-0.5)
    unit = scale * math.log2(math.e)
    line = 4 if lax.axis_size("dp") == 8 and d_own % LANES == 0 else 0
    if line:
        masters = (projection_weight.reshape(d_own, kv * per, n), merge_master, expand_master, shrink_master)
    else:
        wp, we = (lax.all_gather(w.astype(BF).reshape(d_own, -1), "dp", axis=0, tiled=True)
                  for w in (projection_weight, expand_master))
        wm, ws = (lax.all_gather(w.astype(BF), "dp", axis=1, tiled=True) for w in (merge_master, shrink_master))
        masters = (wp,)

    gains = gain_master[None]
    fronts = front(x, gains, token_segment, parents, tree_id, masters, kv, group, line)
    xn1, q, k, v, kt, vt, raw, tags, bars, cosines, sines = fronts[:11]
    if line:
        wp, wm, *low = fronts[11:]
    else:
        low = (we, ws)
    ctx, lse, base, other, gate_sum, up_grad, dh, dhb, dg2, shrink_sum = middle(
        q, k, vt, tags, bars, wm, x, dy, gains, low, kv, group, unit, line)
    backs = back(q, k, v, kt, tags, bars, lse, ctx, dhb, wm, wp, raw, cosines, sines, gains, xn1,
                 base, dg2, other, x, dh, (gate_sum, up_grad) if line else (), kv, group, unit, scale, line)
    input_grad, output, gain_rows = backs[:3]
    if line:
        expand_sum, merge_sum, project_sum = backs[3:]
    else:
        gain_rows = lax.psum(gain_rows, ("dp", "tensor"))
        project_sum, expand_sum = (
            lax.psum_scatter(g, "dp", scatter_dimension=0, tiled=True) for g in (backs[3], jnp.concatenate([gate_sum, up_grad], axis=1)))
        merge_sum, shrink_sum = (
            lax.psum_scatter(g, "dp", scatter_dimension=1, tiled=True) for g in (backs[4], shrink_sum))
    output, input_grad = output[None], input_grad[None]
    gain_grad = gain_rows.reshape(-1)[:gain_master.shape[0]]

    outs = [output, input_grad]
    for weight, mean, square, grad, rate in (
        (projection_weight, projection_first_moment, projection_second_moment, project_sum, RATE_PROJECT),
        (merge_master, merge_mean, merge_square, merge_sum, RATE_MERGE),
        (expand_master, expand_mean, expand_square, expand_sum, RATE_EXPAND),
        (shrink_master, shrink_mean, shrink_square, shrink_sum, RATE_SHRINK),
    ):
        grad = grad.astype(FP).reshape(weight.shape)
        after, mean_next, square_next = adamw_step(weight, mean, square, grad, rate, DECAY)
        outs += [after, mean_next, square_next, after.astype(BF)]
    gain_next, gain_mean_next, gain_square_next = adamw_step(
        gain_master, gain_mean, gain_square, gain_grad, RATE_GAIN, 0.0)
    return (*outs, gain_mean_next, gain_square_next, gain_next)


def solution(mesh):
    tokens = P("dp", None, None)
    project = P("dp", "tensor", None, None)
    columns = P("tensor", "dp")
    expand = P("dp", None, "tensor")
    shared = P("dp", "tensor", None)
    return jax.shard_map(
        shards,
        mesh=mesh,
        in_specs=(tokens, tokens, P(), P("dp", None), P("dp"), *[project] * 3, *[columns] * 3, *[expand] * 3,
                  *[columns] * 3, P(), P(), P()),
        out_specs=(shared, shared, *[project] * 4, *[columns] * 4, *[expand] * 4, *[columns] * 4, P(), P(), P()),
        check_vma=False,
    )
```

```python
import math
from functools import partial

import jax
import jax.numpy as jnp
import numpy as np
from jax import lax
from jax.experimental import pallas as pl
from jax.experimental.pallas import tpu as pltpu
from jax.sharding import PartitionSpec as P

STEP = 5
EPS_NORM = 1e-06
THETA = 1000000.0
BETA_ONE = 0.5
BETA_TWO = 0.5
EPS_ADAM = 1e-08
DECAY = 0.1
RATE_PROJECT = 0.05
RATE_MERGE = 0.3
RATE_EXPAND = 0.05
RATE_SHRINK = 0.03
RATE_GAIN = 0.3

BF = jnp.bfloat16
FP = jnp.float32
ROWS = 256
LANES = 128
SUB = 128
MESH = pl.DeviceIdType.MESH
BLOCKED = -1e30
VMEM_LIMIT = 56 * 2**20


def params(**more):
    return pltpu.CompilerParams(vmem_limit_bytes=VMEM_LIMIT, **more)


def dot(a, b, ca=1, cb=0):
    return lax.dot_general(a, b, (((ca,), (cb,)), ((), ())), preferred_element_type=FP)


def inverse_rms(values):
    return lax.rsqrt(jnp.mean(values * values, axis=-1, keepdims=True) + EPS_NORM)


def rms_pull(values, scales, grad):
    r = inverse_rms(values)
    scaled = grad * scales
    mean = jnp.mean(values * scaled, axis=-1, keepdims=True)
    return r * scaled - values * (r * r * r * mean), grad * values * r


def fold_rows(values):
    n, w = values.shape
    return jnp.sum(values.reshape(n // 8, 8, w), axis=0)


class Place:
    def __init__(self, line):
        self.line = line
        self.dp, self.t = lax.axis_index("dp"), lax.axis_index("tensor")
        self.z, self.y = self.dp // 2, self.dp % 2
        self.x, self.c = self.t // 2, self.t % 2
        self.has_up, self.has_down = self.z < line - 1, self.z > 0
        self.up, self.down = (self.dp + 2, self.t), (self.dp - 2, self.t)
        self.across = (self.dp + 1 - 2 * self.y, self.t)
        self.sibling = (self.dp, self.t + 1 - 2 * self.c)
        self.chip = (self.dp, (1 - self.x) * 2 + self.c)

    def greet(self, tensor, line, meanwhile=None):
        barrier = pltpu.get_barrier_semaphore()

        def signal(device):
            pl.semaphore_signal(barrier, inc=1, device_id=device, device_id_type=MESH)

        if tensor:
            signal(self.sibling)
            signal(self.chip)
        if line:
            signal(self.across)
            pl.when(self.has_up)(lambda: signal(self.up))
            pl.when(self.has_down)(lambda: signal(self.down))
        peers = (2 if tensor else 0) + (1 if line else 0)
        if line:
            peers = peers + jnp.where(self.has_up, 1, 0) + jnp.where(self.has_down, 1, 0)
        if meanwhile is not None:
            meanwhile()
        pl.semaphore_wait(barrier, peers)


def send(src, dst, sent, arrived, device):
    return pltpu.make_async_remote_copy(
        src_ref=src, dst_ref=dst, send_sem=sent, recv_sem=arrived, device_id=device, device_id_type=MESH)


def row_cut(size):
    return lambda j: (pl.ds(pl.multiple_of(j * size, size), size), slice(None))


def column_cut(size):
    return lambda j: (slice(None), pl.ds(pl.multiple_of(j * size, size), size))


class Gather:
    def __init__(self, place, own, full, cut, sems, local):
        self.place, self.own, self.full, self.cut, self.sems, self.local = place, own, full, cut, sems, local

    def copy(self, kind, src, j):
        p = self.place
        device = (p.up, p.down, p.across)[kind]
        return send(src, self.full.at[self.cut(j)], self.sems.at[kind, j], self.sems.at[3, j], device)

    def kept(self):
        return pltpu.make_async_copy(self.own, self.full.at[self.cut(self.place.dp)], self.local)

    def source(self):
        return self.full.at[self.cut(self.place.dp)] if self.own is None else self.own

    def start(self):
        p = self.place
        self.copy(2, self.source(), p.dp).start()
        pl.when(p.has_up)(lambda: self.copy(0, self.source(), p.dp).start())
        pl.when(p.has_down)(lambda: self.copy(1, self.source(), p.dp).start())
        if self.own is not None:
            self.kept().start()

    def arrivals(self, k):
        p = self.place
        return ((0, p.z >= k, (p.z - k) * 2 + p.y, p.has_up), (1, p.z + k < p.line, (p.z + k) * 2 + p.y, p.has_down))

    def hop(self, k):
        for kind, here, j, further in self.arrivals(k):
            @pl.when(here)
            def _(kind=kind, j=j, further=further):
                piece = self.full.at[self.cut(j)]
                self.copy(kind, piece, j).wait_recv()
                pl.when(further)(lambda: self.copy(kind, piece, j).start())
                self.copy(2, piece, j).start()

    def finish(self):
        p = self.place
        if self.own is not None:
            self.kept().wait()
        for zz in range(p.line):
            j = zz * 2 + 1 - p.y
            self.copy(2, self.full.at[self.cut(j)], j).wait_recv()

    def drain(self):
        p = self.place
        self.copy(2, self.source(), p.dp).wait_send()
        pl.when(p.has_up)(lambda: self.copy(0, self.source(), p.dp).wait_send())
        pl.when(p.has_down)(lambda: self.copy(1, self.source(), p.dp).wait_send())
        for k in range(1, p.line):
            for kind, here, j, further in self.arrivals(k):
                @pl.when(here)
                def _(kind=kind, j=j, further=further):
                    piece = self.full.at[self.cut(j)]
                    pl.when(further)(lambda: self.copy(kind, piece, j).wait_send())
                    self.copy(2, piece, j).wait_send()


class Reduce:
    def __init__(self, place, grad, cut, kept, across, lined, sems):
        self.place, self.grad, self.cut, self.kept, self.sems = place, grad, cut, kept, sems
        self.across, self.lined = across, lined

    def cross(self, zz):
        p = self.place
        return send(self.grad.at[self.cut(zz * 2 + 1 - p.y)], self.across.at[zz],
                    self.sems.at[0, zz], self.sems.at[1, zz], p.across)

    def climb(self, t):
        return send(self.across.at[t], self.lined.at[t + 1], self.sems.at[2, t], self.sems.at[3, t], self.place.up)

    def sink(self, t):
        return send(self.across.at[t], self.lined.at[t], self.sems.at[4, t], self.sems.at[5, t], self.place.down)

    def load(self, zz):
        return pltpu.make_async_copy(self.grad.at[self.cut(zz * 2 + self.place.y)], self.kept.at[zz], self.sems.at[6, zz])

    def mine(self, zz):
        if self.kept is None:
            return self.grad[self.cut(zz * 2 + self.place.y)].astype(FP)
        return self.kept[zz].astype(FP)

    def loaded(self, zz):
        if self.kept is not None:
            self.load(zz).wait()

    def turn(self, q):
        z = self.place.z
        low = z < 2
        if q == 0:
            return jnp.where(low, 3, 0)
        if q == 1:
            return jnp.where(low, 2, 1)
        if q == 2:
            return jnp.where(low, 1 - z, 5 - z)
        return z

    def start(self):
        self.cross(self.turn(0)).start()
        if self.kept is not None:
            for zz in range(self.place.line):
                self.load(zz).start()

    def advance(self, q):
        self.cross(self.turn(q - 1)).wait_send()
        self.cross(self.turn(q)).start()

    def hop(self, h):
        p = self.place

        def pass_on(t, coming, more, slot):
            self.loaded(t)
            self.cross(t).wait_recv()

            @pl.when(jnp.logical_not(more))
            def _():
                self.across[t] = (self.mine(t) + self.across[t].astype(FP)).astype(BF)

            @pl.when(more)
            def _():
                coming(t).wait_recv()
                self.across[t] = (self.mine(t) + self.across[t].astype(FP) + self.lined[slot].astype(FP)).astype(BF)

            coming(t).start()

        pl.when(p.z < h)(lambda: pass_on(p.z + p.line - h, self.climb, p.has_down, p.z + p.line - h + 1))
        pl.when(p.z >= p.line - h)(lambda: pass_on(p.z - p.line + h, self.sink, p.has_up, p.z - p.line + h))

    def finish(self, write):
        p = self.place
        self.loaded(p.z)
        self.cross(p.z).wait_recv()
        pl.when(p.has_down)(lambda: self.climb(p.z).wait_recv())
        pl.when(p.has_up)(lambda: self.sink(p.z).wait_recv())
        from_below = jnp.where(p.has_down, self.lined[p.z + 1].astype(FP), 0.0)
        from_above = jnp.where(p.has_up, self.lined[p.z].astype(FP), 0.0)
        write(self.mine(p.z) + self.across[p.z].astype(FP) + from_below + from_above)

    def step(self, k):
        self.advance(k)
        self.hop(k)

    def drain(self):
        p = self.place
        self.cross(p.z).wait_send()
        for zz in range(p.line):
            pl.when(zz > p.z)(lambda zz=zz: self.climb(zz).wait_send())
            pl.when(zz < p.z)(lambda zz=zz: self.sink(zz).wait_send())


def write_to(ref):
    def write(values):
        if len(ref.shape) == 2:
            ref[...] = values
            return
        width = ref.shape[2]
        for j in range(ref.shape[1]):
            ref[:, j, :] = values[:, j * width:(j + 1) * width]

    return write


def reduce_scratch(line, shape, kept=False):
    return [pltpu.VMEM((line, *shape), BF)] * kept + [pltpu.VMEM((line, *shape), BF), pltpu.VMEM((line + 1, *shape), BF),
                                                      pltpu.SemaphoreType.DMA((7, line))]


class Pairs:
    def __init__(self, place, per, held, near, sems, slot_of):
        self.place, self.per, self.held, self.near, self.sems, self.slot_of = place, per, held, near, sems, slot_of

    def near_slot(self, s):
        return (s // (2 * self.per)) * self.per + s % self.per

    def to_sibling(self, s):
        return send(self.held.at[self.slot_of(s)], self.near.at[self.near_slot(s)], self.sems.at[0, s],
                    self.sems.at[1, s], self.place.sibling)

    def sends(self, s):
        return self.place.c != (s // self.per) % 2

    def sent(self, s):
        pl.when(self.sends(s))(lambda: self.to_sibling(s).wait_send())

    def put(self, s, rows, before=None):
        if before is not None:
            pl.when(before[0])(lambda: self.sent(before[1]))
        self.held[self.slot_of(s)] = rows
        pl.when(self.sends(s))(lambda: self.to_sibling(s).start())

    def put_next(self, s, rows):
        self.put(s, rows, (s % self.per >= 1, s - 1))

    def add(self, s, use):
        t = s // self.per

        @pl.when(self.place.c == t % 2)
        def _():
            self.to_sibling(s).wait_recv()
            use(self.place.x == t // 2, s % self.per,
                self.held[self.slot_of(s)].astype(FP) + self.near[self.near_slot(s)].astype(FP))


class Exchange(Pairs):
    def __init__(self, place, per, held, near, far, total, sems):
        super().__init__(place, per, held, near, sems, lambda s: s // per)
        self.far, self.total = far, total

    def rows(self, k):
        return pl.ds(pl.multiple_of(k * SUB, SUB), SUB)

    def to_chip(self, s):
        return send(self.near.at[self.near_slot(s)], self.far.at[s % self.per], self.sems.at[2, s], self.sems.at[3, s],
                    self.place.chip)

    def add_chip(self, s):
        def use(mine, k, summed):
            @pl.when(jnp.logical_not(mine))
            def _():
                self.near[self.near_slot(s)] = summed.astype(BF)
                self.to_chip(s).start()

            @pl.when(mine)
            def _():
                self.total[self.rows(k), :] = summed

        self.add(s, use)

    def take(self, s, use):
        @pl.when(s // self.per == self.place.t)
        def _():
            k = s % self.per
            self.to_chip(s).wait_recv()
            use(s, self.rows(k), self.total[self.rows(k), :] + self.far[k].astype(FP))

    def drain(self):
        p = self.place

        def one(s, carry):
            t = s // self.per
            pl.when(s % self.per == self.per - 1)(lambda: self.sent(s))
            pl.when(jnp.logical_and(p.c == t % 2, p.x != t // 2))(lambda: self.to_chip(s).wait_send())
            return carry

        lax.fori_loop(0, 4 * self.per, one, 0)


def pair_of(step, per):
    t = step % 2
    return t * per + step // 2, (3 - t) * per + step // 2


def pairs_scratch(per, d, exchange):
    rows = [pltpu.VMEM((4, SUB, d), BF), pltpu.VMEM((2 * per, SUB, d), BF)]
    return rows + [pltpu.VMEM((per, SUB, d), BF)] * exchange + [pltpu.SemaphoreType.DMA((4 if exchange else 2, 4 * per))]


class Spread:
    def __init__(self, place, per, stage, full, sems):
        self.place, self.per, self.stage, self.full, self.sems = place, per, stage, full, sems

    def rows(self, s):
        return self.full.at[pl.ds(pl.multiple_of(s * SUB, SUB), SUB), :]

    def source(self, s):
        return self.rows(s) if self.stage is None else self.stage.at[s % self.per]

    def copy(self, kind, src, s):
        device = (self.place.chip, self.place.sibling)[kind]
        return send(src, self.rows(s), self.sems.at[kind, s], self.sems.at[2, s], device)

    def kept(self, s):
        return pltpu.make_async_copy(self.source(s), self.rows(s), self.sems.at[3, s])

    def send(self, s):
        for kind in (0, 1):
            self.copy(kind, self.source(s), s).start()
        if self.stage is not None:
            self.kept(s).start()

    def owns(self, s):
        return s // self.per == self.place.t

    def passes(self, s):
        t = s // self.per
        return jnp.logical_and(self.place.c == t % 2, self.place.x != t // 2)

    def pass_on(self, s):
        @pl.when(self.passes(s))
        def _():
            self.copy(1, self.rows(s), s).wait_recv()
            self.copy(1, self.rows(s), s).start()

    def ready(self, s):
        if self.stage is not None:
            pl.when(self.owns(s))(lambda: self.kept(s).wait())
        pl.when((s // self.per) % 2 != self.place.c)(lambda: self.copy(1, self.rows(s), s).wait_recv())

    def drain(self):
        def one(s, carry):
            @pl.when(self.owns(s))
            def _():
                self.copy(0, self.source(s), s).wait_send()
                self.copy(1, self.source(s), s).wait_send()

            pl.when(self.passes(s))(lambda: self.copy(1, self.rows(s), s).wait_send())
            return carry

        lax.fori_loop(0, 4 * self.per, one, 0)


def whole(shape):
    return pl.BlockSpec(tuple(shape), lambda i: (0,) * len(shape), pipeline_mode=pl.Buffered(1))


ANYWHERE = pl.BlockSpec(memory_space=pl.ANY)
GATHER_SEMS = lambda shards: [pltpu.SemaphoreType.DMA((4, shards)), pltpu.SemaphoreType.DMA]


def make_tables(seg_ref, parents_ref, tree_ref, freq_ref, tags_ref, bars_ref, cos_ref, sin_ref):
    count = parents_ref.shape[1]
    n = LANES
    blocks = sin_ref.shape[0] // ROWS
    lane = lax.broadcasted_iota(jnp.int32, (1, n), 1).astype(FP)
    place_of = lambda b: pl.ds(pl.multiple_of(b * ROWS, ROWS), ROWS)

    def columns(b, carry):
        sin_ref[place_of(b), :] = jnp.broadcast_to(seg_ref[:, place_of(b)].astype(FP), (n, ROWS)).T
        return carry

    def tally(b, carry):
        column = sin_ref[place_of(b), :]
        return (carry[0] + fold_rows(jnp.where(column == lane, 1.0, 0.0)),
                carry[1] + fold_rows(jnp.where(column < lane, 1.0, 0.0)))

    lax.fori_loop(0, blocks, columns, 0)
    sizes, starts = lax.fori_loop(0, blocks, tally, (jnp.zeros((8, n), FP), jnp.zeros((8, n), FP)))
    sizes, starts = (jnp.sum(a, axis=0, keepdims=True) for a in (sizes, starts))
    table = parents_ref[...]
    chosen = jnp.where(lax.broadcasted_iota(jnp.int32, table.shape, 0) == tree_ref[0], table, 0)
    chosen = jnp.sum(chosen.astype(FP), axis=0, keepdims=True)
    parents = jnp.zeros((1, n), FP)
    for b in range(count):
        parents = jnp.where(lane == b, chosen[:, b:b + 1], parents)
    shifts = jnp.where(lane != 0, sizes[:, :1], 0.0) - starts

    def rows(b, carry):
        at = place_of(b)
        column = sin_ref[at, :]
        hot = column == lane
        parent = jnp.sum(jnp.where(hot, parents, 0.0), axis=1, keepdims=True)
        above = jnp.where(jnp.logical_and(lane == parent, lane != 0), sizes, 0.0)
        first = (b * ROWS).astype(FP)
        position = (lax.broadcasted_iota(jnp.int32, (ROWS, 1), 0).astype(FP) + first
                    + jnp.sum(jnp.where(hot, shifts, 0.0) + above, axis=1, keepdims=True))
        tags_ref[at, :] = jnp.where(hot, 1.0, 0.0).astype(BF)
        open_to = jnp.logical_or(jnp.logical_or(hot, lane == parent), jnp.logical_or(lane == 0, lane >= count))
        bars_ref[at, :] = jnp.where(open_to, 0.0, BLOCKED).astype(BF)
        angles = position * freq_ref[...]
        cos_ref[at, :] = jnp.cos(angles)
        turned = jnp.sin(angles)
        sin_ref[at, :] = jnp.where(lane < n // 2, -turned, turned)
        return carry

    lax.fori_loop(0, blocks, rows, 0)


def front_kernel(kv, group, line, *refs):
    refs = list(refs)
    take = lambda count: [refs.pop(0) for _ in range(count)]
    x_ref, gains_ref, seg_ref, parents_ref, tree_ref, freq_ref = take(6)
    masters = take(4) if line else take(1)
    xn_ref, q_ref, k_ref, v_ref, kt_ref, vt_ref, raw_ref, tags_ref, bars_ref, cos_ref, sin_ref = take(11)
    if line:
        wp_out, wm_out, we_low, ws_low = take(4)
        wp_ref, wm_low, p_sems, p_local, m_sems, m_local, out_sem = take(7)
    else:
        wp_ref = masters[0]
    xn_full, xn_sem = take(2)
    i = pl.program_id(0)
    final = pl.num_programs(0) - 1
    d = x_ref.shape[1]
    n = LANES
    per = group + 2
    if line:
        place = Place(line)
        size = masters[0].shape[0]
        project = Gather(place, None, wp_ref, row_cut(size), p_sems, p_local)
        merge = Gather(place, wm_low, wm_out, column_cut(wm_low.shape[1]), m_sems, m_local)
        written = pltpu.make_async_copy(wp_ref, wp_out, out_sem)
    normed = pltpu.make_async_copy(xn_full, xn_ref, xn_sem)

    def round_projection():
        at = pl.ds(pl.multiple_of(place.dp * size, size), size)
        for j in range(kv * per):
            wp_ref[at, j * n:(j + 1) * n] = masters[0][:, j, :].astype(BF)

    def norm(b, carry):
        at = pl.ds(pl.multiple_of(b * ROWS, ROWS), ROWS)
        x = x_ref[at, :].astype(FP)
        xn_full[at, :] = (x * inverse_rms(x) * gains_ref[:, :d]).astype(BF)
        return carry

    @pl.when(i == 0)
    def _():
        if line:
            place.greet(False, True, round_projection)
            project.start()
        lax.fori_loop(0, x_ref.shape[0] // ROWS, norm, 0)
        normed.start()
        if line:
            project.hop(1)
        make_tables(seg_ref, parents_ref, tree_ref, freq_ref, tags_ref, bars_ref, cos_ref, sin_ref)
        if line:
            project.hop(2)
            wm_low[...] = masters[1][...].astype(BF)
            units = masters[2].shape[2]
            for half in range(2):
                we_low[:, half * units:(half + 1) * units] = masters[2][:, half, :].astype(BF)
            ws_low[...] = masters[3][...].astype(BF)
            project.hop(3)
            merge.start()
            project.finish()
            written.start()

    if line:
        for k in range(1, line):
            pl.when(i == k + 1)(lambda k=k: merge.hop(k))
    at = pl.ds(pl.multiple_of(i * ROWS, ROWS), ROWS)
    qkv = dot(xn_full[at, :], wp_ref[...])
    cosines, sines = cos_ref[at, :], sin_ref[at, :]
    gq, gk = gains_ref[:, 2 * d:2 * d + n], gains_ref[:, 2 * d + n:]
    keys, values = [], []
    for h in range(kv):
        for c in range(group + 1):
            raw = qkv[:, (h * per + c) * n:(h * per + c + 1) * n]
            to = (h * (group + 1) + c) * n
            raw_ref[:, to:to + n] = raw
            y = raw * inverse_rms(raw) * (gq if c < group else gk)
            turned = y * cosines + pltpu.roll(y, n // 2, 1) * sines
            if c < group:
                to = (h * group + c) * n
                q_ref[:, to:to + n] = turned.astype(BF)
            else:
                keys.append(turned)
        values.append(qkv[:, (h * per + group + 1) * n:(h * per + group + 2) * n])
    for h in range(kv):
        k_ref[:, h * n:(h + 1) * n] = keys[h].astype(BF)
        v_ref[:, h * n:(h + 1) * n] = values[h].astype(BF)
        kt_ref[h * n:(h + 1) * n, :] = keys[h].T.astype(BF)
        vt_ref[h * n:(h + 1) * n, :] = values[h].T.astype(BF)

    @pl.when(i == final)
    def _():
        normed.wait()
        if line:
            merge.finish()
            merge.drain()
            project.drain()
            written.wait()


def front(x, gains, segments, parents, tree, masters, kv, group, line):
    length, d = x.shape
    n = LANES
    rows = lambda w: pl.BlockSpec((ROWS, w), lambda i: (i, 0))
    cols = pl.BlockSpec((kv * n, ROWS), lambda i: (0, i))
    out = lambda w, t: jax.ShapeDtypeStruct((length, w), t)
    raw_w = kv * (group + 1) * n
    freq = np.float32(THETA ** (-(np.arange(n) % (n // 2)) * 2.0 / n))[None]
    more_specs, more_shapes, scratch = [], [], []
    if line:
        shards = 2 * line
        project, merge, expand, shrink = (m.shape for m in masters)
        wp_shape = (project[0] * shards, project[1] * n)
        more_shapes = [jax.ShapeDtypeStruct(wp_shape, BF), jax.ShapeDtypeStruct((merge[0], merge[1] * shards), BF),
                       jax.ShapeDtypeStruct((expand[0], 2 * expand[2]), BF), jax.ShapeDtypeStruct(shrink, BF)]
        more_specs = [ANYWHERE, ANYWHERE, whole(more_shapes[2].shape), whole(more_shapes[3].shape)]
        scratch = [pltpu.VMEM(wp_shape, BF), pltpu.VMEM(merge, BF), *GATHER_SEMS(shards), *GATHER_SEMS(shards),
                   pltpu.SemaphoreType.DMA]
    table = whole((length, n))
    return pl.pallas_call(
        partial(front_kernel, kv, group, line),
        grid=(length // ROWS,),
        in_specs=[whole(x.shape), whole(gains.shape), whole(segments.shape), whole(parents.shape),
                  pl.BlockSpec(memory_space=pltpu.SMEM), whole(freq.shape), *[whole(m.shape) for m in masters]],
        out_specs=[ANYWHERE, rows(kv * group * n), rows(kv * n), rows(kv * n), cols, cols, rows(raw_w),
                   table, table, table, table, *more_specs],
        out_shape=[out(d, BF), out(kv * group * n, BF), out(kv * n, BF), out(kv * n, BF),
                   jax.ShapeDtypeStruct((kv * n, length), BF), jax.ShapeDtypeStruct((kv * n, length), BF),
                   out(raw_w, FP), out(n, BF), out(n, BF), out(n, FP), out(n, FP), *more_shapes],
        scratch_shapes=[*scratch, pltpu.VMEM((length, d), BF), pltpu.SemaphoreType.DMA],
        compiler_params=params(**({"collective_id": 0, "has_side_effects": True} if line else {})),
        name="front",
    )(x, gains, segments, parents, tree, freq, *masters)


def stacked(ref_block, h, group):
    n = LANES
    return jnp.concatenate(
        [ref_block[:, (h * group + g) * n:(h * group + g + 1) * n] for g in range(group)], axis=0)


def causal_tile(group, keys, rows, after):
    key_at = lax.broadcasted_iota(jnp.int32, (keys, rows * group), 0)
    query_at = lax.broadcasted_iota(jnp.int32, (keys, rows * group), 1) % rows
    return key_at <= query_at + after


def key_chunks(blocks, chunk):
    lax.fori_loop(0, blocks // 2, lambda j, c: (chunk(j * 2 * ROWS, 2 * ROWS, False), c)[1], 0)
    pl.when(blocks % 2 == 1)(lambda: chunk((blocks - 1) * ROWS, 2 * ROWS, True))
    pl.when(blocks % 2 == 0)(lambda: chunk(blocks * ROWS, ROWS, True))


def in_turn(i, first, steps, per, acts):
    for behind, act in acts:
        @pl.when(jnp.logical_and(i - first - behind >= 0, i - first - behind < steps))
        def _(behind=behind, act=act):
            for s in pair_of(i - first - behind, per):
                act(s)


def middle_kernel(kv, group, unit, line, per, steps, *refs):
    refs = list(refs)
    take = lambda count: [refs.pop(0) for _ in range(count)]
    q_ref, k_ref, vt_ref, tags_ref, bars_ref, wm_ref, gains_ref, x_all, dy_all = take(9)
    weights = take(2)
    ctx_out, lse_ref, base_ref, other_ref, gate_out, up_out, dh_ref, dhb_ref, dg_ref, gsh_out = take(10)
    acc_ref, sum_ref, x_ref, dy_ref, we_ref, ws_ref, copy_sems = take(7)
    h_ref, xn_ref, a_ref, dgu_ref, ctx_ref, gup_ref = take(6)
    h_held, h_near, h_far, h_sems, xn_sems = take(5)
    d_held, d_near, d_far, d_sems, stage, dh_sems = take(6)
    b_held, b_near, b_sems = take(3)
    place = Place(line)
    i = pl.program_id(0)
    n = LANES
    share, d = x_ref.shape
    units = ws_ref.shape[0]
    tile = 256
    attended = Exchange(place, per, h_held, h_near, h_far, h_ref, h_sems)
    norms = Spread(place, per, None, xn_ref, xn_sems)
    pulled_back = Exchange(place, per, d_held, d_near, d_far, dh_ref, d_sems)
    grads = Spread(place, per, stage, dhb_ref, dh_sems)
    branch = Pairs(place, per, b_held, b_near, b_sems, lambda s: s // per)
    own_share = x_all.at[pl.ds(pl.multiple_of(place.t * share, share), share), :]
    copies = [pltpu.make_async_copy(own_share, x_ref, copy_sems.at[0]),
              pltpu.make_async_copy(dy_all, dy_ref, copy_sems.at[1])]
    if line:
        gsh_ref = take(1)[0]
        shrink = Reduce(place, gsh_ref, column_cut(gsh_ref.shape[1] // (2 * line)), None, *take(3))
        gate_ref = take(1)[0]
        expand = Reduce(place, gate_ref, row_cut(gate_ref.shape[0] // (2 * line)), None, *take(3))
        cuts = (row_cut(weights[0].shape[0]), column_cut(weights[1].shape[1]))
        first, second = [Gather(place, weights[w], (we_ref, ws_ref)[w], cuts[w], *take(2)) for w in range(2)]
    else:
        gsh_ref, gate_ref = gsh_out, gate_out
        copies += [pltpu.make_async_copy(weights[0], we_ref, copy_sems.at[2]),
                   pltpu.make_async_copy(weights[1], ws_ref, copy_sems.at[3])]
    written = [pltpu.make_async_copy(ctx_ref, ctx_out, copy_sems.at[4]),
               pltpu.make_async_copy(gup_ref, up_out, copy_sems.at[5])]
    rows_of = lambda s: pl.ds(pl.multiple_of(s * SUB, SUB), SUB)

    def at_step(step, *acts):
        @pl.when(i == step)
        def _():
            for act in acts:
                act()

    @pl.when(i == 0)
    def _():
        place.greet(True, bool(line))
        if line:
            first.start()
        for copy in copies:
            copy.start()
        dg_ref[...] = jnp.zeros_like(dg_ref)


    def block(s):
        here = rows_of(s)
        bars = jnp.concatenate([bars_ref[here, :]] * group, axis=0)
        q = q_ref[here, :]
        wide = [jnp.concatenate([stacked(q, h, group), bars], axis=1) for h in range(kv)]
        acc_ref[...] = jnp.zeros_like(acc_ref)
        sum_ref[...] = jnp.zeros_like(sum_ref)

        def chunk(start, size, diagonal):
            at = pl.ds(pl.multiple_of(start, ROWS), size)
            tags = tags_ref[at, :]
            for h in range(kv):
                keys = jnp.concatenate([k_ref[at, h * n:(h + 1) * n], tags], axis=1)
                scores = dot(keys, wide[h], 1, 1)
                e = jnp.exp2(scores * unit)
                if diagonal:
                    e = jnp.where(causal_tile(group, size, SUB, (s % 2) * SUB + size - ROWS), e, 0.0)
                sum_ref[h] += fold_rows(e)
                acc_ref[h] += dot(vt_ref[h * n:(h + 1) * n, at], e.astype(BF))

        key_chunks(s // 2, chunk)
        parts = []
        for h in range(kv):
            sums = jnp.sum(sum_ref[h], axis=0, keepdims=True)
            lse_ref[s, h:h + 1, :] = jnp.log2(sums)
            ctx = (acc_ref[h] / sums).T
            parts += [ctx[g * SUB:(g + 1) * SUB] for g in range(group)]
        ctx_ref[here, :] = jnp.concatenate(parts, axis=1).astype(BF)

    def put_pair(pairs, blocks, part):
        for u, s in enumerate(blocks):
            pairs.put_next(s, part[u * SUB:(u + 1) * SUB])

    @pl.when(i < steps)
    def _():
        blocks = pair_of(i, per)
        for s in blocks:
            block(s)
        ctx = jnp.concatenate([ctx_ref[rows_of(s), :] for s in blocks], axis=0)
        put_pair(attended, blocks, dot(ctx, wm_ref[...]).astype(BF))

    def hidden_rows(s, at, summed):
        hidden = x_ref[at, :].astype(FP) + summed
        h_ref[at, :] = hidden
        xn_ref[rows_of(s), :] = (hidden * inverse_rms(hidden) * gains_ref[:, d:2 * d]).astype(BF)
        norms.send(s)

    at_step(1, copies[0].wait)
    at_step(steps, written[0].start)
    in_turn(i, 0, steps, per, ((1, attended.add_chip), (3, lambda s: attended.take(s, hidden_rows)), (5, norms.pass_on)))
    swiglu, feed = steps + 3, 2 * steps + 3
    if line:
        at_step(1, lambda: first.hop(1))
        at_step(3, lambda: first.hop(2))
        at_step(5, lambda: first.hop(3), second.start)
        at_step(7, lambda: second.hop(1))
        at_step(8, lambda: second.hop(2))
        at_step(9, lambda: second.hop(3), first.finish)
        at_step(feed, second.finish)
    else:
        at_step(swiglu, copies[2].wait, copies[3].wait)


    def gathered(ref, blocks):
        return jnp.concatenate([ref[rows_of(s), :] for s in blocks], axis=0)

    def keep(ref, blocks, values):
        for u, s in enumerate(blocks):
            ref[rows_of(s), :] = values[u * SUB:(u + 1) * SUB]

    def tiles(grad_ref, left_ref, right_ref, start, count, after):
        def one(t, carry):
            cut = pl.ds(pl.multiple_of(t * tile, tile), tile)
            there = pl.ds(pl.multiple_of((t + after) * tile, tile), tile)
            grad_ref[:, cut] = dot(left_ref[...], right_ref[:, there], 0, 0).astype(grad_ref.dtype)
            return carry

        lax.fori_loop(start, start + count, one, 0)

    @pl.when(jnp.logical_and(i >= swiglu, i < feed))
    def _():
        blocks = pair_of(i - swiglu, per)
        for s in blocks:
            norms.ready(s)
        gu = dot(gathered(xn_ref, blocks), we_ref[...])
        gate, up = gu[:, :units], gu[:, units:]
        keep(a_ref, blocks, (gate / (1.0 + jnp.exp(-gate)) * up).astype(BF))
        keep(dgu_ref, blocks, gu.astype(BF))

    at_step(feed - 1, copies[1].wait, lambda: tiles(gsh_ref, a_ref, dy_ref, 0, gsh_ref.shape[1] // tile, 0))
    if line:
        at_step(feed, shrink.start)

    @pl.when(jnp.logical_and(i >= feed, i < feed + steps))
    def _():
        blocks = pair_of(i - feed, per)
        gu = gathered(dgu_ref, blocks).astype(FP)
        gate, up = gu[:, :units], gu[:, units:]
        sig = 1.0 / (1.0 + jnp.exp(-gate))
        da = dot(gathered(dy_ref, blocks), ws_ref[...], 1, 1)
        dgu = jnp.concatenate([da * up * (sig * (1.0 + gate * (1.0 - sig))), da * (gate * sig)], axis=1).astype(BF)
        keep(dgu_ref, blocks, dgu)
        put_pair(pulled_back, blocks, dot(dgu, we_ref[...], 1, 1).astype(BF))

    def grad_rows(s, at, summed):
        pulled, gain_grad = rms_pull(h_ref[at, :], gains_ref[:, d:2 * d], summed)
        dh = dy_ref[rows_of(s), :].astype(FP) + pulled
        dh_ref[at, :] = dh
        dg_ref[...] += fold_rows(gain_grad)
        stage[s % per] = dh.astype(BF)
        grads.send(s)

    def chip_rows(mine, k, summed):
        at = rows_of(k)

        @pl.when(mine)
        def _():
            base_ref[at, :] = h_ref[at, :] + summed

        @pl.when(jnp.logical_not(mine))
        def _():
            other_ref[k] = summed.astype(BF)

    in_turn(i, feed, steps, per, ((1, pulled_back.add_chip), (3, lambda s: pulled_back.take(s, grad_rows)),
                                  (5, grads.pass_on)))

    @pl.when(jnp.logical_and(i >= feed + 3, i < feed + 3 + steps))
    def _():
        blocks = pair_of(i - feed - 3, per)
        put_pair(branch, blocks, dot(gathered(a_ref, blocks), ws_ref[...]).astype(BF))

    in_turn(i, feed, steps, per, ((4, lambda s: branch.add(s, chip_rows)),))
    if line:
        for k, step in enumerate((2, 4, 5), 1):
            at_step(feed + step, lambda k=k: shrink.step(k))
    half = units // tile
    at_step(feed + steps, lambda: tiles(gate_ref, xn_ref, dgu_ref, 0, half, 0))
    if line:
        at_step(feed + steps, expand.start)
        for k in range(1, line):
            at_step(feed + steps + k, lambda k=k: expand.step(k))
    at_step(feed + steps + 1, lambda: tiles(gup_ref, xn_ref, dgu_ref, 0, half, half), written[1].start)

    @pl.when(i == feed + steps + 4)
    def _():
        attended.drain()
        pulled_back.drain()
        norms.drain()
        grads.drain()
        for t in range(4):
            branch.sent(t * per + per - 1)
        lax.fori_loop(0, 4 * per, lambda s, c: (grads.ready(s), c)[1], 0)
        for copy in written:
            copy.wait()
        if line:
            shrink.finish(write_to(gsh_out))
            shrink.drain()
            expand.finish(write_to(gate_out))
            expand.drain()
            first.drain()
            second.drain()


def middle(q, k, vt, tags, bars, wm, x, dy, gains, weights, kv, group, unit, line):
    length = q.shape[0]
    n = LANES
    d = wm.shape[1]
    share = (length // 4, d)
    per = share[0] // SUB
    steps = 2 * per
    we, ws = (w.shape for w in weights)
    shards = 2 * line
    shrink = jax.ShapeDtypeStruct(ws, BF)
    gate = jax.ShapeDtypeStruct((we[0], we[1] // 2), BF)
    more = []
    if line:
        shrink = jax.ShapeDtypeStruct(ws, FP)
        gate = jax.ShapeDtypeStruct(gate.shape, FP)
        we, ws = (we[0] * shards, we[1]), (ws[0], ws[1] * shards)
        more = [pltpu.VMEM(ws, BF), *reduce_scratch(line, shrink.shape), pltpu.VMEM((we[0], we[1] // 2), BF),
                *reduce_scratch(line, gate.shape), *GATHER_SEMS(shards), *GATHER_SEMS(shards)]
    units = ws[0]
    results = [jax.ShapeDtypeStruct(q.shape, BF), jax.ShapeDtypeStruct((length // SUB, 8, SUB * group), FP),
               jax.ShapeDtypeStruct(share, FP), jax.ShapeDtypeStruct((per, SUB, d), BF), gate,
               jax.ShapeDtypeStruct((we[0], units), BF), jax.ShapeDtypeStruct(share, FP),
               jax.ShapeDtypeStruct((length, d), BF), jax.ShapeDtypeStruct((8, d), FP),
               shrink]
    out_specs = [whole(r.shape) for r in results]
    for at in (0, 5, 7):
        out_specs[at] = ANYWHERE
    held = [q, k, vt, tags, bars, wm, gains]
    return pl.pallas_call(
        partial(middle_kernel, kv, group, unit, line, per, steps),
        grid=(3 * steps + 8,),
        in_specs=[whole(a.shape) for a in held] + [ANYWHERE] * 4,
        out_specs=out_specs,
        out_shape=results,
        scratch_shapes=[pltpu.VMEM((kv, n, SUB * group), FP), pltpu.VMEM((kv, 8, SUB * group), FP),
                        pltpu.VMEM(share, BF), pltpu.VMEM((length, d), BF), pltpu.VMEM(we, BF), pltpu.VMEM(ws, BF),
                        pltpu.SemaphoreType.DMA((6,)),
                        pltpu.VMEM(share, FP), pltpu.VMEM((length, d), BF), pltpu.VMEM((length, units), BF),
                        pltpu.VMEM((length, 2 * units), BF), pltpu.VMEM(q.shape, BF), pltpu.VMEM((we[0], units), BF),
                        *pairs_scratch(per, d, True), pltpu.SemaphoreType.DMA((4, 4 * per)),
                        *pairs_scratch(per, d, True), pltpu.VMEM((per, SUB, d), BF),
                        pltpu.SemaphoreType.DMA((4, 4 * per)),
                        *pairs_scratch(per, d, False), *more],
        compiler_params=params(collective_id=1, has_side_effects=True),
        name="middle",
    )(*held, x, dy, *weights)


def back_kernel(kv, group, unit, scale, blocks, per, line, *refs):
    refs = list(refs)
    take = lambda count: [refs.pop(0) for _ in range(count)]
    q_ref, k_ref, v_ref, kt_ref, tags_ref, bars_ref, lse_ref, ctx_block, dh_block, wm_ref = take(10)
    raw_ref, cos_ref, sin_ref, all_gains, base_ref, dg2_ref, other_ref = take(7)
    x_all, dh_all = take(2)
    late_from = take(4)
    grads = take(2) if line else []
    in_ref, out_ref, gains_out = take(3)
    sums = take(3) if line else []
    weight_grads = [] if line else take(2)
    late_to = take(4)
    wp_ref, ctx_ref, dh_ref, xn_ref = late_to
    late_sem = take(1)[0]
    late = [pltpu.make_async_copy(a, b, late_sem.at[w]) for w, (a, b) in enumerate(zip(late_from, late_to))]
    dk_ref, dv_ref, dq_ref, dqkv_ref = take(4)
    b_far, b_sems, x_held, x_near, x_sems = take(5)
    mine_ref, far_ref, x_far, f_sems, x_ref, dh_own, own_sems, heads_ref, fold_ref = take(9)
    place = Place(line)
    i = pl.program_id(0)
    b = blocks - 1 - i
    n = LANES
    pairs = Pairs(place, per, x_held, x_near, x_sems, lambda s: s % x_held.shape[0])
    subs = ROWS // SUB
    share, d = x_ref.shape
    gq, gk = all_gains[:, 2 * d:2 * d + n], all_gains[:, 2 * d + n:]
    tile = 256
    tensors = lax.axis_size("tensor")
    mates = [(place.dp, (place.t + step) % tensors) for step in range(1, tensors)]
    peers = []
    own_rows = pl.ds(pl.multiple_of(place.t * share, share), share)
    own_copies = [pltpu.make_async_copy(x_all.at[own_rows, :], x_ref, own_sems.at[0]),
                  pltpu.make_async_copy(dh_all, dh_own, own_sems.at[1])]
    if line:
        shards = 2 * line
        gm_ref, gp_ref = take(2)
        expand = Reduce(place, grads[1], row_cut(grads[1].shape[0] // shards), *take(4))
        merge = Reduce(place, gm_ref, column_cut(gm_ref.shape[1] // shards), None, *take(3))
        project = Reduce(place, gp_ref, row_cut(gp_ref.shape[0] // shards), None, *take(3))
        shown, over, g_sems = take(3)
        peers = [((place.dp + step) % shards, place.t) for step in range(1, shards)]
    else:
        gp_ref, gm_ref = weight_grads

    def tiles(grad_ref, left_ref, right_ref):
        def one(t, carry):
            cut = pl.ds(pl.multiple_of(t * tile, tile), tile)
            grad_ref[:, cut] = dot(left_ref[...], right_ref[:, cut], 0, 0).astype(grad_ref.dtype)
            return carry

        lax.fori_loop(0, grad_ref.shape[1] // tile, one, 0)

    def write_up(values):
        sums[0][:, 0, :] = grads[0][...]
        sums[0][:, 1, :] = values

    def project_rows(t):
        cut = pl.ds(pl.multiple_of(t * tile, tile), tile)
        gp_ref[cut, :] = dot(xn_ref[:, cut], dqkv_ref[...], 0, 0).astype(BF)

    def chip(k):
        return send(far_ref.at[k], x_far.at[k], f_sems.at[0, k], f_sems.at[1, k], place.chip)

    def branch(k):
        return send(other_ref.at[k], b_far.at[k], b_sems.at[0, k], b_sems.at[1, k], place.chip)

    @pl.when(i == 0)
    def _():
        barrier = pltpu.get_barrier_semaphore()
        for device in mates + peers:
            pl.semaphore_signal(barrier, inc=1, device_id=device, device_id_type=MESH)
        for copy in late:
            copy.start()
        pl.semaphore_wait(barrier, len(mates + peers))
        if line:
            expand.start()
        for k in range(per):
            branch(k).start()
        dk_ref[...] = jnp.zeros_like(dk_ref)
        dv_ref[...] = jnp.zeros_like(dv_ref)
        heads_ref[...] = jnp.zeros_like(heads_ref)

    @pl.when(i < blocks)
    def _():
        here = pl.ds(pl.multiple_of(b * ROWS, ROWS), ROWS)
        dctx = dot(dh_block[...], wm_ref[...], 1, 1).astype(BF)
        ctx, q = ctx_block[...], q_ref[...]
        bars = jnp.concatenate([bars_ref[...]] * group, axis=0)
        wide, queries, outward, centres, lses = [], [], [], [], []
        ones = jnp.ones((8, n), BF)
        for h in range(kv):
            queries.append(stacked(q, h, group))
            wide.append(jnp.concatenate([queries[h], bars], axis=1))
            outward.append(stacked(dctx, h, group))
            both = outward[h].astype(FP) * stacked(ctx, h, group).astype(FP)
            high = both.astype(BF)
            low = (both - high.astype(FP)).astype(BF)
            centres.append((dot(ones, high, 1, 1) + dot(ones, low, 1, 1))[:1])
            lses.append(jnp.concatenate([lse_ref[u, h:h + 1, g * SUB:(g + 1) * SUB]
                                         for g in range(group) for u in range(ROWS // SUB)], axis=1))
        dq_ref[...] = jnp.zeros_like(dq_ref)

        def chunk(start, size, diagonal):
            at = pl.ds(pl.multiple_of(start, ROWS), size)
            tags = tags_ref[at, :]
            for h in range(kv):
                cut = slice(h * n, (h + 1) * n)
                keys = jnp.concatenate([k_ref[at, cut], tags], axis=1)
                p = jnp.exp2(dot(keys, wide[h], 1, 1) * unit - lses[h])
                if diagonal:
                    p = jnp.where(causal_tile(group, size, ROWS, size - ROWS), p, 0.0)
                dp = dot(v_ref[at, cut], outward[h], 1, 1)
                ds = (p * (dp - centres[h])).astype(BF)
                dv_ref[at, cut] += dot(p.astype(BF), outward[h])
                dk_ref[at, cut] += dot(ds, queries[h])
                dq_ref[h] += dot(kt_ref[cut, at], ds)

        key_chunks(b, chunk)

        cosines, sines = cos_ref[...], sin_ref[...]
        pieces = []
        for h in range(kv):
            dq = dq_ref[h].T
            for c in range(group + 1):
                if c < group:
                    grad, gain, row = dq[c * ROWS:(c + 1) * ROWS] * scale, gq, 0
                else:
                    grad, gain, row = dk_ref[here, h * n:(h + 1) * n] * scale, gk, 1
                grad = grad * cosines - pltpu.roll(grad, n // 2, 1) * sines
                at = (h * (group + 1) + c) * n
                piece, gain_grad = rms_pull(raw_ref[:, at:at + n], gain, grad)
                heads_ref[row] += fold_rows(gain_grad)
                pieces.append(piece)
            pieces.append(dv_ref[here, h * n:(h + 1) * n])
        dqkv = jnp.concatenate(pieces, axis=1).astype(BF)
        dqkv_ref[here, :] = dqkv
        pl.when(i == 0)(late[0].wait)
        part = dot(dqkv, wp_ref[...], 1, 1).astype(BF)
        for u in range(subs):
            s = subs * b + u
            pairs.put(s, part[u * SUB:(u + 1) * SUB], (i >= 2, s + 2 * subs))

    def chip_rows(mine, k, summed):
        @pl.when(mine)
        def _():
            mine_ref[pl.ds(pl.multiple_of(k * SUB, SUB), SUB), :] = summed

        @pl.when(jnp.logical_not(mine))
        def _():
            far_ref[k] = summed.astype(BF)
            chip(k).start()

    @pl.when(i >= 1)
    def _():
        for u in range(subs):
            pairs.add(subs * (b + 1) + u, chip_rows)

    @pl.when(i == 3)
    def _():
        for k in range(per):
            branch(k).wait()
            at = slice(k * SUB, (k + 1) * SUB)
            out_ref[at, :] = (base_ref[at, :] + b_far[k].astype(FP)).astype(BF)
        for copy in own_copies:
            copy.start()

    @pl.when(i == 1)
    def _():
        late[1].wait()
        late[2].wait()
        tiles(gm_ref, ctx_ref, dh_ref)

    if line:
        for step, act in enumerate((lambda: expand.step(1), lambda: expand.step(2), lambda: expand.step(3), merge.start,
                                    lambda: merge.step(1), lambda: merge.step(2))):
            pl.when(i == step)(act)

    def input_rows(k):
        at = slice(k * SUB, (k + 1) * SUB)
        chip(k).wait()
        summed = mine_ref[at, :] + x_far[k].astype(FP)
        pulled, gain_grad = rms_pull(x_ref[at, :].astype(FP), all_gains[:, :d], summed)
        in_ref[at, :] = (dh_own[at, :] + pulled).astype(BF)
        fold_ref[...] += fold_rows(gain_grad)

    def folded(ref):
        pieces = [fold_ref[...], dg2_ref[...], heads_ref[0], heads_ref[1]]
        row = jnp.sum(jnp.concatenate(pieces, axis=1), axis=0, keepdims=True)
        count = row.shape[1] // n
        for j in range(count):
            ref[j:j + 1, :] = row[:, j * n:(j + 1) * n]
        ref[count:, :] = jnp.zeros((ref.shape[0] - count, n), FP)

    def show(buffer, me, devices, first):
        copies = [send(buffer.at[me], buffer.at[me], g_sems.at[0, first + step], g_sems.at[1, first + step], device)
                  for step, device in enumerate(devices, 1)]
        for copy in copies:
            copy.start()
        return copies

    def added(buffer, me, devices, first):
        count = len(devices) + 1
        for step in range(1, count):
            who = (me - step + count) % count
            send(buffer.at[who], buffer.at[who], g_sems.at[0, first + step], g_sems.at[1, first + step],
                 place.sibling).wait_recv()
        total = buffer[0]
        for who in range(1, count):
            total = total + buffer[who]
        return total

    @pl.when(i == blocks)
    def _():
        fold_ref[...] = jnp.zeros_like(fold_ref)
        late[3].wait()
        for copy in own_copies:
            copy.wait()
        if not line:
            tiles(gp_ref, xn_ref, dqkv_ref)
            for k in range(per):
                input_rows(k)
            folded(gains_out)
        else:
            project_rows(project.turn(0))
            project.start()
            for q in range(1, line):
                project_rows(project.turn(q))
            merge.step(3)
            expand.finish(write_up)
            project.step(1)
            merge.finish(write_to(sums[1]))
            project.step(2)
            for k in range(per):
                input_rows(k)
            folded(shown.at[place.t])
            copies = show(shown, place.t, mates, 0)
            project.step(3)
            over[place.dp] = added(shown, place.t, mates, 0)
            copies += show(over, place.dp, peers, tensors)
            project.finish(write_to(sums[2]))
            gains_out[...] = added(over, place.dp, peers, tensors)
            for copy in copies:
                copy.wait_send()
            for r in (expand, merge, project):
                r.drain()
        for s in range(2 * subs):
            pairs.sent(s)


def back(q, k, v, kt, tags, bars, lse, ctx, dh, wm, wp, raw, cosines, sines, gains, xn, base, dg2, other, x, dh_own,
         grads, kv, group, unit, scale, line):
    length = q.shape[0]
    n = LANES
    d = wm.shape[1]
    blocks = length // ROWS
    per = other.shape[0]
    share = base.shape
    block_of = lambda i: jnp.maximum(blocks - 1 - i, 0)
    rows = lambda w: pl.BlockSpec((ROWS, w), lambda i: (block_of(i), 0))
    late = [wp, ctx, dh, xn]
    gain_rows = (-(-(gains.shape[1] // n) // 8) * 8, n)
    scratch = [*[pltpu.VMEM(a.shape, BF) for a in late], pltpu.SemaphoreType.DMA((4,)),
               pltpu.VMEM((length, kv * n), FP), pltpu.VMEM((length, kv * n), FP),
               pltpu.VMEM((kv, n, ROWS * group), FP), pltpu.VMEM((length, wp.shape[1]), BF),
               pltpu.VMEM((per, SUB, d), BF), pltpu.SemaphoreType.DMA((2, per)),
               pltpu.VMEM((2 * ROWS // SUB, SUB, d), BF), pltpu.VMEM((2 * per, SUB, d), BF),
               pltpu.SemaphoreType.DMA((2, 4 * per)),
               pltpu.VMEM(share, FP), pltpu.VMEM((per, SUB, d), BF), pltpu.VMEM((per, SUB, d), BF),
               pltpu.SemaphoreType.DMA((2, per)), pltpu.VMEM(share, BF), pltpu.VMEM(share, FP),
               pltpu.SemaphoreType.DMA((2,)), pltpu.VMEM((2, 8, n), FP), pltpu.VMEM((8, d), FP)]
    results = [jax.ShapeDtypeStruct(share, BF), jax.ShapeDtypeStruct(share, BF), jax.ShapeDtypeStruct(gain_rows, FP)]
    if line:
        shards = 2 * line
        own = [grads[0].shape, (wm.shape[0], wm.shape[1] // shards),
               (wp.shape[0] // shards, wp.shape[1])]
        views = ((own[0][0], 2, own[0][1]), own[1], (own[2][0], own[2][1] // n, n))
        results += [jax.ShapeDtypeStruct(s, FP) for s in views]
        scratch += [pltpu.VMEM(wm.shape, BF), pltpu.VMEM(wp.shape, BF)]
        for w, s in enumerate(own):
            scratch += reduce_scratch(line, s, w == 0)
        scratch += [pltpu.VMEM((4, *gain_rows), FP), pltpu.VMEM((shards, *gain_rows), FP),
                    pltpu.SemaphoreType.DMA((2, 4 + shards))]
    else:
        results += [jax.ShapeDtypeStruct(wp.shape, BF), jax.ShapeDtypeStruct(wm.shape, BF)]
    args = [q, k, v, kt, tags, bars, lse, ctx, dh, wm, raw, cosines, sines, gains, base, dg2]
    more = [other, x, dh_own, *late, *grads]
    specs = [whole(a.shape) for a in args] + [ANYWHERE] * len(more)
    if line:
        specs[-2] = whole(grads[0].shape)
    for at in (0, 5, 7, 8, 10, 11, 12):
        specs[at] = rows(args[at].shape[1])
    specs[6] = pl.BlockSpec((ROWS // SUB, 8, SUB * group), lambda i: (block_of(i), 0, 0))
    return pl.pallas_call(
        partial(back_kernel, kv, group, unit, scale, blocks, per, line),
        grid=(blocks + 1,),
        in_specs=specs,
        out_specs=[whole(r.shape) for r in results],
        out_shape=results,
        scratch_shapes=scratch,
        compiler_params=params(collective_id=3, has_side_effects=True),
        name="back",
    )(*args, *more)


def adamw_step(weight, moment_one, moment_two, gradient, step_rate, decay):
    mean_next = BETA_ONE * moment_one + (1.0 - BETA_ONE) * gradient
    square_next = BETA_TWO * moment_two + (1.0 - BETA_TWO) * gradient * gradient
    mean_hat = mean_next / (1.0 - BETA_ONE**STEP)
    square_hat = square_next / (1.0 - BETA_TWO**STEP)
    weight_next = weight - step_rate * (mean_hat / (jnp.sqrt(square_hat) + EPS_ADAM) + decay * weight)
    return weight_next, mean_next, square_next


def shards(
    tokens, cotangent, parents, token_segment, tree_id,
    projection_weight, projection_first_moment, projection_second_moment,
    merge_master, merge_mean, merge_square,
    expand_master, expand_mean, expand_square,
    shrink_master, shrink_mean, shrink_square,
    gain_master, gain_mean, gain_square,
):
    x = tokens[0]
    dy = cotangent[0]
    length, d = x.shape
    d_own, kv, per, n = projection_weight.shape
    group = per - 2
    units = expand_master.shape[2]
    scale = n ** (-0.5)
    unit = scale * math.log2(math.e)
    line = 4 if lax.axis_size("dp") == 8 and d_own % LANES == 0 else 0
    if line:
        masters = (projection_weight.reshape(d_own, kv * per, n), merge_master, expand_master, shrink_master)
    else:
        wp, we = (lax.all_gather(w.astype(BF).reshape(d_own, -1), "dp", axis=0, tiled=True)
                  for w in (projection_weight, expand_master))
        wm, ws = (lax.all_gather(w.astype(BF), "dp", axis=1, tiled=True) for w in (merge_master, shrink_master))
        masters = (wp,)

    gains = gain_master[None]
    fronts = front(x, gains, token_segment, parents, tree_id, masters, kv, group, line)
    xn1, q, k, v, kt, vt, raw, tags, bars, cosines, sines = fronts[:11]
    if line:
        wp, wm, *low = fronts[11:]
    else:
        low = (we, ws)
    ctx, lse, base, other, gate_sum, up_grad, dh, dhb, dg2, shrink_sum = middle(
        q, k, vt, tags, bars, wm, x, dy, gains, low, kv, group, unit, line)
    backs = back(q, k, v, kt, tags, bars, lse, ctx, dhb, wm, wp, raw, cosines, sines, gains, xn1,
                 base, dg2, other, x, dh, (gate_sum, up_grad) if line else (), kv, group, unit, scale, line)
    input_grad, output, gain_rows = backs[:3]
    if line:
        expand_sum, merge_sum, project_sum = backs[3:]
    else:
        gain_rows = lax.psum(gain_rows, ("dp", "tensor"))
        project_sum, expand_sum = (
            lax.psum_scatter(g, "dp", scatter_dimension=0, tiled=True) for g in (backs[3], jnp.concatenate([gate_sum, up_grad], axis=1)))
        merge_sum, shrink_sum = (
            lax.psum_scatter(g, "dp", scatter_dimension=1, tiled=True) for g in (backs[4], shrink_sum))
    output, input_grad = output[None], input_grad[None]
    gain_grad = gain_rows.reshape(-1)[:gain_master.shape[0]]

    outs = [output, input_grad]
    for weight, mean, square, grad, rate in (
        (projection_weight, projection_first_moment, projection_second_moment, project_sum, RATE_PROJECT),
        (merge_master, merge_mean, merge_square, merge_sum, RATE_MERGE),
        (expand_master, expand_mean, expand_square, expand_sum, RATE_EXPAND),
        (shrink_master, shrink_mean, shrink_square, shrink_sum, RATE_SHRINK),
    ):
        grad = grad.astype(FP).reshape(weight.shape)
        after, mean_next, square_next = adamw_step(weight, mean, square, grad, rate, DECAY)
        outs += [after, mean_next, square_next, after.astype(BF)]
    gain_next, gain_mean_next, gain_square_next = adamw_step(
        gain_master, gain_mean, gain_square, gain_grad, RATE_GAIN, 0.0)
    return (*outs, gain_mean_next, gain_square_next, gain_next)


def solution(mesh):
    tokens = P("dp", None, None)
    project = P("dp", "tensor", None, None)
    columns = P("tensor", "dp")
    expand = P("dp", None, "tensor")
    shared = P("dp", "tensor", None)
    return jax.shard_map(
        shards,
        mesh=mesh,
        in_specs=(tokens, tokens, P(), P("dp", None), P("dp"), *[project] * 3, *[columns] * 3, *[expand] * 3,
                  *[columns] * 3, P(), P(), P()),
        out_specs=(shared, shared, *[project] * 4, *[columns] * 4, *[expand] * 4, *[columns] * 4, P(), P(), P()),
        check_vma=False,
    )
```

```python
import math
from functools import partial

import jax
import jax.numpy as jnp
import numpy as np
from jax import lax
from jax.experimental import pallas as pl
from jax.experimental.pallas import tpu as pltpu
from jax.sharding import PartitionSpec as P

STEP = 5
EPS_NORM = 1e-06
THETA = 1000000.0
BETA_ONE = 0.5
BETA_TWO = 0.5
EPS_ADAM = 1e-08
DECAY = 0.1
RATE_PROJECT = 0.05
RATE_MERGE = 0.3
RATE_EXPAND = 0.05
RATE_SHRINK = 0.03
RATE_GAIN = 0.3

BF = jnp.bfloat16
FP = jnp.float32
ROWS = 256
LANES = 128
SUB = 128
MESH = pl.DeviceIdType.MESH
BLOCKED = -1e30
VMEM_LIMIT = 56 * 2**20


def params(**more):
    return pltpu.CompilerParams(vmem_limit_bytes=VMEM_LIMIT, **more)


def dot(a, b, ca=1, cb=0):
    return lax.dot_general(a, b, (((ca,), (cb,)), ((), ())), preferred_element_type=FP)


def inverse_rms(values):
    return lax.rsqrt(jnp.mean(values * values, axis=-1, keepdims=True) + EPS_NORM)


def rms_pull(values, scales, grad):
    r = inverse_rms(values)
    scaled = grad * scales
    mean = jnp.mean(values * scaled, axis=-1, keepdims=True)
    return r * scaled - values * (r * r * r * mean), grad * values * r


def fold_rows(values):
    n, w = values.shape
    return jnp.sum(values.reshape(n // 8, 8, w), axis=0)


class Place:
    def __init__(self, line):
        self.line = line
        self.dp, self.t = lax.axis_index("dp"), lax.axis_index("tensor")
        self.z, self.y = self.dp // 2, self.dp % 2
        self.x, self.c = self.t // 2, self.t % 2
        self.has_up, self.has_down = self.z < line - 1, self.z > 0
        self.up, self.down = (self.dp + 2, self.t), (self.dp - 2, self.t)
        self.across = (self.dp + 1 - 2 * self.y, self.t)
        self.sibling = (self.dp, self.t + 1 - 2 * self.c)
        self.chip = (self.dp, (1 - self.x) * 2 + self.c)

    def greet(self, tensor, line, meanwhile=None):
        barrier = pltpu.get_barrier_semaphore()

        def signal(device):
            pl.semaphore_signal(barrier, inc=1, device_id=device, device_id_type=MESH)

        if tensor:
            signal(self.sibling)
            signal(self.chip)
        if line:
            signal(self.across)
            pl.when(self.has_up)(lambda: signal(self.up))
            pl.when(self.has_down)(lambda: signal(self.down))
        peers = (2 if tensor else 0) + (1 if line else 0)
        if line:
            peers = peers + jnp.where(self.has_up, 1, 0) + jnp.where(self.has_down, 1, 0)
        if meanwhile is not None:
            meanwhile()
        pl.semaphore_wait(barrier, peers)


def send(src, dst, sent, arrived, device):
    return pltpu.make_async_remote_copy(
        src_ref=src, dst_ref=dst, send_sem=sent, recv_sem=arrived, device_id=device, device_id_type=MESH)


def row_cut(size):
    return lambda j: (pl.ds(pl.multiple_of(j * size, size), size), slice(None))


def column_cut(size):
    return lambda j: (slice(None), pl.ds(pl.multiple_of(j * size, size), size))


class Gather:
    def __init__(self, place, own, full, cut, sems, local):
        self.place, self.own, self.full, self.cut, self.sems, self.local = place, own, full, cut, sems, local

    def copy(self, kind, src, j):
        p = self.place
        device = (p.up, p.down, p.across)[kind]
        return send(src, self.full.at[self.cut(j)], self.sems.at[kind, j], self.sems.at[3, j], device)

    def kept(self):
        return pltpu.make_async_copy(self.own, self.full.at[self.cut(self.place.dp)], self.local)

    def source(self):
        return self.full.at[self.cut(self.place.dp)] if self.own is None else self.own

    def start(self):
        p = self.place
        self.copy(2, self.source(), p.dp).start()
        pl.when(p.has_up)(lambda: self.copy(0, self.source(), p.dp).start())
        pl.when(p.has_down)(lambda: self.copy(1, self.source(), p.dp).start())
        if self.own is not None:
            self.kept().start()

    def arrivals(self, k):
        p = self.place
        return ((0, p.z >= k, (p.z - k) * 2 + p.y, p.has_up), (1, p.z + k < p.line, (p.z + k) * 2 + p.y, p.has_down))

    def hop(self, k):
        for kind, here, j, further in self.arrivals(k):
            @pl.when(here)
            def _(kind=kind, j=j, further=further):
                piece = self.full.at[self.cut(j)]
                self.copy(kind, piece, j).wait_recv()
                pl.when(further)(lambda: self.copy(kind, piece, j).start())
                self.copy(2, piece, j).start()

    def finish(self):
        p = self.place
        if self.own is not None:
            self.kept().wait()
        for zz in range(p.line):
            j = zz * 2 + 1 - p.y
            self.copy(2, self.full.at[self.cut(j)], j).wait_recv()

    def drain(self):
        p = self.place
        self.copy(2, self.source(), p.dp).wait_send()
        pl.when(p.has_up)(lambda: self.copy(0, self.source(), p.dp).wait_send())
        pl.when(p.has_down)(lambda: self.copy(1, self.source(), p.dp).wait_send())
        for k in range(1, p.line):
            for kind, here, j, further in self.arrivals(k):
                @pl.when(here)
                def _(kind=kind, j=j, further=further):
                    piece = self.full.at[self.cut(j)]
                    pl.when(further)(lambda: self.copy(kind, piece, j).wait_send())
                    self.copy(2, piece, j).wait_send()


class Reduce:
    def __init__(self, place, grad, cut, kept, across, lined, sems):
        self.place, self.grad, self.cut, self.kept, self.sems = place, grad, cut, kept, sems
        self.across, self.lined = across, lined

    def cross(self, zz):
        p = self.place
        return send(self.grad.at[self.cut(zz * 2 + 1 - p.y)], self.across.at[zz],
                    self.sems.at[0, zz], self.sems.at[1, zz], p.across)

    def climb(self, t):
        return send(self.across.at[t], self.lined.at[t + 1], self.sems.at[2, t], self.sems.at[3, t], self.place.up)

    def sink(self, t):
        return send(self.across.at[t], self.lined.at[t], self.sems.at[4, t], self.sems.at[5, t], self.place.down)

    def load(self, zz):
        return pltpu.make_async_copy(self.grad.at[self.cut(zz * 2 + self.place.y)], self.kept.at[zz], self.sems.at[6, zz])

    def mine(self, zz):
        if self.kept is None:
            return self.grad[self.cut(zz * 2 + self.place.y)].astype(FP)
        return self.kept[zz].astype(FP)

    def loaded(self, zz):
        if self.kept is not None:
            self.load(zz).wait()

    def turn(self, q):
        z = self.place.z
        low = z < 2
        if q == 0:
            return jnp.where(low, 3, 0)
        if q == 1:
            return jnp.where(low, 2, 1)
        if q == 2:
            return jnp.where(low, 1 - z, 5 - z)
        return z

    def start(self):
        self.cross(self.turn(0)).start()
        if self.kept is not None:
            for zz in range(self.place.line):
                self.load(zz).start()

    def advance(self, q):
        self.cross(self.turn(q - 1)).wait_send()
        self.cross(self.turn(q)).start()

    def hop(self, h):
        p = self.place

        def pass_on(t, coming, more, slot):
            self.loaded(t)
            self.cross(t).wait_recv()

            @pl.when(jnp.logical_not(more))
            def _():
                self.across[t] = (self.mine(t) + self.across[t].astype(FP)).astype(BF)

            @pl.when(more)
            def _():
                coming(t).wait_recv()
                self.across[t] = (self.mine(t) + self.across[t].astype(FP) + self.lined[slot].astype(FP)).astype(BF)

            coming(t).start()

        pl.when(p.z < h)(lambda: pass_on(p.z + p.line - h, self.climb, p.has_down, p.z + p.line - h + 1))
        pl.when(p.z >= p.line - h)(lambda: pass_on(p.z - p.line + h, self.sink, p.has_up, p.z - p.line + h))

    def finish(self, write):
        p = self.place
        self.loaded(p.z)
        self.cross(p.z).wait_recv()
        pl.when(p.has_down)(lambda: self.climb(p.z).wait_recv())
        pl.when(p.has_up)(lambda: self.sink(p.z).wait_recv())
        from_below = jnp.where(p.has_down, self.lined[p.z + 1].astype(FP), 0.0)
        from_above = jnp.where(p.has_up, self.lined[p.z].astype(FP), 0.0)
        write(self.mine(p.z) + self.across[p.z].astype(FP) + from_below + from_above)

    def step(self, k):
        self.advance(k)
        self.hop(k)

    def drain(self):
        p = self.place
        self.cross(p.z).wait_send()
        for zz in range(p.line):
            pl.when(zz > p.z)(lambda zz=zz: self.climb(zz).wait_send())
            pl.when(zz < p.z)(lambda zz=zz: self.sink(zz).wait_send())


def write_to(ref):
    def write(values):
        if len(ref.shape) == 2:
            ref[...] = values
            return
        width = ref.shape[2]
        for j in range(ref.shape[1]):
            ref[:, j, :] = values[:, j * width:(j + 1) * width]

    return write


def reduce_scratch(line, shape, kept=False):
    return [pltpu.VMEM((line, *shape), BF)] * kept + [pltpu.VMEM((line, *shape), BF), pltpu.VMEM((line + 1, *shape), BF),
                                                      pltpu.SemaphoreType.DMA((7, line))]


class Pairs:
    def __init__(self, place, per, held, near, sems, slot_of):
        self.place, self.per, self.held, self.near, self.sems, self.slot_of = place, per, held, near, sems, slot_of

    def near_slot(self, s):
        return (s // (2 * self.per)) * self.per + s % self.per

    def to_sibling(self, s):
        return send(self.held.at[self.slot_of(s)], self.near.at[self.near_slot(s)], self.sems.at[0, s],
                    self.sems.at[1, s], self.place.sibling)

    def sends(self, s):
        return self.place.c != (s // self.per) % 2

    def sent(self, s):
        pl.when(self.sends(s))(lambda: self.to_sibling(s).wait_send())

    def put(self, s, rows, before=None):
        if before is not None:
            pl.when(before[0])(lambda: self.sent(before[1]))
        self.held[self.slot_of(s)] = rows
        pl.when(self.sends(s))(lambda: self.to_sibling(s).start())

    def put_next(self, s, rows):
        self.put(s, rows, (s % self.per >= 1, s - 1))

    def add(self, s, use):
        t = s // self.per

        @pl.when(self.place.c == t % 2)
        def _():
            self.to_sibling(s).wait_recv()
            use(self.place.x == t // 2, s % self.per,
                self.held[self.slot_of(s)].astype(FP) + self.near[self.near_slot(s)].astype(FP))


class Exchange(Pairs):
    def __init__(self, place, per, held, near, far, total, sems):
        super().__init__(place, per, held, near, sems, lambda s: s // per)
        self.far, self.total = far, total

    def rows(self, k):
        return pl.ds(pl.multiple_of(k * SUB, SUB), SUB)

    def to_chip(self, s):
        return send(self.near.at[self.near_slot(s)], self.far.at[s % self.per], self.sems.at[2, s], self.sems.at[3, s],
                    self.place.chip)

    def add_chip(self, s):
        def use(mine, k, summed):
            @pl.when(jnp.logical_not(mine))
            def _():
                self.near[self.near_slot(s)] = summed.astype(BF)
                self.to_chip(s).start()

            @pl.when(mine)
            def _():
                self.total[self.rows(k), :] = summed

        self.add(s, use)

    def take(self, s, use):
        @pl.when(s // self.per == self.place.t)
        def _():
            k = s % self.per
            self.to_chip(s).wait_recv()
            use(s, self.rows(k), self.total[self.rows(k), :] + self.far[k].astype(FP))

    def drain(self):
        p = self.place

        def one(s, carry):
            t = s // self.per
            pl.when(s % self.per == self.per - 1)(lambda: self.sent(s))
            pl.when(jnp.logical_and(p.c == t % 2, p.x != t // 2))(lambda: self.to_chip(s).wait_send())
            return carry

        lax.fori_loop(0, 4 * self.per, one, 0)


def pair_of(step, per):
    t = step % 2
    return t * per + step // 2, (3 - t) * per + step // 2


def pairs_scratch(per, d, exchange):
    rows = [pltpu.VMEM((4, SUB, d), BF), pltpu.VMEM((2 * per, SUB, d), BF)]
    return rows + [pltpu.VMEM((per, SUB, d), BF)] * exchange + [pltpu.SemaphoreType.DMA((4 if exchange else 2, 4 * per))]


class Spread:
    def __init__(self, place, per, stage, full, sems):
        self.place, self.per, self.stage, self.full, self.sems = place, per, stage, full, sems

    def rows(self, s):
        return self.full.at[pl.ds(pl.multiple_of(s * SUB, SUB), SUB), :]

    def source(self, s):
        return self.rows(s) if self.stage is None else self.stage.at[s % self.per]

    def copy(self, kind, src, s):
        device = (self.place.chip, self.place.sibling)[kind]
        return send(src, self.rows(s), self.sems.at[kind, s], self.sems.at[2, s], device)

    def kept(self, s):
        return pltpu.make_async_copy(self.source(s), self.rows(s), self.sems.at[3, s])

    def send(self, s):
        for kind in (0, 1):
            self.copy(kind, self.source(s), s).start()
        if self.stage is not None:
            self.kept(s).start()

    def owns(self, s):
        return s // self.per == self.place.t

    def passes(self, s):
        t = s // self.per
        return jnp.logical_and(self.place.c == t % 2, self.place.x != t // 2)

    def pass_on(self, s):
        @pl.when(self.passes(s))
        def _():
            self.copy(1, self.rows(s), s).wait_recv()
            self.copy(1, self.rows(s), s).start()

    def ready(self, s):
        if self.stage is not None:
            pl.when(self.owns(s))(lambda: self.kept(s).wait())
        pl.when((s // self.per) % 2 != self.place.c)(lambda: self.copy(1, self.rows(s), s).wait_recv())

    def drain(self):
        def one(s, carry):
            @pl.when(self.owns(s))
            def _():
                self.copy(0, self.source(s), s).wait_send()
                self.copy(1, self.source(s), s).wait_send()

            pl.when(self.passes(s))(lambda: self.copy(1, self.rows(s), s).wait_send())
            return carry

        lax.fori_loop(0, 4 * self.per, one, 0)


def whole(shape):
    return pl.BlockSpec(tuple(shape), lambda i: (0,) * len(shape), pipeline_mode=pl.Buffered(1))


ANYWHERE = pl.BlockSpec(memory_space=pl.ANY)
GATHER_SEMS = lambda shards: [pltpu.SemaphoreType.DMA((4, shards)), pltpu.SemaphoreType.DMA]


def make_tables(seg_ref, parents_ref, tree_ref, freq_ref, tags_ref, bars_ref, cos_ref, sin_ref):
    count = parents_ref.shape[1]
    n = LANES
    blocks = sin_ref.shape[0] // ROWS
    lane = lax.broadcasted_iota(jnp.int32, (1, n), 1).astype(FP)
    place_of = lambda b: pl.ds(pl.multiple_of(b * ROWS, ROWS), ROWS)

    def columns(b, carry):
        sin_ref[place_of(b), :] = jnp.broadcast_to(seg_ref[:, place_of(b)].astype(FP), (n, ROWS)).T
        return carry

    def tally(b, carry):
        column = sin_ref[place_of(b), :]
        return (carry[0] + fold_rows(jnp.where(column == lane, 1.0, 0.0)),
                carry[1] + fold_rows(jnp.where(column < lane, 1.0, 0.0)))

    lax.fori_loop(0, blocks, columns, 0)
    sizes, starts = lax.fori_loop(0, blocks, tally, (jnp.zeros((8, n), FP), jnp.zeros((8, n), FP)))
    sizes, starts = (jnp.sum(a, axis=0, keepdims=True) for a in (sizes, starts))
    table = parents_ref[...]
    chosen = jnp.where(lax.broadcasted_iota(jnp.int32, table.shape, 0) == tree_ref[0], table, 0)
    chosen = jnp.sum(chosen.astype(FP), axis=0, keepdims=True)
    parents = jnp.zeros((1, n), FP)
    for b in range(count):
        parents = jnp.where(lane == b, chosen[:, b:b + 1], parents)
    shifts = jnp.where(lane != 0, sizes[:, :1], 0.0) - starts

    def rows(b, carry):
        at = place_of(b)
        column = sin_ref[at, :]
        hot = column == lane
        parent = jnp.sum(jnp.where(hot, parents, 0.0), axis=1, keepdims=True)
        above = jnp.where(jnp.logical_and(lane == parent, lane != 0), sizes, 0.0)
        first = (b * ROWS).astype(FP)
        position = (lax.broadcasted_iota(jnp.int32, (ROWS, 1), 0).astype(FP) + first
                    + jnp.sum(jnp.where(hot, shifts, 0.0) + above, axis=1, keepdims=True))
        tags_ref[at, :] = jnp.where(hot, 1.0, 0.0).astype(BF)
        open_to = jnp.logical_or(jnp.logical_or(hot, lane == parent), jnp.logical_or(lane == 0, lane >= count))
        bars_ref[at, :] = jnp.where(open_to, 0.0, BLOCKED).astype(BF)
        angles = position * freq_ref[...]
        cos_ref[at, :] = jnp.cos(angles)
        turned = jnp.sin(angles)
        sin_ref[at, :] = jnp.where(lane < n // 2, -turned, turned)
        return carry

    lax.fori_loop(0, blocks, rows, 0)


def front_kernel(kv, group, line, *refs):
    refs = list(refs)
    take = lambda count: [refs.pop(0) for _ in range(count)]
    x_ref, gains_ref, seg_ref, parents_ref, tree_ref, freq_ref = take(6)
    masters = take(4) if line else take(1)
    xn_ref, q_ref, k_ref, v_ref, kt_ref, vt_ref, raw_ref, tags_ref, bars_ref, cos_ref, sin_ref = take(11)
    if line:
        wp_out, wm_out, we_low, ws_low = take(4)
        wp_ref, wm_low, p_sems, p_local, m_sems, m_local, out_sem = take(7)
    else:
        wp_ref = masters[0]
    xn_full, xn_sem = take(2)
    i = pl.program_id(0)
    final = pl.num_programs(0) - 1
    d = x_ref.shape[1]
    n = LANES
    per = group + 2
    if line:
        place = Place(line)
        size = masters[0].shape[0]
        project = Gather(place, None, wp_ref, row_cut(size), p_sems, p_local)
        merge = Gather(place, wm_low, wm_out, column_cut(wm_low.shape[1]), m_sems, m_local)
        written = pltpu.make_async_copy(wp_ref, wp_out, out_sem)
    normed = pltpu.make_async_copy(xn_full, xn_ref, xn_sem)

    def round_projection():
        at = pl.ds(pl.multiple_of(place.dp * size, size), size)
        for j in range(kv * per):
            wp_ref[at, j * n:(j + 1) * n] = masters[0][:, j, :].astype(BF)

    def norm(b, carry):
        at = pl.ds(pl.multiple_of(b * ROWS, ROWS), ROWS)
        x = x_ref[at, :].astype(FP)
        xn_full[at, :] = (x * inverse_rms(x) * gains_ref[:, :d]).astype(BF)
        return carry

    @pl.when(i == 0)
    def _():
        if line:
            place.greet(False, True, round_projection)
            project.start()
        lax.fori_loop(0, x_ref.shape[0] // ROWS, norm, 0)
        normed.start()
        if line:
            project.hop(1)
        make_tables(seg_ref, parents_ref, tree_ref, freq_ref, tags_ref, bars_ref, cos_ref, sin_ref)
        if line:
            project.hop(2)
            wm_low[...] = masters[1][...].astype(BF)
            units = masters[2].shape[2]
            for half in range(2):
                we_low[:, half * units:(half + 1) * units] = masters[2][:, half, :].astype(BF)
            ws_low[...] = masters[3][...].astype(BF)
            project.hop(3)
            merge.start()
            project.finish()
            written.start()

    if line:
        for k in range(1, line):
            pl.when(i == k + 1)(lambda k=k: merge.hop(k))
    at = pl.ds(pl.multiple_of(i * ROWS, ROWS), ROWS)
    qkv = dot(xn_full[at, :], wp_ref[...])
    cosines, sines = cos_ref[at, :], sin_ref[at, :]
    gq, gk = gains_ref[:, 2 * d:2 * d + n], gains_ref[:, 2 * d + n:]
    keys, values = [], []
    for h in range(kv):
        for c in range(group + 1):
            raw = qkv[:, (h * per + c) * n:(h * per + c + 1) * n]
            to = (h * (group + 1) + c) * n
            raw_ref[:, to:to + n] = raw
            y = raw * inverse_rms(raw) * (gq if c < group else gk)
            turned = y * cosines + pltpu.roll(y, n // 2, 1) * sines
            if c < group:
                to = (h * group + c) * n
                q_ref[:, to:to + n] = turned.astype(BF)
            else:
                keys.append(turned)
        values.append(qkv[:, (h * per + group + 1) * n:(h * per + group + 2) * n])
    for h in range(kv):
        k_ref[:, h * n:(h + 1) * n] = keys[h].astype(BF)
        v_ref[:, h * n:(h + 1) * n] = values[h].astype(BF)
        kt_ref[h * n:(h + 1) * n, :] = keys[h].T.astype(BF)
        vt_ref[h * n:(h + 1) * n, :] = values[h].T.astype(BF)

    @pl.when(i == final)
    def _():
        normed.wait()
        if line:
            merge.finish()
            merge.drain()
            project.drain()
            written.wait()


def front(x, gains, segments, parents, tree, masters, kv, group, line):
    length, d = x.shape
    n = LANES
    rows = lambda w: pl.BlockSpec((ROWS, w), lambda i: (i, 0))
    cols = pl.BlockSpec((kv * n, ROWS), lambda i: (0, i))
    out = lambda w, t: jax.ShapeDtypeStruct((length, w), t)
    raw_w = kv * (group + 1) * n
    freq = np.float32(THETA ** (-(np.arange(n) % (n // 2)) * 2.0 / n))[None]
    more_specs, more_shapes, scratch = [], [], []
    if line:
        shards = 2 * line
        project, merge, expand, shrink = (m.shape for m in masters)
        wp_shape = (project[0] * shards, project[1] * n)
        more_shapes = [jax.ShapeDtypeStruct(wp_shape, BF), jax.ShapeDtypeStruct((merge[0], merge[1] * shards), BF),
                       jax.ShapeDtypeStruct((expand[0], 2 * expand[2]), BF), jax.ShapeDtypeStruct(shrink, BF)]
        more_specs = [ANYWHERE, ANYWHERE, whole(more_shapes[2].shape), whole(more_shapes[3].shape)]
        scratch = [pltpu.VMEM(wp_shape, BF), pltpu.VMEM(merge, BF), *GATHER_SEMS(shards), *GATHER_SEMS(shards),
                   pltpu.SemaphoreType.DMA]
    table = whole((length, n))
    return pl.pallas_call(
        partial(front_kernel, kv, group, line),
        grid=(length // ROWS,),
        in_specs=[whole(x.shape), whole(gains.shape), whole(segments.shape), whole(parents.shape),
                  pl.BlockSpec(memory_space=pltpu.SMEM), whole(freq.shape), *[whole(m.shape) for m in masters]],
        out_specs=[ANYWHERE, rows(kv * group * n), rows(kv * n), rows(kv * n), cols, cols, rows(raw_w),
                   table, table, table, table, *more_specs],
        out_shape=[out(d, BF), out(kv * group * n, BF), out(kv * n, BF), out(kv * n, BF),
                   jax.ShapeDtypeStruct((kv * n, length), BF), jax.ShapeDtypeStruct((kv * n, length), BF),
                   out(raw_w, FP), out(n, BF), out(n, BF), out(n, FP), out(n, FP), *more_shapes],
        scratch_shapes=[*scratch, pltpu.VMEM((length, d), BF), pltpu.SemaphoreType.DMA],
        compiler_params=params(**({"collective_id": 0, "has_side_effects": True} if line else {})),
        name="front",
    )(x, gains, segments, parents, tree, freq, *masters)


def stacked(ref_block, h, group):
    n = LANES
    return jnp.concatenate(
        [ref_block[:, (h * group + g) * n:(h * group + g + 1) * n] for g in range(group)], axis=0)


def causal_tile(group, keys, rows, after):
    key_at = lax.broadcasted_iota(jnp.int32, (keys, rows * group), 0)
    query_at = lax.broadcasted_iota(jnp.int32, (keys, rows * group), 1) % rows
    return key_at <= query_at + after


def key_chunks(blocks, chunk):
    lax.fori_loop(0, blocks // 2, lambda j, c: (chunk(j * 2 * ROWS, 2 * ROWS, False), c)[1], 0)
    pl.when(blocks % 2 == 1)(lambda: chunk((blocks - 1) * ROWS, 2 * ROWS, True))
    pl.when(blocks % 2 == 0)(lambda: chunk(blocks * ROWS, ROWS, True))


def in_turn(i, first, steps, per, acts):
    for behind, act in acts:
        @pl.when(jnp.logical_and(i - first - behind >= 0, i - first - behind < steps))
        def _(behind=behind, act=act):
            for s in pair_of(i - first - behind, per):
                act(s)


def middle_kernel(kv, group, unit, line, per, steps, *refs):
    refs = list(refs)
    take = lambda count: [refs.pop(0) for _ in range(count)]
    q_ref, k_ref, vt_ref, tags_ref, bars_ref, wm_ref, gains_ref, x_all, dy_all = take(9)
    weights = take(2)
    ctx_out, lse_ref, base_ref, other_ref, gate_out, up_out, dh_ref, dhb_ref, dg_ref, gsh_out = take(10)
    acc_ref, sum_ref, x_ref, dy_ref, we_ref, ws_ref, copy_sems = take(7)
    h_ref, xn_ref, a_ref, dgu_ref, ctx_ref, gup_ref = take(6)
    h_held, h_near, h_far, h_sems, xn_sems = take(5)
    d_held, d_near, d_far, d_sems, stage, dh_sems = take(6)
    b_held, b_near, b_sems = take(3)
    place = Place(line)
    i = pl.program_id(0)
    n = LANES
    share, d = x_ref.shape
    units = ws_ref.shape[0]
    attended = Exchange(place, per, h_held, h_near, h_far, h_ref, h_sems)
    norms = Spread(place, per, None, xn_ref, xn_sems)
    pulled_back = Exchange(place, per, d_held, d_near, d_far, dh_ref, d_sems)
    grads = Spread(place, per, stage, dhb_ref, dh_sems)
    branch = Pairs(place, per, b_held, b_near, b_sems, lambda s: s // per)
    own_share = x_all.at[pl.ds(pl.multiple_of(place.t * share, share), share), :]
    copies = [pltpu.make_async_copy(own_share, x_ref, copy_sems.at[0]),
              pltpu.make_async_copy(dy_all, dy_ref, copy_sems.at[1])]
    if line:
        gsh_ref = take(1)[0]
        shrink = Reduce(place, gsh_ref, column_cut(gsh_ref.shape[1] // (2 * line)), None, *take(3))
        gate_ref = take(1)[0]
        expand = Reduce(place, gate_ref, row_cut(gate_ref.shape[0] // (2 * line)), None, *take(3))
        cuts = (row_cut(weights[0].shape[0]), column_cut(weights[1].shape[1]))
        first, second = [Gather(place, weights[w], (we_ref, ws_ref)[w], cuts[w], *take(2)) for w in range(2)]
    else:
        gsh_ref, gate_ref = gsh_out, gate_out
        copies += [pltpu.make_async_copy(weights[0], we_ref, copy_sems.at[2]),
                   pltpu.make_async_copy(weights[1], ws_ref, copy_sems.at[3])]
    written = [pltpu.make_async_copy(ctx_ref, ctx_out, copy_sems.at[4]),
               pltpu.make_async_copy(gup_ref, up_out, copy_sems.at[5])]
    rows_of = lambda s: pl.ds(pl.multiple_of(s * SUB, SUB), SUB)

    def at_step(step, *acts):
        @pl.when(i == step)
        def _():
            for act in acts:
                act()

    @pl.when(i == 0)
    def _():
        place.greet(True, bool(line))
        if line:
            first.start()
        for copy in copies:
            copy.start()
        dg_ref[...] = jnp.zeros_like(dg_ref)


    def block(s):
        here = rows_of(s)
        bars = jnp.concatenate([bars_ref[here, :]] * group, axis=0)
        q = q_ref[here, :]
        wide = [jnp.concatenate([stacked(q, h, group), bars], axis=1) for h in range(kv)]
        acc_ref[...] = jnp.zeros_like(acc_ref)
        sum_ref[...] = jnp.zeros_like(sum_ref)

        def chunk(start, size, diagonal):
            at = pl.ds(pl.multiple_of(start, ROWS), size)
            tags = tags_ref[at, :]
            for h in range(kv):
                keys = jnp.concatenate([k_ref[at, h * n:(h + 1) * n], tags], axis=1)
                scores = dot(keys, wide[h], 1, 1)
                e = jnp.exp2(scores * unit)
                if diagonal:
                    e = jnp.where(causal_tile(group, size, SUB, (s % 2) * SUB + size - ROWS), e, 0.0)
                sum_ref[h] += fold_rows(e)
                acc_ref[h] += dot(vt_ref[h * n:(h + 1) * n, at], e.astype(BF))

        key_chunks(s // 2, chunk)
        parts = []
        for h in range(kv):
            sums = jnp.sum(sum_ref[h], axis=0, keepdims=True)
            lse_ref[s, h:h + 1, :] = jnp.log2(sums)
            ctx = (acc_ref[h] / sums).T
            parts += [ctx[g * SUB:(g + 1) * SUB] for g in range(group)]
        ctx_ref[here, :] = jnp.concatenate(parts, axis=1).astype(BF)

    def put_pair(pairs, blocks, part):
        for u, s in enumerate(blocks):
            pairs.put_next(s, part[u * SUB:(u + 1) * SUB])

    @pl.when(i < steps)
    def _():
        blocks = pair_of(i, per)
        for s in blocks:
            block(s)
        ctx = jnp.concatenate([ctx_ref[rows_of(s), :] for s in blocks], axis=0)
        put_pair(attended, blocks, dot(ctx, wm_ref[...]).astype(BF))

    def hidden_rows(s, at, summed):
        hidden = x_ref[at, :].astype(FP) + summed
        h_ref[at, :] = hidden
        xn_ref[rows_of(s), :] = (hidden * inverse_rms(hidden) * gains_ref[:, d:2 * d]).astype(BF)
        norms.send(s)

    at_step(1, copies[0].wait)
    at_step(steps, written[0].start)
    in_turn(i, 0, steps, per, ((1, attended.add_chip), (3, lambda s: attended.take(s, hidden_rows)), (5, norms.pass_on)))
    swiglu, feed = steps + 3, 2 * steps + 3
    if line:
        at_step(1, lambda: first.hop(1))
        at_step(3, lambda: first.hop(2))
        at_step(5, lambda: first.hop(3), second.start)
        at_step(7, lambda: second.hop(1))
        at_step(8, lambda: second.hop(2))
        at_step(9, lambda: second.hop(3), first.finish)
        at_step(feed, second.finish)
    else:
        at_step(swiglu, copies[2].wait, copies[3].wait)


    def gathered(ref, blocks):
        return jnp.concatenate([ref[rows_of(s), :] for s in blocks], axis=0)

    def keep(ref, blocks, values):
        for u, s in enumerate(blocks):
            ref[rows_of(s), :] = values[u * SUB:(u + 1) * SUB]

    def tiles(grad_ref, left_ref, right_ref, first=0):
        size = grad_ref.shape[0] // 2
        columns = slice(first, first + grad_ref.shape[1])

        def one(t, carry):
            cut = pl.ds(pl.multiple_of(t * size, LANES), size)
            grad_ref[cut, :] = dot(left_ref[:, cut], right_ref[:, columns], 0, 0).astype(grad_ref.dtype)
            return carry

        lax.fori_loop(0, 2, one, 0)

    @pl.when(jnp.logical_and(i >= swiglu, i < feed))
    def _():
        blocks = pair_of(i - swiglu, per)
        for s in blocks:
            norms.ready(s)
        gu = dot(gathered(xn_ref, blocks), we_ref[...])
        gate, up = gu[:, :units], gu[:, units:]
        keep(a_ref, blocks, (gate / (1.0 + jnp.exp(-gate)) * up).astype(BF))
        keep(dgu_ref, blocks, gu.astype(BF))

    at_step(feed - 1, copies[1].wait, lambda: tiles(gsh_ref, a_ref, dy_ref))
    if line:
        at_step(feed, shrink.start)

    @pl.when(jnp.logical_and(i >= feed, i < feed + steps))
    def _():
        blocks = pair_of(i - feed, per)
        gu = gathered(dgu_ref, blocks).astype(FP)
        gate, up = gu[:, :units], gu[:, units:]
        sig = 1.0 / (1.0 + jnp.exp(-gate))
        da = dot(gathered(dy_ref, blocks), ws_ref[...], 1, 1)
        dgu = jnp.concatenate([da * up * (sig * (1.0 + gate * (1.0 - sig))), da * (gate * sig)], axis=1).astype(BF)
        keep(dgu_ref, blocks, dgu)
        put_pair(pulled_back, blocks, dot(dgu, we_ref[...], 1, 1).astype(BF))

    def grad_rows(s, at, summed):
        pulled, gain_grad = rms_pull(h_ref[at, :], gains_ref[:, d:2 * d], summed)
        dh = dy_ref[rows_of(s), :].astype(FP) + pulled
        dh_ref[at, :] = dh
        dg_ref[...] += fold_rows(gain_grad)
        stage[s % per] = dh.astype(BF)
        grads.send(s)

    def chip_rows(mine, k, summed):
        at = rows_of(k)

        @pl.when(mine)
        def _():
            base_ref[at, :] = h_ref[at, :] + summed

        @pl.when(jnp.logical_not(mine))
        def _():
            other_ref[k] = summed.astype(BF)

    in_turn(i, feed, steps, per, ((1, pulled_back.add_chip), (3, lambda s: pulled_back.take(s, grad_rows)),
                                  (5, grads.pass_on)))

    @pl.when(jnp.logical_and(i >= feed + 3, i < feed + 3 + steps))
    def _():
        blocks = pair_of(i - feed - 3, per)
        put_pair(branch, blocks, dot(gathered(a_ref, blocks), ws_ref[...]).astype(BF))

    in_turn(i, feed, steps, per, ((4, lambda s: branch.add(s, chip_rows)),))
    if line:
        for k, step in enumerate((2, 4, 5), 1):
            at_step(feed + step, lambda k=k: shrink.step(k))
    at_step(feed + steps, lambda: tiles(gate_ref, xn_ref, dgu_ref))
    if line:
        at_step(feed + steps, expand.start)
        for k in range(1, line):
            at_step(feed + steps + k, lambda k=k: expand.step(k))
    at_step(feed + steps + 1, lambda: tiles(gup_ref, xn_ref, dgu_ref, units), written[1].start)

    @pl.when(i == feed + steps + 4)
    def _():
        attended.drain()
        pulled_back.drain()
        norms.drain()
        grads.drain()
        for t in range(4):
            branch.sent(t * per + per - 1)
        lax.fori_loop(0, 4 * per, lambda s, c: (grads.ready(s), c)[1], 0)
        for copy in written:
            copy.wait()
        if line:
            shrink.finish(write_to(gsh_out))
            shrink.drain()
            expand.finish(write_to(gate_out))
            expand.drain()
            first.drain()
            second.drain()


def middle(q, k, vt, tags, bars, wm, x, dy, gains, weights, kv, group, unit, line):
    length = q.shape[0]
    n = LANES
    d = wm.shape[1]
    share = (length // 4, d)
    per = share[0] // SUB
    steps = 2 * per
    we, ws = (w.shape for w in weights)
    shards = 2 * line
    shrink = jax.ShapeDtypeStruct(ws, BF)
    gate = jax.ShapeDtypeStruct((we[0], we[1] // 2), BF)
    more = []
    if line:
        shrink = jax.ShapeDtypeStruct(ws, FP)
        gate = jax.ShapeDtypeStruct(gate.shape, FP)
        we, ws = (we[0] * shards, we[1]), (ws[0], ws[1] * shards)
        more = [pltpu.VMEM(ws, BF), *reduce_scratch(line, shrink.shape), pltpu.VMEM((we[0], we[1] // 2), BF),
                *reduce_scratch(line, gate.shape), *GATHER_SEMS(shards), *GATHER_SEMS(shards)]
    units = ws[0]
    results = [jax.ShapeDtypeStruct(q.shape, BF), jax.ShapeDtypeStruct((length // SUB, 8, SUB * group), FP),
               jax.ShapeDtypeStruct(share, FP), jax.ShapeDtypeStruct((per, SUB, d), BF), gate,
               jax.ShapeDtypeStruct((we[0], units), BF), jax.ShapeDtypeStruct(share, FP),
               jax.ShapeDtypeStruct((length, d), BF), jax.ShapeDtypeStruct((8, d), FP),
               shrink]
    out_specs = [whole(r.shape) for r in results]
    for at in (0, 5, 7):
        out_specs[at] = ANYWHERE
    held = [q, k, vt, tags, bars, wm, gains]
    return pl.pallas_call(
        partial(middle_kernel, kv, group, unit, line, per, steps),
        grid=(3 * steps + 8,),
        in_specs=[whole(a.shape) for a in held] + [ANYWHERE] * 4,
        out_specs=out_specs,
        out_shape=results,
        scratch_shapes=[pltpu.VMEM((kv, n, SUB * group), FP), pltpu.VMEM((kv, 8, SUB * group), FP),
                        pltpu.VMEM(share, BF), pltpu.VMEM((length, d), BF), pltpu.VMEM(we, BF), pltpu.VMEM(ws, BF),
                        pltpu.SemaphoreType.DMA((6,)),
                        pltpu.VMEM(share, FP), pltpu.VMEM((length, d), BF), pltpu.VMEM((length, units), BF),
                        pltpu.VMEM((length, 2 * units), BF), pltpu.VMEM(q.shape, BF), pltpu.VMEM((we[0], units), BF),
                        *pairs_scratch(per, d, True), pltpu.SemaphoreType.DMA((4, 4 * per)),
                        *pairs_scratch(per, d, True), pltpu.VMEM((per, SUB, d), BF),
                        pltpu.SemaphoreType.DMA((4, 4 * per)),
                        *pairs_scratch(per, d, False), *more],
        compiler_params=params(collective_id=1, has_side_effects=True),
        name="middle",
    )(*held, x, dy, *weights)


def back_kernel(kv, group, unit, scale, blocks, per, line, *refs):
    refs = list(refs)
    take = lambda count: [refs.pop(0) for _ in range(count)]
    q_ref, k_ref, v_ref, kt_ref, tags_ref, bars_ref, lse_ref, ctx_block, dh_block, wm_ref = take(10)
    raw_ref, cos_ref, sin_ref, all_gains, base_ref, dg2_ref, other_ref = take(7)
    x_all, dh_all = take(2)
    late_from = take(4)
    grads = take(2) if line else []
    in_ref, out_ref, gains_out = take(3)
    sums = take(3) if line else []
    weight_grads = [] if line else take(2)
    late_to = take(4)
    wp_ref, ctx_ref, dh_ref, xn_ref = late_to
    late_sem = take(1)[0]
    late = [pltpu.make_async_copy(a, b, late_sem.at[w]) for w, (a, b) in enumerate(zip(late_from, late_to))]
    dk_ref, dv_ref, dq_ref, dqkv_ref = take(4)
    b_far, b_sems, x_held, x_near, x_sems = take(5)
    mine_ref, far_ref, x_far, f_sems, x_ref, dh_own, own_sems, heads_ref, fold_ref = take(9)
    place = Place(line)
    i = pl.program_id(0)
    b = blocks - 1 - i
    n = LANES
    pairs = Pairs(place, per, x_held, x_near, x_sems, lambda s: s % x_held.shape[0])
    subs = ROWS // SUB
    share, d = x_ref.shape
    gq, gk = all_gains[:, 2 * d:2 * d + n], all_gains[:, 2 * d + n:]
    tile = 256
    tensors = lax.axis_size("tensor")
    mates = [(place.dp, (place.t + step) % tensors) for step in range(1, tensors)]
    peers = []
    own_rows = pl.ds(pl.multiple_of(place.t * share, share), share)
    own_copies = [pltpu.make_async_copy(x_all.at[own_rows, :], x_ref, own_sems.at[0]),
                  pltpu.make_async_copy(dh_all, dh_own, own_sems.at[1])]
    if line:
        shards = 2 * line
        gm_ref, gp_ref = take(2)
        expand = Reduce(place, grads[1], row_cut(grads[1].shape[0] // shards), *take(4))
        merge = Reduce(place, gm_ref, column_cut(gm_ref.shape[1] // shards), None, *take(3))
        project = Reduce(place, gp_ref, row_cut(gp_ref.shape[0] // shards), None, *take(3))
        shown, over, g_sems = take(3)
        peers = [((place.dp + step) % shards, place.t) for step in range(1, shards)]
    else:
        gp_ref, gm_ref = weight_grads

    def tiles(grad_ref, left_ref, right_ref):
        def one(t, carry):
            cut = pl.ds(pl.multiple_of(t * tile, tile), tile)
            grad_ref[cut, :] = dot(left_ref[:, cut], right_ref[...], 0, 0).astype(grad_ref.dtype)
            return carry

        lax.fori_loop(0, grad_ref.shape[0] // tile, one, 0)

    def write_up(values):
        sums[0][:, 0, :] = grads[0][...]
        sums[0][:, 1, :] = values

    def project_rows(t):
        cut = pl.ds(pl.multiple_of(t * tile, tile), tile)
        gp_ref[cut, :] = dot(xn_ref[:, cut], dqkv_ref[...], 0, 0).astype(BF)

    def chip(k):
        return send(far_ref.at[k], x_far.at[k], f_sems.at[0, k], f_sems.at[1, k], place.chip)

    def branch(k):
        return send(other_ref.at[k], b_far.at[k], b_sems.at[0, k], b_sems.at[1, k], place.chip)

    @pl.when(i == 0)
    def _():
        barrier = pltpu.get_barrier_semaphore()
        for device in mates + peers:
            pl.semaphore_signal(barrier, inc=1, device_id=device, device_id_type=MESH)
        for copy in late:
            copy.start()
        pl.semaphore_wait(barrier, len(mates + peers))
        if line:
            expand.start()
        for k in range(per):
            branch(k).start()
        dk_ref[...] = jnp.zeros_like(dk_ref)
        dv_ref[...] = jnp.zeros_like(dv_ref)
        heads_ref[...] = jnp.zeros_like(heads_ref)

    @pl.when(i < blocks)
    def _():
        here = pl.ds(pl.multiple_of(b * ROWS, ROWS), ROWS)
        dctx = dot(dh_block[...], wm_ref[...], 1, 1).astype(BF)
        ctx, q = ctx_block[...], q_ref[...]
        bars = jnp.concatenate([bars_ref[...]] * group, axis=0)
        wide, queries, outward, centres, lses = [], [], [], [], []
        for h in range(kv):
            queries.append(stacked(q, h, group))
            wide.append(jnp.concatenate([queries[h], bars], axis=1))
            outward.append(stacked(dctx, h, group))
            both = outward[h].astype(FP) * stacked(ctx, h, group).astype(FP)
            centres.append(jnp.sum(both.T, axis=0, keepdims=True))
            lses.append(jnp.concatenate([lse_ref[u, h:h + 1, g * SUB:(g + 1) * SUB]
                                         for g in range(group) for u in range(ROWS // SUB)], axis=1))
        dq_ref[...] = jnp.zeros_like(dq_ref)

        def chunk(j, diagonal):
            at = pl.ds(pl.multiple_of(j * ROWS, ROWS), ROWS)
            tags = tags_ref[at, :]
            for h in range(kv):
                cut = slice(h * n, (h + 1) * n)
                keys = jnp.concatenate([k_ref[at, cut], tags], axis=1)
                p = jnp.exp2(dot(keys, wide[h], 1, 1) * unit - lses[h])
                if diagonal:
                    p = jnp.where(causal_tile(group, ROWS, ROWS, 0), p, 0.0)
                dp = dot(v_ref[at, cut], outward[h], 1, 1)
                ds = (p * (dp - centres[h])).astype(BF)
                dv_ref[at, cut] += dot(p.astype(BF), outward[h])
                dk_ref[at, cut] += dot(ds, queries[h])
                dq_ref[h] += dot(kt_ref[cut, at], ds)

        lax.fori_loop(0, b, lambda j, c: (chunk(j, False), c)[1], 0)
        chunk(b, True)

        cosines, sines = cos_ref[...], sin_ref[...]
        pieces = []
        for h in range(kv):
            dq = dq_ref[h].T
            for c in range(group + 1):
                if c < group:
                    grad, gain, row = dq[c * ROWS:(c + 1) * ROWS] * scale, gq, 0
                else:
                    grad, gain, row = dk_ref[here, h * n:(h + 1) * n] * scale, gk, 1
                grad = grad * cosines - pltpu.roll(grad, n // 2, 1) * sines
                at = (h * (group + 1) + c) * n
                piece, gain_grad = rms_pull(raw_ref[:, at:at + n], gain, grad)
                heads_ref[row] += fold_rows(gain_grad)
                pieces.append(piece)
            pieces.append(dv_ref[here, h * n:(h + 1) * n])
        dqkv = jnp.concatenate(pieces, axis=1).astype(BF)
        dqkv_ref[here, :] = dqkv
        pl.when(i == 0)(late[0].wait)
        part = dot(dqkv, wp_ref[...], 1, 1).astype(BF)
        for u in range(subs):
            s = subs * b + u
            pairs.put(s, part[u * SUB:(u + 1) * SUB], (i >= 2, s + 2 * subs))

    def chip_rows(mine, k, summed):
        @pl.when(mine)
        def _():
            mine_ref[pl.ds(pl.multiple_of(k * SUB, SUB), SUB), :] = summed

        @pl.when(jnp.logical_not(mine))
        def _():
            far_ref[k] = summed.astype(BF)
            chip(k).start()

    @pl.when(i >= 1)
    def _():
        for u in range(subs):
            pairs.add(subs * (b + 1) + u, chip_rows)

    @pl.when(i == 3)
    def _():
        for k in range(per):
            branch(k).wait()
            at = slice(k * SUB, (k + 1) * SUB)
            out_ref[at, :] = (base_ref[at, :] + b_far[k].astype(FP)).astype(BF)
        for copy in own_copies:
            copy.start()

    @pl.when(i == 1)
    def _():
        late[1].wait()
        late[2].wait()
        tiles(gm_ref, ctx_ref, dh_ref)

    if line:
        for k in range(1, line):
            pl.when(i == k - 1)(lambda k=k: expand.step(k))
            pl.when(i == k + 2)(lambda k=k: merge.step(k))
        pl.when(i == 2)(merge.start)

    def input_rows(k):
        at = slice(k * SUB, (k + 1) * SUB)
        chip(k).wait()
        summed = mine_ref[at, :] + x_far[k].astype(FP)
        pulled, gain_grad = rms_pull(x_ref[at, :].astype(FP), all_gains[:, :d], summed)
        in_ref[at, :] = (dh_own[at, :] + pulled).astype(BF)
        fold_ref[...] += fold_rows(gain_grad)

    def folded(ref):
        pieces = [fold_ref[...], dg2_ref[...], heads_ref[0], heads_ref[1]]
        row = jnp.sum(jnp.concatenate(pieces, axis=1), axis=0, keepdims=True)
        count = row.shape[1] // n
        for j in range(count):
            ref[j:j + 1, :] = row[:, j * n:(j + 1) * n]
        ref[count:, :] = jnp.zeros((ref.shape[0] - count, n), FP)

    def show(buffer, me, devices, first):
        copies = [send(buffer.at[me], buffer.at[me], g_sems.at[0, first + step], g_sems.at[1, first + step], device)
                  for step, device in enumerate(devices, 1)]
        for copy in copies:
            copy.start()
        return copies

    def added(buffer, me, devices, first):
        count = len(devices) + 1
        for step in range(1, count):
            who = (me - step + count) % count
            send(buffer.at[who], buffer.at[who], g_sems.at[0, first + step], g_sems.at[1, first + step],
                 place.sibling).wait_recv()
        total = buffer[0]
        for who in range(1, count):
            total = total + buffer[who]
        return total

    @pl.when(i == blocks)
    def _():
        fold_ref[...] = jnp.zeros_like(fold_ref)
        late[3].wait()
        for copy in own_copies:
            copy.wait()
        if not line:
            tiles(gp_ref, xn_ref, dqkv_ref)
            for k in range(per):
                input_rows(k)
            folded(gains_out)
        else:
            project_rows(project.turn(0))
            project.start()
            for q in range(1, line):
                project_rows(project.turn(q))
            expand.finish(write_up)
            project.step(1)
            merge.finish(write_to(sums[1]))
            project.step(2)
            for k in range(per):
                input_rows(k)
            folded(shown.at[place.t])
            copies = show(shown, place.t, mates, 0)
            project.step(3)
            over[place.dp] = added(shown, place.t, mates, 0)
            copies += show(over, place.dp, peers, tensors)
            project.finish(write_to(sums[2]))
            gains_out[...] = added(over, place.dp, peers, tensors)
            for copy in copies:
                copy.wait_send()
            for r in (expand, merge, project):
                r.drain()
        for s in range(2 * subs):
            pairs.sent(s)


def back(q, k, v, kt, tags, bars, lse, ctx, dh, wm, wp, raw, cosines, sines, gains, xn, base, dg2, other, x, dh_own,
         grads, kv, group, unit, scale, line):
    length = q.shape[0]
    n = LANES
    d = wm.shape[1]
    blocks = length // ROWS
    per = other.shape[0]
    share = base.shape
    block_of = lambda i: jnp.maximum(blocks - 1 - i, 0)
    rows = lambda w: pl.BlockSpec((ROWS, w), lambda i: (block_of(i), 0))
    late = [wp, ctx, dh, xn]
    gain_rows = (-(-(gains.shape[1] // n) // 8) * 8, n)
    scratch = [*[pltpu.VMEM(a.shape, BF) for a in late], pltpu.SemaphoreType.DMA((4,)),
               pltpu.VMEM((length, kv * n), FP), pltpu.VMEM((length, kv * n), FP),
               pltpu.VMEM((kv, n, ROWS * group), FP), pltpu.VMEM((length, wp.shape[1]), BF),
               pltpu.VMEM((per, SUB, d), BF), pltpu.SemaphoreType.DMA((2, per)),
               pltpu.VMEM((2 * ROWS // SUB, SUB, d), BF), pltpu.VMEM((2 * per, SUB, d), BF),
               pltpu.SemaphoreType.DMA((2, 4 * per)),
               pltpu.VMEM(share, FP), pltpu.VMEM((per, SUB, d), BF), pltpu.VMEM((per, SUB, d), BF),
               pltpu.SemaphoreType.DMA((2, per)), pltpu.VMEM(share, BF), pltpu.VMEM(share, FP),
               pltpu.SemaphoreType.DMA((2,)), pltpu.VMEM((2, 8, n), FP), pltpu.VMEM((8, d), FP)]
    results = [jax.ShapeDtypeStruct(share, BF), jax.ShapeDtypeStruct(share, BF), jax.ShapeDtypeStruct(gain_rows, FP)]
    if line:
        shards = 2 * line
        own = [grads[0].shape, (wm.shape[0], wm.shape[1] // shards),
               (wp.shape[0] // shards, wp.shape[1])]
        views = ((own[0][0], 2, own[0][1]), own[1], (own[2][0], own[2][1] // n, n))
        results += [jax.ShapeDtypeStruct(s, FP) for s in views]
        scratch += [pltpu.VMEM(wm.shape, BF), pltpu.VMEM(wp.shape, BF)]
        for w, s in enumerate(own):
            scratch += reduce_scratch(line, s, w == 0)
        scratch += [pltpu.VMEM((4, *gain_rows), FP), pltpu.VMEM((shards, *gain_rows), FP),
                    pltpu.SemaphoreType.DMA((2, 4 + shards))]
    else:
        results += [jax.ShapeDtypeStruct(wp.shape, BF), jax.ShapeDtypeStruct(wm.shape, BF)]
    args = [q, k, v, kt, tags, bars, lse, ctx, dh, wm, raw, cosines, sines, gains, base, dg2]
    more = [other, x, dh_own, *late, *grads]
    specs = [whole(a.shape) for a in args] + [ANYWHERE] * len(more)
    if line:
        specs[-2] = whole(grads[0].shape)
    for at in (0, 5, 7, 8, 10, 11, 12):
        specs[at] = rows(args[at].shape[1])
    specs[6] = pl.BlockSpec((ROWS // SUB, 8, SUB * group), lambda i: (block_of(i), 0, 0))
    return pl.pallas_call(
        partial(back_kernel, kv, group, unit, scale, blocks, per, line),
        grid=(blocks + 1,),
        in_specs=specs,
        out_specs=[whole(r.shape) for r in results],
        out_shape=results,
        scratch_shapes=scratch,
        compiler_params=params(collective_id=3, has_side_effects=True),
        name="back",
    )(*args, *more)


def adamw_step(weight, moment_one, moment_two, gradient, step_rate, decay):
    mean_next = BETA_ONE * moment_one + (1.0 - BETA_ONE) * gradient
    square_next = BETA_TWO * moment_two + (1.0 - BETA_TWO) * gradient * gradient
    mean_hat = mean_next / (1.0 - BETA_ONE**STEP)
    square_hat = square_next / (1.0 - BETA_TWO**STEP)
    weight_next = weight - step_rate * (mean_hat / (jnp.sqrt(square_hat) + EPS_ADAM) + decay * weight)
    return weight_next, mean_next, square_next


def shards(
    tokens, cotangent, parents, token_segment, tree_id,
    projection_weight, projection_first_moment, projection_second_moment,
    merge_master, merge_mean, merge_square,
    expand_master, expand_mean, expand_square,
    shrink_master, shrink_mean, shrink_square,
    gain_master, gain_mean, gain_square,
):
    x = tokens[0]
    dy = cotangent[0]
    length, d = x.shape
    d_own, kv, per, n = projection_weight.shape
    group = per - 2
    units = expand_master.shape[2]
    scale = n ** (-0.5)
    unit = scale * math.log2(math.e)
    line = 4 if lax.axis_size("dp") == 8 and d_own % LANES == 0 else 0
    if line:
        masters = (projection_weight.reshape(d_own, kv * per, n), merge_master, expand_master, shrink_master)
    else:
        wp, we = (lax.all_gather(w.astype(BF).reshape(d_own, -1), "dp", axis=0, tiled=True)
                  for w in (projection_weight, expand_master))
        wm, ws = (lax.all_gather(w.astype(BF), "dp", axis=1, tiled=True) for w in (merge_master, shrink_master))
        masters = (wp,)

    gains = gain_master[None]
    fronts = front(x, gains, token_segment, parents, tree_id, masters, kv, group, line)
    xn1, q, k, v, kt, vt, raw, tags, bars, cosines, sines = fronts[:11]
    if line:
        wp, wm, *low = fronts[11:]
    else:
        low = (we, ws)
    ctx, lse, base, other, gate_sum, up_grad, dh, dhb, dg2, shrink_sum = middle(
        q, k, vt, tags, bars, wm, x, dy, gains, low, kv, group, unit, line)
    backs = back(q, k, v, kt, tags, bars, lse, ctx, dhb, wm, wp, raw, cosines, sines, gains, xn1,
                 base, dg2, other, x, dh, (gate_sum, up_grad) if line else (), kv, group, unit, scale, line)
    input_grad, output, gain_rows = backs[:3]
    if line:
        expand_sum, merge_sum, project_sum = backs[3:]
    else:
        gain_rows = lax.psum(gain_rows, ("dp", "tensor"))
        project_sum, expand_sum = (
            lax.psum_scatter(g, "dp", scatter_dimension=0, tiled=True) for g in (backs[3], jnp.concatenate([gate_sum, up_grad], axis=1)))
        merge_sum, shrink_sum = (
            lax.psum_scatter(g, "dp", scatter_dimension=1, tiled=True) for g in (backs[4], shrink_sum))
    output, input_grad = output[None], input_grad[None]
    gain_grad = gain_rows.reshape(-1)[:gain_master.shape[0]]

    outs = [output, input_grad]
    for weight, mean, square, grad, rate in (
        (projection_weight, projection_first_moment, projection_second_moment, project_sum, RATE_PROJECT),
        (merge_master, merge_mean, merge_square, merge_sum, RATE_MERGE),
        (expand_master, expand_mean, expand_square, expand_sum, RATE_EXPAND),
        (shrink_master, shrink_mean, shrink_square, shrink_sum, RATE_SHRINK),
    ):
        grad = grad.astype(FP).reshape(weight.shape)
        after, mean_next, square_next = adamw_step(weight, mean, square, grad, rate, DECAY)
        outs += [after, mean_next, square_next, after.astype(BF)]
    gain_next, gain_mean_next, gain_square_next = adamw_step(
        gain_master, gain_mean, gain_square, gain_grad, RATE_GAIN, 0.0)
    return (*outs, gain_mean_next, gain_square_next, gain_next)


def solution(mesh):
    tokens = P("dp", None, None)
    project = P("dp", "tensor", None, None)
    columns = P("tensor", "dp")
    expand = P("dp", None, "tensor")
    shared = P("dp", "tensor", None)
    return jax.shard_map(
        shards,
        mesh=mesh,
        in_specs=(tokens, tokens, P(), P("dp", None), P("dp"), *[project] * 3, *[columns] * 3, *[expand] * 3,
                  *[columns] * 3, P(), P(), P()),
        out_specs=(shared, shared, *[project] * 4, *[columns] * 4, *[expand] * 4, *[columns] * 4, P(), P(), P()),
        check_vma=False,
    )
```

```python
import math
from functools import partial

import jax
import jax.numpy as jnp
import numpy as np
from jax import lax
from jax.experimental import pallas as pl
from jax.experimental.pallas import tpu as pltpu
from jax.sharding import PartitionSpec as P

STEP = 5
EPS_NORM = 1e-06
THETA = 1000000.0
BETA_ONE = 0.5
BETA_TWO = 0.5
EPS_ADAM = 1e-08
DECAY = 0.1
RATE_PROJECT = 0.05
RATE_MERGE = 0.3
RATE_EXPAND = 0.05
RATE_SHRINK = 0.03
RATE_GAIN = 0.3

BF = jnp.bfloat16
FP = jnp.float32
ROWS = 256
LANES = 128
SUB = 128
MESH = pl.DeviceIdType.MESH
BLOCKED = -1e30
VMEM_LIMIT = 56 * 2**20


def params(**more):
    return pltpu.CompilerParams(vmem_limit_bytes=VMEM_LIMIT, **more)


def dot(a, b, ca=1, cb=0):
    return lax.dot_general(a, b, (((ca,), (cb,)), ((), ())), preferred_element_type=FP)


def inverse_rms(values):
    return lax.rsqrt(jnp.mean(values * values, axis=-1, keepdims=True) + EPS_NORM)


def rms_pull(values, scales, grad):
    r = inverse_rms(values)
    scaled = grad * scales
    mean = jnp.mean(values * scaled, axis=-1, keepdims=True)
    return r * scaled - values * (r * r * r * mean), grad * values * r


def fold_rows(values):
    n, w = values.shape
    return jnp.sum(values.reshape(n // 8, 8, w), axis=0)


class Place:
    def __init__(self, line):
        self.line = line
        self.dp, self.t = lax.axis_index("dp"), lax.axis_index("tensor")
        self.z, self.y = self.dp // 2, self.dp % 2
        self.x, self.c = self.t // 2, self.t % 2
        self.has_up, self.has_down = self.z < line - 1, self.z > 0
        self.up, self.down = (self.dp + 2, self.t), (self.dp - 2, self.t)
        self.across = (self.dp + 1 - 2 * self.y, self.t)
        self.sibling = (self.dp, self.t + 1 - 2 * self.c)
        self.chip = (self.dp, (1 - self.x) * 2 + self.c)

    def greet(self, tensor, line, meanwhile=None):
        barrier = pltpu.get_barrier_semaphore()

        def signal(device):
            pl.semaphore_signal(barrier, inc=1, device_id=device, device_id_type=MESH)

        if tensor:
            signal(self.sibling)
            signal(self.chip)
        if line:
            signal(self.across)
            pl.when(self.has_up)(lambda: signal(self.up))
            pl.when(self.has_down)(lambda: signal(self.down))
        peers = (2 if tensor else 0) + (1 if line else 0)
        if line:
            peers = peers + jnp.where(self.has_up, 1, 0) + jnp.where(self.has_down, 1, 0)
        if meanwhile is not None:
            meanwhile()
        pl.semaphore_wait(barrier, peers)


def send(src, dst, sent, arrived, device):
    return pltpu.make_async_remote_copy(
        src_ref=src, dst_ref=dst, send_sem=sent, recv_sem=arrived, device_id=device, device_id_type=MESH)


def row_cut(size):
    return lambda j: (pl.ds(pl.multiple_of(j * size, size), size), slice(None))


def column_cut(size):
    return lambda j: (slice(None), pl.ds(pl.multiple_of(j * size, size), size))


class Gather:
    def __init__(self, place, own, full, cut, sems, local):
        self.place, self.own, self.full, self.cut, self.sems, self.local = place, own, full, cut, sems, local

    def copy(self, kind, src, j):
        p = self.place
        device = (p.up, p.down, p.across)[kind]
        return send(src, self.full.at[self.cut(j)], self.sems.at[kind, j], self.sems.at[3, j], device)

    def kept(self):
        return pltpu.make_async_copy(self.own, self.full.at[self.cut(self.place.dp)], self.local)

    def source(self):
        return self.full.at[self.cut(self.place.dp)] if self.own is None else self.own

    def start(self):
        p = self.place
        self.copy(2, self.source(), p.dp).start()
        pl.when(p.has_up)(lambda: self.copy(0, self.source(), p.dp).start())
        pl.when(p.has_down)(lambda: self.copy(1, self.source(), p.dp).start())
        if self.own is not None:
            self.kept().start()

    def arrivals(self, k):
        p = self.place
        return ((0, p.z >= k, (p.z - k) * 2 + p.y, p.has_up), (1, p.z + k < p.line, (p.z + k) * 2 + p.y, p.has_down))

    def hop(self, k):
        for kind, here, j, further in self.arrivals(k):
            @pl.when(here)
            def _(kind=kind, j=j, further=further):
                piece = self.full.at[self.cut(j)]
                self.copy(kind, piece, j).wait_recv()
                pl.when(further)(lambda: self.copy(kind, piece, j).start())
                self.copy(2, piece, j).start()

    def finish(self):
        p = self.place
        if self.own is not None:
            self.kept().wait()
        for zz in range(p.line):
            j = zz * 2 + 1 - p.y
            self.copy(2, self.full.at[self.cut(j)], j).wait_recv()

    def drain(self):
        p = self.place
        self.copy(2, self.source(), p.dp).wait_send()
        pl.when(p.has_up)(lambda: self.copy(0, self.source(), p.dp).wait_send())
        pl.when(p.has_down)(lambda: self.copy(1, self.source(), p.dp).wait_send())
        for k in range(1, p.line):
            for kind, here, j, further in self.arrivals(k):
                @pl.when(here)
                def _(kind=kind, j=j, further=further):
                    piece = self.full.at[self.cut(j)]
                    pl.when(further)(lambda: self.copy(kind, piece, j).wait_send())
                    self.copy(2, piece, j).wait_send()


class Reduce:
    def __init__(self, place, grad, cut, kept, across, lined, sems):
        self.place, self.grad, self.cut, self.kept, self.sems = place, grad, cut, kept, sems
        self.across, self.lined = across, lined

    def cross(self, zz):
        p = self.place
        return send(self.grad.at[self.cut(zz * 2 + 1 - p.y)], self.across.at[zz],
                    self.sems.at[0, zz], self.sems.at[1, zz], p.across)

    def climb(self, t):
        return send(self.across.at[t], self.lined.at[t + 1], self.sems.at[2, t], self.sems.at[3, t], self.place.up)

    def sink(self, t):
        return send(self.across.at[t], self.lined.at[t], self.sems.at[4, t], self.sems.at[5, t], self.place.down)

    def load(self, zz):
        return pltpu.make_async_copy(self.grad.at[self.cut(zz * 2 + self.place.y)], self.kept.at[zz], self.sems.at[6, zz])

    def mine(self, zz):
        if self.kept is None:
            return self.grad[self.cut(zz * 2 + self.place.y)].astype(FP)
        return self.kept[zz].astype(FP)

    def loaded(self, zz):
        if self.kept is not None:
            self.load(zz).wait()

    def turn(self, q):
        z = self.place.z
        low = z < 2
        if q == 0:
            return jnp.where(low, 3, 0)
        if q == 1:
            return jnp.where(low, 2, 1)
        if q == 2:
            return jnp.where(low, 1 - z, 5 - z)
        return z

    def start(self):
        self.cross(self.turn(0)).start()
        if self.kept is not None:
            for zz in range(self.place.line):
                self.load(zz).start()

    def advance(self, q):
        self.cross(self.turn(q - 1)).wait_send()
        self.cross(self.turn(q)).start()

    def hop(self, h):
        p = self.place

        def pass_on(t, coming, more, slot):
            self.loaded(t)
            self.cross(t).wait_recv()

            @pl.when(jnp.logical_not(more))
            def _():
                self.across[t] = (self.mine(t) + self.across[t].astype(FP)).astype(BF)

            @pl.when(more)
            def _():
                coming(t).wait_recv()
                self.across[t] = (self.mine(t) + self.across[t].astype(FP) + self.lined[slot].astype(FP)).astype(BF)

            coming(t).start()

        pl.when(p.z < h)(lambda: pass_on(p.z + p.line - h, self.climb, p.has_down, p.z + p.line - h + 1))
        pl.when(p.z >= p.line - h)(lambda: pass_on(p.z - p.line + h, self.sink, p.has_up, p.z - p.line + h))

    def finish(self, write):
        p = self.place
        self.loaded(p.z)
        self.cross(p.z).wait_recv()
        pl.when(p.has_down)(lambda: self.climb(p.z).wait_recv())
        pl.when(p.has_up)(lambda: self.sink(p.z).wait_recv())
        from_below = jnp.where(p.has_down, self.lined[p.z + 1].astype(FP), 0.0)
        from_above = jnp.where(p.has_up, self.lined[p.z].astype(FP), 0.0)
        write(self.mine(p.z) + self.across[p.z].astype(FP) + from_below + from_above)

    def step(self, k):
        self.advance(k)
        self.hop(k)

    def drain(self):
        p = self.place
        self.cross(p.z).wait_send()
        for zz in range(p.line):
            pl.when(zz > p.z)(lambda zz=zz: self.climb(zz).wait_send())
            pl.when(zz < p.z)(lambda zz=zz: self.sink(zz).wait_send())


def write_to(ref):
    def write(values):
        if len(ref.shape) == 2:
            ref[...] = values
            return
        width = ref.shape[2]
        for j in range(ref.shape[1]):
            ref[:, j, :] = values[:, j * width:(j + 1) * width]

    return write


def reduce_scratch(line, shape, kept=False):
    return [pltpu.VMEM((line, *shape), BF)] * kept + [pltpu.VMEM((line, *shape), BF), pltpu.VMEM((line + 1, *shape), BF),
                                                      pltpu.SemaphoreType.DMA((7, line))]


class Pairs:
    def __init__(self, place, per, held, near, sems, slot_of):
        self.place, self.per, self.held, self.near, self.sems, self.slot_of = place, per, held, near, sems, slot_of

    def near_slot(self, s):
        return (s // (2 * self.per)) * self.per + s % self.per

    def to_sibling(self, s):
        return send(self.held.at[self.slot_of(s)], self.near.at[self.near_slot(s)], self.sems.at[0, s],
                    self.sems.at[1, s], self.place.sibling)

    def sends(self, s):
        return self.place.c != (s // self.per) % 2

    def sent(self, s):
        pl.when(self.sends(s))(lambda: self.to_sibling(s).wait_send())

    def put(self, s, rows, before=None):
        if before is not None:
            pl.when(before[0])(lambda: self.sent(before[1]))
        self.held[self.slot_of(s)] = rows
        pl.when(self.sends(s))(lambda: self.to_sibling(s).start())

    def put_next(self, s, rows):
        self.put(s, rows, (s % self.per >= 1, s - 1))

    def add(self, s, use):
        t = s // self.per

        @pl.when(self.place.c == t % 2)
        def _():
            self.to_sibling(s).wait_recv()
            use(self.place.x == t // 2, s % self.per,
                self.held[self.slot_of(s)].astype(FP) + self.near[self.near_slot(s)].astype(FP))


class Exchange(Pairs):
    def __init__(self, place, per, held, near, far, total, sems):
        super().__init__(place, per, held, near, sems, lambda s: s // per)
        self.far, self.total = far, total

    def rows(self, k):
        return pl.ds(pl.multiple_of(k * SUB, SUB), SUB)

    def to_chip(self, s):
        return send(self.near.at[self.near_slot(s)], self.far.at[s % self.per], self.sems.at[2, s], self.sems.at[3, s],
                    self.place.chip)

    def add_chip(self, s):
        def use(mine, k, summed):
            @pl.when(jnp.logical_not(mine))
            def _():
                self.near[self.near_slot(s)] = summed.astype(BF)
                self.to_chip(s).start()

            @pl.when(mine)
            def _():
                self.total[self.rows(k), :] = summed

        self.add(s, use)

    def take(self, s, use):
        @pl.when(s // self.per == self.place.t)
        def _():
            k = s % self.per
            self.to_chip(s).wait_recv()
            use(s, self.rows(k), self.total[self.rows(k), :] + self.far[k].astype(FP))

    def drain(self):
        p = self.place

        def one(s, carry):
            t = s // self.per
            pl.when(s % self.per == self.per - 1)(lambda: self.sent(s))
            pl.when(jnp.logical_and(p.c == t % 2, p.x != t // 2))(lambda: self.to_chip(s).wait_send())
            return carry

        lax.fori_loop(0, 4 * self.per, one, 0)


def pair_of(step, per):
    t = step % 2
    return t * per + step // 2, (3 - t) * per + step // 2


def pairs_scratch(per, d, exchange):
    rows = [pltpu.VMEM((4, SUB, d), BF), pltpu.VMEM((2 * per, SUB, d), BF)]
    return rows + [pltpu.VMEM((per, SUB, d), BF)] * exchange + [pltpu.SemaphoreType.DMA((4 if exchange else 2, 4 * per))]


class Spread:
    def __init__(self, place, per, stage, full, sems):
        self.place, self.per, self.stage, self.full, self.sems = place, per, stage, full, sems

    def rows(self, s):
        return self.full.at[pl.ds(pl.multiple_of(s * SUB, SUB), SUB), :]

    def source(self, s):
        return self.rows(s) if self.stage is None else self.stage.at[s % self.per]

    def copy(self, kind, src, s):
        device = (self.place.chip, self.place.sibling)[kind]
        return send(src, self.rows(s), self.sems.at[kind, s], self.sems.at[2, s], device)

    def kept(self, s):
        return pltpu.make_async_copy(self.source(s), self.rows(s), self.sems.at[3, s])

    def send(self, s):
        for kind in (0, 1):
            self.copy(kind, self.source(s), s).start()
        if self.stage is not None:
            self.kept(s).start()

    def owns(self, s):
        return s // self.per == self.place.t

    def passes(self, s):
        t = s // self.per
        return jnp.logical_and(self.place.c == t % 2, self.place.x != t // 2)

    def pass_on(self, s):
        @pl.when(self.passes(s))
        def _():
            self.copy(1, self.rows(s), s).wait_recv()
            self.copy(1, self.rows(s), s).start()

    def ready(self, s):
        if self.stage is not None:
            pl.when(self.owns(s))(lambda: self.kept(s).wait())
        pl.when((s // self.per) % 2 != self.place.c)(lambda: self.copy(1, self.rows(s), s).wait_recv())

    def drain(self):
        def one(s, carry):
            @pl.when(self.owns(s))
            def _():
                self.copy(0, self.source(s), s).wait_send()
                self.copy(1, self.source(s), s).wait_send()

            pl.when(self.passes(s))(lambda: self.copy(1, self.rows(s), s).wait_send())
            return carry

        lax.fori_loop(0, 4 * self.per, one, 0)


def whole(shape):
    return pl.BlockSpec(tuple(shape), lambda i: (0,) * len(shape), pipeline_mode=pl.Buffered(1))


ANYWHERE = pl.BlockSpec(memory_space=pl.ANY)
GATHER_SEMS = lambda shards: [pltpu.SemaphoreType.DMA((4, shards)), pltpu.SemaphoreType.DMA]


def make_tables(seg_ref, parents_ref, tree_ref, freq_ref, tags_ref, bars_ref, cos_ref, sin_ref):
    count = parents_ref.shape[1]
    n = LANES
    blocks = sin_ref.shape[0] // ROWS
    lane = lax.broadcasted_iota(jnp.int32, (1, n), 1).astype(FP)
    place_of = lambda b: pl.ds(pl.multiple_of(b * ROWS, ROWS), ROWS)

    def columns(b, carry):
        sin_ref[place_of(b), :] = jnp.broadcast_to(seg_ref[:, place_of(b)].astype(FP), (n, ROWS)).T
        return carry

    def tally(b, carry):
        column = sin_ref[place_of(b), :]
        return (carry[0] + fold_rows(jnp.where(column == lane, 1.0, 0.0)),
                carry[1] + fold_rows(jnp.where(column < lane, 1.0, 0.0)))

    lax.fori_loop(0, blocks, columns, 0)
    sizes, starts = lax.fori_loop(0, blocks, tally, (jnp.zeros((8, n), FP), jnp.zeros((8, n), FP)))
    sizes, starts = (jnp.sum(a, axis=0, keepdims=True) for a in (sizes, starts))
    table = parents_ref[...]
    chosen = jnp.where(lax.broadcasted_iota(jnp.int32, table.shape, 0) == tree_ref[0], table, 0)
    chosen = jnp.sum(chosen.astype(FP), axis=0, keepdims=True)
    parents = jnp.zeros((1, n), FP)
    for b in range(count):
        parents = jnp.where(lane == b, chosen[:, b:b + 1], parents)
    shifts = jnp.where(lane != 0, sizes[:, :1], 0.0) - starts

    def rows(b, carry):
        at = place_of(b)
        column = sin_ref[at, :]
        hot = column == lane
        parent = jnp.sum(jnp.where(hot, parents, 0.0), axis=1, keepdims=True)
        above = jnp.where(jnp.logical_and(lane == parent, lane != 0), sizes, 0.0)
        first = (b * ROWS).astype(FP)
        position = (lax.broadcasted_iota(jnp.int32, (ROWS, 1), 0).astype(FP) + first
                    + jnp.sum(jnp.where(hot, shifts, 0.0) + above, axis=1, keepdims=True))
        tags_ref[at, :] = jnp.where(hot, 1.0, 0.0).astype(BF)
        open_to = jnp.logical_or(jnp.logical_or(hot, lane == parent), jnp.logical_or(lane == 0, lane >= count))
        bars_ref[at, :] = jnp.where(open_to, 0.0, BLOCKED).astype(BF)
        angles = position * freq_ref[...]
        cos_ref[at, :] = jnp.cos(angles)
        turned = jnp.sin(angles)
        sin_ref[at, :] = jnp.where(lane < n // 2, -turned, turned)
        return carry

    lax.fori_loop(0, blocks, rows, 0)


def front_kernel(kv, group, line, *refs):
    refs = list(refs)
    take = lambda count: [refs.pop(0) for _ in range(count)]
    x_ref, gains_ref, seg_ref, parents_ref, tree_ref, freq_ref = take(6)
    masters = take(4) if line else take(1)
    xn_ref, q_ref, k_ref, v_ref, kt_ref, vt_ref, raw_ref, tags_ref, bars_ref, cos_ref, sin_ref = take(11)
    if line:
        wp_out, wm_out, we_low, ws_low = take(4)
        wp_ref, wm_low, p_sems, p_local, m_sems, m_local, out_sem = take(7)
    else:
        wp_ref = masters[0]
    xn_full, xn_sem = take(2)
    i = pl.program_id(0)
    final = pl.num_programs(0) - 1
    d = x_ref.shape[1]
    n = LANES
    per = group + 2
    if line:
        place = Place(line)
        size = masters[0].shape[0]
        project = Gather(place, None, wp_ref, row_cut(size), p_sems, p_local)
        merge = Gather(place, wm_low, wm_out, column_cut(wm_low.shape[1]), m_sems, m_local)
        written = pltpu.make_async_copy(wp_ref, wp_out, out_sem)
    normed = pltpu.make_async_copy(xn_full, xn_ref, xn_sem)

    def round_projection():
        at = pl.ds(pl.multiple_of(place.dp * size, size), size)
        for j in range(kv * per):
            wp_ref[at, j * n:(j + 1) * n] = masters[0][:, j, :].astype(BF)

    def norm(b, carry):
        at = pl.ds(pl.multiple_of(b * ROWS, ROWS), ROWS)
        x = x_ref[at, :].astype(FP)
        xn_full[at, :] = (x * inverse_rms(x) * gains_ref[:, :d]).astype(BF)
        return carry

    @pl.when(i == 0)
    def _():
        if line:
            place.greet(False, True, round_projection)
            project.start()
        lax.fori_loop(0, x_ref.shape[0] // ROWS, norm, 0)
        normed.start()
        if line:
            project.hop(1)
        make_tables(seg_ref, parents_ref, tree_ref, freq_ref, tags_ref, bars_ref, cos_ref, sin_ref)
        if line:
            project.hop(2)
            wm_low[...] = masters[1][...].astype(BF)
            units = masters[2].shape[2]
            for half in range(2):
                we_low[:, half * units:(half + 1) * units] = masters[2][:, half, :].astype(BF)
            ws_low[...] = masters[3][...].astype(BF)
            project.hop(3)
            merge.start()
            project.finish()
            written.start()

    if line:
        for k in range(1, line):
            pl.when(i == k + 1)(lambda k=k: merge.hop(k))
    at = pl.ds(pl.multiple_of(i * ROWS, ROWS), ROWS)
    qkv = dot(xn_full[at, :], wp_ref[...])
    cosines, sines = cos_ref[at, :], sin_ref[at, :]
    gq, gk = gains_ref[:, 2 * d:2 * d + n], gains_ref[:, 2 * d + n:]
    keys, values = [], []
    for h in range(kv):
        for c in range(group + 1):
            raw = qkv[:, (h * per + c) * n:(h * per + c + 1) * n]
            to = (h * (group + 1) + c) * n
            raw_ref[:, to:to + n] = raw
            y = raw * inverse_rms(raw) * (gq if c < group else gk)
            turned = y * cosines + pltpu.roll(y, n // 2, 1) * sines
            if c < group:
                to = (h * group + c) * n
                q_ref[:, to:to + n] = turned.astype(BF)
            else:
                keys.append(turned)
        values.append(qkv[:, (h * per + group + 1) * n:(h * per + group + 2) * n])
    for h in range(kv):
        k_ref[:, h * n:(h + 1) * n] = keys[h].astype(BF)
        v_ref[:, h * n:(h + 1) * n] = values[h].astype(BF)
        kt_ref[h * n:(h + 1) * n, :] = keys[h].T.astype(BF)
        vt_ref[h * n:(h + 1) * n, :] = values[h].T.astype(BF)

    @pl.when(i == final)
    def _():
        normed.wait()
        if line:
            merge.finish()
            merge.drain()
            project.drain()
            written.wait()


def front(x, gains, segments, parents, tree, masters, kv, group, line):
    length, d = x.shape
    n = LANES
    rows = lambda w: pl.BlockSpec((ROWS, w), lambda i: (i, 0))
    cols = pl.BlockSpec((kv * n, ROWS), lambda i: (0, i))
    out = lambda w, t: jax.ShapeDtypeStruct((length, w), t)
    raw_w = kv * (group + 1) * n
    freq = np.float32(THETA ** (-(np.arange(n) % (n // 2)) * 2.0 / n))[None]
    more_specs, more_shapes, scratch = [], [], []
    if line:
        shards = 2 * line
        project, merge, expand, shrink = (m.shape for m in masters)
        wp_shape = (project[0] * shards, project[1] * n)
        more_shapes = [jax.ShapeDtypeStruct(wp_shape, BF), jax.ShapeDtypeStruct((merge[0], merge[1] * shards), BF),
                       jax.ShapeDtypeStruct((expand[0], 2 * expand[2]), BF), jax.ShapeDtypeStruct(shrink, BF)]
        more_specs = [ANYWHERE, ANYWHERE, whole(more_shapes[2].shape), whole(more_shapes[3].shape)]
        scratch = [pltpu.VMEM(wp_shape, BF), pltpu.VMEM(merge, BF), *GATHER_SEMS(shards), *GATHER_SEMS(shards),
                   pltpu.SemaphoreType.DMA]
    table = whole((length, n))
    return pl.pallas_call(
        partial(front_kernel, kv, group, line),
        grid=(length // ROWS,),
        in_specs=[whole(x.shape), whole(gains.shape), whole(segments.shape), whole(parents.shape),
                  pl.BlockSpec(memory_space=pltpu.SMEM), whole(freq.shape), *[whole(m.shape) for m in masters]],
        out_specs=[ANYWHERE, rows(kv * group * n), rows(kv * n), rows(kv * n), cols, cols, rows(raw_w),
                   table, table, table, table, *more_specs],
        out_shape=[out(d, BF), out(kv * group * n, BF), out(kv * n, BF), out(kv * n, BF),
                   jax.ShapeDtypeStruct((kv * n, length), BF), jax.ShapeDtypeStruct((kv * n, length), BF),
                   out(raw_w, FP), out(n, BF), out(n, BF), out(n, FP), out(n, FP), *more_shapes],
        scratch_shapes=[*scratch, pltpu.VMEM((length, d), BF), pltpu.SemaphoreType.DMA],
        compiler_params=params(**({"collective_id": 0, "has_side_effects": True} if line else {})),
        name="front",
    )(x, gains, segments, parents, tree, freq, *masters)


def stacked(ref_block, h, group):
    n = LANES
    return jnp.concatenate(
        [ref_block[:, (h * group + g) * n:(h * group + g + 1) * n] for g in range(group)], axis=0)


def causal_tile(group, keys, rows, after):
    key_at = lax.broadcasted_iota(jnp.int32, (keys, rows * group), 0)
    query_at = lax.broadcasted_iota(jnp.int32, (keys, rows * group), 1) % rows
    return key_at <= query_at + after


def key_chunks(blocks, chunk):
    lax.fori_loop(0, blocks // 2, lambda j, c: (chunk(j * 2 * ROWS, 2 * ROWS, False), c)[1], 0)
    pl.when(blocks % 2 == 1)(lambda: chunk((blocks - 1) * ROWS, 2 * ROWS, True))
    pl.when(blocks % 2 == 0)(lambda: chunk(blocks * ROWS, ROWS, True))


def in_turn(i, first, steps, per, acts):
    for behind, act in acts:
        @pl.when(jnp.logical_and(i - first - behind >= 0, i - first - behind < steps))
        def _(behind=behind, act=act):
            for s in pair_of(i - first - behind, per):
                act(s)


def middle_kernel(kv, group, unit, line, per, steps, *refs):
    refs = list(refs)
    take = lambda count: [refs.pop(0) for _ in range(count)]
    q_ref, k_ref, vt_ref, tags_ref, bars_ref, wm_ref, gains_ref, x_all, dy_all = take(9)
    weights = take(2)
    ctx_out, lse_ref, base_ref, other_ref, gate_out, up_out, dh_ref, dhb_ref, dg_ref, gsh_out = take(10)
    acc_ref, sum_ref, x_ref, dy_ref, we_ref, ws_ref, copy_sems = take(7)
    h_ref, xn_ref, a_ref, dgu_ref, ctx_ref, gup_ref = take(6)
    h_held, h_near, h_far, h_sems, xn_sems = take(5)
    d_held, d_near, d_far, d_sems, stage, dh_sems = take(6)
    b_held, b_near, b_sems = take(3)
    place = Place(line)
    i = pl.program_id(0)
    n = LANES
    share, d = x_ref.shape
    units = ws_ref.shape[0]
    attended = Exchange(place, per, h_held, h_near, h_far, h_ref, h_sems)
    norms = Spread(place, per, None, xn_ref, xn_sems)
    pulled_back = Exchange(place, per, d_held, d_near, d_far, dh_ref, d_sems)
    grads = Spread(place, per, stage, dhb_ref, dh_sems)
    branch = Pairs(place, per, b_held, b_near, b_sems, lambda s: s // per)
    own_share = x_all.at[pl.ds(pl.multiple_of(place.t * share, share), share), :]
    copies = [pltpu.make_async_copy(own_share, x_ref, copy_sems.at[0]),
              pltpu.make_async_copy(dy_all, dy_ref, copy_sems.at[1])]
    if line:
        gsh_ref = take(1)[0]
        shrink = Reduce(place, gsh_ref, column_cut(gsh_ref.shape[1] // (2 * line)), None, *take(3))
        gate_ref = take(1)[0]
        expand = Reduce(place, gate_ref, row_cut(gate_ref.shape[0] // (2 * line)), None, *take(3))
        cuts = (row_cut(weights[0].shape[0]), column_cut(weights[1].shape[1]))
        first, second = [Gather(place, weights[w], (we_ref, ws_ref)[w], cuts[w], *take(2)) for w in range(2)]
    else:
        gsh_ref, gate_ref = gsh_out, gate_out
        copies += [pltpu.make_async_copy(weights[0], we_ref, copy_sems.at[2]),
                   pltpu.make_async_copy(weights[1], ws_ref, copy_sems.at[3])]
    written = [pltpu.make_async_copy(ctx_ref, ctx_out, copy_sems.at[4]),
               pltpu.make_async_copy(gup_ref, up_out, copy_sems.at[5])]
    rows_of = lambda s: pl.ds(pl.multiple_of(s * SUB, SUB), SUB)

    def at_step(step, *acts):
        @pl.when(i == step)
        def _():
            for act in acts:
                act()

    @pl.when(i == 0)
    def _():
        place.greet(True, bool(line))
        if line:
            first.start()
        for copy in copies:
            copy.start()
        dg_ref[...] = jnp.zeros_like(dg_ref)


    def block(s):
        here = rows_of(s)
        bars = jnp.concatenate([bars_ref[here, :]] * group, axis=0)
        q = q_ref[here, :]
        wide = [jnp.concatenate([stacked(q, h, group), bars], axis=1) for h in range(kv)]
        acc_ref[...] = jnp.zeros_like(acc_ref)
        sum_ref[...] = jnp.zeros_like(sum_ref)

        def chunk(start, size, diagonal):
            at = pl.ds(pl.multiple_of(start, ROWS), size)
            tags = tags_ref[at, :]
            for h in range(kv):
                keys = jnp.concatenate([k_ref[at, h * n:(h + 1) * n], tags], axis=1)
                scores = dot(keys, wide[h], 1, 1)
                e = jnp.exp2(scores * unit)
                if diagonal:
                    e = jnp.where(causal_tile(group, size, SUB, (s % 2) * SUB + size - ROWS), e, 0.0)
                sum_ref[h] += fold_rows(e)
                acc_ref[h] += dot(vt_ref[h * n:(h + 1) * n, at], e.astype(BF))

        key_chunks(s // 2, chunk)
        parts = []
        for h in range(kv):
            sums = jnp.sum(sum_ref[h], axis=0, keepdims=True)
            lse_ref[s, h:h + 1, :] = jnp.log2(sums)
            ctx = (acc_ref[h] / sums).T
            parts += [ctx[g * SUB:(g + 1) * SUB] for g in range(group)]
        ctx_ref[here, :] = jnp.concatenate(parts, axis=1).astype(BF)

    def put_pair(pairs, blocks, part):
        for u, s in enumerate(blocks):
            pairs.put_next(s, part[u * SUB:(u + 1) * SUB])

    @pl.when(i < steps)
    def _():
        blocks = pair_of(i, per)
        for s in blocks:
            block(s)
        ctx = jnp.concatenate([ctx_ref[rows_of(s), :] for s in blocks], axis=0)
        put_pair(attended, blocks, dot(ctx, wm_ref[...]).astype(BF))

    def hidden_rows(s, at, summed):
        hidden = x_ref[at, :].astype(FP) + summed
        h_ref[at, :] = hidden
        xn_ref[rows_of(s), :] = (hidden * inverse_rms(hidden) * gains_ref[:, d:2 * d]).astype(BF)
        norms.send(s)

    at_step(1, copies[0].wait)
    at_step(steps, written[0].start)
    in_turn(i, 0, steps, per, ((1, attended.add_chip), (3, lambda s: attended.take(s, hidden_rows)), (5, norms.pass_on)))
    swiglu, feed = steps + 3, 2 * steps + 3
    if line:
        at_step(1, lambda: first.hop(1))
        at_step(3, lambda: first.hop(2))
        at_step(5, lambda: first.hop(3), second.start)
        at_step(7, lambda: second.hop(1))
        at_step(8, lambda: second.hop(2))
        at_step(9, lambda: second.hop(3), first.finish)
        at_step(feed, second.finish)
    else:
        at_step(swiglu, copies[2].wait, copies[3].wait)


    def gathered(ref, blocks):
        return jnp.concatenate([ref[rows_of(s), :] for s in blocks], axis=0)

    def keep(ref, blocks, values):
        for u, s in enumerate(blocks):
            ref[rows_of(s), :] = values[u * SUB:(u + 1) * SUB]

    def tiles(grad_ref, left_ref, right_ref, first=0):
        size = grad_ref.shape[0] // 2
        columns = slice(first, first + grad_ref.shape[1])

        def one(t, carry):
            cut = pl.ds(pl.multiple_of(t * size, LANES), size)
            grad_ref[cut, :] = dot(left_ref[:, cut], right_ref[:, columns], 0, 0).astype(grad_ref.dtype)
            return carry

        lax.fori_loop(0, 2, one, 0)

    @pl.when(jnp.logical_and(i >= swiglu, i < feed))
    def _():
        blocks = pair_of(i - swiglu, per)
        for s in blocks:
            norms.ready(s)
        gu = dot(gathered(xn_ref, blocks), we_ref[...])
        gate, up = gu[:, :units], gu[:, units:]
        keep(a_ref, blocks, (gate / (1.0 + jnp.exp(-gate)) * up).astype(BF))
        keep(dgu_ref, blocks, gu.astype(BF))

    at_step(feed - 1, copies[1].wait, lambda: tiles(gsh_ref, a_ref, dy_ref))
    if line:
        at_step(feed, shrink.start)

    @pl.when(jnp.logical_and(i >= feed, i < feed + steps))
    def _():
        blocks = pair_of(i - feed, per)
        gu = gathered(dgu_ref, blocks).astype(FP)
        gate, up = gu[:, :units], gu[:, units:]
        sig = 1.0 / (1.0 + jnp.exp(-gate))
        da = dot(gathered(dy_ref, blocks), ws_ref[...], 1, 1)
        dgu = jnp.concatenate([da * up * (sig * (1.0 + gate * (1.0 - sig))), da * (gate * sig)], axis=1).astype(BF)
        keep(dgu_ref, blocks, dgu)
        put_pair(pulled_back, blocks, dot(dgu, we_ref[...], 1, 1).astype(BF))

    def grad_rows(s, at, summed):
        pulled, gain_grad = rms_pull(h_ref[at, :], gains_ref[:, d:2 * d], summed)
        dh = dy_ref[rows_of(s), :].astype(FP) + pulled
        dh_ref[at, :] = dh
        dg_ref[...] += fold_rows(gain_grad)
        stage[s % per] = dh.astype(BF)
        grads.send(s)

    def chip_rows(mine, k, summed):
        at = rows_of(k)

        @pl.when(mine)
        def _():
            base_ref[at, :] = h_ref[at, :] + summed

        @pl.when(jnp.logical_not(mine))
        def _():
            other_ref[k] = summed.astype(BF)

    in_turn(i, feed, steps, per, ((1, pulled_back.add_chip), (3, lambda s: pulled_back.take(s, grad_rows)),
                                  (5, grads.pass_on)))

    @pl.when(jnp.logical_and(i >= feed + 3, i < feed + 3 + steps))
    def _():
        blocks = pair_of(i - feed - 3, per)
        put_pair(branch, blocks, dot(gathered(a_ref, blocks), ws_ref[...]).astype(BF))

    in_turn(i, feed, steps, per, ((4, lambda s: branch.add(s, chip_rows)),))
    if line:
        for k, step in enumerate((2, 4, 5), 1):
            at_step(feed + step, lambda k=k: shrink.step(k))
    at_step(feed + steps, lambda: tiles(gate_ref, xn_ref, dgu_ref))
    if line:
        at_step(feed + steps, expand.start)
        for k in range(1, line):
            at_step(feed + steps + k, lambda k=k: expand.step(k))
    at_step(feed + steps + 1, lambda: tiles(gup_ref, xn_ref, dgu_ref, units), written[1].start)

    @pl.when(i == feed + steps + 4)
    def _():
        attended.drain()
        pulled_back.drain()
        norms.drain()
        grads.drain()
        for t in range(4):
            branch.sent(t * per + per - 1)
        lax.fori_loop(0, 4 * per, lambda s, c: (grads.ready(s), c)[1], 0)
        for copy in written:
            copy.wait()
        if line:
            shrink.finish(write_to(gsh_out))
            shrink.drain()
            expand.finish(write_to(gate_out))
            expand.drain()
            first.drain()
            second.drain()


def middle(q, k, vt, tags, bars, wm, x, dy, gains, weights, kv, group, unit, line):
    length = q.shape[0]
    n = LANES
    d = wm.shape[1]
    share = (length // 4, d)
    per = share[0] // SUB
    steps = 2 * per
    we, ws = (w.shape for w in weights)
    shards = 2 * line
    shrink = jax.ShapeDtypeStruct(ws, BF)
    gate = jax.ShapeDtypeStruct((we[0], we[1] // 2), BF)
    more = []
    if line:
        shrink = jax.ShapeDtypeStruct(ws, FP)
        gate = jax.ShapeDtypeStruct(gate.shape, FP)
        we, ws = (we[0] * shards, we[1]), (ws[0], ws[1] * shards)
        more = [pltpu.VMEM(ws, BF), *reduce_scratch(line, shrink.shape), pltpu.VMEM((we[0], we[1] // 2), BF),
                *reduce_scratch(line, gate.shape), *GATHER_SEMS(shards), *GATHER_SEMS(shards)]
    units = ws[0]
    results = [jax.ShapeDtypeStruct(q.shape, BF), jax.ShapeDtypeStruct((length // SUB, 8, SUB * group), FP),
               jax.ShapeDtypeStruct(share, FP), jax.ShapeDtypeStruct((per, SUB, d), BF), gate,
               jax.ShapeDtypeStruct((we[0], units), BF), jax.ShapeDtypeStruct(share, FP),
               jax.ShapeDtypeStruct((length, d), BF), jax.ShapeDtypeStruct((8, d), FP),
               shrink]
    out_specs = [whole(r.shape) for r in results]
    for at in (0, 5, 7):
        out_specs[at] = ANYWHERE
    held = [q, k, vt, tags, bars, wm, gains]
    return pl.pallas_call(
        partial(middle_kernel, kv, group, unit, line, per, steps),
        grid=(3 * steps + 8,),
        in_specs=[whole(a.shape) for a in held] + [ANYWHERE] * 4,
        out_specs=out_specs,
        out_shape=results,
        scratch_shapes=[pltpu.VMEM((kv, n, SUB * group), FP), pltpu.VMEM((kv, 8, SUB * group), FP),
                        pltpu.VMEM(share, BF), pltpu.VMEM((length, d), BF), pltpu.VMEM(we, BF), pltpu.VMEM(ws, BF),
                        pltpu.SemaphoreType.DMA((6,)),
                        pltpu.VMEM(share, FP), pltpu.VMEM((length, d), BF), pltpu.VMEM((length, units), BF),
                        pltpu.VMEM((length, 2 * units), BF), pltpu.VMEM(q.shape, BF), pltpu.VMEM((we[0], units), BF),
                        *pairs_scratch(per, d, True), pltpu.SemaphoreType.DMA((4, 4 * per)),
                        *pairs_scratch(per, d, True), pltpu.VMEM((per, SUB, d), BF),
                        pltpu.SemaphoreType.DMA((4, 4 * per)),
                        *pairs_scratch(per, d, False), *more],
        compiler_params=params(collective_id=1, has_side_effects=True),
        name="middle",
    )(*held, x, dy, *weights)


def back_kernel(kv, group, unit, scale, blocks, per, line, *refs):
    refs = list(refs)
    take = lambda count: [refs.pop(0) for _ in range(count)]
    q_ref, k_ref, v_ref, kt_ref, tags_ref, bars_ref, lse_ref, ctx_block, dh_block, wm_ref = take(10)
    raw_ref, cos_ref, sin_ref, all_gains, base_ref, dg2_ref, other_ref = take(7)
    x_all, dh_all = take(2)
    late_from = take(4)
    grads = take(2) if line else []
    in_ref, out_ref, gains_out = take(3)
    sums = take(3) if line else []
    weight_grads = [] if line else take(2)
    late_to = take(4)
    wp_ref, ctx_ref, dh_ref, xn_ref = late_to
    late_sem = take(1)[0]
    late = [pltpu.make_async_copy(a, b, late_sem.at[w]) for w, (a, b) in enumerate(zip(late_from, late_to))]
    dk_ref, dv_ref, dq_ref, dqkv_ref = take(4)
    b_far, b_sems, x_held, x_near, x_sems = take(5)
    mine_ref, far_ref, x_far, f_sems, x_ref, dh_own, own_sems, heads_ref, fold_ref = take(9)
    place = Place(line)
    i = pl.program_id(0)
    b = blocks - 1 - i
    n = LANES
    pairs = Pairs(place, per, x_held, x_near, x_sems, lambda s: s % x_held.shape[0])
    subs = ROWS // SUB
    share, d = x_ref.shape
    gq, gk = all_gains[:, 2 * d:2 * d + n], all_gains[:, 2 * d + n:]
    tile = 256
    tensors = lax.axis_size("tensor")
    mates = [(place.dp, (place.t + step) % tensors) for step in range(1, tensors)]
    peers = []
    own_rows = pl.ds(pl.multiple_of(place.t * share, share), share)
    own_copies = [pltpu.make_async_copy(x_all.at[own_rows, :], x_ref, own_sems.at[0]),
                  pltpu.make_async_copy(dh_all, dh_own, own_sems.at[1])]
    if line:
        shards = 2 * line
        gm_ref, gp_ref = take(2)
        expand = Reduce(place, grads[1], row_cut(grads[1].shape[0] // shards), *take(4))
        merge = Reduce(place, gm_ref, column_cut(gm_ref.shape[1] // shards), None, *take(3))
        project = Reduce(place, gp_ref, row_cut(gp_ref.shape[0] // shards), None, *take(3))
        shown, over, g_sems = take(3)
        peers = [((place.dp + step) % shards, place.t) for step in range(1, shards)]
    else:
        gp_ref, gm_ref = weight_grads

    def tiles(grad_ref, left_ref, right_ref):
        def one(t, carry):
            cut = pl.ds(pl.multiple_of(t * tile, tile), tile)
            grad_ref[cut, :] = dot(left_ref[:, cut], right_ref[...], 0, 0).astype(grad_ref.dtype)
            return carry

        lax.fori_loop(0, grad_ref.shape[0] // tile, one, 0)

    def write_up(values):
        sums[0][:, 0, :] = grads[0][...]
        sums[0][:, 1, :] = values

    def project_rows(t):
        cut = pl.ds(pl.multiple_of(t * tile, tile), tile)
        gp_ref[cut, :] = dot(xn_ref[:, cut], dqkv_ref[...], 0, 0).astype(BF)

    def chip(k):
        return send(far_ref.at[k], x_far.at[k], f_sems.at[0, k], f_sems.at[1, k], place.chip)

    def branch(k):
        return send(other_ref.at[k], b_far.at[k], b_sems.at[0, k], b_sems.at[1, k], place.chip)

    @pl.when(i == 0)
    def _():
        barrier = pltpu.get_barrier_semaphore()
        for device in mates + peers:
            pl.semaphore_signal(barrier, inc=1, device_id=device, device_id_type=MESH)
        for copy in late:
            copy.start()
        pl.semaphore_wait(barrier, len(mates + peers))
        if line:
            expand.start()
        for k in range(per):
            branch(k).start()
        dk_ref[...] = jnp.zeros_like(dk_ref)
        dv_ref[...] = jnp.zeros_like(dv_ref)
        heads_ref[...] = jnp.zeros_like(heads_ref)

    @pl.when(i < blocks)
    def _():
        here = pl.ds(pl.multiple_of(b * ROWS, ROWS), ROWS)
        dctx = dot(dh_block[...], wm_ref[...], 1, 1).astype(BF)
        ctx, q = ctx_block[...], q_ref[...]
        bars = jnp.concatenate([bars_ref[...]] * group, axis=0)
        wide, queries, outward, centres, lses = [], [], [], [], []
        ones = jnp.ones((8, n), BF)
        for h in range(kv):
            queries.append(stacked(q, h, group))
            wide.append(jnp.concatenate([queries[h], bars], axis=1))
            outward.append(stacked(dctx, h, group))
            both = outward[h].astype(FP) * stacked(ctx, h, group).astype(FP)
            high = both.astype(BF)
            low = (both - high.astype(FP)).astype(BF)
            centres.append((dot(ones, high, 1, 1) + dot(ones, low, 1, 1))[:1])
            lses.append(jnp.concatenate([lse_ref[u, h:h + 1, g * SUB:(g + 1) * SUB]
                                         for g in range(group) for u in range(ROWS // SUB)], axis=1))
        dq_ref[...] = jnp.zeros_like(dq_ref)

        def chunk(j, diagonal):
            at = pl.ds(pl.multiple_of(j * ROWS, ROWS), ROWS)
            tags = tags_ref[at, :]
            for h in range(kv):
                cut = slice(h * n, (h + 1) * n)
                keys = jnp.concatenate([k_ref[at, cut], tags], axis=1)
                p = jnp.exp2(dot(keys, wide[h], 1, 1) * unit - lses[h])
                if diagonal:
                    p = jnp.where(causal_tile(group, ROWS, ROWS, 0), p, 0.0)
                dp = dot(v_ref[at, cut], outward[h], 1, 1)
                ds = (p * (dp - centres[h])).astype(BF)
                dv_ref[at, cut] += dot(p.astype(BF), outward[h])
                dk_ref[at, cut] += dot(ds, queries[h])
                dq_ref[h] += dot(kt_ref[cut, at], ds)

        lax.fori_loop(0, b, lambda j, c: (chunk(j, False), c)[1], 0)
        chunk(b, True)

        cosines, sines = cos_ref[...], sin_ref[...]
        pieces = []
        for h in range(kv):
            dq = dq_ref[h].T
            for c in range(group + 1):
                if c < group:
                    grad, gain, row = dq[c * ROWS:(c + 1) * ROWS] * scale, gq, 0
                else:
                    grad, gain, row = dk_ref[here, h * n:(h + 1) * n] * scale, gk, 1
                grad = grad * cosines - pltpu.roll(grad, n // 2, 1) * sines
                at = (h * (group + 1) + c) * n
                piece, gain_grad = rms_pull(raw_ref[:, at:at + n], gain, grad)
                heads_ref[row] += fold_rows(gain_grad)
                pieces.append(piece)
            pieces.append(dv_ref[here, h * n:(h + 1) * n])
        dqkv = jnp.concatenate(pieces, axis=1).astype(BF)
        dqkv_ref[here, :] = dqkv
        pl.when(i == 0)(late[0].wait)
        part = dot(dqkv, wp_ref[...], 1, 1).astype(BF)
        for u in range(subs):
            s = subs * b + u
            pairs.put(s, part[u * SUB:(u + 1) * SUB], (i >= 2, s + 2 * subs))

    def chip_rows(mine, k, summed):
        @pl.when(mine)
        def _():
            mine_ref[pl.ds(pl.multiple_of(k * SUB, SUB), SUB), :] = summed

        @pl.when(jnp.logical_not(mine))
        def _():
            far_ref[k] = summed.astype(BF)
            chip(k).start()

    @pl.when(i >= 1)
    def _():
        for u in range(subs):
            pairs.add(subs * (b + 1) + u, chip_rows)

    @pl.when(i == 3)
    def _():
        for k in range(per):
            branch(k).wait()
            at = slice(k * SUB, (k + 1) * SUB)
            out_ref[at, :] = (base_ref[at, :] + b_far[k].astype(FP)).astype(BF)
        for copy in own_copies:
            copy.start()

    @pl.when(i == 1)
    def _():
        late[1].wait()
        late[2].wait()
        tiles(gm_ref, ctx_ref, dh_ref)

    if line:
        for k in range(1, line):
            pl.when(i == k - 1)(lambda k=k: expand.step(k))
            pl.when(i == k + 2)(lambda k=k: merge.step(k))
        pl.when(i == 2)(merge.start)

    def input_rows(k):
        at = slice(k * SUB, (k + 1) * SUB)
        chip(k).wait()
        summed = mine_ref[at, :] + x_far[k].astype(FP)
        pulled, gain_grad = rms_pull(x_ref[at, :].astype(FP), all_gains[:, :d], summed)
        in_ref[at, :] = (dh_own[at, :] + pulled).astype(BF)
        fold_ref[...] += fold_rows(gain_grad)

    def folded(ref):
        pieces = [fold_ref[...], dg2_ref[...], heads_ref[0], heads_ref[1]]
        row = jnp.sum(jnp.concatenate(pieces, axis=1), axis=0, keepdims=True)
        count = row.shape[1] // n
        for j in range(count):
            ref[j:j + 1, :] = row[:, j * n:(j + 1) * n]
        ref[count:, :] = jnp.zeros((ref.shape[0] - count, n), FP)

    def show(buffer, me, devices, first):
        copies = [send(buffer.at[me], buffer.at[me], g_sems.at[0, first + step], g_sems.at[1, first + step], device)
                  for step, device in enumerate(devices, 1)]
        for copy in copies:
            copy.start()
        return copies

    def added(buffer, me, devices, first):
        count = len(devices) + 1
        for step in range(1, count):
            who = (me - step + count) % count
            send(buffer.at[who], buffer.at[who], g_sems.at[0, first + step], g_sems.at[1, first + step],
                 place.sibling).wait_recv()
        total = buffer[0]
        for who in range(1, count):
            total = total + buffer[who]
        return total

    @pl.when(i == blocks)
    def _():
        fold_ref[...] = jnp.zeros_like(fold_ref)
        late[3].wait()
        for copy in own_copies:
            copy.wait()
        if not line:
            tiles(gp_ref, xn_ref, dqkv_ref)
            for k in range(per):
                input_rows(k)
            folded(gains_out)
        else:
            project_rows(project.turn(0))
            project.start()
            for q in range(1, line):
                project_rows(project.turn(q))
            expand.finish(write_up)
            project.step(1)
            merge.finish(write_to(sums[1]))
            project.step(2)
            for k in range(per):
                input_rows(k)
            folded(shown.at[place.t])
            copies = show(shown, place.t, mates, 0)
            project.step(3)
            over[place.dp] = added(shown, place.t, mates, 0)
            copies += show(over, place.dp, peers, tensors)
            project.finish(write_to(sums[2]))
            gains_out[...] = added(over, place.dp, peers, tensors)
            for copy in copies:
                copy.wait_send()
            for r in (expand, merge, project):
                r.drain()
        for s in range(2 * subs):
            pairs.sent(s)


def back(q, k, v, kt, tags, bars, lse, ctx, dh, wm, wp, raw, cosines, sines, gains, xn, base, dg2, other, x, dh_own,
         grads, kv, group, unit, scale, line):
    length = q.shape[0]
    n = LANES
    d = wm.shape[1]
    blocks = length // ROWS
    per = other.shape[0]
    share = base.shape
    block_of = lambda i: jnp.maximum(blocks - 1 - i, 0)
    rows = lambda w: pl.BlockSpec((ROWS, w), lambda i: (block_of(i), 0))
    late = [wp, ctx, dh, xn]
    gain_rows = (-(-(gains.shape[1] // n) // 8) * 8, n)
    scratch = [*[pltpu.VMEM(a.shape, BF) for a in late], pltpu.SemaphoreType.DMA((4,)),
               pltpu.VMEM((length, kv * n), FP), pltpu.VMEM((length, kv * n), FP),
               pltpu.VMEM((kv, n, ROWS * group), FP), pltpu.VMEM((length, wp.shape[1]), BF),
               pltpu.VMEM((per, SUB, d), BF), pltpu.SemaphoreType.DMA((2, per)),
               pltpu.VMEM((2 * ROWS // SUB, SUB, d), BF), pltpu.VMEM((2 * per, SUB, d), BF),
               pltpu.SemaphoreType.DMA((2, 4 * per)),
               pltpu.VMEM(share, FP), pltpu.VMEM((per, SUB, d), BF), pltpu.VMEM((per, SUB, d), BF),
               pltpu.SemaphoreType.DMA((2, per)), pltpu.VMEM(share, BF), pltpu.VMEM(share, FP),
               pltpu.SemaphoreType.DMA((2,)), pltpu.VMEM((2, 8, n), FP), pltpu.VMEM((8, d), FP)]
    results = [jax.ShapeDtypeStruct(share, BF), jax.ShapeDtypeStruct(share, BF), jax.ShapeDtypeStruct(gain_rows, FP)]
    if line:
        shards = 2 * line
        own = [grads[0].shape, (wm.shape[0], wm.shape[1] // shards),
               (wp.shape[0] // shards, wp.shape[1])]
        views = ((own[0][0], 2, own[0][1]), own[1], (own[2][0], own[2][1] // n, n))
        results += [jax.ShapeDtypeStruct(s, FP) for s in views]
        scratch += [pltpu.VMEM(wm.shape, BF), pltpu.VMEM(wp.shape, BF)]
        for w, s in enumerate(own):
            scratch += reduce_scratch(line, s, w == 0)
        scratch += [pltpu.VMEM((4, *gain_rows), FP), pltpu.VMEM((shards, *gain_rows), FP),
                    pltpu.SemaphoreType.DMA((2, 4 + shards))]
    else:
        results += [jax.ShapeDtypeStruct(wp.shape, BF), jax.ShapeDtypeStruct(wm.shape, BF)]
    args = [q, k, v, kt, tags, bars, lse, ctx, dh, wm, raw, cosines, sines, gains, base, dg2]
    more = [other, x, dh_own, *late, *grads]
    specs = [whole(a.shape) for a in args] + [ANYWHERE] * len(more)
    if line:
        specs[-2] = whole(grads[0].shape)
    for at in (0, 5, 7, 8, 10, 11, 12):
        specs[at] = rows(args[at].shape[1])
    specs[6] = pl.BlockSpec((ROWS // SUB, 8, SUB * group), lambda i: (block_of(i), 0, 0))
    return pl.pallas_call(
        partial(back_kernel, kv, group, unit, scale, blocks, per, line),
        grid=(blocks + 1,),
        in_specs=specs,
        out_specs=[whole(r.shape) for r in results],
        out_shape=results,
        scratch_shapes=scratch,
        compiler_params=params(collective_id=3, has_side_effects=True),
        name="back",
    )(*args, *more)


def adamw_step(weight, moment_one, moment_two, gradient, step_rate, decay):
    mean_next = BETA_ONE * moment_one + (1.0 - BETA_ONE) * gradient
    square_next = BETA_TWO * moment_two + (1.0 - BETA_TWO) * gradient * gradient
    mean_hat = mean_next / (1.0 - BETA_ONE**STEP)
    square_hat = square_next / (1.0 - BETA_TWO**STEP)
    weight_next = weight - step_rate * (mean_hat / (jnp.sqrt(square_hat) + EPS_ADAM) + decay * weight)
    return weight_next, mean_next, square_next


def shards(
    tokens, cotangent, parents, token_segment, tree_id,
    projection_weight, projection_first_moment, projection_second_moment,
    merge_master, merge_mean, merge_square,
    expand_master, expand_mean, expand_square,
    shrink_master, shrink_mean, shrink_square,
    gain_master, gain_mean, gain_square,
):
    x = tokens[0]
    dy = cotangent[0]
    length, d = x.shape
    d_own, kv, per, n = projection_weight.shape
    group = per - 2
    units = expand_master.shape[2]
    scale = n ** (-0.5)
    unit = scale * math.log2(math.e)
    line = 4 if lax.axis_size("dp") == 8 and d_own % LANES == 0 else 0
    if line:
        masters = (projection_weight.reshape(d_own, kv * per, n), merge_master, expand_master, shrink_master)
    else:
        wp, we = (lax.all_gather(w.astype(BF).reshape(d_own, -1), "dp", axis=0, tiled=True)
                  for w in (projection_weight, expand_master))
        wm, ws = (lax.all_gather(w.astype(BF), "dp", axis=1, tiled=True) for w in (merge_master, shrink_master))
        masters = (wp,)

    gains = gain_master[None]
    fronts = front(x, gains, token_segment, parents, tree_id, masters, kv, group, line)
    xn1, q, k, v, kt, vt, raw, tags, bars, cosines, sines = fronts[:11]
    if line:
        wp, wm, *low = fronts[11:]
    else:
        low = (we, ws)
    ctx, lse, base, other, gate_sum, up_grad, dh, dhb, dg2, shrink_sum = middle(
        q, k, vt, tags, bars, wm, x, dy, gains, low, kv, group, unit, line)
    backs = back(q, k, v, kt, tags, bars, lse, ctx, dhb, wm, wp, raw, cosines, sines, gains, xn1,
                 base, dg2, other, x, dh, (gate_sum, up_grad) if line else (), kv, group, unit, scale, line)
    input_grad, output, gain_rows = backs[:3]
    if line:
        expand_sum, merge_sum, project_sum = backs[3:]
    else:
        gain_rows = lax.psum(gain_rows, ("dp", "tensor"))
        project_sum, expand_sum = (
            lax.psum_scatter(g, "dp", scatter_dimension=0, tiled=True) for g in (backs[3], jnp.concatenate([gate_sum, up_grad], axis=1)))
        merge_sum, shrink_sum = (
            lax.psum_scatter(g, "dp", scatter_dimension=1, tiled=True) for g in (backs[4], shrink_sum))
    output, input_grad = output[None], input_grad[None]
    gain_grad = gain_rows.reshape(-1)[:gain_master.shape[0]]

    outs = [output, input_grad]
    for weight, mean, square, grad, rate in (
        (projection_weight, projection_first_moment, projection_second_moment, project_sum, RATE_PROJECT),
        (merge_master, merge_mean, merge_square, merge_sum, RATE_MERGE),
        (expand_master, expand_mean, expand_square, expand_sum, RATE_EXPAND),
        (shrink_master, shrink_mean, shrink_square, shrink_sum, RATE_SHRINK),
    ):
        grad = grad.astype(FP).reshape(weight.shape)
        after, mean_next, square_next = adamw_step(weight, mean, square, grad, rate, DECAY)
        outs += [after, mean_next, square_next, after.astype(BF)]
    gain_next, gain_mean_next, gain_square_next = adamw_step(
        gain_master, gain_mean, gain_square, gain_grad, RATE_GAIN, 0.0)
    return (*outs, gain_mean_next, gain_square_next, gain_next)


def solution(mesh):
    tokens = P("dp", None, None)
    project = P("dp", "tensor", None, None)
    columns = P("tensor", "dp")
    expand = P("dp", None, "tensor")
    shared = P("dp", "tensor", None)
    return jax.shard_map(
        shards,
        mesh=mesh,
        in_specs=(tokens, tokens, P(), P("dp", None), P("dp"), *[project] * 3, *[columns] * 3, *[expand] * 3,
                  *[columns] * 3, P(), P(), P()),
        out_specs=(shared, shared, *[project] * 4, *[columns] * 4, *[expand] * 4, *[columns] * 4, P(), P(), P()),
        check_vma=False,
    )
```
